32 devices in a mesh: groups: 2 (over y), gx: 16 (over z, x, core).
Axes of the slice: x: 2, y: 2, z: 4, core: 2. Of those that a mesh axis runs over, the one named last changes fastest.
Arguments:
- iterate: float32 [128, 64, 128], P(('groups', 'gx')), parts along dimension 0, may hold values from -6 to 6
- source: float32 [128, 64, 128], P(('groups', 'gx')), parts along dimension 0, may hold values from -24 to 24
- phase_field: float32 [128, 64, 128], P(('groups', 'gx')), parts along dimension 0, may hold values from 0 to 1
- block_owner: int32 [32], P('groups'), parts along dimension 0, may hold values from 0 to 15, each once
Outputs:
- solved: float32 [128, 64, 128], P(('groups', 'gx')), parts along dimension 0
- owned_correction: float32 [32, 16, 32], P(('groups', 'gx')), parts along dimension 0
The draws below stay inside these ranges and needn't reach their ends.
There are 2 independent parts, one for each index of `groups`. The reference program is written for one: setup_inputs(seed, part) draws one part's arguments, and reference() takes and returns one part's arrays. A program takes and returns all parts, laid end to end along the dimension named above; each array names one. Nothing has to cross between parts.
Inputs may be any that keep to these rules, and one draw needn't show every extreme that they name: `block_owner`: each block index appears exactly once.
All inputs are finite; a program needn't handle non-finite values.
Results may differ from the reference program's by a relative error of at most 0.00002.
Values sent between devices are 32-bit elements; how exact they have to be, the bound alone decides.
No kernel may reach another device: no remote copies, remote signals or barrier semaphores. Data moves between devices by JAX's collectives and lax.ppermute only.
A program may use at most 64 MiB of HBM per device.

```python
import jax
import jax.numpy as jnp
from jax import lax

CX = 4
NY = 64
NZ = 128
LEVELS = 6
SWEEPS = 1
COARSE_SWEEPS = 4
NX = 64
N_GX = 16


def level_of(key, dims, split, smallest, largest):
    factor_of = 1.0
    for dim, shards_of in split:
        heights = jax.random.uniform(jax.random.fold_in(jax.random.fold_in(key, 6), dim), (shards_of,), jnp.float32, smallest / len(split), largest / len(split))
        factor_of = factor_of * jnp.repeat(jnp.exp(heights), dims[dim] // shards_of).reshape((-1,) + (1,) * (len(dims) - 1 - dim))
    return factor_of


def normal_values(own_key, extent, deviation, reach, pieces=(), kind=jnp.bfloat16):
    values = jax.random.normal(own_key, extent, jnp.float32) * deviation
    if len(pieces) > 0:
        values = level_of(own_key, extent, pieces, -0.22, 0.18) * values
    return jnp.clip(values, min=-reach, max=reach).astype(kind)


def setup_inputs(seed: int = 0, part: int = 0) -> dict:
    keys = jax.random.split(jax.random.key(seed), 5)
    own_keys = jax.random.split(jax.random.fold_in(keys[4], part), 5)
    iterate = normal_values(own_keys[0], (NX, NY, NZ), 1.0, 6.0, ((0, 16),), jnp.float32)
    source = normal_values(own_keys[1], (NX, NY, NZ), 4.0, 24.0, ((0, 16),), jnp.float32)
    phase_field = jnp.clip(1.0 * jax.random.uniform(own_keys[2], (NX, NY, NZ), jnp.float32) ** level_of(own_keys[2], (NX, NY, NZ), ((0, 16),), -0.2, 0.2), 0.0, 1.0)
    block_owner = jax.random.permutation(own_keys[3], N_GX).astype(jnp.int32)
    return dict(iterate=iterate, source=source, phase_field=phase_field, block_owner=block_owner)


stiffness = 100.0
epsilon = 0.01


def next_along(values, along):
    widths = [(0, 0)] * values.ndim
    widths[along] = (0, 1)
    return lax.slice_in_dim(jnp.pad(values, widths), 1, values.shape[along] + 1, axis=along)


def prev_along(values, along):
    widths = [(0, 0)] * values.ndim
    widths[along] = (1, 0)
    return lax.slice_in_dim(jnp.pad(values, widths), 0, values.shape[along], axis=along)


def pad_layers(values):
    widths = [(1, 1)] + [(0, 0)] * (values.ndim - 1)
    return jnp.pad(values, widths)


def neighbours(padded, faces_x, faces_y, faces_z):
    middle = padded[1:-1]
    low_y = prev_along(faces_y, 1)
    low_z = prev_along(faces_z, 2)
    summed = faces_x[1:] * padded[2:] + faces_x[:-1] * padded[:-2]
    summed = summed + faces_y * next_along(middle, 1) + low_y * prev_along(middle, 1)
    summed = summed + faces_z * next_along(middle, 2) + low_z * prev_along(middle, 2)
    weight = faces_x[1:] + faces_x[:-1] + faces_y + low_y + faces_z + low_z
    return middle, summed, weight


def relax_colour(padded, source_p, coeffs_p, mask_p, mass_term):
    middle, summed, weight = neighbours(padded, coeffs_p[:-1, 0], coeffs_p[1:-1, 1], coeffs_p[1:-1, 2])
    return jnp.where(mask_p[1:-1], (source_p[1:-1] + summed) / (mass_term + weight), middle)


def apply_operator(padded, coeffs_p, mass_term):
    middle, summed, weight = neighbours(padded, coeffs_p[:-1, 0], coeffs_p[1:-1, 1], coeffs_p[1:-1, 2])
    return (mass_term + weight) * middle - summed


def colours(first_layer, layers, height, depth_cells):
    parity = (first_layer + jnp.arange(layers))[:, None, None] + jnp.arange(height)[None, :, None] + jnp.arange(depth_cells)[None, None, :]
    parity = parity % 2
    return parity == 0, parity == 1


def restrict(values):
    layers, height, depth_cells = values.shape
    return values.reshape(layers // 2, 2, height // 2, 2, depth_cells // 2, 2).sum(axis=(1, 3, 5))


def prolong(values):
    return jnp.repeat(jnp.repeat(jnp.repeat(values, 2, axis=0), 2, axis=1), 2, axis=2)


def coarsen(coeffs):
    layers, height, depth_cells = coeffs.shape[0], coeffs.shape[2], coeffs.shape[3]
    faces_x = coeffs[1::2, 0].reshape(layers // 2, height // 2, 2, depth_cells // 2, 2).sum(axis=(2, 4))
    faces_y = coeffs[:, 1, 1::2, :].reshape(layers // 2, 2, height // 2, depth_cells // 2, 2).sum(axis=(1, 4))
    faces_z = coeffs[:, 2, :, 1::2].reshape(layers // 2, 2, height // 2, 2, depth_cells // 2).sum(axis=(1, 3))
    return jnp.stack([faces_x, faces_y, faces_z], 1)


def sweep_once(field, source, coeffs, mass_term):
    layers, height, depth_cells = field.shape
    even_cells, odd_cells = colours(-1, layers + 2, height, depth_cells)
    coeffs_p = pad_layers(coeffs)
    source_p = pad_layers(source)
    field = relax_colour(pad_layers(field), source_p, coeffs_p, even_cells, mass_term)
    return relax_colour(pad_layers(field), source_p, coeffs_p, odd_cells, mass_term)


def vcycle_level(level, field, source, coeffs):
    mass_term = 8.0 ** (level - 1)
    if level == LEVELS:
        for sweep_turn in range(COARSE_SWEEPS):
            field = sweep_once(field, source, coeffs, mass_term)
        return field, field
    for sweep_turn in range(SWEEPS):
        field = sweep_once(field, source, coeffs, mass_term)
    residual = source - apply_operator(pad_layers(field), pad_layers(coeffs), mass_term)
    coarse_source = restrict(residual)
    coarse_fix, third_fix = vcycle_level(level + 1, jnp.zeros_like(coarse_source), coarse_source, coarsen(coeffs))
    if level == 2:
        third_fix = coarse_fix
    field = field + prolong(coarse_fix)
    for sweep_turn in range(SWEEPS):
        field = sweep_once(field, source, coeffs, mass_term)
    return field, third_fix


def reference(iterate, source, phase_field, block_owner):
    cell_coef = stiffness * (phase_field * phase_field + epsilon)
    keep_x = (jnp.arange(NX) < NX - 1)[:, None, None]
    keep_y = (jnp.arange(NY) < NY - 1)[None, :, None]
    keep_z = (jnp.arange(NZ) < NZ - 1)[None, None, :]
    faces_x = jnp.where(keep_x, 0.5 * (cell_coef + next_along(cell_coef, 0)), 0.0)
    faces_y = jnp.where(keep_y, 0.5 * (cell_coef + next_along(cell_coef, 1)), 0.0)
    faces_z = jnp.where(keep_z, 0.5 * (cell_coef + next_along(cell_coef, 2)), 0.0)
    coeffs = jnp.stack([faces_x, faces_y, faces_z], 1)
    solved, third_fix = vcycle_level(1, iterate, source, coeffs)
    blocks = third_fix.reshape(N_GX, CX // 4, NY // 4, NZ // 4)[block_owner]
    return solved, blocks.reshape(NX // 4, NY // 4, NZ // 4)
```

```python
import jax
import jax.numpy as jnp
from jax import lax
from jax.experimental import pallas as pl
from jax.experimental.pallas import tpu as pltpu
from jax.sharding import PartitionSpec as P

STIFFNESS = 100.0
EPSILON = 0.01
COARSE_SWEEPS = 4
PAD = 8


def from_behind(block, distance):
    devices = range(lax.axis_size("gx"))
    route = [(i - distance, i) for i in devices if i - distance in devices]
    return lax.ppermute(block, "gx", route)


def lanes_of(shape):
    return lax.broadcasted_iota(jnp.int32, shape, len(shape) - 1)


def rows_of(shape):
    return lax.broadcasted_iota(jnp.int32, shape, len(shape) - 2)


def ahead(values, step, axis):
    return pltpu.roll(values, values.shape[axis] - step, axis)


def behind(values, step, axis):
    return pltpu.roll(values, step, axis)


def with_partner(values, step, axis):
    index = lax.broadcasted_iota(jnp.int32, values.shape, axis)
    partner = jnp.where((index & step) == 0, ahead(values, step, axis), behind(values, step, axis))
    return values + partner


def even_row_sum(scratch, rows):
    return scratch[pl.ds(0, rows, 2), :] + scratch[pl.ds(1, rows, 2), :]


def fine_down_kernel(
    where_ref, iterate, source, phase, from_left, from_right,
    coarse_out, field_out, source_out, fx_out, fy_out, fz_out, inv_out,
    cell, e, fx, fy, fz, fzl, inv, held, pair,
):
    layers, height, depth = iterate.shape
    window = 3 * layers
    position, last = where_ref[0], where_ref[1]
    body = pl.ds(PAD, height)
    up, down = pl.ds(PAD + 1, height), pl.ds(PAD - 1, height)
    row, lane = rows_of((height, depth)), lanes_of((height, depth))
    even_sum = ((row + lane) & 1) == 0

    def pick(kind, w):
        if w < layers:
            return from_left[(0, layers, 2 * layers - 1)[kind] + w - (kind == 1)]
        if w < 2 * layers:
            return (iterate, source, phase)[kind][w - layers]
        return from_right[(0, layers, 2 * layers - 1)[kind] + w - 2 * layers]

    edge = jnp.zeros((PAD, depth), jnp.float32)
    for w in range(window):
        for padded in (e, fy):
            padded[w, :PAD] = edge
            padded[w, PAD + height:] = edge
        e[w, body] = pick(0, w)
        value = pick(2, w)
        cell[w, body] = STIFFNESS * (value * value + EPSILON)
        cell[w, PAD + height:] = edge
    for w in range(window):
        here = cell[w, body]
        if w < window - 1:
            face = 0.5 * (here + cell[w + 1, body])
            if w == layers - 1:
                face = jnp.where(position > 0, face, 0.0)
            if w == 2 * layers - 1:
                face = jnp.where(position < last, face, 0.0)
            fx[w] = face
        fy[w, body] = jnp.where(row < height - 1, 0.5 * (here + cell[w, up]), 0.0)
        face = jnp.where(lane < depth - 1, 0.5 * (here + ahead(here, 1, 1)), 0.0)
        fz[w] = face
        fzl[w] = behind(face, 1, 1)
    for w in range(1, window - 1):
        weight = fx[w] + fx[w - 1] + fy[w, body] + fy[w, down] + fz[w] + fzl[w]
        inv[w] = 1.0 / (1.0 + weight)

    def neigh(w):
        here = e[w, body]
        total = fx[w] * e[w + 1, body] + fx[w - 1] * e[w - 1, body]
        total = total + fy[w, body] * e[w, up] + fy[w, down] * e[w, down]
        return total + fz[w] * ahead(here, 1, 1) + fzl[w] * behind(here, 1, 1)

    def mask(w, odd):
        return even_sum if (w + odd) % 2 == 0 else ~even_sum

    for w in range(1, window - 1):
        total = pick(1, w) + neigh(w)
        if layers <= w < 2 * layers:
            held[w - layers] = total
        e[w, body] = jnp.where(mask(w, 0), total * inv[w], e[w, body])
    for w in range(2, window - 2):
        total = (pick(1, w) + neigh(w)) * inv[w]
        e[w, body] = jnp.where(mask(w, 1), total, e[w, body])

    first = layers - 2
    for w in range(first, window - first):
        field_out[w - first] = e[w, body]
    first = layers - 1
    for w in range(first - 1, window - first):
        fx_out[w - first + 1] = fx[w]
    for w in range(first, window - first):
        source_out[w - first] = pick(1, w)
        fy_out[w - first] = fy[w]
        fz_out[w - first] = fz[w]
        inv_out[w - first] = inv[w]

    half = height // 2
    lane = lanes_of((half, depth))
    first_of_two = (lane & 1) == 0

    def residual(w):
        return jnp.where(mask(w, 0), pick(1, w) + neigh(w) - held[w - layers], 0.0)

    def merged(one, two):
        return jnp.where(first_of_two, one, two)

    def slabs(make, reduce_rows, reduce_lanes):
        found = []
        for t in range(2):
            pair[t] = make(layers + 2 * t)
            found.append(reduce_lanes(reduce_rows(pair.at[t])))
        return merged(found[0], found[1])

    def both_rows(scratch):
        return even_row_sum(scratch, half)

    def odd_rows(scratch):
        return scratch[pl.ds(1, half, 2), :]

    def both_lanes(values):
        return with_partner(values, 1, 1)

    def odd_lanes(values):
        return jnp.where(first_of_two, ahead(values, 1, 1), values)

    coarse_out[0] = slabs(lambda w: residual(w) + residual(w + 1), both_rows, both_lanes)
    coarse_out[1] = slabs(lambda w: fx[w + 1], both_rows, both_lanes)
    coarse_out[2] = slabs(lambda w: fy[w, body] + fy[w + 1, body], odd_rows, both_lanes)
    coarse_out[3] = slabs(lambda w: fz[w] + fz[w + 1], both_rows, odd_lanes)


class Level:
    def __init__(self, mass, source, faces, row_step, lane_step):
        self.source, self.row_step, self.lane_step = source, row_step, lane_step
        self.fx, self.fy, self.fz = faces
        self.layers, rows, lanes = source.shape
        nothing = jnp.zeros_like(source[:1])
        self.nothing = nothing
        self.fxl = jnp.concatenate([nothing, self.fx[:-1]], 0)
        self.fyl = behind(self.fy, row_step, 1)
        self.fzl = behind(self.fz, lane_step, 2)
        weight = self.fx + self.fxl + self.fy + self.fyl + self.fz + self.fzl
        self.inv = 1.0 / (mass + weight)
        shape = source.shape
        total = lax.broadcasted_iota(jnp.int32, shape, 0)
        total = total + rows_of(shape) // row_step + lanes_of(shape) // lane_step
        self.even = (total & 1) == 0

    def neigh(self, e):
        upper = jnp.concatenate([e[1:], self.nothing], 0)
        lower = jnp.concatenate([self.nothing, e[:-1]], 0)
        total = self.fx * upper + self.fxl * lower
        total = total + self.fy * ahead(e, self.row_step, 1) + self.fyl * behind(e, self.row_step, 1)
        return total + self.fz * ahead(e, self.lane_step, 2) + self.fzl * behind(e, self.lane_step, 2)

    def start(self):
        e = jnp.where(self.even, self.source * self.inv, 0.0)
        return self.odd_update(e)

    def even_update(self, e):
        return jnp.where(self.even, (self.source + self.neigh(e)) * self.inv, e)

    def odd_update(self, e):
        return jnp.where(self.even, e, (self.source + self.neigh(e)) * self.inv)

    def residual(self, e):
        return jnp.where(self.even, self.neigh(e), 0.0)

    def pairs(self, values):
        halves = values.reshape(self.layers // 2, 2, *values.shape[1:])
        return halves[:, 0] + halves[:, 1]

    def coarse_faces(self):
        row_bit = (rows_of(self.fx.shape) & self.row_step) != 0
        lane_bit = (lanes_of(self.fx.shape) & self.lane_step) != 0
        odd_layers = self.fx.reshape(self.layers // 2, 2, *self.fx.shape[1:])[:, 1]
        fx = self.in_plane(odd_layers)
        fy = self.in_plane(self.pairs(jnp.where(row_bit, self.fy, 0.0)))
        fz = self.in_plane(self.pairs(jnp.where(lane_bit, self.fz, 0.0)))
        return fx, fy, fz

    def in_plane(self, values):
        return with_partner(with_partner(values, self.row_step, 1), self.lane_step, 2)

    def restricted(self, values):
        return self.in_plane(self.pairs(values))


def doubled_layers(values):
    layers = values.shape[0]
    both = jnp.concatenate([values[:, None], values[:, None]], 1)
    return both.reshape(2 * layers, *values.shape[1:])


def small_cycle(mass, source, faces, row_step, lane_step, deeper):
    level = Level(mass, source, faces, row_step, lane_step)
    e = level.start()
    if deeper == 0:
        for turn in range(COARSE_SWEEPS - 1):
            e = level.odd_update(level.even_update(e))
        return e
    fix = small_cycle(
        8.0 * mass, level.restricted(level.residual(e)), level.coarse_faces(),
        2 * row_step, 2 * lane_step, deeper - 1,
    )
    e = e + doubled_layers(fix)
    return level.odd_update(level.even_update(e))


def chunked(count, size, body):
    size = min(size, count)
    if count == size:
        body(0)
    else:
        lax.fori_loop(0, count // size, lambda i, c: (body(i * size), c)[1], 0)


def coarse_kernel(
    where_ref, gathered, field, source, fx_in, fy_in, fz_in, inv_in,
    solved, owned,
    s2, fx2, fxl2, fy2, fz2, fzl2, inv2, e2,
    s3, fx3, fy3, fz3, fzl3, inv3, e3, pair3, small,
    e1, cor,
):
    blocks, _, half, lanes = gathered.shape
    height = 2 * half
    quarter = half // 2
    position, owner = where_ref[0], where_ref[2]
    total = blocks + 4

    body2, up2, down2 = pl.ds(PAD, half), pl.ds(PAD + 1, half), pl.ds(PAD - 1, half)
    row, lane = rows_of((half, lanes)), lanes_of((half, lanes))
    first_of_two = (lane & 1) == 0
    even2 = ((row + (lane & 1) + (lane >> 1)) & 1) == 0
    edge = jnp.zeros((PAD, lanes), jnp.float32)
    blank = jnp.zeros((half, lanes), jnp.float32)
    for j in (0, 1, total - 2, total - 1):
        for plain in (s2, fx2, fxl2, fz2, fzl2, inv2):
            plain[j] = blank
        for padded in (e2, fy2):
            padded[j] = jnp.zeros((half + 2 * PAD, lanes), jnp.float32)

    def setup2(at):
        for i in range(4):
            j = at + i
            s2[j + 2] = gathered[j, 0]
            fx2[j + 2] = gathered[j, 1]
            fy2[j + 2, body2] = gathered[j, 2]
            fz2[j + 2] = gathered[j, 3]
            fzl2[j + 2] = behind(gathered[j, 3], 2, 1)
            for padded in (e2, fy2):
                padded[j + 2, :PAD] = edge
                padded[j + 2, PAD + half:] = edge

    chunked(blocks, 4, setup2)

    def weights2(at):
        for i in range(4):
            j = at + i + 2
            low = jnp.where(first_of_two, ahead(fx2[j - 1], 1, 1), behind(fx2[j], 1, 1))
            weight = fx2[j] + low + fy2[j, body2] + fy2[j, down2] + fz2[j] + fzl2[j]
            inverse = 1.0 / (8.0 + weight)
            fxl2[j] = low
            inv2[j] = inverse
            e2[j, body2] = jnp.where(even2, s2[j] * inverse, 0.0)

    chunked(blocks, 4, weights2)

    def neigh2(at, count):
        here = [e2[at + i, body2] for i in range(-1, count + 1)]
        after = [ahead(v, 1, 1) for v in here]
        before = [behind(v, 1, 1) for v in here]
        found = []
        for i in range(count):
            j = at + i
            upper = jnp.where(first_of_two, after[i + 1], before[i + 2])
            lower = jnp.where(first_of_two, after[i], before[i + 1])
            sums = fx2[j] * upper + fxl2[j] * lower
            sums = sums + fy2[j, body2] * e2[j, up2] + fy2[j, down2] * e2[j, down2]
            sums = sums + fz2[j] * ahead(here[i + 1], 2, 1) + fzl2[j] * behind(here[i + 1], 2, 1)
            found.append(sums)
        return here[1:-1], found

    def update2(at, count, even):
        here, sums = neigh2(at, count)
        fresh = []
        for i in range(count):
            value = (s2[at + i] + sums[i]) * inv2[at + i]
            fresh.append(jnp.where(even2, value, here[i]) if even else jnp.where(even2, here[i], value))
        for i in range(count):
            e2[at + i, body2] = fresh[i]

    chunked(blocks, 4, lambda at: update2(at + 2, 4, False))

    body3, up3, down3 = pl.ds(PAD, quarter), pl.ds(PAD + 1, quarter), pl.ds(PAD - 1, quarter)
    row, lane = rows_of((quarter, lanes)), lanes_of((quarter, lanes))
    parity3 = row + (lane >> 2)
    odd_layer = (lane & 1) != 0
    odd_depth = (lane & 2) != 0
    edge3 = jnp.zeros((quarter + 2 * PAD, lanes), jnp.float32)
    for j in (0, blocks + 1):
        e3[j] = edge3
    fx3[0] = jnp.zeros((quarter, lanes), jnp.float32)

    def group(values):
        return with_partner(with_partner(values, 1, 1), 2, 1)

    def restrict2(at):
        _, sums = neigh2(at + 2, 4)
        for i in range(4):
            pair3[i] = jnp.where(even2, sums[i], 0.0)
        for i in range(4):
            j = at + i
            s3[j] = group(even_row_sum(pair3.at[i], quarter))
            fxs = fx2[j + 2, pl.ds(0, quarter, 2), :] + fx2[j + 2, pl.ds(1, quarter, 2), :]
            fx3[j + 1] = group(jnp.where(odd_layer, fxs, 0.0))
            fy3[j] = edge3
            fy3[j, body3] = group(fy2[j + 2, pl.ds(PAD + 1, quarter, 2), :])
            fzs = fz2[j + 2, pl.ds(0, quarter, 2), :] + fz2[j + 2, pl.ds(1, quarter, 2), :]
            face = group(jnp.where(odd_depth, fzs, 0.0))
            fz3[j] = face
            fzl3[j] = behind(face, 4, 1)

    chunked(blocks, 4, restrict2)

    def is_even3(j):
        return ((parity3 + j) & 1) == 0

    def weights3(at):
        for i in range(4):
            j = at + i
            weight = fx3[j + 1] + fx3[j] + fy3[j, body3] + fy3[j, down3] + fz3[j] + fzl3[j]
            inverse = 1.0 / (64.0 + weight)
            inv3[j] = inverse
            e3[j + 1] = edge3
            e3[j + 1, body3] = jnp.where(is_even3(j), s3[j] * inverse, 0.0)

    chunked(blocks, 4, weights3)

    def neigh3(j):
        here = e3[j + 1, body3]
        sums = fx3[j + 1] * e3[j + 2, body3] + fx3[j] * e3[j, body3]
        sums = sums + fy3[j, body3] * e3[j + 1, up3] + fy3[j, down3] * e3[j + 1, down3]
        return here, sums + fz3[j] * ahead(here, 4, 1) + fzl3[j] * behind(here, 4, 1)

    def update3(at, count, even):
        fresh = []
        for i in range(count):
            j = at + i
            here, sums = neigh3(j)
            value = (s3[j] + sums) * inv3[j]
            where = is_even3(j)
            fresh.append(jnp.where(where, value, here) if even else jnp.where(where, here, value))
        for i in range(count):
            e3[at + i + 1, body3] = fresh[i]

    chunked(blocks, 8, lambda at: update3(at, 8, False))

    def restrict3(at):
        for i in range(0, 4, 2):
            j = at + i
            parts = []
            for k in (j, j + 1):
                _, sums = neigh3(k)
                parts.append(jnp.where(is_even3(k), sums, 0.0))
            pair3[i, :quarter] = parts[0] + parts[1]
            pair3[i + 1, :quarter] = fz3[j] + fz3[j + 1]
        for i in range(0, 4, 2):
            j = at + i
            out = (at + i) // 2
            small[0, out] = with_partner(even_row_sum(pair3.at[i], PAD), 4, 1)
            fxs = fx3[j + 2, pl.ds(0, PAD, 2), :] + fx3[j + 2, pl.ds(1, PAD, 2), :]
            small[1, out] = with_partner(fxs, 4, 1)
            fys = fy3[j, pl.ds(PAD + 1, PAD, 2), :] + fy3[j + 1, pl.ds(PAD + 1, PAD, 2), :]
            small[2, out] = with_partner(fys, 4, 1)
            fzs = even_row_sum(pair3.at[i + 1], PAD)
            odd = (lanes_of((PAD, lanes)) & 4) != 0
            small[3, out] = with_partner(jnp.where(odd, fzs, 0.0), 4, 1)

    chunked(blocks, 4, restrict3)

    small[0] = small_cycle(512.0, small[0], (small[1], small[2], small[3]), 1, 8, 2)

    def prolong3(at):
        for i in range(4):
            j = at + i
            fix = small[0, j // 2]
            pair3[i, pl.ds(0, PAD, 2), :] = fix
            pair3[i, pl.ds(1, PAD, 2), :] = fix
        for i in range(4):
            j = at + i
            e3[j + 1, body3] = e3[j + 1, body3] + pair3[i, :quarter]

    chunked(blocks, 4, prolong3)
    chunked(blocks, 8, lambda at: update3(at, 8, True))
    chunked(blocks, 8, lambda at: update3(at, 8, False))

    wide, narrow = lanes_of((lanes, lanes)), rows_of((lanes, lanes))
    take = jnp.where(narrow == 4 * wide, 1.0, 0.0)
    block = jnp.dot(
        e3[owner + 1, body3], take, precision=lax.Precision.HIGHEST, preferred_element_type=jnp.float32
    )
    owned[0] = block[:, : lanes // 4]

    for k in range(5):
        j = position + k
        inside = (j >= 2) & (j < blocks + 2)
        third = jnp.clip(j - 1, 1, blocks)
        fix = jnp.where(inside, e3[third, body3], 0.0)
        pair3[0, pl.ds(0, quarter, 2), :] = fix
        pair3[0, pl.ds(1, quarter, 2), :] = fix
        e2[j, body2] = e2[j, body2] + pair3[0]
    update2(position + 1, 3, True)
    update2(position + 1, 3, False)

    body1, up1, down1 = pl.ds(PAD, height), pl.ds(PAD + 1, height), pl.ds(PAD - 1, height)
    rows, lane = rows_of((height, lanes)), lanes_of((height, lanes))
    even_sum = ((rows + lane) & 1) == 0
    lane = lanes_of((half, lanes))
    count = field.shape[0]
    for w in range(0, count, 2):
        coarse_layer = w // 2 - 1
        packed = e2[position + 2 + coarse_layer // 2, body2]
        if coarse_layer % 2 == 0:
            plain = jnp.where(first_of_two, packed, behind(packed, 1, 1))
        else:
            plain = jnp.where(first_of_two, ahead(packed, 1, 1), packed)
        cor[pl.ds(0, half, 2), :] = plain
        cor[pl.ds(1, half, 2), :] = plain
        fix = cor[...]
        for v in (w, w + 1):
            e1[v, :PAD] = edge
            e1[v, PAD + height:] = edge
            e1[v, body1] = field[v] + fix

    def smoothed1(w, even):
        here = e1[w, body1]
        face = fz_in[w - 1]
        sums = fx_in[w] * e1[w + 1, body1] + fx_in[w - 1] * e1[w - 1, body1]
        sums = sums + fy_in[w - 1, body1] * e1[w, up1] + fy_in[w - 1, down1] * e1[w, down1]
        sums = sums + face * ahead(here, 1, 1) + behind(face, 1, 1) * behind(here, 1, 1)
        value = (source[w - 1] + sums) * inv_in[w - 1]
        keep = even_sum if (w + even) % 2 == 0 else ~even_sum
        return jnp.where(keep, here, value)

    for w in range(1, count - 1):
        e1[w, body1] = smoothed1(w, 1)
    for w in range(2, count - 2):
        solved[w - 2] = smoothed1(w, 0)


def f32(*shape):
    return jax.ShapeDtypeStruct(shape, jnp.float32)


def vmem(*shape):
    return pltpu.VMEM(shape, jnp.float32)


def on_device(iterate, source, phase_field, block_owner):
    layers, height, depth = iterate.shape
    position = lax.axis_index("gx")
    blocks = lax.axis_size("gx")
    where = jnp.stack([position, jnp.full_like(position, blocks - 1), block_owner[position]]).astype(jnp.int32)
    to_left = jnp.concatenate([iterate, source[:-1], phase_field], 0)
    to_right = jnp.concatenate([iterate, source[1:], phase_field], 0)
    from_left = from_behind(to_right, 1)
    from_right = from_behind(to_left, -1)
    window = 3 * layers
    half, quarter = height // 2, height // 4
    padded = height + 2 * PAD
    scalar = pl.BlockSpec(memory_space=pltpu.SMEM)
    whole = pl.BlockSpec(memory_space=pltpu.VMEM)
    coarse, field, source1, fx, fy, fz, inv = pl.pallas_call(
        fine_down_kernel,
        out_shape=(
            f32(4, half, depth), f32(layers + 4, height, depth), f32(layers + 2, height, depth),
            f32(layers + 3, height, depth), f32(layers + 2, padded, depth), f32(layers + 2, height, depth),
            f32(layers + 2, height, depth),
        ),
        in_specs=[scalar] + [whole] * 5,
        out_specs=[whole] * 7,
        scratch_shapes=[
            vmem(window, padded, depth), vmem(window, padded, depth), vmem(window, height, depth),
            vmem(window, padded, depth), vmem(window, height, depth), vmem(window, height, depth),
            vmem(window, height, depth), vmem(layers, height, depth), vmem(2, height, depth),
        ],
        compiler_params=pltpu.CompilerParams(vmem_limit_bytes=48 * 2**20),
    )(where, iterate, source, phase_field, from_left, from_right)
    gathered = lax.all_gather(coarse, "gx", axis=0, tiled=False)
    total = blocks + 4
    padded2, padded3 = half + 2 * PAD, quarter + 2 * PAD
    solved, owned = pl.pallas_call(
        coarse_kernel,
        out_shape=(f32(layers, height, depth), f32(1, quarter, depth // 4)),
        in_specs=[scalar] + [whole] * 7,
        out_specs=[whole] * 2,
        scratch_shapes=[
            vmem(total, half, depth), vmem(total, half, depth), vmem(total, half, depth),
            vmem(total, padded2, depth), vmem(total, half, depth), vmem(total, half, depth),
            vmem(total, half, depth), vmem(total, padded2, depth),
            vmem(blocks, quarter, depth), vmem(blocks + 1, quarter, depth), vmem(blocks, padded3, depth),
            vmem(blocks, quarter, depth), vmem(blocks, quarter, depth), vmem(blocks, quarter, depth),
            vmem(blocks + 2, padded3, depth), vmem(4, half, depth), vmem(4, blocks // 2, PAD, depth),
            vmem(layers + 4, padded, depth), vmem(height, depth),
        ],
        compiler_params=pltpu.CompilerParams(vmem_limit_bytes=56 * 2**20),
    )(where, gathered, field, source1, fx, fy, fz, inv)
    return solved, owned


def solution(mesh):
    split = P(("groups", "gx"), None, None)
    return jax.shard_map(
        on_device,
        mesh=mesh,
        in_specs=(split, split, split, P("groups")),
        out_specs=(split, split),
        check_vma=False,
    )
```

```python
import jax
import jax.numpy as jnp
from jax import lax
from jax.experimental import pallas as pl
from jax.experimental.pallas import tpu as pltpu
from jax.sharding import PartitionSpec as P

STIFFNESS = 100.0
EPSILON = 0.01
COARSE_SWEEPS = 4
PAD = 8


def from_behind(block, distance):
    devices = range(lax.axis_size("gx"))
    route = [(i - distance, i) for i in devices if i - distance in devices]
    return lax.ppermute(block, "gx", route)


def lanes_of(shape):
    return lax.broadcasted_iota(jnp.int32, shape, len(shape) - 1)


def rows_of(shape):
    return lax.broadcasted_iota(jnp.int32, shape, len(shape) - 2)


def ahead(values, step, axis):
    return pltpu.roll(values, values.shape[axis] - step, axis)


def behind(values, step, axis):
    return pltpu.roll(values, step, axis)


def with_partner(values, step, axis):
    index = lax.broadcasted_iota(jnp.int32, values.shape, axis)
    partner = jnp.where((index & step) == 0, ahead(values, step, axis), behind(values, step, axis))
    return values + partner


def even_row_sum(scratch, rows):
    return scratch[pl.ds(0, rows, 2), :] + scratch[pl.ds(1, rows, 2), :]


def edge_kernel(iterate, source, phase, to_left, to_right):
    layers, height, depth = iterate.shape
    row, lane = rows_of((height, depth)), lanes_of((height, depth))
    even_sum = ((row + lane) & 1) == 0
    odd_lane = (lanes_of((height // 2, depth)) & 1) != 0
    cell = []
    for w in range(layers):
        value = phase[w]
        cell.append(STIFFNESS * (value * value + EPSILON))
    for out, near, step in ((to_left, 0, 1), (to_right, layers - 1, -1)):
        inner, far = near + step, near + 2 * step
        here, e = cell[inner], iterate[inner]
        face_near, face_far = 0.5 * (here + cell[near]), 0.5 * (here + cell[far])
        fy = jnp.where(row < height - 1, 0.5 * (here + ahead(here, 1, 0)), 0.0)
        fz = jnp.where(lane < depth - 1, 0.5 * (here + ahead(here, 1, 1)), 0.0)
        fyl, fzl = behind(fy, 1, 0), behind(fz, 1, 1)
        total = face_near * iterate[near] + face_far * iterate[far]
        total = total + fy * ahead(e, 1, 0) + fyl * behind(e, 1, 0)
        total = total + fz * ahead(e, 1, 1) + fzl * behind(e, 1, 1)
        weight = 1.0 + (face_near + face_far + fy + fyl + fz + fzl)
        even = even_sum if inner % 2 == 0 else ~even_sum
        out[:height] = cell[near]
        out[height:2 * height] = here
        out[2 * height:3 * height] = source[near]
        out[3 * height:4 * height] = jnp.where(even, (source[inner] + total) / weight, e)
        out[4 * height:] = odd_cells(iterate.at[near], height // 2, odd_lane if near % 2 == 0 else ~odd_lane)


def odd_cells(ref, rows, first):
    return jnp.where(first, ref[pl.ds(0, rows, 2), :], ref[pl.ds(1, rows, 2), :])


def into_both_rows(ref, values):
    rows = values.shape[0]
    ref[pl.ds(0, rows, 2), :] = values
    ref[pl.ds(1, rows, 2), :] = values


def fine_down_kernel(
    where_ref, iterate, source, phase, from_left, from_right,
    to_left, to_right, field_out, source_out, fx, fy, fz, inv,
    cell, e, fzl, held, pair,
):
    layers, height, depth = iterate.shape
    window = layers + 4
    position, last = where_ref[0], where_ref[1]
    body = pl.ds(PAD, height)
    up, down = pl.ds(PAD + 1, height), pl.ds(PAD - 1, height)
    row, lane = rows_of((height, depth)), lanes_of((height, depth))
    even_sum = ((row + lane) & 1) == 0
    half = height // 2

    def part(ref, k):
        return ref[k * height:(k + 1) * height]

    edge = jnp.zeros((PAD, depth), jnp.float32)
    for w in range(window):
        for padded in (e, fy):
            padded[w, :PAD] = edge
            padded[w, PAD + height:] = edge
        cell[w, PAD + height:] = edge
    for ref, outer, inner in ((from_left, 0, 1), (from_right, window - 1, window - 2)):
        cell[inner, body] = part(ref, 0)
        cell[outer, body] = part(ref, 1)
        source_out[inner] = part(ref, 2)
        e[outer, body] = part(ref, 3)
        into_both_rows(pair.at[0], ref[4 * height:])
        e[inner, body] = pair[0]
    for w in range(layers):
        value = phase[w]
        cell[w + 2, body] = STIFFNESS * (value * value + EPSILON)
        e[w + 2, body] = iterate[w]
        source_out[w + 2] = source[w]
    for w in range(window):
        here = cell[w, body]
        if w < window - 1:
            face = 0.5 * (here + cell[w + 1, body])
            if w == 1:
                face = jnp.where(position > 0, face, 0.0)
            if w == window - 3:
                face = jnp.where(position < last, face, 0.0)
            fx[w] = face
        if 0 < w < window - 1:
            fy[w, body] = jnp.where(row < height - 1, 0.5 * (here + cell[w, up]), 0.0)
            face = jnp.where(lane < depth - 1, 0.5 * (here + ahead(here, 1, 1)), 0.0)
            fz[w] = face
            fzl[w] = behind(face, 1, 1)
    for w in range(1, window - 1):
        weight = fx[w] + fx[w - 1] + fy[w, body] + fy[w, down] + fz[w] + fzl[w]
        inv[w] = 1.0 / (1.0 + weight)

    def neigh(w):
        here = e[w, body]
        total = fx[w] * e[w + 1, body] + fx[w - 1] * e[w - 1, body]
        total = total + fy[w, body] * e[w, up] + fy[w, down] * e[w, down]
        return total + fz[w] * ahead(here, 1, 1) + fzl[w] * behind(here, 1, 1)

    def mask(w, odd):
        return even_sum if (w + odd) % 2 == 0 else ~even_sum

    for w in range(1, window - 1):
        total = source_out[w] + neigh(w)
        if 2 <= w < layers + 2:
            held[w - 2] = total
        e[w, body] = jnp.where(mask(w, 0), total * inv[w], e[w, body])
    for w in range(1, window - 1):
        total = (source_out[w] + neigh(w)) * inv[w]
        e[w, body] = jnp.where(mask(w, 1), total, e[w, body])
        field_out[w] = e[w, body]

    lane = lanes_of((half, depth))
    first_of_two = (lane & 1) == 0

    def residual(w):
        return jnp.where(mask(w, 0), source_out[w] + neigh(w) - held[w - 2], 0.0)

    def slabs(make, reduce_rows, reduce_lanes, start=2):
        found = []
        for t in range(2):
            pair[t] = make(start + 2 * t)
            found.append(reduce_lanes(reduce_rows(pair.at[t])))
        return jnp.where(first_of_two, found[0], found[1])

    def both_rows(scratch):
        return even_row_sum(scratch, half)

    def odd_rows(scratch):
        return scratch[pl.ds(1, half, 2), :]

    def both_lanes(values):
        return with_partner(values, 1, 1)

    def odd_lanes(values):
        return jnp.where(first_of_two, ahead(values, 1, 1), values)

    coarse_source = slabs(lambda w: residual(w) + residual(w + 1), both_rows, both_lanes)
    coarse_fy = slabs(lambda w: fy[w, body] + fy[w + 1, body], odd_rows, both_lanes)
    coarse_fz = slabs(lambda w: fz[w] + fz[w + 1], both_rows, odd_lanes)
    to_left[1] = slabs(lambda w: fx[w + 1], both_rows, both_lanes)
    to_right[1] = slabs(lambda w: fx[w - 1], both_rows, both_lanes)
    for out in (to_left, to_right):
        out[0], out[2], out[3] = coarse_source, coarse_fy, coarse_fz
    odd_lane = ~first_of_two
    for out, w in ((to_left, 3), (to_right, window - 4)):
        pair[0] = e[w, body]
        out[4] = odd_cells(pair.at[0], half, odd_lane if w % 2 == 0 else ~odd_lane)


def neigh2(e2, fx2, fxl2, fy2, fz2, fzl2, first_of_two, tiles):
    half = fx2.shape[1]
    body, up, down = pl.ds(PAD, half), pl.ds(PAD + 1, half), pl.ds(PAD - 1, half)
    needed = range(tiles[0], tiles[-1] + 3)
    here = {j: e2[j, body] for j in needed}
    after = {j: ahead(here[j], 1, 1) for j in needed}
    before = {j: behind(here[j], 1, 1) for j in needed}
    found = []
    for j in tiles:
        k = j + 1
        upper = jnp.where(first_of_two, after[k], before[k + 1])
        lower = jnp.where(first_of_two, after[k - 1], before[k])
        sums = fx2[j] * upper + fxl2[j] * lower
        sums = sums + fy2[j, body] * e2[k, up] + fy2[j, down] * e2[k, down]
        sums = sums + fz2[j] * ahead(here[k], 2, 1) + fzl2[j] * behind(here[k], 2, 1)
        found.append(sums)
    return found


def parities2(half, lanes):
    row, lane = rows_of((half, lanes)), lanes_of((half, lanes))
    return (lane & 1) == 0, ((row + (lane & 1) + (lane >> 1)) & 1) == 0


def group(values):
    return with_partner(with_partner(values, 1, 1), 2, 1)


def middle_down_kernel(
    where_ref, own_left, own_right, from_left, from_right,
    slots, e2_out, s2, fx2, fxl2, fy2, fz2, inv2,
    e2, fzl2, pair,
):
    _, half, lanes = own_left.shape
    quarter = half // 2
    position = where_ref[0]
    first_of_two, even2 = parities2(half, lanes)
    body, down = pl.ds(PAD, half), pl.ds(PAD - 1, half)
    edge = jnp.zeros((PAD, lanes), jnp.float32)
    for j in range(5):
        e2[j] = jnp.zeros((half + 2 * PAD, lanes), jnp.float32)
    for j, ref in enumerate((from_left, own_left, from_right)):
        s2[j] = ref[0]
        fy2[j, :PAD] = edge
        fy2[j, body] = ref[2]
        fy2[j, PAD + half:] = edge
        fz2[j] = ref[3]
        fzl2[j] = behind(ref[3], 2, 1)
    fx2[0] = jnp.where(first_of_two, ahead(from_left[1], 1, 1), behind(own_right[1], 1, 1))
    fx2[1] = own_left[1]
    fx2[2] = from_right[1]
    fxl2[0] = from_left[1]
    fxl2[1] = own_right[1]
    fxl2[2] = jnp.where(first_of_two, ahead(own_left[1], 1, 1), behind(from_right[1], 1, 1))
    for j in range(3):
        weight = fx2[j] + fxl2[j] + fy2[j, body] + fy2[j, down] + fz2[j] + fzl2[j]
        inverse = 1.0 / (8.0 + weight)
        inv2[j] = inverse
        e2[j + 1, body] = jnp.where(even2, s2[j] * inverse, 0.0)

    def neigh(tiles):
        return neigh2(e2, fx2, fxl2, fy2, fz2, fzl2, first_of_two, tiles)

    fresh = [
        jnp.where(even2, e2[j + 1, body], (s2[j] + sums) * inv2[j]) for j, sums in enumerate(neigh((0, 1, 2)))
    ]
    for j in range(3):
        e2[j + 1, body] = fresh[j]
        e2_out[j] = fresh[j]
    pair[0] = jnp.where(even2, neigh((1,))[0], 0.0)
    lane = lanes_of((quarter, lanes))
    odd_layer, odd_depth, item = (lane & 1) != 0, (lane & 2) != 0, lane & 3
    source = group(even_row_sum(pair.at[0], quarter))
    fx = group(jnp.where(odd_layer, even_row_sum(fx2.at[1], quarter), 0.0))
    fy = group(fy2[1, pl.ds(PAD + 1, quarter, 2), :])
    fz = group(jnp.where(odd_depth, even_row_sum(fz2.at[1], quarter), 0.0))
    tile = jnp.where(item == 0, source, jnp.where(item == 1, fx, jnp.where(item == 2, fy, fz)))
    first = (((lane & 1) + (lane >> 1)) & 1) != 0
    pair[0] = jnp.where(first_of_two, fresh[2], fresh[1])
    pair[1] = jnp.where(first_of_two, fresh[1], fresh[0])
    for_left = odd_cells(pair.at[0], quarter, first)
    for_right = odd_cells(pair.at[1], quarter, first)
    for d in range(slots.shape[0]):
        slots[d, 0] = tile
        slots[d, 1] = jnp.where(position < d, for_right, for_left)


class Level:
    def __init__(self, mass, source, faces, row_step, lane_step):
        self.source, self.row_step, self.lane_step = source, row_step, lane_step
        self.fx, self.fy, self.fz = faces
        self.layers, rows, lanes = source.shape
        nothing = jnp.zeros_like(source[:1])
        self.nothing = nothing
        self.fxl = jnp.concatenate([nothing, self.fx[:-1]], 0)
        self.fyl = behind(self.fy, row_step, 1)
        self.fzl = behind(self.fz, lane_step, 2)
        weight = self.fx + self.fxl + self.fy + self.fyl + self.fz + self.fzl
        self.inv = 1.0 / (mass + weight)
        shape = source.shape
        total = lax.broadcasted_iota(jnp.int32, shape, 0)
        total = total + rows_of(shape) // row_step + lanes_of(shape) // lane_step
        self.even = (total & 1) == 0

    def neigh(self, e):
        upper = jnp.concatenate([e[1:], self.nothing], 0)
        lower = jnp.concatenate([self.nothing, e[:-1]], 0)
        total = self.fx * upper + self.fxl * lower
        total = total + self.fy * ahead(e, self.row_step, 1) + self.fyl * behind(e, self.row_step, 1)
        return total + self.fz * ahead(e, self.lane_step, 2) + self.fzl * behind(e, self.lane_step, 2)

    def start(self):
        e = jnp.where(self.even, self.source * self.inv, 0.0)
        return self.odd_update(e)

    def even_update(self, e):
        return jnp.where(self.even, (self.source + self.neigh(e)) * self.inv, e)

    def odd_update(self, e):
        return jnp.where(self.even, e, (self.source + self.neigh(e)) * self.inv)

    def residual(self, e):
        return jnp.where(self.even, self.neigh(e), 0.0)

    def pairs(self, values):
        halves = values.reshape(self.layers // 2, 2, *values.shape[1:])
        return halves[:, 0] + halves[:, 1]

    def coarse_faces(self):
        row_bit = (rows_of(self.fx.shape) & self.row_step) != 0
        lane_bit = (lanes_of(self.fx.shape) & self.lane_step) != 0
        odd_layers = self.fx.reshape(self.layers // 2, 2, *self.fx.shape[1:])[:, 1]
        fx = self.in_plane(odd_layers)
        fy = self.in_plane(self.pairs(jnp.where(row_bit, self.fy, 0.0)))
        fz = self.in_plane(self.pairs(jnp.where(lane_bit, self.fz, 0.0)))
        return fx, fy, fz

    def in_plane(self, values):
        return with_partner(with_partner(values, self.row_step, 1), self.lane_step, 2)

    def restricted(self, values):
        return self.in_plane(self.pairs(values))


def doubled_layers(values):
    layers = values.shape[0]
    both = jnp.concatenate([values[:, None], values[:, None]], 1)
    return both.reshape(2 * layers, *values.shape[1:])


def small_cycle(mass, source, faces, row_step, lane_step, deeper):
    level = Level(mass, source, faces, row_step, lane_step)
    e = level.start()
    if deeper == 0:
        for turn in range(COARSE_SWEEPS - 1):
            e = level.odd_update(level.even_update(e))
        return e
    fix = small_cycle(
        8.0 * mass, level.restricted(level.residual(e)), level.coarse_faces(),
        2 * row_step, 2 * lane_step, deeper - 1,
    )
    e = e + doubled_layers(fix)
    return level.odd_update(level.even_update(e))


def chunked(count, size, body):
    size = min(size, count)
    if count == size:
        body(0)
    else:
        lax.fori_loop(0, count // size, lambda i, c: (body(i * size), c)[1], 0)


def coarse_kernel(
    where_ref, gathered, e2_in, s2, fx2, fxl2, fy2, fz2, inv2,
    field, source, fx_in, fy_in, fz_in, inv_in, from_left, from_right,
    solved, owned,
    s3, fx3, fy3, fz3, fzl3, inv3, e3, pair3, small, e2, fzl2, e1, cor,
):
    blocks, _, quarter, lanes = gathered.shape
    half, height = 2 * quarter, 4 * quarter
    position, last, owner = where_ref[0], where_ref[1], where_ref[2]

    body3, up3, down3 = pl.ds(PAD, quarter), pl.ds(PAD + 1, quarter), pl.ds(PAD - 1, quarter)
    row, lane = rows_of((quarter, lanes)), lanes_of((quarter, lanes))
    parity3 = row + (lane >> 2)
    item = lane & 3
    edge3 = jnp.zeros((quarter + 2 * PAD, lanes), jnp.float32)
    for j in (0, blocks + 1):
        e3[j] = edge3
    fx3[0] = jnp.zeros((quarter, lanes), jnp.float32)

    def unpack(at):
        for i in range(4):
            j = at + i
            tile = gathered[j, 0]
            moved = {0: tile}
            for step in (1, 2, 3):
                moved[step] = ahead(tile, step, 1)
                moved[-step] = behind(tile, step, 1)
            spread = []
            for k in range(4):
                value = moved[k]
                for slot in (1, 2, 3):
                    value = jnp.where(item == slot, moved[k - slot], value)
                spread.append(value)
            s3[j] = spread[0]
            fx3[j + 1] = spread[1]
            fy3[j] = edge3
            fy3[j, body3] = spread[2]
            fz3[j] = spread[3]
            fzl3[j] = behind(spread[3], 4, 1)

    chunked(blocks, 4, unpack)

    def is_even3(j):
        return ((parity3 + j) & 1) == 0

    def weights3(at):
        for i in range(4):
            j = at + i
            weight = fx3[j + 1] + fx3[j] + fy3[j, body3] + fy3[j, down3] + fz3[j] + fzl3[j]
            inverse = 1.0 / (64.0 + weight)
            inv3[j] = inverse
            e3[j + 1] = edge3
            e3[j + 1, body3] = jnp.where(is_even3(j), s3[j] * inverse, 0.0)

    chunked(blocks, 4, weights3)

    def neigh3(j):
        here = e3[j + 1, body3]
        sums = fx3[j + 1] * e3[j + 2, body3] + fx3[j] * e3[j, body3]
        sums = sums + fy3[j, body3] * e3[j + 1, up3] + fy3[j, down3] * e3[j + 1, down3]
        return here, sums + fz3[j] * ahead(here, 4, 1) + fzl3[j] * behind(here, 4, 1)

    def update3(at, count, even):
        fresh = []
        for i in range(count):
            j = at + i
            here, sums = neigh3(j)
            value = (s3[j] + sums) * inv3[j]
            where = is_even3(j)
            fresh.append(jnp.where(where, value, here) if even else jnp.where(where, here, value))
        for i in range(count):
            e3[at + i + 1, body3] = fresh[i]

    chunked(blocks, 8, lambda at: update3(at, 8, False))

    def restrict3(at):
        for i in range(0, 4, 2):
            j = at + i
            parts = []
            for k in (j, j + 1):
                _, sums = neigh3(k)
                parts.append(jnp.where(is_even3(k), sums, 0.0))
            pair3[i, :quarter] = parts[0] + parts[1]
            pair3[i + 1, :quarter] = fz3[j] + fz3[j + 1]
        for i in range(0, 4, 2):
            j = at + i
            out = (at + i) // 2
            small[0, out] = with_partner(even_row_sum(pair3.at[i], PAD), 4, 1)
            fxs = fx3[j + 2, pl.ds(0, PAD, 2), :] + fx3[j + 2, pl.ds(1, PAD, 2), :]
            small[1, out] = with_partner(fxs, 4, 1)
            fys = fy3[j, pl.ds(PAD + 1, PAD, 2), :] + fy3[j + 1, pl.ds(PAD + 1, PAD, 2), :]
            small[2, out] = with_partner(fys, 4, 1)
            fzs = even_row_sum(pair3.at[i + 1], PAD)
            odd = (lanes_of((PAD, lanes)) & 4) != 0
            small[3, out] = with_partner(jnp.where(odd, fzs, 0.0), 4, 1)

    chunked(blocks, 4, restrict3)

    small[0] = small_cycle(512.0, small[0], (small[1], small[2], small[3]), 1, 8, 2)

    def prolong3(at):
        for i in range(4):
            j = at + i
            fix = small[0, j // 2]
            pair3[i, pl.ds(0, PAD, 2), :] = fix
            pair3[i, pl.ds(1, PAD, 2), :] = fix
        for i in range(4):
            j = at + i
            e3[j + 1, body3] = e3[j + 1, body3] + pair3[i, :quarter]

    chunked(blocks, 4, prolong3)
    chunked(blocks, 8, lambda at: update3(at, 8, True))
    chunked(blocks, 8, lambda at: update3(at, 8, False))

    wide, narrow = lanes_of((lanes, lanes)), rows_of((lanes, lanes))
    take = jnp.where(narrow == 4 * wide, 1.0, 0.0)
    block = jnp.dot(
        e3[owner + 1, body3], take, precision=lax.Precision.HIGHEST, preferred_element_type=jnp.float32
    )
    owned[0] = block[:, : lanes // 4]

    first_of_two, even2 = parities2(half, lanes)
    body2 = pl.ds(PAD, half)
    edge = jnp.zeros((PAD, lanes), jnp.float32)
    left = gathered[jnp.maximum(position - 1, 0), 1]
    right = gathered[jnp.minimum(position + 1, last), 1]
    into_both_rows(pair3.at[0], left)
    into_both_rows(pair3.at[1], right)
    left, right = pair3[0], pair3[1]
    before = (
        left, jnp.where(first_of_two, left, e2_in[0]), e2_in[1], jnp.where(first_of_two, e2_in[2], right), right
    )
    for k in range(5):
        third = jnp.clip(position + k - 1, 1, blocks)
        into_both_rows(pair3.at[k % 4], e3[third, body3])
        e2[k, :PAD] = edge
        e2[k, PAD + half:] = edge
        e2[k, body2] = before[k] + pair3[k % 4]
    for j in range(3):
        fzl2[j] = behind(fz2[j], 2, 1)
    for even in (True, False):
        fresh = []
        for j, sums in enumerate(neigh2(e2, fx2, fxl2, fy2, fz2, fzl2, first_of_two, (0, 1, 2))):
            value, here = (s2[j] + sums) * inv2[j], e2[j + 1, body2]
            fresh.append(jnp.where(even2, value, here) if even else jnp.where(even2, here, value))
        for j in range(3):
            e2[j + 1, body2] = fresh[j]

    body1, up1, down1 = pl.ds(PAD, height), pl.ds(PAD + 1, height), pl.ds(PAD - 1, height)
    rows, lane = rows_of((height, lanes)), lanes_of((height, lanes))
    even_sum = ((rows + lane) & 1) == 0
    count = e1.shape[0]
    for w in range(0, count, 2):
        coarse_layer = w // 2 - 1
        packed = e2[2 + coarse_layer // 2, body2]
        if coarse_layer % 2 == 0:
            plain = jnp.where(first_of_two, packed, behind(packed, 1, 1))
        else:
            plain = jnp.where(first_of_two, ahead(packed, 1, 1), packed)
        into_both_rows(cor.at[0], plain)
        fix = cor[0]
        for v in (w, w + 1):
            e1[v, :PAD] = edge
            e1[v, PAD + height:] = edge
            if v in (0, count - 1):
                into_both_rows(cor.at[1], (from_left if v == 0 else from_right)[4])
                e1[v, body1] = cor[1] + fix
            else:
                e1[v, body1] = field[v] + fix

    def smoothed1(w, even):
        here = e1[w, body1]
        face = fz_in[w]
        sums = fx_in[w] * e1[w + 1, body1] + fx_in[w - 1] * e1[w - 1, body1]
        sums = sums + fy_in[w, body1] * e1[w, up1] + fy_in[w, down1] * e1[w, down1]
        sums = sums + face * ahead(here, 1, 1) + behind(face, 1, 1) * behind(here, 1, 1)
        value = (source[w] + sums) * inv_in[w]
        keep = even_sum if (w + even) % 2 == 0 else ~even_sum
        return jnp.where(keep, here, value)

    for w in range(1, count - 1):
        e1[w, body1] = smoothed1(w, 1)
    for w in range(2, count - 2):
        solved[w - 2] = smoothed1(w, 0)


def f32(*shape):
    return jax.ShapeDtypeStruct(shape, jnp.float32)


def vmem(*shape):
    return pltpu.VMEM(shape, jnp.float32)


def call(kernel, outs, scratch, scalars, operands):
    def size(shape):
        count = 4
        for extent in shape:
            count *= extent
        return count

    asked = 8 * 2**20 + sum(size(s.shape) for s in scratch) + sum(size(o.shape) for o in outs)
    asked += sum(size(o.shape) for o in operands)
    return pl.pallas_call(
        kernel,
        out_shape=tuple(outs),
        in_specs=[pl.BlockSpec(memory_space=pltpu.SMEM)] * len(scalars)
        + [pl.BlockSpec(memory_space=pltpu.VMEM)] * len(operands),
        out_specs=tuple([pl.BlockSpec(memory_space=pltpu.VMEM)] * len(outs)),
        scratch_shapes=scratch,
        compiler_params=pltpu.CompilerParams(vmem_limit_bytes=asked),
    )(*scalars, *operands)


def on_device(iterate, source, phase_field, block_owner):
    layers, height, depth = iterate.shape
    half, quarter = height // 2, height // 4
    blocks = lax.axis_size("gx")
    window = layers + 4
    padded, padded2, padded3 = height + 2 * PAD, half + 2 * PAD, quarter + 2 * PAD
    to_left, to_right = call(
        edge_kernel, [f32(4 * height + half, depth)] * 2, [], (), (iterate, source, phase_field)
    )
    halos = from_behind(to_right, 1), from_behind(to_left, -1)
    position = lax.axis_index("gx")
    where = jnp.stack([position, jnp.full_like(position, blocks - 1), block_owner[position]]).astype(jnp.int32)
    plain = f32(window, height, depth)
    to_left, to_right, *fine = call(
        fine_down_kernel,
        [f32(5, half, depth)] * 2 + [plain, plain, plain, f32(window, padded, depth), plain, plain],
        [
            vmem(window, padded, depth), vmem(window, padded, depth), vmem(window, height, depth),
            vmem(layers, height, depth), vmem(2, height, depth),
        ],
        (where,), (iterate, source, phase_field, *halos),
    )
    halos = from_behind(to_right, 1), from_behind(to_left, -1)
    plain = f32(3, half, depth)
    slots, *middle = call(
        middle_down_kernel,
        [f32(blocks, 2, quarter, depth), plain, plain, plain, plain, f32(3, padded2, depth), plain, plain],
        [vmem(5, padded2, depth), vmem(3, half, depth), vmem(2, half, depth)],
        (where,), (to_left, to_right, *halos),
    )
    gathered = lax.all_to_all(slots, "gx", 0, 0, tiled=True)
    solved, owned = call(
        coarse_kernel,
        [f32(layers, height, depth), f32(1, quarter, depth // 4)],
        [
            vmem(blocks, quarter, depth), vmem(blocks + 1, quarter, depth), vmem(blocks, padded3, depth),
            vmem(blocks, quarter, depth), vmem(blocks, quarter, depth), vmem(blocks, quarter, depth),
            vmem(blocks + 2, padded3, depth), vmem(4, half, depth), vmem(4, blocks // 2, PAD, depth),
            vmem(5, padded2, depth), vmem(3, half, depth), vmem(window, padded, depth), vmem(2, height, depth),
        ],
        (where,), (gathered, *middle, *fine, *halos),
    )
    return solved, owned


def solution(mesh):
    split = P(("groups", "gx"), None, None)
    return jax.shard_map(
        on_device,
        mesh=mesh,
        in_specs=(split, split, split, P("groups")),
        out_specs=(split, split),
        check_vma=False,
    )
```

```python
import jax
import jax.numpy as jnp
from jax import lax
from jax.experimental import pallas as pl
from jax.experimental.pallas import tpu as pltpu
from jax.sharding import PartitionSpec as P

STIFFNESS = 100.0
EPSILON = 0.01
COARSE_SWEEPS = 4
PAD = 8


def swapped(across, within):
    count = lax.axis_size("gx")
    chips = [(i, i + 1 if i % 2 else i - 1) for i in range(1, count - 1)]
    cores = [(i, i ^ 1) for i in range(count)]
    return lax.ppermute(across, "gx", chips), lax.ppermute(within, "gx", cores)


def by_side(across, within):
    on_left = lax.axis_index("gx") % 2 == 0
    return jnp.where(on_left, across, within), jnp.where(on_left, within, across)


def store_by_side(across, within, pieces):
    on_left = lax.axis_index("gx") % 2 == 0

    @pl.when(on_left)
    def _():
        for index, left, right in pieces:
            across[index] = left
            within[index] = right

    @pl.when(jnp.logical_not(on_left))
    def _():
        for index, left, right in pieces:
            across[index] = right
            within[index] = left


def lanes_of(shape):
    return lax.broadcasted_iota(jnp.int32, shape, len(shape) - 1)


def rows_of(shape):
    return lax.broadcasted_iota(jnp.int32, shape, len(shape) - 2)


def ahead(values, step, axis):
    return pltpu.roll(values, values.shape[axis] - step, axis)


def behind(values, step, axis):
    return pltpu.roll(values, step, axis)


def with_partner(values, step, axis):
    index = lax.broadcasted_iota(jnp.int32, values.shape, axis)
    partner = jnp.where((index & step) == 0, ahead(values, step, axis), behind(values, step, axis))
    return values + partner


def even_row_sum(scratch, rows):
    return scratch[pl.ds(0, rows, 2), :] + scratch[pl.ds(1, rows, 2), :]


def three_parts(ref):
    third = ref.shape[0] // 3
    return [ref.at[pl.ds(k * third, third)] for k in range(3)]


def edge_kernel(inputs, across, within):
    iterate, source, phase = three_parts(inputs)
    layers, height, depth = iterate.shape
    row, lane = rows_of((height, depth)), lanes_of((height, depth))
    even_sum = ((row + lane) & 1) == 0
    odd_lane = (lanes_of((height // 2, depth)) & 1) != 0
    cell = []
    for w in range(layers):
        value = phase[w]
        cell.append(STIFFNESS * (value * value + EPSILON))
    sides = []
    for near, step in ((0, 1), (layers - 1, -1)):
        inner, far = near + step, near + 2 * step
        here, e = cell[inner], iterate[inner]
        face_near, face_far = 0.5 * (here + cell[near]), 0.5 * (here + cell[far])
        fy = jnp.where(row < height - 1, 0.5 * (here + ahead(here, 1, 0)), 0.0)
        fz = jnp.where(lane < depth - 1, 0.5 * (here + ahead(here, 1, 1)), 0.0)
        fyl, fzl = behind(fy, 1, 0), behind(fz, 1, 1)
        total = face_near * iterate[near] + face_far * iterate[far]
        total = total + fy * ahead(e, 1, 0) + fyl * behind(e, 1, 0)
        total = total + fz * ahead(e, 1, 1) + fzl * behind(e, 1, 1)
        weight = 1.0 + (face_near + face_far + fy + fyl + fz + fzl)
        even = even_sum if inner % 2 == 0 else ~even_sum
        border = odd_cells(iterate.at[near], height // 2, odd_lane if near % 2 == 0 else ~odd_lane)
        updated = jnp.where(even, (source[inner] + total) / weight, e)
        sides.append((cell[near], here, source[near], updated, border))
    places = [pl.ds(k * height, height) for k in range(4)] + [pl.ds(4 * height, height // 2)]
    store_by_side(across, within, list(zip(places, *sides)))


def odd_cells(ref, rows, first):
    return jnp.where(first, ref[pl.ds(0, rows, 2), :], ref[pl.ds(1, rows, 2), :])


def into_both_rows(ref, values):
    rows = values.shape[0]
    ref[pl.ds(0, rows, 2), :] = values
    ref[pl.ds(1, rows, 2), :] = values


def fine_down_kernel(
    inputs, across_in, within_in,
    across, within, fx2_out, field_out, source_out, fx, fy, fz, inv,
    cell, e, fzl, held, pair,
):
    iterate, source, phase = three_parts(inputs)
    layers, height, depth = iterate.shape
    window = layers + 4
    position, last = lax.axis_index("gx"), lax.axis_size("gx") - 1
    body = pl.ds(PAD, height)
    up, down = pl.ds(PAD + 1, height), pl.ds(PAD - 1, height)
    row, lane = rows_of((height, depth)), lanes_of((height, depth))
    even_sum = ((row + lane) & 1) == 0
    half = height // 2

    def part(ref, k):
        return ref[k * height:(k + 1) * height]

    edge = jnp.zeros((PAD, depth), jnp.float32)
    for w in range(window):
        for padded in (e, fy):
            padded[w, :PAD] = edge
            padded[w, PAD + height:] = edge
        cell[w, PAD + height:] = edge
    halos = [by_side(part(across_in, k), part(within_in, k)) for k in range(4)]
    borders = by_side(across_in[4 * height:], within_in[4 * height:])
    for side, outer, inner in ((0, 0, 1), (1, window - 1, window - 2)):
        cell[inner, body] = halos[0][side]
        cell[outer, body] = halos[1][side]
        source_out[inner] = halos[2][side]
        e[outer, body] = halos[3][side]
        into_both_rows(pair.at[side], borders[side])
        e[inner, body] = pair[side]
    for w in range(layers):
        value = phase[w]
        cell[w + 2, body] = STIFFNESS * (value * value + EPSILON)
        e[w + 2, body] = iterate[w]
        source_out[w + 2] = source[w]
    for w in range(window):
        here = cell[w, body]
        if w < window - 1:
            face = 0.5 * (here + cell[w + 1, body])
            if w == 1:
                face = jnp.where(position > 0, face, 0.0)
            if w == window - 3:
                face = jnp.where(position < last, face, 0.0)
            fx[w] = face
        if 0 < w < window - 1:
            fy[w, body] = jnp.where(row < height - 1, 0.5 * (here + cell[w, up]), 0.0)
            face = jnp.where(lane < depth - 1, 0.5 * (here + ahead(here, 1, 1)), 0.0)
            fz[w] = face
            fzl[w] = behind(face, 1, 1)
    for w in range(1, window - 1):
        weight = fx[w] + fx[w - 1] + fy[w, body] + fy[w, down] + fz[w] + fzl[w]
        inv[w] = 1.0 / (1.0 + weight)

    def neigh(w):
        here = e[w, body]
        total = fx[w] * e[w + 1, body] + fx[w - 1] * e[w - 1, body]
        total = total + fy[w, body] * e[w, up] + fy[w, down] * e[w, down]
        return total + fz[w] * ahead(here, 1, 1) + fzl[w] * behind(here, 1, 1)

    def mask(w, odd):
        return even_sum if (w + odd) % 2 == 0 else ~even_sum

    for w in range(1, window - 1):
        total = source_out[w] + neigh(w)
        if 2 <= w < layers + 2:
            held[w - 2] = total
        e[w, body] = jnp.where(mask(w, 0), total * inv[w], e[w, body])
    for w in range(1, window - 1):
        total = (source_out[w] + neigh(w)) * inv[w]
        e[w, body] = jnp.where(mask(w, 1), total, e[w, body])
        field_out[w] = e[w, body]

    lane = lanes_of((half, depth))
    first_of_two = (lane & 1) == 0

    def residual(w):
        return jnp.where(mask(w, 0), source_out[w] + neigh(w) - held[w - 2], 0.0)

    def slabs(make, reduce_rows, reduce_lanes, start=2):
        found = []
        for t in range(2):
            pair[t] = make(start + 2 * t)
            found.append(reduce_lanes(reduce_rows(pair.at[t])))
        return jnp.where(first_of_two, found[0], found[1])

    def both_rows(scratch):
        return even_row_sum(scratch, half)

    def odd_rows(scratch):
        return scratch[pl.ds(1, half, 2), :]

    def both_lanes(values):
        return with_partner(values, 1, 1)

    def odd_lanes(values):
        return jnp.where(first_of_two, ahead(values, 1, 1), values)

    coarse_source = slabs(lambda w: residual(w) + residual(w + 1), both_rows, both_lanes)
    coarse_fy = slabs(lambda w: fy[w, body] + fy[w + 1, body], odd_rows, both_lanes)
    coarse_fz = slabs(lambda w: fz[w] + fz[w + 1], both_rows, odd_lanes)
    left_fx = slabs(lambda w: fx[w + 1], both_rows, both_lanes)
    right_fx = slabs(lambda w: fx[w - 1], both_rows, both_lanes)
    fx2_out[0], fx2_out[1] = left_fx, right_fx
    borders = []
    for t, w in enumerate((3, window - 4)):
        pair[t] = e[w, body]
        borders.append(odd_cells(pair.at[t], half, ~first_of_two if w % 2 == 0 else first_of_two))
    pieces = [(0, coarse_source), (2, coarse_fy), (3, coarse_fz)]
    pieces = [(k, value, value) for k, value in pieces]
    store_by_side(across, within, pieces + [(1, left_fx, right_fx), (4, *borders)])


def neigh2(e2, fx2, fxl2, fy2, fz2, fzl2, first_of_two, tiles):
    half = fx2.shape[1]
    body, up, down = pl.ds(PAD, half), pl.ds(PAD + 1, half), pl.ds(PAD - 1, half)
    needed = range(tiles[0], tiles[-1] + 3)
    here = {j: e2[j, body] for j in needed}
    after = {j: ahead(here[j], 1, 1) for j in needed}
    before = {j: behind(here[j], 1, 1) for j in needed}
    found = []
    for j in tiles:
        k = j + 1
        upper = jnp.where(first_of_two, after[k], before[k + 1])
        lower = jnp.where(first_of_two, after[k - 1], before[k])
        sums = fx2[j] * upper + fxl2[j] * lower
        sums = sums + fy2[j, body] * e2[k, up] + fy2[j, down] * e2[k, down]
        sums = sums + fz2[j] * ahead(here[k], 2, 1) + fzl2[j] * behind(here[k], 2, 1)
        found.append(sums)
    return found


def parities2(half, lanes):
    row, lane = rows_of((half, lanes)), lanes_of((half, lanes))
    return (lane & 1) == 0, ((row + (lane & 1) + (lane >> 1)) & 1) == 0


def group(values):
    return with_partner(with_partner(values, 1, 1), 2, 1)


def middle_down_kernel(
    own, own_fx, across_in, within_in,
    slots, e2_out, s2, fx2, fxl2, fy2, fz2, inv2,
    e2, fzl2, pair,
):
    _, half, lanes = own.shape
    quarter = half // 2
    position = lax.axis_index("gx")
    first_of_two, even2 = parities2(half, lanes)
    body, down = pl.ds(PAD, half), pl.ds(PAD - 1, half)
    edge = jnp.zeros((PAD, lanes), jnp.float32)
    for j in range(5):
        e2[j] = jnp.zeros((half + 2 * PAD, lanes), jnp.float32)
    def three(k):
        left, right = by_side(across_in[k], within_in[k])
        return left, own[k], right

    for j, (source, fy, fz) in enumerate(zip(three(0), three(2), three(3))):
        s2[j] = source
        fy2[j, :PAD] = edge
        fy2[j, body] = fy
        fy2[j, PAD + half:] = edge
        fz2[j] = fz
        fzl2[j] = behind(fz, 2, 1)
    left_fx, _, right_fx = three(1)
    fx2[0] = jnp.where(first_of_two, ahead(left_fx, 1, 1), behind(own_fx[1], 1, 1))
    fx2[1] = own_fx[0]
    fx2[2] = right_fx
    fxl2[0] = left_fx
    fxl2[1] = own_fx[1]
    fxl2[2] = jnp.where(first_of_two, ahead(own_fx[0], 1, 1), behind(right_fx, 1, 1))
    for j in range(3):
        weight = fx2[j] + fxl2[j] + fy2[j, body] + fy2[j, down] + fz2[j] + fzl2[j]
        inverse = 1.0 / (8.0 + weight)
        inv2[j] = inverse
        e2[j + 1, body] = jnp.where(even2, s2[j] * inverse, 0.0)

    def neigh(tiles):
        return neigh2(e2, fx2, fxl2, fy2, fz2, fzl2, first_of_two, tiles)

    fresh = [
        jnp.where(even2, e2[j + 1, body], (s2[j] + sums) * inv2[j]) for j, sums in enumerate(neigh((0, 1, 2)))
    ]
    for j in range(3):
        e2[j + 1, body] = fresh[j]
        e2_out[j] = fresh[j]
    pair[0] = jnp.where(even2, neigh((1,))[0], 0.0)
    lane = lanes_of((quarter, lanes))
    odd_layer, odd_depth, item = (lane & 1) != 0, (lane & 2) != 0, lane & 3
    source = group(even_row_sum(pair.at[0], quarter))
    fx = group(jnp.where(odd_layer, even_row_sum(fx2.at[1], quarter), 0.0))
    fy = group(fy2[1, pl.ds(PAD + 1, quarter, 2), :])
    fz = group(jnp.where(odd_depth, even_row_sum(fz2.at[1], quarter), 0.0))
    tile = jnp.where(item == 0, source, jnp.where(item == 1, fx, jnp.where(item == 2, fy, fz)))
    first = (((lane & 1) + (lane >> 1)) & 1) != 0
    pair[0] = jnp.where(first_of_two, fresh[2], fresh[1])
    pair[1] = jnp.where(first_of_two, fresh[1], fresh[0])
    for_left = odd_cells(pair.at[0], quarter, first)
    for_right = odd_cells(pair.at[1], quarter, first)
    for d in range(slots.shape[0]):
        slots[d, 0] = tile
        slots[d, 1] = jnp.where(position < d, for_right, for_left)


class Level:
    def __init__(self, mass, source, faces, row_step, lane_step):
        self.source, self.row_step, self.lane_step = source, row_step, lane_step
        self.fx, self.fy, self.fz = faces
        self.layers, rows, lanes = source.shape
        nothing = jnp.zeros_like(source[:1])
        self.nothing = nothing
        self.fxl = jnp.concatenate([nothing, self.fx[:-1]], 0)
        self.fyl = behind(self.fy, row_step, 1)
        self.fzl = behind(self.fz, lane_step, 2)
        weight = self.fx + self.fxl + self.fy + self.fyl + self.fz + self.fzl
        self.inv = 1.0 / (mass + weight)
        shape = source.shape
        total = lax.broadcasted_iota(jnp.int32, shape, 0)
        total = total + rows_of(shape) // row_step + lanes_of(shape) // lane_step
        self.even = (total & 1) == 0

    def neigh(self, e):
        upper = jnp.concatenate([e[1:], self.nothing], 0)
        lower = jnp.concatenate([self.nothing, e[:-1]], 0)
        total = self.fx * upper + self.fxl * lower
        total = total + self.fy * ahead(e, self.row_step, 1) + self.fyl * behind(e, self.row_step, 1)
        return total + self.fz * ahead(e, self.lane_step, 2) + self.fzl * behind(e, self.lane_step, 2)

    def start(self):
        e = jnp.where(self.even, self.source * self.inv, 0.0)
        return self.odd_update(e)

    def even_update(self, e):
        return jnp.where(self.even, (self.source + self.neigh(e)) * self.inv, e)

    def odd_update(self, e):
        return jnp.where(self.even, e, (self.source + self.neigh(e)) * self.inv)

    def residual(self, e):
        return jnp.where(self.even, self.neigh(e), 0.0)

    def pairs(self, values):
        halves = values.reshape(self.layers // 2, 2, *values.shape[1:])
        return halves[:, 0] + halves[:, 1]

    def coarse_faces(self):
        row_bit = (rows_of(self.fx.shape) & self.row_step) != 0
        lane_bit = (lanes_of(self.fx.shape) & self.lane_step) != 0
        odd_layers = self.fx.reshape(self.layers // 2, 2, *self.fx.shape[1:])[:, 1]
        fx = self.in_plane(odd_layers)
        fy = self.in_plane(self.pairs(jnp.where(row_bit, self.fy, 0.0)))
        fz = self.in_plane(self.pairs(jnp.where(lane_bit, self.fz, 0.0)))
        return fx, fy, fz

    def in_plane(self, values):
        return with_partner(with_partner(values, self.row_step, 1), self.lane_step, 2)

    def restricted(self, values):
        return self.in_plane(self.pairs(values))


def doubled_layers(values):
    layers = values.shape[0]
    both = jnp.concatenate([values[:, None], values[:, None]], 1)
    return both.reshape(2 * layers, *values.shape[1:])


def small_cycle(mass, source, faces, row_step, lane_step, deeper):
    level = Level(mass, source, faces, row_step, lane_step)
    e = level.start()
    if deeper == 0:
        for turn in range(COARSE_SWEEPS - 1):
            e = level.odd_update(level.even_update(e))
        return e
    fix = small_cycle(
        8.0 * mass, level.restricted(level.residual(e)), level.coarse_faces(),
        2 * row_step, 2 * lane_step, deeper - 1,
    )
    e = e + doubled_layers(fix)
    return level.odd_update(level.even_update(e))


def chunked(count, size, body):
    size = min(size, count)
    if count == size:
        body(0)
    else:
        lax.fori_loop(0, count // size, lambda i, c: (body(i * size), c)[1], 0)


def coarse_kernel(
    owner_of, gathered, e2_in, s2, fx2, fxl2, fy2, fz2, inv2,
    field, source, fx_in, fy_in, fz_in, inv_in, across_in, within_in,
    solved, owned,
    s3, fx3, fy3, fz3, fzl3, inv3, e3, pair3, small, e2, fzl2, e1, cor,
):
    blocks, _, quarter, lanes = gathered.shape
    half, height = 2 * quarter, 4 * quarter
    position, last = lax.axis_index("gx"), blocks - 1
    owner = owner_of[position]

    body3, up3, down3 = pl.ds(PAD, quarter), pl.ds(PAD + 1, quarter), pl.ds(PAD - 1, quarter)
    row, lane = rows_of((quarter, lanes)), lanes_of((quarter, lanes))
    parity3 = row + (lane >> 2)
    item = lane & 3
    edge3 = jnp.zeros((quarter + 2 * PAD, lanes), jnp.float32)
    for j in (0, blocks + 1):
        e3[j] = edge3
    fx3[0] = jnp.zeros((quarter, lanes), jnp.float32)

    def unpack(at):
        for i in range(4):
            j = at + i
            tile = gathered[j, 0]
            moved = {0: tile}
            for step in (1, 2, 3):
                moved[step] = ahead(tile, step, 1)
                moved[-step] = behind(tile, step, 1)
            spread = []
            for k in range(4):
                value = moved[k]
                for slot in (1, 2, 3):
                    value = jnp.where(item == slot, moved[k - slot], value)
                spread.append(value)
            s3[j] = spread[0]
            fx3[j + 1] = spread[1]
            fy3[j] = edge3
            fy3[j, body3] = spread[2]
            fz3[j] = spread[3]
            fzl3[j] = behind(spread[3], 4, 1)

    chunked(blocks, 4, unpack)

    def is_even3(j):
        return ((parity3 + j) & 1) == 0

    def weights3(at):
        for i in range(4):
            j = at + i
            weight = fx3[j + 1] + fx3[j] + fy3[j, body3] + fy3[j, down3] + fz3[j] + fzl3[j]
            inverse = 1.0 / (64.0 + weight)
            inv3[j] = inverse
            e3[j + 1] = edge3
            e3[j + 1, body3] = jnp.where(is_even3(j), s3[j] * inverse, 0.0)

    chunked(blocks, 4, weights3)

    def neigh3(j):
        here = e3[j + 1, body3]
        sums = fx3[j + 1] * e3[j + 2, body3] + fx3[j] * e3[j, body3]
        sums = sums + fy3[j, body3] * e3[j + 1, up3] + fy3[j, down3] * e3[j + 1, down3]
        return here, sums + fz3[j] * ahead(here, 4, 1) + fzl3[j] * behind(here, 4, 1)

    def update3(at, count, even):
        fresh = []
        for i in range(count):
            j = at + i
            here, sums = neigh3(j)
            value = (s3[j] + sums) * inv3[j]
            where = is_even3(j)
            fresh.append(jnp.where(where, value, here) if even else jnp.where(where, here, value))
        for i in range(count):
            e3[at + i + 1, body3] = fresh[i]

    chunked(blocks, 8, lambda at: update3(at, 8, False))

    def restrict3(at):
        for i in range(0, 4, 2):
            j = at + i
            parts = []
            for k in (j, j + 1):
                _, sums = neigh3(k)
                parts.append(jnp.where(is_even3(k), sums, 0.0))
            pair3[i, :quarter] = parts[0] + parts[1]
            pair3[i + 1, :quarter] = fz3[j] + fz3[j + 1]
        for i in range(0, 4, 2):
            j = at + i
            out = (at + i) // 2
            small[0, out] = with_partner(even_row_sum(pair3.at[i], PAD), 4, 1)
            fxs = fx3[j + 2, pl.ds(0, PAD, 2), :] + fx3[j + 2, pl.ds(1, PAD, 2), :]
            small[1, out] = with_partner(fxs, 4, 1)
            fys = fy3[j, pl.ds(PAD + 1, PAD, 2), :] + fy3[j + 1, pl.ds(PAD + 1, PAD, 2), :]
            small[2, out] = with_partner(fys, 4, 1)
            fzs = even_row_sum(pair3.at[i + 1], PAD)
            odd = (lanes_of((PAD, lanes)) & 4) != 0
            small[3, out] = with_partner(jnp.where(odd, fzs, 0.0), 4, 1)

    chunked(blocks, 4, restrict3)

    small[0] = small_cycle(512.0, small[0], (small[1], small[2], small[3]), 1, 8, 2)

    def prolong3(at):
        for i in range(4):
            j = at + i
            fix = small[0, j // 2]
            pair3[i, pl.ds(0, PAD, 2), :] = fix
            pair3[i, pl.ds(1, PAD, 2), :] = fix
        for i in range(4):
            j = at + i
            e3[j + 1, body3] = e3[j + 1, body3] + pair3[i, :quarter]

    chunked(blocks, 4, prolong3)
    chunked(blocks, 8, lambda at: update3(at, 8, True))
    chunked(blocks, 8, lambda at: update3(at, 8, False))

    wide, narrow = lanes_of((lanes, lanes)), rows_of((lanes, lanes))
    take = jnp.where(narrow == 4 * wide, 1.0, 0.0)
    block = jnp.dot(
        e3[owner + 1, body3], take, precision=lax.Precision.HIGHEST, preferred_element_type=jnp.float32
    )
    owned[0] = block[:, : lanes // 4]

    first_of_two, even2 = parities2(half, lanes)
    body2 = pl.ds(PAD, half)
    edge = jnp.zeros((PAD, lanes), jnp.float32)
    left = gathered[jnp.maximum(position - 1, 0), 1]
    right = gathered[jnp.minimum(position + 1, last), 1]
    into_both_rows(pair3.at[0], left)
    into_both_rows(pair3.at[1], right)
    left, right = pair3[0], pair3[1]
    before = (
        left, jnp.where(first_of_two, left, e2_in[0]), e2_in[1], jnp.where(first_of_two, e2_in[2], right), right
    )
    for k in range(5):
        third = jnp.clip(position + k - 1, 1, blocks)
        into_both_rows(pair3.at[k % 4], e3[third, body3])
        e2[k, :PAD] = edge
        e2[k, PAD + half:] = edge
        e2[k, body2] = before[k] + pair3[k % 4]
    for j in range(3):
        fzl2[j] = behind(fz2[j], 2, 1)
    for even in (True, False):
        fresh = []
        for j, sums in enumerate(neigh2(e2, fx2, fxl2, fy2, fz2, fzl2, first_of_two, (0, 1, 2))):
            value, here = (s2[j] + sums) * inv2[j], e2[j + 1, body2]
            fresh.append(jnp.where(even2, value, here) if even else jnp.where(even2, here, value))
        for j in range(3):
            e2[j + 1, body2] = fresh[j]

    body1, up1, down1 = pl.ds(PAD, height), pl.ds(PAD + 1, height), pl.ds(PAD - 1, height)
    rows, lane = rows_of((height, lanes)), lanes_of((height, lanes))
    even_sum = ((rows + lane) & 1) == 0
    count = e1.shape[0]
    borders = by_side(across_in[4], within_in[4])
    for w in range(0, count, 2):
        coarse_layer = w // 2 - 1
        packed = e2[2 + coarse_layer // 2, body2]
        if coarse_layer % 2 == 0:
            plain = jnp.where(first_of_two, packed, behind(packed, 1, 1))
        else:
            plain = jnp.where(first_of_two, ahead(packed, 1, 1), packed)
        into_both_rows(cor.at[0], plain)
        fix = cor[0]
        for v in (w, w + 1):
            e1[v, :PAD] = edge
            e1[v, PAD + height:] = edge
            if v in (0, count - 1):
                into_both_rows(cor.at[1], borders[0 if v == 0 else 1])
                e1[v, body1] = cor[1] + fix
            else:
                e1[v, body1] = field[v] + fix

    def smoothed1(w, even):
        here = e1[w, body1]
        face = fz_in[w]
        sums = fx_in[w] * e1[w + 1, body1] + fx_in[w - 1] * e1[w - 1, body1]
        sums = sums + fy_in[w, body1] * e1[w, up1] + fy_in[w, down1] * e1[w, down1]
        sums = sums + face * ahead(here, 1, 1) + behind(face, 1, 1) * behind(here, 1, 1)
        value = (source[w] + sums) * inv_in[w]
        keep = even_sum if (w + even) % 2 == 0 else ~even_sum
        return jnp.where(keep, here, value)

    for w in range(1, count - 1):
        e1[w, body1] = smoothed1(w, 1)
    for w in range(2, count - 2):
        solved[w - 2] = smoothed1(w, 0)


def f32(*shape):
    return jax.ShapeDtypeStruct(shape, jnp.float32)


def vmem(*shape):
    return pltpu.VMEM(shape, jnp.float32)


def call(kernel, outs, scratch, scalars, operands, space=pltpu.VMEM):
    def size(shape):
        count = 4
        for extent in shape:
            count *= extent
        return count

    asked = 8 * 2**20 + sum(size(s.shape) for s in scratch) + sum(size(o.shape) for o in outs)
    asked += sum(size(o.shape) for o in operands)
    return pl.pallas_call(
        kernel,
        out_shape=tuple(outs),
        in_specs=[pl.BlockSpec(memory_space=pltpu.SMEM)] * len(scalars)
        + [pl.BlockSpec(memory_space=space)] * len(operands),
        out_specs=tuple([pl.BlockSpec(memory_space=pltpu.VMEM)] * len(outs)),
        scratch_shapes=scratch,
        compiler_params=pltpu.CompilerParams(vmem_limit_bytes=asked),
    )(*scalars, *operands)


def on_device(iterate, source, phase_field, block_owner):
    layers, height, depth = iterate.shape
    half, quarter = height // 2, height // 4
    blocks = lax.axis_size("gx")
    window = layers + 4
    padded, padded2, padded3 = height + 2 * PAD, half + 2 * PAD, quarter + 2 * PAD
    inputs = jnp.concatenate([iterate, source, phase_field], 0)
    sent = call(edge_kernel, [f32(4 * height + half, depth)] * 2, [], (), (inputs,))
    plain = f32(window, height, depth)
    across, within, fx2, *fine = call(
        fine_down_kernel,
        [f32(5, half, depth)] * 2
        + [f32(2, half, depth), plain, plain, plain, f32(window, padded, depth), plain, plain],
        [
            vmem(window, padded, depth), vmem(window, padded, depth), vmem(window, height, depth),
            vmem(layers, height, depth), vmem(2, height, depth),
        ],
        (), (inputs, *swapped(*sent)),
    )
    halos = swapped(across, within)
    plain = f32(3, half, depth)
    slots, *middle = call(
        middle_down_kernel,
        [f32(blocks, 2, quarter, depth), plain, plain, plain, plain, f32(3, padded2, depth), plain, plain],
        [vmem(5, padded2, depth), vmem(3, half, depth), vmem(2, half, depth)],
        (), (across, fx2, *halos),
    )
    gathered = lax.all_to_all(slots, "gx", 0, 0, tiled=True)
    solved, owned = call(
        coarse_kernel,
        [f32(layers, height, depth), f32(1, quarter, depth // 4)],
        [
            vmem(blocks, quarter, depth), vmem(blocks + 1, quarter, depth), vmem(blocks, padded3, depth),
            vmem(blocks, quarter, depth), vmem(blocks, quarter, depth), vmem(blocks, quarter, depth),
            vmem(blocks + 2, padded3, depth), vmem(4, half, depth), vmem(4, blocks // 2, PAD, depth),
            vmem(5, padded2, depth), vmem(3, half, depth), vmem(window, padded, depth), vmem(2, height, depth),
        ],
        (block_owner,), (gathered, *middle, *fine, *halos),
    )
    return solved, owned


def solution(mesh):
    split = P(("groups", "gx"), None, None)
    return jax.shard_map(
        on_device,
        mesh=mesh,
        in_specs=(split, split, split, P("groups")),
        out_specs=(split, split),
        check_vma=False,
    )
```

```python
import jax
import jax.numpy as jnp
from jax import lax
from jax.experimental import pallas as pl
from jax.experimental.pallas import tpu as pltpu
from jax.sharding import PartitionSpec as P

STIFFNESS = 100.0
EPSILON = 0.01
COARSE_SWEEPS = 4
PAD = 8


def swapped(across, within):
    chips = [(i, i + 1 if i % 2 else i - 1) for i in range(1, lax.axis_size("gx") - 1)]
    return lax.ppermute(across, "gx", chips), within_chip(within)


def within_chip(block):
    return lax.ppermute(block, "gx", [(i, i ^ 1) for i in range(lax.axis_size("gx"))])


def by_side(across, within):
    on_left = lax.axis_index("gx") % 2 == 0
    return jnp.where(on_left, across, within), jnp.where(on_left, within, across)


def store_by_side(across, within, pieces):
    on_left = lax.axis_index("gx") % 2 == 0

    @pl.when(on_left)
    def _():
        for index, left, right in pieces:
            across[index] = left
            within[index] = right

    @pl.when(jnp.logical_not(on_left))
    def _():
        for index, left, right in pieces:
            across[index] = right
            within[index] = left


def lanes_of(shape):
    return lax.broadcasted_iota(jnp.int32, shape, len(shape) - 1)


def rows_of(shape):
    return lax.broadcasted_iota(jnp.int32, shape, len(shape) - 2)


def ahead(values, step, axis):
    return pltpu.roll(values, values.shape[axis] - step, axis)


def behind(values, step, axis):
    return pltpu.roll(values, step, axis)


def with_partner(values, step, axis):
    index = lax.broadcasted_iota(jnp.int32, values.shape, axis)
    partner = jnp.where((index & step) == 0, ahead(values, step, axis), behind(values, step, axis))
    return values + partner


def even_row_sum(scratch, rows):
    return scratch[pl.ds(0, rows, 2), :] + scratch[pl.ds(1, rows, 2), :]


def three_parts(ref):
    third = ref.shape[0] // 3
    return [ref.at[pl.ds(k * third, third)] for k in range(3)]


def edge_kernel(inputs, across, within):
    iterate, source, phase = three_parts(inputs)
    layers, height, depth = iterate.shape
    row, lane = rows_of((height, depth)), lanes_of((height, depth))
    even_sum = ((row + lane) & 1) == 0
    odd_lane = (lanes_of((height // 2, depth)) & 1) != 0
    cell = []
    for w in range(layers):
        value = phase[w]
        cell.append(STIFFNESS * (value * value + EPSILON))
    sides = []
    for near, step in ((0, 1), (layers - 1, -1)):
        inner, far = near + step, near + 2 * step
        here, e = cell[inner], iterate[inner]
        face_near, face_far = 0.5 * (here + cell[near]), 0.5 * (here + cell[far])
        fy = jnp.where(row < height - 1, 0.5 * (here + ahead(here, 1, 0)), 0.0)
        fz = jnp.where(lane < depth - 1, 0.5 * (here + ahead(here, 1, 1)), 0.0)
        fyl, fzl = behind(fy, 1, 0), behind(fz, 1, 1)
        total = face_near * iterate[near] + face_far * iterate[far]
        total = total + fy * ahead(e, 1, 0) + fyl * behind(e, 1, 0)
        total = total + fz * ahead(e, 1, 1) + fzl * behind(e, 1, 1)
        weight = 1.0 + (face_near + face_far + fy + fyl + fz + fzl)
        even = even_sum if inner % 2 == 0 else ~even_sum
        border = odd_cells(iterate.at[near], height // 2, odd_lane if near % 2 == 0 else ~odd_lane)
        updated = jnp.where(even, (source[inner] + total) / weight, e)
        sides.append((cell[near], here, source[near], updated, border))
    places = [pl.ds(k * height, height) for k in range(4)] + [pl.ds(4 * height, height // 2)]
    store_by_side(across, within, list(zip(places, *sides)))


def odd_cells(ref, rows, first):
    return jnp.where(first, ref[pl.ds(0, rows, 2), :], ref[pl.ds(1, rows, 2), :])


def into_both_rows(ref, values):
    rows = values.shape[0]
    ref[pl.ds(0, rows, 2), :] = values
    ref[pl.ds(1, rows, 2), :] = values


def fine_down_kernel(
    owner_of, inputs, across_in, within_in,
    across, within, fx2_out, field_out, source_out, fx, fy, fz, inv,
    cell, e, fzl, held, pair,
):
    iterate, source, phase = three_parts(inputs)
    layers, height, depth = iterate.shape
    window = layers + 4
    position, last = lax.axis_index("gx"), lax.axis_size("gx") - 1
    body = pl.ds(PAD, height)
    up, down = pl.ds(PAD + 1, height), pl.ds(PAD - 1, height)
    row, lane = rows_of((height, depth)), lanes_of((height, depth))
    even_sum = ((row + lane) & 1) == 0
    half = height // 2

    def part(ref, k):
        return ref[k * height:(k + 1) * height]

    edge = jnp.zeros((PAD, depth), jnp.float32)
    for w in range(window):
        for padded in (e, fy):
            padded[w, :PAD] = edge
            padded[w, PAD + height:] = edge
        cell[w, PAD + height:] = edge
    halos = [by_side(part(across_in, k), part(within_in, k)) for k in range(4)]
    borders = by_side(across_in[4 * height:], within_in[4 * height:])
    for side, outer, inner in ((0, 0, 1), (1, window - 1, window - 2)):
        cell[inner, body] = halos[0][side]
        cell[outer, body] = halos[1][side]
        source_out[inner] = halos[2][side]
        e[outer, body] = halos[3][side]
        into_both_rows(pair.at[side], borders[side])
        e[inner, body] = pair[side]
    for w in range(layers):
        value = phase[w]
        cell[w + 2, body] = STIFFNESS * (value * value + EPSILON)
        e[w + 2, body] = iterate[w]
        source_out[w + 2] = source[w]
    for w in range(window):
        here = cell[w, body]
        if w < window - 1:
            face = 0.5 * (here + cell[w + 1, body])
            if w == 1:
                face = jnp.where(position > 0, face, 0.0)
            if w == window - 3:
                face = jnp.where(position < last, face, 0.0)
            fx[w] = face
        if 0 < w < window - 1:
            fy[w, body] = jnp.where(row < height - 1, 0.5 * (here + cell[w, up]), 0.0)
            face = jnp.where(lane < depth - 1, 0.5 * (here + ahead(here, 1, 1)), 0.0)
            fz[w] = face
            fzl[w] = behind(face, 1, 1)
    for w in range(1, window - 1):
        weight = fx[w] + fx[w - 1] + fy[w, body] + fy[w, down] + fz[w] + fzl[w]
        inv[w] = 1.0 / (1.0 + weight)

    def neigh(w):
        here = e[w, body]
        total = fx[w] * e[w + 1, body] + fx[w - 1] * e[w - 1, body]
        total = total + fy[w, body] * e[w, up] + fy[w, down] * e[w, down]
        return total + fz[w] * ahead(here, 1, 1) + fzl[w] * behind(here, 1, 1)

    def mask(w, odd):
        return even_sum if (w + odd) % 2 == 0 else ~even_sum

    for w in range(1, window - 1):
        total = source_out[w] + neigh(w)
        if 2 <= w < layers + 2:
            held[w - 2] = total
        e[w, body] = jnp.where(mask(w, 0), total * inv[w], e[w, body])
    for w in range(1, window - 1):
        total = (source_out[w] + neigh(w)) * inv[w]
        e[w, body] = jnp.where(mask(w, 1), total, e[w, body])
        field_out[w] = e[w, body]

    lane = lanes_of((half, depth))
    first_of_two = (lane & 1) == 0

    def residual(w):
        return jnp.where(mask(w, 0), source_out[w] + neigh(w) - held[w - 2], 0.0)

    def slabs(make, reduce_rows, reduce_lanes, start=2):
        found = []
        for t in range(2):
            pair[t] = make(start + 2 * t)
            found.append(reduce_lanes(reduce_rows(pair.at[t])))
        return jnp.where(first_of_two, found[0], found[1])

    def both_rows(scratch):
        return even_row_sum(scratch, half)

    def odd_rows(scratch):
        return scratch[pl.ds(1, half, 2), :]

    def both_lanes(values):
        return with_partner(values, 1, 1)

    def odd_lanes(values):
        return jnp.where(first_of_two, ahead(values, 1, 1), values)

    coarse_source = slabs(lambda w: residual(w) + residual(w + 1), both_rows, both_lanes)
    coarse_fy = slabs(lambda w: fy[w, body] + fy[w + 1, body], odd_rows, both_lanes)
    coarse_fz = slabs(lambda w: fz[w] + fz[w + 1], both_rows, odd_lanes)
    left_fx = slabs(lambda w: fx[w + 1], both_rows, both_lanes)
    right_fx = slabs(lambda w: fx[w - 1], both_rows, both_lanes)
    fx2_out[0], fx2_out[1] = left_fx, right_fx
    borders = []
    for t, w in enumerate((3, window - 4)):
        pair[t] = e[w, body]
        borders.append(odd_cells(pair.at[t], half, ~first_of_two if w % 2 == 0 else first_of_two))
    pieces = [(0, coarse_source), (2, coarse_fy), (3, coarse_fz)]
    pieces = [(k, value, value) for k, value in pieces]
    store_by_side(across, within, pieces + [(1, left_fx, right_fx), (4, *borders)])


def neigh2(e2, fx2, fxl2, fy2, fz2, fzl2, first_of_two, tiles):
    half = fx2.shape[1]
    body, up, down = pl.ds(PAD, half), pl.ds(PAD + 1, half), pl.ds(PAD - 1, half)
    needed = range(tiles[0], tiles[-1] + 3)
    here = {j: e2[j, body] for j in needed}
    after = {j: ahead(here[j], 1, 1) for j in needed}
    before = {j: behind(here[j], 1, 1) for j in needed}
    found = []
    for j in tiles:
        k = j + 1
        upper = jnp.where(first_of_two, after[k], before[k + 1])
        lower = jnp.where(first_of_two, after[k - 1], before[k])
        sums = fx2[j] * upper + fxl2[j] * lower
        sums = sums + fy2[j, body] * e2[k, up] + fy2[j, down] * e2[k, down]
        sums = sums + fz2[j] * ahead(here[k], 2, 1) + fzl2[j] * behind(here[k], 2, 1)
        found.append(sums)
    return found


def parities2(half, lanes):
    row, lane = rows_of((half, lanes)), lanes_of((half, lanes))
    return (lane & 1) == 0, ((row + (lane & 1) + (lane >> 1)) & 1) == 0


def group(values):
    return with_partner(with_partner(values, 1, 1), 2, 1)


def middle_down_kernel(
    own, own_fx, across_in, within_in,
    slots, e2_out, s2, fx2, fxl2, fy2, fz2, inv2,
    e2, fzl2, pair,
):
    _, half, lanes = own.shape
    quarter = half // 2
    position = lax.axis_index("gx")
    first_of_two, even2 = parities2(half, lanes)
    body, down = pl.ds(PAD, half), pl.ds(PAD - 1, half)
    edge = jnp.zeros((PAD, lanes), jnp.float32)
    for j in range(5):
        e2[j] = jnp.zeros((half + 2 * PAD, lanes), jnp.float32)
    def three(k):
        left, right = by_side(across_in[k], within_in[k])
        return left, own[k], right

    for j, (source, fy, fz) in enumerate(zip(three(0), three(2), three(3))):
        s2[j] = source
        fy2[j, :PAD] = edge
        fy2[j, body] = fy
        fy2[j, PAD + half:] = edge
        fz2[j] = fz
        fzl2[j] = behind(fz, 2, 1)
    left_fx, _, right_fx = three(1)
    fx2[0] = jnp.where(first_of_two, ahead(left_fx, 1, 1), behind(own_fx[1], 1, 1))
    fx2[1] = own_fx[0]
    fx2[2] = right_fx
    fxl2[0] = left_fx
    fxl2[1] = own_fx[1]
    fxl2[2] = jnp.where(first_of_two, ahead(own_fx[0], 1, 1), behind(right_fx, 1, 1))
    for j in range(3):
        weight = fx2[j] + fxl2[j] + fy2[j, body] + fy2[j, down] + fz2[j] + fzl2[j]
        inverse = 1.0 / (8.0 + weight)
        inv2[j] = inverse
        e2[j + 1, body] = jnp.where(even2, s2[j] * inverse, 0.0)

    def neigh(tiles):
        return neigh2(e2, fx2, fxl2, fy2, fz2, fzl2, first_of_two, tiles)

    fresh = [
        jnp.where(even2, e2[j + 1, body], (s2[j] + sums) * inv2[j]) for j, sums in enumerate(neigh((0, 1, 2)))
    ]
    for j in range(3):
        e2[j + 1, body] = fresh[j]
        e2_out[j] = fresh[j]
    pair[0] = jnp.where(even2, neigh((1,))[0], 0.0)
    lane = lanes_of((quarter, lanes))
    odd_layer, odd_depth, item = (lane & 1) != 0, (lane & 2) != 0, lane & 3
    source = group(even_row_sum(pair.at[0], quarter))
    fx = group(jnp.where(odd_layer, even_row_sum(fx2.at[1], quarter), 0.0))
    fy = group(fy2[1, pl.ds(PAD + 1, quarter, 2), :])
    fz = group(jnp.where(odd_depth, even_row_sum(fz2.at[1], quarter), 0.0))
    tile = jnp.where(item == 0, source, jnp.where(item == 1, fx, jnp.where(item == 2, fy, fz)))
    first = (((lane & 1) + (lane >> 1)) & 1) != 0
    pair[0] = jnp.where(first_of_two, fresh[2], fresh[1])
    pair[1] = jnp.where(first_of_two, fresh[1], fresh[0])
    for_left = odd_cells(pair.at[0], quarter, first)
    for_right = odd_cells(pair.at[1], quarter, first)
    for c in range(slots.shape[0]):
        slots[c, 0] = tile
        slots[c, 1] = jnp.where(position < 2 * c + 1 - position % 2, for_right, for_left)


class Level:
    def __init__(self, mass, source, faces, row_step, lane_step):
        self.source, self.row_step, self.lane_step = source, row_step, lane_step
        self.fx, self.fy, self.fz = faces
        self.layers, rows, lanes = source.shape
        nothing = jnp.zeros_like(source[:1])
        self.nothing = nothing
        self.fxl = jnp.concatenate([nothing, self.fx[:-1]], 0)
        self.fyl = behind(self.fy, row_step, 1)
        self.fzl = behind(self.fz, lane_step, 2)
        weight = self.fx + self.fxl + self.fy + self.fyl + self.fz + self.fzl
        self.inv = 1.0 / (mass + weight)
        shape = source.shape
        total = lax.broadcasted_iota(jnp.int32, shape, 0)
        total = total + rows_of(shape) // row_step + lanes_of(shape) // lane_step
        self.even = (total & 1) == 0

    def neigh(self, e):
        upper = jnp.concatenate([e[1:], self.nothing], 0)
        lower = jnp.concatenate([self.nothing, e[:-1]], 0)
        total = self.fx * upper + self.fxl * lower
        total = total + self.fy * ahead(e, self.row_step, 1) + self.fyl * behind(e, self.row_step, 1)
        return total + self.fz * ahead(e, self.lane_step, 2) + self.fzl * behind(e, self.lane_step, 2)

    def start(self):
        e = jnp.where(self.even, self.source * self.inv, 0.0)
        return self.odd_update(e)

    def even_update(self, e):
        return jnp.where(self.even, (self.source + self.neigh(e)) * self.inv, e)

    def odd_update(self, e):
        return jnp.where(self.even, e, (self.source + self.neigh(e)) * self.inv)

    def residual(self, e):
        return jnp.where(self.even, self.neigh(e), 0.0)

    def pairs(self, values):
        halves = values.reshape(self.layers // 2, 2, *values.shape[1:])
        return halves[:, 0] + halves[:, 1]

    def coarse_faces(self):
        row_bit = (rows_of(self.fx.shape) & self.row_step) != 0
        lane_bit = (lanes_of(self.fx.shape) & self.lane_step) != 0
        odd_layers = self.fx.reshape(self.layers // 2, 2, *self.fx.shape[1:])[:, 1]
        fx = self.in_plane(odd_layers)
        fy = self.in_plane(self.pairs(jnp.where(row_bit, self.fy, 0.0)))
        fz = self.in_plane(self.pairs(jnp.where(lane_bit, self.fz, 0.0)))
        return fx, fy, fz

    def in_plane(self, values):
        return with_partner(with_partner(values, self.row_step, 1), self.lane_step, 2)

    def restricted(self, values):
        return self.in_plane(self.pairs(values))


def doubled_layers(values):
    layers = values.shape[0]
    both = jnp.concatenate([values[:, None], values[:, None]], 1)
    return both.reshape(2 * layers, *values.shape[1:])


def small_cycle(mass, source, faces, row_step, lane_step, deeper):
    level = Level(mass, source, faces, row_step, lane_step)
    e = level.start()
    if deeper == 0:
        for turn in range(COARSE_SWEEPS - 1):
            e = level.odd_update(level.even_update(e))
        return e
    fix = small_cycle(
        8.0 * mass, level.restricted(level.residual(e)), level.coarse_faces(),
        2 * row_step, 2 * lane_step, deeper - 1,
    )
    e = e + doubled_layers(fix)
    return level.odd_update(level.even_update(e))


def chunked(count, size, body):
    size = min(size, count)
    if count == size:
        body(0)
    else:
        lax.fori_loop(0, count // size, lambda i, c: (body(i * size), c)[1], 0)


def coarse_kernel(
    owner_of, same_cores, other_cores, e2_in, s2, fx2, fxl2, fy2, fz2, inv2,
    field, source, fx_in, fy_in, fz_in, inv_in, across_in, within_in,
    solved, owned,
    s3, fx3, fy3, fz3, fzl3, inv3, e3, pair3, small, e2, fzl2, e1, cor,
):
    chips, _, quarter, lanes = same_cores.shape
    blocks = 2 * chips
    half, height = 2 * quarter, 4 * quarter
    position, last = lax.axis_index("gx"), blocks - 1
    owner = owner_of[position]

    body3, up3, down3 = pl.ds(PAD, quarter), pl.ds(PAD + 1, quarter), pl.ds(PAD - 1, quarter)
    row, lane = rows_of((quarter, lanes)), lanes_of((quarter, lanes))
    parity3 = row + (lane >> 2)
    item = lane & 3
    edge3 = jnp.zeros((quarter + 2 * PAD, lanes), jnp.float32)
    for j in (0, blocks + 1):
        e3[j] = edge3
    fx3[0] = jnp.zeros((quarter, lanes), jnp.float32)

    def unpack(at):
        tiles = []
        for i in range(0, 4, 2):
            chip = (at + i) // 2
            tiles.extend(by_side(same_cores[chip, 0], other_cores[chip, 0]))
        for i, tile in enumerate(tiles):
            j = at + i
            moved = {0: tile}
            for step in (1, 2, 3):
                moved[step] = ahead(tile, step, 1)
                moved[-step] = behind(tile, step, 1)
            spread = []
            for k in range(4):
                value = moved[k]
                for slot in (1, 2, 3):
                    value = jnp.where(item == slot, moved[k - slot], value)
                spread.append(value)
            s3[j] = spread[0]
            fx3[j + 1] = spread[1]
            fy3[j] = edge3
            fy3[j, body3] = spread[2]
            fz3[j] = spread[3]
            fzl3[j] = behind(spread[3], 4, 1)

    chunked(blocks, 4, unpack)

    def is_even3(j):
        return ((parity3 + j) & 1) == 0

    def weights3(at):
        for i in range(4):
            j = at + i
            weight = fx3[j + 1] + fx3[j] + fy3[j, body3] + fy3[j, down3] + fz3[j] + fzl3[j]
            inverse = 1.0 / (64.0 + weight)
            inv3[j] = inverse
            e3[j + 1] = edge3
            e3[j + 1, body3] = jnp.where(is_even3(j), s3[j] * inverse, 0.0)

    chunked(blocks, 4, weights3)

    def neigh3(j):
        here = e3[j + 1, body3]
        sums = fx3[j + 1] * e3[j + 2, body3] + fx3[j] * e3[j, body3]
        sums = sums + fy3[j, body3] * e3[j + 1, up3] + fy3[j, down3] * e3[j + 1, down3]
        return here, sums + fz3[j] * ahead(here, 4, 1) + fzl3[j] * behind(here, 4, 1)

    def update3(at, count, even):
        fresh = []
        for i in range(count):
            j = at + i
            here, sums = neigh3(j)
            value = (s3[j] + sums) * inv3[j]
            where = is_even3(j)
            fresh.append(jnp.where(where, value, here) if even else jnp.where(where, here, value))
        for i in range(count):
            e3[at + i + 1, body3] = fresh[i]

    chunked(blocks, 8, lambda at: update3(at, 8, False))

    def restrict3(at):
        for i in range(0, 4, 2):
            j = at + i
            parts = []
            for k in (j, j + 1):
                _, sums = neigh3(k)
                parts.append(jnp.where(is_even3(k), sums, 0.0))
            pair3[i, :quarter] = parts[0] + parts[1]
            pair3[i + 1, :quarter] = fz3[j] + fz3[j + 1]
        for i in range(0, 4, 2):
            j = at + i
            out = (at + i) // 2
            small[0, out] = with_partner(even_row_sum(pair3.at[i], PAD), 4, 1)
            fxs = fx3[j + 2, pl.ds(0, PAD, 2), :] + fx3[j + 2, pl.ds(1, PAD, 2), :]
            small[1, out] = with_partner(fxs, 4, 1)
            fys = fy3[j, pl.ds(PAD + 1, PAD, 2), :] + fy3[j + 1, pl.ds(PAD + 1, PAD, 2), :]
            small[2, out] = with_partner(fys, 4, 1)
            fzs = even_row_sum(pair3.at[i + 1], PAD)
            odd = (lanes_of((PAD, lanes)) & 4) != 0
            small[3, out] = with_partner(jnp.where(odd, fzs, 0.0), 4, 1)

    chunked(blocks, 4, restrict3)

    small[0] = small_cycle(512.0, small[0], (small[1], small[2], small[3]), 1, 8, 2)

    def prolong3(at):
        for i in range(4):
            j = at + i
            fix = small[0, j // 2]
            pair3[i, pl.ds(0, PAD, 2), :] = fix
            pair3[i, pl.ds(1, PAD, 2), :] = fix
        for i in range(4):
            j = at + i
            e3[j + 1, body3] = e3[j + 1, body3] + pair3[i, :quarter]

    chunked(blocks, 4, prolong3)
    chunked(blocks, 8, lambda at: update3(at, 8, True))
    chunked(blocks, 8, lambda at: update3(at, 8, False))

    wide, narrow = lanes_of((lanes, lanes)), rows_of((lanes, lanes))
    take = jnp.where(narrow == 4 * wide, 1.0, 0.0)
    block = jnp.dot(
        e3[owner + 1, body3], take, precision=lax.Precision.HIGHEST, preferred_element_type=jnp.float32
    )
    owned[0] = block[:, : lanes // 4]

    first_of_two, even2 = parities2(half, lanes)
    body2 = pl.ds(PAD, half)
    edge = jnp.zeros((PAD, lanes), jnp.float32)
    left = other_cores[jnp.maximum(position - 1, 0) // 2, 1]
    right = other_cores[jnp.minimum(position + 1, last) // 2, 1]
    into_both_rows(pair3.at[0], left)
    into_both_rows(pair3.at[1], right)
    left, right = pair3[0], pair3[1]
    before = (
        left, jnp.where(first_of_two, left, e2_in[0]), e2_in[1], jnp.where(first_of_two, e2_in[2], right), right
    )
    for k in range(5):
        third = jnp.clip(position + k - 1, 1, blocks)
        into_both_rows(pair3.at[k % 4], e3[third, body3])
        e2[k, :PAD] = edge
        e2[k, PAD + half:] = edge
        e2[k, body2] = before[k] + pair3[k % 4]
    for j in range(3):
        fzl2[j] = behind(fz2[j], 2, 1)
    for even in (True, False):
        fresh = []
        for j, sums in enumerate(neigh2(e2, fx2, fxl2, fy2, fz2, fzl2, first_of_two, (0, 1, 2))):
            value, here = (s2[j] + sums) * inv2[j], e2[j + 1, body2]
            fresh.append(jnp.where(even2, value, here) if even else jnp.where(even2, here, value))
        for j in range(3):
            e2[j + 1, body2] = fresh[j]

    body1, up1, down1 = pl.ds(PAD, height), pl.ds(PAD + 1, height), pl.ds(PAD - 1, height)
    rows, lane = rows_of((height, lanes)), lanes_of((height, lanes))
    even_sum = ((rows + lane) & 1) == 0
    count = e1.shape[0]
    borders = by_side(across_in[4], within_in[4])
    for w in range(0, count, 2):
        coarse_layer = w // 2 - 1
        packed = e2[2 + coarse_layer // 2, body2]
        if coarse_layer % 2 == 0:
            plain = jnp.where(first_of_two, packed, behind(packed, 1, 1))
        else:
            plain = jnp.where(first_of_two, ahead(packed, 1, 1), packed)
        into_both_rows(cor.at[0], plain)
        fix = cor[0]
        for v in (w, w + 1):
            e1[v, :PAD] = edge
            e1[v, PAD + height:] = edge
            if v in (0, count - 1):
                into_both_rows(cor.at[1], borders[0 if v == 0 else 1])
                e1[v, body1] = cor[1] + fix
            else:
                e1[v, body1] = field[v] + fix

    def smoothed1(w, even):
        here = e1[w, body1]
        face = fz_in[w]
        sums = fx_in[w] * e1[w + 1, body1] + fx_in[w - 1] * e1[w - 1, body1]
        sums = sums + fy_in[w, body1] * e1[w, up1] + fy_in[w, down1] * e1[w, down1]
        sums = sums + face * ahead(here, 1, 1) + behind(face, 1, 1) * behind(here, 1, 1)
        value = (source[w] + sums) * inv_in[w]
        keep = even_sum if (w + even) % 2 == 0 else ~even_sum
        return jnp.where(keep, here, value)

    for w in range(1, count - 1):
        e1[w, body1] = smoothed1(w, 1)
    for w in range(2, count - 2):
        solved[w - 2] = smoothed1(w, 0)


def f32(*shape):
    return jax.ShapeDtypeStruct(shape, jnp.float32)


def vmem(*shape):
    return pltpu.VMEM(shape, jnp.float32)


def call(kernel, outs, scratch, scalars, operands, space=pltpu.VMEM):
    def size(shape):
        count = 4
        for extent in shape:
            count *= extent
        return count

    asked = 8 * 2**20 + sum(size(s.shape) for s in scratch) + sum(size(o.shape) for o in outs)
    asked += sum(size(o.shape) for o in operands)
    return pl.pallas_call(
        kernel,
        out_shape=tuple(outs),
        in_specs=[pl.BlockSpec(memory_space=pltpu.SMEM)] * len(scalars)
        + [pl.BlockSpec(memory_space=space)] * len(operands),
        out_specs=tuple([pl.BlockSpec(memory_space=pltpu.VMEM)] * len(outs)),
        scratch_shapes=scratch,
        compiler_params=pltpu.CompilerParams(vmem_limit_bytes=asked),
    )(*scalars, *operands)


def on_device(iterate, source, phase_field, block_owner):
    layers, height, depth = iterate.shape
    half, quarter = height // 2, height // 4
    blocks = lax.axis_size("gx")
    window = layers + 4
    padded, padded2, padded3 = height + 2 * PAD, half + 2 * PAD, quarter + 2 * PAD
    inputs = jnp.concatenate([iterate, source, phase_field], 0)
    sent = call(edge_kernel, [f32(4 * height + half, depth)] * 2, [], (), (inputs,))
    plain = f32(window, height, depth)
    across, within, fx2, *fine = call(
        fine_down_kernel,
        [f32(5, half, depth)] * 2
        + [f32(2, half, depth), plain, plain, plain, f32(window, padded, depth), plain, plain],
        [
            vmem(window, padded, depth), vmem(window, padded, depth), vmem(window, height, depth),
            vmem(layers, height, depth), vmem(2, height, depth),
        ],
        (block_owner,), (inputs, *swapped(*sent)),
    )
    halos = swapped(across, within)
    plain = f32(3, half, depth)
    slots, *middle = call(
        middle_down_kernel,
        [f32(blocks // 2, 2, quarter, depth), plain, plain, plain, plain, f32(3, padded2, depth), plain, plain],
        [vmem(5, padded2, depth), vmem(3, half, depth), vmem(2, half, depth)],
        (), (across, fx2, *halos),
    )
    kinds = [list(range(core, blocks, 2)) for core in range(2)]
    same_cores = lax.all_to_all(slots, "gx", 0, 0, axis_index_groups=kinds, tiled=True)
    other_cores = within_chip(same_cores)
    solved, owned = call(
        coarse_kernel,
        [f32(layers, height, depth), f32(1, quarter, depth // 4)],
        [
            vmem(blocks, quarter, depth), vmem(blocks + 1, quarter, depth), vmem(blocks, padded3, depth),
            vmem(blocks, quarter, depth), vmem(blocks, quarter, depth), vmem(blocks, quarter, depth),
            vmem(blocks + 2, padded3, depth), vmem(4, half, depth), vmem(4, blocks // 2, PAD, depth),
            vmem(5, padded2, depth), vmem(3, half, depth), vmem(window, padded, depth), vmem(2, height, depth),
        ],
        (block_owner,), (same_cores, other_cores, *middle, *fine, *halos),
    )
    return solved, owned


def solution(mesh):
    split = P(("groups", "gx"), None, None)
    return jax.shard_map(
        on_device,
        mesh=mesh,
        in_specs=(split, split, split, P("groups")),
        out_specs=(split, split),
        check_vma=False,
    )
```

```python
import jax
import jax.numpy as jnp
from jax import lax
from jax.experimental import pallas as pl
from jax.experimental.pallas import tpu as pltpu
from jax.sharding import PartitionSpec as P

STIFFNESS = 100.0
EPSILON = 0.01
COARSE_SWEEPS = 4
PAD = 8


def swapped(across, within):
    chips = [(i, i + 1 if i % 2 else i - 1) for i in range(1, lax.axis_size("gx") - 1)]
    return lax.ppermute(across, "gx", chips), within_chip(within)


def within_chip(block):
    return lax.ppermute(block, "gx", [(i, i ^ 1) for i in range(lax.axis_size("gx"))])


def by_side(across, within):
    on_left = lax.axis_index("gx") % 2 == 0
    return jnp.where(on_left, across, within), jnp.where(on_left, within, across)


def store_by_side(across, within, pieces):
    on_left = lax.axis_index("gx") % 2 == 0

    @pl.when(on_left)
    def _():
        for index, left, right in pieces:
            across[index] = left
            within[index] = right

    @pl.when(jnp.logical_not(on_left))
    def _():
        for index, left, right in pieces:
            across[index] = right
            within[index] = left


def lanes_of(shape):
    return lax.broadcasted_iota(jnp.int32, shape, len(shape) - 1)


def rows_of(shape):
    return lax.broadcasted_iota(jnp.int32, shape, len(shape) - 2)


def ahead(values, step, axis):
    return pltpu.roll(values, values.shape[axis] - step, axis)


def behind(values, step, axis):
    return pltpu.roll(values, step, axis)


def with_partner(values, step, axis):
    index = lax.broadcasted_iota(jnp.int32, values.shape, axis)
    partner = jnp.where((index & step) == 0, ahead(values, step, axis), behind(values, step, axis))
    return values + partner


def even_row_sum(scratch, rows):
    return scratch[pl.ds(0, rows, 2), :] + scratch[pl.ds(1, rows, 2), :]


def three_parts(ref):
    third = ref.shape[0] // 3
    return [ref.at[pl.ds(k * third, third)] for k in range(3)]


def edge_kernel(inputs, across, within):
    iterate, source, phase = three_parts(inputs)
    layers, height, depth = iterate.shape
    row, lane = rows_of((height, depth)), lanes_of((height, depth))
    even_sum = ((row + lane) & 1) == 0
    odd_lane = (lanes_of((height // 2, depth)) & 1) != 0
    cell = []
    for w in range(layers):
        value = phase[w]
        cell.append(STIFFNESS * (value * value + EPSILON))
    sides = []
    for near, step in ((0, 1), (layers - 1, -1)):
        inner, far = near + step, near + 2 * step
        here, e = cell[inner], iterate[inner]
        face_near, face_far = 0.5 * (here + cell[near]), 0.5 * (here + cell[far])
        fy = jnp.where(row < height - 1, 0.5 * (here + ahead(here, 1, 0)), 0.0)
        fz = jnp.where(lane < depth - 1, 0.5 * (here + ahead(here, 1, 1)), 0.0)
        fyl, fzl = behind(fy, 1, 0), behind(fz, 1, 1)
        total = face_near * iterate[near] + face_far * iterate[far]
        total = total + fy * ahead(e, 1, 0) + fyl * behind(e, 1, 0)
        total = total + fz * ahead(e, 1, 1) + fzl * behind(e, 1, 1)
        weight = 1.0 + (face_near + face_far + fy + fyl + fz + fzl)
        even = even_sum if inner % 2 == 0 else ~even_sum
        border = odd_cells(iterate.at[near], height // 2, odd_lane if near % 2 == 0 else ~odd_lane)
        updated = jnp.where(even, (source[inner] + total) / weight, e)
        sides.append((cell[near], here, source[near], updated, border))
    places = [pl.ds(k * height, height) for k in range(4)] + [pl.ds(4 * height, height // 2)]
    store_by_side(across, within, list(zip(places, *sides)))


def odd_cells(ref, rows, first):
    return jnp.where(first, ref[pl.ds(0, rows, 2), :], ref[pl.ds(1, rows, 2), :])


def into_both_rows(ref, values):
    rows = values.shape[0]
    ref[pl.ds(0, rows, 2), :] = values
    ref[pl.ds(1, rows, 2), :] = values


def fine_down_kernel(
    owner_of, inputs, across_in, within_in,
    across, within, fx2_out, field_out, source_out, fx, fy, fz, inv,
    cell, e, fzl, held, pair,
):
    iterate, source, phase = three_parts(inputs)
    layers, height, depth = iterate.shape
    window = layers + 4
    position, last = lax.axis_index("gx"), lax.axis_size("gx") - 1
    body = pl.ds(PAD, height)
    up, down = pl.ds(PAD + 1, height), pl.ds(PAD - 1, height)
    row, lane = rows_of((height, depth)), lanes_of((height, depth))
    even_sum = ((row + lane) & 1) == 0
    half = height // 2

    def part(ref, k):
        return ref[k * height:(k + 1) * height]

    edge = jnp.zeros((PAD, depth), jnp.float32)
    for w in range(window):
        for padded in (e, fy):
            padded[w, :PAD] = edge
            padded[w, PAD + height:] = edge
        cell[w, PAD + height:] = edge
    halos = [by_side(part(across_in, k), part(within_in, k)) for k in range(4)]
    borders = by_side(across_in[4 * height:], within_in[4 * height:])
    for side, outer, inner in ((0, 0, 1), (1, window - 1, window - 2)):
        cell[inner, body] = halos[0][side]
        cell[outer, body] = halos[1][side]
        source_out[inner] = halos[2][side]
        e[outer, body] = halos[3][side]
        into_both_rows(pair.at[side], borders[side])
        e[inner, body] = pair[side]
    for w in range(layers):
        value = phase[w]
        cell[w + 2, body] = STIFFNESS * (value * value + EPSILON)
        e[w + 2, body] = iterate[w]
        source_out[w + 2] = source[w]
    for w in range(window):
        here = cell[w, body]
        if w < window - 1:
            face = 0.5 * (here + cell[w + 1, body])
            if w == 1:
                face = jnp.where(position > 0, face, 0.0)
            if w == window - 3:
                face = jnp.where(position < last, face, 0.0)
            fx[w] = face
        if 0 < w < window - 1:
            fy[w, body] = jnp.where(row < height - 1, 0.5 * (here + cell[w, up]), 0.0)
            face = jnp.where(lane < depth - 1, 0.5 * (here + ahead(here, 1, 1)), 0.0)
            fz[w] = face
            fzl[w] = behind(face, 1, 1)
    for w in range(1, window - 1):
        weight = fx[w] + fx[w - 1] + fy[w, body] + fy[w, down] + fz[w] + fzl[w]
        inv[w] = 1.0 / (1.0 + weight)

    def neigh(w):
        here = e[w, body]
        total = fx[w] * e[w + 1, body] + fx[w - 1] * e[w - 1, body]
        total = total + fy[w, body] * e[w, up] + fy[w, down] * e[w, down]
        return total + fz[w] * ahead(here, 1, 1) + fzl[w] * behind(here, 1, 1)

    def mask(w, odd):
        return even_sum if (w + odd) % 2 == 0 else ~even_sum

    for w in range(1, window - 1):
        total = source_out[w] + neigh(w)
        if 2 <= w < layers + 2:
            held[w - 2] = total
        e[w, body] = jnp.where(mask(w, 0), total * inv[w], e[w, body])
    for w in range(1, window - 1):
        total = (source_out[w] + neigh(w)) * inv[w]
        e[w, body] = jnp.where(mask(w, 1), total, e[w, body])
        field_out[w] = e[w, body]

    lane = lanes_of((half, depth))
    first_of_two = (lane & 1) == 0

    def residual(w):
        return jnp.where(mask(w, 0), source_out[w] + neigh(w) - held[w - 2], 0.0)

    def slabs(make, reduce_rows, reduce_lanes, start=2):
        found = []
        for t in range(2):
            pair[t] = make(start + 2 * t)
            found.append(reduce_lanes(reduce_rows(pair.at[t])))
        return jnp.where(first_of_two, found[0], found[1])

    def both_rows(scratch):
        return even_row_sum(scratch, half)

    def odd_rows(scratch):
        return scratch[pl.ds(1, half, 2), :]

    def both_lanes(values):
        return with_partner(values, 1, 1)

    def odd_lanes(values):
        return jnp.where(first_of_two, ahead(values, 1, 1), values)

    coarse_source = slabs(lambda w: residual(w) + residual(w + 1), both_rows, both_lanes)
    coarse_fy = slabs(lambda w: fy[w, body] + fy[w + 1, body], odd_rows, both_lanes)
    coarse_fz = slabs(lambda w: fz[w] + fz[w + 1], both_rows, odd_lanes)
    left_fx = slabs(lambda w: fx[w + 1], both_rows, both_lanes)
    right_fx = slabs(lambda w: fx[w - 1], both_rows, both_lanes)
    fx2_out[0], fx2_out[1] = left_fx, right_fx
    borders = []
    for t, w in enumerate((3, window - 4)):
        pair[t] = e[w, body]
        borders.append(odd_cells(pair.at[t], half, ~first_of_two if w % 2 == 0 else first_of_two))
    pieces = [(0, coarse_source), (2, coarse_fy), (3, coarse_fz)]
    pieces = [(k, value, value) for k, value in pieces]
    store_by_side(across, within, pieces + [(1, left_fx, right_fx), (4, *borders)])


def neigh2(e2, fx2, fxl2, fy2, fz2, fzl2, first_of_two, tiles):
    half = fx2.shape[1]
    body, up, down = pl.ds(PAD, half), pl.ds(PAD + 1, half), pl.ds(PAD - 1, half)
    needed = range(tiles[0], tiles[-1] + 3)
    here = {j: e2[j, body] for j in needed}
    after = {j: ahead(here[j], 1, 1) for j in needed}
    before = {j: behind(here[j], 1, 1) for j in needed}
    found = []
    for j in tiles:
        k = j + 1
        upper = jnp.where(first_of_two, after[k], before[k + 1])
        lower = jnp.where(first_of_two, after[k - 1], before[k])
        sums = fx2[j] * upper + fxl2[j] * lower
        sums = sums + fy2[j, body] * e2[k, up] + fy2[j, down] * e2[k, down]
        sums = sums + fz2[j] * ahead(here[k], 2, 1) + fzl2[j] * behind(here[k], 2, 1)
        found.append(sums)
    return found


def parities2(half, lanes):
    row, lane = rows_of((half, lanes)), lanes_of((half, lanes))
    return (lane & 1) == 0, ((row + (lane & 1) + (lane >> 1)) & 1) == 0


def group(values):
    return with_partner(with_partner(values, 1, 1), 2, 1)


def middle_down_kernel(
    own, own_fx, across_in, within_in,
    slots, e2_out, s2, fx2, fxl2, fy2, fz2, inv2,
    e2, fzl2, pair,
):
    _, half, lanes = own.shape
    quarter = half // 2
    position = lax.axis_index("gx")
    first_of_two, even2 = parities2(half, lanes)
    body, down = pl.ds(PAD, half), pl.ds(PAD - 1, half)
    edge = jnp.zeros((PAD, lanes), jnp.float32)
    for j in range(5):
        e2[j] = jnp.zeros((half + 2 * PAD, lanes), jnp.float32)
    def three(k):
        left, right = by_side(across_in[k], within_in[k])
        return left, own[k], right

    for j, (source, fy, fz) in enumerate(zip(three(0), three(2), three(3))):
        s2[j] = source
        fy2[j, :PAD] = edge
        fy2[j, body] = fy
        fy2[j, PAD + half:] = edge
        fz2[j] = fz
        fzl2[j] = behind(fz, 2, 1)
    left_fx, _, right_fx = three(1)
    fx2[0] = jnp.where(first_of_two, ahead(left_fx, 1, 1), behind(own_fx[1], 1, 1))
    fx2[1] = own_fx[0]
    fx2[2] = right_fx
    fxl2[0] = left_fx
    fxl2[1] = own_fx[1]
    fxl2[2] = jnp.where(first_of_two, ahead(own_fx[0], 1, 1), behind(right_fx, 1, 1))
    for j in range(3):
        weight = fx2[j] + fxl2[j] + fy2[j, body] + fy2[j, down] + fz2[j] + fzl2[j]
        inverse = 1.0 / (8.0 + weight)
        inv2[j] = inverse
        e2[j + 1, body] = jnp.where(even2, s2[j] * inverse, 0.0)

    def neigh(tiles):
        return neigh2(e2, fx2, fxl2, fy2, fz2, fzl2, first_of_two, tiles)

    fresh = [
        jnp.where(even2, e2[j + 1, body], (s2[j] + sums) * inv2[j]) for j, sums in enumerate(neigh((0, 1, 2)))
    ]
    for j in range(3):
        e2[j + 1, body] = fresh[j]
        e2_out[j] = fresh[j]
    pair[0] = jnp.where(even2, neigh((1,))[0], 0.0)
    lane = lanes_of((quarter, lanes))
    odd_layer, odd_depth, item = (lane & 1) != 0, (lane & 2) != 0, lane & 3
    source = group(even_row_sum(pair.at[0], quarter))
    fx = group(jnp.where(odd_layer, even_row_sum(fx2.at[1], quarter), 0.0))
    fy = group(fy2[1, pl.ds(PAD + 1, quarter, 2), :])
    fz = group(jnp.where(odd_depth, even_row_sum(fz2.at[1], quarter), 0.0))
    tile = jnp.where(item == 0, source, jnp.where(item == 1, fx, jnp.where(item == 2, fy, fz)))
    first = (((lane & 1) + (lane >> 1)) & 1) != 0
    pair[0] = jnp.where(first_of_two, fresh[2], fresh[1])
    pair[1] = jnp.where(first_of_two, fresh[1], fresh[0])
    for_left = odd_cells(pair.at[0], quarter, first)
    for_right = odd_cells(pair.at[1], quarter, first)
    for c in range(slots.shape[0]):
        slots[c, 0] = tile
        slots[c, 1] = jnp.where(position < 2 * c + 1 - position % 2, for_right, for_left)


class Level:
    def __init__(self, mass, source, faces, row_step, lane_step):
        self.source, self.row_step, self.lane_step = source, row_step, lane_step
        self.fx, self.fy, self.fz = faces
        self.layers, rows, lanes = source.shape
        nothing = jnp.zeros_like(source[:1])
        self.nothing = nothing
        self.fxl = jnp.concatenate([nothing, self.fx[:-1]], 0)
        self.fyl = behind(self.fy, row_step, 1)
        self.fzl = behind(self.fz, lane_step, 2)
        weight = self.fx + self.fxl + self.fy + self.fyl + self.fz + self.fzl
        self.inv = 1.0 / (mass + weight)
        shape = source.shape
        total = lax.broadcasted_iota(jnp.int32, shape, 0)
        total = total + rows_of(shape) // row_step + lanes_of(shape) // lane_step
        self.even = (total & 1) == 0

    def neigh(self, e):
        upper = jnp.concatenate([e[1:], self.nothing], 0)
        lower = jnp.concatenate([self.nothing, e[:-1]], 0)
        total = self.fx * upper + self.fxl * lower
        total = total + self.fy * ahead(e, self.row_step, 1) + self.fyl * behind(e, self.row_step, 1)
        return total + self.fz * ahead(e, self.lane_step, 2) + self.fzl * behind(e, self.lane_step, 2)

    def start(self):
        e = jnp.where(self.even, self.source * self.inv, 0.0)
        return self.odd_update(e)

    def even_update(self, e):
        return jnp.where(self.even, (self.source + self.neigh(e)) * self.inv, e)

    def odd_update(self, e):
        return jnp.where(self.even, e, (self.source + self.neigh(e)) * self.inv)

    def residual(self, e):
        return jnp.where(self.even, self.neigh(e), 0.0)

    def pairs(self, values):
        halves = values.reshape(self.layers // 2, 2, *values.shape[1:])
        return halves[:, 0] + halves[:, 1]

    def coarse_faces(self):
        row_bit = (rows_of(self.fx.shape) & self.row_step) != 0
        lane_bit = (lanes_of(self.fx.shape) & self.lane_step) != 0
        odd_layers = self.fx.reshape(self.layers // 2, 2, *self.fx.shape[1:])[:, 1]
        fx = self.in_plane(odd_layers)
        fy = self.in_plane(self.pairs(jnp.where(row_bit, self.fy, 0.0)))
        fz = self.in_plane(self.pairs(jnp.where(lane_bit, self.fz, 0.0)))
        return fx, fy, fz

    def in_plane(self, values):
        return with_partner(with_partner(values, self.row_step, 1), self.lane_step, 2)

    def restricted(self, values):
        return self.in_plane(self.pairs(values))


def doubled_layers(values):
    layers = values.shape[0]
    both = jnp.concatenate([values[:, None], values[:, None]], 1)
    return both.reshape(2 * layers, *values.shape[1:])


def small_cycle(mass, source, faces, row_step, lane_step, deeper):
    level = Level(mass, source, faces, row_step, lane_step)
    e = level.start()
    if deeper == 0:
        for turn in range(COARSE_SWEEPS - 1):
            e = level.odd_update(level.even_update(e))
        return e
    fix = small_cycle(
        8.0 * mass, level.restricted(level.residual(e)), level.coarse_faces(),
        2 * row_step, 2 * lane_step, deeper - 1,
    )
    e = e + doubled_layers(fix)
    return level.odd_update(level.even_update(e))


def chunked(count, size, body):
    size = min(size, count)
    if count == size:
        body(0)
    else:
        lax.fori_loop(0, count // size, lambda i, c: (body(i * size), c)[1], 0)


def coarse_kernel(
    owner_of, same_cores, other_cores, e2_in, s2, fx2, fxl2, fy2, fz2, inv2,
    field, source, fx_in, fy_in, fz_in, inv_in, across_in, within_in,
    solved, owned,
    s3, fx3, fy3, fz3, fzl3, inv3, e3, pair3, small, e2, fzl2, e1, cor, owner_here, sem,
):
    fetch = pltpu.make_async_copy(owner_of, owner_here, sem)
    fetch.start()
    chips, _, quarter, lanes = same_cores.shape
    blocks = 2 * chips
    half, height = 2 * quarter, 4 * quarter
    position, last = lax.axis_index("gx"), blocks - 1

    body3, up3, down3 = pl.ds(PAD, quarter), pl.ds(PAD + 1, quarter), pl.ds(PAD - 1, quarter)
    row, lane = rows_of((quarter, lanes)), lanes_of((quarter, lanes))
    parity3 = row + (lane >> 2)
    item = lane & 3
    edge3 = jnp.zeros((quarter + 2 * PAD, lanes), jnp.float32)
    for j in (0, blocks + 1):
        e3[j] = edge3
    fx3[0] = jnp.zeros((quarter, lanes), jnp.float32)

    def unpack(at):
        tiles = []
        for i in range(0, min(16, blocks), 2):
            chip = (at + i) // 2
            tiles.extend(by_side(same_cores[chip, 0], other_cores[chip, 0]))
        for i, tile in enumerate(tiles):
            j = at + i
            moved = {0: tile}
            for step in (1, 2, 3):
                moved[step] = ahead(tile, step, 1)
                moved[-step] = behind(tile, step, 1)
            spread = []
            for k in range(4):
                value = moved[k]
                for slot in (1, 2, 3):
                    value = jnp.where(item == slot, moved[k - slot], value)
                spread.append(value)
            s3[j] = spread[0]
            fx3[j + 1] = spread[1]
            fy3[j] = edge3
            fy3[j, body3] = spread[2]
            fz3[j] = spread[3]
            fzl3[j] = behind(spread[3], 4, 1)

    chunked(blocks, 16, unpack)

    def is_even3(j):
        return ((parity3 + j) & 1) == 0

    def weights3(at):
        for i in range(min(16, blocks)):
            j = at + i
            weight = fx3[j + 1] + fx3[j] + fy3[j, body3] + fy3[j, down3] + fz3[j] + fzl3[j]
            inverse = 1.0 / (64.0 + weight)
            inv3[j] = inverse
            e3[j + 1] = edge3
            e3[j + 1, body3] = jnp.where(is_even3(j), s3[j] * inverse, 0.0)

    chunked(blocks, 16, weights3)

    def neigh3(j):
        here = e3[j + 1, body3]
        sums = fx3[j + 1] * e3[j + 2, body3] + fx3[j] * e3[j, body3]
        sums = sums + fy3[j, body3] * e3[j + 1, up3] + fy3[j, down3] * e3[j + 1, down3]
        return here, sums + fz3[j] * ahead(here, 4, 1) + fzl3[j] * behind(here, 4, 1)

    def update3(at, count, even):
        fresh = []
        for i in range(count):
            j = at + i
            here, sums = neigh3(j)
            value = (s3[j] + sums) * inv3[j]
            where = is_even3(j)
            fresh.append(jnp.where(where, value, here) if even else jnp.where(where, here, value))
        for i in range(count):
            e3[at + i + 1, body3] = fresh[i]

    chunked(blocks, 16, lambda at: update3(at, min(16, blocks), False))

    def restrict3(at):
        for i in range(0, min(16, blocks), 2):
            j = at + i
            parts = []
            for k in (j, j + 1):
                _, sums = neigh3(k)
                parts.append(jnp.where(is_even3(k), sums, 0.0))
            pair3[i, :quarter] = parts[0] + parts[1]
            pair3[i + 1, :quarter] = fz3[j] + fz3[j + 1]
        for i in range(0, min(16, blocks), 2):
            j = at + i
            out = (at + i) // 2
            small[0, out] = with_partner(even_row_sum(pair3.at[i], PAD), 4, 1)
            fxs = fx3[j + 2, pl.ds(0, PAD, 2), :] + fx3[j + 2, pl.ds(1, PAD, 2), :]
            small[1, out] = with_partner(fxs, 4, 1)
            fys = fy3[j, pl.ds(PAD + 1, PAD, 2), :] + fy3[j + 1, pl.ds(PAD + 1, PAD, 2), :]
            small[2, out] = with_partner(fys, 4, 1)
            fzs = even_row_sum(pair3.at[i + 1], PAD)
            odd = (lanes_of((PAD, lanes)) & 4) != 0
            small[3, out] = with_partner(jnp.where(odd, fzs, 0.0), 4, 1)

    chunked(blocks, 16, restrict3)

    small[0] = small_cycle(512.0, small[0], (small[1], small[2], small[3]), 1, 8, 2)

    def prolong3(at):
        for i in range(min(16, blocks)):
            j = at + i
            fix = small[0, j // 2]
            pair3[i, pl.ds(0, PAD, 2), :] = fix
            pair3[i, pl.ds(1, PAD, 2), :] = fix
        for i in range(min(16, blocks)):
            j = at + i
            e3[j + 1, body3] = e3[j + 1, body3] + pair3[i, :quarter]

    chunked(blocks, 16, prolong3)
    chunked(blocks, 16, lambda at: update3(at, min(16, blocks), True))
    chunked(blocks, 16, lambda at: update3(at, min(16, blocks), False))

    fetch.wait()
    owner = owner_here[position]
    wide, narrow = lanes_of((lanes, lanes)), rows_of((lanes, lanes))
    take = jnp.where(narrow == 4 * wide, 1.0, 0.0)
    block = jnp.dot(
        e3[owner + 1, body3], take, precision=lax.Precision.HIGHEST, preferred_element_type=jnp.float32
    )
    owned[0] = block[:, : lanes // 4]

    first_of_two, even2 = parities2(half, lanes)
    body2 = pl.ds(PAD, half)
    edge = jnp.zeros((PAD, lanes), jnp.float32)
    left = other_cores[jnp.maximum(position - 1, 0) // 2, 1]
    right = other_cores[jnp.minimum(position + 1, last) // 2, 1]
    into_both_rows(pair3.at[0], left)
    into_both_rows(pair3.at[1], right)
    left, right = pair3[0], pair3[1]
    before = (
        left, jnp.where(first_of_two, left, e2_in[0]), e2_in[1], jnp.where(first_of_two, e2_in[2], right), right
    )
    for k in range(5):
        third = jnp.clip(position + k - 1, 1, blocks)
        into_both_rows(pair3.at[k % 4], e3[third, body3])
        e2[k, :PAD] = edge
        e2[k, PAD + half:] = edge
        e2[k, body2] = before[k] + pair3[k % 4]
    for j in range(3):
        fzl2[j] = behind(fz2[j], 2, 1)
    for even in (True, False):
        fresh = []
        for j, sums in enumerate(neigh2(e2, fx2, fxl2, fy2, fz2, fzl2, first_of_two, (0, 1, 2))):
            value, here = (s2[j] + sums) * inv2[j], e2[j + 1, body2]
            fresh.append(jnp.where(even2, value, here) if even else jnp.where(even2, here, value))
        for j in range(3):
            e2[j + 1, body2] = fresh[j]

    body1, up1, down1 = pl.ds(PAD, height), pl.ds(PAD + 1, height), pl.ds(PAD - 1, height)
    rows, lane = rows_of((height, lanes)), lanes_of((height, lanes))
    even_sum = ((rows + lane) & 1) == 0
    count = e1.shape[0]
    borders = by_side(across_in[4], within_in[4])
    for w in range(0, count, 2):
        coarse_layer = w // 2 - 1
        packed = e2[2 + coarse_layer // 2, body2]
        if coarse_layer % 2 == 0:
            plain = jnp.where(first_of_two, packed, behind(packed, 1, 1))
        else:
            plain = jnp.where(first_of_two, ahead(packed, 1, 1), packed)
        into_both_rows(cor.at[0], plain)
        fix = cor[0]
        for v in (w, w + 1):
            e1[v, :PAD] = edge
            e1[v, PAD + height:] = edge
            if v in (0, count - 1):
                into_both_rows(cor.at[1], borders[0 if v == 0 else 1])
                e1[v, body1] = cor[1] + fix
            else:
                e1[v, body1] = field[v] + fix

    def smoothed1(w, even):
        here = e1[w, body1]
        face = fz_in[w]
        sums = fx_in[w] * e1[w + 1, body1] + fx_in[w - 1] * e1[w - 1, body1]
        sums = sums + fy_in[w, body1] * e1[w, up1] + fy_in[w, down1] * e1[w, down1]
        sums = sums + face * ahead(here, 1, 1) + behind(face, 1, 1) * behind(here, 1, 1)
        value = (source[w] + sums) * inv_in[w]
        keep = even_sum if (w + even) % 2 == 0 else ~even_sum
        return jnp.where(keep, here, value)

    for w in range(1, count - 1):
        e1[w, body1] = smoothed1(w, 1)
    for w in range(2, count - 2):
        solved[w - 2] = smoothed1(w, 0)


def f32(*shape):
    return jax.ShapeDtypeStruct(shape, jnp.float32)


def vmem(*shape):
    return pltpu.VMEM(shape, jnp.float32)


def call(kernel, outs, scratch, operands):
    def size(shape):
        count = 4
        for extent in shape:
            count *= extent
        return count

    sized = [array for array in (*scratch, *outs, *operands) if hasattr(array, "shape")]
    asked = 8 * 2**20 + sum(size(array.shape) for array in sized)
    return pl.pallas_call(
        kernel,
        out_shape=tuple(outs),
        in_specs=[pl.BlockSpec(memory_space=pltpu.VMEM)] * len(operands),
        out_specs=tuple([pl.BlockSpec(memory_space=pltpu.VMEM)] * len(outs)),
        scratch_shapes=scratch,
        compiler_params=pltpu.CompilerParams(vmem_limit_bytes=asked),
    )(*operands)


def on_device(iterate, source, phase_field, block_owner):
    layers, height, depth = iterate.shape
    half, quarter = height // 2, height // 4
    blocks = lax.axis_size("gx")
    window = layers + 4
    padded, padded2, padded3 = height + 2 * PAD, half + 2 * PAD, quarter + 2 * PAD
    inputs = sum(
        jnp.pad(block, ((k * layers, (2 - k) * layers), (0, 0), (0, 0)))
        for k, block in enumerate((iterate, source, phase_field))
    )
    sent = call(edge_kernel, [f32(4 * height + half, depth)] * 2, [], (inputs,))
    plain = f32(window, height, depth)
    across, within, fx2, *fine = call(
        fine_down_kernel,
        [f32(5, half, depth)] * 2
        + [f32(2, half, depth), plain, plain, plain, f32(window, padded, depth), plain, plain],
        [
            vmem(window, padded, depth), vmem(window, padded, depth), vmem(window, height, depth),
            vmem(layers, height, depth), vmem(2, height, depth),
        ],
        (block_owner, inputs, *swapped(*sent)),
    )
    halos = swapped(across, within)
    plain = f32(3, half, depth)
    slots, *middle = call(
        middle_down_kernel,
        [f32(blocks // 2, 2, quarter, depth), plain, plain, plain, plain, f32(3, padded2, depth), plain, plain],
        [vmem(5, padded2, depth), vmem(3, half, depth), vmem(2, half, depth)],
        (across, fx2, *halos),
    )
    kinds = [list(range(core, blocks, 2)) for core in range(2)]
    same_cores = lax.all_to_all(slots, "gx", 0, 0, axis_index_groups=kinds, tiled=True)
    other_cores = within_chip(same_cores)
    solved, owned = call(
        coarse_kernel,
        [f32(layers, height, depth), f32(1, quarter, depth // 4)],
        [
            vmem(blocks, quarter, depth), vmem(blocks + 1, quarter, depth), vmem(blocks, padded3, depth),
            vmem(blocks, quarter, depth), vmem(blocks, quarter, depth), vmem(blocks, quarter, depth),
            vmem(blocks + 2, padded3, depth), vmem(16, half, depth), vmem(4, blocks // 2, PAD, depth),
            vmem(5, padded2, depth), vmem(3, half, depth), vmem(window, padded, depth), vmem(2, height, depth),
            pltpu.SMEM((blocks,), jnp.int32), pltpu.SemaphoreType.DMA,
        ],
        (block_owner, same_cores, other_cores, *middle, *fine, *halos),
    )
    return solved, owned


def solution(mesh):
    split = P(("groups", "gx"), None, None)
    return jax.shard_map(
        on_device,
        mesh=mesh,
        in_specs=(split, split, split, P("groups")),
        out_specs=(split, split),
        check_vma=False,
    )
```

```python
import jax
import jax.numpy as jnp
from jax import lax
from jax.experimental import pallas as pl
from jax.experimental.pallas import tpu as pltpu
from jax.sharding import PartitionSpec as P

STIFFNESS = 100.0
EPSILON = 0.01
COARSE_SWEEPS = 4
PAD = 8


def swapped(across, within):
    chips = [(i, i + 1 if i % 2 else i - 1) for i in range(1, lax.axis_size("gx") - 1)]
    return lax.ppermute(across, "gx", chips), within_chip(within)


def within_chip(block):
    return lax.ppermute(block, "gx", [(i, i ^ 1) for i in range(lax.axis_size("gx"))])


def by_side(across, within):
    on_left = lax.axis_index("gx") % 2 == 0
    return jnp.where(on_left, across, within), jnp.where(on_left, within, across)


def store_by_side(across, within, pieces):
    on_left = lax.axis_index("gx") % 2 == 0

    @pl.when(on_left)
    def _():
        for index, left, right in pieces:
            across[index] = left
            within[index] = right

    @pl.when(jnp.logical_not(on_left))
    def _():
        for index, left, right in pieces:
            across[index] = right
            within[index] = left


def lanes_of(shape):
    return lax.broadcasted_iota(jnp.int32, shape, len(shape) - 1)


def rows_of(shape):
    return lax.broadcasted_iota(jnp.int32, shape, len(shape) - 2)


def ahead(values, step, axis):
    return pltpu.roll(values, values.shape[axis] - step, axis)


def behind(values, step, axis):
    return pltpu.roll(values, step, axis)


def with_partner(values, step, axis):
    index = lax.broadcasted_iota(jnp.int32, values.shape, axis)
    partner = jnp.where((index & step) == 0, ahead(values, step, axis), behind(values, step, axis))
    return values + partner


def even_row_sum(scratch, rows):
    return scratch[pl.ds(0, rows, 2), :] + scratch[pl.ds(1, rows, 2), :]


def three_parts(ref):
    third = ref.shape[0] // 3
    return [ref.at[pl.ds(k * third, third)] for k in range(3)]


def edge_kernel(inputs, across, within):
    iterate, source, phase = three_parts(inputs)
    layers, height, depth = iterate.shape
    half = height // 2
    row, lane = rows_of((height, depth)), lanes_of((height, depth))
    even_sum = ((row + lane) & 1) == 0
    odd_lane = (lanes_of((half, depth)) & 1) != 0
    cell = []
    for w in range(layers):
        value = phase[w]
        cell.append(STIFFNESS * (value * value + EPSILON))

    def in_layer(w):
        here, e = cell[w], iterate[w]
        fy = jnp.where(row < height - 1, 0.5 * (here + ahead(here, 1, 0)), 0.0)
        fz = jnp.where(lane < depth - 1, 0.5 * (here + ahead(here, 1, 1)), 0.0)
        fyl, fzl = behind(fy, 1, 0), behind(fz, 1, 1)
        total = fy * ahead(e, 1, 0) + fyl * behind(e, 1, 0)
        return total + fz * ahead(e, 1, 1) + fzl * behind(e, 1, 1), fy + fyl + fz + fzl

    sides = []
    for near, step in ((0, 1), (layers - 1, -1)):
        inner, far = near + step, near + 2 * step
        face_near, face_far = 0.5 * (cell[inner] + cell[near]), 0.5 * (cell[inner] + cell[far])
        total, weight = in_layer(inner)
        total = total + face_near * iterate[near] + face_far * iterate[far]
        updated = (source[inner] + total) / (1.0 + (face_near + face_far + weight))
        total, _ = in_layer(near)
        even = even_sum if near % 2 == 0 else ~even_sum
        known = source[near] + jnp.where(even, total + face_near * iterate[inner], face_near * updated)
        sides.append((cell[near], cell[inner], known, odd_cells(iterate.at[near], half, odd_lane ^ (near % 2 != 0))))
    places = [pl.ds(k * height, height) for k in range(3)] + [pl.ds(3 * height, half)]
    store_by_side(across, within, list(zip(places, *sides)))


def odd_cells(ref, rows, first):
    return jnp.where(first, ref[pl.ds(0, rows, 2), :], ref[pl.ds(1, rows, 2), :])


def into_both_rows(ref, values):
    rows = values.shape[0]
    ref[pl.ds(0, rows, 2), :] = values
    ref[pl.ds(1, rows, 2), :] = values


def fine_down_kernel(
    owner_of, inputs, across_in, within_in,
    across, within, fx2_out, e, fx, fx_outer, fy, fz, inv,
    cell, fzl, held, pair,
):
    iterate, source, phase = three_parts(inputs)
    layers, height, depth = iterate.shape
    window = layers + 2
    position, last = lax.axis_index("gx"), lax.axis_size("gx") - 1
    body = pl.ds(PAD, height)
    up, down = pl.ds(PAD + 1, height), pl.ds(PAD - 1, height)
    row, lane = rows_of((height, depth)), lanes_of((height, depth))
    even_sum = ((row + lane) & 1) == 0
    half = height // 2
    own = range(1, layers + 1)
    outer = ((0, 0), (1, window - 1))

    def part(ref, k):
        return ref[k * height:(k + 1) * height]

    def mask(w, odd):
        return even_sum if (w + odd) % 2 == 1 else ~even_sum

    edge = jnp.zeros((PAD, depth), jnp.float32)
    for w in range(window):
        for padded in (e, fy):
            padded[w, :PAD] = edge
            padded[w, PAD + height:] = edge
        cell[w, PAD + height:] = edge
    halos = [by_side(part(across_in, k), part(within_in, k)) for k in range(3)]
    borders = by_side(across_in[3 * height:], within_in[3 * height:])
    for side, w in outer:
        cell[w, body] = halos[0][side]
        fx_outer[side] = 0.5 * (halos[0][side] + halos[1][side])
        into_both_rows(pair.at[side], borders[side])
        e[w, body] = pair[side]
    for w in own:
        value = phase[w - 1]
        cell[w, body] = STIFFNESS * (value * value + EPSILON)
        e[w, body] = iterate[w - 1]
    for w in range(window):
        here = cell[w, body]
        if w < window - 1:
            face = 0.5 * (here + cell[w + 1, body])
            if w == 0:
                face = jnp.where(position > 0, face, 0.0)
            if w == window - 2:
                face = jnp.where(position < last, face, 0.0)
            fx[w] = face
        fy[w, body] = jnp.where(row < height - 1, 0.5 * (here + cell[w, up]), 0.0)
        face = jnp.where(lane < depth - 1, 0.5 * (here + ahead(here, 1, 1)), 0.0)
        fz[w] = face
        fzl[w] = behind(face, 1, 1)
    for w in range(window):
        beyond = fx[w] if w < window - 1 else fx_outer[1]
        before = fx[w - 1] if w > 0 else fx_outer[0]
        weight = beyond + before + fy[w, body] + fy[w, down] + fz[w] + fzl[w]
        inv[w] = 1.0 / (1.0 + weight)

    def in_layer(w):
        here = e[w, body]
        total = fy[w, body] * e[w, up] + fy[w, down] * e[w, down]
        return total + fz[w] * ahead(here, 1, 1) + fzl[w] * behind(here, 1, 1)

    def neigh(w):
        return fx[w] * e[w + 1, body] + fx[w - 1] * e[w - 1, body] + in_layer(w)

    def towards_own(side, w):
        return fx[0] * e[1, body] if side == 0 else fx[w - 1] * e[w - 1, body]

    for w in own:
        total = source[w - 1] + neigh(w)
        held[w - 1] = total
        e[w, body] = jnp.where(mask(w, 0), total * inv[w], e[w, body])
    for side, w in outer:
        total = halos[2][side] + towards_own(side, w)
        e[w, body] = jnp.where(mask(w, 0), total * inv[w], e[w, body])
    for side, w in outer:
        total = (halos[2][side] + in_layer(w) + towards_own(side, w)) * inv[w]
        e[w, body] = jnp.where(mask(w, 1), total, e[w, body])
    for w in own:
        total = (source[w - 1] + neigh(w)) * inv[w]
        e[w, body] = jnp.where(mask(w, 1), total, e[w, body])

    lane = lanes_of((half, depth))
    first_of_two = (lane & 1) == 0

    def residual(w):
        return jnp.where(mask(w, 0), source[w - 1] + neigh(w) - held[w - 1], 0.0)

    def slabs(make, reduce_rows, reduce_lanes):
        found = []
        for t in range(2):
            pair[t] = make(1 + 2 * t)
            found.append(reduce_lanes(reduce_rows(pair.at[t])))
        return jnp.where(first_of_two, found[0], found[1])

    def both_rows(scratch):
        return even_row_sum(scratch, half)

    def odd_rows(scratch):
        return scratch[pl.ds(1, half, 2), :]

    def both_lanes(values):
        return with_partner(values, 1, 1)

    def odd_lanes(values):
        return jnp.where(first_of_two, ahead(values, 1, 1), values)

    coarse_source = slabs(lambda w: residual(w) + residual(w + 1), both_rows, both_lanes)
    coarse_fy = slabs(lambda w: fy[w, body] + fy[w + 1, body], odd_rows, both_lanes)
    coarse_fz = slabs(lambda w: fz[w] + fz[w + 1], both_rows, odd_lanes)
    left_fx = slabs(lambda w: fx[w + 1], both_rows, both_lanes)
    right_fx = slabs(lambda w: fx[w - 1], both_rows, both_lanes)
    fx2_out[0], fx2_out[1] = left_fx, right_fx
    known = []
    for t, (w, face, inner) in enumerate(((1, 1, 2), (layers, layers - 1, layers - 1))):
        pair[t] = source[w - 1] + fx[face] * e[inner, body]
        known.append(odd_cells(pair.at[t], half, first_of_two if w % 2 == 1 else ~first_of_two))
    pieces = [(0, coarse_source), (2, coarse_fy), (3, coarse_fz)]
    pieces = [(k, value, value) for k, value in pieces]
    store_by_side(across, within, pieces + [(1, left_fx, right_fx), (4, *known)])


def neigh2(e2, fx2, fxl2, fy2, fz2, fzl2, first_of_two, tiles):
    half = fx2.shape[1]
    body, up, down = pl.ds(PAD, half), pl.ds(PAD + 1, half), pl.ds(PAD - 1, half)
    needed = range(tiles[0], tiles[-1] + 3)
    here = {j: e2[j, body] for j in needed}
    after = {j: ahead(here[j], 1, 1) for j in needed}
    before = {j: behind(here[j], 1, 1) for j in needed}
    found = []
    for j in tiles:
        k = j + 1
        upper = jnp.where(first_of_two, after[k], before[k + 1])
        lower = jnp.where(first_of_two, after[k - 1], before[k])
        sums = fx2[j] * upper + fxl2[j] * lower
        sums = sums + fy2[j, body] * e2[k, up] + fy2[j, down] * e2[k, down]
        sums = sums + fz2[j] * ahead(here[k], 2, 1) + fzl2[j] * behind(here[k], 2, 1)
        found.append(sums)
    return found


def parities2(half, lanes):
    row, lane = rows_of((half, lanes)), lanes_of((half, lanes))
    return (lane & 1) == 0, ((row + (lane & 1) + (lane >> 1)) & 1) == 0


def group(values):
    return with_partner(with_partner(values, 1, 1), 2, 1)


def middle_down_kernel(
    own, own_fx, across_in, within_in,
    slots, e2_out, s2, fx2, fxl2, fy2, fz2, inv2,
    e2, fzl2, pair,
):
    _, half, lanes = own.shape
    quarter = half // 2
    position = lax.axis_index("gx")
    first_of_two, even2 = parities2(half, lanes)
    body, down = pl.ds(PAD, half), pl.ds(PAD - 1, half)
    edge = jnp.zeros((PAD, lanes), jnp.float32)
    for j in range(5):
        e2[j] = jnp.zeros((half + 2 * PAD, lanes), jnp.float32)
    def three(k):
        left, right = by_side(across_in[k], within_in[k])
        return left, own[k], right

    for j, (source, fy, fz) in enumerate(zip(three(0), three(2), three(3))):
        s2[j] = source
        fy2[j, :PAD] = edge
        fy2[j, body] = fy
        fy2[j, PAD + half:] = edge
        fz2[j] = fz
        fzl2[j] = behind(fz, 2, 1)
    left_fx, _, right_fx = three(1)
    fx2[0] = jnp.where(first_of_two, ahead(left_fx, 1, 1), behind(own_fx[1], 1, 1))
    fx2[1] = own_fx[0]
    fx2[2] = right_fx
    fxl2[0] = left_fx
    fxl2[1] = own_fx[1]
    fxl2[2] = jnp.where(first_of_two, ahead(own_fx[0], 1, 1), behind(right_fx, 1, 1))
    for j in range(3):
        weight = fx2[j] + fxl2[j] + fy2[j, body] + fy2[j, down] + fz2[j] + fzl2[j]
        inverse = 1.0 / (8.0 + weight)
        inv2[j] = inverse
        e2[j + 1, body] = jnp.where(even2, s2[j] * inverse, 0.0)

    def neigh(tiles):
        return neigh2(e2, fx2, fxl2, fy2, fz2, fzl2, first_of_two, tiles)

    fresh = [
        jnp.where(even2, e2[j + 1, body], (s2[j] + sums) * inv2[j]) for j, sums in enumerate(neigh((0, 1, 2)))
    ]
    for j in range(3):
        e2[j + 1, body] = fresh[j]
        e2_out[j] = fresh[j]
    pair[0] = jnp.where(even2, neigh((1,))[0], 0.0)
    lane = lanes_of((quarter, lanes))
    odd_layer, odd_depth, item = (lane & 1) != 0, (lane & 2) != 0, lane & 3
    source = group(even_row_sum(pair.at[0], quarter))
    fx = group(jnp.where(odd_layer, even_row_sum(fx2.at[1], quarter), 0.0))
    fy = group(fy2[1, pl.ds(PAD + 1, quarter, 2), :])
    fz = group(jnp.where(odd_depth, even_row_sum(fz2.at[1], quarter), 0.0))
    tile = jnp.where(item == 0, source, jnp.where(item == 1, fx, jnp.where(item == 2, fy, fz)))
    first = (((lane & 1) + (lane >> 1)) & 1) != 0
    pair[0] = jnp.where(first_of_two, fresh[2], fresh[1])
    pair[1] = jnp.where(first_of_two, fresh[1], fresh[0])
    for_left = odd_cells(pair.at[0], quarter, first)
    for_right = odd_cells(pair.at[1], quarter, first)
    for c in range(slots.shape[0]):
        slots[c, 0] = tile
        slots[c, 1] = jnp.where(position < 2 * c + 1 - position % 2, for_right, for_left)


class Level:
    def __init__(self, mass, source, faces, row_step, lane_step):
        self.source, self.row_step, self.lane_step = source, row_step, lane_step
        self.fx, self.fy, self.fz = faces
        self.layers, rows, lanes = source.shape
        nothing = jnp.zeros_like(source[:1])
        self.nothing = nothing
        self.fxl = jnp.concatenate([nothing, self.fx[:-1]], 0)
        self.fyl = behind(self.fy, row_step, 1)
        self.fzl = behind(self.fz, lane_step, 2)
        weight = self.fx + self.fxl + self.fy + self.fyl + self.fz + self.fzl
        self.inv = 1.0 / (mass + weight)
        shape = source.shape
        total = lax.broadcasted_iota(jnp.int32, shape, 0)
        total = total + rows_of(shape) // row_step + lanes_of(shape) // lane_step
        self.even = (total & 1) == 0

    def neigh(self, e):
        upper = jnp.concatenate([e[1:], self.nothing], 0)
        lower = jnp.concatenate([self.nothing, e[:-1]], 0)
        total = self.fx * upper + self.fxl * lower
        total = total + self.fy * ahead(e, self.row_step, 1) + self.fyl * behind(e, self.row_step, 1)
        return total + self.fz * ahead(e, self.lane_step, 2) + self.fzl * behind(e, self.lane_step, 2)

    def start(self):
        e = jnp.where(self.even, self.source * self.inv, 0.0)
        return self.odd_update(e)

    def even_update(self, e):
        return jnp.where(self.even, (self.source + self.neigh(e)) * self.inv, e)

    def odd_update(self, e):
        return jnp.where(self.even, e, (self.source + self.neigh(e)) * self.inv)

    def residual(self, e):
        return jnp.where(self.even, self.neigh(e), 0.0)

    def pairs(self, values):
        halves = values.reshape(self.layers // 2, 2, *values.shape[1:])
        return halves[:, 0] + halves[:, 1]

    def coarse_faces(self):
        row_bit = (rows_of(self.fx.shape) & self.row_step) != 0
        lane_bit = (lanes_of(self.fx.shape) & self.lane_step) != 0
        odd_layers = self.fx.reshape(self.layers // 2, 2, *self.fx.shape[1:])[:, 1]
        fx = self.in_plane(odd_layers)
        fy = self.in_plane(self.pairs(jnp.where(row_bit, self.fy, 0.0)))
        fz = self.in_plane(self.pairs(jnp.where(lane_bit, self.fz, 0.0)))
        return fx, fy, fz

    def in_plane(self, values):
        return with_partner(with_partner(values, self.row_step, 1), self.lane_step, 2)

    def restricted(self, values):
        return self.in_plane(self.pairs(values))


def doubled_layers(values):
    layers = values.shape[0]
    both = jnp.concatenate([values[:, None], values[:, None]], 1)
    return both.reshape(2 * layers, *values.shape[1:])


def small_cycle(mass, source, faces, row_step, lane_step, deeper):
    level = Level(mass, source, faces, row_step, lane_step)
    e = level.start()
    if deeper == 0:
        for turn in range(COARSE_SWEEPS - 1):
            e = level.odd_update(level.even_update(e))
        return e
    fix = small_cycle(
        8.0 * mass, level.restricted(level.residual(e)), level.coarse_faces(),
        2 * row_step, 2 * lane_step, deeper - 1,
    )
    e = e + doubled_layers(fix)
    return level.odd_update(level.even_update(e))


def chunked(count, size, body):
    size = min(size, count)
    if count == size:
        body(0)
    else:
        lax.fori_loop(0, count // size, lambda i, c: (body(i * size), c)[1], 0)


def coarse_kernel(
    owner_of, same_cores, other_cores, e2_in, s2, fx2, fxl2, fy2, fz2, inv2,
    inputs, field, fx_in, fx_outer, fy_in, fz_in, inv_in, across_in, within_in,
    solved, owned,
    s3, fx3, fy3, fz3, fzl3, inv3, e3, pair3, small, e2, fzl2, e1, cor, owner_here, sem,
):
    fetch = pltpu.make_async_copy(owner_of, owner_here, sem)
    fetch.start()
    chips, _, quarter, lanes = same_cores.shape
    blocks = 2 * chips
    half, height = 2 * quarter, 4 * quarter
    position, last = lax.axis_index("gx"), blocks - 1

    body3, up3, down3 = pl.ds(PAD, quarter), pl.ds(PAD + 1, quarter), pl.ds(PAD - 1, quarter)
    row, lane = rows_of((quarter, lanes)), lanes_of((quarter, lanes))
    parity3 = row + (lane >> 2)
    item = lane & 3
    edge3 = jnp.zeros((quarter + 2 * PAD, lanes), jnp.float32)
    for j in (0, blocks + 1):
        e3[j] = edge3
    fx3[0] = jnp.zeros((quarter, lanes), jnp.float32)

    def unpack(at):
        tiles = []
        for i in range(0, min(16, blocks), 2):
            chip = (at + i) // 2
            tiles.extend(by_side(same_cores[chip, 0], other_cores[chip, 0]))
        for i, tile in enumerate(tiles):
            j = at + i
            moved = {0: tile}
            for step in (1, 2, 3):
                moved[step] = ahead(tile, step, 1)
                moved[-step] = behind(tile, step, 1)
            spread = []
            for k in range(4):
                value = moved[k]
                for slot in (1, 2, 3):
                    value = jnp.where(item == slot, moved[k - slot], value)
                spread.append(value)
            s3[j] = spread[0]
            fx3[j + 1] = spread[1]
            fy3[j] = edge3
            fy3[j, body3] = spread[2]
            fz3[j] = spread[3]
            fzl3[j] = behind(spread[3], 4, 1)

    chunked(blocks, 16, unpack)

    def is_even3(j):
        return ((parity3 + j) & 1) == 0

    def weights3(at):
        for i in range(min(16, blocks)):
            j = at + i
            weight = fx3[j + 1] + fx3[j] + fy3[j, body3] + fy3[j, down3] + fz3[j] + fzl3[j]
            inverse = 1.0 / (64.0 + weight)
            inv3[j] = inverse
            e3[j + 1] = edge3
            e3[j + 1, body3] = jnp.where(is_even3(j), s3[j] * inverse, 0.0)

    chunked(blocks, 16, weights3)

    def neigh3(j):
        here = e3[j + 1, body3]
        sums = fx3[j + 1] * e3[j + 2, body3] + fx3[j] * e3[j, body3]
        sums = sums + fy3[j, body3] * e3[j + 1, up3] + fy3[j, down3] * e3[j + 1, down3]
        return here, sums + fz3[j] * ahead(here, 4, 1) + fzl3[j] * behind(here, 4, 1)

    def update3(at, count, even):
        fresh = []
        for i in range(count):
            j = at + i
            here, sums = neigh3(j)
            value = (s3[j] + sums) * inv3[j]
            where = is_even3(j)
            fresh.append(jnp.where(where, value, here) if even else jnp.where(where, here, value))
        for i in range(count):
            e3[at + i + 1, body3] = fresh[i]

    chunked(blocks, 16, lambda at: update3(at, min(16, blocks), False))

    def restrict3(at):
        for i in range(0, min(16, blocks), 2):
            j = at + i
            parts = []
            for k in (j, j + 1):
                _, sums = neigh3(k)
                parts.append(jnp.where(is_even3(k), sums, 0.0))
            pair3[i, :quarter] = parts[0] + parts[1]
            pair3[i + 1, :quarter] = fz3[j] + fz3[j + 1]
        for i in range(0, min(16, blocks), 2):
            j = at + i
            out = (at + i) // 2
            small[0, out] = with_partner(even_row_sum(pair3.at[i], PAD), 4, 1)
            fxs = fx3[j + 2, pl.ds(0, PAD, 2), :] + fx3[j + 2, pl.ds(1, PAD, 2), :]
            small[1, out] = with_partner(fxs, 4, 1)
            fys = fy3[j, pl.ds(PAD + 1, PAD, 2), :] + fy3[j + 1, pl.ds(PAD + 1, PAD, 2), :]
            small[2, out] = with_partner(fys, 4, 1)
            fzs = even_row_sum(pair3.at[i + 1], PAD)
            odd = (lanes_of((PAD, lanes)) & 4) != 0
            small[3, out] = with_partner(jnp.where(odd, fzs, 0.0), 4, 1)

    chunked(blocks, 16, restrict3)

    small[0] = small_cycle(512.0, small[0], (small[1], small[2], small[3]), 1, 8, 2)

    def prolong3(at):
        for i in range(min(16, blocks)):
            j = at + i
            fix = small[0, j // 2]
            pair3[i, pl.ds(0, PAD, 2), :] = fix
            pair3[i, pl.ds(1, PAD, 2), :] = fix
        for i in range(min(16, blocks)):
            j = at + i
            e3[j + 1, body3] = e3[j + 1, body3] + pair3[i, :quarter]

    chunked(blocks, 16, prolong3)
    chunked(blocks, 16, lambda at: update3(at, min(16, blocks), True))
    chunked(blocks, 16, lambda at: update3(at, min(16, blocks), False))

    fetch.wait()
    owner = owner_here[position]
    wide, narrow = lanes_of((lanes, lanes)), rows_of((lanes, lanes))
    take = jnp.where(narrow == 4 * wide, 1.0, 0.0)
    block = jnp.dot(
        e3[owner + 1, body3], take, precision=lax.Precision.HIGHEST, preferred_element_type=jnp.float32
    )
    owned[0] = block[:, : lanes // 4]

    first_of_two, even2 = parities2(half, lanes)
    body2 = pl.ds(PAD, half)
    edge = jnp.zeros((PAD, lanes), jnp.float32)
    left = other_cores[jnp.maximum(position - 1, 0) // 2, 1]
    right = other_cores[jnp.minimum(position + 1, last) // 2, 1]
    into_both_rows(pair3.at[0], left)
    into_both_rows(pair3.at[1], right)
    left, right = pair3[0], pair3[1]
    before = (
        left, jnp.where(first_of_two, left, e2_in[0]), e2_in[1], jnp.where(first_of_two, e2_in[2], right), right
    )
    for k in range(5):
        third = jnp.clip(position + k - 1, 1, blocks)
        into_both_rows(pair3.at[k % 4], e3[third, body3])
        e2[k, :PAD] = edge
        e2[k, PAD + half:] = edge
        e2[k, body2] = before[k] + pair3[k % 4]
    for j in range(3):
        fzl2[j] = behind(fz2[j], 2, 1)
    for even in (True, False):
        fresh = []
        for j, sums in enumerate(neigh2(e2, fx2, fxl2, fy2, fz2, fzl2, first_of_two, (0, 1, 2))):
            value, here = (s2[j] + sums) * inv2[j], e2[j + 1, body2]
            fresh.append(jnp.where(even2, value, here) if even else jnp.where(even2, here, value))
        for j in range(3):
            e2[j + 1, body2] = fresh[j]

    _, source, _ = three_parts(inputs)
    body1, up1, down1 = pl.ds(PAD, height), pl.ds(PAD + 1, height), pl.ds(PAD - 1, height)
    rows, lane = rows_of((height, lanes)), lanes_of((height, lanes))
    even_sum = ((rows + lane) & 1) == 0
    count = e1.shape[0]
    fixes = []
    for w in range(count):
        tile, t = divmod((w - 1) // 2, 2)
        packed = e2[2 + tile, body2]
        if t == 0:
            plain = jnp.where(first_of_two, packed, behind(packed, 1, 1))
        else:
            plain = jnp.where(first_of_two, ahead(packed, 1, 1), packed)
        if w % 2 == 1 or w == 0:
            into_both_rows(cor.at[len(fixes) % 2], plain)
            fixes.append(cor[len(fixes) % 2])
        e1[w, :PAD] = edge
        e1[w, PAD + height:] = edge
        e1[w, body1] = field[w, body1] + fixes[-1]

    def in_layer1(w):
        here, face = e1[w, body1], fz_in[w]
        sums = fy_in[w, body1] * e1[w, up1] + fy_in[w, down1] * e1[w, down1]
        return sums + face * ahead(here, 1, 1) + behind(face, 1, 1) * behind(here, 1, 1)

    def smoothed1(w, odd):
        keep = even_sum if (w + odd) % 2 == 0 else ~even_sum
        sums = fx_in[w] * e1[w + 1, body1] + fx_in[w - 1] * e1[w - 1, body1] + in_layer1(w)
        return jnp.where(keep, e1[w, body1], (source[w - 1] + sums) * inv_in[w])

    for w in range(1, count - 1):
        e1[w, body1] = smoothed1(w, 0)
    borders = by_side(across_in[4], within_in[4])
    for side, w, near in ((0, 0, 1), (1, count - 1, count - 2)):
        into_both_rows(cor.at[side], borders[side])
        sums = cor[side] + fx_outer[side] * fixes[0 if side == 0 else -1]
        sums = sums + fx_in[min(w, near)] * e1[near, body1] + in_layer1(w)
        e1[w, body1] = sums * inv_in[w]
    for w in range(1, count - 1):
        solved[w - 1] = smoothed1(w, 1)


def f32(*shape):
    return jax.ShapeDtypeStruct(shape, jnp.float32)


def vmem(*shape):
    return pltpu.VMEM(shape, jnp.float32)


def call(kernel, outs, scratch, operands):
    def size(shape):
        count = 4
        for extent in shape:
            count *= extent
        return count

    sized = [array for array in (*scratch, *outs, *operands) if hasattr(array, "shape")]
    asked = 8 * 2**20 + sum(size(array.shape) for array in sized)
    return pl.pallas_call(
        kernel,
        out_shape=tuple(outs),
        in_specs=[pl.BlockSpec(memory_space=pltpu.VMEM)] * len(operands),
        out_specs=tuple([pl.BlockSpec(memory_space=pltpu.VMEM)] * len(outs)),
        scratch_shapes=scratch,
        compiler_params=pltpu.CompilerParams(vmem_limit_bytes=asked),
    )(*operands)


def on_device(iterate, source, phase_field, block_owner):
    layers, height, depth = iterate.shape
    half, quarter = height // 2, height // 4
    blocks = lax.axis_size("gx")
    window = layers + 2
    padded, padded2, padded3 = height + 2 * PAD, half + 2 * PAD, quarter + 2 * PAD
    inputs = sum(
        jnp.pad(block, ((k * layers, (2 - k) * layers), (0, 0), (0, 0)))
        for k, block in enumerate((iterate, source, phase_field))
    )
    sent = call(edge_kernel, [f32(3 * height + half, depth)] * 2, [], (inputs,))
    plain, tall = f32(window, height, depth), f32(window, padded, depth)
    across, within, fx2, *fine = call(
        fine_down_kernel,
        [f32(5, half, depth)] * 2
        + [f32(2, half, depth), tall, f32(window - 1, height, depth), f32(2, height, depth), tall, plain, plain],
        [
            vmem(window, padded, depth), vmem(window, height, depth), vmem(layers, height, depth),
            vmem(2, height, depth),
        ],
        (block_owner, inputs, *swapped(*sent)),
    )
    halos = swapped(across, within)
    plain = f32(3, half, depth)
    slots, *middle = call(
        middle_down_kernel,
        [f32(blocks // 2, 2, quarter, depth), plain, plain, plain, plain, f32(3, padded2, depth), plain, plain],
        [vmem(5, padded2, depth), vmem(3, half, depth), vmem(2, half, depth)],
        (across, fx2, *halos),
    )
    kinds = [list(range(core, blocks, 2)) for core in range(2)]
    same_cores = lax.all_to_all(slots, "gx", 0, 0, axis_index_groups=kinds, tiled=True)
    other_cores = within_chip(same_cores)
    solved, owned = call(
        coarse_kernel,
        [f32(layers, height, depth), f32(1, quarter, depth // 4)],
        [
            vmem(blocks, quarter, depth), vmem(blocks + 1, quarter, depth), vmem(blocks, padded3, depth),
            vmem(blocks, quarter, depth), vmem(blocks, quarter, depth), vmem(blocks, quarter, depth),
            vmem(blocks + 2, padded3, depth), vmem(16, half, depth), vmem(4, blocks // 2, PAD, depth),
            vmem(5, padded2, depth), vmem(3, half, depth), vmem(window, padded, depth), vmem(2, height, depth),
            pltpu.SMEM((blocks,), jnp.int32), pltpu.SemaphoreType.DMA,
        ],
        (block_owner, same_cores, other_cores, *middle, inputs, *fine, *halos),
    )
    return solved, owned


def solution(mesh):
    split = P(("groups", "gx"), None, None)
    return jax.shard_map(
        on_device,
        mesh=mesh,
        in_specs=(split, split, split, P("groups")),
        out_specs=(split, split),
        check_vma=False,
    )
```

```python
import jax
import jax.numpy as jnp
from jax import lax
from jax.experimental import pallas as pl
from jax.experimental.pallas import tpu as pltpu
from jax.sharding import PartitionSpec as P

STIFFNESS = 100.0
EPSILON = 0.01
COARSE_SWEEPS = 4
PAD = 8


def swapped(across, within):
    chips = [(i, i + 1 if i % 2 else i - 1) for i in range(1, lax.axis_size("gx") - 1)]
    return lax.ppermute(across, "gx", chips), within_chip(within)


def within_chip(block):
    return lax.ppermute(block, "gx", [(i, i ^ 1) for i in range(lax.axis_size("gx"))])


def by_side(across, within):
    on_left = lax.axis_index("gx") % 2 == 0
    return jnp.where(on_left, across, within), jnp.where(on_left, within, across)


def store_by_side(across, within, pieces):
    on_left = lax.axis_index("gx") % 2 == 0

    @pl.when(on_left)
    def _():
        for index, left, right in pieces:
            across[index] = left
            within[index] = right

    @pl.when(jnp.logical_not(on_left))
    def _():
        for index, left, right in pieces:
            across[index] = right
            within[index] = left


def lanes_of(shape):
    return lax.broadcasted_iota(jnp.int32, shape, len(shape) - 1)


def rows_of(shape):
    return lax.broadcasted_iota(jnp.int32, shape, len(shape) - 2)


def ahead(values, step, axis):
    return pltpu.roll(values, values.shape[axis] - step, axis)


def behind(values, step, axis):
    return pltpu.roll(values, step, axis)


def with_partner(values, step, axis):
    index = lax.broadcasted_iota(jnp.int32, values.shape, axis)
    partner = jnp.where((index & step) == 0, ahead(values, step, axis), behind(values, step, axis))
    return values + partner


def even_row_sum(scratch, rows):
    return scratch[pl.ds(0, rows, 2), :] + scratch[pl.ds(1, rows, 2), :]


def three_parts(ref):
    third = ref.shape[0] // 3
    return [ref.at[pl.ds(k * third, third)] for k in range(3)]


def edge_kernel(inputs, across, within):
    iterate, source, phase = three_parts(inputs)
    layers, height, depth = iterate.shape
    half = height // 2
    row, lane = rows_of((height, depth)), lanes_of((height, depth))
    even_sum = ((row + lane) & 1) == 0
    odd_lane = (lanes_of((half, depth)) & 1) != 0
    cell = []
    for w in range(layers):
        value = phase[w]
        cell.append(STIFFNESS * (value * value + EPSILON))

    def in_layer(w):
        here, e = cell[w], iterate[w]
        fy = jnp.where(row < height - 1, 0.5 * (here + ahead(here, 1, 0)), 0.0)
        fz = jnp.where(lane < depth - 1, 0.5 * (here + ahead(here, 1, 1)), 0.0)
        fyl, fzl = behind(fy, 1, 0), behind(fz, 1, 1)
        total = fy * ahead(e, 1, 0) + fyl * behind(e, 1, 0)
        return total + fz * ahead(e, 1, 1) + fzl * behind(e, 1, 1), fy + fyl + fz + fzl

    sides = []
    for near, step in ((0, 1), (layers - 1, -1)):
        inner, far = near + step, near + 2 * step
        face_near, face_far = 0.5 * (cell[inner] + cell[near]), 0.5 * (cell[inner] + cell[far])
        total, weight = in_layer(inner)
        total = total + face_near * iterate[near] + face_far * iterate[far]
        updated = (source[inner] + total) / (1.0 + (face_near + face_far + weight))
        total, _ = in_layer(near)
        even = even_sum if near % 2 == 0 else ~even_sum
        known = source[near] + jnp.where(even, total + face_near * iterate[inner], face_near * updated)
        sides.append((cell[near], cell[inner], known, odd_cells(iterate.at[near], half, odd_lane ^ (near % 2 != 0))))
    places = [pl.ds(k * height, height) for k in range(3)] + [pl.ds(3 * height, half)]
    store_by_side(across, within, list(zip(places, *sides)))


def odd_cells(ref, rows, first):
    return jnp.where(first, ref[pl.ds(0, rows, 2), :], ref[pl.ds(1, rows, 2), :])


def into_both_rows(ref, values):
    rows = values.shape[0]
    ref[pl.ds(0, rows, 2), :] = values
    ref[pl.ds(1, rows, 2), :] = values


def fine_down_kernel(
    owner_of, inputs, across_in, within_in,
    across, within, fx2_out, e, fx, fx_outer, fy, fz, inv,
    cell, fzl, held, pair,
):
    iterate, source, phase = three_parts(inputs)
    layers, height, depth = iterate.shape
    window = layers + 2
    position, last = lax.axis_index("gx"), lax.axis_size("gx") - 1
    body = pl.ds(PAD, height)
    up, down = pl.ds(PAD + 1, height), pl.ds(PAD - 1, height)
    row, lane = rows_of((height, depth)), lanes_of((height, depth))
    even_sum = ((row + lane) & 1) == 0
    half = height // 2
    own = range(1, layers + 1)
    outer = ((0, 0), (1, window - 1))

    def part(ref, k):
        return ref[k * height:(k + 1) * height]

    def mask(w, odd):
        return even_sum if (w + odd) % 2 == 1 else ~even_sum

    edge = jnp.zeros((PAD, depth), jnp.float32)
    for w in range(window):
        for padded in (e, fy):
            padded[w, :PAD] = edge
            padded[w, PAD + height:] = edge
        cell[w, PAD + height:] = edge
    halos = [by_side(part(across_in, k), part(within_in, k)) for k in range(3)]
    borders = by_side(across_in[3 * height:], within_in[3 * height:])
    for side, w in outer:
        cell[w, body] = halos[0][side]
        fx_outer[side] = 0.5 * (halos[0][side] + halos[1][side])
        into_both_rows(pair.at[side], borders[side])
        e[w, body] = pair[side]
    for w in own:
        value = phase[w - 1]
        cell[w, body] = STIFFNESS * (value * value + EPSILON)
        e[w, body] = iterate[w - 1]
    for w in range(window):
        here = cell[w, body]
        if w < window - 1:
            face = 0.5 * (here + cell[w + 1, body])
            if w == 0:
                face = jnp.where(position > 0, face, 0.0)
            if w == window - 2:
                face = jnp.where(position < last, face, 0.0)
            fx[w] = face
        fy[w, body] = jnp.where(row < height - 1, 0.5 * (here + cell[w, up]), 0.0)
        face = jnp.where(lane < depth - 1, 0.5 * (here + ahead(here, 1, 1)), 0.0)
        fz[w] = face
        fzl[w] = behind(face, 1, 1)
    for w in range(window):
        beyond = fx[w] if w < window - 1 else fx_outer[1]
        before = fx[w - 1] if w > 0 else fx_outer[0]
        weight = beyond + before + fy[w, body] + fy[w, down] + fz[w] + fzl[w]
        inv[w] = 1.0 / (1.0 + weight)

    def in_layer(w):
        here = e[w, body]
        total = fy[w, body] * e[w, up] + fy[w, down] * e[w, down]
        return total + fz[w] * ahead(here, 1, 1) + fzl[w] * behind(here, 1, 1)

    def neigh(w):
        return fx[w] * e[w + 1, body] + fx[w - 1] * e[w - 1, body] + in_layer(w)

    def towards_own(side, w):
        return fx[0] * e[1, body] if side == 0 else fx[w - 1] * e[w - 1, body]

    for w in own:
        total = source[w - 1] + neigh(w)
        held[w - 1] = total
        e[w, body] = jnp.where(mask(w, 0), total * inv[w], e[w, body])
    for side, w in outer:
        total = halos[2][side] + towards_own(side, w)
        e[w, body] = jnp.where(mask(w, 0), total * inv[w], e[w, body])
    for side, w in outer:
        total = (halos[2][side] + in_layer(w) + towards_own(side, w)) * inv[w]
        e[w, body] = jnp.where(mask(w, 1), total, e[w, body])
    for w in own:
        total = (source[w - 1] + neigh(w)) * inv[w]
        e[w, body] = jnp.where(mask(w, 1), total, e[w, body])

    lane = lanes_of((half, depth))
    first_of_two = (lane & 1) == 0

    def residual(w):
        return jnp.where(mask(w, 0), source[w - 1] + neigh(w) - held[w - 1], 0.0)

    def slabs(make, reduce_rows, reduce_lanes):
        found = []
        for t in range(2):
            pair[t] = make(1 + 2 * t)
            found.append(reduce_lanes(reduce_rows(pair.at[t])))
        return jnp.where(first_of_two, found[0], found[1])

    def both_rows(scratch):
        return even_row_sum(scratch, half)

    def odd_rows(scratch):
        return scratch[pl.ds(1, half, 2), :]

    def both_lanes(values):
        return with_partner(values, 1, 1)

    def odd_lanes(values):
        return jnp.where(first_of_two, ahead(values, 1, 1), values)

    coarse_source = slabs(lambda w: residual(w) + residual(w + 1), both_rows, both_lanes)
    coarse_fy = slabs(lambda w: fy[w, body] + fy[w + 1, body], odd_rows, both_lanes)
    coarse_fz = slabs(lambda w: fz[w] + fz[w + 1], both_rows, odd_lanes)
    left_fx = slabs(lambda w: fx[w + 1], both_rows, both_lanes)
    right_fx = slabs(lambda w: fx[w - 1], both_rows, both_lanes)
    fx2_out[0], fx2_out[1] = left_fx, right_fx
    known = []
    for t, (w, face, inner) in enumerate(((1, 1, 2), (layers, layers - 1, layers - 1))):
        pair[t] = source[w - 1] + fx[face] * e[inner, body]
        known.append(odd_cells(pair.at[t], half, first_of_two if w % 2 == 1 else ~first_of_two))
    pieces = [(0, coarse_source), (2, coarse_fy), (3, coarse_fz)]
    pieces = [(k, value, value) for k, value in pieces]
    store_by_side(across, within, pieces + [(1, left_fx, right_fx), (4, *known)])


def neigh2(e2, fx2, fxl2, fy2, fz2, fzl2, first_of_two, tiles):
    half = fx2.shape[1]
    body, up, down = pl.ds(PAD, half), pl.ds(PAD + 1, half), pl.ds(PAD - 1, half)
    needed = range(tiles[0], tiles[-1] + 3)
    here = {j: e2[j, body] for j in needed}
    after = {j: ahead(here[j], 1, 1) for j in needed}
    before = {j: behind(here[j], 1, 1) for j in needed}
    found = []
    for j in tiles:
        k = j + 1
        upper = jnp.where(first_of_two, after[k], before[k + 1])
        lower = jnp.where(first_of_two, after[k - 1], before[k])
        sums = fx2[j] * upper + fxl2[j] * lower
        sums = sums + fy2[j, body] * e2[k, up] + fy2[j, down] * e2[k, down]
        sums = sums + fz2[j] * ahead(here[k], 2, 1) + fzl2[j] * behind(here[k], 2, 1)
        found.append(sums)
    return found


def parities2(half, lanes):
    row, lane = rows_of((half, lanes)), lanes_of((half, lanes))
    return (lane & 1) == 0, ((row + (lane & 1) + (lane >> 1)) & 1) == 0


def group(values):
    return with_partner(with_partner(values, 1, 1), 2, 1)


def middle_down_kernel(
    own, own_fx, across_in, within_in,
    slots, e2_out, s2, fx2, fxl2, fy2, fz2, inv2,
    e2, fzl2, pair,
):
    _, half, lanes = own.shape
    quarter = half // 2
    position = lax.axis_index("gx")
    first_of_two, even2 = parities2(half, lanes)
    body, down = pl.ds(PAD, half), pl.ds(PAD - 1, half)
    edge = jnp.zeros((PAD, lanes), jnp.float32)
    for j in range(5):
        e2[j] = jnp.zeros((half + 2 * PAD, lanes), jnp.float32)
    def three(k):
        left, right = by_side(across_in[k], within_in[k])
        return left, own[k], right

    for j, (source, fy, fz) in enumerate(zip(three(0), three(2), three(3))):
        s2[j] = source
        fy2[j, :PAD] = edge
        fy2[j, body] = fy
        fy2[j, PAD + half:] = edge
        fz2[j] = fz
        fzl2[j] = behind(fz, 2, 1)
    left_fx, _, right_fx = three(1)
    fx2[0] = jnp.where(first_of_two, ahead(left_fx, 1, 1), behind(own_fx[1], 1, 1))
    fx2[1] = own_fx[0]
    fx2[2] = right_fx
    fxl2[0] = left_fx
    fxl2[1] = own_fx[1]
    fxl2[2] = jnp.where(first_of_two, ahead(own_fx[0], 1, 1), behind(right_fx, 1, 1))
    for j in range(3):
        weight = fx2[j] + fxl2[j] + fy2[j, body] + fy2[j, down] + fz2[j] + fzl2[j]
        inverse = 1.0 / (8.0 + weight)
        inv2[j] = inverse
        e2[j + 1, body] = jnp.where(even2, s2[j] * inverse, 0.0)

    def neigh(tiles):
        return neigh2(e2, fx2, fxl2, fy2, fz2, fzl2, first_of_two, tiles)

    fresh = [
        jnp.where(even2, e2[j + 1, body], (s2[j] + sums) * inv2[j]) for j, sums in enumerate(neigh((0, 1, 2)))
    ]
    for j in range(3):
        e2[j + 1, body] = fresh[j]
        e2_out[j] = fresh[j]
    pair[0] = jnp.where(even2, neigh((1,))[0], 0.0)
    lane = lanes_of((quarter, lanes))
    odd_layer, odd_depth, item = (lane & 1) != 0, (lane & 2) != 0, (lane - position) & 3
    source = group(even_row_sum(pair.at[0], quarter))
    fx = group(jnp.where(odd_layer, even_row_sum(fx2.at[1], quarter), 0.0))
    fy = group(fy2[1, pl.ds(PAD + 1, quarter, 2), :])
    fz = group(jnp.where(odd_depth, even_row_sum(fz2.at[1], quarter), 0.0))
    tile = jnp.where(item == 0, source, jnp.where(item == 1, fx, jnp.where(item == 2, fy, fz)))
    first = (((lane & 1) + (lane >> 1)) & 1) != 0
    pair[0] = jnp.where(first_of_two, fresh[2], fresh[1])
    pair[1] = jnp.where(first_of_two, fresh[1], fresh[0])
    for_left = odd_cells(pair.at[0], quarter, first)
    for_right = odd_cells(pair.at[1], quarter, first)
    for c in range(slots.shape[0]):
        slots[c, 0] = tile
        slots[c, 1] = jnp.where(position < 2 * c + 1 - position % 2, for_right, for_left)


class Level:
    def __init__(self, mass, source, faces, row_step, lane_step):
        self.source, self.row_step, self.lane_step = source, row_step, lane_step
        self.fx, self.fy, self.fz = faces
        self.layers = source.shape[0]
        self.setup()
        self.fxl = self.lower(self.fx)
        self.fyl = behind(self.fy, row_step, 1)
        self.fzl = behind(self.fz, lane_step, 2)
        weight = (self.fx + self.fxl) + (self.fy + self.fyl) + (self.fz + self.fzl)
        self.inv = 1.0 / (mass + weight)

    def setup(self):
        shape = self.source.shape
        total = lax.broadcasted_iota(jnp.int32, shape, 0)
        total = total + rows_of(shape) // self.row_step + lanes_of(shape) // self.lane_step
        self.even = (total & 1) == 0

    def upper(self, e):
        return jnp.concatenate([e[1:], jnp.zeros_like(e[:1])], 0)

    def lower(self, e):
        return jnp.concatenate([jnp.zeros_like(e[:1]), e[:-1]], 0)

    def neigh(self, e):
        total = self.fx * self.upper(e) + self.fxl * self.lower(e)
        total = total + self.fy * ahead(e, self.row_step, 1) + self.fyl * behind(e, self.row_step, 1)
        return total + self.fz * ahead(e, self.lane_step, 2) + self.fzl * behind(e, self.lane_step, 2)

    def update(self, e):
        return (self.source + self.neigh(e)) * self.inv

    def cycle(self, deeper):
        odd = self.update(self.source * self.inv)
        residual = jnp.where(self.even, self.neigh(odd), 0.0)
        fix = deeper(self.restricted(residual), self.coarse_faces())
        even = self.update(odd + self.prolonged(fix))
        return jnp.where(self.even, even, self.update(even))

    def pairs(self, values):
        halves = values.reshape(self.layers // 2, 2, *values.shape[1:])
        return halves[:, 0] + halves[:, 1]

    def in_plane(self, values):
        return with_partner(with_partner(values, self.row_step, 1), self.lane_step, 2)

    def restricted(self, values):
        return self.in_plane(self.pairs(values))

    def coarse_faces(self):
        row_bit = (rows_of(self.fx.shape) & self.row_step) != 0
        lane_bit = (lanes_of(self.fx.shape) & self.lane_step) != 0
        odd_layers = self.fx.reshape(self.layers // 2, 2, *self.fx.shape[1:])[:, 1]
        fy = self.restricted(jnp.where(row_bit, self.fy, 0.0))
        fz = self.restricted(jnp.where(lane_bit, self.fz, 0.0))
        return self.in_plane(odd_layers), fy, fz

    def prolonged(self, fix):
        both = jnp.concatenate([fix[:, None], fix[:, None]], 1)
        return both.reshape(self.layers, *fix.shape[1:])


class Packed(Level):
    def __init__(self, mass, source, faces, scratch):
        self.scratch = scratch
        super().__init__(mass, source, faces, 1, 4)

    def setup(self):
        shape = self.source.shape
        lane = lanes_of(shape)
        self.slot = lane & 3
        self.even = ((rows_of(shape) + self.slot + (lane >> 2)) & 1) == 0

    def upper(self, e):
        return jnp.where(self.slot == 3, super().upper(behind(e, 3, 2)), ahead(e, 1, 2))

    def lower(self, e):
        return jnp.where(self.slot == 0, super().lower(ahead(e, 3, 2)), behind(e, 1, 2))

    def rows_once(self, ref, start):
        rows = ref.shape[1] // 2
        return jnp.concatenate([ref[j, pl.ds(start, rows, 2), :][None] for j in range(self.layers)], 0)

    def opened(self, values):
        values = with_partner(with_partner(values, 1, 2), 4, 2)
        second = (lanes_of(values.shape) & 2) != 0
        one, two = jnp.where(second, behind(values, 2, 2), values), jnp.where(second, values, ahead(values, 2, 2))
        both = jnp.concatenate([one[:, None], two[:, None]], 1)
        return both.reshape(2 * self.layers, *values.shape[1:])

    def restricted(self, values):
        self.scratch[0] = values
        return self.opened(self.rows_once(self.scratch.at[0], 0) + self.rows_once(self.scratch.at[0], 1))

    def coarse_faces(self):
        lane_bit = (lanes_of(self.fx.shape) & 4) != 0
        self.scratch[1] = jnp.where((self.slot & 1) != 0, self.fx, 0.0)
        self.scratch[2] = self.fy
        self.scratch[3] = jnp.where(lane_bit, self.fz, 0.0)
        fx, fz = [self.rows_once(self.scratch.at[k], 0) + self.rows_once(self.scratch.at[k], 1) for k in (1, 3)]
        return self.opened(fx), self.opened(self.rows_once(self.scratch.at[2], 1)), self.opened(fz)

    def prolonged(self, fix):
        halves = fix.reshape(self.layers, 2, *fix.shape[1:])
        packed = jnp.where((lanes_of(halves[:, 0].shape) & 2) == 0, halves[:, 0], halves[:, 1])
        for j in range(self.layers):
            into_both_rows(self.scratch.at[0, j], packed[j])
        return self.scratch[0]


def coarsest(mass, source, faces, row_step, lane_step):
    level = Level(mass, source, faces, row_step, lane_step)
    rows, lanes = source.shape[1] // row_step, source.shape[2] // lane_step
    frames = [(m, k) for m in range(rows) for k in range(lanes)]

    def spread(values):
        copies = {}
        for m in range(rows):
            turned = behind(values, m * row_step, 1) if m else values
            for k in range(lanes):
                copies[m, k] = behind(turned, k * lane_step, 2) if k else turned
        return copies

    inv = level.inv
    start, fx, fxl, fy, fyl, fz, fzl = [
        spread(values * inv)
        for values in (source, level.fx, level.fxl, level.fy, level.fyl, level.fz, level.fzl)
    ]

    def update(e):
        fresh = {}
        for m, k in frames:
            here = e[m, k]
            total = start[m, k] + fx[m, k] * level.upper(here) + fxl[m, k] * level.lower(here)
            total = total + (fy[m, k] * e[(m - 1) % rows, k] + fyl[m, k] * e[(m + 1) % rows, k])
            fresh[m, k] = total + (fz[m, k] * e[m, (k - 1) % lanes] + fzl[m, k] * e[m, (k + 1) % lanes])
        return fresh

    even = start
    odd = update(even)
    for turn in range(COARSE_SWEEPS - 1):
        even = update(odd)
        odd = update(even)
    return jnp.where(level.even, even[0, 0], odd[0, 0])


def small_cycle(mass, source, faces, row_step, lane_step, between):
    if between == 0:
        return coarsest(mass, source, faces, row_step, lane_step)
    level = Level(mass, source, faces, row_step, lane_step)
    return level.cycle(
        lambda inner, inner_faces: small_cycle(
            8.0 * mass, inner, inner_faces, 2 * row_step, 2 * lane_step, between - 1
        )
    )


def coarse_kernel(
    owner_of, same_cores, other_cores, e2_in, s2, fx2, fxl2, fy2, fz2, inv2,
    inputs, field, fx_in, fx_outer, fy_in, fz_in, inv_in, across_in, within_in,
    solved_out, owned_out,
    e3, turn3, pair, e2, fzl2, e1, cor, solved, owned, owner_here, fetch_sem, sems,
):
    fetch = pltpu.make_async_copy(owner_of, owner_here, fetch_sem)
    fetch.start()
    chips, _, quarter, lanes = same_cores.shape
    blocks = 2 * chips
    half, height = 2 * quarter, 4 * quarter
    position, last = lax.axis_index("gx"), blocks - 1

    slot = lanes_of((quarter, lanes)) & 3
    tiles = []
    for chip in range(chips):
        tiles.extend(by_side(same_cores[chip, 0], other_cores[chip, 0]))
    items = []
    for k in range(4):
        packs = []
        for j in range(0, blocks, 4):
            value = tiles[j + (3 - k) % 4]
            for at in range(3):
                value = jnp.where(slot == at, tiles[j + (at - k) % 4], value)
            if k:
                value = jnp.where(slot < 4 - k, ahead(value, k, 1), behind(value, 4 - k, 1))
            packs.append(value[None])
        items.append(jnp.concatenate(packs, 0))
    third = Packed(64.0, items[0], items[1:], turn3)
    e3[...] = third.cycle(lambda inner, faces: small_cycle(512.0, inner, faces, 1, 8, 2))

    fetch.wait()
    owner = owner_here[position]
    wide, narrow = lanes_of((lanes, lanes)), rows_of((lanes, lanes))
    take = jnp.where(narrow == 4 * wide + owner % 4, 1.0, 0.0)
    block = jnp.dot(
        e3[owner // 4], take, precision=lax.Precision.HIGHEST, preferred_element_type=jnp.float32
    )
    owned[0] = block[:, : lanes // 4]
    copies = [pltpu.make_async_copy(owned, owned_out, sems.at[0])]
    copies[0].start()

    first_of_two, even2 = parities2(half, lanes)
    body2 = pl.ds(PAD, half)
    edge = jnp.zeros((PAD, lanes), jnp.float32)
    left = other_cores[jnp.maximum(position - 1, 0) // 2, 1]
    right = other_cores[jnp.minimum(position + 1, last) // 2, 1]
    into_both_rows(pair.at[5], left)
    into_both_rows(pair.at[6], right)
    left, right = pair[5], pair[6]
    before = (
        left, jnp.where(first_of_two, left, e2_in[0]), e2_in[1], jnp.where(first_of_two, e2_in[2], right), right
    )
    for k in range(5):
        j = jnp.clip(position + k - 2, 0, last)
        into_both_rows(pair.at[k], group(jnp.where(slot == j % 4, e3[j // 4], 0.0)))
        e2[k, :PAD] = edge
        e2[k, PAD + half:] = edge
        e2[k, body2] = before[k] + pair[k]
    for j in range(3):
        fzl2[j] = behind(fz2[j], 2, 1)

    def update2():
        sums = neigh2(e2, fx2, fxl2, fy2, fz2, fzl2, first_of_two, (0, 1, 2))
        return [(s2[j] + sums[j]) * inv2[j] for j in range(3)]

    fresh = update2()
    for j in range(3):
        e2[j + 1, body2] = fresh[j]
    fixes2 = [jnp.where(even2, even, odd) for even, odd in zip(fresh, update2())]

    _, source, _ = three_parts(inputs)
    body1, up1, down1 = pl.ds(PAD, height), pl.ds(PAD + 1, height), pl.ds(PAD - 1, height)
    rows, lane = rows_of((height, lanes)), lanes_of((height, lanes))
    even_sum = ((rows + lane) & 1) == 0
    count = e1.shape[0]
    fixes = []
    for w in range(count):
        tile, t = divmod((w - 1) // 2, 2)
        packed = fixes2[1 + tile]
        if w % 2 == 1 or w == 0:
            if t == 0:
                plain = jnp.where(first_of_two, packed, behind(packed, 1, 1))
            else:
                plain = jnp.where(first_of_two, ahead(packed, 1, 1), packed)
            into_both_rows(cor.at[len(fixes)], plain)
            fixes.append(cor[len(fixes)])
        e1[w, :PAD] = edge
        e1[w, PAD + height:] = edge
        e1[w, body1] = field[w, body1] + fixes[-1]

    def in_layer1(w):
        here, face = e1[w, body1], fz_in[w]
        sums = fy_in[w, body1] * e1[w, up1] + fy_in[w, down1] * e1[w, down1]
        return sums + face * ahead(here, 1, 1) + behind(face, 1, 1) * behind(here, 1, 1)

    def smoothed1(w, odd):
        keep = even_sum if (w + odd) % 2 == 0 else ~even_sum
        sums = fx_in[w] * e1[w + 1, body1] + fx_in[w - 1] * e1[w - 1, body1] + in_layer1(w)
        return jnp.where(keep, e1[w, body1], (source[w - 1] + sums) * inv_in[w])

    borders = by_side(across_in[4], within_in[4])
    for w in range(1, count - 1):
        e1[w, body1] = smoothed1(w, 0)
    for side, w, near in ((0, 0, 1), (1, count - 1, count - 2)):
        into_both_rows(cor.at[4 + side], borders[side])
        sums = cor[4 + side] + fx_outer[side] * fixes[0 if side == 0 else -1]
        sums = sums + fx_in[min(w, near)] * e1[near, body1] + in_layer1(w)
        e1[w, body1] = sums * inv_in[w]
    for w in range(1, count - 1):
        solved[w - 1] = smoothed1(w, 1)
        copies.append(pltpu.make_async_copy(solved.at[w - 1], solved_out.at[w - 1], sems.at[w]))
        copies[-1].start()
    for copy in copies:
        copy.wait()


def f32(*shape):
    return jax.ShapeDtypeStruct(shape, jnp.float32)


def vmem(*shape):
    return pltpu.VMEM(shape, jnp.float32)


def call(kernel, outs, scratch, operands, out_space=pltpu.VMEM):
    def size(shape):
        count = 4
        for extent in shape:
            count *= extent
        return count

    sized = [array for array in (*scratch, *outs, *operands) if hasattr(array, "shape")]
    asked = 8 * 2**20 + sum(size(array.shape) for array in sized)
    return pl.pallas_call(
        kernel,
        out_shape=tuple(outs),
        in_specs=[pl.BlockSpec(memory_space=pltpu.VMEM)] * len(operands),
        out_specs=tuple([pl.BlockSpec(memory_space=out_space)] * len(outs)),
        scratch_shapes=scratch,
        compiler_params=pltpu.CompilerParams(vmem_limit_bytes=asked),
    )(*operands)


def on_device(iterate, source, phase_field, block_owner):
    layers, height, depth = iterate.shape
    half, quarter = height // 2, height // 4
    blocks = lax.axis_size("gx")
    window = layers + 2
    padded, padded2 = height + 2 * PAD, half + 2 * PAD
    inputs = sum(
        jnp.pad(block, ((k * layers, (2 - k) * layers), (0, 0), (0, 0)))
        for k, block in enumerate((iterate, source, phase_field))
    )
    sent = call(edge_kernel, [f32(3 * height + half, depth)] * 2, [], (inputs,))
    plain, tall = f32(window, height, depth), f32(window, padded, depth)
    across, within, fx2, *fine = call(
        fine_down_kernel,
        [f32(5, half, depth)] * 2
        + [f32(2, half, depth), tall, f32(window - 1, height, depth), f32(2, height, depth), tall, plain, plain],
        [
            vmem(window, padded, depth), vmem(window, height, depth), vmem(layers, height, depth),
            vmem(2, height, depth),
        ],
        (block_owner, inputs, *swapped(*sent)),
    )
    halos = swapped(across, within)
    plain = f32(3, half, depth)
    slots, *middle = call(
        middle_down_kernel,
        [f32(blocks // 2, 2, quarter, depth), plain, plain, plain, plain, f32(3, padded2, depth), plain, plain],
        [vmem(5, padded2, depth), vmem(3, half, depth), vmem(2, half, depth)],
        (across, fx2, *halos),
    )
    kinds = [list(range(core, blocks, 2)) for core in range(2)]
    same_cores = lax.all_to_all(slots, "gx", 0, 0, axis_index_groups=kinds, tiled=True)
    other_cores = within_chip(same_cores)
    solved, owned = call(
        coarse_kernel,
        [f32(layers, height, depth), f32(1, quarter, depth // 4)],
        [
            vmem(blocks // 4, quarter, depth), vmem(4, blocks // 4, quarter, depth), vmem(7, half, depth),
            vmem(5, padded2, depth), vmem(3, half, depth), vmem(window, padded, depth), vmem(6, height, depth),
            vmem(layers, height, depth), vmem(1, quarter, depth // 4), pltpu.SMEM((blocks,), jnp.int32),
            pltpu.SemaphoreType.DMA, pltpu.SemaphoreType.DMA((layers + 1,)),
        ],
        (block_owner, same_cores, other_cores, *middle, inputs, *fine, *halos),
        pl.ANY,
    )
    return solved, owned


def solution(mesh):
    split = P(("groups", "gx"), None, None)
    return jax.shard_map(
        on_device,
        mesh=mesh,
        in_specs=(split, split, split, P("groups")),
        out_specs=(split, split),
        check_vma=False,
    )
```

```python
import jax
import jax.numpy as jnp
from jax import lax
from jax.experimental import pallas as pl
from jax.experimental.pallas import tpu as pltpu
from jax.sharding import PartitionSpec as P

STIFFNESS = 100.0
EPSILON = 0.01
COARSE_SWEEPS = 4
PAD = 8


def swapped(across, within):
    chips = [(i, i + 1 if i % 2 else i - 1) for i in range(1, lax.axis_size("gx") - 1)]
    return lax.ppermute(across, "gx", chips), within_chip(within)


def within_chip(block):
    return lax.ppermute(block, "gx", [(i, i ^ 1) for i in range(lax.axis_size("gx"))])


def by_side(across, within):
    on_left = lax.axis_index("gx") % 2 == 0
    return jnp.where(on_left, across, within), jnp.where(on_left, within, across)


def store_by_side(across, within, pieces):
    on_left = lax.axis_index("gx") % 2 == 0

    @pl.when(on_left)
    def _():
        for index, left, right in pieces:
            across[index] = left
            within[index] = right

    @pl.when(jnp.logical_not(on_left))
    def _():
        for index, left, right in pieces:
            across[index] = right
            within[index] = left


def lanes_of(shape):
    return lax.broadcasted_iota(jnp.int32, shape, len(shape) - 1)


def rows_of(shape):
    return lax.broadcasted_iota(jnp.int32, shape, len(shape) - 2)


def ahead(values, step, axis):
    return pltpu.roll(values, values.shape[axis] - step, axis)


def behind(values, step, axis):
    return pltpu.roll(values, step, axis)


def with_partner(values, step, axis):
    index = lax.broadcasted_iota(jnp.int32, values.shape, axis)
    partner = jnp.where((index & step) == 0, ahead(values, step, axis), behind(values, step, axis))
    return values + partner


def even_row_sum(scratch, rows):
    return scratch[pl.ds(0, rows, 2), :] + scratch[pl.ds(1, rows, 2), :]


def three_parts(ref):
    third = ref.shape[0] // 3
    return [ref.at[pl.ds(k * third, third)] for k in range(3)]


def edge_kernel(inputs, across, within):
    iterate, source, phase = three_parts(inputs)
    layers, height, depth = iterate.shape
    half = height // 2
    row, lane = rows_of((height, depth)), lanes_of((height, depth))
    even_sum = ((row + lane) & 1) == 0
    odd_lane = (lanes_of((half, depth)) & 1) != 0
    cell = []
    for w in range(layers):
        value = phase[w]
        cell.append(STIFFNESS * (value * value + EPSILON))

    def in_layer(w):
        here, e = cell[w], iterate[w]
        fy = jnp.where(row < height - 1, 0.5 * (here + ahead(here, 1, 0)), 0.0)
        fz = jnp.where(lane < depth - 1, 0.5 * (here + ahead(here, 1, 1)), 0.0)
        fyl, fzl = behind(fy, 1, 0), behind(fz, 1, 1)
        total = fy * ahead(e, 1, 0) + fyl * behind(e, 1, 0)
        return total + fz * ahead(e, 1, 1) + fzl * behind(e, 1, 1), fy + fyl + fz + fzl

    sides = []
    for near, step in ((0, 1), (layers - 1, -1)):
        inner, far = near + step, near + 2 * step
        face_near, face_far = 0.5 * (cell[inner] + cell[near]), 0.5 * (cell[inner] + cell[far])
        total, weight = in_layer(inner)
        total = total + face_near * iterate[near] + face_far * iterate[far]
        updated = (source[inner] + total) / (1.0 + (face_near + face_far + weight))
        total, _ = in_layer(near)
        even = even_sum if near % 2 == 0 else ~even_sum
        known = source[near] + jnp.where(even, total + face_near * iterate[inner], face_near * updated)
        sides.append((cell[near], cell[inner], known, odd_cells(iterate.at[near], half, odd_lane ^ (near % 2 != 0))))
    places = [pl.ds(k * height, height) for k in range(3)] + [pl.ds(3 * height, half)]
    store_by_side(across, within, list(zip(places, *sides)))


def odd_cells(ref, rows, first):
    return jnp.where(first, ref[pl.ds(0, rows, 2), :], ref[pl.ds(1, rows, 2), :])


def into_both_rows(ref, values):
    rows = values.shape[0]
    ref[pl.ds(0, rows, 2), :] = values
    ref[pl.ds(1, rows, 2), :] = values


def fine_down_kernel(
    owner_of, inputs, across_in, within_in,
    across, within, fx2_out, e, fx, fx_outer, fy, fz, fzl, inv,
    cell, held, pair,
):
    iterate, source, phase = three_parts(inputs)
    layers, height, depth = iterate.shape
    window = layers + 2
    position, last = lax.axis_index("gx"), lax.axis_size("gx") - 1
    body = pl.ds(PAD, height)
    up, down = pl.ds(PAD + 1, height), pl.ds(PAD - 1, height)
    row, lane = rows_of((height, depth)), lanes_of((height, depth))
    even_sum = ((row + lane) & 1) == 0
    half = height // 2
    own = range(1, layers + 1)
    outer = ((0, 0), (1, window - 1))

    def part(ref, k):
        return ref[k * height:(k + 1) * height]

    def mask(w, odd):
        return even_sum if (w + odd) % 2 == 1 else ~even_sum

    edge = jnp.zeros((PAD, depth), jnp.float32)
    for w in range(window):
        for padded in (e, fy):
            padded[w, :PAD] = edge
            padded[w, PAD + height:] = edge
        cell[w, PAD + height:] = edge
    halos = [by_side(part(across_in, k), part(within_in, k)) for k in range(3)]
    borders = by_side(across_in[3 * height:], within_in[3 * height:])
    for side, w in outer:
        cell[w, body] = halos[0][side]
        fx_outer[side] = 0.5 * (halos[0][side] + halos[1][side])
        into_both_rows(pair.at[side], borders[side])
        e[w, body] = pair[side]
    for w in own:
        value = phase[w - 1]
        cell[w, body] = STIFFNESS * (value * value + EPSILON)
        e[w, body] = iterate[w - 1]
    for w in range(window):
        here = cell[w, body]
        if w < window - 1:
            face = 0.5 * (here + cell[w + 1, body])
            if w == 0:
                face = jnp.where(position > 0, face, 0.0)
            if w == window - 2:
                face = jnp.where(position < last, face, 0.0)
            fx[w] = face
        fy[w, body] = jnp.where(row < height - 1, 0.5 * (here + cell[w, up]), 0.0)
        face = jnp.where(lane < depth - 1, 0.5 * (here + ahead(here, 1, 1)), 0.0)
        fz[w] = face
        fzl[w] = behind(face, 1, 1)
    for w in range(window):
        beyond = fx[w] if w < window - 1 else fx_outer[1]
        before = fx[w - 1] if w > 0 else fx_outer[0]
        weight = beyond + before + fy[w, body] + fy[w, down] + fz[w] + fzl[w]
        inv[w] = 1.0 / (1.0 + weight)

    def in_layer(w):
        here = e[w, body]
        total = fy[w, body] * e[w, up] + fy[w, down] * e[w, down]
        return total + fz[w] * ahead(here, 1, 1) + fzl[w] * behind(here, 1, 1)

    def neigh(w):
        return fx[w] * e[w + 1, body] + fx[w - 1] * e[w - 1, body] + in_layer(w)

    def towards_own(side, w):
        return fx[0] * e[1, body] if side == 0 else fx[w - 1] * e[w - 1, body]

    for w in own:
        total = source[w - 1] + neigh(w)
        held[w - 1] = total
        e[w, body] = jnp.where(mask(w, 0), total * inv[w], e[w, body])
    for side, w in outer:
        total = halos[2][side] + towards_own(side, w)
        e[w, body] = jnp.where(mask(w, 0), total * inv[w], e[w, body])
    for side, w in outer:
        total = (halos[2][side] + in_layer(w) + towards_own(side, w)) * inv[w]
        e[w, body] = jnp.where(mask(w, 1), total, e[w, body])
    for w in own:
        total = (source[w - 1] + neigh(w)) * inv[w]
        e[w, body] = jnp.where(mask(w, 1), total, e[w, body])

    lane = lanes_of((half, depth))
    first_of_two = (lane & 1) == 0

    def residual(w):
        return jnp.where(mask(w, 0), source[w - 1] + neigh(w) - held[w - 1], 0.0)

    def slabs(make, reduce_rows, reduce_lanes):
        found = []
        for t in range(2):
            pair[t] = make(1 + 2 * t)
            found.append(reduce_lanes(reduce_rows(pair.at[t])))
        return jnp.where(first_of_two, found[0], found[1])

    def both_rows(scratch):
        return even_row_sum(scratch, half)

    def odd_rows(scratch):
        return scratch[pl.ds(1, half, 2), :]

    def both_lanes(values):
        return with_partner(values, 1, 1)

    def odd_lanes(values):
        return jnp.where(first_of_two, ahead(values, 1, 1), values)

    coarse_source = slabs(lambda w: residual(w) + residual(w + 1), both_rows, both_lanes)
    coarse_fy = slabs(lambda w: fy[w, body] + fy[w + 1, body], odd_rows, both_lanes)
    coarse_fz = slabs(lambda w: fz[w] + fz[w + 1], both_rows, odd_lanes)
    left_fx = slabs(lambda w: fx[w + 1], both_rows, both_lanes)
    right_fx = slabs(lambda w: fx[w - 1], both_rows, both_lanes)
    fx2_out[0], fx2_out[1] = left_fx, right_fx
    known = []
    for t, (w, face, inner) in enumerate(((1, 1, 2), (layers, layers - 1, layers - 1))):
        pair[t] = source[w - 1] + fx[face] * e[inner, body]
        known.append(odd_cells(pair.at[t], half, first_of_two if w % 2 == 1 else ~first_of_two))
    pieces = [(0, coarse_source), (2, coarse_fy), (3, coarse_fz)]
    pieces = [(k, value, value) for k, value in pieces]
    store_by_side(across, within, pieces + [(1, left_fx, right_fx), (4, *known)])


def neigh2(e2, fx2, fxl2, fy2, fz2, fzl2, first_of_two, tiles):
    half = fx2.shape[1]
    body, up, down = pl.ds(PAD, half), pl.ds(PAD + 1, half), pl.ds(PAD - 1, half)
    needed = range(tiles[0], tiles[-1] + 3)
    here = {j: e2[j, body] for j in needed}
    after = {j: ahead(here[j], 1, 1) for j in needed}
    before = {j: behind(here[j], 1, 1) for j in needed}
    found = []
    for j in tiles:
        k = j + 1
        upper = jnp.where(first_of_two, after[k], before[k + 1])
        lower = jnp.where(first_of_two, after[k - 1], before[k])
        sums = fx2[j] * upper + fxl2[j] * lower
        sums = sums + fy2[j, body] * e2[k, up] + fy2[j, down] * e2[k, down]
        sums = sums + fz2[j] * ahead(here[k], 2, 1) + fzl2[j] * behind(here[k], 2, 1)
        found.append(sums)
    return found


def parities2(half, lanes):
    row, lane = rows_of((half, lanes)), lanes_of((half, lanes))
    return (lane & 1) == 0, ((row + (lane & 1) + (lane >> 1)) & 1) == 0


def group(values):
    return with_partner(with_partner(values, 1, 1), 2, 1)


def middle_down_kernel(
    own, own_fx, across_in, within_in,
    slots, e2_out, s2, fx2, fxl2, fy2, fz2, fzl2, inv2,
    e2, pair,
):
    _, half, lanes = own.shape
    quarter = half // 2
    position = lax.axis_index("gx")
    first_of_two, even2 = parities2(half, lanes)
    body, down = pl.ds(PAD, half), pl.ds(PAD - 1, half)
    edge = jnp.zeros((PAD, lanes), jnp.float32)
    for j in range(5):
        e2[j] = jnp.zeros((half + 2 * PAD, lanes), jnp.float32)
    def three(k):
        left, right = by_side(across_in[k], within_in[k])
        return left, own[k], right

    for j, (source, fy, fz) in enumerate(zip(three(0), three(2), three(3))):
        s2[j] = source
        fy2[j, :PAD] = edge
        fy2[j, body] = fy
        fy2[j, PAD + half:] = edge
        fz2[j] = fz
        fzl2[j] = behind(fz, 2, 1)
    left_fx, _, right_fx = three(1)
    fx2[0] = jnp.where(first_of_two, ahead(left_fx, 1, 1), behind(own_fx[1], 1, 1))
    fx2[1] = own_fx[0]
    fx2[2] = right_fx
    fxl2[0] = left_fx
    fxl2[1] = own_fx[1]
    fxl2[2] = jnp.where(first_of_two, ahead(own_fx[0], 1, 1), behind(right_fx, 1, 1))
    for j in range(3):
        weight = fx2[j] + fxl2[j] + fy2[j, body] + fy2[j, down] + fz2[j] + fzl2[j]
        inverse = 1.0 / (8.0 + weight)
        inv2[j] = inverse
        e2[j + 1, body] = jnp.where(even2, s2[j] * inverse, 0.0)

    def neigh(tiles):
        return neigh2(e2, fx2, fxl2, fy2, fz2, fzl2, first_of_two, tiles)

    fresh = [
        jnp.where(even2, e2[j + 1, body], (s2[j] + sums) * inv2[j]) for j, sums in enumerate(neigh((0, 1, 2)))
    ]
    for j in range(3):
        e2[j + 1, body] = fresh[j]
        e2_out[j] = fresh[j]
    pair[0] = jnp.where(even2, neigh((1,))[0], 0.0)
    lane = lanes_of((quarter, lanes))
    slot = position // (slots.shape[0] // 2)
    odd_layer, odd_depth, item = (lane & 1) != 0, (lane & 2) != 0, (lane - slot) & 3
    source = group(even_row_sum(pair.at[0], quarter))
    fx = group(jnp.where(odd_layer, even_row_sum(fx2.at[1], quarter), 0.0))
    fy = group(fy2[1, pl.ds(PAD + 1, quarter, 2), :])
    fz = group(jnp.where(odd_depth, even_row_sum(fz2.at[1], quarter), 0.0))
    tile = jnp.where(item == 0, source, jnp.where(item == 1, fx, jnp.where(item == 2, fy, fz)))
    first = (((lane & 1) + (lane >> 1)) & 1) != 0
    pair[0] = jnp.where(first_of_two, fresh[2], fresh[1])
    pair[1] = jnp.where(first_of_two, fresh[1], fresh[0])
    for_left = odd_cells(pair.at[0], quarter, first)
    for_right = odd_cells(pair.at[1], quarter, first)
    for c in range(slots.shape[0]):
        slots[c, 0] = tile
        slots[c, 1] = jnp.where(position < 2 * c + 1 - position % 2, for_right, for_left)


def joined(one, two):
    return jnp.concatenate([part for part in (one, two) if part.shape[0]], 0)


class Level:
    def __init__(self, mass, source, faces, row_step, lane_step, slot_step):
        self.source, self.row_step, self.lane_step, self.slot_step = source, row_step, lane_step, slot_step
        self.fx, self.fy, self.fz = faces
        self.tiles = source.shape[0]
        shape = source.shape
        self.lane = lanes_of(shape)
        layer = lax.broadcasted_iota(jnp.int32, shape, 0) if self.tiles > 1 else self.lane // slot_step
        self.even = ((layer + rows_of(shape) // row_step + self.lane // lane_step) & 1) == 0
        self.fxl = self.lower(self.fx)
        self.fyl = self.row_shifts(self.fy)[1]
        self.fzl = behind(self.fz, lane_step, 2)
        weight = (self.fx + self.fxl) + (self.fy + self.fyl) + (self.fz + self.fzl)
        self.inv = 1.0 / (mass + weight)

    def upper(self, e):
        return joined(e[1:], ahead(e[:1], self.slot_step, 2))

    def lower(self, e):
        return joined(behind(e[-1:], self.slot_step, 2), e[:-1])

    def row_shifts(self, e):
        return ahead(e, self.row_step, 1), behind(e, self.row_step, 1)

    def neigh(self, e):
        above, below = self.row_shifts(e)
        total = (self.fx * self.upper(e) + self.fxl * self.lower(e)) + (self.fy * above + self.fyl * below)
        return total + (self.fz * ahead(e, self.lane_step, 2) + self.fzl * behind(e, self.lane_step, 2))

    def update(self, e):
        return (self.source + self.neigh(e)) * self.inv

    def cycle(self, deeper):
        odd = self.update(self.source * self.inv)
        residual = jnp.where(self.even, self.neigh(odd), 0.0)
        fix = deeper(self.restricted(residual), self.coarse_faces())
        even = self.update(odd + self.prolonged(fix))
        return jnp.where(self.even, even, self.update(even))

    def coarse_slot_step(self):
        return self.slot_step if self.tiles > 1 else 2 * self.slot_step

    def pairs(self, values):
        if self.tiles == 1:
            return with_partner(values, self.slot_step, 2)
        halves = values.reshape(self.tiles // 2, 2, *values.shape[1:])
        return halves[:, 0] + halves[:, 1]

    def odd_layers(self, values):
        if self.tiles == 1:
            return with_partner(jnp.where((self.lane & self.slot_step) != 0, values, 0.0), self.slot_step, 2)
        return values.reshape(self.tiles // 2, 2, *values.shape[1:])[:, 1]

    def row_pairs(self, values):
        return with_partner(values, self.row_step, 1)

    def odd_rows(self, values):
        odd = (rows_of(values.shape) & self.row_step) != 0
        return with_partner(jnp.where(odd, values, 0.0), self.row_step, 1)

    def restricted(self, values):
        return with_partner(self.row_pairs(self.pairs(values)), self.lane_step, 2)

    def coarse_faces(self):
        fx = with_partner(self.row_pairs(self.odd_layers(self.fx)), self.lane_step, 2)
        fy = with_partner(self.odd_rows(self.pairs(self.fy)), self.lane_step, 2)
        return fx, fy, self.restricted(jnp.where((self.lane & self.lane_step) != 0, self.fz, 0.0))

    def prolonged(self, fix):
        if self.tiles == 1:
            return fix
        both = jnp.concatenate([fix[:, None], fix[:, None]], 1)
        return both.reshape(self.tiles, *fix.shape[1:])


class Rows(Level):
    def __init__(self, mass, source, faces, scratch):
        self.scratch, self.used = scratch, 0
        self.rows = source.shape[1]
        super().__init__(mass, source, faces, 1, 4, 1)

    def place(self):
        self.used += 1
        return self.scratch.at[self.used % self.scratch.shape[0]]

    def row_shifts(self, e):
        place = self.place()
        edge = jnp.zeros((e.shape[0], PAD, e.shape[2]), jnp.float32)
        place[:, :PAD] = edge
        place[:, PAD + self.rows:] = edge
        place[:, pl.ds(PAD, self.rows)] = e
        return place[:, pl.ds(PAD + 1, self.rows)], place[:, pl.ds(PAD - 1, self.rows)]

    def every_other(self, values, starts):
        place, tiles = self.place(), values.shape[0]
        place[:tiles, : self.rows] = values
        found = 0.0
        for start in starts:
            found = found + jnp.concatenate(
                [place[j, pl.ds(start, self.rows // 2, 2), :][None] for j in range(tiles)], 0
            )
        return found

    def row_pairs(self, values):
        return self.every_other(values, (0, 1))

    def odd_rows(self, values):
        return self.every_other(values, (1,))

    def prolonged(self, fix):
        place, tiles = self.place(), fix.shape[0]
        for j in range(tiles):
            into_both_rows(place.at[j, pl.ds(0, self.rows)], fix[j])
        return super().prolonged(place[:tiles, : self.rows])


def coarsest(mass, source, faces, *steps):
    row_step, lane_step, slot_step = steps
    level = Level(mass, source, faces, *steps)
    counts = source.shape[1] // row_step, source.shape[2] // lane_step, 4 // slot_step
    frames = [(m, k, q) for m in range(counts[0]) for k in range(counts[1]) for q in range(counts[2])]
    place = level.lane & 3

    def spread(values):
        copies = {}
        for m, k, q in frames:
            if k:
                copies[m, k, q] = behind(copies[m, 0, q], k * lane_step, 2)
            elif q:
                by = q * slot_step
                one, two = behind(copies[m, 0, 0], by, 2), ahead(copies[m, 0, 0], 4 - by, 2)
                copies[m, k, q] = jnp.where(place >= by, one, two)
            else:
                copies[m, k, q] = behind(values, m * row_step, 1) if m else values
        return copies

    start, inv, fx, fy, fz = [spread(values) for values in (source * level.inv, level.inv, level.fx, level.fy, level.fz)]

    def shifted(copies, frame, axis, by):
        moved = list(frame)
        moved[axis] = (frame[axis] - by) % counts[axis]
        return copies[tuple(moved)]

    def along_x(copies, frame, by):
        here, wrapped = copies[frame], shifted(copies, frame, 2, by)
        return joined(here[1:], wrapped[:1]) if by > 0 else joined(wrapped[-1:], here[:-1])

    weights = {}
    for frame in frames:
        pairs = [
            (fx[frame], along_x(fx, frame, -1)),
            (fy[frame], shifted(fy, frame, 0, -1)),
            (fz[frame], shifted(fz, frame, 1, -1)),
        ]
        weights[frame] = [(up * inv[frame], low * inv[frame]) for up, low in pairs]

    def update(e):
        fresh = {}
        for frame in frames:
            (x_up, x_low), (y_up, y_low), (z_up, z_low) = weights[frame]
            total = x_up * along_x(e, frame, 1) + x_low * along_x(e, frame, -1)
            total = total + (y_up * shifted(e, frame, 0, 1) + y_low * shifted(e, frame, 0, -1))
            total = total + (z_up * shifted(e, frame, 1, 1) + z_low * shifted(e, frame, 1, -1))
            fresh[frame] = start[frame] + total
        return fresh

    even = start
    odd = update(even)
    for turn in range(COARSE_SWEEPS - 1):
        even = update(odd)
        odd = update(even)
    return jnp.where(level.even, even[0, 0, 0], odd[0, 0, 0])


def small_cycle(mass, source, faces, row_step, lane_step, slot_step, between):
    if between == 0:
        return coarsest(mass, source, faces, row_step, lane_step, slot_step)
    level = Level(mass, source, faces, row_step, lane_step, slot_step)
    return level.cycle(
        lambda inner, inner_faces: small_cycle(
            8.0 * mass, inner, inner_faces, 2 * row_step, 2 * lane_step, level.coarse_slot_step(), between - 1
        )
    )


def coarse_kernel(
    owner_of, same_cores, other_cores, e2_in, s2, fx2, fxl2, fy2, fz2, fzl2, inv2,
    inputs, field, fx_in, fx_outer, fy_in, fz_in, fzl_in, inv_in, across_in, within_in,
    solved_out, owned_out,
    e3, rows3, pair, e2, e1, cor, solved, owned, owner_here, fetch_sem, sems,
):
    fetch = pltpu.make_async_copy(owner_of, owner_here, fetch_sem)
    fetch.start()
    chips, _, quarter, lanes = same_cores.shape
    blocks = 2 * chips
    half, height = 2 * quarter, 4 * quarter
    position, last = lax.axis_index("gx"), blocks - 1

    slot = lanes_of((quarter, lanes)) & 3
    spread = blocks // 4
    tiles = []
    for chip in range(chips):
        tiles.extend(by_side(same_cores[chip, 0], other_cores[chip, 0]))
    items = []
    for k in range(4):
        packs = []
        for j in range(spread):
            value = tiles[j + (3 - k) % 4 * spread]
            for at in range(3):
                value = jnp.where(slot == at, tiles[j + (at - k) % 4 * spread], value)
            if k:
                value = jnp.where(slot < 4 - k, ahead(value, k, 1), behind(value, 4 - k, 1))
            packs.append(value[None])
        items.append(jnp.concatenate(packs, 0))
    third = Rows(64.0, items[0], items[1:], rows3)
    e3[...] = third.cycle(
        lambda inner, faces: small_cycle(512.0, inner, faces, 1, 8, third.coarse_slot_step(), 2)
    )

    fetch.wait()
    owner = owner_here[position]
    wide, narrow = lanes_of((lanes, lanes)), rows_of((lanes, lanes))
    take = jnp.where(narrow == 4 * wide + owner // spread, 1.0, 0.0)
    block = jnp.dot(
        e3[owner % spread], take, precision=lax.Precision.HIGHEST, preferred_element_type=jnp.float32
    )
    owned[0] = block[:, : lanes // 4]
    copies = [pltpu.make_async_copy(owned, owned_out, sems.at[0])]
    copies[0].start()

    first_of_two, even2 = parities2(half, lanes)
    body2 = pl.ds(PAD, half)
    edge = jnp.zeros((PAD, lanes), jnp.float32)
    left = other_cores[jnp.maximum(position - 1, 0) // 2, 1]
    right = other_cores[jnp.minimum(position + 1, last) // 2, 1]
    into_both_rows(pair.at[5], left)
    into_both_rows(pair.at[6], right)
    left, right = pair[5], pair[6]
    before = (
        left, jnp.where(first_of_two, left, e2_in[0]), e2_in[1], jnp.where(first_of_two, e2_in[2], right), right
    )
    for k in range(5):
        j = jnp.clip(position + k - 2, 0, last)
        into_both_rows(pair.at[k], group(jnp.where(slot == j // spread, e3[j % spread], 0.0)))
        e2[k, :PAD] = edge
        e2[k, PAD + half:] = edge
        e2[k, body2] = before[k] + pair[k]

    def update2():
        sums = neigh2(e2, fx2, fxl2, fy2, fz2, fzl2, first_of_two, (0, 1, 2))
        return [(s2[j] + sums[j]) * inv2[j] for j in range(3)]

    fresh = update2()
    for j in range(3):
        e2[j + 1, body2] = fresh[j]
    fixes2 = [jnp.where(even2, even, odd) for even, odd in zip(fresh, update2())]

    _, source, _ = three_parts(inputs)
    body1, up1, down1 = pl.ds(PAD, height), pl.ds(PAD + 1, height), pl.ds(PAD - 1, height)
    rows, lane = rows_of((height, lanes)), lanes_of((height, lanes))
    even_sum = ((rows + lane) & 1) == 0
    count = e1.shape[0]
    fixes = []
    for w in range(count):
        tile, t = divmod((w - 1) // 2, 2)
        packed = fixes2[1 + tile]
        if w % 2 == 1 or w == 0:
            if t == 0:
                plain = jnp.where(first_of_two, packed, behind(packed, 1, 1))
            else:
                plain = jnp.where(first_of_two, ahead(packed, 1, 1), packed)
            into_both_rows(cor.at[len(fixes)], plain)
            fixes.append(cor[len(fixes)])
        e1[w, :PAD] = edge
        e1[w, PAD + height:] = edge
        e1[w, body1] = field[w, body1] + fixes[-1]

    def in_layer1(w):
        here = e1[w, body1]
        sums = fy_in[w, body1] * e1[w, up1] + fy_in[w, down1] * e1[w, down1]
        return sums + fz_in[w] * ahead(here, 1, 1) + fzl_in[w] * behind(here, 1, 1)

    def smoothed1(w, odd):
        keep = even_sum if (w + odd) % 2 == 0 else ~even_sum
        sums = fx_in[w] * e1[w + 1, body1] + fx_in[w - 1] * e1[w - 1, body1] + in_layer1(w)
        return jnp.where(keep, e1[w, body1], (source[w - 1] + sums) * inv_in[w])

    borders = by_side(across_in[4], within_in[4])
    for w in range(1, count - 1):
        e1[w, body1] = smoothed1(w, 0)
    for side, w, near in ((0, 0, 1), (1, count - 1, count - 2)):
        into_both_rows(cor.at[4 + side], borders[side])
        sums = cor[4 + side] + fx_outer[side] * fixes[0 if side == 0 else -1]
        sums = sums + fx_in[min(w, near)] * e1[near, body1] + in_layer1(w)
        e1[w, body1] = sums * inv_in[w]
    for w in range(1, count - 1):
        solved[w - 1] = smoothed1(w, 1)
        copies.append(pltpu.make_async_copy(solved.at[w - 1], solved_out.at[w - 1], sems.at[w]))
        copies[-1].start()
    for copy in copies:
        copy.wait()


def f32(*shape):
    return jax.ShapeDtypeStruct(shape, jnp.float32)


def vmem(*shape):
    return pltpu.VMEM(shape, jnp.float32)


def call(kernel, outs, scratch, operands, out_space=pltpu.VMEM):
    def size(shape):
        count = 4
        for extent in shape:
            count *= extent
        return count

    sized = [array for array in (*scratch, *outs, *operands) if hasattr(array, "shape")]
    asked = 8 * 2**20 + sum(size(array.shape) for array in sized)
    return pl.pallas_call(
        kernel,
        out_shape=tuple(outs),
        in_specs=[pl.BlockSpec(memory_space=pltpu.VMEM)] * len(operands),
        out_specs=tuple([pl.BlockSpec(memory_space=out_space)] * len(outs)),
        scratch_shapes=scratch,
        compiler_params=pltpu.CompilerParams(vmem_limit_bytes=asked),
    )(*operands)


def on_device(iterate, source, phase_field, block_owner):
    layers, height, depth = iterate.shape
    half, quarter = height // 2, height // 4
    blocks = lax.axis_size("gx")
    window = layers + 2
    padded, padded2 = height + 2 * PAD, half + 2 * PAD
    inputs = sum(
        jnp.pad(block, ((k * layers, (2 - k) * layers), (0, 0), (0, 0)))
        for k, block in enumerate((iterate, source, phase_field))
    )
    sent = call(edge_kernel, [f32(3 * height + half, depth)] * 2, [], (inputs,))
    plain, tall = f32(window, height, depth), f32(window, padded, depth)
    across, within, fx2, *fine = call(
        fine_down_kernel,
        [f32(5, half, depth)] * 2
        + [f32(2, half, depth), tall, f32(window - 1, height, depth), f32(2, height, depth), tall]
        + [plain] * 3,
        [vmem(window, padded, depth), vmem(layers, height, depth), vmem(2, height, depth)],
        (block_owner, inputs, *swapped(*sent)),
    )
    halos = swapped(across, within)
    plain = f32(3, half, depth)
    slots, *middle = call(
        middle_down_kernel,
        [f32(blocks // 2, 2, quarter, depth), plain, plain, plain, plain, f32(3, padded2, depth)] + [plain] * 3,
        [vmem(5, padded2, depth), vmem(2, half, depth)],
        (across, fx2, *halos),
    )
    kinds = [list(range(core, blocks, 2)) for core in range(2)]
    same_cores = lax.all_to_all(slots, "gx", 0, 0, axis_index_groups=kinds, tiled=True)
    other_cores = within_chip(same_cores)
    solved, owned = call(
        coarse_kernel,
        [f32(layers, height, depth), f32(1, quarter, depth // 4)],
        [
            vmem(blocks // 4, quarter, depth), vmem(4, blocks // 4, quarter + 2 * PAD, depth), vmem(7, half, depth),
            vmem(5, padded2, depth), vmem(window, padded, depth), vmem(6, height, depth),
            vmem(layers, height, depth), vmem(1, quarter, depth // 4), pltpu.SMEM((blocks,), jnp.int32),
            pltpu.SemaphoreType.DMA, pltpu.SemaphoreType.DMA((layers + 1,)),
        ],
        (block_owner, same_cores, other_cores, *middle, inputs, *fine, *halos),
        pl.ANY,
    )
    return solved, owned


def solution(mesh):
    split = P(("groups", "gx"), None, None)
    return jax.shard_map(
        on_device,
        mesh=mesh,
        in_specs=(split, split, split, P("groups")),
        out_specs=(split, split),
        check_vma=False,
    )
```

```python
import jax
import jax.numpy as jnp
from jax import lax
from jax.experimental import pallas as pl
from jax.experimental.pallas import tpu as pltpu
from jax.sharding import PartitionSpec as P

STIFFNESS = 100.0
EPSILON = 0.01
COARSE_SWEEPS = 4
PAD = 8


def between_chips(block):
    return lax.ppermute(block, "gx", [(i, i + 1 if i % 2 else i - 1) for i in range(1, lax.axis_size("gx") - 1)])


def within_chip(block):
    return lax.ppermute(block, "gx", [(i, i ^ 1) for i in range(lax.axis_size("gx"))])


def by_side(across, within):
    on_left = lax.axis_index("gx") % 2 == 0
    return jnp.where(on_left, across, within), jnp.where(on_left, within, across)


def store_by_side(across, within, pieces):
    on_left = lax.axis_index("gx") % 2 == 0

    @pl.when(on_left)
    def _():
        for index, left, right in pieces:
            across[index] = left
            within[index] = right

    @pl.when(jnp.logical_not(on_left))
    def _():
        for index, left, right in pieces:
            across[index] = right
            within[index] = left


def lanes_of(shape):
    return lax.broadcasted_iota(jnp.int32, shape, len(shape) - 1)


def rows_of(shape):
    return lax.broadcasted_iota(jnp.int32, shape, len(shape) - 2)


def ahead(values, step, axis):
    return pltpu.roll(values, values.shape[axis] - step, axis)


def behind(values, step, axis):
    return pltpu.roll(values, step, axis)


def with_partner(values, step, axis):
    index = lax.broadcasted_iota(jnp.int32, values.shape, axis)
    partner = jnp.where((index & step) == 0, ahead(values, step, axis), behind(values, step, axis))
    return values + partner


def even_row_sum(scratch, rows):
    return scratch[pl.ds(0, rows, 2), :] + scratch[pl.ds(1, rows, 2), :]


def three_parts(ref):
    third = ref.shape[0] // 3
    return [ref.at[pl.ds(k * third, third)] for k in range(3)]


def edge_kernel(inputs, across, within):
    iterate, source, phase = three_parts(inputs)
    layers, height, depth = iterate.shape
    half = height // 2
    row, lane = rows_of((height, depth)), lanes_of((height, depth))
    even_sum = ((row + lane) & 1) == 0
    odd_lane = (lanes_of((half, depth)) & 1) != 0
    cell = []
    for w in range(layers):
        value = phase[w]
        cell.append(STIFFNESS * (value * value + EPSILON))

    def in_layer(w):
        here, e = cell[w], iterate[w]
        fy = jnp.where(row < height - 1, 0.5 * (here + ahead(here, 1, 0)), 0.0)
        fz = jnp.where(lane < depth - 1, 0.5 * (here + ahead(here, 1, 1)), 0.0)
        fyl, fzl = behind(fy, 1, 0), behind(fz, 1, 1)
        total = fy * ahead(e, 1, 0) + fyl * behind(e, 1, 0)
        return total + fz * ahead(e, 1, 1) + fzl * behind(e, 1, 1), fy + fyl + fz + fzl

    sides = []
    for near, step in ((0, 1), (layers - 1, -1)):
        inner, far = near + step, near + 2 * step
        face_near, face_far = 0.5 * (cell[inner] + cell[near]), 0.5 * (cell[inner] + cell[far])
        total, weight = in_layer(inner)
        total = total + face_near * iterate[near] + face_far * iterate[far]
        updated = (source[inner] + total) / (1.0 + (face_near + face_far + weight))
        total, _ = in_layer(near)
        even = even_sum if near % 2 == 0 else ~even_sum
        known = source[near] + jnp.where(even, total + face_near * iterate[inner], face_near * updated)
        sides.append((cell[near], cell[inner], known, odd_cells(iterate.at[near], half, odd_lane ^ (near % 2 != 0))))
    places = [pl.ds(k * height, height) for k in range(3)] + [pl.ds(3 * height, half)]
    store_by_side(across, within, list(zip(places, *sides)))


def odd_cells(ref, rows, first):
    return jnp.where(first, ref[pl.ds(0, rows, 2), :], ref[pl.ds(1, rows, 2), :])


def into_both_rows(ref, values):
    rows = values.shape[0]
    ref[pl.ds(0, rows, 2), :] = values
    ref[pl.ds(1, rows, 2), :] = values


def fine_down_kernel(
    owner_of, inputs, across_in, within_in,
    across, within, fx2_out, e, fx, fx_outer, fy, fz, fzl, inv,
    cell, held, pair,
):
    iterate, source, phase = three_parts(inputs)
    layers, height, depth = iterate.shape
    window = layers + 2
    position, last = lax.axis_index("gx"), lax.axis_size("gx") - 1
    body = pl.ds(PAD, height)
    up, down = pl.ds(PAD + 1, height), pl.ds(PAD - 1, height)
    row, lane = rows_of((height, depth)), lanes_of((height, depth))
    even_sum = ((row + lane) & 1) == 0
    half = height // 2
    own = range(1, layers + 1)
    outer = ((0, 0), (1, window - 1))

    def part(ref, k):
        return ref[k * height:(k + 1) * height]

    def mask(w, odd):
        return even_sum if (w + odd) % 2 == 1 else ~even_sum

    edge = jnp.zeros((PAD, depth), jnp.float32)
    for w in range(window):
        for padded in (e, fy):
            padded[w, :PAD] = edge
            padded[w, PAD + height:] = edge
        cell[w, PAD + height:] = edge
    halos = [by_side(part(across_in, k), part(within_in, k)) for k in range(3)]
    borders = by_side(across_in[3 * height:], within_in[3 * height:])
    for side, w in outer:
        cell[w, body] = halos[0][side]
        fx_outer[side] = 0.5 * (halos[0][side] + halos[1][side])
        into_both_rows(pair.at[side], borders[side])
        e[w, body] = pair[side]
    for w in own:
        value = phase[w - 1]
        cell[w, body] = STIFFNESS * (value * value + EPSILON)
        e[w, body] = iterate[w - 1]
    for w in range(window):
        here = cell[w, body]
        if w < window - 1:
            face = 0.5 * (here + cell[w + 1, body])
            if w == 0:
                face = jnp.where(position > 0, face, 0.0)
            if w == window - 2:
                face = jnp.where(position < last, face, 0.0)
            fx[w] = face
        fy[w, body] = jnp.where(row < height - 1, 0.5 * (here + cell[w, up]), 0.0)
        face = jnp.where(lane < depth - 1, 0.5 * (here + ahead(here, 1, 1)), 0.0)
        fz[w] = face
        fzl[w] = behind(face, 1, 1)
    for w in range(window):
        beyond = fx[w] if w < window - 1 else fx_outer[1]
        before = fx[w - 1] if w > 0 else fx_outer[0]
        weight = beyond + before + fy[w, body] + fy[w, down] + fz[w] + fzl[w]
        inv[w] = 1.0 / (1.0 + weight)

    def in_layer(w):
        here = e[w, body]
        total = fy[w, body] * e[w, up] + fy[w, down] * e[w, down]
        return total + fz[w] * ahead(here, 1, 1) + fzl[w] * behind(here, 1, 1)

    def neigh(w):
        return fx[w] * e[w + 1, body] + fx[w - 1] * e[w - 1, body] + in_layer(w)

    def towards_own(side, w):
        return fx[0] * e[1, body] if side == 0 else fx[w - 1] * e[w - 1, body]

    for w in own:
        total = source[w - 1] + neigh(w)
        held[w - 1] = total
        e[w, body] = jnp.where(mask(w, 0), total * inv[w], e[w, body])
    for side, w in outer:
        total = halos[2][side] + towards_own(side, w)
        e[w, body] = jnp.where(mask(w, 0), total * inv[w], e[w, body])
    for side, w in outer:
        total = (halos[2][side] + in_layer(w) + towards_own(side, w)) * inv[w]
        e[w, body] = jnp.where(mask(w, 1), total, e[w, body])
    for w in own:
        total = (source[w - 1] + neigh(w)) * inv[w]
        e[w, body] = jnp.where(mask(w, 1), total, e[w, body])

    lane = lanes_of((half, depth))
    first_of_two = (lane & 1) == 0

    def residual(w):
        return jnp.where(mask(w, 0), source[w - 1] + neigh(w) - held[w - 1], 0.0)

    def slabs(make, reduce_rows, reduce_lanes):
        found = []
        for t in range(2):
            pair[t] = make(1 + 2 * t)
            found.append(reduce_lanes(reduce_rows(pair.at[t])))
        return jnp.where(first_of_two, found[0], found[1])

    def both_rows(scratch):
        return even_row_sum(scratch, half)

    def odd_rows(scratch):
        return scratch[pl.ds(1, half, 2), :]

    def both_lanes(values):
        return with_partner(values, 1, 1)

    def odd_lanes(values):
        return jnp.where(first_of_two, ahead(values, 1, 1), values)

    coarse_source = slabs(lambda w: residual(w) + residual(w + 1), both_rows, both_lanes)
    coarse_fy = slabs(lambda w: fy[w, body] + fy[w + 1, body], odd_rows, both_lanes)
    coarse_fz = slabs(lambda w: fz[w] + fz[w + 1], both_rows, odd_lanes)
    left_fx = slabs(lambda w: fx[w + 1], both_rows, both_lanes)
    right_fx = slabs(lambda w: fx[w - 1], both_rows, both_lanes)
    fx2_out[0], fx2_out[1] = left_fx, right_fx
    known = []
    for t, (w, face, inner) in enumerate(((1, 1, 2), (layers, layers - 1, layers - 1))):
        pair[t] = source[w - 1] + fx[face] * e[inner, body]
        known.append(odd_cells(pair.at[t], half, first_of_two if w % 2 == 1 else ~first_of_two))
    pieces = [(0, coarse_source), (2, coarse_fy), (3, coarse_fz)]
    pieces = [(k, value, value) for k, value in pieces]
    store_by_side(across, within, pieces + [(1, left_fx, right_fx), (4, *known)])


def neigh2(e2, fx2, fxl2, fy2, fz2, fzl2, first_of_two, tiles):
    half = fx2.shape[1]
    body, up, down = pl.ds(PAD, half), pl.ds(PAD + 1, half), pl.ds(PAD - 1, half)
    needed = range(tiles[0], tiles[-1] + 3)
    here = {j: e2[j, body] for j in needed}
    after = {j: ahead(here[j], 1, 1) for j in needed}
    before = {j: behind(here[j], 1, 1) for j in needed}
    found = []
    for j in tiles:
        k = j + 1
        upper = jnp.where(first_of_two, after[k], before[k + 1])
        lower = jnp.where(first_of_two, after[k - 1], before[k])
        sums = fx2[j] * upper + fxl2[j] * lower
        sums = sums + fy2[j, body] * e2[k, up] + fy2[j, down] * e2[k, down]
        sums = sums + fz2[j] * ahead(here[k], 2, 1) + fzl2[j] * behind(here[k], 2, 1)
        found.append(sums)
    return found


def parities2(half, lanes):
    row, lane = rows_of((half, lanes)), lanes_of((half, lanes))
    return (lane & 1) == 0, ((row + (lane & 1) + (lane >> 1)) & 1) == 0


def group(values):
    return with_partner(with_partner(values, 1, 1), 2, 1)


def packed_odd(values, pair):
    half, lanes = values.shape
    lane = lanes_of((half // 2, lanes))
    pair[...] = values
    return odd_cells(pair, half // 2, (((lane & 1) + (lane >> 1)) & 1) != 0)


def chip_kernel(outer, own_fx, within_in, across, fx2, fxl2, fy2, fz2, fzl2, e2, pair):
    _, half, lanes = outer.shape
    first_of_two, even2 = parities2(half, lanes)
    body, down = pl.ds(PAD, half), pl.ds(PAD - 1, half)
    edge = jnp.zeros((PAD, lanes), jnp.float32)
    for j in range(4):
        e2[j] = jnp.zeros((half + 2 * PAD, lanes), jnp.float32)
    sources = by_side(outer[0], within_in[0])
    for j, (fy, fz) in enumerate(zip(by_side(outer[2], within_in[2]), by_side(outer[3], within_in[3]))):
        fy2[j, :PAD] = edge
        fy2[j, body] = fy
        fy2[j, PAD + half:] = edge
        fz2[j] = fz
        fzl2[j] = behind(fz, 2, 1)
    fx_own, fxl_own = own_fx[0], own_fx[1]
    fxl_left, _ = by_side(fxl_own, within_in[1])
    fx_right, _ = by_side(within_in[1], fx_own)
    fx2[0], _ = by_side(fx_own, jnp.where(first_of_two, ahead(fxl_left, 1, 1), behind(fxl_own, 1, 1)))
    fxl2[1], _ = by_side(jnp.where(first_of_two, ahead(fx_own, 1, 1), behind(fx_right, 1, 1)), fxl_own)
    fxl2[0], fx2[1] = fxl_left, fx_right
    inverse = []
    for j in range(2):
        weight = fx2[j] + fxl2[j] + fy2[j, body] + fy2[j, down] + fz2[j] + fzl2[j]
        inverse.append(1.0 / (8.0 + weight))
        e2[j + 1, body] = sources[j] * inverse[j]
    sums = neigh2(e2, fx2, fxl2, fy2, fz2, fzl2, first_of_two, (0, 1))
    left, right = [(sources[j] + sums[j]) * inverse[j] for j in range(2)]
    for k in range(5):
        across[k * half:(k + 1) * half] = outer[k]
    across[5 * half:] = packed_odd(jnp.where(first_of_two, right, left), pair)


def middle_down_kernel(
    own, own_fx, across_in, within_in,
    slots, halo, e2_out, s2, fx2, fxl2, fy2, fz2, fzl2, inv2,
    e2, pair,
):
    _, half, lanes = own.shape
    quarter = half // 2
    position = lax.axis_index("gx")
    first_of_two, even2 = parities2(half, lanes)
    body, down = pl.ds(PAD, half), pl.ds(PAD - 1, half)
    edge = jnp.zeros((PAD, lanes), jnp.float32)
    for j in range(5):
        e2[j] = jnp.zeros((half + 2 * PAD, lanes), jnp.float32)

    def three(k):
        left, right = by_side(across_in[k * half:(k + 1) * half], within_in[k])
        return left, own[k], right

    for j, (source, fy, fz) in enumerate(zip(three(0), three(2), three(3))):
        s2[j] = source
        fy2[j, :PAD] = edge
        fy2[j, body] = fy
        fy2[j, PAD + half:] = edge
        fz2[j] = fz
        fzl2[j] = behind(fz, 2, 1)
    left_fx, _, right_fx = three(1)
    fx2[0] = jnp.where(first_of_two, ahead(left_fx, 1, 1), behind(own_fx[1], 1, 1))
    fx2[1] = own_fx[0]
    fx2[2] = right_fx
    fxl2[0] = left_fx
    fxl2[1] = own_fx[1]
    fxl2[2] = jnp.where(first_of_two, ahead(own_fx[0], 1, 1), behind(right_fx, 1, 1))
    for j in range(3):
        weight = fx2[j] + fxl2[j] + fy2[j, body] + fy2[j, down] + fz2[j] + fzl2[j]
        inverse = 1.0 / (8.0 + weight)
        inv2[j] = inverse
        e2[j + 1, body] = s2[j] * inverse

    def neigh(tiles):
        return neigh2(e2, fx2, fxl2, fy2, fz2, fzl2, first_of_two, tiles)

    fresh = [(s2[j] + sums) * inv2[j] for j, sums in enumerate(neigh((0, 1, 2)))]
    for j in range(3):
        e2[j + 1, body] = fresh[j]
        e2_out[j] = fresh[j]
    pair[0] = jnp.where(even2, neigh((1,))[0], 0.0)
    lane = lanes_of((quarter, lanes))
    slot = position // (slots.shape[0] // 2)
    odd_layer, odd_depth, item = (lane & 1) != 0, (lane & 2) != 0, (lane - slot) & 3
    source = group(even_row_sum(pair.at[0], quarter))
    fx = group(jnp.where(odd_layer, even_row_sum(fx2.at[1], quarter), 0.0))
    fy = group(fy2[1, pl.ds(PAD + 1, quarter, 2), :])
    fz = group(jnp.where(odd_depth, even_row_sum(fz2.at[1], quarter), 0.0))
    tile = jnp.where(item == 0, source, jnp.where(item == 1, fx, jnp.where(item == 2, fy, fz)))
    for c in range(slots.shape[0]):
        slots[c] = tile
    for_right, _ = by_side(
        jnp.where(first_of_two, fresh[1], fresh[0]), jnp.where(first_of_two, fresh[2], fresh[1])
    )
    halo[...] = packed_odd(for_right, pair.at[1])


def joined(one, two):
    return jnp.concatenate([part for part in (one, two) if part.shape[0]], 0)


class Level:
    def __init__(self, mass, source, faces, row_step, lane_step, slot_step):
        self.source, self.row_step, self.lane_step, self.slot_step = source, row_step, lane_step, slot_step
        self.fx, self.fy, self.fz = faces
        self.tiles = source.shape[0]
        shape = source.shape
        self.lane = lanes_of(shape)
        layer = lax.broadcasted_iota(jnp.int32, shape, 0) if self.tiles > 1 else self.lane // slot_step
        self.even = ((layer + rows_of(shape) // row_step + self.lane // lane_step) & 1) == 0
        self.fxl = self.lower(self.fx)
        self.fyl = self.row_shifts(self.fy)[1]
        self.fzl = behind(self.fz, lane_step, 2)
        weight = (self.fx + self.fxl) + (self.fy + self.fyl) + (self.fz + self.fzl)
        self.inv = 1.0 / (mass + weight)

    def upper(self, e):
        return joined(e[1:], ahead(e[:1], self.slot_step, 2))

    def lower(self, e):
        return joined(behind(e[-1:], self.slot_step, 2), e[:-1])

    def row_shifts(self, e):
        return ahead(e, self.row_step, 1), behind(e, self.row_step, 1)

    def neigh(self, e):
        above, below = self.row_shifts(e)
        total = (self.fx * self.upper(e) + self.fxl * self.lower(e)) + (self.fy * above + self.fyl * below)
        return total + (self.fz * ahead(e, self.lane_step, 2) + self.fzl * behind(e, self.lane_step, 2))

    def update(self, e):
        return (self.source + self.neigh(e)) * self.inv

    def cycle(self, deeper):
        odd = self.update(self.source * self.inv)
        residual = jnp.where(self.even, self.neigh(odd), 0.0)
        fix = deeper(self.restricted(residual), self.coarse_faces())
        even = self.update(odd + self.prolonged(fix))
        return jnp.where(self.even, even, self.update(even))

    def coarse_slot_step(self):
        return self.slot_step if self.tiles > 1 else 2 * self.slot_step

    def pairs(self, values):
        if self.tiles == 1:
            return with_partner(values, self.slot_step, 2)
        halves = values.reshape(self.tiles // 2, 2, *values.shape[1:])
        return halves[:, 0] + halves[:, 1]

    def odd_layers(self, values):
        if self.tiles == 1:
            return with_partner(jnp.where((self.lane & self.slot_step) != 0, values, 0.0), self.slot_step, 2)
        return values.reshape(self.tiles // 2, 2, *values.shape[1:])[:, 1]

    def row_pairs(self, values):
        return with_partner(values, self.row_step, 1)

    def odd_rows(self, values):
        odd = (rows_of(values.shape) & self.row_step) != 0
        return with_partner(jnp.where(odd, values, 0.0), self.row_step, 1)

    def restricted(self, values):
        return with_partner(self.row_pairs(self.pairs(values)), self.lane_step, 2)

    def coarse_faces(self):
        fx = with_partner(self.row_pairs(self.odd_layers(self.fx)), self.lane_step, 2)
        fy = with_partner(self.odd_rows(self.pairs(self.fy)), self.lane_step, 2)
        return fx, fy, self.restricted(jnp.where((self.lane & self.lane_step) != 0, self.fz, 0.0))

    def prolonged(self, fix):
        if self.tiles == 1:
            return fix
        both = jnp.concatenate([fix[:, None], fix[:, None]], 1)
        return both.reshape(self.tiles, *fix.shape[1:])


class Rows(Level):
    def __init__(self, mass, source, faces, scratch):
        self.scratch, self.used = scratch, 0
        self.rows = source.shape[1]
        super().__init__(mass, source, faces, 1, 4, 1)

    def place(self):
        self.used += 1
        return self.scratch.at[self.used % self.scratch.shape[0]]

    def row_shifts(self, e):
        place = self.place()
        edge = jnp.zeros((e.shape[0], PAD, e.shape[2]), jnp.float32)
        place[:, :PAD] = edge
        place[:, PAD + self.rows:] = edge
        place[:, pl.ds(PAD, self.rows)] = e
        return place[:, pl.ds(PAD + 1, self.rows)], place[:, pl.ds(PAD - 1, self.rows)]

    def every_other(self, values, starts):
        place, tiles = self.place(), values.shape[0]
        place[:tiles, : self.rows] = values
        found = 0.0
        for start in starts:
            found = found + jnp.concatenate(
                [place[j, pl.ds(start, self.rows // 2, 2), :][None] for j in range(tiles)], 0
            )
        return found

    def row_pairs(self, values):
        return self.every_other(values, (0, 1))

    def odd_rows(self, values):
        return self.every_other(values, (1,))

    def prolonged(self, fix):
        place, tiles = self.place(), fix.shape[0]
        for j in range(tiles):
            into_both_rows(place.at[j, pl.ds(0, self.rows)], fix[j])
        return super().prolonged(place[:tiles, : self.rows])


def coarsest(mass, source, faces, *steps):
    row_step, lane_step, slot_step = steps
    level = Level(mass, source, faces, *steps)
    counts = source.shape[1] // row_step, source.shape[2] // lane_step, 4 // slot_step
    frames = [(m, k, q) for m in range(counts[0]) for k in range(counts[1]) for q in range(counts[2])]
    place = level.lane & 3

    def spread(values):
        copies = {}
        for m, k, q in frames:
            if k:
                copies[m, k, q] = behind(copies[m, 0, q], k * lane_step, 2)
            elif q:
                by = q * slot_step
                one, two = behind(copies[m, 0, 0], by, 2), ahead(copies[m, 0, 0], 4 - by, 2)
                copies[m, k, q] = jnp.where(place >= by, one, two)
            else:
                copies[m, k, q] = behind(values, m * row_step, 1) if m else values
        return copies

    start, inv, fx, fy, fz = [spread(values) for values in (source * level.inv, level.inv, level.fx, level.fy, level.fz)]

    def shifted(copies, frame, axis, by):
        moved = list(frame)
        moved[axis] = (frame[axis] - by) % counts[axis]
        return copies[tuple(moved)]

    def along_x(copies, frame, by):
        here, wrapped = copies[frame], shifted(copies, frame, 2, by)
        return joined(here[1:], wrapped[:1]) if by > 0 else joined(wrapped[-1:], here[:-1])

    weights = {}
    for frame in frames:
        pairs = [
            (fx[frame], along_x(fx, frame, -1)),
            (fy[frame], shifted(fy, frame, 0, -1)),
            (fz[frame], shifted(fz, frame, 1, -1)),
        ]
        weights[frame] = [(up * inv[frame], low * inv[frame]) for up, low in pairs]

    def update(e):
        fresh = {}
        for frame in frames:
            (x_up, x_low), (y_up, y_low), (z_up, z_low) = weights[frame]
            total = x_up * along_x(e, frame, 1) + x_low * along_x(e, frame, -1)
            total = total + (y_up * shifted(e, frame, 0, 1) + y_low * shifted(e, frame, 0, -1))
            total = total + (z_up * shifted(e, frame, 1, 1) + z_low * shifted(e, frame, 1, -1))
            fresh[frame] = start[frame] + total
        return fresh

    even = start
    odd = update(even)
    for turn in range(COARSE_SWEEPS - 1):
        even = update(odd)
        odd = update(even)
    return jnp.where(level.even, even[0, 0, 0], odd[0, 0, 0])


def small_cycle(mass, source, faces, row_step, lane_step, slot_step, between):
    if between == 0:
        return coarsest(mass, source, faces, row_step, lane_step, slot_step)
    level = Level(mass, source, faces, row_step, lane_step, slot_step)
    return level.cycle(
        lambda inner, inner_faces: small_cycle(
            8.0 * mass, inner, inner_faces, 2 * row_step, 2 * lane_step, level.coarse_slot_step(), between - 1
        )
    )


def coarse_kernel(
    owner_of, same_cores, other_cores, e2_in, s2, fx2, fxl2, fy2, fz2, fzl2, inv2,
    inputs, field, fx_in, fx_outer, fy_in, fz_in, fzl_in, inv_in, across_in, within_in, halo_in,
    solved_out, owned_out,
    e3, rows3, pair, e2, e1, cor, solved, owned, owner_here, fetch_sem, sems,
):
    fetch = pltpu.make_async_copy(owner_of, owner_here, fetch_sem)
    fetch.start()
    chips, quarter, lanes = same_cores.shape
    blocks = 2 * chips
    half, height = 2 * quarter, 4 * quarter
    position, last = lax.axis_index("gx"), blocks - 1

    slot = lanes_of((quarter, lanes)) & 3
    spread = blocks // 4
    tiles = []
    for chip in range(chips):
        tiles.extend(by_side(same_cores[chip], other_cores[chip]))
    items = []
    for k in range(4):
        packs = []
        for j in range(spread):
            value = tiles[j + (3 - k) % 4 * spread]
            for at in range(3):
                value = jnp.where(slot == at, tiles[j + (at - k) % 4 * spread], value)
            if k:
                value = jnp.where(slot < 4 - k, ahead(value, k, 1), behind(value, 4 - k, 1))
            packs.append(value[None])
        items.append(jnp.concatenate(packs, 0))
    third = Rows(64.0, items[0], items[1:], rows3)
    e3[...] = third.cycle(
        lambda inner, faces: small_cycle(512.0, inner, faces, 1, 8, third.coarse_slot_step(), 2)
    )

    fetch.wait()
    owner = owner_here[position]
    wide, narrow = lanes_of((lanes, lanes)), rows_of((lanes, lanes))
    take = jnp.where(narrow == 4 * wide + owner // spread, 1.0, 0.0)
    block = jnp.dot(
        e3[owner % spread], take, precision=lax.Precision.HIGHEST, preferred_element_type=jnp.float32
    )
    owned[0] = block[:, : lanes // 4]
    copies = [pltpu.make_async_copy(owned, owned_out, sems.at[0])]
    copies[0].start()

    first_of_two, even2 = parities2(half, lanes)
    body2 = pl.ds(PAD, half)
    edge = jnp.zeros((PAD, lanes), jnp.float32)
    left, right = by_side(across_in[5 * half:], halo_in[...])
    into_both_rows(pair.at[5], left)
    into_both_rows(pair.at[6], right)
    left, right = pair[5], pair[6]
    before = (
        left, jnp.where(first_of_two, left, e2_in[0]), e2_in[1], jnp.where(first_of_two, e2_in[2], right), right
    )
    for k in range(5):
        j = jnp.clip(position + k - 2, 0, last)
        into_both_rows(pair.at[k], group(jnp.where(slot == j // spread, e3[j % spread], 0.0)))
        e2[k, :PAD] = edge
        e2[k, PAD + half:] = edge
        e2[k, body2] = before[k] + pair[k]

    def update2():
        sums = neigh2(e2, fx2, fxl2, fy2, fz2, fzl2, first_of_two, (0, 1, 2))
        return [(s2[j] + sums[j]) * inv2[j] for j in range(3)]

    fresh = update2()
    for j in range(3):
        e2[j + 1, body2] = fresh[j]
    fixes2 = [jnp.where(even2, even, odd) for even, odd in zip(fresh, update2())]

    _, source, _ = three_parts(inputs)
    body1, up1, down1 = pl.ds(PAD, height), pl.ds(PAD + 1, height), pl.ds(PAD - 1, height)
    rows, lane = rows_of((height, lanes)), lanes_of((height, lanes))
    even_sum = ((rows + lane) & 1) == 0
    count = e1.shape[0]
    fixes = []
    for w in range(count):
        tile, t = divmod((w - 1) // 2, 2)
        packed = fixes2[1 + tile]
        if w % 2 == 1 or w == 0:
            if t == 0:
                plain = jnp.where(first_of_two, packed, behind(packed, 1, 1))
            else:
                plain = jnp.where(first_of_two, ahead(packed, 1, 1), packed)
            into_both_rows(cor.at[len(fixes)], plain)
            fixes.append(cor[len(fixes)])
        e1[w, :PAD] = edge
        e1[w, PAD + height:] = edge
        e1[w, body1] = field[w, body1] + fixes[-1]

    def in_layer1(w):
        here = e1[w, body1]
        sums = fy_in[w, body1] * e1[w, up1] + fy_in[w, down1] * e1[w, down1]
        return sums + fz_in[w] * ahead(here, 1, 1) + fzl_in[w] * behind(here, 1, 1)

    def smoothed1(w, odd):
        keep = even_sum if (w + odd) % 2 == 0 else ~even_sum
        sums = fx_in[w] * e1[w + 1, body1] + fx_in[w - 1] * e1[w - 1, body1] + in_layer1(w)
        return jnp.where(keep, e1[w, body1], (source[w - 1] + sums) * inv_in[w])

    borders = by_side(across_in[4 * half:5 * half], within_in[4])
    for w in range(1, count - 1):
        e1[w, body1] = smoothed1(w, 0)
    for side, w, near in ((0, 0, 1), (1, count - 1, count - 2)):
        into_both_rows(cor.at[4 + side], borders[side])
        sums = cor[4 + side] + fx_outer[side] * fixes[0 if side == 0 else -1]
        sums = sums + fx_in[min(w, near)] * e1[near, body1] + in_layer1(w)
        e1[w, body1] = sums * inv_in[w]
    for w in range(1, count - 1):
        solved[w - 1] = smoothed1(w, 1)
        copies.append(pltpu.make_async_copy(solved.at[w - 1], solved_out.at[w - 1], sems.at[w]))
        copies[-1].start()
    for copy in copies:
        copy.wait()


def f32(*shape):
    return jax.ShapeDtypeStruct(shape, jnp.float32)


def vmem(*shape):
    return pltpu.VMEM(shape, jnp.float32)


def call(kernel, outs, scratch, operands, out_space=pltpu.VMEM):
    def size(shape):
        count = 4
        for extent in shape:
            count *= extent
        return count

    sized = [array for array in (*scratch, *outs, *operands) if hasattr(array, "shape")]
    asked = 8 * 2**20 + sum(size(array.shape) for array in sized)
    return pl.pallas_call(
        kernel,
        out_shape=tuple(outs),
        in_specs=[pl.BlockSpec(memory_space=pltpu.VMEM)] * len(operands),
        out_specs=tuple([pl.BlockSpec(memory_space=out_space)] * len(outs)),
        scratch_shapes=scratch,
        compiler_params=pltpu.CompilerParams(vmem_limit_bytes=asked),
    )(*operands)


def on_device(iterate, source, phase_field, block_owner):
    layers, height, depth = iterate.shape
    half, quarter = height // 2, height // 4
    blocks = lax.axis_size("gx")
    window = layers + 2
    padded, padded2 = height + 2 * PAD, half + 2 * PAD
    inputs = sum(
        jnp.pad(block, ((k * layers, (2 - k) * layers), (0, 0), (0, 0)))
        for k, block in enumerate((iterate, source, phase_field))
    )
    sent = call(edge_kernel, [f32(3 * height + half, depth)] * 2, [], (inputs,))
    plain, tall = f32(window, height, depth), f32(window, padded, depth)
    outer, within, fx2, *fine = call(
        fine_down_kernel,
        [f32(5, half, depth)] * 2
        + [f32(2, half, depth), tall, f32(window - 1, height, depth), f32(2, height, depth), tall]
        + [plain] * 3,
        [vmem(window, padded, depth), vmem(layers, height, depth), vmem(2, height, depth)],
        (block_owner, inputs, between_chips(sent[0]), within_chip(sent[1])),
    )
    within_in = within_chip(within)
    plain, tall = f32(3, half, depth), f32(3, padded2, depth)
    across, = call(
        chip_kernel,
        [f32(5 * half + quarter, depth)],
        [
            vmem(2, half, depth), vmem(2, half, depth), vmem(2, padded2, depth), vmem(2, half, depth),
            vmem(2, half, depth), vmem(4, padded2, depth), vmem(half, depth),
        ],
        (outer, fx2, within_in),
    )
    across_in = between_chips(across)
    slots, halo, *middle = call(
        middle_down_kernel,
        [f32(blocks // 2, quarter, depth), f32(quarter, depth)] + [plain] * 4 + [tall] + [plain] * 3,
        [vmem(5, padded2, depth), vmem(2, half, depth)],
        (outer, fx2, across_in, within_in),
    )
    halo_in = within_chip(halo)
    kinds = [list(range(core, blocks, 2)) for core in range(2)]
    same_cores = lax.all_to_all(slots, "gx", 0, 0, axis_index_groups=kinds, tiled=True)
    other_cores = within_chip(same_cores)
    solved, owned = call(
        coarse_kernel,
        [f32(layers, height, depth), f32(1, quarter, depth // 4)],
        [
            vmem(blocks // 4, quarter, depth), vmem(4, blocks // 4, quarter + 2 * PAD, depth), vmem(7, half, depth),
            vmem(5, padded2, depth), vmem(window, padded, depth), vmem(6, height, depth),
            vmem(layers, height, depth), vmem(1, quarter, depth // 4), pltpu.SMEM((blocks,), jnp.int32),
            pltpu.SemaphoreType.DMA, pltpu.SemaphoreType.DMA((layers + 1,)),
        ],
        (block_owner, same_cores, other_cores, *middle, inputs, *fine, across_in, within_in, halo_in),
        pl.ANY,
    )
    return solved, owned


def solution(mesh):
    split = P(("groups", "gx"), None, None)
    return jax.shard_map(
        on_device,
        mesh=mesh,
        in_specs=(split, split, split, P("groups")),
        out_specs=(split, split),
        check_vma=False,
    )
```

```python
import jax
import jax.numpy as jnp
from jax import lax
from jax.experimental import pallas as pl
from jax.experimental.pallas import tpu as pltpu
from jax.sharding import PartitionSpec as P

STIFFNESS = 100.0
EPSILON = 0.01
COARSE_SWEEPS = 4
PAD = 8


def between_chips(block):
    return lax.ppermute(block, "gx", [(i, i + 1 if i % 2 else i - 1) for i in range(1, lax.axis_size("gx") - 1)])


def within_chip(block):
    return lax.ppermute(block, "gx", [(i, i ^ 1) for i in range(lax.axis_size("gx"))])


def by_side(across, within):
    on_left = lax.axis_index("gx") % 2 == 0
    return jnp.where(on_left, across, within), jnp.where(on_left, within, across)


def lanes_of(shape):
    return lax.broadcasted_iota(jnp.int32, shape, len(shape) - 1)


def rows_of(shape):
    return lax.broadcasted_iota(jnp.int32, shape, len(shape) - 2)


def ahead(values, step, axis):
    return pltpu.roll(values, values.shape[axis] - step, axis)


def behind(values, step, axis):
    return pltpu.roll(values, step, axis)


def with_partner(values, step, axis):
    index = lax.broadcasted_iota(jnp.int32, values.shape, axis)
    partner = jnp.where((index & step) == 0, ahead(values, step, axis), behind(values, step, axis))
    return values + partner


def even_row_sum(scratch, rows):
    return scratch[pl.ds(0, rows, 2), :] + scratch[pl.ds(1, rows, 2), :]


def core_of():
    return lax.axis_index("gx") % 2


def own_layer(u, layers):
    return u + core_of() * (layers - 1 - 2 * u)


def three_parts(ref):
    third = ref.shape[0] // 3
    return [ref.at[pl.ds(k * third, third)] for k in range(3)]


def odd_cells(ref, rows, first):
    return jnp.where(first, ref[pl.ds(0, rows, 2), :], ref[pl.ds(1, rows, 2), :])


def into_both_rows(ref, values):
    rows = values.shape[0]
    ref[pl.ds(0, rows, 2), :] = values
    ref[pl.ds(1, rows, 2), :] = values


def cell_coef(value):
    return STIFFNESS * (value * value + EPSILON)


class Plane:
    def __init__(self, height, depth):
        self.height, self.half, self.depth = height, height // 2, depth
        self.row, self.lane = rows_of((height, depth)), lanes_of((height, depth))
        self.parity = self.row + self.lane + core_of()
        self.half_lane = lanes_of((self.half, depth))
        self.body = pl.ds(PAD, height)
        self.up, self.down = pl.ds(PAD + 1, height), pl.ds(PAD - 1, height)

    def even(self, u):
        return ((self.parity + u) & 1) == 0

    def odd_first(self, u):
        return ((self.half_lane + core_of() + u) & 1) != 0

    def put(self, ref, values):
        edge = jnp.zeros((PAD, self.depth), jnp.float32)
        ref[:PAD] = edge
        ref[PAD + self.height:] = edge
        ref[self.body] = values

    def face_y(self, here):
        return jnp.where(self.row < self.height - 1, 0.5 * (here + ahead(here, 1, 0)), 0.0)

    def face_z(self, here):
        return jnp.where(self.lane < self.depth - 1, 0.5 * (here + ahead(here, 1, 1)), 0.0)

    def packed(self, outer, inner, core):
        return jnp.where((self.half_lane & 1) == core, outer, inner)

    def both_rows(self, ref):
        return even_row_sum(ref, self.half)

    def summed(self, values, ref):
        ref[...] = values
        return with_partner(self.both_rows(ref), 1, 1)

    def odd_rows(self, values, ref):
        ref[...] = values
        return with_partner(ref[pl.ds(1, self.half, 2), :], 1, 1)

    def odd_lanes(self, values, ref):
        ref[...] = values
        sums = self.both_rows(ref)
        return jnp.where((self.half_lane & 1) == 0, ahead(sums, 1, 1), sums)


def in_layer(plane, fy, fz, fzl, padded):
    here = padded[plane.body]
    total = fy[plane.body] * padded[plane.up] + fy[plane.down] * padded[plane.down]
    return total + (fz[...] * ahead(here, 1, 1) + fzl[...] * behind(here, 1, 1))


def edge_kernel(inputs, out):
    iterate, source, phase = three_parts(inputs)
    layers, height, depth = iterate.shape
    plane = Plane(height, depth)
    near, inner, far = [own_layer(u, layers) for u in (layers - 1, layers - 2, layers - 3)]
    coef_near, coef_inner, coef_far = [cell_coef(phase[k]) for k in (near, inner, far)]

    def around(here, e):
        fy, fz = plane.face_y(here), plane.face_z(here)
        fyl, fzl = behind(fy, 1, 0), behind(fz, 1, 1)
        total = fy * ahead(e, 1, 0) + fyl * behind(e, 1, 0)
        return total + fz * ahead(e, 1, 1) + fzl * behind(e, 1, 1), fy + fyl + fz + fzl

    face_near, face_far = 0.5 * (coef_inner + coef_near), 0.5 * (coef_inner + coef_far)
    total, weight = around(coef_inner, iterate[inner])
    total = total + face_near * iterate[near] + face_far * iterate[far]
    updated = (source[inner] + total) / (1.0 + (face_near + face_far + weight))
    total, _ = around(coef_near, iterate[near])
    known = jnp.where(plane.even(layers - 1), total + face_near * iterate[inner], face_near * updated)
    out[:height] = coef_near
    out[height:2 * height] = coef_inner
    out[2 * height:3 * height] = source[near] + known
    out[3 * height:] = odd_cells(iterate.at[near], plane.half, plane.odd_first(layers - 1))


def chip_rows(height):
    half, at, places = height // 2, 0, {}
    for name, size in (
        ("coef0", height), ("coef1", height), ("coef2", height), ("known0", height),
        ("old0", half), ("known1", half), ("old1", half), ("source2", half), ("fx2", half), ("fy2", half), ("fz2", half),
    ):
        places[name] = pl.ds(at, size)
        at += size
    return places, at


def chip_kernel(
    inputs, within_in,
    message, known1, new, fx, fy, fz, fzl, inv,
    cell, old, even, change, turn,
):
    iterate, source, phase = three_parts(inputs)
    layers, height, depth = iterate.shape
    plane = Plane(height, depth)
    body, half = plane.body, plane.half
    places, _ = chip_rows(height)
    margin = layers

    def part(k):
        return within_in[k * height:(k + 1) * height]

    def s(u):
        return source[own_layer(u, layers)]

    for u in range(layers):
        cell[u] = cell_coef(phase[own_layer(u, layers)])
        plane.put(old.at[u], iterate[own_layer(u, layers)])
    cell[margin] = part(0)
    into_both_rows(turn.at[0], within_in[3 * height:])
    plane.put(old.at[margin], turn[0])
    for u in range(margin + 1):
        here = cell[u]
        fx[u] = 0.5 * (here + (cell[u + 1] if u < margin else part(1)))
        plane.put(fy.at[u], plane.face_y(here))
        face = plane.face_z(here)
        fz[u] = face
        fzl[u] = behind(face, 1, 1)
    for u in range(1, margin + 1):
        weight = (fx[u] + fx[u - 1]) + (fy[u, body] + fy[u, plane.down]) + (fz[u] + fzl[u])
        inv[u - 1] = 1.0 / (1.0 + weight)

    def around(ref, u):
        return in_layer(plane, fy.at[u], fz.at[u], fzl.at[u], ref.at[u])

    for u in range(1, margin):
        total = s(u) + around(old, u) + (fx[u] * old[u + 1, body] + fx[u - 1] * old[u - 1, body])
        plane.put(even.at[u], total * inv[u - 1])
    plane.put(even.at[margin], (part(2) + fx[margin - 1] * old[margin - 1, body]) * inv[margin - 1])
    for u in range(2, margin + 1):
        if u < margin:
            total = s(u) + around(even, u) + (fx[u] * even[u + 1, body] + fx[u - 1] * even[u - 1, body])
        else:
            total = part(2) + around(even, u) + fx[u - 1] * even[u - 1, body]
        fresh = total * inv[u - 1]
        new[u - 2] = fresh
        plane.put(change.at[u], fresh - old[u, body])

    one = fx[1] * change[2, body]
    two = around(change, 2) + fx[2] * change[3, body]
    three = around(change, 3) + (fx[2] * change[2, body] + fx[3] * change[4, body])
    outer = jnp.where(plane.even(1), one, 0.0)
    inner = jnp.where(plane.even(2), two, 0.0) + jnp.where(plane.even(3), three, 0.0)
    core = core_of()

    def tile(name, outer, inner):
        message[places[name], :] = plane.packed(outer, inner, core)

    tile("source2", plane.summed(outer, turn.at[1]), plane.summed(inner, turn.at[2]))
    tile("fx2", plane.summed(fx[1], turn.at[3]), plane.summed(fx[3], turn.at[4]))
    tile("fy2", *[plane.odd_rows(fy[u, body] + fy[u + 1, body], turn.at[5 + u // 2]) for u in (0, 2)])
    tile("fz2", *[plane.odd_lanes(fz[u] + fz[u + 1], turn.at[7 + u // 2]) for u in (0, 2)])
    for u in range(3):
        message[places["coef%d" % u], :] = cell[u]
    first = s(0) + around(old, 0) + fx[0] * old[1, body]
    second = s(0) + fx[0] * even[1, body]
    message[places["known0"], :] = jnp.where(plane.even(0), first, second)
    total = s(1) + around(even, 1) + fx[1] * even[2, body]
    known1[...] = total
    turn[9] = total
    message[places["known1"], :] = odd_cells(turn.at[9], half, plane.odd_first(1))
    for u in range(2):
        message[places["old%d" % u], :] = odd_cells(iterate.at[own_layer(u, layers)], half, plane.odd_first(u))


def border_kernel(
    owner_of, inputs, message, known1, new_in, fx_in, fy_in, fz_in, fzl_in, inv_in, across_in,
    within, outer2, fx2_in, new, known, fx, fy, fz, fzl, inv,
    old, even, change, turn, face_y, face_z, face_zl,
):
    iterate, source, _ = three_parts(inputs)
    layers, height, depth = iterate.shape
    plane = Plane(height, depth)
    body, half = plane.body, plane.half
    places, _ = chip_rows(height)
    core, last = core_of(), lax.axis_size("gx") - 1
    position = lax.axis_index("gx")

    def mine(name):
        return message[places[name], :]

    def theirs(name):
        return across_in[places[name], :]

    def opened(name, k):
        into_both_rows(turn.at[k], theirs(name))
        return turn[k]

    for k in range(2):
        here = theirs("coef%d" % k)
        plane.put(face_y.at[k], plane.face_y(here))
        face = plane.face_z(here)
        face_z[k] = face
        face_zl[k] = behind(face, 1, 1)
    fy[...], fz[...], fzl[...] = face_y[0], face_z[0], face_zl[0]
    there = position - 1 + 2 * core
    border = jnp.where((there >= 0) & (there <= last), 0.5 * (mine("coef0") + theirs("coef0")), 0.0)
    face1 = 0.5 * (theirs("coef0") + theirs("coef1"))
    face2 = 0.5 * (theirs("coef1") + theirs("coef2"))
    fx[0], fx[1] = border, face1

    def inverse(faces, fy, fz, fzl):
        weight = faces + (fy[body] + fy[plane.down]) + (fz[...] + fzl[...])
        return 1.0 / (1.0 + weight)

    inv_own = inverse(fx_in[0] + border, fy_in.at[0], fz_in.at[0], fzl_in.at[0])
    inv_near = inverse(border + face1, face_y.at[0], face_z.at[0], face_zl.at[0])
    inv_far = inverse(face1 + face2, face_y.at[1], face_z.at[1], face_zl.at[1])
    inv[0], inv[1] = inv_near, inv_own
    old_own, old_next = iterate[own_layer(0, layers)], iterate[own_layer(1, layers)]
    old_near, old_far = opened("old0", 0), opened("old1", 1)
    even_own = (mine("known0") + border * old_near) * inv_own
    even_near = (theirs("known0") + border * old_own) * inv_near
    plane.put(even.at[0], even_near)
    plane.put(even.at[1], even_own)

    def near(ref, k):
        return in_layer(plane, face_y.at[k], face_z.at[k], face_zl.at[k], ref)

    def own(ref, u):
        return in_layer(plane, fy_in.at[u], fz_in.at[u], fzl_in.at[u], ref)

    odd_own = (mine("known0") + own(even.at[1], 0) + border * even_near) * inv_own
    odd_near = (theirs("known0") + near(even.at[0], 0) + border * even_own) * inv_near
    odd_next = (known1[...] + fx_in[0] * even_own) * inv_in[0]
    odd_far = (opened("known1", 2) + face1 * even_near) * inv_far
    new[0], new[1], new[2] = odd_near, odd_own, odd_next
    moved = odd_far - old_far, odd_near - old_near, odd_own - old_own, odd_next - old_next
    for k, values in enumerate(moved):
        plane.put(change.at[k], values)
    far, near_by, here, following = moved
    plane.put(old.at[0], old_near)
    known[...] = theirs("known0") + face1 * far - near(old.at[0], 0)

    def residual(u, values):
        return jnp.where(plane.even(u), values, 0.0)

    own_outer = residual(1, own(change.at[3], 1) + fx_in[0] * here)
    own_outer = own_outer + residual(0, own(change.at[2], 0) + (fx_in[0] * following + border * near_by))
    own_inner = residual(2, fx_in[1] * following)
    its_outer = residual(-1, near(change.at[1], 0) + (face1 * far + border * here))
    its_outer = its_outer + residual(-2, near(change.at[0], 1) + face1 * near_by)
    its_inner = residual(-3, face2 * far)
    sums = [plane.summed(values, turn.at[3 + k]) for k, values in enumerate((own_outer, own_inner, its_outer, its_inner))]
    within[0] = mine("source2") + plane.packed(sums[0], sums[1], core)
    outer2[0] = theirs("source2") + plane.packed(sums[2], sums[3], 1 - core)
    for k, name in ((1, "fx2"), (2, "fy2"), (3, "fz2")):
        outer2[k] = theirs(name)
    fx2_in[...] = mine("fx2")
    middle = jnp.where((plane.half_lane & 1) == 0, ahead(mine("fx2"), 1, 1), behind(mine("fx2"), 1, 1))
    within[1] = plane.packed(plane.summed(border, turn.at[7]), middle, core)
    within[2], within[3] = mine("fy2"), mine("fz2")
    turn[0] = source[own_layer(layers - 1, layers)] + fx_in[layers - 2] * new_in[layers - 4]
    within[4] = odd_cells(turn.at[0], half, jnp.logical_not(plane.odd_first(layers - 1)))


def neigh2(e2, fx2, fxl2, fy2, fz2, fzl2, first_of_two, tiles):
    half = fx2.shape[1]
    body, up, down = pl.ds(PAD, half), pl.ds(PAD + 1, half), pl.ds(PAD - 1, half)
    needed = range(tiles[0], tiles[-1] + 3)
    here = {j: e2[j, body] for j in needed}
    after = {j: ahead(here[j], 1, 1) for j in needed}
    before = {j: behind(here[j], 1, 1) for j in needed}
    found = []
    for j in tiles:
        k = j + 1
        upper = jnp.where(first_of_two, after[k], before[k + 1])
        lower = jnp.where(first_of_two, after[k - 1], before[k])
        sums = fx2[j] * upper + fxl2[j] * lower
        sums = sums + fy2[j, body] * e2[k, up] + fy2[j, down] * e2[k, down]
        sums = sums + fz2[j] * ahead(here[k], 2, 1) + fzl2[j] * behind(here[k], 2, 1)
        found.append(sums)
    return found


def parities2(half, lanes):
    row, lane = rows_of((half, lanes)), lanes_of((half, lanes))
    return (lane & 1) == 0, ((row + (lane & 1) + (lane >> 1)) & 1) == 0


def group(values):
    return with_partner(with_partner(values, 1, 1), 2, 1)


def middle_down_kernel(
    own, fx2_in, outer, within_in,
    slots, e2_out, s2, fx2, fxl2, fy2, fz2, fzl2, inv2,
    e2, pair,
):
    _, half, lanes = own.shape
    quarter = half // 2
    position = lax.axis_index("gx")
    first_of_two, even2 = parities2(half, lanes)
    body, down = pl.ds(PAD, half), pl.ds(PAD - 1, half)
    edge = jnp.zeros((PAD, lanes), jnp.float32)
    for j in range(5):
        e2[j] = jnp.zeros((half + 2 * PAD, lanes), jnp.float32)
    def three(k):
        left, right = by_side(outer[k], within_in[k])
        return left, own[k], right

    for j, (source, fy, fz) in enumerate(zip(three(0), three(2), three(3))):
        s2[j] = source
        fy2[j, :PAD] = edge
        fy2[j, body] = fy
        fy2[j, PAD + half:] = edge
        fz2[j] = fz
        fzl2[j] = behind(fz, 2, 1)
    left_fx, _, right_fx = three(1)
    own_fx = by_side(fx2_in[...], own[1])
    fx2[0] = jnp.where(first_of_two, ahead(left_fx, 1, 1), behind(own_fx[1], 1, 1))
    fx2[1] = own_fx[0]
    fx2[2] = right_fx
    fxl2[0] = left_fx
    fxl2[1] = own_fx[1]
    fxl2[2] = jnp.where(first_of_two, ahead(own_fx[0], 1, 1), behind(right_fx, 1, 1))
    for j in range(3):
        weight = fx2[j] + fxl2[j] + fy2[j, body] + fy2[j, down] + fz2[j] + fzl2[j]
        inverse = 1.0 / (8.0 + weight)
        inv2[j] = inverse
        e2[j + 1, body] = jnp.where(even2, s2[j] * inverse, 0.0)

    def neigh(tiles):
        return neigh2(e2, fx2, fxl2, fy2, fz2, fzl2, first_of_two, tiles)

    fresh = [
        jnp.where(even2, e2[j + 1, body], (s2[j] + sums) * inv2[j]) for j, sums in enumerate(neigh((0, 1, 2)))
    ]
    for j in range(3):
        e2[j + 1, body] = fresh[j]
        e2_out[j] = fresh[j]
    pair[0] = jnp.where(even2, neigh((1,))[0], 0.0)
    lane = lanes_of((quarter, lanes))
    slot = position // (slots.shape[0] // 2)
    odd_layer, odd_depth, item = (lane & 1) != 0, (lane & 2) != 0, (lane - slot) & 3
    source = group(even_row_sum(pair.at[0], quarter))
    fx = group(jnp.where(odd_layer, even_row_sum(fx2.at[1], quarter), 0.0))
    fy = group(fy2[1, pl.ds(PAD + 1, quarter, 2), :])
    fz = group(jnp.where(odd_depth, even_row_sum(fz2.at[1], quarter), 0.0))
    tile = jnp.where(item == 0, source, jnp.where(item == 1, fx, jnp.where(item == 2, fy, fz)))
    first = (((lane & 1) + (lane >> 1)) & 1) != 0
    pair[0] = jnp.where(first_of_two, fresh[2], fresh[1])
    pair[1] = jnp.where(first_of_two, fresh[1], fresh[0])
    for_left = odd_cells(pair.at[0], quarter, first)
    for_right = odd_cells(pair.at[1], quarter, first)
    for c in range(slots.shape[0]):
        slots[c, 0] = tile
        slots[c, 1] = jnp.where(position < 2 * c + 1 - position % 2, for_right, for_left)


def joined(one, two):
    return jnp.concatenate([part for part in (one, two) if part.shape[0]], 0)


class Level:
    def __init__(self, mass, source, faces, row_step, lane_step, slot_step):
        self.source, self.row_step, self.lane_step, self.slot_step = source, row_step, lane_step, slot_step
        self.fx, self.fy, self.fz = faces
        self.tiles = source.shape[0]
        shape = source.shape
        self.lane = lanes_of(shape)
        layer = lax.broadcasted_iota(jnp.int32, shape, 0) if self.tiles > 1 else self.lane // slot_step
        self.even = ((layer + rows_of(shape) // row_step + self.lane // lane_step) & 1) == 0
        self.fxl = self.lower(self.fx)
        self.fyl = self.row_shifts(self.fy)[1]
        self.fzl = behind(self.fz, lane_step, 2)
        weight = (self.fx + self.fxl) + (self.fy + self.fyl) + (self.fz + self.fzl)
        self.inv = 1.0 / (mass + weight)

    def upper(self, e):
        return joined(e[1:], ahead(e[:1], self.slot_step, 2))

    def lower(self, e):
        return joined(behind(e[-1:], self.slot_step, 2), e[:-1])

    def row_shifts(self, e):
        return ahead(e, self.row_step, 1), behind(e, self.row_step, 1)

    def neigh(self, e):
        above, below = self.row_shifts(e)
        total = (self.fx * self.upper(e) + self.fxl * self.lower(e)) + (self.fy * above + self.fyl * below)
        return total + (self.fz * ahead(e, self.lane_step, 2) + self.fzl * behind(e, self.lane_step, 2))

    def update(self, e):
        return (self.source + self.neigh(e)) * self.inv

    def cycle(self, deeper):
        odd = self.update(self.source * self.inv)
        residual = jnp.where(self.even, self.neigh(odd), 0.0)
        fix = deeper(self.restricted(residual), self.coarse_faces())
        even = self.update(odd + self.prolonged(fix))
        return jnp.where(self.even, even, self.update(even))

    def coarse_slot_step(self):
        return self.slot_step if self.tiles > 1 else 2 * self.slot_step

    def pairs(self, values):
        if self.tiles == 1:
            return with_partner(values, self.slot_step, 2)
        halves = values.reshape(self.tiles // 2, 2, *values.shape[1:])
        return halves[:, 0] + halves[:, 1]

    def odd_layers(self, values):
        if self.tiles == 1:
            return with_partner(jnp.where((self.lane & self.slot_step) != 0, values, 0.0), self.slot_step, 2)
        return values.reshape(self.tiles // 2, 2, *values.shape[1:])[:, 1]

    def row_pairs(self, values):
        return with_partner(values, self.row_step, 1)

    def odd_rows(self, values):
        odd = (rows_of(values.shape) & self.row_step) != 0
        return with_partner(jnp.where(odd, values, 0.0), self.row_step, 1)

    def restricted(self, values):
        return with_partner(self.row_pairs(self.pairs(values)), self.lane_step, 2)

    def coarse_faces(self):
        fx = with_partner(self.row_pairs(self.odd_layers(self.fx)), self.lane_step, 2)
        fy = with_partner(self.odd_rows(self.pairs(self.fy)), self.lane_step, 2)
        return fx, fy, self.restricted(jnp.where((self.lane & self.lane_step) != 0, self.fz, 0.0))

    def prolonged(self, fix):
        if self.tiles == 1:
            return fix
        both = jnp.concatenate([fix[:, None], fix[:, None]], 1)
        return both.reshape(self.tiles, *fix.shape[1:])


class Rows(Level):
    def __init__(self, mass, source, faces, scratch):
        self.scratch, self.used = scratch, 0
        self.rows = source.shape[1]
        super().__init__(mass, source, faces, 1, 4, 1)

    def place(self):
        self.used += 1
        return self.scratch.at[self.used % self.scratch.shape[0]]

    def row_shifts(self, e):
        place = self.place()
        edge = jnp.zeros((e.shape[0], PAD, e.shape[2]), jnp.float32)
        place[:, :PAD] = edge
        place[:, PAD + self.rows:] = edge
        place[:, pl.ds(PAD, self.rows)] = e
        return place[:, pl.ds(PAD + 1, self.rows)], place[:, pl.ds(PAD - 1, self.rows)]

    def every_other(self, values, starts):
        place, tiles = self.place(), values.shape[0]
        place[:tiles, : self.rows] = values
        found = 0.0
        for start in starts:
            found = found + jnp.concatenate(
                [place[j, pl.ds(start, self.rows // 2, 2), :][None] for j in range(tiles)], 0
            )
        return found

    def row_pairs(self, values):
        return self.every_other(values, (0, 1))

    def odd_rows(self, values):
        return self.every_other(values, (1,))

    def prolonged(self, fix):
        place, tiles = self.place(), fix.shape[0]
        for j in range(tiles):
            into_both_rows(place.at[j, pl.ds(0, self.rows)], fix[j])
        return super().prolonged(place[:tiles, : self.rows])


def coarsest(mass, source, faces, *steps):
    row_step, lane_step, slot_step = steps
    level = Level(mass, source, faces, *steps)
    counts = source.shape[1] // row_step, source.shape[2] // lane_step, 4 // slot_step
    frames = [(m, k, q) for m in range(counts[0]) for k in range(counts[1]) for q in range(counts[2])]
    place = level.lane & 3

    def spread(values):
        copies = {}
        for m, k, q in frames:
            if k:
                copies[m, k, q] = behind(copies[m, 0, q], k * lane_step, 2)
            elif q:
                by = q * slot_step
                one, two = behind(copies[m, 0, 0], by, 2), ahead(copies[m, 0, 0], 4 - by, 2)
                copies[m, k, q] = jnp.where(place >= by, one, two)
            else:
                copies[m, k, q] = behind(values, m * row_step, 1) if m else values
        return copies

    start, inv, fx, fy, fz = [spread(values) for values in (source * level.inv, level.inv, level.fx, level.fy, level.fz)]

    def shifted(copies, frame, axis, by):
        moved = list(frame)
        moved[axis] = (frame[axis] - by) % counts[axis]
        return copies[tuple(moved)]

    def along_x(copies, frame, by):
        here, wrapped = copies[frame], shifted(copies, frame, 2, by)
        return joined(here[1:], wrapped[:1]) if by > 0 else joined(wrapped[-1:], here[:-1])

    weights = {}
    for frame in frames:
        pairs = [
            (fx[frame], along_x(fx, frame, -1)),
            (fy[frame], shifted(fy, frame, 0, -1)),
            (fz[frame], shifted(fz, frame, 1, -1)),
        ]
        weights[frame] = [(up * inv[frame], low * inv[frame]) for up, low in pairs]

    def update(e):
        fresh = {}
        for frame in frames:
            (x_up, x_low), (y_up, y_low), (z_up, z_low) = weights[frame]
            total = x_up * along_x(e, frame, 1) + x_low * along_x(e, frame, -1)
            total = total + (y_up * shifted(e, frame, 0, 1) + y_low * shifted(e, frame, 0, -1))
            total = total + (z_up * shifted(e, frame, 1, 1) + z_low * shifted(e, frame, 1, -1))
            fresh[frame] = start[frame] + total
        return fresh

    even = start
    odd = update(even)
    for turn in range(COARSE_SWEEPS - 1):
        even = update(odd)
        odd = update(even)
    return jnp.where(level.even, even[0, 0, 0], odd[0, 0, 0])


def small_cycle(mass, source, faces, row_step, lane_step, slot_step, between):
    if between == 0:
        return coarsest(mass, source, faces, row_step, lane_step, slot_step)
    level = Level(mass, source, faces, row_step, lane_step, slot_step)
    return level.cycle(
        lambda inner, inner_faces: small_cycle(
            8.0 * mass, inner, inner_faces, 2 * row_step, 2 * lane_step, level.coarse_slot_step(), between - 1
        )
    )


def coarse_kernel(
    owner_of, same_cores, other_cores, e2_in, s2, fx2, fxl2, fy2, fz2, fzl2, inv2,
    inputs, new_in, fx_in, fy_in, fz_in, fzl_in, inv_in,
    new_out, known_out, fx_out, fy_out, fz_out, fzl_out, inv_out, within_in,
    solved_out, owned_out,
    e3, rows3, pair, e2, e1, cor, solved, owned, owner_here, fetch_sem, sems,
):
    fetch = pltpu.make_async_copy(owner_of, owner_here, fetch_sem)
    fetch.start()
    chips, _, quarter, lanes = same_cores.shape
    blocks = 2 * chips
    half, height = 2 * quarter, 4 * quarter
    position, last = lax.axis_index("gx"), blocks - 1

    slot = lanes_of((quarter, lanes)) & 3
    spread = blocks // 4
    tiles = []
    for chip in range(chips):
        tiles.extend(by_side(same_cores[chip, 0], other_cores[chip, 0]))
    items = []
    for k in range(4):
        packs = []
        for j in range(spread):
            value = tiles[j + (3 - k) % 4 * spread]
            for at in range(3):
                value = jnp.where(slot == at, tiles[j + (at - k) % 4 * spread], value)
            if k:
                value = jnp.where(slot < 4 - k, ahead(value, k, 1), behind(value, 4 - k, 1))
            packs.append(value[None])
        items.append(jnp.concatenate(packs, 0))
    third = Rows(64.0, items[0], items[1:], rows3)
    e3[...] = third.cycle(
        lambda inner, faces: small_cycle(512.0, inner, faces, 1, 8, third.coarse_slot_step(), 2)
    )

    fetch.wait()
    owner = owner_here[position]
    wide, narrow = lanes_of((lanes, lanes)), rows_of((lanes, lanes))
    take = jnp.where(narrow == 4 * wide + owner // spread, 1.0, 0.0)
    block = jnp.dot(
        e3[owner % spread], take, precision=lax.Precision.HIGHEST, preferred_element_type=jnp.float32
    )
    owned[0] = block[:, : lanes // 4]
    copies = [pltpu.make_async_copy(owned, owned_out, sems.at[0])]
    copies[0].start()

    first_of_two, even2 = parities2(half, lanes)
    body2 = pl.ds(PAD, half)
    edge = jnp.zeros((PAD, lanes), jnp.float32)
    left = other_cores[jnp.maximum(position - 1, 0) // 2, 1]
    right = other_cores[jnp.minimum(position + 1, last) // 2, 1]
    into_both_rows(pair.at[5], left)
    into_both_rows(pair.at[6], right)
    left, right = pair[5], pair[6]
    before = (
        left, jnp.where(first_of_two, left, e2_in[0]), e2_in[1], jnp.where(first_of_two, e2_in[2], right), right
    )
    for k in range(5):
        j = jnp.clip(position + k - 2, 0, last)
        into_both_rows(pair.at[k], group(jnp.where(slot == j // spread, e3[j % spread], 0.0)))
        e2[k, :PAD] = edge
        e2[k, PAD + half:] = edge
        e2[k, body2] = before[k] + pair[k]

    def update2():
        sums = neigh2(e2, fx2, fxl2, fy2, fz2, fzl2, first_of_two, (0, 1, 2))
        return [(s2[j] + sums[j]) * inv2[j] for j in range(3)]

    fresh = update2()
    for j in range(3):
        e2[j + 1, body2] = fresh[j]
    fixes2 = [jnp.where(even2, even, odd) for even, odd in zip(fresh, update2())]

    _, source, _ = three_parts(inputs)
    layers = source.shape[0]
    plane = Plane(height, lanes)
    body1 = plane.body
    core = core_of()
    near_lane = (lanes_of((half, lanes)) & 1) == core
    swaps = [jnp.where(first_of_two, ahead(v, 1, 1), behind(v, 1, 1)) for v in fixes2]
    outer, inner = by_side(fixes2[0], fixes2[2])
    outer_swap, inner_swap = by_side(swaps[0], swaps[2])
    coarse = (
        jnp.where(near_lane, outer_swap, outer), jnp.where(near_lane, fixes2[1], swaps[1]),
        jnp.where(near_lane, swaps[1], fixes2[1]), jnp.where(near_lane, inner, inner_swap),
    )
    fixes = []
    for k in range(4):
        into_both_rows(cor.at[k], coarse[k])
        fixes.append(cor[k])
    for u in range(-1, layers + 1):
        before = new_out[u + 1] if u < 2 else new_in[u - 2]
        plane.put(e1.at[u + 1], before + fixes[(u + 2) // 2])

    def fx1(u):
        return fx_in[u] if u >= 0 else fx_out[-1 - u]

    def inv1(u):
        return inv_in[u - 1] if u > 0 else inv_out[u + 1]

    def around1(u):
        if u < 0:
            return in_layer(plane, fy_out, fz_out, fzl_out, e1.at[0])
        return in_layer(plane, fy_in.at[u], fz_in.at[u], fzl_in.at[u], e1.at[u + 1])

    def updated1(u):
        sums = around1(u) + (fx1(u) * e1[u + 2, body1] + fx1(u - 1) * e1[u, body1])
        return (source[own_layer(u, layers)] + sums) * inv1(u)

    for u in range(layers):
        e1[u + 1, body1] = jnp.where(plane.even(u), updated1(u), e1[u + 1, body1])
    e1[0, body1] = (known_out[...] + fx1(-2) * fixes[0] + (around1(-1) + fx1(-1) * e1[1, body1])) * inv1(-1)
    into_both_rows(cor.at[4], within_in[4])
    sums = cor[4] + fx1(layers) * fixes[3] + (around1(layers) + fx1(layers - 1) * e1[layers, body1])
    e1[layers + 1, body1] = sums * inv1(layers)
    for u in range(layers):
        solved[u] = jnp.where(plane.even(u), e1[u + 1, body1], updated1(u))
        copies.append(
            pltpu.make_async_copy(solved.at[u], solved_out.at[own_layer(u, layers)], sems.at[u + 1])
        )
        copies[-1].start()
    for copy in copies:
        copy.wait()


def f32(*shape):
    return jax.ShapeDtypeStruct(shape, jnp.float32)


def vmem(*shape):
    return pltpu.VMEM(shape, jnp.float32)


def call(kernel, outs, scratch, operands, out_space=pltpu.VMEM):
    def size(shape):
        count = 4
        for extent in shape:
            count *= extent
        return count

    sized = [array for array in (*scratch, *outs, *operands) if hasattr(array, "shape")]
    asked = 8 * 2**20 + sum(size(array.shape) for array in sized)
    return pl.pallas_call(
        kernel,
        out_shape=tuple(outs),
        in_specs=[pl.BlockSpec(memory_space=pltpu.VMEM)] * len(operands),
        out_specs=tuple([pl.BlockSpec(memory_space=out_space)] * len(outs)),
        scratch_shapes=scratch,
        compiler_params=pltpu.CompilerParams(vmem_limit_bytes=asked),
    )(*operands)


def on_device(iterate, source, phase_field, block_owner):
    layers, height, depth = iterate.shape
    half, quarter = height // 2, height // 4
    blocks = lax.axis_size("gx")
    padded, padded2 = height + 2 * PAD, half + 2 * PAD
    inputs = sum(
        jnp.pad(block, ((k * layers, (2 - k) * layers), (0, 0), (0, 0)))
        for k, block in enumerate((iterate, source, phase_field))
    )
    edge, = call(edge_kernel, [f32(3 * height + half, depth)], [], (inputs,))
    layer, tile, five = (height, depth), (half, depth), layers + 1
    message, known1, *fine = call(
        chip_kernel,
        [
            f32(chip_rows(height)[1], depth), f32(*layer), f32(3, *layer), f32(five, *layer),
            f32(five, padded, depth), f32(five, *layer), f32(five, *layer), f32(layers, *layer),
        ],
        [vmem(five, *layer)] + [vmem(five, padded, depth)] * 3 + [vmem(10, *layer)],
        (inputs, within_chip(edge)),
    )
    within, outer, fx2, *border = call(
        border_kernel,
        [
            f32(5, *tile), f32(4, *tile), f32(*tile), f32(3, *layer), f32(*layer), f32(2, *layer),
            f32(padded, depth), f32(*layer), f32(*layer), f32(2, *layer),
        ],
        [
            vmem(1, padded, depth), vmem(2, padded, depth), vmem(4, padded, depth), vmem(8, *layer),
            vmem(2, padded, depth), vmem(2, *layer), vmem(2, *layer),
        ],
        (block_owner, inputs, message, known1, *fine, between_chips(message)),
    )
    within_in = within_chip(within)
    plain = f32(3, *tile)
    slots, *middle = call(
        middle_down_kernel,
        [f32(blocks // 2, 2, quarter, depth), plain, plain, plain, plain, f32(3, padded2, depth)] + [plain] * 3,
        [vmem(5, padded2, depth), vmem(2, *tile)],
        (within, fx2, outer, within_in),
    )
    kinds = [list(range(core, blocks, 2)) for core in range(2)]
    same_cores = lax.all_to_all(slots, "gx", 0, 0, axis_index_groups=kinds, tiled=True)
    other_cores = within_chip(same_cores)
    solved, owned = call(
        coarse_kernel,
        [f32(layers, *layer), f32(1, quarter, depth // 4)],
        [
            vmem(blocks // 4, quarter, depth), vmem(4, blocks // 4, quarter + 2 * PAD, depth), vmem(7, *tile),
            vmem(5, padded2, depth), vmem(layers + 2, padded, depth), vmem(5, *layer), vmem(layers, *layer),
            vmem(1, quarter, depth // 4), pltpu.SMEM((blocks,), jnp.int32),
            pltpu.SemaphoreType.DMA, pltpu.SemaphoreType.DMA((layers + 1,)),
        ],
        (block_owner, same_cores, other_cores, *middle, inputs, *fine, *border, within_in),
        pl.ANY,
    )
    return solved, owned


def solution(mesh):
    split = P(("groups", "gx"), None, None)
    return jax.shard_map(
        on_device,
        mesh=mesh,
        in_specs=(split, split, split, P("groups")),
        out_specs=(split, split),
        check_vma=False,
    )
```

```python
import jax
import jax.numpy as jnp
from jax import lax
from jax.experimental import pallas as pl
from jax.experimental.pallas import tpu as pltpu
from jax.sharding import PartitionSpec as P

STIFFNESS = 100.0
EPSILON = 0.01
COARSE_SWEEPS = 4
PAD = 8


def between_chips(block):
    return lax.ppermute(block, "gx", [(i, i + 1 if i % 2 else i - 1) for i in range(1, lax.axis_size("gx") - 1)])


def within_chip(block):
    return lax.ppermute(block, "gx", [(i, i ^ 1) for i in range(lax.axis_size("gx"))])


def by_side(across, within):
    on_left = lax.axis_index("gx") % 2 == 0
    return jnp.where(on_left, across, within), jnp.where(on_left, within, across)


def lanes_of(shape):
    return lax.broadcasted_iota(jnp.int32, shape, len(shape) - 1)


def rows_of(shape):
    return lax.broadcasted_iota(jnp.int32, shape, len(shape) - 2)


def ahead(values, step, axis):
    return pltpu.roll(values, values.shape[axis] - step, axis)


def behind(values, step, axis):
    return pltpu.roll(values, step, axis)


def with_partner(values, step, axis):
    index = lax.broadcasted_iota(jnp.int32, values.shape, axis)
    partner = jnp.where((index & step) == 0, ahead(values, step, axis), behind(values, step, axis))
    return values + partner


def even_row_sum(scratch, rows):
    return scratch[pl.ds(0, rows, 2), :] + scratch[pl.ds(1, rows, 2), :]


def core_of():
    return lax.axis_index("gx") % 2


def own_layer(u, layers):
    return u + core_of() * (layers - 1 - 2 * u)


def three_parts(ref):
    third = ref.shape[0] // 3
    return [ref.at[pl.ds(k * third, third)] for k in range(3)]


def odd_cells(ref, rows, first):
    return jnp.where(first, ref[pl.ds(0, rows, 2), :], ref[pl.ds(1, rows, 2), :])


def into_both_rows(ref, values):
    rows = values.shape[0]
    ref[pl.ds(0, rows, 2), :] = values
    ref[pl.ds(1, rows, 2), :] = values


def cell_coef(value):
    return STIFFNESS * (value * value + EPSILON)


class Plane:
    def __init__(self, height, depth):
        self.height, self.half, self.depth = height, height // 2, depth
        self.row, self.lane = rows_of((height, depth)), lanes_of((height, depth))
        self.parity = self.row + self.lane + core_of()
        self.half_lane = lanes_of((self.half, depth))
        self.body = pl.ds(PAD, height)
        self.up, self.down = pl.ds(PAD + 1, height), pl.ds(PAD - 1, height)

    def even(self, u):
        return ((self.parity + u) & 1) == 0

    def odd_first(self, u):
        return ((self.half_lane + core_of() + u) & 1) != 0

    def put(self, ref, values):
        edge = jnp.zeros((PAD, self.depth), jnp.float32)
        ref[:PAD] = edge
        ref[PAD + self.height:] = edge
        ref[self.body] = values

    def face_y(self, here):
        return jnp.where(self.row < self.height - 1, 0.5 * (here + ahead(here, 1, 0)), 0.0)

    def face_z(self, here):
        return jnp.where(self.lane < self.depth - 1, 0.5 * (here + ahead(here, 1, 1)), 0.0)

    def packed(self, outer, inner, core):
        return jnp.where((self.half_lane & 1) == core, outer, inner)

    def both_rows(self, ref):
        return even_row_sum(ref, self.half)

    def summed(self, values, ref):
        ref[...] = values
        return with_partner(self.both_rows(ref), 1, 1)

    def odd_rows(self, values, ref):
        ref[...] = values
        return with_partner(ref[pl.ds(1, self.half, 2), :], 1, 1)

    def odd_lanes(self, values, ref):
        ref[...] = values
        sums = self.both_rows(ref)
        return jnp.where((self.half_lane & 1) == 0, ahead(sums, 1, 1), sums)


def in_layer(plane, fy, fz, fzl, padded):
    here = padded[plane.body]
    total = fy[plane.body] * padded[plane.up] + fy[plane.down] * padded[plane.down]
    return total + (fz[...] * ahead(here, 1, 1) + fzl[...] * behind(here, 1, 1))


def edge_kernel(inputs, out):
    iterate, source, phase = three_parts(inputs)
    layers, height, depth = iterate.shape
    plane = Plane(height, depth)
    near, inner, far = [own_layer(u, layers) for u in (layers - 1, layers - 2, layers - 3)]
    coef_near, coef_inner, coef_far = [cell_coef(phase[k]) for k in (near, inner, far)]

    def around(here, e):
        fy, fz = plane.face_y(here), plane.face_z(here)
        fyl, fzl = behind(fy, 1, 0), behind(fz, 1, 1)
        total = fy * ahead(e, 1, 0) + fyl * behind(e, 1, 0)
        return total + fz * ahead(e, 1, 1) + fzl * behind(e, 1, 1), fy + fyl + fz + fzl

    face_near, face_far = 0.5 * (coef_inner + coef_near), 0.5 * (coef_inner + coef_far)
    total, weight = around(coef_inner, iterate[inner])
    total = total + face_near * iterate[near] + face_far * iterate[far]
    updated = (source[inner] + total) / (1.0 + (face_near + face_far + weight))
    total, _ = around(coef_near, iterate[near])
    known = jnp.where(plane.even(layers - 1), total + face_near * iterate[inner], face_near * updated)
    out[:height] = coef_near
    out[height:2 * height] = coef_inner
    out[2 * height:3 * height] = source[near] + known
    out[3 * height:] = odd_cells(iterate.at[near], plane.half, plane.odd_first(layers - 1))


def chip_rows(height):
    half, at, places = height // 2, 0, {}
    for name, size in (
        ("coef0", height), ("coef1", height), ("known0", height), ("old0", half), ("moved1", half), ("face2", half),
        ("source2", half), ("fx2", half), ("far2", half),
    ):
        places[name] = pl.ds(at, size)
        at += size
    return places, at


def chip_kernel(
    owner_of, inputs, within_in,
    message, own2, known1, new, fx, fy, fz, fzl, inv,
    cell, old, even, change, turn,
):
    iterate, source, phase = three_parts(inputs)
    layers, height, depth = iterate.shape
    plane = Plane(height, depth)
    body, half = plane.body, plane.half
    places, _ = chip_rows(height)
    margin = layers

    def part(k):
        return within_in[k * height:(k + 1) * height]

    def s(u):
        return source[own_layer(u, layers)]

    for u in range(layers):
        cell[u] = cell_coef(phase[own_layer(u, layers)])
        plane.put(old.at[u], iterate[own_layer(u, layers)])
    cell[margin] = part(0)
    into_both_rows(turn.at[0], within_in[3 * height:])
    plane.put(old.at[margin], turn[0])
    for u in range(margin + 1):
        here = cell[u]
        fx[u] = 0.5 * (here + (cell[u + 1] if u < margin else part(1)))
        plane.put(fy.at[u], plane.face_y(here))
        face = plane.face_z(here)
        fz[u] = face
        fzl[u] = behind(face, 1, 1)
    for u in range(1, margin + 1):
        weight = (fx[u] + fx[u - 1]) + (fy[u, body] + fy[u, plane.down]) + (fz[u] + fzl[u])
        inv[u - 1] = 1.0 / (1.0 + weight)

    def around(ref, u):
        return in_layer(plane, fy.at[u], fz.at[u], fzl.at[u], ref.at[u])

    for u in range(1, margin):
        total = s(u) + around(old, u) + (fx[u] * old[u + 1, body] + fx[u - 1] * old[u - 1, body])
        plane.put(even.at[u], total * inv[u - 1])
    plane.put(even.at[margin], (part(2) + fx[margin - 1] * old[margin - 1, body]) * inv[margin - 1])
    for u in range(2, margin + 1):
        if u < margin:
            total = s(u) + around(even, u) + (fx[u] * even[u + 1, body] + fx[u - 1] * even[u - 1, body])
        else:
            total = part(2) + around(even, u) + fx[u - 1] * even[u - 1, body]
        fresh = total * inv[u - 1]
        new[u - 2] = fresh
        plane.put(change.at[u], fresh - old[u, body])

    one = fx[1] * change[2, body]
    two = around(change, 2) + fx[2] * change[3, body]
    three = around(change, 3) + (fx[2] * change[2, body] + fx[3] * change[4, body])
    outer = jnp.where(plane.even(1), one, 0.0)
    inner = jnp.where(plane.even(2), two, 0.0) + jnp.where(plane.even(3), three, 0.0)
    core = core_of()

    def tile(name, outer, inner):
        message[places[name], :] = plane.packed(outer, inner, core)

    tile("source2", plane.summed(outer, turn.at[1]), plane.summed(inner, turn.at[2]))
    tile("fx2", plane.summed(fx[1], turn.at[3]), plane.summed(fx[3], turn.at[4]))
    fy2 = [plane.odd_rows(fy[u, body] + fy[u + 1, body], turn.at[5 + u // 2]) for u in (0, 2)]
    fz2 = [plane.odd_lanes(fz[u] + fz[u + 1], turn.at[7 + u // 2]) for u in (0, 2)]
    own2[0], own2[1] = plane.packed(*fy2, core), plane.packed(*fz2, core)
    tile("far2", fy2[1], fz2[1])
    for u in range(2):
        message[places["coef%d" % u], :] = cell[u]
    first = s(0) + around(old, 0) + fx[0] * old[1, body]
    second = s(0) + fx[0] * even[1, body]
    message[places["known0"], :] = jnp.where(plane.even(0), first, second)
    message[places["old0"], :] = odd_cells(iterate.at[own_layer(0, layers)], half, plane.odd_first(0))
    total = s(1) + around(even, 1) + fx[1] * even[2, body]
    known1[...] = total
    turn[9] = total * inv[0] - old[1, body]
    message[places["moved1"], :] = odd_cells(turn.at[9], half, plane.odd_first(1))
    message[places["face2"], :] = odd_cells(fx.at[1], half, plane.odd_first(1))


def border_kernel(
    inputs, message, own2, known1, new_in, fx_in, fy_in, fz_in, fzl_in, inv_in, across_in,
    within, outer2, fx2_in, new, known, fx, fy, fz, fzl, inv,
    old, even, change, turn, face_y, face_z, face_zl,
):
    iterate, source, _ = three_parts(inputs)
    layers, height, depth = iterate.shape
    plane = Plane(height, depth)
    body, half = plane.body, plane.half
    places, _ = chip_rows(height)
    core, last = core_of(), lax.axis_size("gx") - 1
    position = lax.axis_index("gx")

    def mine(name):
        return message[places[name], :]

    def theirs(name):
        return across_in[places[name], :]

    def opened(name, k):
        into_both_rows(turn.at[k], theirs(name))
        return turn[k]

    for k in range(2):
        here = theirs("coef%d" % k)
        plane.put(face_y.at[k], plane.face_y(here))
        face = plane.face_z(here)
        face_z[k] = face
        face_zl[k] = behind(face, 1, 1)
    fy[...], fz[...], fzl[...] = face_y[0], face_z[0], face_zl[0]
    there = position - 1 + 2 * core
    border = jnp.where((there >= 0) & (there <= last), 0.5 * (mine("coef0") + theirs("coef0")), 0.0)
    face1 = 0.5 * (theirs("coef0") + theirs("coef1"))
    face2 = opened("face2", 2)
    fx[0], fx[1] = border, face1

    def inverse(faces, fy, fz, fzl):
        weight = faces + (fy[body] + fy[plane.down]) + (fz[...] + fzl[...])
        return 1.0 / (1.0 + weight)

    inv_own = inverse(fx_in[0] + border, fy_in.at[0], fz_in.at[0], fzl_in.at[0])
    inv_near = inverse(border + face1, face_y.at[0], face_z.at[0], face_zl.at[0])
    inv_far = inverse(face1 + face2, face_y.at[1], face_z.at[1], face_zl.at[1])
    inv[0], inv[1] = inv_near, inv_own
    old_own, old_next = iterate[own_layer(0, layers)], iterate[own_layer(1, layers)]
    old_near, far = opened("old0", 0), opened("moved1", 1)
    even_own = (mine("known0") + border * old_near) * inv_own
    even_near = (theirs("known0") + border * old_own) * inv_near
    plane.put(even.at[0], even_near)
    plane.put(even.at[1], even_own)

    def near(ref, k):
        return in_layer(plane, face_y.at[k], face_z.at[k], face_zl.at[k], ref)

    def own(ref, u):
        return in_layer(plane, fy_in.at[u], fz_in.at[u], fzl_in.at[u], ref)

    odd_own = (mine("known0") + own(even.at[1], 0) + border * even_near) * inv_own
    odd_near = (theirs("known0") + near(even.at[0], 0) + border * even_own) * inv_near
    odd_next = (known1[...] + fx_in[0] * even_own) * inv_in[0]
    far = far + face1 * even_near * inv_far
    new[0], new[1], new[2] = odd_near, odd_own, odd_next
    near_by, here, following = odd_near - old_near, odd_own - old_own, odd_next - old_next
    for k, values in enumerate((far, near_by, here, following)):
        plane.put(change.at[k], values)
    plane.put(old.at[0], old_near)
    known[...] = theirs("known0") + face1 * far - near(old.at[0], 0)

    def residual(u, values):
        return jnp.where(plane.even(u), values, 0.0)

    own_outer = residual(1, own(change.at[3], 1) + fx_in[0] * here)
    own_outer = own_outer + residual(0, own(change.at[2], 0) + (fx_in[0] * following + border * near_by))
    own_inner = residual(2, fx_in[1] * following)
    its_outer = residual(-1, near(change.at[1], 0) + (face1 * far + border * here))
    its_outer = its_outer + residual(-2, near(change.at[0], 1) + face1 * near_by)
    its_inner = residual(-3, face2 * far)
    sums = [plane.summed(values, turn.at[3 + k]) for k, values in enumerate((own_outer, own_inner, its_outer, its_inner))]
    within[0] = mine("source2") + plane.packed(sums[0], sums[1], core)
    outer2[0] = theirs("source2") + plane.packed(sums[2], sums[3], 1 - core)
    outer2[1] = theirs("fx2")
    far2 = theirs("far2")
    far2_swap = jnp.where((plane.half_lane & 1) == 0, ahead(far2, 1, 1), behind(far2, 1, 1))
    near_fy2 = plane.odd_rows(face_y[0, body] + face_y[1, body], turn.at[1])
    near_fz2 = plane.odd_lanes(face_z[0] + face_z[1], turn.at[2])
    outer2[2] = plane.packed(near_fy2, far2_swap, 1 - core)
    outer2[3] = plane.packed(near_fz2, far2, 1 - core)
    fx2_in[...] = mine("fx2")
    middle = jnp.where((plane.half_lane & 1) == 0, ahead(mine("fx2"), 1, 1), behind(mine("fx2"), 1, 1))
    within[1] = plane.packed(plane.summed(border, turn.at[7]), middle, core)
    within[2], within[3] = own2[0], own2[1]
    turn[0] = source[own_layer(layers - 1, layers)] + fx_in[layers - 2] * new_in[layers - 4]
    within[4] = odd_cells(turn.at[0], half, jnp.logical_not(plane.odd_first(layers - 1)))


def neigh2(e2, fx2, fxl2, fy2, fz2, fzl2, first_of_two, tiles):
    half = fx2.shape[1]
    body, up, down = pl.ds(PAD, half), pl.ds(PAD + 1, half), pl.ds(PAD - 1, half)
    needed = range(tiles[0], tiles[-1] + 3)
    here = {j: e2[j, body] for j in needed}
    after = {j: ahead(here[j], 1, 1) for j in needed}
    before = {j: behind(here[j], 1, 1) for j in needed}
    found = []
    for j in tiles:
        k = j + 1
        upper = jnp.where(first_of_two, after[k], before[k + 1])
        lower = jnp.where(first_of_two, after[k - 1], before[k])
        sums = fx2[j] * upper + fxl2[j] * lower
        sums = sums + fy2[j, body] * e2[k, up] + fy2[j, down] * e2[k, down]
        sums = sums + fz2[j] * ahead(here[k], 2, 1) + fzl2[j] * behind(here[k], 2, 1)
        found.append(sums)
    return found


def parities2(half, lanes):
    row, lane = rows_of((half, lanes)), lanes_of((half, lanes))
    return (lane & 1) == 0, ((row + (lane & 1) + (lane >> 1)) & 1) == 0


def group(values):
    return with_partner(with_partner(values, 1, 1), 2, 1)


def middle_down_kernel(
    own, fx2_in, outer, within_in,
    slots, e2_out, s2, fx2, fxl2, fy2, fz2, fzl2, inv2,
    e2, pair,
):
    _, half, lanes = own.shape
    quarter = half // 2
    position = lax.axis_index("gx")
    first_of_two, even2 = parities2(half, lanes)
    body, down = pl.ds(PAD, half), pl.ds(PAD - 1, half)
    edge = jnp.zeros((PAD, lanes), jnp.float32)
    for j in range(5):
        e2[j] = jnp.zeros((half + 2 * PAD, lanes), jnp.float32)
    def three(k):
        left, right = by_side(outer[k], within_in[k])
        return left, own[k], right

    for j, (source, fy, fz) in enumerate(zip(three(0), three(2), three(3))):
        s2[j] = source
        fy2[j, :PAD] = edge
        fy2[j, body] = fy
        fy2[j, PAD + half:] = edge
        fz2[j] = fz
        fzl2[j] = behind(fz, 2, 1)
    left_fx, _, right_fx = three(1)
    own_fx = by_side(fx2_in[...], own[1])
    fx2[0] = jnp.where(first_of_two, ahead(left_fx, 1, 1), behind(own_fx[1], 1, 1))
    fx2[1] = own_fx[0]
    fx2[2] = right_fx
    fxl2[0] = left_fx
    fxl2[1] = own_fx[1]
    fxl2[2] = jnp.where(first_of_two, ahead(own_fx[0], 1, 1), behind(right_fx, 1, 1))
    for j in range(3):
        weight = fx2[j] + fxl2[j] + fy2[j, body] + fy2[j, down] + fz2[j] + fzl2[j]
        inverse = 1.0 / (8.0 + weight)
        inv2[j] = inverse
        e2[j + 1, body] = jnp.where(even2, s2[j] * inverse, 0.0)

    def neigh(tiles):
        return neigh2(e2, fx2, fxl2, fy2, fz2, fzl2, first_of_two, tiles)

    fresh = [
        jnp.where(even2, e2[j + 1, body], (s2[j] + sums) * inv2[j]) for j, sums in enumerate(neigh((0, 1, 2)))
    ]
    for j in range(3):
        e2[j + 1, body] = fresh[j]
        e2_out[j] = fresh[j]
    pair[0] = jnp.where(even2, neigh((1,))[0], 0.0)
    lane = lanes_of((quarter, lanes))
    slot = position // (slots.shape[0] // 2)
    odd_layer, odd_depth, item = (lane & 1) != 0, (lane & 2) != 0, (lane - slot) & 3
    source = group(even_row_sum(pair.at[0], quarter))
    fx = group(jnp.where(odd_layer, even_row_sum(fx2.at[1], quarter), 0.0))
    fy = group(fy2[1, pl.ds(PAD + 1, quarter, 2), :])
    fz = group(jnp.where(odd_depth, even_row_sum(fz2.at[1], quarter), 0.0))
    tile = jnp.where(item == 0, source, jnp.where(item == 1, fx, jnp.where(item == 2, fy, fz)))
    first = (((lane & 1) + (lane >> 1)) & 1) != 0
    pair[0] = jnp.where(first_of_two, fresh[2], fresh[1])
    pair[1] = jnp.where(first_of_two, fresh[1], fresh[0])
    for_left = odd_cells(pair.at[0], quarter, first)
    for_right = odd_cells(pair.at[1], quarter, first)
    for c in range(slots.shape[0]):
        slots[c, 0] = tile
        slots[c, 1] = jnp.where(position < 2 * c + 1 - position % 2, for_right, for_left)


def joined(one, two):
    return jnp.concatenate([part for part in (one, two) if part.shape[0]], 0)


class Level:
    def __init__(self, mass, source, faces, row_step, lane_step, slot_step):
        self.source, self.row_step, self.lane_step, self.slot_step = source, row_step, lane_step, slot_step
        self.fx, self.fy, self.fz = faces
        self.tiles = source.shape[0]
        shape = source.shape
        self.lane = lanes_of(shape)
        layer = lax.broadcasted_iota(jnp.int32, shape, 0) if self.tiles > 1 else self.lane // slot_step
        self.even = ((layer + rows_of(shape) // row_step + self.lane // lane_step) & 1) == 0
        self.fxl = self.lower(self.fx)
        self.fyl = self.row_shifts(self.fy)[1]
        self.fzl = behind(self.fz, lane_step, 2)
        weight = (self.fx + self.fxl) + (self.fy + self.fyl) + (self.fz + self.fzl)
        self.inv = 1.0 / (mass + weight)

    def upper(self, e):
        return joined(e[1:], ahead(e[:1], self.slot_step, 2))

    def lower(self, e):
        return joined(behind(e[-1:], self.slot_step, 2), e[:-1])

    def row_shifts(self, e):
        return ahead(e, self.row_step, 1), behind(e, self.row_step, 1)

    def neigh(self, e):
        above, below = self.row_shifts(e)
        total = (self.fx * self.upper(e) + self.fxl * self.lower(e)) + (self.fy * above + self.fyl * below)
        return total + (self.fz * ahead(e, self.lane_step, 2) + self.fzl * behind(e, self.lane_step, 2))

    def update(self, e):
        return (self.source + self.neigh(e)) * self.inv

    def cycle(self, deeper):
        odd = self.update(self.source * self.inv)
        residual = jnp.where(self.even, self.neigh(odd), 0.0)
        fix = deeper(self.restricted(residual), self.coarse_faces())
        even = self.update(odd + self.prolonged(fix))
        return jnp.where(self.even, even, self.update(even))

    def coarse_slot_step(self):
        return self.slot_step if self.tiles > 1 else 2 * self.slot_step

    def pairs(self, values):
        if self.tiles == 1:
            return with_partner(values, self.slot_step, 2)
        halves = values.reshape(self.tiles // 2, 2, *values.shape[1:])
        return halves[:, 0] + halves[:, 1]

    def odd_layers(self, values):
        if self.tiles == 1:
            return with_partner(jnp.where((self.lane & self.slot_step) != 0, values, 0.0), self.slot_step, 2)
        return values.reshape(self.tiles // 2, 2, *values.shape[1:])[:, 1]

    def row_pairs(self, values):
        return with_partner(values, self.row_step, 1)

    def odd_rows(self, values):
        odd = (rows_of(values.shape) & self.row_step) != 0
        return with_partner(jnp.where(odd, values, 0.0), self.row_step, 1)

    def restricted(self, values):
        return with_partner(self.row_pairs(self.pairs(values)), self.lane_step, 2)

    def coarse_faces(self):
        fx = with_partner(self.row_pairs(self.odd_layers(self.fx)), self.lane_step, 2)
        fy = with_partner(self.odd_rows(self.pairs(self.fy)), self.lane_step, 2)
        return fx, fy, self.restricted(jnp.where((self.lane & self.lane_step) != 0, self.fz, 0.0))

    def prolonged(self, fix):
        if self.tiles == 1:
            return fix
        both = jnp.concatenate([fix[:, None], fix[:, None]], 1)
        return both.reshape(self.tiles, *fix.shape[1:])


class Rows(Level):
    def __init__(self, mass, source, faces, scratch):
        self.scratch, self.used = scratch, 0
        self.rows = source.shape[1]
        super().__init__(mass, source, faces, 1, 4, 1)

    def place(self):
        self.used += 1
        return self.scratch.at[self.used % self.scratch.shape[0]]

    def row_shifts(self, e):
        place = self.place()
        edge = jnp.zeros((e.shape[0], PAD, e.shape[2]), jnp.float32)
        place[:, :PAD] = edge
        place[:, PAD + self.rows:] = edge
        place[:, pl.ds(PAD, self.rows)] = e
        return place[:, pl.ds(PAD + 1, self.rows)], place[:, pl.ds(PAD - 1, self.rows)]

    def every_other(self, values, starts):
        place, tiles = self.place(), values.shape[0]
        place[:tiles, : self.rows] = values
        found = 0.0
        for start in starts:
            found = found + jnp.concatenate(
                [place[j, pl.ds(start, self.rows // 2, 2), :][None] for j in range(tiles)], 0
            )
        return found

    def row_pairs(self, values):
        return self.every_other(values, (0, 1))

    def odd_rows(self, values):
        return self.every_other(values, (1,))

    def prolonged(self, fix):
        place, tiles = self.place(), fix.shape[0]
        for j in range(tiles):
            into_both_rows(place.at[j, pl.ds(0, self.rows)], fix[j])
        return super().prolonged(place[:tiles, : self.rows])


def coarsest(mass, source, faces, *steps):
    row_step, lane_step, slot_step = steps
    level = Level(mass, source, faces, *steps)
    counts = source.shape[1] // row_step, source.shape[2] // lane_step, 4 // slot_step
    frames = [(m, k, q) for m in range(counts[0]) for k in range(counts[1]) for q in range(counts[2])]
    place = level.lane & 3

    def spread(values):
        copies = {}
        for m, k, q in frames:
            if k:
                copies[m, k, q] = behind(copies[m, 0, q], k * lane_step, 2)
            elif q:
                by = q * slot_step
                one, two = behind(copies[m, 0, 0], by, 2), ahead(copies[m, 0, 0], 4 - by, 2)
                copies[m, k, q] = jnp.where(place >= by, one, two)
            else:
                copies[m, k, q] = behind(values, m * row_step, 1) if m else values
        return copies

    start, inv, fx, fy, fz = [spread(values) for values in (source * level.inv, level.inv, level.fx, level.fy, level.fz)]

    def shifted(copies, frame, axis, by):
        moved = list(frame)
        moved[axis] = (frame[axis] - by) % counts[axis]
        return copies[tuple(moved)]

    def along_x(copies, frame, by):
        here, wrapped = copies[frame], shifted(copies, frame, 2, by)
        return joined(here[1:], wrapped[:1]) if by > 0 else joined(wrapped[-1:], here[:-1])

    weights = {}
    for frame in frames:
        pairs = [
            (fx[frame], along_x(fx, frame, -1)),
            (fy[frame], shifted(fy, frame, 0, -1)),
            (fz[frame], shifted(fz, frame, 1, -1)),
        ]
        weights[frame] = [(up * inv[frame], low * inv[frame]) for up, low in pairs]

    def update(e):
        fresh = {}
        for frame in frames:
            (x_up, x_low), (y_up, y_low), (z_up, z_low) = weights[frame]
            total = x_up * along_x(e, frame, 1) + x_low * along_x(e, frame, -1)
            total = total + (y_up * shifted(e, frame, 0, 1) + y_low * shifted(e, frame, 0, -1))
            total = total + (z_up * shifted(e, frame, 1, 1) + z_low * shifted(e, frame, 1, -1))
            fresh[frame] = start[frame] + total
        return fresh

    even = start
    odd = update(even)
    for turn in range(COARSE_SWEEPS - 1):
        even = update(odd)
        odd = update(even)
    return jnp.where(level.even, even[0, 0, 0], odd[0, 0, 0])


def small_cycle(mass, source, faces, row_step, lane_step, slot_step, between):
    if between == 0:
        return coarsest(mass, source, faces, row_step, lane_step, slot_step)
    level = Level(mass, source, faces, row_step, lane_step, slot_step)
    return level.cycle(
        lambda inner, inner_faces: small_cycle(
            8.0 * mass, inner, inner_faces, 2 * row_step, 2 * lane_step, level.coarse_slot_step(), between - 1
        )
    )


def coarse_kernel(
    owner_of, same_cores, other_cores, e2_in, s2, fx2, fxl2, fy2, fz2, fzl2, inv2,
    inputs, new_in, fx_in, fy_in, fz_in, fzl_in, inv_in,
    new_out, known_out, fx_out, fy_out, fz_out, fzl_out, inv_out, within_in,
    solved_out, owned_out,
    e3, rows3, pair, e2, e1, cor, solved, owned, owner_here, fetch_sem, sems,
):
    fetch = pltpu.make_async_copy(owner_of, owner_here, fetch_sem)
    fetch.start()
    chips, _, quarter, lanes = same_cores.shape
    blocks = 2 * chips
    half, height = 2 * quarter, 4 * quarter
    position, last = lax.axis_index("gx"), blocks - 1

    slot = lanes_of((quarter, lanes)) & 3
    spread = blocks // 4
    tiles = []
    for chip in range(chips):
        tiles.extend(by_side(same_cores[chip, 0], other_cores[chip, 0]))
    items = []
    for k in range(4):
        packs = []
        for j in range(spread):
            value = tiles[j + (3 - k) % 4 * spread]
            for at in range(3):
                value = jnp.where(slot == at, tiles[j + (at - k) % 4 * spread], value)
            if k:
                value = jnp.where(slot < 4 - k, ahead(value, k, 1), behind(value, 4 - k, 1))
            packs.append(value[None])
        items.append(jnp.concatenate(packs, 0))
    third = Rows(64.0, items[0], items[1:], rows3)
    e3[...] = third.cycle(
        lambda inner, faces: small_cycle(512.0, inner, faces, 1, 8, third.coarse_slot_step(), 2)
    )

    fetch.wait()
    owner = owner_here[position]
    wide, narrow = lanes_of((lanes, lanes)), rows_of((lanes, lanes))
    take = jnp.where(narrow == 4 * wide + owner // spread, 1.0, 0.0)
    block = jnp.dot(
        e3[owner % spread], take, precision=lax.Precision.HIGHEST, preferred_element_type=jnp.float32
    )
    owned[0] = block[:, : lanes // 4]
    copies = [pltpu.make_async_copy(owned, owned_out, sems.at[0])]
    copies[0].start()

    first_of_two, even2 = parities2(half, lanes)
    body2 = pl.ds(PAD, half)
    edge = jnp.zeros((PAD, lanes), jnp.float32)
    left = other_cores[jnp.maximum(position - 1, 0) // 2, 1]
    right = other_cores[jnp.minimum(position + 1, last) // 2, 1]
    into_both_rows(pair.at[5], left)
    into_both_rows(pair.at[6], right)
    left, right = pair[5], pair[6]
    before = (
        left, jnp.where(first_of_two, left, e2_in[0]), e2_in[1], jnp.where(first_of_two, e2_in[2], right), right
    )
    for k in range(5):
        j = jnp.clip(position + k - 2, 0, last)
        into_both_rows(pair.at[k], group(jnp.where(slot == j // spread, e3[j % spread], 0.0)))
        e2[k, :PAD] = edge
        e2[k, PAD + half:] = edge
        e2[k, body2] = before[k] + pair[k]

    def update2():
        sums = neigh2(e2, fx2, fxl2, fy2, fz2, fzl2, first_of_two, (0, 1, 2))
        return [(s2[j] + sums[j]) * inv2[j] for j in range(3)]

    fresh = update2()
    for j in range(3):
        e2[j + 1, body2] = fresh[j]
    fixes2 = [jnp.where(even2, even, odd) for even, odd in zip(fresh, update2())]

    _, source, _ = three_parts(inputs)
    layers = source.shape[0]
    plane = Plane(height, lanes)
    body1 = plane.body
    core = core_of()
    near_lane = (lanes_of((half, lanes)) & 1) == core
    swaps = [jnp.where(first_of_two, ahead(v, 1, 1), behind(v, 1, 1)) for v in fixes2]
    outer, inner = by_side(fixes2[0], fixes2[2])
    outer_swap, inner_swap = by_side(swaps[0], swaps[2])
    coarse = (
        jnp.where(near_lane, outer_swap, outer), jnp.where(near_lane, fixes2[1], swaps[1]),
        jnp.where(near_lane, swaps[1], fixes2[1]), jnp.where(near_lane, inner, inner_swap),
    )
    fixes = []
    for k in range(4):
        into_both_rows(cor.at[k], coarse[k])
        fixes.append(cor[k])
    for u in range(-1, layers + 1):
        before = new_out[u + 1] if u < 2 else new_in[u - 2]
        plane.put(e1.at[u + 1], before + fixes[(u + 2) // 2])

    def fx1(u):
        return fx_in[u] if u >= 0 else fx_out[-1 - u]

    def inv1(u):
        return inv_in[u - 1] if u > 0 else inv_out[u + 1]

    def around1(u):
        if u < 0:
            return in_layer(plane, fy_out, fz_out, fzl_out, e1.at[0])
        return in_layer(plane, fy_in.at[u], fz_in.at[u], fzl_in.at[u], e1.at[u + 1])

    def updated1(u):
        sums = around1(u) + (fx1(u) * e1[u + 2, body1] + fx1(u - 1) * e1[u, body1])
        return (source[own_layer(u, layers)] + sums) * inv1(u)

    for u in range(layers):
        e1[u + 1, body1] = jnp.where(plane.even(u), updated1(u), e1[u + 1, body1])
    e1[0, body1] = (known_out[...] + fx1(-2) * fixes[0] + (around1(-1) + fx1(-1) * e1[1, body1])) * inv1(-1)
    into_both_rows(cor.at[4], within_in[4])
    sums = cor[4] + fx1(layers) * fixes[3] + (around1(layers) + fx1(layers - 1) * e1[layers, body1])
    e1[layers + 1, body1] = sums * inv1(layers)
    for u in range(layers):
        solved[u] = jnp.where(plane.even(u), e1[u + 1, body1], updated1(u))
        copies.append(
            pltpu.make_async_copy(solved.at[u], solved_out.at[own_layer(u, layers)], sems.at[u + 1])
        )
        copies[-1].start()
    for copy in copies:
        copy.wait()


def f32(*shape):
    return jax.ShapeDtypeStruct(shape, jnp.float32)


def vmem(*shape):
    return pltpu.VMEM(shape, jnp.float32)


def call(kernel, outs, scratch, operands, out_space=pltpu.VMEM):
    def size(shape):
        count = 4
        for extent in shape:
            count *= extent
        return count

    sized = [array for array in (*scratch, *outs, *operands) if hasattr(array, "shape")]
    asked = 8 * 2**20 + sum(size(array.shape) for array in sized)
    return pl.pallas_call(
        kernel,
        out_shape=tuple(outs),
        in_specs=[pl.BlockSpec(memory_space=pltpu.VMEM)] * len(operands),
        out_specs=tuple([pl.BlockSpec(memory_space=out_space)] * len(outs)),
        scratch_shapes=scratch,
        compiler_params=pltpu.CompilerParams(vmem_limit_bytes=asked),
    )(*operands)


def on_device(iterate, source, phase_field, block_owner):
    layers, height, depth = iterate.shape
    half, quarter = height // 2, height // 4
    blocks = lax.axis_size("gx")
    padded, padded2 = height + 2 * PAD, half + 2 * PAD
    inputs = sum(
        jnp.pad(block, ((k * layers, (2 - k) * layers), (0, 0), (0, 0)))
        for k, block in enumerate((iterate, source, phase_field))
    )
    edge, = call(edge_kernel, [f32(3 * height + half, depth)], [], (inputs,))
    layer, tile, five = (height, depth), (half, depth), layers + 1
    message, own2, known1, *fine = call(
        chip_kernel,
        [
            f32(chip_rows(height)[1], depth), f32(2, *tile), f32(*layer), f32(3, *layer), f32(five, *layer),
            f32(five, padded, depth), f32(five, *layer), f32(five, *layer), f32(layers, *layer),
        ],
        [vmem(five, *layer)] + [vmem(five, padded, depth)] * 3 + [vmem(10, *layer)],
        (block_owner, inputs, within_chip(edge)),
    )
    within, outer, fx2, *border = call(
        border_kernel,
        [
            f32(5, *tile), f32(4, *tile), f32(*tile), f32(3, *layer), f32(*layer), f32(2, *layer),
            f32(padded, depth), f32(*layer), f32(*layer), f32(2, *layer),
        ],
        [
            vmem(1, padded, depth), vmem(2, padded, depth), vmem(4, padded, depth), vmem(8, *layer),
            vmem(2, padded, depth), vmem(2, *layer), vmem(2, *layer),
        ],
        (inputs, message, own2, known1, *fine, between_chips(message)),
    )
    within_in = within_chip(within)
    plain = f32(3, *tile)
    slots, *middle = call(
        middle_down_kernel,
        [f32(blocks // 2, 2, quarter, depth), plain, plain, plain, plain, f32(3, padded2, depth)] + [plain] * 3,
        [vmem(5, padded2, depth), vmem(2, *tile)],
        (within, fx2, outer, within_in),
    )
    kinds = [list(range(core, blocks, 2)) for core in range(2)]
    same_cores = lax.all_to_all(slots, "gx", 0, 0, axis_index_groups=kinds, tiled=True)
    other_cores = within_chip(same_cores)
    solved, owned = call(
        coarse_kernel,
        [f32(layers, *layer), f32(1, quarter, depth // 4)],
        [
            vmem(blocks // 4, quarter, depth), vmem(4, blocks // 4, quarter + 2 * PAD, depth), vmem(7, *tile),
            vmem(5, padded2, depth), vmem(layers + 2, padded, depth), vmem(5, *layer), vmem(layers, *layer),
            vmem(1, quarter, depth // 4), pltpu.SMEM((blocks,), jnp.int32),
            pltpu.SemaphoreType.DMA, pltpu.SemaphoreType.DMA((layers + 1,)),
        ],
        (block_owner, same_cores, other_cores, *middle, inputs, *fine, *border, within_in),
        pl.ANY,
    )
    return solved, owned


def solution(mesh):
    split = P(("groups", "gx"), None, None)
    return jax.shard_map(
        on_device,
        mesh=mesh,
        in_specs=(split, split, split, P("groups")),
        out_specs=(split, split),
        check_vma=False,
    )
```

```python
import jax
import jax.numpy as jnp
from jax import lax
from jax.experimental import pallas as pl
from jax.experimental.pallas import tpu as pltpu
from jax.sharding import PartitionSpec as P

STIFFNESS = 100.0
EPSILON = 0.01
COARSE_SWEEPS = 4
PAD = 8


def between_chips(block):
    return lax.ppermute(block, "gx", [(i, i + 1 if i % 2 else i - 1) for i in range(1, lax.axis_size("gx") - 1)])


def within_chip(block):
    return lax.ppermute(block, "gx", [(i, i ^ 1) for i in range(lax.axis_size("gx"))])


def by_side(across, within):
    on_left = lax.axis_index("gx") % 2 == 0
    return jnp.where(on_left, across, within), jnp.where(on_left, within, across)


def lanes_of(shape):
    return lax.broadcasted_iota(jnp.int32, shape, len(shape) - 1)


def rows_of(shape):
    return lax.broadcasted_iota(jnp.int32, shape, len(shape) - 2)


def ahead(values, step, axis):
    return pltpu.roll(values, values.shape[axis] - step, axis)


def behind(values, step, axis):
    return pltpu.roll(values, step, axis)


def with_partner(values, step, axis):
    index = lax.broadcasted_iota(jnp.int32, values.shape, axis)
    partner = jnp.where((index & step) == 0, ahead(values, step, axis), behind(values, step, axis))
    return values + partner


def even_row_sum(scratch, rows):
    return scratch[pl.ds(0, rows, 2), :] + scratch[pl.ds(1, rows, 2), :]


def core_of():
    return lax.axis_index("gx") % 2


def own_layer(u, layers):
    return u + core_of() * (layers - 1 - 2 * u)


def three_parts(ref):
    third = ref.shape[0] // 3
    return [ref.at[pl.ds(k * third, third)] for k in range(3)]


def odd_cells(ref, rows, first):
    return jnp.where(first, ref[pl.ds(0, rows, 2), :], ref[pl.ds(1, rows, 2), :])


def into_both_rows(ref, values):
    rows = values.shape[0]
    ref[pl.ds(0, rows, 2), :] = values
    ref[pl.ds(1, rows, 2), :] = values


def cell_coef(value):
    return STIFFNESS * (value * value + EPSILON)


class Plane:
    def __init__(self, height, depth):
        self.height, self.half, self.depth = height, height // 2, depth
        self.row, self.lane = rows_of((height, depth)), lanes_of((height, depth))
        self.parity = self.row + self.lane + core_of()
        self.half_lane = lanes_of((self.half, depth))
        self.body = pl.ds(PAD, height)
        self.up, self.down = pl.ds(PAD + 1, height), pl.ds(PAD - 1, height)

    def even(self, u):
        return ((self.parity + u) & 1) == 0

    def odd_first(self, u):
        return ((self.half_lane + core_of() + u) & 1) != 0

    def put(self, ref, values):
        edge = jnp.zeros((PAD, self.depth), jnp.float32)
        ref[:PAD] = edge
        ref[PAD + self.height:] = edge
        ref[self.body] = values

    def face_y(self, here):
        return jnp.where(self.row < self.height - 1, 0.5 * (here + ahead(here, 1, 0)), 0.0)

    def face_z(self, here):
        return jnp.where(self.lane < self.depth - 1, 0.5 * (here + ahead(here, 1, 1)), 0.0)

    def packed(self, outer, inner, core):
        return jnp.where((self.half_lane & 1) == core, outer, inner)

    def both_rows(self, ref):
        return even_row_sum(ref, self.half)

    def summed(self, values, ref):
        ref[...] = values
        return with_partner(self.both_rows(ref), 1, 1)

    def odd_rows(self, values, ref):
        ref[...] = values
        return with_partner(ref[pl.ds(1, self.half, 2), :], 1, 1)

    def odd_lanes(self, values, ref):
        ref[...] = values
        sums = self.both_rows(ref)
        return jnp.where((self.half_lane & 1) == 0, ahead(sums, 1, 1), sums)


def in_layer(plane, fy, fz, fzl, padded):
    here = padded[plane.body]
    total = fy[plane.body] * padded[plane.up] + fy[plane.down] * padded[plane.down]
    return total + (fz[...] * ahead(here, 1, 1) + fzl[...] * behind(here, 1, 1))


def edge_kernel(inputs, out):
    iterate, source, phase = three_parts(inputs)
    layers, height, depth = iterate.shape
    plane = Plane(height, depth)
    near, inner, far = [own_layer(u, layers) for u in (layers - 1, layers - 2, layers - 3)]
    coef_near, coef_inner, coef_far = [cell_coef(phase[k]) for k in (near, inner, far)]

    def around(here, e):
        fy, fz = plane.face_y(here), plane.face_z(here)
        fyl, fzl = behind(fy, 1, 0), behind(fz, 1, 1)
        total = fy * ahead(e, 1, 0) + fyl * behind(e, 1, 0)
        return total + fz * ahead(e, 1, 1) + fzl * behind(e, 1, 1), fy + fyl + fz + fzl

    face_near, face_far = 0.5 * (coef_inner + coef_near), 0.5 * (coef_inner + coef_far)
    total, weight = around(coef_inner, iterate[inner])
    total = total + face_near * iterate[near] + face_far * iterate[far]
    updated = (source[inner] + total) / (1.0 + (face_near + face_far + weight))
    total, _ = around(coef_near, iterate[near])
    known = jnp.where(plane.even(layers - 1), total + face_near * iterate[inner], face_near * updated)
    out[:height] = coef_near
    out[height:2 * height] = coef_inner
    out[2 * height:3 * height] = source[near] + known
    out[3 * height:] = odd_cells(iterate.at[near], plane.half, plane.odd_first(layers - 1))


def chip_rows(height):
    half, at, places = height // 2, 0, {}
    for name, size in (
        ("coef0", height), ("coef1", height), ("known0", height), ("old0", half), ("moved1", half), ("face2", half),
        ("source2", half), ("fx2", half), ("far2", half),
    ):
        places[name] = pl.ds(at, size)
        at += size
    return places, at


def own_kernel(owner_of, inputs, cell, old, fx, fy, fz, fzl, inv, even):
    iterate, source, phase = three_parts(inputs)
    layers, height, depth = iterate.shape
    plane = Plane(height, depth)
    body = plane.body
    for u in range(layers):
        cell[u] = cell_coef(phase[own_layer(u, layers)])
        plane.put(old.at[u], iterate[own_layer(u, layers)])
    for u in range(layers):
        here = cell[u]
        if u < layers - 1:
            fx[u] = 0.5 * (here + cell[u + 1])
        plane.put(fy.at[u], plane.face_y(here))
        face = plane.face_z(here)
        fz[u] = face
        fzl[u] = behind(face, 1, 1)
    for u in (1, 2):
        weight = (fx[u] + fx[u - 1]) + (fy[u, body] + fy[u, plane.down]) + (fz[u] + fzl[u])
        inverse = 1.0 / (1.0 + weight)
        inv[u - 1] = inverse
        around = in_layer(plane, fy.at[u], fz.at[u], fzl.at[u], old.at[u])
        total = source[own_layer(u, layers)] + around + (fx[u] * old[u + 1, body] + fx[u - 1] * old[u - 1, body])
        plane.put(even.at[u - 1], total * inverse)


def chip_kernel(
    inputs, cell, old_own, fx_own, fy_own, fz_own, fzl_own, inv_own, even_own, within_in,
    message, own2, known1, new, fx_more, fy_margin, fz_margin, fzl_margin, inv_more,
    old_margin, even_more, change, turn,
):
    iterate, source, phase = three_parts(inputs)
    layers, height, depth = iterate.shape
    plane = Plane(height, depth)
    body, half = plane.body, plane.half
    places, _ = chip_rows(height)
    margin = layers

    def part(k):
        return within_in[k * height:(k + 1) * height]

    def s(u):
        return source[own_layer(u, layers)]

    into_both_rows(turn.at[0], within_in[3 * height:])
    plane.put(old_margin, turn[0])
    fx_more[0] = 0.5 * (cell[layers - 1] + part(0))
    fx_more[1] = 0.5 * (part(0) + part(1))
    plane.put(fy_margin, plane.face_y(part(0)))
    face = plane.face_z(part(0))
    fz_margin[...] = face
    fzl_margin[...] = behind(face, 1, 1)
    fx = [fx_own.at[u] for u in range(3)] + [fx_more.at[0], fx_more.at[1]]
    fy = [fy_own.at[u] for u in range(layers)] + [fy_margin]
    fz = [fz_own.at[u] for u in range(layers)] + [fz_margin]
    fzl = [fzl_own.at[u] for u in range(layers)] + [fzl_margin]
    old = [old_own.at[u] for u in range(layers)] + [old_margin]
    inv = [None, inv_own.at[0], inv_own.at[1], inv_more.at[0], inv_more.at[1]]
    even = [None, even_own.at[0], even_own.at[1], even_more.at[0], even_more.at[1]]
    for u in (margin - 1, margin):
        weight = (fx[u][...] + fx[u - 1][...]) + (fy[u][body] + fy[u][plane.down]) + (fz[u][...] + fzl[u][...])
        inv[u][...] = 1.0 / (1.0 + weight)

    def around(ref, u):
        return in_layer(plane, fy[u], fz[u], fzl[u], ref[u])

    u = margin - 1
    total = s(u) + around(old, u) + (fx[u][...] * old[u + 1][body] + fx[u - 1][...] * old[u - 1][body])
    plane.put(even[u], total * inv[u][...])
    plane.put(even[margin], (part(2) + fx[u][...] * old[u][body]) * inv[margin][...])
    for u in range(2, margin + 1):
        if u < margin:
            total = s(u) + around(even, u) + (fx[u][...] * even[u + 1][body] + fx[u - 1][...] * even[u - 1][body])
        else:
            total = part(2) + around(even, u) + fx[u - 1][...] * even[u - 1][body]
        fresh = total * inv[u][...]
        new[u - 2] = fresh
        plane.put(change.at[u - 2], fresh - old[u][body])
    change = {u: change.at[u - 2] for u in range(2, margin + 1)}

    one = fx[1][...] * change[2][body]
    two = around(change, 2) + fx[2][...] * change[3][body]
    three = around(change, 3) + (fx[2][...] * change[2][body] + fx[3][...] * change[4][body])
    outer = jnp.where(plane.even(1), one, 0.0)
    inner = jnp.where(plane.even(2), two, 0.0) + jnp.where(plane.even(3), three, 0.0)
    core = core_of()

    def tile(name, outer, inner):
        message[places[name], :] = plane.packed(outer, inner, core)

    tile("source2", plane.summed(outer, turn.at[1]), plane.summed(inner, turn.at[2]))
    tile("fx2", plane.summed(fx[1][...], turn.at[3]), plane.summed(fx[3][...], turn.at[4]))
    fy2 = [plane.odd_rows(fy[u][body] + fy[u + 1][body], turn.at[5 + u // 2]) for u in (0, 2)]
    fz2 = [plane.odd_lanes(fz[u][...] + fz[u + 1][...], turn.at[7 + u // 2]) for u in (0, 2)]
    own2[0], own2[1] = plane.packed(*fy2, core), plane.packed(*fz2, core)
    tile("far2", fy2[1], fz2[1])
    for u in range(2):
        message[places["coef%d" % u], :] = cell[u]
    first = s(0) + around(old, 0) + fx[0][...] * old[1][body]
    second = s(0) + fx[0][...] * even[1][body]
    message[places["known0"], :] = jnp.where(plane.even(0), first, second)
    message[places["old0"], :] = odd_cells(iterate.at[own_layer(0, layers)], half, plane.odd_first(0))
    total = s(1) + around(even, 1) + fx[1][...] * even[2][body]
    known1[...] = total
    turn[9] = total * inv[1][...] - old[1][body]
    message[places["moved1"], :] = odd_cells(turn.at[9], half, plane.odd_first(1))
    message[places["face2"], :] = odd_cells(fx[1], half, plane.odd_first(1))


def border_kernel(
    inputs, message, own2, known1, new_in, fx_in, fy_in, fz_in, fzl_in, inv_in, across_in,
    within, outer2, fx2_in, new, known, fx, fy, fz, fzl, inv,
    old, even, change, turn, face_y, face_z, face_zl,
):
    iterate, source, _ = three_parts(inputs)
    layers, height, depth = iterate.shape
    plane = Plane(height, depth)
    body, half = plane.body, plane.half
    places, _ = chip_rows(height)
    core, last = core_of(), lax.axis_size("gx") - 1
    position = lax.axis_index("gx")

    def mine(name):
        return message[places[name], :]

    def theirs(name):
        return across_in[places[name], :]

    def opened(name, k):
        into_both_rows(turn.at[k], theirs(name))
        return turn[k]

    for k in range(2):
        here = theirs("coef%d" % k)
        plane.put(face_y.at[k], plane.face_y(here))
        face = plane.face_z(here)
        face_z[k] = face
        face_zl[k] = behind(face, 1, 1)
    fy[...], fz[...], fzl[...] = face_y[0], face_z[0], face_zl[0]
    there = position - 1 + 2 * core
    border = jnp.where((there >= 0) & (there <= last), 0.5 * (mine("coef0") + theirs("coef0")), 0.0)
    face1 = 0.5 * (theirs("coef0") + theirs("coef1"))
    face2 = opened("face2", 2)
    fx[0], fx[1] = border, face1

    def inverse(faces, fy, fz, fzl):
        weight = faces + (fy[body] + fy[plane.down]) + (fz[...] + fzl[...])
        return 1.0 / (1.0 + weight)

    inv_own = inverse(fx_in[0] + border, fy_in.at[0], fz_in.at[0], fzl_in.at[0])
    inv_near = inverse(border + face1, face_y.at[0], face_z.at[0], face_zl.at[0])
    inv_far = inverse(face1 + face2, face_y.at[1], face_z.at[1], face_zl.at[1])
    inv[0], inv[1] = inv_near, inv_own
    old_own, old_next = iterate[own_layer(0, layers)], iterate[own_layer(1, layers)]
    old_near, far = opened("old0", 0), opened("moved1", 1)
    even_own = (mine("known0") + border * old_near) * inv_own
    even_near = (theirs("known0") + border * old_own) * inv_near
    plane.put(even.at[0], even_near)
    plane.put(even.at[1], even_own)

    def near(ref, k):
        return in_layer(plane, face_y.at[k], face_z.at[k], face_zl.at[k], ref)

    def own(ref, u):
        return in_layer(plane, fy_in.at[u], fz_in.at[u], fzl_in.at[u], ref)

    odd_own = (mine("known0") + own(even.at[1], 0) + border * even_near) * inv_own
    odd_near = (theirs("known0") + near(even.at[0], 0) + border * even_own) * inv_near
    odd_next = (known1[...] + fx_in[0] * even_own) * inv_in[0]
    far = far + face1 * even_near * inv_far
    new[0], new[1], new[2] = odd_near, odd_own, odd_next
    near_by, here, following = odd_near - old_near, odd_own - old_own, odd_next - old_next
    for k, values in enumerate((far, near_by, here, following)):
        plane.put(change.at[k], values)
    plane.put(old.at[0], old_near)
    known[...] = theirs("known0") + face1 * far - near(old.at[0], 0)

    def residual(u, values):
        return jnp.where(plane.even(u), values, 0.0)

    own_outer = residual(1, own(change.at[3], 1) + fx_in[0] * here)
    own_outer = own_outer + residual(0, own(change.at[2], 0) + (fx_in[0] * following + border * near_by))
    own_inner = residual(2, fx_in[1] * following)
    its_outer = residual(-1, near(change.at[1], 0) + (face1 * far + border * here))
    its_outer = its_outer + residual(-2, near(change.at[0], 1) + face1 * near_by)
    its_inner = residual(-3, face2 * far)
    sums = [plane.summed(values, turn.at[3 + k]) for k, values in enumerate((own_outer, own_inner, its_outer, its_inner))]
    within[0] = mine("source2") + plane.packed(sums[0], sums[1], core)
    outer2[0] = theirs("source2") + plane.packed(sums[2], sums[3], 1 - core)
    outer2[1] = theirs("fx2")
    far2 = theirs("far2")
    far2_swap = jnp.where((plane.half_lane & 1) == 0, ahead(far2, 1, 1), behind(far2, 1, 1))
    near_fy2 = plane.odd_rows(face_y[0, body] + face_y[1, body], turn.at[1])
    near_fz2 = plane.odd_lanes(face_z[0] + face_z[1], turn.at[2])
    outer2[2] = plane.packed(near_fy2, far2_swap, 1 - core)
    outer2[3] = plane.packed(near_fz2, far2, 1 - core)
    fx2_in[...] = mine("fx2")
    middle = jnp.where((plane.half_lane & 1) == 0, ahead(mine("fx2"), 1, 1), behind(mine("fx2"), 1, 1))
    within[1] = plane.packed(plane.summed(border, turn.at[7]), middle, core)
    within[2], within[3] = own2[0], own2[1]
    turn[0] = source[own_layer(layers - 1, layers)] + fx_in[layers - 2] * new_in[layers - 4]
    within[4] = odd_cells(turn.at[0], half, jnp.logical_not(plane.odd_first(layers - 1)))


def neigh2(e2, fx2, fxl2, fy2, fz2, fzl2, first_of_two, tiles):
    half = fx2.shape[1]
    body, up, down = pl.ds(PAD, half), pl.ds(PAD + 1, half), pl.ds(PAD - 1, half)
    needed = range(tiles[0], tiles[-1] + 3)
    here = {j: e2[j, body] for j in needed}
    after = {j: ahead(here[j], 1, 1) for j in needed}
    before = {j: behind(here[j], 1, 1) for j in needed}
    found = []
    for j in tiles:
        k = j + 1
        upper = jnp.where(first_of_two, after[k], before[k + 1])
        lower = jnp.where(first_of_two, after[k - 1], before[k])
        sums = fx2[j] * upper + fxl2[j] * lower
        sums = sums + fy2[j, body] * e2[k, up] + fy2[j, down] * e2[k, down]
        sums = sums + fz2[j] * ahead(here[k], 2, 1) + fzl2[j] * behind(here[k], 2, 1)
        found.append(sums)
    return found


def parities2(half, lanes):
    row, lane = rows_of((half, lanes)), lanes_of((half, lanes))
    return (lane & 1) == 0, ((row + (lane & 1) + (lane >> 1)) & 1) == 0


def group(values):
    return with_partner(with_partner(values, 1, 1), 2, 1)


def middle_down_kernel(
    own, fx2_in, outer, within_in,
    slots, e2_out, s2, fx2, fxl2, fy2, fz2, fzl2, inv2,
    e2, pair,
):
    _, half, lanes = own.shape
    quarter = half // 2
    position = lax.axis_index("gx")
    first_of_two, even2 = parities2(half, lanes)
    body, down = pl.ds(PAD, half), pl.ds(PAD - 1, half)
    edge = jnp.zeros((PAD, lanes), jnp.float32)
    for j in range(5):
        e2[j] = jnp.zeros((half + 2 * PAD, lanes), jnp.float32)
    def three(k):
        left, right = by_side(outer[k], within_in[k])
        return left, own[k], right

    for j, (source, fy, fz) in enumerate(zip(three(0), three(2), three(3))):
        s2[j] = source
        fy2[j, :PAD] = edge
        fy2[j, body] = fy
        fy2[j, PAD + half:] = edge
        fz2[j] = fz
        fzl2[j] = behind(fz, 2, 1)
    left_fx, _, right_fx = three(1)
    own_fx = by_side(fx2_in[...], own[1])
    fx2[0] = jnp.where(first_of_two, ahead(left_fx, 1, 1), behind(own_fx[1], 1, 1))
    fx2[1] = own_fx[0]
    fx2[2] = right_fx
    fxl2[0] = left_fx
    fxl2[1] = own_fx[1]
    fxl2[2] = jnp.where(first_of_two, ahead(own_fx[0], 1, 1), behind(right_fx, 1, 1))
    for j in range(3):
        weight = fx2[j] + fxl2[j] + fy2[j, body] + fy2[j, down] + fz2[j] + fzl2[j]
        inverse = 1.0 / (8.0 + weight)
        inv2[j] = inverse
        e2[j + 1, body] = jnp.where(even2, s2[j] * inverse, 0.0)

    def neigh(tiles):
        return neigh2(e2, fx2, fxl2, fy2, fz2, fzl2, first_of_two, tiles)

    fresh = [
        jnp.where(even2, e2[j + 1, body], (s2[j] + sums) * inv2[j]) for j, sums in enumerate(neigh((0, 1, 2)))
    ]
    for j in range(3):
        e2[j + 1, body] = fresh[j]
        e2_out[j] = fresh[j]
    pair[0] = jnp.where(even2, neigh((1,))[0], 0.0)
    lane = lanes_of((quarter, lanes))
    slot = position // (slots.shape[0] // 2)
    odd_layer, odd_depth, item = (lane & 1) != 0, (lane & 2) != 0, (lane - slot) & 3
    source = group(even_row_sum(pair.at[0], quarter))
    fx = group(jnp.where(odd_layer, even_row_sum(fx2.at[1], quarter), 0.0))
    fy = group(fy2[1, pl.ds(PAD + 1, quarter, 2), :])
    fz = group(jnp.where(odd_depth, even_row_sum(fz2.at[1], quarter), 0.0))
    fxl = group(jnp.where(odd_layer, 0.0, even_row_sum(fxl2.at[1], quarter)))
    weight = (fx + fxl) + (fy + behind(fy, 1, 0)) + (fz + behind(fz, 4, 1))
    start = source / (64.0 + weight)
    tile = jnp.where(item == 0, start, jnp.where(item == 1, fx, jnp.where(item == 2, fy, fz)))
    first = (((lane & 1) + (lane >> 1)) & 1) != 0
    pair[0] = jnp.where(first_of_two, fresh[2], fresh[1])
    pair[1] = jnp.where(first_of_two, fresh[1], fresh[0])
    for_left = odd_cells(pair.at[0], quarter, first)
    for_right = odd_cells(pair.at[1], quarter, first)
    for c in range(slots.shape[0]):
        slots[c, 0] = tile
        slots[c, 1] = jnp.where(position < 2 * c + 1 - position % 2, for_right, for_left)


def joined(one, two):
    return jnp.concatenate([part for part in (one, two) if part.shape[0]], 0)


class Level:
    def __init__(self, mass, source, faces, row_step, lane_step, slot_step):
        self.source, self.row_step, self.lane_step, self.slot_step = source, row_step, lane_step, slot_step
        self.fx, self.fy, self.fz = faces
        self.tiles = source.shape[0]
        shape = source.shape
        self.lane = lanes_of(shape)
        layer = lax.broadcasted_iota(jnp.int32, shape, 0) if self.tiles > 1 else self.lane // slot_step
        self.even = ((layer + rows_of(shape) // row_step + self.lane // lane_step) & 1) == 0
        self.fxl = self.lower(self.fx)
        self.fyl = self.row_shifts(self.fy)[1]
        self.fzl = behind(self.fz, lane_step, 2)
        weight = (self.fx + self.fxl) + (self.fy + self.fyl) + (self.fz + self.fzl)
        self.inv = 1.0 / (mass + weight)

    def upper(self, e):
        return joined(e[1:], ahead(e[:1], self.slot_step, 2))

    def lower(self, e):
        return joined(behind(e[-1:], self.slot_step, 2), e[:-1])

    def row_shifts(self, e):
        return ahead(e, self.row_step, 1), behind(e, self.row_step, 1)

    def neigh(self, e):
        above, below = self.row_shifts(e)
        total = (self.fx * self.upper(e) + self.fxl * self.lower(e)) + (self.fy * above + self.fyl * below)
        return total + (self.fz * ahead(e, self.lane_step, 2) + self.fzl * behind(e, self.lane_step, 2))

    def start(self):
        return self.source * self.inv

    def update(self, e):
        return self.start() + self.neigh(e) * self.inv

    def cycle(self, deeper):
        odd = self.update(self.start())
        residual = jnp.where(self.even, self.neigh(odd), 0.0)
        fix = deeper(self.restricted(residual), self.coarse_faces())
        even = self.update(odd + self.prolonged(fix))
        return jnp.where(self.even, even, self.update(even))

    def coarse_slot_step(self):
        return self.slot_step if self.tiles > 1 else 2 * self.slot_step

    def pairs(self, values):
        if self.tiles == 1:
            return with_partner(values, self.slot_step, 2)
        halves = values.reshape(self.tiles // 2, 2, *values.shape[1:])
        return halves[:, 0] + halves[:, 1]

    def odd_layers(self, values):
        if self.tiles == 1:
            return with_partner(jnp.where((self.lane & self.slot_step) != 0, values, 0.0), self.slot_step, 2)
        return values.reshape(self.tiles // 2, 2, *values.shape[1:])[:, 1]

    def row_pairs(self, values):
        return with_partner(values, self.row_step, 1)

    def odd_rows(self, values):
        odd = (rows_of(values.shape) & self.row_step) != 0
        return with_partner(jnp.where(odd, values, 0.0), self.row_step, 1)

    def restricted(self, values):
        return with_partner(self.row_pairs(self.pairs(values)), self.lane_step, 2)

    def coarse_faces(self):
        fx = with_partner(self.row_pairs(self.odd_layers(self.fx)), self.lane_step, 2)
        fy = with_partner(self.odd_rows(self.pairs(self.fy)), self.lane_step, 2)
        return fx, fy, self.restricted(jnp.where((self.lane & self.lane_step) != 0, self.fz, 0.0))

    def prolonged(self, fix):
        if self.tiles == 1:
            return fix
        both = jnp.concatenate([fix[:, None], fix[:, None]], 1)
        return both.reshape(self.tiles, *fix.shape[1:])


class Rows(Level):
    def __init__(self, mass, source, faces, scratch):
        self.scratch, self.used = scratch, 0
        self.rows = source.shape[1]
        super().__init__(mass, source, faces, 1, 4, 1)

    def start(self):
        return self.source

    def place(self):
        self.used += 1
        return self.scratch.at[self.used % self.scratch.shape[0]]

    def row_shifts(self, e):
        place = self.place()
        edge = jnp.zeros((e.shape[0], PAD, e.shape[2]), jnp.float32)
        place[:, :PAD] = edge
        place[:, PAD + self.rows:] = edge
        place[:, pl.ds(PAD, self.rows)] = e
        return place[:, pl.ds(PAD + 1, self.rows)], place[:, pl.ds(PAD - 1, self.rows)]

    def every_other(self, values, starts):
        place, tiles = self.place(), values.shape[0]
        place[:tiles, : self.rows] = values
        found = 0.0
        for start in starts:
            found = found + jnp.concatenate(
                [place[j, pl.ds(start, self.rows // 2, 2), :][None] for j in range(tiles)], 0
            )
        return found

    def row_pairs(self, values):
        return self.every_other(values, (0, 1))

    def odd_rows(self, values):
        return self.every_other(values, (1,))

    def prolonged(self, fix):
        place, tiles = self.place(), fix.shape[0]
        for j in range(tiles):
            into_both_rows(place.at[j, pl.ds(0, self.rows)], fix[j])
        return super().prolonged(place[:tiles, : self.rows])


def coarsest(mass, source, faces, *steps):
    row_step, lane_step, slot_step = steps
    level = Level(mass, source, faces, *steps)
    counts = source.shape[1] // row_step, source.shape[2] // lane_step, 4 // slot_step
    frames = [(m, k, q) for m in range(counts[0]) for k in range(counts[1]) for q in range(counts[2])]
    place = level.lane & 3

    def spread(values):
        copies = {}
        for m, k, q in frames:
            if k:
                copies[m, k, q] = behind(copies[m, 0, q], k * lane_step, 2)
            elif q:
                by = q * slot_step
                one, two = behind(copies[m, 0, 0], by, 2), ahead(copies[m, 0, 0], 4 - by, 2)
                copies[m, k, q] = jnp.where(place >= by, one, two)
            else:
                copies[m, k, q] = behind(values, m * row_step, 1) if m else values
        return copies

    start, inv, fx, fy, fz = [spread(values) for values in (source * level.inv, level.inv, level.fx, level.fy, level.fz)]

    def shifted(copies, frame, axis, by):
        moved = list(frame)
        moved[axis] = (frame[axis] - by) % counts[axis]
        return copies[tuple(moved)]

    def along_x(copies, frame, by):
        here, wrapped = copies[frame], shifted(copies, frame, 2, by)
        return joined(here[1:], wrapped[:1]) if by > 0 else joined(wrapped[-1:], here[:-1])

    weights = {}
    for frame in frames:
        pairs = [
            (fx[frame], along_x(fx, frame, -1)),
            (fy[frame], shifted(fy, frame, 0, -1)),
            (fz[frame], shifted(fz, frame, 1, -1)),
        ]
        weights[frame] = [(up * inv[frame], low * inv[frame]) for up, low in pairs]

    def update(e):
        fresh = {}
        for frame in frames:
            (x_up, x_low), (y_up, y_low), (z_up, z_low) = weights[frame]
            total = x_up * along_x(e, frame, 1) + x_low * along_x(e, frame, -1)
            total = total + (y_up * shifted(e, frame, 0, 1) + y_low * shifted(e, frame, 0, -1))
            total = total + (z_up * shifted(e, frame, 1, 1) + z_low * shifted(e, frame, 1, -1))
            fresh[frame] = start[frame] + total
        return fresh

    even = start
    odd = update(even)
    for turn in range(COARSE_SWEEPS - 1):
        even = update(odd)
        odd = update(even)
    return jnp.where(level.even, even[0, 0, 0], odd[0, 0, 0])


def small_cycle(mass, source, faces, row_step, lane_step, slot_step, between):
    if between == 0:
        return coarsest(mass, source, faces, row_step, lane_step, slot_step)
    level = Level(mass, source, faces, row_step, lane_step, slot_step)
    return level.cycle(
        lambda inner, inner_faces: small_cycle(
            8.0 * mass, inner, inner_faces, 2 * row_step, 2 * lane_step, level.coarse_slot_step(), between - 1
        )
    )


def coarse_kernel(
    owner_of, same_cores, other_cores, e2_in, s2, fx2, fxl2, fy2, fz2, fzl2, inv2,
    inputs, new_in, fx_more, fy_margin, fz_margin, fzl_margin, inv_more, fx_in, fy_in, fz_in, fzl_in, inv_in,
    new_out, known_out, fx_out, fy_out, fz_out, fzl_out, inv_out, within_in,
    solved_out, owned_out,
    e3, rows3, pair, e2, e1, cor, solved, owned, owner_here, fetch_sem, sems,
):
    fetch = pltpu.make_async_copy(owner_of, owner_here, fetch_sem)
    fetch.start()
    chips, _, quarter, lanes = same_cores.shape
    blocks = 2 * chips
    half, height = 2 * quarter, 4 * quarter
    position, last = lax.axis_index("gx"), blocks - 1

    slot = lanes_of((quarter, lanes)) & 3
    spread = blocks // 4
    tiles = []
    for chip in range(chips):
        tiles.extend(by_side(same_cores[chip, 0], other_cores[chip, 0]))
    items = []
    for k in range(4):
        packs = []
        for j in range(spread):
            value = tiles[j + (3 - k) % 4 * spread]
            for at in range(3):
                value = jnp.where(slot == at, tiles[j + (at - k) % 4 * spread], value)
            if k:
                value = jnp.where(slot < 4 - k, ahead(value, k, 1), behind(value, 4 - k, 1))
            packs.append(value[None])
        items.append(jnp.concatenate(packs, 0))
    third = Rows(64.0, items[0], items[1:], rows3)
    e3[...] = third.cycle(
        lambda inner, faces: small_cycle(512.0, inner, faces, 1, 8, third.coarse_slot_step(), 2)
    )

    fetch.wait()
    owner = owner_here[position]
    wide, narrow = lanes_of((lanes, lanes)), rows_of((lanes, lanes))
    take = jnp.where(narrow == 4 * wide + owner // spread, 1.0, 0.0)
    block = jnp.dot(
        e3[owner % spread], take, precision=lax.Precision.HIGHEST, preferred_element_type=jnp.float32
    )
    owned[0] = block[:, : lanes // 4]
    copies = [pltpu.make_async_copy(owned, owned_out, sems.at[0])]
    copies[0].start()

    first_of_two, even2 = parities2(half, lanes)
    body2 = pl.ds(PAD, half)
    edge = jnp.zeros((PAD, lanes), jnp.float32)
    left = other_cores[jnp.maximum(position - 1, 0) // 2, 1]
    right = other_cores[jnp.minimum(position + 1, last) // 2, 1]
    into_both_rows(pair.at[5], left)
    into_both_rows(pair.at[6], right)
    left, right = pair[5], pair[6]
    before = (
        left, jnp.where(first_of_two, left, e2_in[0]), e2_in[1], jnp.where(first_of_two, e2_in[2], right), right
    )
    for k in range(5):
        j = jnp.clip(position + k - 2, 0, last)
        here = e3[j % spread]
        turned = [pltpu.roll(here, (at - j // spread) % lanes, 1) for at in range(4)]
        value = turned[3]
        for at in range(3):
            value = jnp.where(slot == at, turned[at], value)
        into_both_rows(pair.at[k], value)
        e2[k, :PAD] = edge
        e2[k, PAD + half:] = edge
        e2[k, body2] = before[k] + pair[k]

    def update2():
        sums = neigh2(e2, fx2, fxl2, fy2, fz2, fzl2, first_of_two, (0, 1, 2))
        return [(s2[j] + sums[j]) * inv2[j] for j in range(3)]

    fresh = update2()
    for j in range(3):
        e2[j + 1, body2] = fresh[j]
    fixes2 = [jnp.where(even2, even, odd) for even, odd in zip(fresh, update2())]

    _, source, _ = three_parts(inputs)
    layers = source.shape[0]
    plane = Plane(height, lanes)
    body1 = plane.body
    core = core_of()
    near_lane = (lanes_of((half, lanes)) & 1) == core
    swaps = [jnp.where(first_of_two, ahead(v, 1, 1), behind(v, 1, 1)) for v in fixes2]
    outer, inner = by_side(fixes2[0], fixes2[2])
    outer_swap, inner_swap = by_side(swaps[0], swaps[2])
    coarse = (
        jnp.where(near_lane, outer_swap, outer), jnp.where(near_lane, fixes2[1], swaps[1]),
        jnp.where(near_lane, swaps[1], fixes2[1]), jnp.where(near_lane, inner, inner_swap),
    )
    fixes = []
    for k in range(4):
        into_both_rows(cor.at[k], coarse[k])
        fixes.append(cor[k])
    for u in range(-1, layers + 1):
        before = new_out[u + 1] if u < 2 else new_in[u - 2]
        plane.put(e1.at[u + 1], before + fixes[(u + 2) // 2])

    def fx1(u):
        if u < 0:
            return fx_out[-1 - u]
        return fx_in[u] if u < layers - 1 else fx_more[u - layers + 1]

    def inv1(u):
        if u <= 0:
            return inv_out[u + 1]
        return inv_in[u - 1] if u < layers - 1 else inv_more[u - layers + 1]

    def around1(u):
        if u < 0:
            return in_layer(plane, fy_out, fz_out, fzl_out, e1.at[0])
        if u == layers:
            return in_layer(plane, fy_margin, fz_margin, fzl_margin, e1.at[u + 1])
        return in_layer(plane, fy_in.at[u], fz_in.at[u], fzl_in.at[u], e1.at[u + 1])

    def updated1(u):
        sums = around1(u) + (fx1(u) * e1[u + 2, body1] + fx1(u - 1) * e1[u, body1])
        return (source[own_layer(u, layers)] + sums) * inv1(u)

    for u in range(layers):
        e1[u + 1, body1] = jnp.where(plane.even(u), updated1(u), e1[u + 1, body1])
    e1[0, body1] = (known_out[...] + fx1(-2) * fixes[0] + (around1(-1) + fx1(-1) * e1[1, body1])) * inv1(-1)
    into_both_rows(cor.at[4], within_in[4])
    sums = cor[4] + fx1(layers) * fixes[3] + (around1(layers) + fx1(layers - 1) * e1[layers, body1])
    e1[layers + 1, body1] = sums * inv1(layers)
    for u in range(layers):
        solved[u] = jnp.where(plane.even(u), e1[u + 1, body1], updated1(u))
        copies.append(
            pltpu.make_async_copy(solved.at[u], solved_out.at[own_layer(u, layers)], sems.at[u + 1])
        )
        copies[-1].start()
    for copy in copies:
        copy.wait()


def f32(*shape):
    return jax.ShapeDtypeStruct(shape, jnp.float32)


def vmem(*shape):
    return pltpu.VMEM(shape, jnp.float32)


def call(kernel, outs, scratch, operands, out_space=pltpu.VMEM):
    def size(shape):
        count = 4
        for extent in shape:
            count *= extent
        return count

    sized = [array for array in (*scratch, *outs, *operands) if hasattr(array, "shape")]
    asked = 8 * 2**20 + sum(size(array.shape) for array in sized)
    return pl.pallas_call(
        kernel,
        out_shape=tuple(outs),
        in_specs=[pl.BlockSpec(memory_space=pltpu.VMEM)] * len(operands),
        out_specs=tuple([pl.BlockSpec(memory_space=out_space)] * len(outs)),
        scratch_shapes=scratch,
        compiler_params=pltpu.CompilerParams(vmem_limit_bytes=asked),
    )(*operands)


def on_device(iterate, source, phase_field, block_owner):
    layers, height, depth = iterate.shape
    half, quarter = height // 2, height // 4
    blocks = lax.axis_size("gx")
    padded, padded2 = height + 2 * PAD, half + 2 * PAD
    inputs = sum(
        jnp.pad(block, ((k * layers, (2 - k) * layers), (0, 0), (0, 0)))
        for k, block in enumerate((iterate, source, phase_field))
    )
    edge, = call(edge_kernel, [f32(3 * height + half, depth)], [], (inputs,))
    edge_in = within_chip(edge)
    layer, tile, tall = (height, depth), (half, depth), (padded, depth)
    cell, old, *fine, even = call(
        own_kernel,
        [
            f32(layers, *layer), f32(layers, *tall), f32(layers - 1, *layer), f32(layers, *tall),
            f32(layers, *layer), f32(layers, *layer), f32(2, *layer), f32(2, *tall),
        ],
        [], (block_owner, inputs),
    )
    message, own2, known1, new, *margin = call(
        chip_kernel,
        [
            f32(chip_rows(height)[1], depth), f32(2, *tile), f32(*layer), f32(3, *layer),
            f32(2, *layer), f32(*tall), f32(*layer), f32(*layer), f32(2, *layer),
        ],
        [vmem(*tall), vmem(2, *tall), vmem(3, *tall), vmem(10, *layer)],
        (inputs, cell, old, *fine, even, edge_in),
    )
    within, outer, fx2, *border = call(
        border_kernel,
        [
            f32(5, *tile), f32(4, *tile), f32(*tile), f32(3, *layer), f32(*layer), f32(2, *layer),
            f32(padded, depth), f32(*layer), f32(*layer), f32(2, *layer),
        ],
        [
            vmem(1, padded, depth), vmem(2, padded, depth), vmem(4, padded, depth), vmem(8, *layer),
            vmem(2, padded, depth), vmem(2, *layer), vmem(2, *layer),
        ],
        (inputs, message, own2, known1, new, *fine, between_chips(message)),
    )
    within_in = within_chip(within)
    plain = f32(3, *tile)
    slots, *middle = call(
        middle_down_kernel,
        [f32(blocks // 2, 2, quarter, depth), plain, plain, plain, plain, f32(3, padded2, depth)] + [plain] * 3,
        [vmem(5, padded2, depth), vmem(2, *tile)],
        (within, fx2, outer, within_in),
    )
    kinds = [list(range(core, blocks, 2)) for core in range(2)]
    same_cores = lax.all_to_all(slots, "gx", 0, 0, axis_index_groups=kinds, tiled=True)
    other_cores = within_chip(same_cores)
    solved, owned = call(
        coarse_kernel,
        [f32(layers, *layer), f32(1, quarter, depth // 4)],
        [
            vmem(blocks // 4, quarter, depth), vmem(4, blocks // 4, quarter + 2 * PAD, depth), vmem(7, *tile),
            vmem(5, padded2, depth), vmem(layers + 2, padded, depth), vmem(5, *layer), vmem(layers, *layer),
            vmem(1, quarter, depth // 4), pltpu.SMEM((blocks,), jnp.int32),
            pltpu.SemaphoreType.DMA, pltpu.SemaphoreType.DMA((layers + 1,)),
        ],
        (block_owner, same_cores, other_cores, *middle, inputs, new, *margin, *fine, *border, within_in),
        pl.ANY,
    )
    return solved, owned


def solution(mesh):
    split = P(("groups", "gx"), None, None)
    return jax.shard_map(
        on_device,
        mesh=mesh,
        in_specs=(split, split, split, P("groups")),
        out_specs=(split, split),
        check_vma=False,
    )
```

```python
import jax
import jax.numpy as jnp
from jax import lax
from jax.experimental import pallas as pl
from jax.experimental.pallas import tpu as pltpu
from jax.sharding import PartitionSpec as P

STIFFNESS = 100.0
EPSILON = 0.01
COARSE_SWEEPS = 4
PAD = 8


def between_chips(block):
    return lax.ppermute(block, "gx", [(i, i + 1 if i % 2 else i - 1) for i in range(1, lax.axis_size("gx") - 1)])


def within_chip(block):
    return lax.ppermute(block, "gx", [(i, i ^ 1) for i in range(lax.axis_size("gx"))])


def by_side(across, within):
    on_left = lax.axis_index("gx") % 2 == 0
    return jnp.where(on_left, across, within), jnp.where(on_left, within, across)


def lanes_of(shape):
    return lax.broadcasted_iota(jnp.int32, shape, len(shape) - 1)


def rows_of(shape):
    return lax.broadcasted_iota(jnp.int32, shape, len(shape) - 2)


def ahead(values, step, axis):
    return pltpu.roll(values, values.shape[axis] - step, axis)


def behind(values, step, axis):
    return pltpu.roll(values, step, axis)


def with_partner(values, step, axis):
    index = lax.broadcasted_iota(jnp.int32, values.shape, axis)
    partner = jnp.where((index & step) == 0, ahead(values, step, axis), behind(values, step, axis))
    return values + partner


def even_row_sum(scratch, rows):
    return scratch[pl.ds(0, rows, 2), :] + scratch[pl.ds(1, rows, 2), :]


def core_of():
    return lax.axis_index("gx") % 2


def own_layer(u, layers):
    return u + core_of() * (layers - 1 - 2 * u)


def three_parts(ref):
    third = ref.shape[0] // 3
    return [ref.at[pl.ds(k * third, third)] for k in range(3)]


def odd_cells(ref, rows, first):
    return jnp.where(first, ref[pl.ds(0, rows, 2), :], ref[pl.ds(1, rows, 2), :])


def into_both_rows(ref, values):
    rows = values.shape[0]
    ref[pl.ds(0, rows, 2), :] = values
    ref[pl.ds(1, rows, 2), :] = values


def cell_coef(value):
    return STIFFNESS * (value * value + EPSILON)


class Plane:
    def __init__(self, height, depth):
        self.height, self.half, self.depth = height, height // 2, depth
        self.row, self.lane = rows_of((height, depth)), lanes_of((height, depth))
        self.parity = self.row + self.lane + core_of()
        self.half_lane = lanes_of((self.half, depth))
        self.body = pl.ds(PAD, height)
        self.up, self.down = pl.ds(PAD + 1, height), pl.ds(PAD - 1, height)

    def even(self, u):
        return ((self.parity + u) & 1) == 0

    def odd_first(self, u):
        return ((self.half_lane + core_of() + u) & 1) != 0

    def put(self, ref, values):
        edge = jnp.zeros((PAD, self.depth), jnp.float32)
        ref[:PAD] = edge
        ref[PAD + self.height:] = edge
        ref[self.body] = values

    def face_y(self, here):
        return jnp.where(self.row < self.height - 1, 0.5 * (here + ahead(here, 1, 0)), 0.0)

    def face_z(self, here):
        return jnp.where(self.lane < self.depth - 1, 0.5 * (here + ahead(here, 1, 1)), 0.0)

    def packed(self, outer, inner, core):
        return jnp.where((self.half_lane & 1) == core, outer, inner)

    def both_rows(self, ref):
        return even_row_sum(ref, self.half)

    def summed(self, values, ref):
        ref[...] = values
        return with_partner(self.both_rows(ref), 1, 1)

    def odd_rows(self, values, ref):
        ref[...] = values
        return with_partner(ref[pl.ds(1, self.half, 2), :], 1, 1)

    def odd_lanes(self, values, ref):
        ref[...] = values
        sums = self.both_rows(ref)
        return jnp.where((self.half_lane & 1) == 0, ahead(sums, 1, 1), sums)


def in_layer(plane, fy, fz, fzl, padded):
    here = padded[plane.body]
    total = fy[plane.body] * padded[plane.up] + fy[plane.down] * padded[plane.down]
    return total + (fz[...] * ahead(here, 1, 1) + fzl[...] * behind(here, 1, 1))


def edge_kernel(inputs, out):
    iterate, source, phase = three_parts(inputs)
    layers, height, depth = iterate.shape
    plane = Plane(height, depth)
    near, inner, far = [own_layer(u, layers) for u in (layers - 1, layers - 2, layers - 3)]
    coef_near, coef_inner, coef_far = [cell_coef(phase[k]) for k in (near, inner, far)]

    def around(here, e):
        fy, fz = plane.face_y(here), plane.face_z(here)
        fyl, fzl = behind(fy, 1, 0), behind(fz, 1, 1)
        total = fy * ahead(e, 1, 0) + fyl * behind(e, 1, 0)
        return total + fz * ahead(e, 1, 1) + fzl * behind(e, 1, 1), fy + fyl + fz + fzl

    face_near, face_far = 0.5 * (coef_inner + coef_near), 0.5 * (coef_inner + coef_far)
    total, weight = around(coef_inner, iterate[inner])
    total = total + face_near * iterate[near] + face_far * iterate[far]
    updated = (source[inner] + total) / (1.0 + (face_near + face_far + weight))
    total, _ = around(coef_near, iterate[near])
    known = jnp.where(plane.even(layers - 1), total + face_near * iterate[inner], face_near * updated)
    out[:height] = coef_near
    out[height:2 * height] = coef_inner
    out[2 * height:3 * height] = source[near] + known
    out[3 * height:] = odd_cells(iterate.at[near], plane.half, plane.odd_first(layers - 1))


def chip_rows(height):
    half, at, places = height // 2, 0, {}
    for name, size in (
        ("coef0", height), ("coef1", height), ("known0", height), ("old0", half), ("moved1", half), ("face2", half),
        ("source2", half), ("fx2", half), ("far2", half),
    ):
        places[name] = pl.ds(at, size)
        at += size
    return places, at


def own_kernel(owner_of, inputs, cell, old, fx, fy, fz, fzl, inv, even):
    iterate, source, phase = three_parts(inputs)
    layers, height, depth = iterate.shape
    plane = Plane(height, depth)
    body = plane.body
    for u in range(layers):
        cell[u] = cell_coef(phase[own_layer(u, layers)])
        plane.put(old.at[u], iterate[own_layer(u, layers)])
    for u in range(layers):
        here = cell[u]
        if u < layers - 1:
            fx[u] = 0.5 * (here + cell[u + 1])
        plane.put(fy.at[u], plane.face_y(here))
        face = plane.face_z(here)
        fz[u] = face
        fzl[u] = behind(face, 1, 1)
    for u in (1, 2):
        weight = (fx[u] + fx[u - 1]) + (fy[u, body] + fy[u, plane.down]) + (fz[u] + fzl[u])
        inverse = 1.0 / (1.0 + weight)
        inv[u - 1] = inverse
        around = in_layer(plane, fy.at[u], fz.at[u], fzl.at[u], old.at[u])
        total = source[own_layer(u, layers)] + around + (fx[u] * old[u + 1, body] + fx[u - 1] * old[u - 1, body])
        plane.put(even.at[u - 1], total * inverse)


def chip_kernel(
    inputs, cell, old_own, fx_own, fy_own, fz_own, fzl_own, inv_own, even_own, within_in,
    message, own2, known1, new, fx_more, fy_margin, fz_margin, fzl_margin, inv_more,
    old_margin, even_more, change, turn,
):
    iterate, source, phase = three_parts(inputs)
    layers, height, depth = iterate.shape
    plane = Plane(height, depth)
    body, half = plane.body, plane.half
    places, _ = chip_rows(height)
    margin = layers

    def part(k):
        return within_in[k * height:(k + 1) * height]

    def s(u):
        return source[own_layer(u, layers)]

    into_both_rows(turn.at[0], within_in[3 * height:])
    plane.put(old_margin, turn[0])
    fx_more[0] = 0.5 * (cell[layers - 1] + part(0))
    fx_more[1] = 0.5 * (part(0) + part(1))
    plane.put(fy_margin, plane.face_y(part(0)))
    face = plane.face_z(part(0))
    fz_margin[...] = face
    fzl_margin[...] = behind(face, 1, 1)
    fx = [fx_own.at[u] for u in range(3)] + [fx_more.at[0], fx_more.at[1]]
    fy = [fy_own.at[u] for u in range(layers)] + [fy_margin]
    fz = [fz_own.at[u] for u in range(layers)] + [fz_margin]
    fzl = [fzl_own.at[u] for u in range(layers)] + [fzl_margin]
    old = [old_own.at[u] for u in range(layers)] + [old_margin]
    inv = [None, inv_own.at[0], inv_own.at[1], inv_more.at[0], inv_more.at[1]]
    even = [None, even_own.at[0], even_own.at[1], even_more.at[0], even_more.at[1]]
    for u in (margin - 1, margin):
        weight = (fx[u][...] + fx[u - 1][...]) + (fy[u][body] + fy[u][plane.down]) + (fz[u][...] + fzl[u][...])
        inv[u][...] = 1.0 / (1.0 + weight)

    def around(ref, u):
        return in_layer(plane, fy[u], fz[u], fzl[u], ref[u])

    u = margin - 1
    total = s(u) + around(old, u) + (fx[u][...] * old[u + 1][body] + fx[u - 1][...] * old[u - 1][body])
    plane.put(even[u], total * inv[u][...])
    plane.put(even[margin], (part(2) + fx[u][...] * old[u][body]) * inv[margin][...])
    for u in range(2, margin + 1):
        if u < margin:
            total = s(u) + around(even, u) + (fx[u][...] * even[u + 1][body] + fx[u - 1][...] * even[u - 1][body])
        else:
            total = part(2) + around(even, u) + fx[u - 1][...] * even[u - 1][body]
        fresh = total * inv[u][...]
        new[u - 2] = fresh
        plane.put(change.at[u - 2], fresh - old[u][body])
    change = {u: change.at[u - 2] for u in range(2, margin + 1)}

    one = fx[1][...] * change[2][body]
    two = around(change, 2) + fx[2][...] * change[3][body]
    three = around(change, 3) + (fx[2][...] * change[2][body] + fx[3][...] * change[4][body])
    outer = jnp.where(plane.even(1), one, 0.0)
    inner = jnp.where(plane.even(2), two, 0.0) + jnp.where(plane.even(3), three, 0.0)
    core = core_of()

    def tile(name, outer, inner):
        message[places[name], :] = plane.packed(outer, inner, core)

    tile("source2", plane.summed(outer, turn.at[1]), plane.summed(inner, turn.at[2]))
    tile("fx2", plane.summed(fx[1][...], turn.at[3]), plane.summed(fx[3][...], turn.at[4]))
    fy2 = [plane.odd_rows(fy[u][body] + fy[u + 1][body], turn.at[5 + u // 2]) for u in (0, 2)]
    fz2 = [plane.odd_lanes(fz[u][...] + fz[u + 1][...], turn.at[7 + u // 2]) for u in (0, 2)]
    own2[0], own2[1] = plane.packed(*fy2, core), plane.packed(*fz2, core)
    tile("far2", fy2[1], fz2[1])
    for u in range(2):
        message[places["coef%d" % u], :] = cell[u]
    first = s(0) + around(old, 0) + fx[0][...] * old[1][body]
    second = s(0) + fx[0][...] * even[1][body]
    message[places["known0"], :] = jnp.where(plane.even(0), first, second)
    message[places["old0"], :] = odd_cells(iterate.at[own_layer(0, layers)], half, plane.odd_first(0))
    total = s(1) + around(even, 1) + fx[1][...] * even[2][body]
    known1[...] = total
    turn[9] = total * inv[1][...] - old[1][body]
    message[places["moved1"], :] = odd_cells(turn.at[9], half, plane.odd_first(1))
    message[places["face2"], :] = odd_cells(fx[1], half, plane.odd_first(1))


def border_kernel(
    inputs, message, own2, known1, new_in, fx_in, fy_in, fz_in, fzl_in, inv_in, across_in,
    within, fx2_in, new, known, fx, fy, fz, fzl, inv,
    old, even, change, turn, face_y, face_z, face_zl,
):
    iterate, source, _ = three_parts(inputs)
    layers, height, depth = iterate.shape
    plane = Plane(height, depth)
    body, half = plane.body, plane.half
    places, _ = chip_rows(height)
    core, last = core_of(), lax.axis_size("gx") - 1
    position = lax.axis_index("gx")

    def mine(name):
        return message[places[name], :]

    def theirs(name):
        return across_in[places[name], :]

    def opened(name, k):
        into_both_rows(turn.at[k], theirs(name))
        return turn[k]

    for k in range(2):
        here = theirs("coef%d" % k)
        plane.put(face_y.at[k], plane.face_y(here))
        face = plane.face_z(here)
        face_z[k] = face
        face_zl[k] = behind(face, 1, 1)
    fy[...], fz[...], fzl[...] = face_y[0], face_z[0], face_zl[0]
    there = position - 1 + 2 * core
    border = jnp.where((there >= 0) & (there <= last), 0.5 * (mine("coef0") + theirs("coef0")), 0.0)
    face1 = 0.5 * (theirs("coef0") + theirs("coef1"))
    face2 = opened("face2", 2)
    fx[0], fx[1] = border, face1

    def inverse(faces, fy, fz, fzl):
        weight = faces + (fy[body] + fy[plane.down]) + (fz[...] + fzl[...])
        return 1.0 / (1.0 + weight)

    inv_own = inverse(fx_in[0] + border, fy_in.at[0], fz_in.at[0], fzl_in.at[0])
    inv_near = inverse(border + face1, face_y.at[0], face_z.at[0], face_zl.at[0])
    inv_far = inverse(face1 + face2, face_y.at[1], face_z.at[1], face_zl.at[1])
    inv[0], inv[1] = inv_near, inv_own
    old_own, old_next = iterate[own_layer(0, layers)], iterate[own_layer(1, layers)]
    old_near, far = opened("old0", 0), opened("moved1", 1)
    even_own = (mine("known0") + border * old_near) * inv_own
    even_near = (theirs("known0") + border * old_own) * inv_near
    plane.put(even.at[0], even_near)
    plane.put(even.at[1], even_own)

    def near(ref, k):
        return in_layer(plane, face_y.at[k], face_z.at[k], face_zl.at[k], ref)

    def own(ref, u):
        return in_layer(plane, fy_in.at[u], fz_in.at[u], fzl_in.at[u], ref)

    odd_own = (mine("known0") + own(even.at[1], 0) + border * even_near) * inv_own
    odd_near = (theirs("known0") + near(even.at[0], 0) + border * even_own) * inv_near
    odd_next = (known1[...] + fx_in[0] * even_own) * inv_in[0]
    far = far + face1 * even_near * inv_far
    new[0], new[1], new[2] = odd_near, odd_own, odd_next
    near_by, here, following = odd_near - old_near, odd_own - old_own, odd_next - old_next
    for k, values in enumerate((far, near_by, here, following)):
        plane.put(change.at[k], values)
    plane.put(old.at[0], old_near)
    known[...] = theirs("known0") + face1 * far - near(old.at[0], 0)

    def residual(u, values):
        return jnp.where(plane.even(u), values, 0.0)

    own_outer = residual(1, own(change.at[3], 1) + fx_in[0] * here)
    own_outer = own_outer + residual(0, own(change.at[2], 0) + (fx_in[0] * following + border * near_by))
    own_inner = residual(2, fx_in[1] * following)
    its_outer = residual(-1, near(change.at[1], 0) + (face1 * far + border * here))
    its_outer = its_outer + residual(-2, near(change.at[0], 1) + face1 * near_by)
    its_inner = residual(-3, face2 * far)
    sums = [plane.summed(values, turn.at[3 + k]) for k, values in enumerate((own_outer, own_inner, its_outer, its_inner))]
    within[0] = mine("source2") + plane.packed(sums[0], sums[1], core)
    within[5] = theirs("source2") + plane.packed(sums[2], sums[3], 1 - core)
    within[6] = theirs("fx2")
    far2 = theirs("far2")
    far2_swap = jnp.where((plane.half_lane & 1) == 0, ahead(far2, 1, 1), behind(far2, 1, 1))
    near_fy2 = plane.odd_rows(face_y[0, body] + face_y[1, body], turn.at[1])
    near_fz2 = plane.odd_lanes(face_z[0] + face_z[1], turn.at[2])
    within[7] = plane.packed(near_fy2, far2_swap, 1 - core)
    within[8] = plane.packed(near_fz2, far2, 1 - core)
    fx2_in[...] = mine("fx2")
    middle = jnp.where((plane.half_lane & 1) == 0, ahead(mine("fx2"), 1, 1), behind(mine("fx2"), 1, 1))
    within[1] = plane.packed(plane.summed(border, turn.at[7]), middle, core)
    within[2], within[3] = own2[0], own2[1]
    turn[0] = source[own_layer(layers - 1, layers)] + fx_in[layers - 2] * new_in[layers - 4]
    within[4] = odd_cells(turn.at[0], half, jnp.logical_not(plane.odd_first(layers - 1)))


def neigh2(e2, fx2, fxl2, fy2, fz2, fzl2, first_of_two, tiles):
    half = fx2.shape[1]
    body, up, down = pl.ds(PAD, half), pl.ds(PAD + 1, half), pl.ds(PAD - 1, half)
    needed = range(tiles[0], tiles[-1] + 3)
    here = {j: e2[j, body] for j in needed}
    after = {j: ahead(here[j], 1, 1) for j in needed}
    before = {j: behind(here[j], 1, 1) for j in needed}
    found = []
    for j in tiles:
        k = j + 1
        upper = jnp.where(first_of_two, after[k], before[k + 1])
        lower = jnp.where(first_of_two, after[k - 1], before[k])
        sums = fx2[j] * upper + fxl2[j] * lower
        sums = sums + fy2[j, body] * e2[k, up] + fy2[j, down] * e2[k, down]
        sums = sums + fz2[j] * ahead(here[k], 2, 1) + fzl2[j] * behind(here[k], 2, 1)
        found.append(sums)
    return found


def parities2(half, lanes):
    row, lane = rows_of((half, lanes)), lanes_of((half, lanes))
    return (lane & 1) == 0, ((row + (lane & 1) + (lane >> 1)) & 1) == 0


def group(values):
    return with_partner(with_partner(values, 1, 1), 2, 1)


def packed_odd(values, pair):
    half, lanes = values.shape
    lane = lanes_of((half // 2, lanes))
    pair[...] = values
    return odd_cells(pair, half // 2, (((lane & 1) + (lane >> 1)) & 1) != 0)


def middle_down_kernel(
    own, fx2_in, within_in,
    slots, e2_out, s2, fx2, fxl2, fy2, fz2, fzl2, inv2,
    e2, pair,
):
    _, half, lanes = own.shape
    quarter = half // 2
    first_of_two, even2 = parities2(half, lanes)
    body, down = pl.ds(PAD, half), pl.ds(PAD - 1, half)
    edge = jnp.zeros((PAD, lanes), jnp.float32)
    for j in (0, 5):
        e2[j] = jnp.zeros((half + 2 * PAD, lanes), jnp.float32)

    def pair_of(k):
        return by_side(own[k], within_in[k])

    def four(k):
        (left, right), (far_left, far_right) = pair_of(k), pair_of(5 + k)
        return far_left, left, right, far_right

    for j, (source, fy, fz) in enumerate(zip(four(0), four(2), four(3))):
        s2[j] = source
        fy2[j, :PAD] = edge
        fy2[j, body] = fy
        fy2[j, PAD + half:] = edge
        fz2[j] = fz
        fzl2[j] = behind(fz, 2, 1)

    def between(left, right):
        return jnp.where(first_of_two, ahead(left, 1, 1), behind(right, 1, 1))

    fxl0, fxl1, fxr2, fxr3 = four(1)
    inner = fx2_in[...]
    fxr1, _ = by_side(inner, between(fxl1, inner))
    fxl2_, _ = by_side(between(inner, fxr2), inner)
    for j, (face, low) in enumerate(
        ((between(fxl0, fxl1), fxl0), (fxr1, fxl1), (fxr2, fxl2_), (fxr3, between(fxr2, fxr3)))
    ):
        fx2[j], fxl2[j] = face, low
        weight = face + low + fy2[j, body] + fy2[j, down] + fz2[j] + fzl2[j]
        inverse = 1.0 / (8.0 + weight)
        inv2[j] = inverse
        e2[j + 1, :PAD] = edge
        e2[j + 1, PAD + half:] = edge
        e2[j + 1, body] = s2[j] * inverse

    def neigh(tiles):
        return neigh2(e2, fx2, fxl2, fy2, fz2, fzl2, first_of_two, tiles)

    fresh = [(s2[j] + sums) * inv2[j] for j, sums in enumerate(neigh((0, 1, 2, 3)))]
    for j in range(4):
        e2[j + 1, body] = fresh[j]
        e2_out[j] = fresh[j]
    lane = lanes_of((quarter, lanes))
    odd_layer, odd_depth = (lane & 1) != 0, (lane & 2) != 0
    chips = slots.shape[0]
    for k, sums in enumerate(neigh((1, 2))):
        j = k + 1
        pair[k] = jnp.where(even2, sums, 0.0)
        item = (lane - (lax.axis_index("gx") // 2 * 2 + k) // (chips // 2)) & 3
        source = group(even_row_sum(pair.at[k], quarter))
        fx = group(jnp.where(odd_layer, even_row_sum(fx2.at[j], quarter), 0.0))
        fxl = group(jnp.where(odd_layer, 0.0, even_row_sum(fxl2.at[j], quarter)))
        fy = group(fy2[j, pl.ds(PAD + 1, quarter, 2), :])
        fz = group(jnp.where(odd_depth, even_row_sum(fz2.at[j], quarter), 0.0))
        weight = (fx + fxl) + (fy + behind(fy, 1, 0)) + (fz + behind(fz, 4, 1))
        start = source / (64.0 + weight)
        tile = jnp.where(item == 0, start, jnp.where(item == 1, fx, jnp.where(item == 2, fy, fz)))
        for c in range(chips):
            slots[c, k] = tile
    halo = packed_odd(jnp.where(first_of_two, fresh[2], fresh[1]), pair.at[2])
    for c in range(chips):
        slots[c, 2] = halo


def joined(one, two):
    return jnp.concatenate([part for part in (one, two) if part.shape[0]], 0)


class Level:
    def __init__(self, mass, source, faces, row_step, lane_step, slot_step):
        self.source, self.row_step, self.lane_step, self.slot_step = source, row_step, lane_step, slot_step
        self.fx, self.fy, self.fz = faces
        self.tiles = source.shape[0]
        shape = source.shape
        self.lane = lanes_of(shape)
        layer = lax.broadcasted_iota(jnp.int32, shape, 0) if self.tiles > 1 else self.lane // slot_step
        self.even = ((layer + rows_of(shape) // row_step + self.lane // lane_step) & 1) == 0
        self.fxl = self.lower(self.fx)
        self.fyl = self.row_shifts(self.fy)[1]
        self.fzl = behind(self.fz, lane_step, 2)
        weight = (self.fx + self.fxl) + (self.fy + self.fyl) + (self.fz + self.fzl)
        self.inv = 1.0 / (mass + weight)

    def upper(self, e):
        return joined(e[1:], ahead(e[:1], self.slot_step, 2))

    def lower(self, e):
        return joined(behind(e[-1:], self.slot_step, 2), e[:-1])

    def row_shifts(self, e):
        return ahead(e, self.row_step, 1), behind(e, self.row_step, 1)

    def neigh(self, e):
        above, below = self.row_shifts(e)
        total = (self.fx * self.upper(e) + self.fxl * self.lower(e)) + (self.fy * above + self.fyl * below)
        return total + (self.fz * ahead(e, self.lane_step, 2) + self.fzl * behind(e, self.lane_step, 2))

    def start(self):
        return self.source * self.inv

    def update(self, e):
        return self.start() + self.neigh(e) * self.inv

    def cycle(self, deeper):
        odd = self.update(self.start())
        residual = jnp.where(self.even, self.neigh(odd), 0.0)
        fix = deeper(self.restricted(residual), self.coarse_faces())
        even = self.update(odd + self.prolonged(fix))
        return jnp.where(self.even, even, self.update(even))

    def coarse_slot_step(self):
        return self.slot_step if self.tiles > 1 else 2 * self.slot_step

    def pairs(self, values):
        if self.tiles == 1:
            return with_partner(values, self.slot_step, 2)
        halves = values.reshape(self.tiles // 2, 2, *values.shape[1:])
        return halves[:, 0] + halves[:, 1]

    def odd_layers(self, values):
        if self.tiles == 1:
            return with_partner(jnp.where((self.lane & self.slot_step) != 0, values, 0.0), self.slot_step, 2)
        return values.reshape(self.tiles // 2, 2, *values.shape[1:])[:, 1]

    def row_pairs(self, values):
        return with_partner(values, self.row_step, 1)

    def odd_rows(self, values):
        odd = (rows_of(values.shape) & self.row_step) != 0
        return with_partner(jnp.where(odd, values, 0.0), self.row_step, 1)

    def restricted(self, values):
        return with_partner(self.row_pairs(self.pairs(values)), self.lane_step, 2)

    def coarse_faces(self):
        fx = with_partner(self.row_pairs(self.odd_layers(self.fx)), self.lane_step, 2)
        fy = with_partner(self.odd_rows(self.pairs(self.fy)), self.lane_step, 2)
        return fx, fy, self.restricted(jnp.where((self.lane & self.lane_step) != 0, self.fz, 0.0))

    def prolonged(self, fix):
        if self.tiles == 1:
            return fix
        both = jnp.concatenate([fix[:, None], fix[:, None]], 1)
        return both.reshape(self.tiles, *fix.shape[1:])


class Rows(Level):
    def __init__(self, mass, source, faces, scratch):
        self.scratch, self.used = scratch, 0
        self.rows = source.shape[1]
        super().__init__(mass, source, faces, 1, 4, 1)

    def start(self):
        return self.source

    def place(self):
        self.used += 1
        return self.scratch.at[self.used % self.scratch.shape[0]]

    def row_shifts(self, e):
        place = self.place()
        edge = jnp.zeros((e.shape[0], PAD, e.shape[2]), jnp.float32)
        place[:, :PAD] = edge
        place[:, PAD + self.rows:] = edge
        place[:, pl.ds(PAD, self.rows)] = e
        return place[:, pl.ds(PAD + 1, self.rows)], place[:, pl.ds(PAD - 1, self.rows)]

    def every_other(self, values, starts):
        place, tiles = self.place(), values.shape[0]
        place[:tiles, : self.rows] = values
        found = 0.0
        for start in starts:
            found = found + jnp.concatenate(
                [place[j, pl.ds(start, self.rows // 2, 2), :][None] for j in range(tiles)], 0
            )
        return found

    def row_pairs(self, values):
        return self.every_other(values, (0, 1))

    def odd_rows(self, values):
        return self.every_other(values, (1,))

    def prolonged(self, fix):
        place, tiles = self.place(), fix.shape[0]
        for j in range(tiles):
            into_both_rows(place.at[j, pl.ds(0, self.rows)], fix[j])
        return super().prolonged(place[:tiles, : self.rows])


def coarsest(mass, source, faces, *steps):
    row_step, lane_step, slot_step = steps
    level = Level(mass, source, faces, *steps)
    counts = source.shape[1] // row_step, source.shape[2] // lane_step, 4 // slot_step
    frames = [(m, k, q) for m in range(counts[0]) for k in range(counts[1]) for q in range(counts[2])]
    place = level.lane & 3

    def spread(values):
        copies = {}
        for m, k, q in frames:
            if k:
                copies[m, k, q] = behind(copies[m, 0, q], k * lane_step, 2)
            elif q:
                by = q * slot_step
                one, two = behind(copies[m, 0, 0], by, 2), ahead(copies[m, 0, 0], 4 - by, 2)
                copies[m, k, q] = jnp.where(place >= by, one, two)
            else:
                copies[m, k, q] = behind(values, m * row_step, 1) if m else values
        return copies

    start, inv, fx, fy, fz = [spread(values) for values in (source * level.inv, level.inv, level.fx, level.fy, level.fz)]

    def shifted(copies, frame, axis, by):
        moved = list(frame)
        moved[axis] = (frame[axis] - by) % counts[axis]
        return copies[tuple(moved)]

    def along_x(copies, frame, by):
        here, wrapped = copies[frame], shifted(copies, frame, 2, by)
        return joined(here[1:], wrapped[:1]) if by > 0 else joined(wrapped[-1:], here[:-1])

    weights = {}
    for frame in frames:
        pairs = [
            (fx[frame], along_x(fx, frame, -1)),
            (fy[frame], shifted(fy, frame, 0, -1)),
            (fz[frame], shifted(fz, frame, 1, -1)),
        ]
        weights[frame] = [(up * inv[frame], low * inv[frame]) for up, low in pairs]

    def update(e):
        fresh = {}
        for frame in frames:
            (x_up, x_low), (y_up, y_low), (z_up, z_low) = weights[frame]
            total = x_up * along_x(e, frame, 1) + x_low * along_x(e, frame, -1)
            total = total + (y_up * shifted(e, frame, 0, 1) + y_low * shifted(e, frame, 0, -1))
            total = total + (z_up * shifted(e, frame, 1, 1) + z_low * shifted(e, frame, 1, -1))
            fresh[frame] = start[frame] + total
        return fresh

    even = start
    odd = update(even)
    for turn in range(COARSE_SWEEPS - 1):
        even = update(odd)
        odd = update(even)
    return jnp.where(level.even, even[0, 0, 0], odd[0, 0, 0])


def small_cycle(mass, source, faces, row_step, lane_step, slot_step, between):
    if between == 0:
        return coarsest(mass, source, faces, row_step, lane_step, slot_step)
    level = Level(mass, source, faces, row_step, lane_step, slot_step)
    return level.cycle(
        lambda inner, inner_faces: small_cycle(
            8.0 * mass, inner, inner_faces, 2 * row_step, 2 * lane_step, level.coarse_slot_step(), between - 1
        )
    )


def coarse_kernel(
    owner_of, gathered, e2_in, s2_in, fx2_in, fxl2_in, fy2_in, fz2_in, fzl2_in, inv2_in,
    inputs, new_in, fx_more, fy_margin, fz_margin, fzl_margin, inv_more, fx_in, fy_in, fz_in, fzl_in, inv_in,
    new_out, known_out, fx_out, fy_out, fz_out, fzl_out, inv_out, within_in,
    solved_out, owned_out,
    e3, rows3, pair, e2, e1, cor, solved, owned, owner_here, fetch_sem, sems,
):
    fetch = pltpu.make_async_copy(owner_of, owner_here, fetch_sem)
    fetch.start()
    chips, _, quarter, lanes = gathered.shape
    blocks = 2 * chips
    half, height = 2 * quarter, 4 * quarter
    position, last = lax.axis_index("gx"), blocks - 1

    slot = lanes_of((quarter, lanes)) & 3
    spread = blocks // 4
    tiles = [gathered[chip, k] for chip in range(chips) for k in range(2)]
    items = []
    for k in range(4):
        packs = []
        for j in range(spread):
            value = tiles[j + (3 - k) % 4 * spread]
            for at in range(3):
                value = jnp.where(slot == at, tiles[j + (at - k) % 4 * spread], value)
            if k:
                value = jnp.where(slot < 4 - k, ahead(value, k, 1), behind(value, 4 - k, 1))
            packs.append(value[None])
        items.append(jnp.concatenate(packs, 0))
    third = Rows(64.0, items[0], items[1:], rows3)
    e3[...] = third.cycle(
        lambda inner, faces: small_cycle(512.0, inner, faces, 1, 8, third.coarse_slot_step(), 2)
    )

    fetch.wait()
    owner = owner_here[position]
    wide, narrow = lanes_of((lanes, lanes)), rows_of((lanes, lanes))
    take = jnp.where(narrow == 4 * wide + owner // spread, 1.0, 0.0)
    block = jnp.dot(
        e3[owner % spread], take, precision=lax.Precision.HIGHEST, preferred_element_type=jnp.float32
    )
    owned[0] = block[:, : lanes // 4]
    copies = [pltpu.make_async_copy(owned, owned_out, sems.at[0])]
    copies[0].start()

    first_of_two, even2 = parities2(half, lanes)
    body2 = pl.ds(PAD, half)
    edge = jnp.zeros((PAD, lanes), jnp.float32)
    core = core_of()
    s2, fx2, fxl2, fy2, fz2, fzl2, inv2 = [
        ref.at[pl.ds(core, 3)] for ref in (s2_in, fx2_in, fxl2_in, fy2_in, fz2_in, fzl2_in, inv2_in)
    ]
    next_chip = jnp.clip(position // 2 - 1 + 2 * core, 0, chips - 1)
    into_both_rows(pair.at[5], gathered[next_chip, 2])
    halo = pair[5]
    before = (
        by_side(halo, e2_in[0])[0], by_side(jnp.where(first_of_two, halo, e2_in[0]), e2_in[1])[0],
        by_side(e2_in[1], e2_in[2])[0],
        by_side(e2_in[2], jnp.where(first_of_two, e2_in[3], halo))[0], by_side(e2_in[3], halo)[0],
    )
    for k in range(5):
        j = jnp.clip(position + k - 2, 0, last)
        into_both_rows(pair.at[k], group(jnp.where(slot == j // spread, e3[j % spread], 0.0)))
        e2[k, :PAD] = edge
        e2[k, PAD + half:] = edge
        e2[k, body2] = before[k] + pair[k]

    def update2():
        sums = neigh2(e2, fx2, fxl2, fy2, fz2, fzl2, first_of_two, (0, 1, 2))
        return [(s2[j] + sums[j]) * inv2[j] for j in range(3)]

    fresh = update2()
    for j in range(3):
        e2[j + 1, body2] = fresh[j]
    fixes2 = [jnp.where(even2, even, odd) for even, odd in zip(fresh, update2())]

    _, source, _ = three_parts(inputs)
    layers = source.shape[0]
    plane = Plane(height, lanes)
    body1 = plane.body
    near_lane = (lanes_of((half, lanes)) & 1) == core
    swaps = [jnp.where(first_of_two, ahead(v, 1, 1), behind(v, 1, 1)) for v in fixes2]
    outer, inner = by_side(fixes2[0], fixes2[2])
    outer_swap, inner_swap = by_side(swaps[0], swaps[2])
    coarse = (
        jnp.where(near_lane, outer_swap, outer), jnp.where(near_lane, fixes2[1], swaps[1]),
        jnp.where(near_lane, swaps[1], fixes2[1]), jnp.where(near_lane, inner, inner_swap),
    )
    fixes = []
    for k in range(4):
        into_both_rows(cor.at[k], coarse[k])
        fixes.append(cor[k])
    for u in range(-1, layers + 1):
        before = new_out[u + 1] if u < 2 else new_in[u - 2]
        plane.put(e1.at[u + 1], before + fixes[(u + 2) // 2])

    def fx1(u):
        if u < 0:
            return fx_out[-1 - u]
        return fx_in[u] if u < layers - 1 else fx_more[u - layers + 1]

    def inv1(u):
        if u <= 0:
            return inv_out[u + 1]
        return inv_in[u - 1] if u < layers - 1 else inv_more[u - layers + 1]

    def around1(u):
        if u < 0:
            return in_layer(plane, fy_out, fz_out, fzl_out, e1.at[0])
        if u == layers:
            return in_layer(plane, fy_margin, fz_margin, fzl_margin, e1.at[u + 1])
        return in_layer(plane, fy_in.at[u], fz_in.at[u], fzl_in.at[u], e1.at[u + 1])

    def updated1(u):
        sums = around1(u) + (fx1(u) * e1[u + 2, body1] + fx1(u - 1) * e1[u, body1])
        return (source[own_layer(u, layers)] + sums) * inv1(u)

    for u in range(layers):
        e1[u + 1, body1] = jnp.where(plane.even(u), updated1(u), e1[u + 1, body1])
    e1[0, body1] = (known_out[...] + fx1(-2) * fixes[0] + (around1(-1) + fx1(-1) * e1[1, body1])) * inv1(-1)
    into_both_rows(cor.at[4], within_in[4])
    sums = cor[4] + fx1(layers) * fixes[3] + (around1(layers) + fx1(layers - 1) * e1[layers, body1])
    e1[layers + 1, body1] = sums * inv1(layers)
    for u in range(layers):
        solved[u] = jnp.where(plane.even(u), e1[u + 1, body1], updated1(u))
        copies.append(
            pltpu.make_async_copy(solved.at[u], solved_out.at[own_layer(u, layers)], sems.at[u + 1])
        )
        copies[-1].start()
    for copy in copies:
        copy.wait()


def f32(*shape):
    return jax.ShapeDtypeStruct(shape, jnp.float32)


def vmem(*shape):
    return pltpu.VMEM(shape, jnp.float32)


def call(kernel, outs, scratch, operands, out_space=pltpu.VMEM):
    def size(shape):
        count = 4
        for extent in shape:
            count *= extent
        return count

    sized = [array for array in (*scratch, *outs, *operands) if hasattr(array, "shape")]
    asked = 8 * 2**20 + sum(size(array.shape) for array in sized)
    return pl.pallas_call(
        kernel,
        out_shape=tuple(outs),
        in_specs=[pl.BlockSpec(memory_space=pltpu.VMEM)] * len(operands),
        out_specs=tuple([pl.BlockSpec(memory_space=out_space)] * len(outs)),
        scratch_shapes=scratch,
        compiler_params=pltpu.CompilerParams(vmem_limit_bytes=asked),
    )(*operands)


def on_device(iterate, source, phase_field, block_owner):
    layers, height, depth = iterate.shape
    half, quarter = height // 2, height // 4
    blocks = lax.axis_size("gx")
    padded, padded2 = height + 2 * PAD, half + 2 * PAD
    inputs = sum(
        jnp.pad(block, ((k * layers, (2 - k) * layers), (0, 0), (0, 0)))
        for k, block in enumerate((iterate, source, phase_field))
    )
    edge, = call(edge_kernel, [f32(3 * height + half, depth)], [], (inputs,))
    edge_in = within_chip(edge)
    layer, tile, tall = (height, depth), (half, depth), (padded, depth)
    cell, old, *fine, even = call(
        own_kernel,
        [
            f32(layers, *layer), f32(layers, *tall), f32(layers - 1, *layer), f32(layers, *tall),
            f32(layers, *layer), f32(layers, *layer), f32(2, *layer), f32(2, *tall),
        ],
        [], (block_owner, inputs),
    )
    message, own2, known1, new, *margin = call(
        chip_kernel,
        [
            f32(chip_rows(height)[1], depth), f32(2, *tile), f32(*layer), f32(3, *layer),
            f32(2, *layer), f32(*tall), f32(*layer), f32(*layer), f32(2, *layer),
        ],
        [vmem(*tall), vmem(2, *tall), vmem(3, *tall), vmem(10, *layer)],
        (inputs, cell, old, *fine, even, edge_in),
    )
    within, fx2, *border = call(
        border_kernel,
        [
            f32(9, *tile), f32(*tile), f32(3, *layer), f32(*layer), f32(2, *layer),
            f32(padded, depth), f32(*layer), f32(*layer), f32(2, *layer),
        ],
        [
            vmem(1, padded, depth), vmem(2, padded, depth), vmem(4, padded, depth), vmem(8, *layer),
            vmem(2, padded, depth), vmem(2, *layer), vmem(2, *layer),
        ],
        (inputs, message, own2, known1, new, *fine, between_chips(message)),
    )
    within_in = within_chip(within)
    plain = f32(4, *tile)
    slots, *middle = call(
        middle_down_kernel,
        [f32(blocks // 2, 3, quarter, depth), plain, plain, plain, plain, f32(4, padded2, depth)] + [plain] * 3,
        [vmem(6, padded2, depth), vmem(3, *tile)],
        (within, fx2, within_in),
    )
    kinds = [list(range(core, blocks, 2)) for core in range(2)]
    gathered = lax.all_to_all(slots, "gx", 0, 0, axis_index_groups=kinds, tiled=True)
    solved, owned = call(
        coarse_kernel,
        [f32(layers, *layer), f32(1, quarter, depth // 4)],
        [
            vmem(blocks // 4, quarter, depth), vmem(4, blocks // 4, quarter + 2 * PAD, depth), vmem(7, *tile),
            vmem(5, padded2, depth), vmem(layers + 2, padded, depth), vmem(5, *layer), vmem(layers, *layer),
            vmem(1, quarter, depth // 4), pltpu.SMEM((blocks,), jnp.int32),
            pltpu.SemaphoreType.DMA, pltpu.SemaphoreType.DMA((layers + 1,)),
        ],
        (block_owner, gathered, *middle, inputs, new, *margin, *fine, *border, within_in),
        pl.ANY,
    )
    return solved, owned


def solution(mesh):
    split = P(("groups", "gx"), None, None)
    return jax.shard_map(
        on_device,
        mesh=mesh,
        in_specs=(split, split, split, P("groups")),
        out_specs=(split, split),
        check_vma=False,
    )
```

```python
import jax
import jax.numpy as jnp
from jax import lax
from jax.experimental import pallas as pl
from jax.experimental.pallas import tpu as pltpu
from jax.sharding import PartitionSpec as P

STIFFNESS = 100.0
EPSILON = 0.01
COARSE_SWEEPS = 4
PAD = 8


def between_chips(block):
    return lax.ppermute(block, "gx", [(i, i + 1 if i % 2 else i - 1) for i in range(1, lax.axis_size("gx") - 1)])


def within_chip(block):
    return lax.ppermute(block, "gx", [(i, i ^ 1) for i in range(lax.axis_size("gx"))])


def by_side(across, within):
    on_left = lax.axis_index("gx") % 2 == 0
    return jnp.where(on_left, across, within), jnp.where(on_left, within, across)


def lanes_of(shape):
    return lax.broadcasted_iota(jnp.int32, shape, len(shape) - 1)


def rows_of(shape):
    return lax.broadcasted_iota(jnp.int32, shape, len(shape) - 2)


def ahead(values, step, axis):
    return pltpu.roll(values, values.shape[axis] - step, axis)


def behind(values, step, axis):
    return pltpu.roll(values, step, axis)


def with_partner(values, step, axis):
    index = lax.broadcasted_iota(jnp.int32, values.shape, axis)
    partner = jnp.where((index & step) == 0, ahead(values, step, axis), behind(values, step, axis))
    return values + partner


def even_row_sum(scratch, rows):
    return scratch[pl.ds(0, rows, 2), :] + scratch[pl.ds(1, rows, 2), :]


def core_of():
    return lax.axis_index("gx") % 2


def own_layer(u, layers):
    return u + core_of() * (layers - 1 - 2 * u)


def three_parts(ref):
    third = ref.shape[0] // 3
    return [ref.at[pl.ds(k * third, third)] for k in range(3)]


def odd_cells(ref, rows, first):
    return jnp.where(first, ref[pl.ds(0, rows, 2), :], ref[pl.ds(1, rows, 2), :])


def into_both_rows(ref, values):
    rows = values.shape[0]
    ref[pl.ds(0, rows, 2), :] = values
    ref[pl.ds(1, rows, 2), :] = values


def cell_coef(value):
    return STIFFNESS * (value * value + EPSILON)


class Plane:
    def __init__(self, height, depth):
        self.height, self.half, self.depth = height, height // 2, depth
        self.row, self.lane = rows_of((height, depth)), lanes_of((height, depth))
        self.parity = self.row + self.lane + core_of()
        self.half_lane = lanes_of((self.half, depth))
        self.body = pl.ds(PAD, height)
        self.up, self.down = pl.ds(PAD + 1, height), pl.ds(PAD - 1, height)

    def even(self, u):
        return ((self.parity + u) & 1) == 0

    def odd_first(self, u):
        return ((self.half_lane + core_of() + u) & 1) != 0

    def put(self, ref, values):
        edge = jnp.zeros((PAD, self.depth), jnp.float32)
        ref[:PAD] = edge
        ref[PAD + self.height:] = edge
        ref[self.body] = values

    def face_y(self, here):
        return jnp.where(self.row < self.height - 1, 0.5 * (here + ahead(here, 1, 0)), 0.0)

    def face_z(self, here):
        return jnp.where(self.lane < self.depth - 1, 0.5 * (here + ahead(here, 1, 1)), 0.0)

    def packed(self, outer, inner, core):
        return jnp.where((self.half_lane & 1) == core, outer, inner)

    def both_rows(self, ref):
        return even_row_sum(ref, self.half)

    def summed(self, values, ref):
        ref[...] = values
        return with_partner(self.both_rows(ref), 1, 1)

    def odd_rows(self, values, ref):
        ref[...] = values
        return with_partner(ref[pl.ds(1, self.half, 2), :], 1, 1)

    def odd_lanes(self, values, ref):
        ref[...] = values
        sums = self.both_rows(ref)
        return jnp.where((self.half_lane & 1) == 0, ahead(sums, 1, 1), sums)


def in_layer(plane, fy, fz, fzl, padded):
    here = padded[plane.body]
    total = fy[plane.body] * padded[plane.up] + fy[plane.down] * padded[plane.down]
    return total + (fz[...] * ahead(here, 1, 1) + fzl[...] * behind(here, 1, 1))


def edge_kernel(inputs, out):
    iterate, source, phase = three_parts(inputs)
    layers, height, depth = iterate.shape
    plane = Plane(height, depth)
    near, inner, far = [own_layer(u, layers) for u in (layers - 1, layers - 2, layers - 3)]
    coef_near, coef_inner, coef_far = [cell_coef(phase[k]) for k in (near, inner, far)]

    def around(here, e):
        fy, fz = plane.face_y(here), plane.face_z(here)
        fyl, fzl = behind(fy, 1, 0), behind(fz, 1, 1)
        total = fy * ahead(e, 1, 0) + fyl * behind(e, 1, 0)
        return total + fz * ahead(e, 1, 1) + fzl * behind(e, 1, 1), fy + fyl + fz + fzl

    face_near, face_far = 0.5 * (coef_inner + coef_near), 0.5 * (coef_inner + coef_far)
    total, weight = around(coef_inner, iterate[inner])
    total = total + face_near * iterate[near] + face_far * iterate[far]
    updated = (source[inner] + total) / (1.0 + (face_near + face_far + weight))
    total, _ = around(coef_near, iterate[near])
    known = jnp.where(plane.even(layers - 1), total + face_near * iterate[inner], face_near * updated)
    out[:height] = coef_near
    out[height:2 * height] = coef_inner
    out[2 * height:3 * height] = source[near] + known
    out[3 * height:] = odd_cells(iterate.at[near], plane.half, plane.odd_first(layers - 1))


def chip_rows(height):
    half, at, places = height // 2, 0, {}
    for name, size in (
        ("coef0", height), ("coef1", height), ("known0", height), ("old0", half), ("moved1", half), ("face2", half),
        ("source2", half), ("fx2", half), ("far2", half),
    ):
        places[name] = pl.ds(at, size)
        at += size
    return places, at


def own_kernel(owner_of, inputs, cell, old, fx, fy, fz, fzl, inv, even):
    iterate, source, phase = three_parts(inputs)
    layers, height, depth = iterate.shape
    plane = Plane(height, depth)
    body = plane.body
    for u in range(layers):
        cell[u] = cell_coef(phase[own_layer(u, layers)])
        plane.put(old.at[u], iterate[own_layer(u, layers)])
    for u in range(layers):
        here = cell[u]
        if u < layers - 1:
            fx[u] = 0.5 * (here + cell[u + 1])
        plane.put(fy.at[u], plane.face_y(here))
        face = plane.face_z(here)
        fz[u] = face
        fzl[u] = behind(face, 1, 1)
    for u in (1, 2):
        weight = (fx[u] + fx[u - 1]) + (fy[u, body] + fy[u, plane.down]) + (fz[u] + fzl[u])
        inverse = 1.0 / (1.0 + weight)
        inv[u - 1] = inverse
        around = in_layer(plane, fy.at[u], fz.at[u], fzl.at[u], old.at[u])
        total = source[own_layer(u, layers)] + around + (fx[u] * old[u + 1, body] + fx[u - 1] * old[u - 1, body])
        plane.put(even.at[u - 1], total * inverse)


def chip_kernel(
    inputs, cell, old_own, fx_own, fy_own, fz_own, fzl_own, inv_own, even_own, within_in,
    message, own2, known1, new, fx_more, fy_margin, fz_margin, fzl_margin, inv_more,
    old_margin, even_more, change, turn,
):
    iterate, source, phase = three_parts(inputs)
    layers, height, depth = iterate.shape
    plane = Plane(height, depth)
    body, half = plane.body, plane.half
    places, _ = chip_rows(height)
    margin = layers

    def part(k):
        return within_in[k * height:(k + 1) * height]

    def s(u):
        return source[own_layer(u, layers)]

    into_both_rows(turn.at[0], within_in[3 * height:])
    plane.put(old_margin, turn[0])
    fx_more[0] = 0.5 * (cell[layers - 1] + part(0))
    fx_more[1] = 0.5 * (part(0) + part(1))
    plane.put(fy_margin, plane.face_y(part(0)))
    face = plane.face_z(part(0))
    fz_margin[...] = face
    fzl_margin[...] = behind(face, 1, 1)
    fx = [fx_own.at[u] for u in range(3)] + [fx_more.at[0], fx_more.at[1]]
    fy = [fy_own.at[u] for u in range(layers)] + [fy_margin]
    fz = [fz_own.at[u] for u in range(layers)] + [fz_margin]
    fzl = [fzl_own.at[u] for u in range(layers)] + [fzl_margin]
    old = [old_own.at[u] for u in range(layers)] + [old_margin]
    inv = [None, inv_own.at[0], inv_own.at[1], inv_more.at[0], inv_more.at[1]]
    even = [None, even_own.at[0], even_own.at[1], even_more.at[0], even_more.at[1]]
    for u in (margin - 1, margin):
        weight = (fx[u][...] + fx[u - 1][...]) + (fy[u][body] + fy[u][plane.down]) + (fz[u][...] + fzl[u][...])
        inv[u][...] = 1.0 / (1.0 + weight)

    def around(ref, u):
        return in_layer(plane, fy[u], fz[u], fzl[u], ref[u])

    u = margin - 1
    total = s(u) + around(old, u) + (fx[u][...] * old[u + 1][body] + fx[u - 1][...] * old[u - 1][body])
    plane.put(even[u], total * inv[u][...])
    plane.put(even[margin], (part(2) + fx[u][...] * old[u][body]) * inv[margin][...])
    for u in range(2, margin + 1):
        if u < margin:
            total = s(u) + around(even, u) + (fx[u][...] * even[u + 1][body] + fx[u - 1][...] * even[u - 1][body])
        else:
            total = part(2) + around(even, u) + fx[u - 1][...] * even[u - 1][body]
        fresh = total * inv[u][...]
        new[u - 2] = fresh
        plane.put(change.at[u - 2], fresh - old[u][body])
    change = {u: change.at[u - 2] for u in range(2, margin + 1)}

    one = fx[1][...] * change[2][body]
    two = around(change, 2) + fx[2][...] * change[3][body]
    three = around(change, 3) + (fx[2][...] * change[2][body] + fx[3][...] * change[4][body])
    outer = jnp.where(plane.even(1), one, 0.0)
    inner = jnp.where(plane.even(2), two, 0.0) + jnp.where(plane.even(3), three, 0.0)
    core = core_of()

    def tile(name, outer, inner):
        message[places[name], :] = plane.packed(outer, inner, core)

    tile("source2", plane.summed(outer, turn.at[1]), plane.summed(inner, turn.at[2]))
    tile("fx2", plane.summed(fx[1][...], turn.at[3]), plane.summed(fx[3][...], turn.at[4]))
    fy2 = [plane.odd_rows(fy[u][body] + fy[u + 1][body], turn.at[5 + u // 2]) for u in (0, 2)]
    fz2 = [plane.odd_lanes(fz[u][...] + fz[u + 1][...], turn.at[7 + u // 2]) for u in (0, 2)]
    own2[0], own2[1] = plane.packed(*fy2, core), plane.packed(*fz2, core)
    tile("far2", fy2[1], fz2[1])
    for u in range(2):
        message[places["coef%d" % u], :] = cell[u]
    first = s(0) + around(old, 0) + fx[0][...] * old[1][body]
    second = s(0) + fx[0][...] * even[1][body]
    message[places["known0"], :] = jnp.where(plane.even(0), first, second)
    message[places["old0"], :] = odd_cells(iterate.at[own_layer(0, layers)], half, plane.odd_first(0))
    total = s(1) + around(even, 1) + fx[1][...] * even[2][body]
    known1[...] = total
    turn[9] = total * inv[1][...] - old[1][body]
    message[places["moved1"], :] = odd_cells(turn.at[9], half, plane.odd_first(1))
    message[places["face2"], :] = odd_cells(fx[1], half, plane.odd_first(1))


def border_kernel(
    inputs, message, own2, known1, new_in, fx_in, fy_in, fz_in, fzl_in, inv_in, across_in,
    within, fx2_in, new, known, fx, fy, fz, fzl, inv,
    old, even, change, turn, face_y, face_z, face_zl,
):
    iterate, source, _ = three_parts(inputs)
    layers, height, depth = iterate.shape
    plane = Plane(height, depth)
    body, half = plane.body, plane.half
    places, _ = chip_rows(height)
    core, last = core_of(), lax.axis_size("gx") - 1
    position = lax.axis_index("gx")

    def mine(name):
        return message[places[name], :]

    def theirs(name):
        return across_in[places[name], :]

    def opened(name, k):
        into_both_rows(turn.at[k], theirs(name))
        return turn[k]

    for k in range(2):
        here = theirs("coef%d" % k)
        plane.put(face_y.at[k], plane.face_y(here))
        face = plane.face_z(here)
        face_z[k] = face
        face_zl[k] = behind(face, 1, 1)
    fy[...], fz[...], fzl[...] = face_y[0], face_z[0], face_zl[0]
    there = position - 1 + 2 * core
    border = jnp.where((there >= 0) & (there <= last), 0.5 * (mine("coef0") + theirs("coef0")), 0.0)
    face1 = 0.5 * (theirs("coef0") + theirs("coef1"))
    face2 = opened("face2", 2)
    fx[0], fx[1] = border, face1

    def inverse(faces, fy, fz, fzl):
        weight = faces + (fy[body] + fy[plane.down]) + (fz[...] + fzl[...])
        return 1.0 / (1.0 + weight)

    inv_own = inverse(fx_in[0] + border, fy_in.at[0], fz_in.at[0], fzl_in.at[0])
    inv_near = inverse(border + face1, face_y.at[0], face_z.at[0], face_zl.at[0])
    inv_far = inverse(face1 + face2, face_y.at[1], face_z.at[1], face_zl.at[1])
    inv[0], inv[1] = inv_near, inv_own
    old_own, old_next = iterate[own_layer(0, layers)], iterate[own_layer(1, layers)]
    old_near, far = opened("old0", 0), opened("moved1", 1)
    even_own = (mine("known0") + border * old_near) * inv_own
    even_near = (theirs("known0") + border * old_own) * inv_near
    plane.put(even.at[0], even_near)
    plane.put(even.at[1], even_own)

    def near(ref, k):
        return in_layer(plane, face_y.at[k], face_z.at[k], face_zl.at[k], ref)

    def own(ref, u):
        return in_layer(plane, fy_in.at[u], fz_in.at[u], fzl_in.at[u], ref)

    odd_own = (mine("known0") + own(even.at[1], 0) + border * even_near) * inv_own
    odd_near = (theirs("known0") + near(even.at[0], 0) + border * even_own) * inv_near
    odd_next = (known1[...] + fx_in[0] * even_own) * inv_in[0]
    far = far + face1 * even_near * inv_far
    new[0], new[1], new[2] = odd_near, odd_own, odd_next
    near_by, here, following = odd_near - old_near, odd_own - old_own, odd_next - old_next
    for k, values in enumerate((far, near_by, here, following)):
        plane.put(change.at[k], values)
    plane.put(old.at[0], old_near)
    known[...] = theirs("known0") + face1 * far - near(old.at[0], 0)

    def residual(u, values):
        return jnp.where(plane.even(u), values, 0.0)

    own_outer = residual(1, own(change.at[3], 1) + fx_in[0] * here)
    own_outer = own_outer + residual(0, own(change.at[2], 0) + (fx_in[0] * following + border * near_by))
    own_inner = residual(2, fx_in[1] * following)
    its_outer = residual(-1, near(change.at[1], 0) + (face1 * far + border * here))
    its_outer = its_outer + residual(-2, near(change.at[0], 1) + face1 * near_by)
    its_inner = residual(-3, face2 * far)
    sums = [plane.summed(values, turn.at[3 + k]) for k, values in enumerate((own_outer, own_inner, its_outer, its_inner))]
    within[0] = mine("source2") + plane.packed(sums[0], sums[1], core)
    within[5] = theirs("source2") + plane.packed(sums[2], sums[3], 1 - core)
    within[6] = theirs("fx2")
    far2 = theirs("far2")
    far2_swap = jnp.where((plane.half_lane & 1) == 0, ahead(far2, 1, 1), behind(far2, 1, 1))
    near_fy2 = plane.odd_rows(face_y[0, body] + face_y[1, body], turn.at[1])
    near_fz2 = plane.odd_lanes(face_z[0] + face_z[1], turn.at[2])
    within[7] = plane.packed(near_fy2, far2_swap, 1 - core)
    within[8] = plane.packed(near_fz2, far2, 1 - core)
    fx2_in[...] = mine("fx2")
    middle = jnp.where((plane.half_lane & 1) == 0, ahead(mine("fx2"), 1, 1), behind(mine("fx2"), 1, 1))
    within[1] = plane.packed(plane.summed(border, turn.at[7]), middle, core)
    within[2], within[3] = own2[0], own2[1]
    turn[0] = source[own_layer(layers - 1, layers)] + fx_in[layers - 2] * new_in[layers - 4]
    within[4] = odd_cells(turn.at[0], half, jnp.logical_not(plane.odd_first(layers - 1)))


def neigh2(e2, fx2, fxl2, fy2, fz2, fzl2, first_of_two, tiles):
    half = fx2.shape[1]
    body, up, down = pl.ds(PAD, half), pl.ds(PAD + 1, half), pl.ds(PAD - 1, half)
    needed = range(tiles[0], tiles[-1] + 3)
    here = {j: e2[j, body] for j in needed}
    after = {j: ahead(here[j], 1, 1) for j in needed}
    before = {j: behind(here[j], 1, 1) for j in needed}
    found = []
    for j in tiles:
        k = j + 1
        upper = jnp.where(first_of_two, after[k], before[k + 1])
        lower = jnp.where(first_of_two, after[k - 1], before[k])
        sums = fx2[j] * upper + fxl2[j] * lower
        sums = sums + fy2[j, body] * e2[k, up] + fy2[j, down] * e2[k, down]
        sums = sums + fz2[j] * ahead(here[k], 2, 1) + fzl2[j] * behind(here[k], 2, 1)
        found.append(sums)
    return found


def parities2(half, lanes):
    row, lane = rows_of((half, lanes)), lanes_of((half, lanes))
    return (lane & 1) == 0, ((row + (lane & 1) + (lane >> 1)) & 1) == 0


def group(values):
    return with_partner(with_partner(values, 1, 1), 2, 1)


def packed_odd(values, pair):
    half, lanes = values.shape
    lane = lanes_of((half // 2, lanes))
    pair[...] = values
    return odd_cells(pair, half // 2, (((lane & 1) + (lane >> 1)) & 1) != 0)


def middle_down_kernel(
    own, fx2_in, within_in,
    slots, e2_out, s2, fx2, fxl2, fy2, fz2, fzl2, inv2,
    e2, pair,
):
    _, half, lanes = own.shape
    quarter = half // 2
    first_of_two, even2 = parities2(half, lanes)
    body, down = pl.ds(PAD, half), pl.ds(PAD - 1, half)
    edge = jnp.zeros((PAD, lanes), jnp.float32)
    for j in (0, 5):
        e2[j] = jnp.zeros((half + 2 * PAD, lanes), jnp.float32)

    def pair_of(k):
        return by_side(own[k], within_in[k])

    def four(k):
        (left, right), (far_left, far_right) = pair_of(k), pair_of(5 + k)
        return far_left, left, right, far_right

    for j, (source, fy, fz) in enumerate(zip(four(0), four(2), four(3))):
        s2[j] = source
        fy2[j, :PAD] = edge
        fy2[j, body] = fy
        fy2[j, PAD + half:] = edge
        fz2[j] = fz
        fzl2[j] = behind(fz, 2, 1)

    def between(left, right):
        return jnp.where(first_of_two, ahead(left, 1, 1), behind(right, 1, 1))

    fxl0, fxl1, fxr2, fxr3 = four(1)
    inner = fx2_in[...]
    fxr1, _ = by_side(inner, between(fxl1, inner))
    fxl2_, _ = by_side(between(inner, fxr2), inner)
    for j, (face, low) in enumerate(
        ((between(fxl0, fxl1), fxl0), (fxr1, fxl1), (fxr2, fxl2_), (fxr3, between(fxr2, fxr3)))
    ):
        fx2[j], fxl2[j] = face, low
        weight = face + low + fy2[j, body] + fy2[j, down] + fz2[j] + fzl2[j]
        inverse = 1.0 / (8.0 + weight)
        inv2[j] = inverse
        e2[j + 1, :PAD] = edge
        e2[j + 1, PAD + half:] = edge
        e2[j + 1, body] = s2[j] * inverse

    def neigh(tiles):
        return neigh2(e2, fx2, fxl2, fy2, fz2, fzl2, first_of_two, tiles)

    fresh = [(s2[j] + sums) * inv2[j] for j, sums in enumerate(neigh((0, 1, 2, 3)))]
    for j in range(4):
        e2[j + 1, body] = fresh[j]
        e2_out[j] = fresh[j]
    lane = lanes_of((quarter, lanes))
    odd_layer, odd_depth = (lane & 1) != 0, (lane & 2) != 0
    chips = slots.shape[0]
    for k, sums in enumerate(neigh((1, 2))):
        j = k + 1
        pair[k] = jnp.where(even2, sums, 0.0)
        item = (lane - (lax.axis_index("gx") // 2 * 2 + k) // (chips // 2)) & 3
        source = group(even_row_sum(pair.at[k], quarter))
        fx = group(jnp.where(odd_layer, even_row_sum(fx2.at[j], quarter), 0.0))
        fxl = group(jnp.where(odd_layer, 0.0, even_row_sum(fxl2.at[j], quarter)))
        fy = group(fy2[j, pl.ds(PAD + 1, quarter, 2), :])
        fz = group(jnp.where(odd_depth, even_row_sum(fz2.at[j], quarter), 0.0))
        weight = (fx + fxl) + (fy + behind(fy, 1, 0)) + (fz + behind(fz, 4, 1))
        start = source / (64.0 + weight)
        tile = jnp.where(item == 0, start, jnp.where(item == 1, fx, jnp.where(item == 2, fy, fz)))
        for c in range(chips):
            slots[c, k] = tile
    halo = packed_odd(jnp.where(first_of_two, fresh[2], fresh[1]), pair.at[2])
    for c in range(chips):
        slots[c, 2] = halo


def joined(one, two):
    return jnp.concatenate([part for part in (one, two) if part.shape[0]], 0)


class Level:
    def __init__(self, mass, source, faces, row_step, lane_step, slot_step):
        self.source, self.row_step, self.lane_step, self.slot_step = source, row_step, lane_step, slot_step
        self.fx, self.fy, self.fz = faces
        self.tiles = source.shape[0]
        shape = source.shape
        self.lane = lanes_of(shape)
        layer = lax.broadcasted_iota(jnp.int32, shape, 0) if self.tiles > 1 else self.lane // slot_step
        self.even = ((layer + rows_of(shape) // row_step + self.lane // lane_step) & 1) == 0
        self.fxl = self.lower(self.fx)
        self.fyl = self.row_shifts(self.fy)[1]
        self.fzl = behind(self.fz, lane_step, 2)
        weight = (self.fx + self.fxl) + (self.fy + self.fyl) + (self.fz + self.fzl)
        self.inv = 1.0 / (mass + weight)

    def upper(self, e):
        return joined(e[1:], ahead(e[:1], self.slot_step, 2))

    def lower(self, e):
        return joined(behind(e[-1:], self.slot_step, 2), e[:-1])

    def row_shifts(self, e):
        return ahead(e, self.row_step, 1), behind(e, self.row_step, 1)

    def neigh(self, e):
        above, below = self.row_shifts(e)
        total = (self.fx * self.upper(e) + self.fxl * self.lower(e)) + (self.fy * above + self.fyl * below)
        return total + (self.fz * ahead(e, self.lane_step, 2) + self.fzl * behind(e, self.lane_step, 2))

    def start(self):
        return self.source * self.inv

    def update(self, e):
        return self.start() + self.neigh(e) * self.inv

    def cycle(self, deeper):
        odd = self.update(self.start())
        residual = jnp.where(self.even, self.neigh(odd), 0.0)
        fix = deeper(self.restricted(residual), self.coarse_faces())
        even = self.update(odd + self.prolonged(fix))
        return jnp.where(self.even, even, self.update(even))

    def coarse_slot_step(self):
        return self.slot_step if self.tiles > 1 else 2 * self.slot_step

    def pairs(self, values):
        if self.tiles == 1:
            return with_partner(values, self.slot_step, 2)
        halves = values.reshape(self.tiles // 2, 2, *values.shape[1:])
        return halves[:, 0] + halves[:, 1]

    def odd_layers(self, values):
        if self.tiles == 1:
            return with_partner(jnp.where((self.lane & self.slot_step) != 0, values, 0.0), self.slot_step, 2)
        return values.reshape(self.tiles // 2, 2, *values.shape[1:])[:, 1]

    def row_pairs(self, values):
        return with_partner(values, self.row_step, 1)

    def odd_rows(self, values):
        odd = (rows_of(values.shape) & self.row_step) != 0
        return with_partner(jnp.where(odd, values, 0.0), self.row_step, 1)

    def restricted(self, values):
        return with_partner(self.row_pairs(self.pairs(values)), self.lane_step, 2)

    def coarse_faces(self):
        fx = with_partner(self.row_pairs(self.odd_layers(self.fx)), self.lane_step, 2)
        fy = with_partner(self.odd_rows(self.pairs(self.fy)), self.lane_step, 2)
        return fx, fy, self.restricted(jnp.where((self.lane & self.lane_step) != 0, self.fz, 0.0))

    def prolonged(self, fix):
        if self.tiles == 1:
            return fix
        both = jnp.concatenate([fix[:, None], fix[:, None]], 1)
        return both.reshape(self.tiles, *fix.shape[1:])


class Rows(Level):
    def __init__(self, mass, source, faces, scratch):
        self.scratch, self.used = scratch, 0
        self.rows = source.shape[1]
        super().__init__(mass, source, faces, 1, 4, 1)

    def start(self):
        return self.source

    def place(self):
        self.used += 1
        return self.scratch.at[self.used % self.scratch.shape[0]]

    def row_shifts(self, e):
        place = self.place()
        edge = jnp.zeros((e.shape[0], PAD, e.shape[2]), jnp.float32)
        place[:, :PAD] = edge
        place[:, PAD + self.rows:] = edge
        place[:, pl.ds(PAD, self.rows)] = e
        return place[:, pl.ds(PAD + 1, self.rows)], place[:, pl.ds(PAD - 1, self.rows)]

    def every_other(self, values, starts):
        place, tiles = self.place(), values.shape[0]
        place[:tiles, : self.rows] = values
        found = 0.0
        for start in starts:
            found = found + jnp.concatenate(
                [place[j, pl.ds(start, self.rows // 2, 2), :][None] for j in range(tiles)], 0
            )
        return found

    def row_pairs(self, values):
        return self.every_other(values, (0, 1))

    def odd_rows(self, values):
        return self.every_other(values, (1,))

    def prolonged(self, fix):
        place, tiles = self.place(), fix.shape[0]
        for j in range(tiles):
            into_both_rows(place.at[j, pl.ds(0, self.rows)], fix[j])
        return super().prolonged(place[:tiles, : self.rows])


def coarsest(mass, source, faces, *steps):
    row_step, lane_step, slot_step = steps
    level = Level(mass, source, faces, *steps)
    counts = source.shape[1] // row_step, source.shape[2] // lane_step, 4 // slot_step
    frames = [(m, k, q) for m in range(counts[0]) for k in range(counts[1]) for q in range(counts[2])]
    place = level.lane & 3

    def spread(values):
        copies = {}
        for m, k, q in frames:
            if k:
                copies[m, k, q] = behind(copies[m, 0, q], k * lane_step, 2)
            elif q:
                by = q * slot_step
                one, two = behind(copies[m, 0, 0], by, 2), ahead(copies[m, 0, 0], 4 - by, 2)
                copies[m, k, q] = jnp.where(place >= by, one, two)
            else:
                copies[m, k, q] = behind(values, m * row_step, 1) if m else values
        return copies

    start, inv, fx, fy, fz = [spread(values) for values in (source * level.inv, level.inv, level.fx, level.fy, level.fz)]

    def shifted(copies, frame, axis, by):
        moved = list(frame)
        moved[axis] = (frame[axis] - by) % counts[axis]
        return copies[tuple(moved)]

    def along_x(copies, frame, by):
        here, wrapped = copies[frame], shifted(copies, frame, 2, by)
        return joined(here[1:], wrapped[:1]) if by > 0 else joined(wrapped[-1:], here[:-1])

    weights = {}
    for frame in frames:
        pairs = [
            (fx[frame], along_x(fx, frame, -1)),
            (fy[frame], shifted(fy, frame, 0, -1)),
            (fz[frame], shifted(fz, frame, 1, -1)),
        ]
        weights[frame] = [(up * inv[frame], low * inv[frame]) for up, low in pairs]

    def update(e):
        fresh = {}
        for frame in frames:
            (x_up, x_low), (y_up, y_low), (z_up, z_low) = weights[frame]
            total = x_up * along_x(e, frame, 1) + x_low * along_x(e, frame, -1)
            total = total + (y_up * shifted(e, frame, 0, 1) + y_low * shifted(e, frame, 0, -1))
            total = total + (z_up * shifted(e, frame, 1, 1) + z_low * shifted(e, frame, 1, -1))
            fresh[frame] = start[frame] + total
        return fresh

    even = start
    odd = update(even)
    for turn in range(COARSE_SWEEPS - 1):
        even = update(odd)
        odd = update(even)
    return jnp.where(level.even, even[0, 0, 0], odd[0, 0, 0])


def small_cycle(mass, source, faces, row_step, lane_step, slot_step, between):
    if between == 0:
        return coarsest(mass, source, faces, row_step, lane_step, slot_step)
    level = Level(mass, source, faces, row_step, lane_step, slot_step)
    return level.cycle(
        lambda inner, inner_faces: small_cycle(
            8.0 * mass, inner, inner_faces, 2 * row_step, 2 * lane_step, level.coarse_slot_step(), between - 1
        )
    )


def coarse_kernel(
    owner_of, gathered, e2_in, s2_in, fx2_in, fxl2_in, fy2_in, fz2_in, fzl2_in, inv2_in,
    inputs, new_in, fx_more, fy_margin, fz_margin, fzl_margin, inv_more, fx_in, fy_in, fz_in, fzl_in, inv_in,
    new_out, known_out, fx_out, fy_out, fz_out, fzl_out, inv_out, within_in,
    solved_out, owned_out,
    e3, rows3, pair, e2, e1, cor, solved, owned, owner_here, fetch_sem, sems,
):
    fetch = pltpu.make_async_copy(owner_of, owner_here, fetch_sem)
    fetch.start()
    chips, _, quarter, lanes = gathered.shape
    blocks = 2 * chips
    half, height = 2 * quarter, 4 * quarter
    position, last = lax.axis_index("gx"), blocks - 1

    slot = lanes_of((quarter, lanes)) & 3
    spread = blocks // 4
    tiles = [gathered[chip, k] for chip in range(chips) for k in range(2)]
    items = []
    for k in range(4):
        packs = []
        for j in range(spread):
            value = tiles[j + (3 - k) % 4 * spread]
            for at in range(3):
                value = jnp.where(slot == at, tiles[j + (at - k) % 4 * spread], value)
            if k:
                value = jnp.where(slot < 4 - k, ahead(value, k, 1), behind(value, 4 - k, 1))
            packs.append(value[None])
        items.append(jnp.concatenate(packs, 0))
    third = Rows(64.0, items[0], items[1:], rows3)
    e3[...] = third.cycle(
        lambda inner, faces: small_cycle(512.0, inner, faces, 1, 8, third.coarse_slot_step(), 2)
    )

    fetch.wait()
    owner = owner_here[position]
    wide, narrow = lanes_of((lanes, lanes)), rows_of((lanes, lanes))
    take = jnp.where(narrow == 4 * wide + owner // spread, 1.0, 0.0)
    block = jnp.dot(
        e3[owner % spread], take, precision=lax.Precision.HIGHEST, preferred_element_type=jnp.float32
    )
    owned[0] = block[:, : lanes // 4]
    copies = [pltpu.make_async_copy(owned, owned_out, sems.at[0])]
    copies[0].start()

    first_of_two, even2 = parities2(half, lanes)
    body2 = pl.ds(PAD, half)
    edge = jnp.zeros((PAD, lanes), jnp.float32)
    core = core_of()
    s2, fx2, fxl2, fy2, fz2, fzl2, inv2 = [
        ref.at[pl.ds(core, 3)] for ref in (s2_in, fx2_in, fxl2_in, fy2_in, fz2_in, fzl2_in, inv2_in)
    ]
    next_chip = jnp.clip(position // 2 - 1 + 2 * core, 0, chips - 1)
    into_both_rows(pair.at[5], gathered[next_chip, 2])
    halo = pair[5]
    before = (
        by_side(halo, e2_in[0])[0], by_side(jnp.where(first_of_two, halo, e2_in[0]), e2_in[1])[0],
        by_side(e2_in[1], e2_in[2])[0],
        by_side(e2_in[2], jnp.where(first_of_two, e2_in[3], halo))[0], by_side(e2_in[3], halo)[0],
    )
    for k in range(5):
        j = jnp.clip(position + k - 2, 0, last)
        into_both_rows(pair.at[k], group(jnp.where(slot == j // spread, e3[j % spread], 0.0)))
        e2[k, :PAD] = edge
        e2[k, PAD + half:] = edge
        e2[k, body2] = before[k] + pair[k]

    def update2():
        sums = neigh2(e2, fx2, fxl2, fy2, fz2, fzl2, first_of_two, (0, 1, 2))
        return [(s2[j] + sums[j]) * inv2[j] for j in range(3)]

    fresh = update2()
    for j in range(3):
        e2[j + 1, body2] = fresh[j]
    fixes2 = [jnp.where(even2, even, odd) for even, odd in zip(fresh, update2())]

    _, source, _ = three_parts(inputs)
    layers = source.shape[0]
    plane = Plane(height, lanes)
    body1 = plane.body
    near_lane = (lanes_of((half, lanes)) & 1) == core
    swaps = [jnp.where(first_of_two, ahead(v, 1, 1), behind(v, 1, 1)) for v in fixes2]
    outer, inner = by_side(fixes2[0], fixes2[2])
    outer_swap, inner_swap = by_side(swaps[0], swaps[2])
    coarse = (
        jnp.where(near_lane, outer_swap, outer), jnp.where(near_lane, fixes2[1], swaps[1]),
        jnp.where(near_lane, swaps[1], fixes2[1]), jnp.where(near_lane, inner, inner_swap),
    )
    fixes = []
    for k in range(4):
        into_both_rows(cor.at[k], coarse[k])
        fixes.append(cor[k])
    for u in range(-1, layers + 1):
        before = new_out[u + 1] if u < 2 else new_in[u - 2]
        plane.put(e1.at[u + 1], before + fixes[(u + 2) // 2])

    def fx1(u):
        if u < 0:
            return fx_out[-1 - u]
        return fx_in[u] if u < layers - 1 else fx_more[u - layers + 1]

    def inv1(u):
        if u <= 0:
            return inv_out[u + 1]
        return inv_in[u - 1] if u < layers - 1 else inv_more[u - layers + 1]

    def around1(u):
        if u < 0:
            return in_layer(plane, fy_out, fz_out, fzl_out, e1.at[0])
        if u == layers:
            return in_layer(plane, fy_margin, fz_margin, fzl_margin, e1.at[u + 1])
        return in_layer(plane, fy_in.at[u], fz_in.at[u], fzl_in.at[u], e1.at[u + 1])

    def updated1(u):
        sums = around1(u) + (fx1(u) * e1[u + 2, body1] + fx1(u - 1) * e1[u, body1])
        return (source[own_layer(u, layers)] + sums) * inv1(u)

    for u in range(layers):
        e1[u + 1, body1] = jnp.where(plane.even(u), updated1(u), e1[u + 1, body1])
    e1[0, body1] = (known_out[...] + fx1(-2) * fixes[0] + (around1(-1) + fx1(-1) * e1[1, body1])) * inv1(-1)
    into_both_rows(cor.at[4], within_in[4])
    sums = cor[4] + fx1(layers) * fixes[3] + (around1(layers) + fx1(layers - 1) * e1[layers, body1])
    e1[layers + 1, body1] = sums * inv1(layers)
    for u in range(layers):
        solved[u] = jnp.where(plane.even(u), e1[u + 1, body1], updated1(u))
        copies.append(
            pltpu.make_async_copy(solved.at[u], solved_out.at[own_layer(u, layers)], sems.at[u + 1])
        )
        copies[-1].start()
    for copy in copies:
        copy.wait()


def f32(*shape):
    return jax.ShapeDtypeStruct(shape, jnp.float32)


def vmem(*shape):
    return pltpu.VMEM(shape, jnp.float32)


def call(kernel, outs, scratch, operands, out_space=pltpu.VMEM):
    def size(shape):
        count = 4
        for extent in shape:
            count *= extent
        return count

    sized = [array for array in (*scratch, *outs, *operands) if hasattr(array, "shape")]
    asked = 8 * 2**20 + sum(size(array.shape) for array in sized)
    return pl.pallas_call(
        kernel,
        out_shape=tuple(outs),
        in_specs=[pl.BlockSpec(memory_space=pltpu.VMEM)] * len(operands),
        out_specs=tuple([pl.BlockSpec(memory_space=out_space)] * len(outs)),
        scratch_shapes=scratch,
        compiler_params=pltpu.CompilerParams(vmem_limit_bytes=asked),
    )(*operands)


def on_device(iterate, source, phase_field, block_owner):
    layers, height, depth = iterate.shape
    half, quarter = height // 2, height // 4
    blocks = lax.axis_size("gx")
    padded, padded2 = height + 2 * PAD, half + 2 * PAD
    inputs = sum(
        jnp.pad(block, ((k * layers, (2 - k) * layers), (0, 0), (0, 0)))
        for k, block in enumerate((iterate, source, phase_field))
    )
    edge, = call(edge_kernel, [f32(3 * height + half, depth)], [], (inputs,))
    edge_in = within_chip(edge)
    layer, tile, tall = (height, depth), (half, depth), (padded, depth)
    cell, old, *fine, even = call(
        own_kernel,
        [
            f32(layers, *layer), f32(layers, *tall), f32(layers - 1, *layer), f32(layers, *tall),
            f32(layers, *layer), f32(layers, *layer), f32(2, *layer), f32(2, *tall),
        ],
        [], (block_owner, inputs),
    )
    message, own2, known1, new, *margin = call(
        chip_kernel,
        [
            f32(chip_rows(height)[1], depth), f32(2, *tile), f32(*layer), f32(3, *layer),
            f32(2, *layer), f32(*tall), f32(*layer), f32(*layer), f32(2, *layer),
        ],
        [vmem(*tall), vmem(2, *tall), vmem(3, *tall), vmem(10, *layer)],
        (inputs, cell, old, *fine, even, edge_in),
    )
    within, fx2, *border = call(
        border_kernel,
        [
            f32(9, *tile), f32(*tile), f32(3, *layer), f32(*layer), f32(2, *layer),
            f32(padded, depth), f32(*layer), f32(*layer), f32(2, *layer),
        ],
        [
            vmem(1, padded, depth), vmem(2, padded, depth), vmem(4, padded, depth), vmem(8, *layer),
            vmem(2, padded, depth), vmem(2, *layer), vmem(2, *layer),
        ],
        (inputs, message, own2, known1, new, *fine, between_chips(message)),
    )
    within_in = within_chip(within)
    plain = f32(4, *tile)
    slots, *middle = call(
        middle_down_kernel,
        [f32(blocks // 2, 3, quarter, depth), plain, plain, plain, plain, f32(4, padded2, depth)] + [plain] * 3,
        [vmem(6, padded2, depth), vmem(3, *tile)],
        (within, fx2, within_in),
    )
    kinds = [[2 * chip + (chip + core) % 2 for chip in range(blocks // 2)] for core in range(2)]
    gathered = lax.all_to_all(slots, "gx", 0, 0, axis_index_groups=kinds, tiled=True)
    solved, owned = call(
        coarse_kernel,
        [f32(layers, *layer), f32(1, quarter, depth // 4)],
        [
            vmem(blocks // 4, quarter, depth), vmem(4, blocks // 4, quarter + 2 * PAD, depth), vmem(7, *tile),
            vmem(5, padded2, depth), vmem(layers + 2, padded, depth), vmem(5, *layer), vmem(layers, *layer),
            vmem(1, quarter, depth // 4), pltpu.SMEM((blocks,), jnp.int32),
            pltpu.SemaphoreType.DMA, pltpu.SemaphoreType.DMA((layers + 1,)),
        ],
        (block_owner, gathered, *middle, inputs, new, *margin, *fine, *border, within_in),
        pl.ANY,
    )
    return solved, owned


def solution(mesh):
    split = P(("groups", "gx"), None, None)
    return jax.shard_map(
        on_device,
        mesh=mesh,
        in_specs=(split, split, split, P("groups")),
        out_specs=(split, split),
        check_vma=False,
    )
```

```python
import jax
import jax.numpy as jnp
from jax import lax
from jax.experimental import pallas as pl
from jax.experimental.pallas import tpu as pltpu
from jax.sharding import PartitionSpec as P

STIFFNESS = 100.0
EPSILON = 0.01
COARSE_SWEEPS = 4
PAD = 8


def between_chips(block):
    return lax.ppermute(block, "gx", [(i, i + 1 if i % 2 else i - 1) for i in range(1, lax.axis_size("gx") - 1)])


def within_chip(block):
    return lax.ppermute(block, "gx", [(i, i ^ 1) for i in range(lax.axis_size("gx"))])


def by_side(across, within):
    on_left = lax.axis_index("gx") % 2 == 0
    return jnp.where(on_left, across, within), jnp.where(on_left, within, across)


def lanes_of(shape):
    return lax.broadcasted_iota(jnp.int32, shape, len(shape) - 1)


def rows_of(shape):
    return lax.broadcasted_iota(jnp.int32, shape, len(shape) - 2)


def ahead(values, step, axis):
    return pltpu.roll(values, values.shape[axis] - step, axis)


def behind(values, step, axis):
    return pltpu.roll(values, step, axis)


def with_partner(values, step, axis):
    index = lax.broadcasted_iota(jnp.int32, values.shape, axis)
    partner = jnp.where((index & step) == 0, ahead(values, step, axis), behind(values, step, axis))
    return values + partner


def even_row_sum(scratch, rows):
    return scratch[pl.ds(0, rows, 2), :] + scratch[pl.ds(1, rows, 2), :]


def core_of():
    return lax.axis_index("gx") % 2


def own_layer(u, layers):
    return u + core_of() * (layers - 1 - 2 * u)


def three_parts(ref):
    third = ref.shape[0] // 3
    return [ref.at[pl.ds(k * third, third)] for k in range(3)]


def odd_cells(ref, rows, first):
    return jnp.where(first, ref[pl.ds(0, rows, 2), :], ref[pl.ds(1, rows, 2), :])


def into_both_rows(ref, values):
    rows = values.shape[0]
    ref[pl.ds(0, rows, 2), :] = values
    ref[pl.ds(1, rows, 2), :] = values


def cell_coef(value):
    return STIFFNESS * (value * value + EPSILON)


class Plane:
    def __init__(self, height, depth):
        self.height, self.half, self.depth = height, height // 2, depth
        self.row, self.lane = rows_of((height, depth)), lanes_of((height, depth))
        self.parity = self.row + self.lane + core_of()
        self.half_lane = lanes_of((self.half, depth))
        self.body = pl.ds(PAD, height)
        self.up, self.down = pl.ds(PAD + 1, height), pl.ds(PAD - 1, height)

    def even(self, u):
        return ((self.parity + u) & 1) == 0

    def odd_first(self, u):
        return ((self.half_lane + core_of() + u) & 1) != 0

    def put(self, ref, values):
        edge = jnp.zeros((PAD, self.depth), jnp.float32)
        ref[:PAD] = edge
        ref[PAD + self.height:] = edge
        ref[self.body] = values

    def face_y(self, here):
        return jnp.where(self.row < self.height - 1, 0.5 * (here + ahead(here, 1, 0)), 0.0)

    def face_z(self, here):
        return jnp.where(self.lane < self.depth - 1, 0.5 * (here + ahead(here, 1, 1)), 0.0)

    def packed(self, outer, inner, core):
        return jnp.where((self.half_lane & 1) == core, outer, inner)

    def both_rows(self, ref):
        return even_row_sum(ref, self.half)

    def summed(self, values, ref):
        ref[...] = values
        return with_partner(self.both_rows(ref), 1, 1)

    def odd_rows(self, values, ref):
        ref[...] = values
        return with_partner(ref[pl.ds(1, self.half, 2), :], 1, 1)

    def odd_lanes(self, values, ref):
        ref[...] = values
        sums = self.both_rows(ref)
        return jnp.where((self.half_lane & 1) == 0, ahead(sums, 1, 1), sums)


def in_layer(plane, fy, fz, fzl, padded):
    here = padded[plane.body]
    total = fy[plane.body] * padded[plane.up] + fy[plane.down] * padded[plane.down]
    return total + (fz[...] * ahead(here, 1, 1) + fzl[...] * behind(here, 1, 1))


def edge_kernel(inputs, out):
    iterate, source, phase = three_parts(inputs)
    layers, height, depth = iterate.shape
    plane = Plane(height, depth)
    near, inner, far = [own_layer(u, layers) for u in (layers - 1, layers - 2, layers - 3)]
    coef_near, coef_inner, coef_far = [cell_coef(phase[k]) for k in (near, inner, far)]

    def around(here, e):
        fy, fz = plane.face_y(here), plane.face_z(here)
        fyl, fzl = behind(fy, 1, 0), behind(fz, 1, 1)
        total = fy * ahead(e, 1, 0) + fyl * behind(e, 1, 0)
        return total + fz * ahead(e, 1, 1) + fzl * behind(e, 1, 1), fy + fyl + fz + fzl

    face_near, face_far = 0.5 * (coef_inner + coef_near), 0.5 * (coef_inner + coef_far)
    total, weight = around(coef_inner, iterate[inner])
    total = total + face_near * iterate[near] + face_far * iterate[far]
    updated = (source[inner] + total) / (1.0 + (face_near + face_far + weight))
    total, _ = around(coef_near, iterate[near])
    known = jnp.where(plane.even(layers - 1), total + face_near * iterate[inner], face_near * updated)
    out[:height] = coef_near
    out[height:2 * height] = coef_inner
    out[2 * height:3 * height] = source[near] + known
    out[3 * height:] = odd_cells(iterate.at[near], plane.half, plane.odd_first(layers - 1))


def chip_rows(height):
    half, at, places = height // 2, 0, {}
    for name, size in (
        ("coef0", height), ("coef1", height), ("known0", height), ("old0", half), ("moved1", half), ("face2", half),
        ("source2", half), ("fx2", half), ("far2", half),
    ):
        places[name] = pl.ds(at, size)
        at += size
    return places, at


def own_kernel(owner_of, inputs, cell, old, fx, fy, fz, fzl, inv, even):
    iterate, source, phase = three_parts(inputs)
    layers, height, depth = iterate.shape
    plane = Plane(height, depth)
    body = plane.body
    for u in range(layers):
        cell[u] = cell_coef(phase[own_layer(u, layers)])
        plane.put(old.at[u], iterate[own_layer(u, layers)])
    for u in range(layers):
        here = cell[u]
        if u < layers - 1:
            fx[u] = 0.5 * (here + cell[u + 1])
        plane.put(fy.at[u], plane.face_y(here))
        face = plane.face_z(here)
        fz[u] = face
        fzl[u] = behind(face, 1, 1)
    for u in (1, 2):
        weight = (fx[u] + fx[u - 1]) + (fy[u, body] + fy[u, plane.down]) + (fz[u] + fzl[u])
        inverse = 1.0 / (1.0 + weight)
        inv[u - 1] = inverse
        around = in_layer(plane, fy.at[u], fz.at[u], fzl.at[u], old.at[u])
        total = source[own_layer(u, layers)] + around + (fx[u] * old[u + 1, body] + fx[u - 1] * old[u - 1, body])
        plane.put(even.at[u - 1], total * inverse)


def chip_kernel(
    inputs, cell, old_own, fx_own, fy_own, fz_own, fzl_own, inv_own, even_own, within_in,
    message, own2, known1, new, fx_more, fy_margin, fz_margin, fzl_margin, inv_more,
    old_margin, even_more, change, turn,
):
    iterate, source, phase = three_parts(inputs)
    layers, height, depth = iterate.shape
    plane = Plane(height, depth)
    body, half = plane.body, plane.half
    places, _ = chip_rows(height)
    margin = layers

    def part(k):
        return within_in[k * height:(k + 1) * height]

    def s(u):
        return source[own_layer(u, layers)]

    into_both_rows(turn.at[0], within_in[3 * height:])
    plane.put(old_margin, turn[0])
    fx_more[0] = 0.5 * (cell[layers - 1] + part(0))
    fx_more[1] = 0.5 * (part(0) + part(1))
    plane.put(fy_margin, plane.face_y(part(0)))
    face = plane.face_z(part(0))
    fz_margin[...] = face
    fzl_margin[...] = behind(face, 1, 1)
    fx = [fx_own.at[u] for u in range(3)] + [fx_more.at[0], fx_more.at[1]]
    fy = [fy_own.at[u] for u in range(layers)] + [fy_margin]
    fz = [fz_own.at[u] for u in range(layers)] + [fz_margin]
    fzl = [fzl_own.at[u] for u in range(layers)] + [fzl_margin]
    old = [old_own.at[u] for u in range(layers)] + [old_margin]
    inv = [None, inv_own.at[0], inv_own.at[1], inv_more.at[0], inv_more.at[1]]
    even = [None, even_own.at[0], even_own.at[1], even_more.at[0], even_more.at[1]]
    for u in (margin - 1, margin):
        weight = (fx[u][...] + fx[u - 1][...]) + (fy[u][body] + fy[u][plane.down]) + (fz[u][...] + fzl[u][...])
        inv[u][...] = 1.0 / (1.0 + weight)

    def around(ref, u):
        return in_layer(plane, fy[u], fz[u], fzl[u], ref[u])

    u = margin - 1
    total = s(u) + around(old, u) + (fx[u][...] * old[u + 1][body] + fx[u - 1][...] * old[u - 1][body])
    plane.put(even[u], total * inv[u][...])
    plane.put(even[margin], (part(2) + fx[u][...] * old[u][body]) * inv[margin][...])
    for u in range(2, margin + 1):
        if u < margin:
            total = s(u) + around(even, u) + (fx[u][...] * even[u + 1][body] + fx[u - 1][...] * even[u - 1][body])
        else:
            total = part(2) + around(even, u) + fx[u - 1][...] * even[u - 1][body]
        fresh = total * inv[u][...]
        new[u - 2] = fresh
        plane.put(change.at[u - 2], fresh - old[u][body])
    change = {u: change.at[u - 2] for u in range(2, margin + 1)}

    one = fx[1][...] * change[2][body]
    two = around(change, 2) + fx[2][...] * change[3][body]
    three = around(change, 3) + (fx[2][...] * change[2][body] + fx[3][...] * change[4][body])
    outer = jnp.where(plane.even(1), one, 0.0)
    inner = jnp.where(plane.even(2), two, 0.0) + jnp.where(plane.even(3), three, 0.0)
    core = core_of()

    def tile(name, outer, inner):
        message[places[name], :] = plane.packed(outer, inner, core)

    tile("source2", plane.summed(outer, turn.at[1]), plane.summed(inner, turn.at[2]))
    tile("fx2", plane.summed(fx[1][...], turn.at[3]), plane.summed(fx[3][...], turn.at[4]))
    fy2 = [plane.odd_rows(fy[u][body] + fy[u + 1][body], turn.at[5 + u // 2]) for u in (0, 2)]
    fz2 = [plane.odd_lanes(fz[u][...] + fz[u + 1][...], turn.at[7 + u // 2]) for u in (0, 2)]
    own2[0], own2[1] = plane.packed(*fy2, core), plane.packed(*fz2, core)
    tile("far2", fy2[1], fz2[1])
    for u in range(2):
        message[places["coef%d" % u], :] = cell[u]
    first = s(0) + around(old, 0) + fx[0][...] * old[1][body]
    second = s(0) + fx[0][...] * even[1][body]
    message[places["known0"], :] = jnp.where(plane.even(0), first, second)
    message[places["old0"], :] = odd_cells(iterate.at[own_layer(0, layers)], half, plane.odd_first(0))
    total = s(1) + around(even, 1) + fx[1][...] * even[2][body]
    known1[...] = total
    turn[9] = total * inv[1][...] - old[1][body]
    message[places["moved1"], :] = odd_cells(turn.at[9], half, plane.odd_first(1))
    message[places["face2"], :] = odd_cells(fx[1], half, plane.odd_first(1))


def border_kernel(
    inputs, message, own2, known1, new_in, fx_in, fy_in, fz_in, fzl_in, inv_in, across_in,
    within, fx2_in, new, known, fx, fy, fz, fzl, inv,
    old, even, change, turn, face_y, face_z, face_zl,
):
    iterate, source, _ = three_parts(inputs)
    layers, height, depth = iterate.shape
    plane = Plane(height, depth)
    body, half = plane.body, plane.half
    places, _ = chip_rows(height)
    core, last = core_of(), lax.axis_size("gx") - 1
    position = lax.axis_index("gx")

    def mine(name):
        return message[places[name], :]

    def theirs(name):
        return across_in[places[name], :]

    def opened(name, k):
        into_both_rows(turn.at[k], theirs(name))
        return turn[k]

    for k in range(2):
        here = theirs("coef%d" % k)
        plane.put(face_y.at[k], plane.face_y(here))
        face = plane.face_z(here)
        face_z[k] = face
        face_zl[k] = behind(face, 1, 1)
    fy[...], fz[...], fzl[...] = face_y[0], face_z[0], face_zl[0]
    there = position - 1 + 2 * core
    border = jnp.where((there >= 0) & (there <= last), 0.5 * (mine("coef0") + theirs("coef0")), 0.0)
    face1 = 0.5 * (theirs("coef0") + theirs("coef1"))
    face2 = opened("face2", 2)
    fx[0], fx[1] = border, face1

    def inverse(faces, fy, fz, fzl):
        weight = faces + (fy[body] + fy[plane.down]) + (fz[...] + fzl[...])
        return 1.0 / (1.0 + weight)

    inv_own = inverse(fx_in[0] + border, fy_in.at[0], fz_in.at[0], fzl_in.at[0])
    inv_near = inverse(border + face1, face_y.at[0], face_z.at[0], face_zl.at[0])
    inv_far = inverse(face1 + face2, face_y.at[1], face_z.at[1], face_zl.at[1])
    inv[0], inv[1] = inv_near, inv_own
    old_own, old_next = iterate[own_layer(0, layers)], iterate[own_layer(1, layers)]
    old_near, far = opened("old0", 0), opened("moved1", 1)
    even_own = (mine("known0") + border * old_near) * inv_own
    even_near = (theirs("known0") + border * old_own) * inv_near
    plane.put(even.at[0], even_near)
    plane.put(even.at[1], even_own)

    def near(ref, k):
        return in_layer(plane, face_y.at[k], face_z.at[k], face_zl.at[k], ref)

    def own(ref, u):
        return in_layer(plane, fy_in.at[u], fz_in.at[u], fzl_in.at[u], ref)

    odd_own = (mine("known0") + own(even.at[1], 0) + border * even_near) * inv_own
    odd_near = (theirs("known0") + near(even.at[0], 0) + border * even_own) * inv_near
    odd_next = (known1[...] + fx_in[0] * even_own) * inv_in[0]
    far = far + face1 * even_near * inv_far
    new[0], new[1], new[2] = odd_near, odd_own, odd_next
    near_by, here, following = odd_near - old_near, odd_own - old_own, odd_next - old_next
    for k, values in enumerate((far, near_by, here, following)):
        plane.put(change.at[k], values)
    plane.put(old.at[0], old_near)
    known[...] = theirs("known0") + face1 * far - near(old.at[0], 0)

    def residual(u, values):
        return jnp.where(plane.even(u), values, 0.0)

    own_outer = residual(1, own(change.at[3], 1) + fx_in[0] * here)
    own_outer = own_outer + residual(0, own(change.at[2], 0) + (fx_in[0] * following + border * near_by))
    own_inner = residual(2, fx_in[1] * following)
    its_outer = residual(-1, near(change.at[1], 0) + (face1 * far + border * here))
    its_outer = its_outer + residual(-2, near(change.at[0], 1) + face1 * near_by)
    its_inner = residual(-3, face2 * far)
    sums = [plane.summed(values, turn.at[3 + k]) for k, values in enumerate((own_outer, own_inner, its_outer, its_inner))]
    within[0] = mine("source2") + plane.packed(sums[0], sums[1], core)
    within[5] = theirs("source2") + plane.packed(sums[2], sums[3], 1 - core)
    within[6] = theirs("fx2")
    far2 = theirs("far2")
    far2_swap = jnp.where((plane.half_lane & 1) == 0, ahead(far2, 1, 1), behind(far2, 1, 1))
    near_fy2 = plane.odd_rows(face_y[0, body] + face_y[1, body], turn.at[1])
    near_fz2 = plane.odd_lanes(face_z[0] + face_z[1], turn.at[2])
    within[7] = plane.packed(near_fy2, far2_swap, 1 - core)
    within[8] = plane.packed(near_fz2, far2, 1 - core)
    fx2_in[...] = mine("fx2")
    middle = jnp.where((plane.half_lane & 1) == 0, ahead(mine("fx2"), 1, 1), behind(mine("fx2"), 1, 1))
    within[1] = plane.packed(plane.summed(border, turn.at[7]), middle, core)
    within[2], within[3] = own2[0], own2[1]
    turn[0] = source[own_layer(layers - 1, layers)] + fx_in[layers - 2] * new_in[layers - 4]
    within[4] = odd_cells(turn.at[0], half, jnp.logical_not(plane.odd_first(layers - 1)))


def neigh2(e2, fx2, fxl2, fy2, fz2, fzl2, first_of_two, tiles):
    half = fx2.shape[1]
    body, up, down = pl.ds(PAD, half), pl.ds(PAD + 1, half), pl.ds(PAD - 1, half)
    needed = range(tiles[0], tiles[-1] + 3)
    here = {j: e2[j, body] for j in needed}
    after = {j: ahead(here[j], 1, 1) for j in needed}
    before = {j: behind(here[j], 1, 1) for j in needed}
    found = []
    for j in tiles:
        k = j + 1
        upper = jnp.where(first_of_two, after[k], before[k + 1])
        lower = jnp.where(first_of_two, after[k - 1], before[k])
        sums = fx2[j] * upper + fxl2[j] * lower
        sums = sums + fy2[j, body] * e2[k, up] + fy2[j, down] * e2[k, down]
        sums = sums + fz2[j] * ahead(here[k], 2, 1) + fzl2[j] * behind(here[k], 2, 1)
        found.append(sums)
    return found


def parities2(half, lanes):
    row, lane = rows_of((half, lanes)), lanes_of((half, lanes))
    return (lane & 1) == 0, ((row + (lane & 1) + (lane >> 1)) & 1) == 0


def group(values):
    return with_partner(with_partner(values, 1, 1), 2, 1)


def packed_odd(values, pair):
    half, lanes = values.shape
    lane = lanes_of((half // 2, lanes))
    pair[...] = values
    return odd_cells(pair, half // 2, (((lane & 1) + (lane >> 1)) & 1) != 0)


def middle_down_kernel(
    own, fx2_in, within_in,
    slots, e2_out, s2, fx2, fxl2, fy2, fz2, fzl2, inv2,
    e2, pair,
):
    _, half, lanes = own.shape
    quarter = half // 2
    first_of_two, even2 = parities2(half, lanes)
    body, down = pl.ds(PAD, half), pl.ds(PAD - 1, half)
    edge = jnp.zeros((PAD, lanes), jnp.float32)
    for j in (0, 5):
        e2[j] = jnp.zeros((half + 2 * PAD, lanes), jnp.float32)

    def pair_of(k):
        return by_side(own[k], within_in[k])

    def four(k):
        (left, right), (far_left, far_right) = pair_of(k), pair_of(5 + k)
        return far_left, left, right, far_right

    for j, (source, fy, fz) in enumerate(zip(four(0), four(2), four(3))):
        s2[j] = source
        fy2[j, :PAD] = edge
        fy2[j, body] = fy
        fy2[j, PAD + half:] = edge
        fz2[j] = fz
        fzl2[j] = behind(fz, 2, 1)

    def between(left, right):
        return jnp.where(first_of_two, ahead(left, 1, 1), behind(right, 1, 1))

    fxl0, fxl1, fxr2, fxr3 = four(1)
    inner = fx2_in[...]
    fxr1, _ = by_side(inner, between(fxl1, inner))
    fxl2_, _ = by_side(between(inner, fxr2), inner)
    for j, (face, low) in enumerate(
        ((between(fxl0, fxl1), fxl0), (fxr1, fxl1), (fxr2, fxl2_), (fxr3, between(fxr2, fxr3)))
    ):
        fx2[j], fxl2[j] = face, low
        weight = face + low + fy2[j, body] + fy2[j, down] + fz2[j] + fzl2[j]
        inverse = 1.0 / (8.0 + weight)
        inv2[j] = inverse
        e2[j + 1, :PAD] = edge
        e2[j + 1, PAD + half:] = edge
        e2[j + 1, body] = s2[j] * inverse

    def neigh(tiles):
        return neigh2(e2, fx2, fxl2, fy2, fz2, fzl2, first_of_two, tiles)

    fresh = [(s2[j] + sums) * inv2[j] for j, sums in enumerate(neigh((0, 1, 2, 3)))]
    for j in range(4):
        e2[j + 1, body] = fresh[j]
        e2_out[j] = fresh[j]
    lane = lanes_of((quarter, lanes))
    odd_layer, odd_depth = (lane & 1) != 0, (lane & 2) != 0
    chips = slots.shape[0]
    for k, sums in enumerate(neigh((1, 2))):
        j = k + 1
        pair[k] = jnp.where(even2, sums, 0.0)
        item = (lane - (lax.axis_index("gx") // 2 * 2 + k) // (chips // 2)) & 3
        source = group(even_row_sum(pair.at[k], quarter))
        fx = group(jnp.where(odd_layer, even_row_sum(fx2.at[j], quarter), 0.0))
        fxl = group(jnp.where(odd_layer, 0.0, even_row_sum(fxl2.at[j], quarter)))
        fy = group(fy2[j, pl.ds(PAD + 1, quarter, 2), :])
        fz = group(jnp.where(odd_depth, even_row_sum(fz2.at[j], quarter), 0.0))
        weight = (fx + fxl) + (fy + behind(fy, 1, 0)) + (fz + behind(fz, 4, 1))
        start = source / (64.0 + weight)
        tile = jnp.where(item == 0, start, jnp.where(item == 1, fx, jnp.where(item == 2, fy, fz)))
        for c in range(chips):
            slots[c, k] = tile
    halo = packed_odd(jnp.where(first_of_two, fresh[2], fresh[1]), pair.at[2])
    for c in range(chips):
        slots[c, 2] = halo


def joined(one, two):
    return jnp.concatenate([part for part in (one, two) if part.shape[0]], 0)


class Level:
    def __init__(self, mass, source, faces, row_step, lane_step, slot_step):
        self.source, self.row_step, self.lane_step, self.slot_step = source, row_step, lane_step, slot_step
        self.fx, self.fy, self.fz = faces
        self.tiles = source.shape[0]
        shape = source.shape
        self.lane = lanes_of(shape)
        layer = lax.broadcasted_iota(jnp.int32, shape, 0) if self.tiles > 1 else self.lane // slot_step
        self.even = ((layer + rows_of(shape) // row_step + self.lane // lane_step) & 1) == 0
        self.fxl = self.lower(self.fx)
        self.fyl = self.row_shifts(self.fy)[1]
        self.fzl = behind(self.fz, lane_step, 2)
        weight = (self.fx + self.fxl) + (self.fy + self.fyl) + (self.fz + self.fzl)
        self.inv = 1.0 / (mass + weight)

    def upper(self, e):
        return joined(e[1:], ahead(e[:1], self.slot_step, 2))

    def lower(self, e):
        return joined(behind(e[-1:], self.slot_step, 2), e[:-1])

    def row_shifts(self, e):
        return ahead(e, self.row_step, 1), behind(e, self.row_step, 1)

    def neigh(self, e):
        above, below = self.row_shifts(e)
        total = (self.fx * self.upper(e) + self.fxl * self.lower(e)) + (self.fy * above + self.fyl * below)
        return total + (self.fz * ahead(e, self.lane_step, 2) + self.fzl * behind(e, self.lane_step, 2))

    def start(self):
        return self.source * self.inv

    def update(self, e):
        return self.start() + self.neigh(e) * self.inv

    def cycle(self, deeper):
        odd = self.update(self.start())
        residual = jnp.where(self.even, self.neigh(odd), 0.0)
        fix = deeper(self.restricted(residual), self.coarse_faces())
        even = self.update(odd + self.prolonged(fix))
        return jnp.where(self.even, even, self.update(even))

    def coarse_slot_step(self):
        return self.slot_step if self.tiles > 1 else 2 * self.slot_step

    def pairs(self, values):
        if self.tiles == 1:
            return with_partner(values, self.slot_step, 2)
        halves = values.reshape(self.tiles // 2, 2, *values.shape[1:])
        return halves[:, 0] + halves[:, 1]

    def odd_layers(self, values):
        if self.tiles == 1:
            return with_partner(jnp.where((self.lane & self.slot_step) != 0, values, 0.0), self.slot_step, 2)
        return values.reshape(self.tiles // 2, 2, *values.shape[1:])[:, 1]

    def row_pairs(self, values):
        return with_partner(values, self.row_step, 1)

    def odd_rows(self, values):
        odd = (rows_of(values.shape) & self.row_step) != 0
        return with_partner(jnp.where(odd, values, 0.0), self.row_step, 1)

    def restricted(self, values):
        return with_partner(self.row_pairs(self.pairs(values)), self.lane_step, 2)

    def coarse_faces(self):
        fx = with_partner(self.row_pairs(self.odd_layers(self.fx)), self.lane_step, 2)
        fy = with_partner(self.odd_rows(self.pairs(self.fy)), self.lane_step, 2)
        return fx, fy, self.restricted(jnp.where((self.lane & self.lane_step) != 0, self.fz, 0.0))

    def prolonged(self, fix):
        if self.tiles == 1:
            return fix
        both = jnp.concatenate([fix[:, None], fix[:, None]], 1)
        return both.reshape(self.tiles, *fix.shape[1:])


class Rows(Level):
    def __init__(self, mass, source, faces, scratch):
        self.scratch, self.used = scratch, 0
        self.rows = source.shape[1]
        super().__init__(mass, source, faces, 1, 4, 1)

    def start(self):
        return self.source

    def place(self):
        self.used += 1
        return self.scratch.at[self.used % self.scratch.shape[0]]

    def row_shifts(self, e):
        place = self.place()
        edge = jnp.zeros((e.shape[0], PAD, e.shape[2]), jnp.float32)
        place[:, :PAD] = edge
        place[:, PAD + self.rows:] = edge
        place[:, pl.ds(PAD, self.rows)] = e
        return place[:, pl.ds(PAD + 1, self.rows)], place[:, pl.ds(PAD - 1, self.rows)]

    def every_other(self, values, starts):
        place, tiles = self.place(), values.shape[0]
        place[:tiles, : self.rows] = values
        found = 0.0
        for start in starts:
            found = found + jnp.concatenate(
                [place[j, pl.ds(start, self.rows // 2, 2), :][None] for j in range(tiles)], 0
            )
        return found

    def row_pairs(self, values):
        return self.every_other(values, (0, 1))

    def odd_rows(self, values):
        return self.every_other(values, (1,))

    def prolonged(self, fix):
        place, tiles = self.place(), fix.shape[0]
        for j in range(tiles):
            into_both_rows(place.at[j, pl.ds(0, self.rows)], fix[j])
        return super().prolonged(place[:tiles, : self.rows])


def coarsest(mass, source, faces, *steps):
    row_step, lane_step, slot_step = steps
    level = Level(mass, source, faces, *steps)
    counts = source.shape[1] // row_step, source.shape[2] // lane_step, 4 // slot_step
    frames = [(m, k, q) for m in range(counts[0]) for k in range(counts[1]) for q in range(counts[2])]
    place = level.lane & 3

    def spread(values):
        copies = {}
        for m, k, q in frames:
            if k:
                copies[m, k, q] = behind(copies[m, 0, q], k * lane_step, 2)
            elif q:
                by = q * slot_step
                one, two = behind(copies[m, 0, 0], by, 2), ahead(copies[m, 0, 0], 4 - by, 2)
                copies[m, k, q] = jnp.where(place >= by, one, two)
            else:
                copies[m, k, q] = behind(values, m * row_step, 1) if m else values
        return copies

    start, inv, fx, fy, fz = [spread(values) for values in (source * level.inv, level.inv, level.fx, level.fy, level.fz)]

    def shifted(copies, frame, axis, by):
        moved = list(frame)
        moved[axis] = (frame[axis] - by) % counts[axis]
        return copies[tuple(moved)]

    def along_x(copies, frame, by):
        here, wrapped = copies[frame], shifted(copies, frame, 2, by)
        return joined(here[1:], wrapped[:1]) if by > 0 else joined(wrapped[-1:], here[:-1])

    weights = {}
    for frame in frames:
        pairs = [
            (fx[frame], along_x(fx, frame, -1)),
            (fy[frame], shifted(fy, frame, 0, -1)),
            (fz[frame], shifted(fz, frame, 1, -1)),
        ]
        weights[frame] = [(up * inv[frame], low * inv[frame]) for up, low in pairs]

    def update(e):
        fresh = {}
        for frame in frames:
            (x_up, x_low), (y_up, y_low), (z_up, z_low) = weights[frame]
            total = x_up * along_x(e, frame, 1) + x_low * along_x(e, frame, -1)
            total = total + (y_up * shifted(e, frame, 0, 1) + y_low * shifted(e, frame, 0, -1))
            total = total + (z_up * shifted(e, frame, 1, 1) + z_low * shifted(e, frame, 1, -1))
            fresh[frame] = start[frame] + total
        return fresh

    even = start
    odd = update(even)
    for turn in range(COARSE_SWEEPS - 1):
        even = update(odd)
        odd = update(even)
    return jnp.where(level.even, even[0, 0, 0], odd[0, 0, 0])


def small_cycle(mass, source, faces, row_step, lane_step, slot_step, between):
    if between == 0:
        return coarsest(mass, source, faces, row_step, lane_step, slot_step)
    level = Level(mass, source, faces, row_step, lane_step, slot_step)
    return level.cycle(
        lambda inner, inner_faces: small_cycle(
            8.0 * mass, inner, inner_faces, 2 * row_step, 2 * lane_step, level.coarse_slot_step(), between - 1
        )
    )


def coarse_kernel(
    owner_of, gathered, e2_in, s2_in, fx2_in, fxl2_in, fy2_in, fz2_in, fzl2_in, inv2_in,
    inputs, new_in, fx_more, fy_margin, fz_margin, fzl_margin, inv_more, fx_in, fy_in, fz_in, fzl_in, inv_in,
    new_out, known_out, fx_out, fy_out, fz_out, fzl_out, inv_out, within_in,
    solved_out, owned_out,
    e3, rows3, pair, e2, e1, cor, solved, owned, owner_here, fetch_sem, sems,
):
    fetch = pltpu.make_async_copy(owner_of, owner_here, fetch_sem)
    fetch.start()
    chips, _, quarter, lanes = gathered.shape
    blocks = 2 * chips
    half, height = 2 * quarter, 4 * quarter
    position, last = lax.axis_index("gx"), blocks - 1

    slot = lanes_of((quarter, lanes)) & 3
    spread = blocks // 4
    tiles = [gathered[chip, k] for chip in reversed(range(chips)) for k in range(2)]
    items = []
    for k in range(4):
        packs = []
        for j in range(spread):
            value = tiles[j + (3 - k) % 4 * spread]
            for at in range(3):
                value = jnp.where(slot == at, tiles[j + (at - k) % 4 * spread], value)
            if k:
                value = jnp.where(slot < 4 - k, ahead(value, k, 1), behind(value, 4 - k, 1))
            packs.append(value[None])
        items.append(jnp.concatenate(packs, 0))
    third = Rows(64.0, items[0], items[1:], rows3)
    e3[...] = third.cycle(
        lambda inner, faces: small_cycle(512.0, inner, faces, 1, 8, third.coarse_slot_step(), 2)
    )

    fetch.wait()
    owner = owner_here[position]
    wide, narrow = lanes_of((lanes, lanes)), rows_of((lanes, lanes))
    take = jnp.where(narrow == 4 * wide + owner // spread, 1.0, 0.0)
    block = jnp.dot(
        e3[owner % spread], take, precision=lax.Precision.HIGHEST, preferred_element_type=jnp.float32
    )
    owned[0] = block[:, : lanes // 4]
    copies = [pltpu.make_async_copy(owned, owned_out, sems.at[0])]
    copies[0].start()

    first_of_two, even2 = parities2(half, lanes)
    body2 = pl.ds(PAD, half)
    edge = jnp.zeros((PAD, lanes), jnp.float32)
    core = core_of()
    s2, fx2, fxl2, fy2, fz2, fzl2, inv2 = [
        ref.at[pl.ds(core, 3)] for ref in (s2_in, fx2_in, fxl2_in, fy2_in, fz2_in, fzl2_in, inv2_in)
    ]
    next_chip = jnp.clip(position // 2 - 1 + 2 * core, 0, chips - 1)
    into_both_rows(pair.at[5], gathered[chips - 1 - next_chip, 2])
    halo = pair[5]
    before = (
        by_side(halo, e2_in[0])[0], by_side(jnp.where(first_of_two, halo, e2_in[0]), e2_in[1])[0],
        by_side(e2_in[1], e2_in[2])[0],
        by_side(e2_in[2], jnp.where(first_of_two, e2_in[3], halo))[0], by_side(e2_in[3], halo)[0],
    )
    for k in range(5):
        j = jnp.clip(position + k - 2, 0, last)
        into_both_rows(pair.at[k], group(jnp.where(slot == j // spread, e3[j % spread], 0.0)))
        e2[k, :PAD] = edge
        e2[k, PAD + half:] = edge
        e2[k, body2] = before[k] + pair[k]

    def update2():
        sums = neigh2(e2, fx2, fxl2, fy2, fz2, fzl2, first_of_two, (0, 1, 2))
        return [(s2[j] + sums[j]) * inv2[j] for j in range(3)]

    fresh = update2()
    for j in range(3):
        e2[j + 1, body2] = fresh[j]
    fixes2 = [jnp.where(even2, even, odd) for even, odd in zip(fresh, update2())]

    _, source, _ = three_parts(inputs)
    layers = source.shape[0]
    plane = Plane(height, lanes)
    body1 = plane.body
    near_lane = (lanes_of((half, lanes)) & 1) == core
    swaps = [jnp.where(first_of_two, ahead(v, 1, 1), behind(v, 1, 1)) for v in fixes2]
    outer, inner = by_side(fixes2[0], fixes2[2])
    outer_swap, inner_swap = by_side(swaps[0], swaps[2])
    coarse = (
        jnp.where(near_lane, outer_swap, outer), jnp.where(near_lane, fixes2[1], swaps[1]),
        jnp.where(near_lane, swaps[1], fixes2[1]), jnp.where(near_lane, inner, inner_swap),
    )
    fixes = []
    for k in range(4):
        into_both_rows(cor.at[k], coarse[k])
        fixes.append(cor[k])
    for u in range(-1, layers + 1):
        before = new_out[u + 1] if u < 2 else new_in[u - 2]
        plane.put(e1.at[u + 1], before + fixes[(u + 2) // 2])

    def fx1(u):
        if u < 0:
            return fx_out[-1 - u]
        return fx_in[u] if u < layers - 1 else fx_more[u - layers + 1]

    def inv1(u):
        if u <= 0:
            return inv_out[u + 1]
        return inv_in[u - 1] if u < layers - 1 else inv_more[u - layers + 1]

    def around1(u):
        if u < 0:
            return in_layer(plane, fy_out, fz_out, fzl_out, e1.at[0])
        if u == layers:
            return in_layer(plane, fy_margin, fz_margin, fzl_margin, e1.at[u + 1])
        return in_layer(plane, fy_in.at[u], fz_in.at[u], fzl_in.at[u], e1.at[u + 1])

    def updated1(u):
        sums = around1(u) + (fx1(u) * e1[u + 2, body1] + fx1(u - 1) * e1[u, body1])
        return (source[own_layer(u, layers)] + sums) * inv1(u)

    for u in range(layers):
        e1[u + 1, body1] = jnp.where(plane.even(u), updated1(u), e1[u + 1, body1])
    e1[0, body1] = (known_out[...] + fx1(-2) * fixes[0] + (around1(-1) + fx1(-1) * e1[1, body1])) * inv1(-1)
    into_both_rows(cor.at[4], within_in[4])
    sums = cor[4] + fx1(layers) * fixes[3] + (around1(layers) + fx1(layers - 1) * e1[layers, body1])
    e1[layers + 1, body1] = sums * inv1(layers)
    for u in range(layers):
        solved[u] = jnp.where(plane.even(u), e1[u + 1, body1], updated1(u))
        copies.append(
            pltpu.make_async_copy(solved.at[u], solved_out.at[own_layer(u, layers)], sems.at[u + 1])
        )
        copies[-1].start()
    for copy in copies:
        copy.wait()


def f32(*shape):
    return jax.ShapeDtypeStruct(shape, jnp.float32)


def vmem(*shape):
    return pltpu.VMEM(shape, jnp.float32)


def call(kernel, outs, scratch, operands, out_space=pltpu.VMEM):
    def size(shape):
        count = 4
        for extent in shape:
            count *= extent
        return count

    sized = [array for array in (*scratch, *outs, *operands) if hasattr(array, "shape")]
    asked = 8 * 2**20 + sum(size(array.shape) for array in sized)
    return pl.pallas_call(
        kernel,
        out_shape=tuple(outs),
        in_specs=[pl.BlockSpec(memory_space=pltpu.VMEM)] * len(operands),
        out_specs=tuple([pl.BlockSpec(memory_space=out_space)] * len(outs)),
        scratch_shapes=scratch,
        compiler_params=pltpu.CompilerParams(vmem_limit_bytes=asked),
    )(*operands)


def on_device(iterate, source, phase_field, block_owner):
    layers, height, depth = iterate.shape
    half, quarter = height // 2, height // 4
    blocks = lax.axis_size("gx")
    padded, padded2 = height + 2 * PAD, half + 2 * PAD
    inputs = sum(
        jnp.pad(block, ((k * layers, (2 - k) * layers), (0, 0), (0, 0)))
        for k, block in enumerate((iterate, source, phase_field))
    )
    edge, = call(edge_kernel, [f32(3 * height + half, depth)], [], (inputs,))
    edge_in = within_chip(edge)
    layer, tile, tall = (height, depth), (half, depth), (padded, depth)
    cell, old, *fine, even = call(
        own_kernel,
        [
            f32(layers, *layer), f32(layers, *tall), f32(layers - 1, *layer), f32(layers, *tall),
            f32(layers, *layer), f32(layers, *layer), f32(2, *layer), f32(2, *tall),
        ],
        [], (block_owner, inputs),
    )
    message, own2, known1, new, *margin = call(
        chip_kernel,
        [
            f32(chip_rows(height)[1], depth), f32(2, *tile), f32(*layer), f32(3, *layer),
            f32(2, *layer), f32(*tall), f32(*layer), f32(*layer), f32(2, *layer),
        ],
        [vmem(*tall), vmem(2, *tall), vmem(3, *tall), vmem(10, *layer)],
        (inputs, cell, old, *fine, even, edge_in),
    )
    within, fx2, *border = call(
        border_kernel,
        [
            f32(9, *tile), f32(*tile), f32(3, *layer), f32(*layer), f32(2, *layer),
            f32(padded, depth), f32(*layer), f32(*layer), f32(2, *layer),
        ],
        [
            vmem(1, padded, depth), vmem(2, padded, depth), vmem(4, padded, depth), vmem(8, *layer),
            vmem(2, padded, depth), vmem(2, *layer), vmem(2, *layer),
        ],
        (inputs, message, own2, known1, new, *fine, between_chips(message)),
    )
    within_in = within_chip(within)
    plain = f32(4, *tile)
    slots, *middle = call(
        middle_down_kernel,
        [f32(blocks // 2, 3, quarter, depth), plain, plain, plain, plain, f32(4, padded2, depth)] + [plain] * 3,
        [vmem(6, padded2, depth), vmem(3, *tile)],
        (within, fx2, within_in),
    )
    kinds = [[2 * chip + (chip + core) % 2 for chip in reversed(range(blocks // 2))] for core in range(2)]
    gathered = lax.all_to_all(slots, "gx", 0, 0, axis_index_groups=kinds, tiled=True)
    solved, owned = call(
        coarse_kernel,
        [f32(layers, *layer), f32(1, quarter, depth // 4)],
        [
            vmem(blocks // 4, quarter, depth), vmem(4, blocks // 4, quarter + 2 * PAD, depth), vmem(7, *tile),
            vmem(5, padded2, depth), vmem(layers + 2, padded, depth), vmem(5, *layer), vmem(layers, *layer),
            vmem(1, quarter, depth // 4), pltpu.SMEM((blocks,), jnp.int32),
            pltpu.SemaphoreType.DMA, pltpu.SemaphoreType.DMA((layers + 1,)),
        ],
        (block_owner, gathered, *middle, inputs, new, *margin, *fine, *border, within_in),
        pl.ANY,
    )
    return solved, owned


def solution(mesh):
    split = P(("groups", "gx"), None, None)
    return jax.shard_map(
        on_device,
        mesh=mesh,
        in_specs=(split, split, split, P("groups")),
        out_specs=(split, split),
        check_vma=False,
    )
```

```python
import jax
import jax.numpy as jnp
from jax import lax
from jax.experimental import pallas as pl
from jax.experimental.pallas import tpu as pltpu
from jax.sharding import PartitionSpec as P

STIFFNESS = 100.0
EPSILON = 0.01
COARSE_SWEEPS = 4
PAD = 8


def between_chips(block):
    return lax.ppermute(block, "gx", [(i, i + 1 if i % 2 else i - 1) for i in range(1, lax.axis_size("gx") - 1)])


def within_chip(block):
    return lax.ppermute(block, "gx", [(i, i ^ 1) for i in range(lax.axis_size("gx"))])


def chip_order(chips):
    half = chips // 2
    return [0, *range(chips - 2, half - 1, -1), chips - 1, *range(half - 1, 0, -1)]


def place_of(chip, chips):
    late = jnp.where(chip == chips - 1, chips // 2, chips - 1 - chip)
    return jnp.where(chip >= chips // 2, late, (chips - chip) % chips)


def by_side(across, within):
    on_left = lax.axis_index("gx") % 2 == 0
    return jnp.where(on_left, across, within), jnp.where(on_left, within, across)


def lanes_of(shape):
    return lax.broadcasted_iota(jnp.int32, shape, len(shape) - 1)


def rows_of(shape):
    return lax.broadcasted_iota(jnp.int32, shape, len(shape) - 2)


def ahead(values, step, axis):
    return pltpu.roll(values, values.shape[axis] - step, axis)


def behind(values, step, axis):
    return pltpu.roll(values, step, axis)


def with_partner(values, step, axis):
    index = lax.broadcasted_iota(jnp.int32, values.shape, axis)
    partner = jnp.where((index & step) == 0, ahead(values, step, axis), behind(values, step, axis))
    return values + partner


def even_row_sum(scratch, rows):
    return scratch[pl.ds(0, rows, 2), :] + scratch[pl.ds(1, rows, 2), :]


def core_of():
    return lax.axis_index("gx") % 2


def own_layer(u, layers):
    return u + core_of() * (layers - 1 - 2 * u)


def three_parts(ref):
    third = ref.shape[0] // 3
    return [ref.at[pl.ds(k * third, third)] for k in range(3)]


def odd_cells(ref, rows, first):
    return jnp.where(first, ref[pl.ds(0, rows, 2), :], ref[pl.ds(1, rows, 2), :])


def into_both_rows(ref, values):
    rows = values.shape[0]
    ref[pl.ds(0, rows, 2), :] = values
    ref[pl.ds(1, rows, 2), :] = values


def cell_coef(value):
    return STIFFNESS * (value * value + EPSILON)


class Plane:
    def __init__(self, height, depth):
        self.height, self.half, self.depth = height, height // 2, depth
        self.row, self.lane = rows_of((height, depth)), lanes_of((height, depth))
        self.parity = self.row + self.lane + core_of()
        self.half_lane = lanes_of((self.half, depth))
        self.body = pl.ds(PAD, height)
        self.up, self.down = pl.ds(PAD + 1, height), pl.ds(PAD - 1, height)

    def even(self, u):
        return ((self.parity + u) & 1) == 0

    def odd_first(self, u):
        return ((self.half_lane + core_of() + u) & 1) != 0

    def put(self, ref, values):
        edge = jnp.zeros((PAD, self.depth), jnp.float32)
        ref[:PAD] = edge
        ref[PAD + self.height:] = edge
        ref[self.body] = values

    def face_y(self, here):
        return jnp.where(self.row < self.height - 1, 0.5 * (here + ahead(here, 1, 0)), 0.0)

    def face_z(self, here):
        return jnp.where(self.lane < self.depth - 1, 0.5 * (here + ahead(here, 1, 1)), 0.0)

    def packed(self, outer, inner, core):
        return jnp.where((self.half_lane & 1) == core, outer, inner)

    def both_rows(self, ref):
        return even_row_sum(ref, self.half)

    def summed(self, values, ref):
        ref[...] = values
        return with_partner(self.both_rows(ref), 1, 1)

    def odd_rows(self, values, ref):
        ref[...] = values
        return with_partner(ref[pl.ds(1, self.half, 2), :], 1, 1)

    def odd_lanes(self, values, ref):
        ref[...] = values
        sums = self.both_rows(ref)
        return jnp.where((self.half_lane & 1) == 0, ahead(sums, 1, 1), sums)


def in_layer(plane, fy, fz, fzl, padded):
    here = padded[plane.body]
    total = fy[plane.body] * padded[plane.up] + fy[plane.down] * padded[plane.down]
    return total + (fz[...] * ahead(here, 1, 1) + fzl[...] * behind(here, 1, 1))


def edge_kernel(inputs, out):
    iterate, source, phase = three_parts(inputs)
    layers, height, depth = iterate.shape
    plane = Plane(height, depth)
    near, inner, far = [own_layer(u, layers) for u in (layers - 1, layers - 2, layers - 3)]
    coef_near, coef_inner, coef_far = [cell_coef(phase[k]) for k in (near, inner, far)]

    def around(here, e):
        fy, fz = plane.face_y(here), plane.face_z(here)
        fyl, fzl = behind(fy, 1, 0), behind(fz, 1, 1)
        total = fy * ahead(e, 1, 0) + fyl * behind(e, 1, 0)
        return total + fz * ahead(e, 1, 1) + fzl * behind(e, 1, 1), fy + fyl + fz + fzl

    face_near, face_far = 0.5 * (coef_inner + coef_near), 0.5 * (coef_inner + coef_far)
    total, weight = around(coef_inner, iterate[inner])
    total = total + face_near * iterate[near] + face_far * iterate[far]
    updated = (source[inner] + total) / (1.0 + (face_near + face_far + weight))
    total, _ = around(coef_near, iterate[near])
    known = jnp.where(plane.even(layers - 1), total + face_near * iterate[inner], face_near * updated)
    out[:height] = coef_near
    out[height:2 * height] = coef_inner
    out[2 * height:3 * height] = source[near] + known
    out[3 * height:] = odd_cells(iterate.at[near], plane.half, plane.odd_first(layers - 1))


def chip_rows(height):
    half, at, places = height // 2, 0, {}
    for name, size in (
        ("coef0", height), ("coef1", height), ("known0", height), ("old0", half), ("moved1", half), ("face2", half),
        ("source2", half), ("fx2", half), ("far2", half),
    ):
        places[name] = pl.ds(at, size)
        at += size
    return places, at


def own_kernel(owner_of, inputs, cell, old, fx, fy, fz, fzl, inv, even):
    iterate, source, phase = three_parts(inputs)
    layers, height, depth = iterate.shape
    plane = Plane(height, depth)
    body = plane.body
    for u in range(layers):
        cell[u] = cell_coef(phase[own_layer(u, layers)])
        plane.put(old.at[u], iterate[own_layer(u, layers)])
    for u in range(layers):
        here = cell[u]
        if u < layers - 1:
            fx[u] = 0.5 * (here + cell[u + 1])
        plane.put(fy.at[u], plane.face_y(here))
        face = plane.face_z(here)
        fz[u] = face
        fzl[u] = behind(face, 1, 1)
    for u in (1, 2):
        weight = (fx[u] + fx[u - 1]) + (fy[u, body] + fy[u, plane.down]) + (fz[u] + fzl[u])
        inverse = 1.0 / (1.0 + weight)
        inv[u - 1] = inverse
        around = in_layer(plane, fy.at[u], fz.at[u], fzl.at[u], old.at[u])
        total = source[own_layer(u, layers)] + around + (fx[u] * old[u + 1, body] + fx[u - 1] * old[u - 1, body])
        plane.put(even.at[u - 1], total * inverse)


def chip_kernel(
    inputs, cell, old_own, fx_own, fy_own, fz_own, fzl_own, inv_own, even_own, within_in,
    message, own2, known1, new, fx_more, fy_margin, fz_margin, fzl_margin, inv_more,
    old_margin, even_more, change, turn,
):
    iterate, source, phase = three_parts(inputs)
    layers, height, depth = iterate.shape
    plane = Plane(height, depth)
    body, half = plane.body, plane.half
    places, _ = chip_rows(height)
    margin = layers

    def part(k):
        return within_in[k * height:(k + 1) * height]

    def s(u):
        return source[own_layer(u, layers)]

    into_both_rows(turn.at[0], within_in[3 * height:])
    plane.put(old_margin, turn[0])
    fx_more[0] = 0.5 * (cell[layers - 1] + part(0))
    fx_more[1] = 0.5 * (part(0) + part(1))
    plane.put(fy_margin, plane.face_y(part(0)))
    face = plane.face_z(part(0))
    fz_margin[...] = face
    fzl_margin[...] = behind(face, 1, 1)
    fx = [fx_own.at[u] for u in range(3)] + [fx_more.at[0], fx_more.at[1]]
    fy = [fy_own.at[u] for u in range(layers)] + [fy_margin]
    fz = [fz_own.at[u] for u in range(layers)] + [fz_margin]
    fzl = [fzl_own.at[u] for u in range(layers)] + [fzl_margin]
    old = [old_own.at[u] for u in range(layers)] + [old_margin]
    inv = [None, inv_own.at[0], inv_own.at[1], inv_more.at[0], inv_more.at[1]]
    even = [None, even_own.at[0], even_own.at[1], even_more.at[0], even_more.at[1]]
    for u in (margin - 1, margin):
        weight = (fx[u][...] + fx[u - 1][...]) + (fy[u][body] + fy[u][plane.down]) + (fz[u][...] + fzl[u][...])
        inv[u][...] = 1.0 / (1.0 + weight)

    def around(ref, u):
        return in_layer(plane, fy[u], fz[u], fzl[u], ref[u])

    u = margin - 1
    total = s(u) + around(old, u) + (fx[u][...] * old[u + 1][body] + fx[u - 1][...] * old[u - 1][body])
    plane.put(even[u], total * inv[u][...])
    plane.put(even[margin], (part(2) + fx[u][...] * old[u][body]) * inv[margin][...])
    for u in range(2, margin + 1):
        if u < margin:
            total = s(u) + around(even, u) + (fx[u][...] * even[u + 1][body] + fx[u - 1][...] * even[u - 1][body])
        else:
            total = part(2) + around(even, u) + fx[u - 1][...] * even[u - 1][body]
        fresh = total * inv[u][...]
        new[u - 2] = fresh
        plane.put(change.at[u - 2], fresh - old[u][body])
    change = {u: change.at[u - 2] for u in range(2, margin + 1)}

    one = fx[1][...] * change[2][body]
    two = around(change, 2) + fx[2][...] * change[3][body]
    three = around(change, 3) + (fx[2][...] * change[2][body] + fx[3][...] * change[4][body])
    outer = jnp.where(plane.even(1), one, 0.0)
    inner = jnp.where(plane.even(2), two, 0.0) + jnp.where(plane.even(3), three, 0.0)
    core = core_of()

    def tile(name, outer, inner):
        message[places[name], :] = plane.packed(outer, inner, core)

    tile("source2", plane.summed(outer, turn.at[1]), plane.summed(inner, turn.at[2]))
    tile("fx2", plane.summed(fx[1][...], turn.at[3]), plane.summed(fx[3][...], turn.at[4]))
    fy2 = [plane.odd_rows(fy[u][body] + fy[u + 1][body], turn.at[5 + u // 2]) for u in (0, 2)]
    fz2 = [plane.odd_lanes(fz[u][...] + fz[u + 1][...], turn.at[7 + u // 2]) for u in (0, 2)]
    own2[0], own2[1] = plane.packed(*fy2, core), plane.packed(*fz2, core)
    tile("far2", fy2[1], fz2[1])
    for u in range(2):
        message[places["coef%d" % u], :] = cell[u]
    first = s(0) + around(old, 0) + fx[0][...] * old[1][body]
    second = s(0) + fx[0][...] * even[1][body]
    message[places["known0"], :] = jnp.where(plane.even(0), first, second)
    message[places["old0"], :] = odd_cells(iterate.at[own_layer(0, layers)], half, plane.odd_first(0))
    total = s(1) + around(even, 1) + fx[1][...] * even[2][body]
    known1[...] = total
    turn[9] = total * inv[1][...] - old[1][body]
    message[places["moved1"], :] = odd_cells(turn.at[9], half, plane.odd_first(1))
    message[places["face2"], :] = odd_cells(fx[1], half, plane.odd_first(1))


def border_kernel(
    inputs, message, own2, known1, new_in, fx_in, fy_in, fz_in, fzl_in, inv_in, across_in,
    within, fx2_in, new, known, fx, fy, fz, fzl, inv,
    old, even, change, turn, face_y, face_z, face_zl,
):
    iterate, source, _ = three_parts(inputs)
    layers, height, depth = iterate.shape
    plane = Plane(height, depth)
    body, half = plane.body, plane.half
    places, _ = chip_rows(height)
    core, last = core_of(), lax.axis_size("gx") - 1
    position = lax.axis_index("gx")

    def mine(name):
        return message[places[name], :]

    def theirs(name):
        return across_in[places[name], :]

    def opened(name, k):
        into_both_rows(turn.at[k], theirs(name))
        return turn[k]

    for k in range(2):
        here = theirs("coef%d" % k)
        plane.put(face_y.at[k], plane.face_y(here))
        face = plane.face_z(here)
        face_z[k] = face
        face_zl[k] = behind(face, 1, 1)
    fy[...], fz[...], fzl[...] = face_y[0], face_z[0], face_zl[0]
    there = position - 1 + 2 * core
    border = jnp.where((there >= 0) & (there <= last), 0.5 * (mine("coef0") + theirs("coef0")), 0.0)
    face1 = 0.5 * (theirs("coef0") + theirs("coef1"))
    face2 = opened("face2", 2)
    fx[0], fx[1] = border, face1

    def inverse(faces, fy, fz, fzl):
        weight = faces + (fy[body] + fy[plane.down]) + (fz[...] + fzl[...])
        return 1.0 / (1.0 + weight)

    inv_own = inverse(fx_in[0] + border, fy_in.at[0], fz_in.at[0], fzl_in.at[0])
    inv_near = inverse(border + face1, face_y.at[0], face_z.at[0], face_zl.at[0])
    inv_far = inverse(face1 + face2, face_y.at[1], face_z.at[1], face_zl.at[1])
    inv[0], inv[1] = inv_near, inv_own
    old_own, old_next = iterate[own_layer(0, layers)], iterate[own_layer(1, layers)]
    old_near, far = opened("old0", 0), opened("moved1", 1)
    even_own = (mine("known0") + border * old_near) * inv_own
    even_near = (theirs("known0") + border * old_own) * inv_near
    plane.put(even.at[0], even_near)
    plane.put(even.at[1], even_own)

    def near(ref, k):
        return in_layer(plane, face_y.at[k], face_z.at[k], face_zl.at[k], ref)

    def own(ref, u):
        return in_layer(plane, fy_in.at[u], fz_in.at[u], fzl_in.at[u], ref)

    odd_own = (mine("known0") + own(even.at[1], 0) + border * even_near) * inv_own
    odd_near = (theirs("known0") + near(even.at[0], 0) + border * even_own) * inv_near
    odd_next = (known1[...] + fx_in[0] * even_own) * inv_in[0]
    far = far + face1 * even_near * inv_far
    new[0], new[1], new[2] = odd_near, odd_own, odd_next
    near_by, here, following = odd_near - old_near, odd_own - old_own, odd_next - old_next
    for k, values in enumerate((far, near_by, here, following)):
        plane.put(change.at[k], values)
    plane.put(old.at[0], old_near)
    known[...] = theirs("known0") + face1 * far - near(old.at[0], 0)

    def residual(u, values):
        return jnp.where(plane.even(u), values, 0.0)

    own_outer = residual(1, own(change.at[3], 1) + fx_in[0] * here)
    own_outer = own_outer + residual(0, own(change.at[2], 0) + (fx_in[0] * following + border * near_by))
    own_inner = residual(2, fx_in[1] * following)
    its_outer = residual(-1, near(change.at[1], 0) + (face1 * far + border * here))
    its_outer = its_outer + residual(-2, near(change.at[0], 1) + face1 * near_by)
    its_inner = residual(-3, face2 * far)
    sums = [plane.summed(values, turn.at[3 + k]) for k, values in enumerate((own_outer, own_inner, its_outer, its_inner))]
    within[0] = mine("source2") + plane.packed(sums[0], sums[1], core)
    within[5] = theirs("source2") + plane.packed(sums[2], sums[3], 1 - core)
    within[6] = theirs("fx2")
    far2 = theirs("far2")
    far2_swap = jnp.where((plane.half_lane & 1) == 0, ahead(far2, 1, 1), behind(far2, 1, 1))
    near_fy2 = plane.odd_rows(face_y[0, body] + face_y[1, body], turn.at[1])
    near_fz2 = plane.odd_lanes(face_z[0] + face_z[1], turn.at[2])
    within[7] = plane.packed(near_fy2, far2_swap, 1 - core)
    within[8] = plane.packed(near_fz2, far2, 1 - core)
    fx2_in[...] = mine("fx2")
    middle = jnp.where((plane.half_lane & 1) == 0, ahead(mine("fx2"), 1, 1), behind(mine("fx2"), 1, 1))
    within[1] = plane.packed(plane.summed(border, turn.at[7]), middle, core)
    within[2], within[3] = own2[0], own2[1]
    turn[0] = source[own_layer(layers - 1, layers)] + fx_in[layers - 2] * new_in[layers - 4]
    within[4] = odd_cells(turn.at[0], half, jnp.logical_not(plane.odd_first(layers - 1)))


def neigh2(e2, fx2, fxl2, fy2, fz2, fzl2, first_of_two, tiles):
    half = fx2.shape[1]
    body, up, down = pl.ds(PAD, half), pl.ds(PAD + 1, half), pl.ds(PAD - 1, half)
    needed = range(tiles[0], tiles[-1] + 3)
    here = {j: e2[j, body] for j in needed}
    after = {j: ahead(here[j], 1, 1) for j in needed}
    before = {j: behind(here[j], 1, 1) for j in needed}
    found = []
    for j in tiles:
        k = j + 1
        upper = jnp.where(first_of_two, after[k], before[k + 1])
        lower = jnp.where(first_of_two, after[k - 1], before[k])
        sums = fx2[j] * upper + fxl2[j] * lower
        sums = sums + fy2[j, body] * e2[k, up] + fy2[j, down] * e2[k, down]
        sums = sums + fz2[j] * ahead(here[k], 2, 1) + fzl2[j] * behind(here[k], 2, 1)
        found.append(sums)
    return found


def parities2(half, lanes):
    row, lane = rows_of((half, lanes)), lanes_of((half, lanes))
    return (lane & 1) == 0, ((row + (lane & 1) + (lane >> 1)) & 1) == 0


def group(values):
    return with_partner(with_partner(values, 1, 1), 2, 1)


def packed_odd(values, pair):
    half, lanes = values.shape
    lane = lanes_of((half // 2, lanes))
    pair[...] = values
    return odd_cells(pair, half // 2, (((lane & 1) + (lane >> 1)) & 1) != 0)


def middle_down_kernel(
    own, fx2_in, within_in,
    slots, e2_out, s2, fx2, fxl2, fy2, fz2, fzl2, inv2,
    e2, pair,
):
    _, half, lanes = own.shape
    quarter = half // 2
    first_of_two, even2 = parities2(half, lanes)
    body, down = pl.ds(PAD, half), pl.ds(PAD - 1, half)
    edge = jnp.zeros((PAD, lanes), jnp.float32)
    for j in (0, 5):
        e2[j] = jnp.zeros((half + 2 * PAD, lanes), jnp.float32)

    def pair_of(k):
        return by_side(own[k], within_in[k])

    def four(k):
        (left, right), (far_left, far_right) = pair_of(k), pair_of(5 + k)
        return far_left, left, right, far_right

    for j, (source, fy, fz) in enumerate(zip(four(0), four(2), four(3))):
        s2[j] = source
        fy2[j, :PAD] = edge
        fy2[j, body] = fy
        fy2[j, PAD + half:] = edge
        fz2[j] = fz
        fzl2[j] = behind(fz, 2, 1)

    def between(left, right):
        return jnp.where(first_of_two, ahead(left, 1, 1), behind(right, 1, 1))

    fxl0, fxl1, fxr2, fxr3 = four(1)
    inner = fx2_in[...]
    fxr1, _ = by_side(inner, between(fxl1, inner))
    fxl2_, _ = by_side(between(inner, fxr2), inner)
    for j, (face, low) in enumerate(
        ((between(fxl0, fxl1), fxl0), (fxr1, fxl1), (fxr2, fxl2_), (fxr3, between(fxr2, fxr3)))
    ):
        fx2[j], fxl2[j] = face, low
        weight = face + low + fy2[j, body] + fy2[j, down] + fz2[j] + fzl2[j]
        inverse = 1.0 / (8.0 + weight)
        inv2[j] = inverse
        e2[j + 1, :PAD] = edge
        e2[j + 1, PAD + half:] = edge
        e2[j + 1, body] = s2[j] * inverse

    def neigh(tiles):
        return neigh2(e2, fx2, fxl2, fy2, fz2, fzl2, first_of_two, tiles)

    fresh = [(s2[j] + sums) * inv2[j] for j, sums in enumerate(neigh((0, 1, 2, 3)))]
    for j in range(4):
        e2[j + 1, body] = fresh[j]
        e2_out[j] = fresh[j]
    lane = lanes_of((quarter, lanes))
    odd_layer, odd_depth = (lane & 1) != 0, (lane & 2) != 0
    chips = slots.shape[0]
    for k, sums in enumerate(neigh((1, 2))):
        j = k + 1
        pair[k] = jnp.where(even2, sums, 0.0)
        item = (lane - (lax.axis_index("gx") // 2 * 2 + k) // (chips // 2)) & 3
        source = group(even_row_sum(pair.at[k], quarter))
        fx = group(jnp.where(odd_layer, even_row_sum(fx2.at[j], quarter), 0.0))
        fxl = group(jnp.where(odd_layer, 0.0, even_row_sum(fxl2.at[j], quarter)))
        fy = group(fy2[j, pl.ds(PAD + 1, quarter, 2), :])
        fz = group(jnp.where(odd_depth, even_row_sum(fz2.at[j], quarter), 0.0))
        weight = (fx + fxl) + (fy + behind(fy, 1, 0)) + (fz + behind(fz, 4, 1))
        start = source / (64.0 + weight)
        tile = jnp.where(item == 0, start, jnp.where(item == 1, fx, jnp.where(item == 2, fy, fz)))
        for c in range(chips):
            slots[c, k] = tile
    halo = packed_odd(jnp.where(first_of_two, fresh[2], fresh[1]), pair.at[2])
    for c in range(chips):
        slots[c, 2] = halo


def joined(one, two):
    return jnp.concatenate([part for part in (one, two) if part.shape[0]], 0)


class Level:
    def __init__(self, mass, source, faces, row_step, lane_step, slot_step):
        self.source, self.row_step, self.lane_step, self.slot_step = source, row_step, lane_step, slot_step
        self.fx, self.fy, self.fz = faces
        self.tiles = source.shape[0]
        shape = source.shape
        self.lane = lanes_of(shape)
        layer = lax.broadcasted_iota(jnp.int32, shape, 0) if self.tiles > 1 else self.lane // slot_step
        self.even = ((layer + rows_of(shape) // row_step + self.lane // lane_step) & 1) == 0
        self.fxl = self.lower(self.fx)
        self.fyl = self.row_shifts(self.fy)[1]
        self.fzl = behind(self.fz, lane_step, 2)
        weight = (self.fx + self.fxl) + (self.fy + self.fyl) + (self.fz + self.fzl)
        self.inv = 1.0 / (mass + weight)

    def upper(self, e):
        return joined(e[1:], ahead(e[:1], self.slot_step, 2))

    def lower(self, e):
        return joined(behind(e[-1:], self.slot_step, 2), e[:-1])

    def row_shifts(self, e):
        return ahead(e, self.row_step, 1), behind(e, self.row_step, 1)

    def neigh(self, e):
        above, below = self.row_shifts(e)
        total = (self.fx * self.upper(e) + self.fxl * self.lower(e)) + (self.fy * above + self.fyl * below)
        return total + (self.fz * ahead(e, self.lane_step, 2) + self.fzl * behind(e, self.lane_step, 2))

    def start(self):
        return self.source * self.inv

    def update(self, e):
        return self.start() + self.neigh(e) * self.inv

    def cycle(self, deeper):
        odd = self.update(self.start())
        residual = jnp.where(self.even, self.neigh(odd), 0.0)
        fix = deeper(self.restricted(residual), self.coarse_faces())
        even = self.update(odd + self.prolonged(fix))
        return jnp.where(self.even, even, self.update(even))

    def coarse_slot_step(self):
        return self.slot_step if self.tiles > 1 else 2 * self.slot_step

    def pairs(self, values):
        if self.tiles == 1:
            return with_partner(values, self.slot_step, 2)
        halves = values.reshape(self.tiles // 2, 2, *values.shape[1:])
        return halves[:, 0] + halves[:, 1]

    def odd_layers(self, values):
        if self.tiles == 1:
            return with_partner(jnp.where((self.lane & self.slot_step) != 0, values, 0.0), self.slot_step, 2)
        return values.reshape(self.tiles // 2, 2, *values.shape[1:])[:, 1]

    def row_pairs(self, values):
        return with_partner(values, self.row_step, 1)

    def odd_rows(self, values):
        odd = (rows_of(values.shape) & self.row_step) != 0
        return with_partner(jnp.where(odd, values, 0.0), self.row_step, 1)

    def restricted(self, values):
        return with_partner(self.row_pairs(self.pairs(values)), self.lane_step, 2)

    def coarse_faces(self):
        fx = with_partner(self.row_pairs(self.odd_layers(self.fx)), self.lane_step, 2)
        fy = with_partner(self.odd_rows(self.pairs(self.fy)), self.lane_step, 2)
        return fx, fy, self.restricted(jnp.where((self.lane & self.lane_step) != 0, self.fz, 0.0))

    def prolonged(self, fix):
        if self.tiles == 1:
            return fix
        both = jnp.concatenate([fix[:, None], fix[:, None]], 1)
        return both.reshape(self.tiles, *fix.shape[1:])


class Rows(Level):
    def __init__(self, mass, source, faces, scratch):
        self.scratch, self.used = scratch, 0
        self.rows = source.shape[1]
        super().__init__(mass, source, faces, 1, 4, 1)

    def start(self):
        return self.source

    def place(self):
        self.used += 1
        return self.scratch.at[self.used % self.scratch.shape[0]]

    def row_shifts(self, e):
        place = self.place()
        edge = jnp.zeros((e.shape[0], PAD, e.shape[2]), jnp.float32)
        place[:, :PAD] = edge
        place[:, PAD + self.rows:] = edge
        place[:, pl.ds(PAD, self.rows)] = e
        return place[:, pl.ds(PAD + 1, self.rows)], place[:, pl.ds(PAD - 1, self.rows)]

    def every_other(self, values, starts):
        place, tiles = self.place(), values.shape[0]
        place[:tiles, : self.rows] = values
        found = 0.0
        for start in starts:
            found = found + jnp.concatenate(
                [place[j, pl.ds(start, self.rows // 2, 2), :][None] for j in range(tiles)], 0
            )
        return found

    def row_pairs(self, values):
        return self.every_other(values, (0, 1))

    def odd_rows(self, values):
        return self.every_other(values, (1,))

    def prolonged(self, fix):
        place, tiles = self.place(), fix.shape[0]
        for j in range(tiles):
            into_both_rows(place.at[j, pl.ds(0, self.rows)], fix[j])
        return super().prolonged(place[:tiles, : self.rows])


def coarsest(mass, source, faces, *steps):
    row_step, lane_step, slot_step = steps
    level = Level(mass, source, faces, *steps)
    counts = source.shape[1] // row_step, source.shape[2] // lane_step, 4 // slot_step
    frames = [(m, k, q) for m in range(counts[0]) for k in range(counts[1]) for q in range(counts[2])]
    place = level.lane & 3

    def spread(values):
        copies = {}
        for m, k, q in frames:
            if k:
                copies[m, k, q] = behind(copies[m, 0, q], k * lane_step, 2)
            elif q:
                by = q * slot_step
                one, two = behind(copies[m, 0, 0], by, 2), ahead(copies[m, 0, 0], 4 - by, 2)
                copies[m, k, q] = jnp.where(place >= by, one, two)
            else:
                copies[m, k, q] = behind(values, m * row_step, 1) if m else values
        return copies

    start, inv, fx, fy, fz = [spread(values) for values in (source * level.inv, level.inv, level.fx, level.fy, level.fz)]

    def shifted(copies, frame, axis, by):
        moved = list(frame)
        moved[axis] = (frame[axis] - by) % counts[axis]
        return copies[tuple(moved)]

    def along_x(copies, frame, by):
        here, wrapped = copies[frame], shifted(copies, frame, 2, by)
        return joined(here[1:], wrapped[:1]) if by > 0 else joined(wrapped[-1:], here[:-1])

    weights = {}
    for frame in frames:
        pairs = [
            (fx[frame], along_x(fx, frame, -1)),
            (fy[frame], shifted(fy, frame, 0, -1)),
            (fz[frame], shifted(fz, frame, 1, -1)),
        ]
        weights[frame] = [(up * inv[frame], low * inv[frame]) for up, low in pairs]

    def update(e):
        fresh = {}
        for frame in frames:
            (x_up, x_low), (y_up, y_low), (z_up, z_low) = weights[frame]
            total = x_up * along_x(e, frame, 1) + x_low * along_x(e, frame, -1)
            total = total + (y_up * shifted(e, frame, 0, 1) + y_low * shifted(e, frame, 0, -1))
            total = total + (z_up * shifted(e, frame, 1, 1) + z_low * shifted(e, frame, 1, -1))
            fresh[frame] = start[frame] + total
        return fresh

    even = start
    odd = update(even)
    for turn in range(COARSE_SWEEPS - 1):
        even = update(odd)
        odd = update(even)
    return jnp.where(level.even, even[0, 0, 0], odd[0, 0, 0])


def small_cycle(mass, source, faces, row_step, lane_step, slot_step, between):
    if between == 0:
        return coarsest(mass, source, faces, row_step, lane_step, slot_step)
    level = Level(mass, source, faces, row_step, lane_step, slot_step)
    return level.cycle(
        lambda inner, inner_faces: small_cycle(
            8.0 * mass, inner, inner_faces, 2 * row_step, 2 * lane_step, level.coarse_slot_step(), between - 1
        )
    )


def coarse_kernel(
    owner_of, gathered, e2_in, s2_in, fx2_in, fxl2_in, fy2_in, fz2_in, fzl2_in, inv2_in,
    inputs, new_in, fx_more, fy_margin, fz_margin, fzl_margin, inv_more, fx_in, fy_in, fz_in, fzl_in, inv_in,
    new_out, known_out, fx_out, fy_out, fz_out, fzl_out, inv_out, within_in,
    solved_out, owned_out,
    e3, rows3, pair, e2, e1, cor, solved, owned, owner_here, fetch_sem, sems,
):
    fetch = pltpu.make_async_copy(owner_of, owner_here, fetch_sem)
    fetch.start()
    chips, _, quarter, lanes = gathered.shape
    blocks = 2 * chips
    half, height = 2 * quarter, 4 * quarter
    position, last = lax.axis_index("gx"), blocks - 1

    slot = lanes_of((quarter, lanes)) & 3
    spread = blocks // 4
    order = chip_order(chips)
    tiles = [gathered[order.index(chip), k] for chip in range(chips) for k in range(2)]
    items = []
    for k in range(4):
        packs = []
        for j in range(spread):
            value = tiles[j + (3 - k) % 4 * spread]
            for at in range(3):
                value = jnp.where(slot == at, tiles[j + (at - k) % 4 * spread], value)
            if k:
                value = jnp.where(slot < 4 - k, ahead(value, k, 1), behind(value, 4 - k, 1))
            packs.append(value[None])
        items.append(jnp.concatenate(packs, 0))
    third = Rows(64.0, items[0], items[1:], rows3)
    e3[...] = third.cycle(
        lambda inner, faces: small_cycle(512.0, inner, faces, 1, 8, third.coarse_slot_step(), 2)
    )

    fetch.wait()
    owner = owner_here[position]
    wide, narrow = lanes_of((lanes, lanes)), rows_of((lanes, lanes))
    take = jnp.where(narrow == 4 * wide + owner // spread, 1.0, 0.0)
    block = jnp.dot(
        e3[owner % spread], take, precision=lax.Precision.HIGHEST, preferred_element_type=jnp.float32
    )
    owned[0] = block[:, : lanes // 4]
    copies = [pltpu.make_async_copy(owned, owned_out, sems.at[0])]
    copies[0].start()

    first_of_two, even2 = parities2(half, lanes)
    body2 = pl.ds(PAD, half)
    edge = jnp.zeros((PAD, lanes), jnp.float32)
    core = core_of()
    s2, fx2, fxl2, fy2, fz2, fzl2, inv2 = [
        ref.at[pl.ds(core, 3)] for ref in (s2_in, fx2_in, fxl2_in, fy2_in, fz2_in, fzl2_in, inv2_in)
    ]
    next_chip = jnp.clip(position // 2 - 1 + 2 * core, 0, chips - 1)
    into_both_rows(pair.at[5], gathered[place_of(next_chip, chips), 2])
    halo = pair[5]
    before = (
        by_side(halo, e2_in[0])[0], by_side(jnp.where(first_of_two, halo, e2_in[0]), e2_in[1])[0],
        by_side(e2_in[1], e2_in[2])[0],
        by_side(e2_in[2], jnp.where(first_of_two, e2_in[3], halo))[0], by_side(e2_in[3], halo)[0],
    )
    for k in range(5):
        j = jnp.clip(position + k - 2, 0, last)
        into_both_rows(pair.at[k], group(jnp.where(slot == j // spread, e3[j % spread], 0.0)))
        e2[k, :PAD] = edge
        e2[k, PAD + half:] = edge
        e2[k, body2] = before[k] + pair[k]

    def update2():
        sums = neigh2(e2, fx2, fxl2, fy2, fz2, fzl2, first_of_two, (0, 1, 2))
        return [(s2[j] + sums[j]) * inv2[j] for j in range(3)]

    fresh = update2()
    for j in range(3):
        e2[j + 1, body2] = fresh[j]
    fixes2 = [jnp.where(even2, even, odd) for even, odd in zip(fresh, update2())]

    _, source, _ = three_parts(inputs)
    layers = source.shape[0]
    plane = Plane(height, lanes)
    body1 = plane.body
    near_lane = (lanes_of((half, lanes)) & 1) == core
    swaps = [jnp.where(first_of_two, ahead(v, 1, 1), behind(v, 1, 1)) for v in fixes2]
    outer, inner = by_side(fixes2[0], fixes2[2])
    outer_swap, inner_swap = by_side(swaps[0], swaps[2])
    coarse = (
        jnp.where(near_lane, outer_swap, outer), jnp.where(near_lane, fixes2[1], swaps[1]),
        jnp.where(near_lane, swaps[1], fixes2[1]), jnp.where(near_lane, inner, inner_swap),
    )
    fixes = []
    for k in range(4):
        into_both_rows(cor.at[k], coarse[k])
        fixes.append(cor[k])
    for u in range(-1, layers + 1):
        before = new_out[u + 1] if u < 2 else new_in[u - 2]
        plane.put(e1.at[u + 1], before + fixes[(u + 2) // 2])

    def fx1(u):
        if u < 0:
            return fx_out[-1 - u]
        return fx_in[u] if u < layers - 1 else fx_more[u - layers + 1]

    def inv1(u):
        if u <= 0:
            return inv_out[u + 1]
        return inv_in[u - 1] if u < layers - 1 else inv_more[u - layers + 1]

    def around1(u):
        if u < 0:
            return in_layer(plane, fy_out, fz_out, fzl_out, e1.at[0])
        if u == layers:
            return in_layer(plane, fy_margin, fz_margin, fzl_margin, e1.at[u + 1])
        return in_layer(plane, fy_in.at[u], fz_in.at[u], fzl_in.at[u], e1.at[u + 1])

    def updated1(u):
        sums = around1(u) + (fx1(u) * e1[u + 2, body1] + fx1(u - 1) * e1[u, body1])
        return (source[own_layer(u, layers)] + sums) * inv1(u)

    for u in range(layers):
        e1[u + 1, body1] = jnp.where(plane.even(u), updated1(u), e1[u + 1, body1])
    e1[0, body1] = (known_out[...] + fx1(-2) * fixes[0] + (around1(-1) + fx1(-1) * e1[1, body1])) * inv1(-1)
    into_both_rows(cor.at[4], within_in[4])
    sums = cor[4] + fx1(layers) * fixes[3] + (around1(layers) + fx1(layers - 1) * e1[layers, body1])
    e1[layers + 1, body1] = sums * inv1(layers)
    for u in range(layers):
        solved[u] = jnp.where(plane.even(u), e1[u + 1, body1], updated1(u))
        copies.append(
            pltpu.make_async_copy(solved.at[u], solved_out.at[own_layer(u, layers)], sems.at[u + 1])
        )
        copies[-1].start()
    for copy in copies:
        copy.wait()


def f32(*shape):
    return jax.ShapeDtypeStruct(shape, jnp.float32)


def vmem(*shape):
    return pltpu.VMEM(shape, jnp.float32)


def call(kernel, outs, scratch, operands, out_space=pltpu.VMEM):
    def size(shape):
        count = 4
        for extent in shape:
            count *= extent
        return count

    sized = [array for array in (*scratch, *outs, *operands) if hasattr(array, "shape")]
    asked = 8 * 2**20 + sum(size(array.shape) for array in sized)
    return pl.pallas_call(
        kernel,
        out_shape=tuple(outs),
        in_specs=[pl.BlockSpec(memory_space=pltpu.VMEM)] * len(operands),
        out_specs=tuple([pl.BlockSpec(memory_space=out_space)] * len(outs)),
        scratch_shapes=scratch,
        compiler_params=pltpu.CompilerParams(vmem_limit_bytes=asked),
    )(*operands)


def on_device(iterate, source, phase_field, block_owner):
    layers, height, depth = iterate.shape
    half, quarter = height // 2, height // 4
    blocks = lax.axis_size("gx")
    padded, padded2 = height + 2 * PAD, half + 2 * PAD
    inputs = sum(
        jnp.pad(block, ((k * layers, (2 - k) * layers), (0, 0), (0, 0)))
        for k, block in enumerate((iterate, source, phase_field))
    )
    edge, = call(edge_kernel, [f32(3 * height + half, depth)], [], (inputs,))
    edge_in = within_chip(edge)
    layer, tile, tall = (height, depth), (half, depth), (padded, depth)
    cell, old, *fine, even = call(
        own_kernel,
        [
            f32(layers, *layer), f32(layers, *tall), f32(layers - 1, *layer), f32(layers, *tall),
            f32(layers, *layer), f32(layers, *layer), f32(2, *layer), f32(2, *tall),
        ],
        [], (block_owner, inputs),
    )
    message, own2, known1, new, *margin = call(
        chip_kernel,
        [
            f32(chip_rows(height)[1], depth), f32(2, *tile), f32(*layer), f32(3, *layer),
            f32(2, *layer), f32(*tall), f32(*layer), f32(*layer), f32(2, *layer),
        ],
        [vmem(*tall), vmem(2, *tall), vmem(3, *tall), vmem(10, *layer)],
        (inputs, cell, old, *fine, even, edge_in),
    )
    within, fx2, *border = call(
        border_kernel,
        [
            f32(9, *tile), f32(*tile), f32(3, *layer), f32(*layer), f32(2, *layer),
            f32(padded, depth), f32(*layer), f32(*layer), f32(2, *layer),
        ],
        [
            vmem(1, padded, depth), vmem(2, padded, depth), vmem(4, padded, depth), vmem(8, *layer),
            vmem(2, padded, depth), vmem(2, *layer), vmem(2, *layer),
        ],
        (inputs, message, own2, known1, new, *fine, between_chips(message)),
    )
    within_in = within_chip(within)
    plain = f32(4, *tile)
    slots, *middle = call(
        middle_down_kernel,
        [f32(blocks // 2, 3, quarter, depth), plain, plain, plain, plain, f32(4, padded2, depth)] + [plain] * 3,
        [vmem(6, padded2, depth), vmem(3, *tile)],
        (within, fx2, within_in),
    )
    kinds = [[2 * chip + (chip + core) % 2 for chip in chip_order(blocks // 2)] for core in range(2)]
    gathered = lax.all_to_all(slots, "gx", 0, 0, axis_index_groups=kinds, tiled=True)
    solved, owned = call(
        coarse_kernel,
        [f32(layers, *layer), f32(1, quarter, depth // 4)],
        [
            vmem(blocks // 4, quarter, depth), vmem(4, blocks // 4, quarter + 2 * PAD, depth), vmem(7, *tile),
            vmem(5, padded2, depth), vmem(layers + 2, padded, depth), vmem(5, *layer), vmem(layers, *layer),
            vmem(1, quarter, depth // 4), pltpu.SMEM((blocks,), jnp.int32),
            pltpu.SemaphoreType.DMA, pltpu.SemaphoreType.DMA((layers + 1,)),
        ],
        (block_owner, gathered, *middle, inputs, new, *margin, *fine, *border, within_in),
        pl.ANY,
    )
    return solved, owned


def solution(mesh):
    split = P(("groups", "gx"), None, None)
    return jax.shard_map(
        on_device,
        mesh=mesh,
        in_specs=(split, split, split, P("groups")),
        out_specs=(split, split),
        check_vma=False,
    )
```

```python
import jax
import jax.numpy as jnp
from jax import lax
from jax.experimental import pallas as pl
from jax.experimental.pallas import tpu as pltpu
from jax.sharding import PartitionSpec as P

STIFFNESS = 100.0
EPSILON = 0.01
COARSE_SWEEPS = 4
PAD = 8


def between_chips(block):
    return lax.ppermute(block, "gx", [(i, i + 1 if i % 2 else i - 1) for i in range(1, lax.axis_size("gx") - 1)])


def within_chip(block):
    return lax.ppermute(block, "gx", [(i, i ^ 1) for i in range(lax.axis_size("gx"))])


def by_side(across, within):
    on_left = lax.axis_index("gx") % 2 == 0
    return jnp.where(on_left, across, within), jnp.where(on_left, within, across)


def lanes_of(shape):
    return lax.broadcasted_iota(jnp.int32, shape, len(shape) - 1)


def rows_of(shape):
    return lax.broadcasted_iota(jnp.int32, shape, len(shape) - 2)


def ahead(values, step, axis):
    return pltpu.roll(values, values.shape[axis] - step, axis)


def behind(values, step, axis):
    return pltpu.roll(values, step, axis)


def with_partner(values, step, axis):
    index = lax.broadcasted_iota(jnp.int32, values.shape, axis)
    partner = jnp.where((index & step) == 0, ahead(values, step, axis), behind(values, step, axis))
    return values + partner


def even_row_sum(scratch, rows):
    return scratch[pl.ds(0, rows, 2), :] + scratch[pl.ds(1, rows, 2), :]


def core_of():
    return lax.axis_index("gx") % 2


def own_layer(u, layers):
    return u + core_of() * (layers - 1 - 2 * u)


def three_parts(ref):
    third = ref.shape[0] // 3
    return [ref.at[pl.ds(k * third, third)] for k in range(3)]


def odd_cells(ref, rows, first):
    return jnp.where(first, ref[pl.ds(0, rows, 2), :], ref[pl.ds(1, rows, 2), :])


def into_both_rows(ref, values):
    rows = values.shape[0]
    ref[pl.ds(0, rows, 2), :] = values
    ref[pl.ds(1, rows, 2), :] = values


def cell_coef(value):
    return STIFFNESS * (value * value + EPSILON)


class Plane:
    def __init__(self, height, depth):
        self.height, self.half, self.depth = height, height // 2, depth
        self.row, self.lane = rows_of((height, depth)), lanes_of((height, depth))
        self.parity = self.row + self.lane + core_of()
        self.half_lane = lanes_of((self.half, depth))
        self.body = pl.ds(PAD, height)
        self.up, self.down = pl.ds(PAD + 1, height), pl.ds(PAD - 1, height)

    def even(self, u):
        return ((self.parity + u) & 1) == 0

    def odd_first(self, u):
        return ((self.half_lane + core_of() + u) & 1) != 0

    def put(self, ref, values):
        edge = jnp.zeros((PAD, self.depth), jnp.float32)
        ref[:PAD] = edge
        ref[PAD + self.height:] = edge
        ref[self.body] = values

    def face_y(self, here):
        return jnp.where(self.row < self.height - 1, 0.5 * (here + ahead(here, 1, 0)), 0.0)

    def face_z(self, here):
        return jnp.where(self.lane < self.depth - 1, 0.5 * (here + ahead(here, 1, 1)), 0.0)

    def packed(self, outer, inner, core):
        return jnp.where((self.half_lane & 1) == core, outer, inner)

    def both_rows(self, ref):
        return even_row_sum(ref, self.half)

    def summed(self, values, ref):
        ref[...] = values
        return with_partner(self.both_rows(ref), 1, 1)

    def odd_rows(self, values, ref):
        ref[...] = values
        return with_partner(ref[pl.ds(1, self.half, 2), :], 1, 1)

    def odd_lanes(self, values, ref):
        ref[...] = values
        sums = self.both_rows(ref)
        return jnp.where((self.half_lane & 1) == 0, ahead(sums, 1, 1), sums)


def in_layer(plane, fy, fz, fzl, padded):
    here = padded[plane.body]
    total = fy[plane.body] * padded[plane.up] + fy[plane.down] * padded[plane.down]
    return total + (fz[...] * ahead(here, 1, 1) + fzl[...] * behind(here, 1, 1))


def edge_kernel(inputs, out):
    iterate, source, phase = three_parts(inputs)
    layers, height, depth = iterate.shape
    plane = Plane(height, depth)
    near, inner, far = [own_layer(u, layers) for u in (layers - 1, layers - 2, layers - 3)]
    coef_near, coef_inner, coef_far = [cell_coef(phase[k]) for k in (near, inner, far)]

    def around(here, e):
        fy, fz = plane.face_y(here), plane.face_z(here)
        fyl, fzl = behind(fy, 1, 0), behind(fz, 1, 1)
        total = fy * ahead(e, 1, 0) + fyl * behind(e, 1, 0)
        return total + fz * ahead(e, 1, 1) + fzl * behind(e, 1, 1), fy + fyl + fz + fzl

    face_near, face_far = 0.5 * (coef_inner + coef_near), 0.5 * (coef_inner + coef_far)
    total, weight = around(coef_inner, iterate[inner])
    total = total + face_near * iterate[near] + face_far * iterate[far]
    updated = (source[inner] + total) / (1.0 + (face_near + face_far + weight))
    total, _ = around(coef_near, iterate[near])
    known = jnp.where(plane.even(layers - 1), total + face_near * iterate[inner], face_near * updated)
    out[:height] = coef_near
    out[height:2 * height] = coef_inner
    out[2 * height:3 * height] = source[near] + known
    out[3 * height:] = odd_cells(iterate.at[near], plane.half, plane.odd_first(layers - 1))


def chip_rows(height):
    half, at, places = height // 2, 0, {}
    for name, size in (
        ("coef0", height), ("coef1", height), ("known0", height), ("old0", half), ("moved1", half), ("face2", half),
        ("source2", half), ("fx2", half), ("far2", half),
    ):
        places[name] = pl.ds(at, size)
        at += size
    return places, at


def own_kernel(owner_of, inputs, cell, old, fx, fy, fz, fzl, inv, even):
    iterate, source, phase = three_parts(inputs)
    layers, height, depth = iterate.shape
    plane = Plane(height, depth)
    body = plane.body
    for u in range(layers):
        cell[u] = cell_coef(phase[own_layer(u, layers)])
        plane.put(old.at[u], iterate[own_layer(u, layers)])
    for u in range(layers):
        here = cell[u]
        if u < layers - 1:
            fx[u] = 0.5 * (here + cell[u + 1])
        plane.put(fy.at[u], plane.face_y(here))
        face = plane.face_z(here)
        fz[u] = face
        fzl[u] = behind(face, 1, 1)
    for u in (1, 2):
        weight = (fx[u] + fx[u - 1]) + (fy[u, body] + fy[u, plane.down]) + (fz[u] + fzl[u])
        inverse = 1.0 / (1.0 + weight)
        inv[u - 1] = inverse
        around = in_layer(plane, fy.at[u], fz.at[u], fzl.at[u], old.at[u])
        total = source[own_layer(u, layers)] + around + (fx[u] * old[u + 1, body] + fx[u - 1] * old[u - 1, body])
        plane.put(even.at[u - 1], total * inverse)


def chip_kernel(
    inputs, cell, old_own, fx_own, fy_own, fz_own, fzl_own, inv_own, even_own, within_in,
    message, own2, known1, new, fx_more, fy_margin, fz_margin, fzl_margin, inv_more,
    old_margin, even_more, change, turn,
):
    iterate, source, phase = three_parts(inputs)
    layers, height, depth = iterate.shape
    plane = Plane(height, depth)
    body, half = plane.body, plane.half
    places, _ = chip_rows(height)
    margin = layers

    def part(k):
        return within_in[k * height:(k + 1) * height]

    def s(u):
        return source[own_layer(u, layers)]

    into_both_rows(turn.at[0], within_in[3 * height:])
    plane.put(old_margin, turn[0])
    fx_more[0] = 0.5 * (cell[layers - 1] + part(0))
    fx_more[1] = 0.5 * (part(0) + part(1))
    plane.put(fy_margin, plane.face_y(part(0)))
    face = plane.face_z(part(0))
    fz_margin[...] = face
    fzl_margin[...] = behind(face, 1, 1)
    fx = [fx_own.at[u] for u in range(3)] + [fx_more.at[0], fx_more.at[1]]
    fy = [fy_own.at[u] for u in range(layers)] + [fy_margin]
    fz = [fz_own.at[u] for u in range(layers)] + [fz_margin]
    fzl = [fzl_own.at[u] for u in range(layers)] + [fzl_margin]
    old = [old_own.at[u] for u in range(layers)] + [old_margin]
    inv = [None, inv_own.at[0], inv_own.at[1], inv_more.at[0], inv_more.at[1]]
    even = [None, even_own.at[0], even_own.at[1], even_more.at[0], even_more.at[1]]
    for u in (margin - 1, margin):
        weight = (fx[u][...] + fx[u - 1][...]) + (fy[u][body] + fy[u][plane.down]) + (fz[u][...] + fzl[u][...])
        inv[u][...] = 1.0 / (1.0 + weight)

    def around(ref, u):
        return in_layer(plane, fy[u], fz[u], fzl[u], ref[u])

    u = margin - 1
    total = s(u) + around(old, u) + (fx[u][...] * old[u + 1][body] + fx[u - 1][...] * old[u - 1][body])
    plane.put(even[u], total * inv[u][...])
    plane.put(even[margin], (part(2) + fx[u][...] * old[u][body]) * inv[margin][...])
    for u in range(2, margin + 1):
        if u < margin:
            total = s(u) + around(even, u) + (fx[u][...] * even[u + 1][body] + fx[u - 1][...] * even[u - 1][body])
        else:
            total = part(2) + around(even, u) + fx[u - 1][...] * even[u - 1][body]
        fresh = total * inv[u][...]
        new[u - 2] = fresh
        plane.put(change.at[u - 2], fresh - old[u][body])
    change = {u: change.at[u - 2] for u in range(2, margin + 1)}

    one = fx[1][...] * change[2][body]
    two = around(change, 2) + fx[2][...] * change[3][body]
    three = around(change, 3) + (fx[2][...] * change[2][body] + fx[3][...] * change[4][body])
    outer = jnp.where(plane.even(1), one, 0.0)
    inner = jnp.where(plane.even(2), two, 0.0) + jnp.where(plane.even(3), three, 0.0)
    core = core_of()

    def tile(name, outer, inner):
        message[places[name], :] = plane.packed(outer, inner, core)

    tile("source2", plane.summed(outer, turn.at[1]), plane.summed(inner, turn.at[2]))
    tile("fx2", plane.summed(fx[1][...], turn.at[3]), plane.summed(fx[3][...], turn.at[4]))
    fy2 = [plane.odd_rows(fy[u][body] + fy[u + 1][body], turn.at[5 + u // 2]) for u in (0, 2)]
    fz2 = [plane.odd_lanes(fz[u][...] + fz[u + 1][...], turn.at[7 + u // 2]) for u in (0, 2)]
    own2[0], own2[1] = plane.packed(*fy2, core), plane.packed(*fz2, core)
    tile("far2", fy2[1], fz2[1])
    for u in range(2):
        message[places["coef%d" % u], :] = cell[u]
    first = s(0) + around(old, 0) + fx[0][...] * old[1][body]
    second = s(0) + fx[0][...] * even[1][body]
    message[places["known0"], :] = jnp.where(plane.even(0), first, second)
    message[places["old0"], :] = odd_cells(iterate.at[own_layer(0, layers)], half, plane.odd_first(0))
    total = s(1) + around(even, 1) + fx[1][...] * even[2][body]
    known1[...] = total
    turn[9] = total * inv[1][...] - old[1][body]
    message[places["moved1"], :] = odd_cells(turn.at[9], half, plane.odd_first(1))
    message[places["face2"], :] = odd_cells(fx[1], half, plane.odd_first(1))


def border_kernel(
    inputs, message, own2, known1, new_in, fx_in, fy_in, fz_in, fzl_in, inv_in, across_in,
    within, fx2_in, new, known, fx, fy, fz, fzl, inv,
    old, even, change, turn, face_y, face_z, face_zl,
):
    iterate, source, _ = three_parts(inputs)
    layers, height, depth = iterate.shape
    plane = Plane(height, depth)
    body, half = plane.body, plane.half
    places, _ = chip_rows(height)
    core, last = core_of(), lax.axis_size("gx") - 1
    position = lax.axis_index("gx")

    def mine(name):
        return message[places[name], :]

    def theirs(name):
        return across_in[places[name], :]

    def opened(name, k):
        into_both_rows(turn.at[k], theirs(name))
        return turn[k]

    for k in range(2):
        here = theirs("coef%d" % k)
        plane.put(face_y.at[k], plane.face_y(here))
        face = plane.face_z(here)
        face_z[k] = face
        face_zl[k] = behind(face, 1, 1)
    fy[...], fz[...], fzl[...] = face_y[0], face_z[0], face_zl[0]
    there = position - 1 + 2 * core
    border = jnp.where((there >= 0) & (there <= last), 0.5 * (mine("coef0") + theirs("coef0")), 0.0)
    face1 = 0.5 * (theirs("coef0") + theirs("coef1"))
    face2 = opened("face2", 2)
    fx[0], fx[1] = border, face1

    def inverse(faces, fy, fz, fzl):
        weight = faces + (fy[body] + fy[plane.down]) + (fz[...] + fzl[...])
        return 1.0 / (1.0 + weight)

    inv_own = inverse(fx_in[0] + border, fy_in.at[0], fz_in.at[0], fzl_in.at[0])
    inv_near = inverse(border + face1, face_y.at[0], face_z.at[0], face_zl.at[0])
    inv_far = inverse(face1 + face2, face_y.at[1], face_z.at[1], face_zl.at[1])
    inv[0], inv[1] = inv_near, inv_own
    old_own, old_next = iterate[own_layer(0, layers)], iterate[own_layer(1, layers)]
    old_near, far = opened("old0", 0), opened("moved1", 1)
    even_own = (mine("known0") + border * old_near) * inv_own
    even_near = (theirs("known0") + border * old_own) * inv_near
    plane.put(even.at[0], even_near)
    plane.put(even.at[1], even_own)

    def near(ref, k):
        return in_layer(plane, face_y.at[k], face_z.at[k], face_zl.at[k], ref)

    def own(ref, u):
        return in_layer(plane, fy_in.at[u], fz_in.at[u], fzl_in.at[u], ref)

    odd_own = (mine("known0") + own(even.at[1], 0) + border * even_near) * inv_own
    odd_near = (theirs("known0") + near(even.at[0], 0) + border * even_own) * inv_near
    odd_next = (known1[...] + fx_in[0] * even_own) * inv_in[0]
    far = far + face1 * even_near * inv_far
    new[0], new[1], new[2] = odd_near, odd_own, odd_next
    near_by, here, following = odd_near - old_near, odd_own - old_own, odd_next - old_next
    for k, values in enumerate((far, near_by, here, following)):
        plane.put(change.at[k], values)
    plane.put(old.at[0], old_near)
    known[...] = theirs("known0") + face1 * far - near(old.at[0], 0)

    def residual(u, values):
        return jnp.where(plane.even(u), values, 0.0)

    own_outer = residual(1, own(change.at[3], 1) + fx_in[0] * here)
    own_outer = own_outer + residual(0, own(change.at[2], 0) + (fx_in[0] * following + border * near_by))
    own_inner = residual(2, fx_in[1] * following)
    its_outer = residual(-1, near(change.at[1], 0) + (face1 * far + border * here))
    its_outer = its_outer + residual(-2, near(change.at[0], 1) + face1 * near_by)
    its_inner = residual(-3, face2 * far)
    sums = [plane.summed(values, turn.at[3 + k]) for k, values in enumerate((own_outer, own_inner, its_outer, its_inner))]
    within[0] = mine("source2") + plane.packed(sums[0], sums[1], core)
    within[5] = theirs("source2") + plane.packed(sums[2], sums[3], 1 - core)
    within[6] = theirs("fx2")
    far2 = theirs("far2")
    far2_swap = jnp.where((plane.half_lane & 1) == 0, ahead(far2, 1, 1), behind(far2, 1, 1))
    near_fy2 = plane.odd_rows(face_y[0, body] + face_y[1, body], turn.at[1])
    near_fz2 = plane.odd_lanes(face_z[0] + face_z[1], turn.at[2])
    within[7] = plane.packed(near_fy2, far2_swap, 1 - core)
    within[8] = plane.packed(near_fz2, far2, 1 - core)
    fx2_in[...] = mine("fx2")
    middle = jnp.where((plane.half_lane & 1) == 0, ahead(mine("fx2"), 1, 1), behind(mine("fx2"), 1, 1))
    within[1] = plane.packed(plane.summed(border, turn.at[7]), middle, core)
    within[2], within[3] = own2[0], own2[1]
    turn[0] = source[own_layer(layers - 1, layers)] + fx_in[layers - 2] * new_in[layers - 4]
    within[4] = odd_cells(turn.at[0], half, jnp.logical_not(plane.odd_first(layers - 1)))


def neigh2(e2, fx2, fxl2, fy2, fz2, fzl2, first_of_two, tiles):
    half = fx2.shape[1]
    body, up, down = pl.ds(PAD, half), pl.ds(PAD + 1, half), pl.ds(PAD - 1, half)
    needed = range(tiles[0], tiles[-1] + 3)
    here = {j: e2[j, body] for j in needed}
    after = {j: ahead(here[j], 1, 1) for j in needed}
    before = {j: behind(here[j], 1, 1) for j in needed}
    found = []
    for j in tiles:
        k = j + 1
        upper = jnp.where(first_of_two, after[k], before[k + 1])
        lower = jnp.where(first_of_two, after[k - 1], before[k])
        sums = fx2[j] * upper + fxl2[j] * lower
        sums = sums + fy2[j, body] * e2[k, up] + fy2[j, down] * e2[k, down]
        sums = sums + fz2[j] * ahead(here[k], 2, 1) + fzl2[j] * behind(here[k], 2, 1)
        found.append(sums)
    return found


def parities2(half, lanes):
    row, lane = rows_of((half, lanes)), lanes_of((half, lanes))
    return (lane & 1) == 0, ((row + (lane & 1) + (lane >> 1)) & 1) == 0


def group(values):
    return with_partner(with_partner(values, 1, 1), 2, 1)


def packed_odd(values, pair):
    half, lanes = values.shape
    lane = lanes_of((half // 2, lanes))
    pair[...] = values
    return odd_cells(pair, half // 2, (((lane & 1) + (lane >> 1)) & 1) != 0)


def middle_down_kernel(
    own, fx2_in, within_in,
    slots, e2_out, s2, fx2, fxl2, fy2, fz2, fzl2, inv2,
    e2, pair,
):
    _, half, lanes = own.shape
    quarter = half // 2
    first_of_two, even2 = parities2(half, lanes)
    body, down = pl.ds(PAD, half), pl.ds(PAD - 1, half)
    edge = jnp.zeros((PAD, lanes), jnp.float32)
    for j in (0, 5):
        e2[j] = jnp.zeros((half + 2 * PAD, lanes), jnp.float32)

    def pair_of(k):
        return by_side(own[k], within_in[k])

    def four(k):
        (left, right), (far_left, far_right) = pair_of(k), pair_of(5 + k)
        return far_left, left, right, far_right

    for j, (source, fy, fz) in enumerate(zip(four(0), four(2), four(3))):
        s2[j] = source
        fy2[j, :PAD] = edge
        fy2[j, body] = fy
        fy2[j, PAD + half:] = edge
        fz2[j] = fz
        fzl2[j] = behind(fz, 2, 1)

    def between(left, right):
        return jnp.where(first_of_two, ahead(left, 1, 1), behind(right, 1, 1))

    fxl0, fxl1, fxr2, fxr3 = four(1)
    inner = fx2_in[...]
    fxr1, _ = by_side(inner, between(fxl1, inner))
    fxl2_, _ = by_side(between(inner, fxr2), inner)
    for j, (face, low) in enumerate(
        ((between(fxl0, fxl1), fxl0), (fxr1, fxl1), (fxr2, fxl2_), (fxr3, between(fxr2, fxr3)))
    ):
        fx2[j], fxl2[j] = face, low
        weight = face + low + fy2[j, body] + fy2[j, down] + fz2[j] + fzl2[j]
        inverse = 1.0 / (8.0 + weight)
        inv2[j] = inverse
        e2[j + 1, :PAD] = edge
        e2[j + 1, PAD + half:] = edge
        e2[j + 1, body] = s2[j] * inverse

    def neigh(tiles):
        return neigh2(e2, fx2, fxl2, fy2, fz2, fzl2, first_of_two, tiles)

    fresh = [(s2[j] + sums) * inv2[j] for j, sums in enumerate(neigh((0, 1, 2, 3)))]
    for j in range(4):
        e2[j + 1, body] = fresh[j]
        e2_out[j] = fresh[j]
    lane = lanes_of((quarter, lanes))
    odd_layer, odd_depth = (lane & 1) != 0, (lane & 2) != 0
    chips = slots.shape[0]
    for k, sums in enumerate(neigh((1, 2))):
        j = k + 1
        pair[k] = jnp.where(even2, sums, 0.0)
        item = (lane - (lax.axis_index("gx") // 2 * 2 + k) // (chips // 2)) & 3
        source = group(even_row_sum(pair.at[k], quarter))
        fx = group(jnp.where(odd_layer, even_row_sum(fx2.at[j], quarter), 0.0))
        fxl = group(jnp.where(odd_layer, 0.0, even_row_sum(fxl2.at[j], quarter)))
        fy = group(fy2[j, pl.ds(PAD + 1, quarter, 2), :])
        fz = group(jnp.where(odd_depth, even_row_sum(fz2.at[j], quarter), 0.0))
        weight = (fx + fxl) + (fy + behind(fy, 1, 0)) + (fz + behind(fz, 4, 1))
        start = source / (64.0 + weight)
        tile = jnp.where(item == 0, start, jnp.where(item == 1, fx, jnp.where(item == 2, fy, fz)))
        for c in range(chips):
            slots[c, k] = tile
    halo = packed_odd(jnp.where(first_of_two, fresh[2], fresh[1]), pair.at[2])
    for c in range(chips):
        slots[c, 2] = halo


def joined(one, two):
    return jnp.concatenate([part for part in (one, two) if part.shape[0]], 0)


class Level:
    def __init__(self, mass, source, faces, row_step, lane_step, slot_step):
        self.source, self.row_step, self.lane_step, self.slot_step = source, row_step, lane_step, slot_step
        self.fx, self.fy, self.fz = faces
        self.tiles = source.shape[0]
        shape = source.shape
        self.lane = lanes_of(shape)
        layer = lax.broadcasted_iota(jnp.int32, shape, 0) if self.tiles > 1 else self.lane // slot_step
        self.even = ((layer + rows_of(shape) // row_step + self.lane // lane_step) & 1) == 0
        self.fxl = self.lower(self.fx)
        self.fyl = self.row_shifts(self.fy)[1]
        self.fzl = behind(self.fz, lane_step, 2)
        weight = (self.fx + self.fxl) + (self.fy + self.fyl) + (self.fz + self.fzl)
        self.inv = 1.0 / (mass + weight)

    def upper(self, e):
        return joined(e[1:], ahead(e[:1], self.slot_step, 2))

    def lower(self, e):
        return joined(behind(e[-1:], self.slot_step, 2), e[:-1])

    def row_shifts(self, e):
        return ahead(e, self.row_step, 1), behind(e, self.row_step, 1)

    def neigh(self, e):
        above, below = self.row_shifts(e)
        total = (self.fx * self.upper(e) + self.fxl * self.lower(e)) + (self.fy * above + self.fyl * below)
        return total + (self.fz * ahead(e, self.lane_step, 2) + self.fzl * behind(e, self.lane_step, 2))

    def start(self):
        return self.source * self.inv

    def update(self, e):
        return self.start() + self.neigh(e) * self.inv

    def cycle(self, deeper):
        odd = self.update(self.start())
        residual = jnp.where(self.even, self.neigh(odd), 0.0)
        fix = deeper(self.restricted(residual), self.coarse_faces())
        even = self.update(odd + self.prolonged(fix))
        return jnp.where(self.even, even, self.update(even))

    def coarse_slot_step(self):
        return self.slot_step if self.tiles > 1 else 2 * self.slot_step

    def pairs(self, values):
        if self.tiles == 1:
            return with_partner(values, self.slot_step, 2)
        halves = values.reshape(self.tiles // 2, 2, *values.shape[1:])
        return halves[:, 0] + halves[:, 1]

    def odd_layers(self, values):
        if self.tiles == 1:
            return with_partner(jnp.where((self.lane & self.slot_step) != 0, values, 0.0), self.slot_step, 2)
        return values.reshape(self.tiles // 2, 2, *values.shape[1:])[:, 1]

    def row_pairs(self, values):
        return with_partner(values, self.row_step, 1)

    def odd_rows(self, values):
        odd = (rows_of(values.shape) & self.row_step) != 0
        return with_partner(jnp.where(odd, values, 0.0), self.row_step, 1)

    def restricted(self, values):
        return with_partner(self.row_pairs(self.pairs(values)), self.lane_step, 2)

    def coarse_faces(self):
        fx = with_partner(self.row_pairs(self.odd_layers(self.fx)), self.lane_step, 2)
        fy = with_partner(self.odd_rows(self.pairs(self.fy)), self.lane_step, 2)
        return fx, fy, self.restricted(jnp.where((self.lane & self.lane_step) != 0, self.fz, 0.0))

    def prolonged(self, fix):
        if self.tiles == 1:
            return fix
        both = jnp.concatenate([fix[:, None], fix[:, None]], 1)
        return both.reshape(self.tiles, *fix.shape[1:])


class Rows(Level):
    def __init__(self, mass, source, faces, scratch):
        self.scratch, self.used = scratch, 0
        self.rows = source.shape[1]
        super().__init__(mass, source, faces, 1, 4, 1)

    def start(self):
        return self.source

    def place(self):
        self.used += 1
        return self.scratch.at[self.used % self.scratch.shape[0]]

    def row_shifts(self, e):
        place = self.place()
        edge = jnp.zeros((e.shape[0], PAD, e.shape[2]), jnp.float32)
        place[:, :PAD] = edge
        place[:, PAD + self.rows:] = edge
        place[:, pl.ds(PAD, self.rows)] = e
        return place[:, pl.ds(PAD + 1, self.rows)], place[:, pl.ds(PAD - 1, self.rows)]

    def every_other(self, values, starts):
        place, tiles = self.place(), values.shape[0]
        place[:tiles, : self.rows] = values
        found = 0.0
        for start in starts:
            found = found + jnp.concatenate(
                [place[j, pl.ds(start, self.rows // 2, 2), :][None] for j in range(tiles)], 0
            )
        return found

    def row_pairs(self, values):
        return self.every_other(values, (0, 1))

    def odd_rows(self, values):
        return self.every_other(values, (1,))

    def prolonged(self, fix):
        place, tiles = self.place(), fix.shape[0]
        for j in range(tiles):
            into_both_rows(place.at[j, pl.ds(0, self.rows)], fix[j])
        return super().prolonged(place[:tiles, : self.rows])


def coarsest(mass, source, faces, *steps):
    row_step, lane_step, slot_step = steps
    level = Level(mass, source, faces, *steps)
    counts = source.shape[1] // row_step, source.shape[2] // lane_step, 4 // slot_step
    frames = [(m, k, q) for m in range(counts[0]) for k in range(counts[1]) for q in range(counts[2])]
    place = level.lane & 3

    def spread(values):
        copies = {}
        for m, k, q in frames:
            if k:
                copies[m, k, q] = behind(copies[m, 0, q], k * lane_step, 2)
            elif q:
                by = q * slot_step
                one, two = behind(copies[m, 0, 0], by, 2), ahead(copies[m, 0, 0], 4 - by, 2)
                copies[m, k, q] = jnp.where(place >= by, one, two)
            else:
                copies[m, k, q] = behind(values, m * row_step, 1) if m else values
        return copies

    start, inv, fx, fy, fz = [spread(values) for values in (source * level.inv, level.inv, level.fx, level.fy, level.fz)]

    def shifted(copies, frame, axis, by):
        moved = list(frame)
        moved[axis] = (frame[axis] - by) % counts[axis]
        return copies[tuple(moved)]

    def along_x(copies, frame, by):
        here, wrapped = copies[frame], shifted(copies, frame, 2, by)
        return joined(here[1:], wrapped[:1]) if by > 0 else joined(wrapped[-1:], here[:-1])

    weights = {}
    for frame in frames:
        pairs = [
            (fx[frame], along_x(fx, frame, -1)),
            (fy[frame], shifted(fy, frame, 0, -1)),
            (fz[frame], shifted(fz, frame, 1, -1)),
        ]
        weights[frame] = [(up * inv[frame], low * inv[frame]) for up, low in pairs]

    def update(e):
        fresh = {}
        for frame in frames:
            (x_up, x_low), (y_up, y_low), (z_up, z_low) = weights[frame]
            total = x_up * along_x(e, frame, 1) + x_low * along_x(e, frame, -1)
            total = total + (y_up * shifted(e, frame, 0, 1) + y_low * shifted(e, frame, 0, -1))
            total = total + (z_up * shifted(e, frame, 1, 1) + z_low * shifted(e, frame, 1, -1))
            fresh[frame] = start[frame] + total
        return fresh

    even = start
    odd = update(even)
    for turn in range(COARSE_SWEEPS - 1):
        even = update(odd)
        odd = update(even)
    return jnp.where(level.even, even[0, 0, 0], odd[0, 0, 0])


def small_cycle(mass, source, faces, row_step, lane_step, slot_step, between):
    if between == 0:
        return coarsest(mass, source, faces, row_step, lane_step, slot_step)
    level = Level(mass, source, faces, row_step, lane_step, slot_step)
    return level.cycle(
        lambda inner, inner_faces: small_cycle(
            8.0 * mass, inner, inner_faces, 2 * row_step, 2 * lane_step, level.coarse_slot_step(), between - 1
        )
    )


def coarse_kernel(
    owner_of, gathered, e2_in, s2_in, fx2_in, fxl2_in, fy2_in, fz2_in, fzl2_in, inv2_in,
    inputs, new_in, fx_more, fy_margin, fz_margin, fzl_margin, inv_more, fx_in, fy_in, fz_in, fzl_in, inv_in,
    new_out, known_out, fx_out, fy_out, fz_out, fzl_out, inv_out, within_in,
    solved_out, owned_out,
    e3, rows3, pair, e2, e1, cor, solved, owned, owner_here, fetch_sem, sems,
):
    fetch = pltpu.make_async_copy(owner_of, owner_here, fetch_sem)
    fetch.start()
    chips, _, quarter, lanes = gathered.shape
    blocks = 2 * chips
    half, height = 2 * quarter, 4 * quarter
    position, last = lax.axis_index("gx"), blocks - 1

    slot = lanes_of((quarter, lanes)) & 3
    spread = blocks // 4
    downwards = (position // 2 + position) % 2

    def place(chip):
        return chip + downwards * (chips - 1 - 2 * chip)

    tiles = [gathered[place(chip), k] for chip in range(chips) for k in range(2)]
    items = []
    for k in range(4):
        packs = []
        for j in range(spread):
            value = tiles[j + (3 - k) % 4 * spread]
            for at in range(3):
                value = jnp.where(slot == at, tiles[j + (at - k) % 4 * spread], value)
            if k:
                value = jnp.where(slot < 4 - k, ahead(value, k, 1), behind(value, 4 - k, 1))
            packs.append(value[None])
        items.append(jnp.concatenate(packs, 0))
    third = Rows(64.0, items[0], items[1:], rows3)
    e3[...] = third.cycle(
        lambda inner, faces: small_cycle(512.0, inner, faces, 1, 8, third.coarse_slot_step(), 2)
    )

    fetch.wait()
    owner = owner_here[position]
    wide, narrow = lanes_of((lanes, lanes)), rows_of((lanes, lanes))
    take = jnp.where(narrow == 4 * wide + owner // spread, 1.0, 0.0)
    block = jnp.dot(
        e3[owner % spread], take, precision=lax.Precision.HIGHEST, preferred_element_type=jnp.float32
    )
    owned[0] = block[:, : lanes // 4]
    copies = [pltpu.make_async_copy(owned, owned_out, sems.at[0])]
    copies[0].start()

    first_of_two, even2 = parities2(half, lanes)
    body2 = pl.ds(PAD, half)
    edge = jnp.zeros((PAD, lanes), jnp.float32)
    core = core_of()
    s2, fx2, fxl2, fy2, fz2, fzl2, inv2 = [
        ref.at[pl.ds(core, 3)] for ref in (s2_in, fx2_in, fxl2_in, fy2_in, fz2_in, fzl2_in, inv2_in)
    ]
    next_chip = jnp.clip(position // 2 - 1 + 2 * core, 0, chips - 1)
    into_both_rows(pair.at[5], gathered[place(next_chip), 2])
    halo = pair[5]
    before = (
        by_side(halo, e2_in[0])[0], by_side(jnp.where(first_of_two, halo, e2_in[0]), e2_in[1])[0],
        by_side(e2_in[1], e2_in[2])[0],
        by_side(e2_in[2], jnp.where(first_of_two, e2_in[3], halo))[0], by_side(e2_in[3], halo)[0],
    )
    for k in range(5):
        j = jnp.clip(position + k - 2, 0, last)
        into_both_rows(pair.at[k], group(jnp.where(slot == j // spread, e3[j % spread], 0.0)))
        e2[k, :PAD] = edge
        e2[k, PAD + half:] = edge
        e2[k, body2] = before[k] + pair[k]

    def update2():
        sums = neigh2(e2, fx2, fxl2, fy2, fz2, fzl2, first_of_two, (0, 1, 2))
        return [(s2[j] + sums[j]) * inv2[j] for j in range(3)]

    fresh = update2()
    for j in range(3):
        e2[j + 1, body2] = fresh[j]
    fixes2 = [jnp.where(even2, even, odd) for even, odd in zip(fresh, update2())]

    _, source, _ = three_parts(inputs)
    layers = source.shape[0]
    plane = Plane(height, lanes)
    body1 = plane.body
    near_lane = (lanes_of((half, lanes)) & 1) == core
    swaps = [jnp.where(first_of_two, ahead(v, 1, 1), behind(v, 1, 1)) for v in fixes2]
    outer, inner = by_side(fixes2[0], fixes2[2])
    outer_swap, inner_swap = by_side(swaps[0], swaps[2])
    coarse = (
        jnp.where(near_lane, outer_swap, outer), jnp.where(near_lane, fixes2[1], swaps[1]),
        jnp.where(near_lane, swaps[1], fixes2[1]), jnp.where(near_lane, inner, inner_swap),
    )
    fixes = []
    for k in range(4):
        into_both_rows(cor.at[k], coarse[k])
        fixes.append(cor[k])
    for u in range(-1, layers + 1):
        before = new_out[u + 1] if u < 2 else new_in[u - 2]
        plane.put(e1.at[u + 1], before + fixes[(u + 2) // 2])

    def fx1(u):
        if u < 0:
            return fx_out[-1 - u]
        return fx_in[u] if u < layers - 1 else fx_more[u - layers + 1]

    def inv1(u):
        if u <= 0:
            return inv_out[u + 1]
        return inv_in[u - 1] if u < layers - 1 else inv_more[u - layers + 1]

    def around1(u):
        if u < 0:
            return in_layer(plane, fy_out, fz_out, fzl_out, e1.at[0])
        if u == layers:
            return in_layer(plane, fy_margin, fz_margin, fzl_margin, e1.at[u + 1])
        return in_layer(plane, fy_in.at[u], fz_in.at[u], fzl_in.at[u], e1.at[u + 1])

    def updated1(u):
        sums = around1(u) + (fx1(u) * e1[u + 2, body1] + fx1(u - 1) * e1[u, body1])
        return (source[own_layer(u, layers)] + sums) * inv1(u)

    for u in range(layers):
        e1[u + 1, body1] = jnp.where(plane.even(u), updated1(u), e1[u + 1, body1])
    e1[0, body1] = (known_out[...] + fx1(-2) * fixes[0] + (around1(-1) + fx1(-1) * e1[1, body1])) * inv1(-1)
    into_both_rows(cor.at[4], within_in[4])
    sums = cor[4] + fx1(layers) * fixes[3] + (around1(layers) + fx1(layers - 1) * e1[layers, body1])
    e1[layers + 1, body1] = sums * inv1(layers)
    for u in range(layers):
        solved[u] = jnp.where(plane.even(u), e1[u + 1, body1], updated1(u))
        copies.append(
            pltpu.make_async_copy(solved.at[u], solved_out.at[own_layer(u, layers)], sems.at[u + 1])
        )
        copies[-1].start()
    for copy in copies:
        copy.wait()


def f32(*shape):
    return jax.ShapeDtypeStruct(shape, jnp.float32)


def vmem(*shape):
    return pltpu.VMEM(shape, jnp.float32)


def call(kernel, outs, scratch, operands, out_space=pltpu.VMEM):
    def size(shape):
        count = 4
        for extent in shape:
            count *= extent
        return count

    sized = [array for array in (*scratch, *outs, *operands) if hasattr(array, "shape")]
    asked = 8 * 2**20 + sum(size(array.shape) for array in sized)
    return pl.pallas_call(
        kernel,
        out_shape=tuple(outs),
        in_specs=[pl.BlockSpec(memory_space=pltpu.VMEM)] * len(operands),
        out_specs=tuple([pl.BlockSpec(memory_space=out_space)] * len(outs)),
        scratch_shapes=scratch,
        compiler_params=pltpu.CompilerParams(vmem_limit_bytes=asked),
    )(*operands)


def on_device(iterate, source, phase_field, block_owner):
    layers, height, depth = iterate.shape
    half, quarter = height // 2, height // 4
    blocks = lax.axis_size("gx")
    padded, padded2 = height + 2 * PAD, half + 2 * PAD
    inputs = sum(
        jnp.pad(block, ((k * layers, (2 - k) * layers), (0, 0), (0, 0)))
        for k, block in enumerate((iterate, source, phase_field))
    )
    edge, = call(edge_kernel, [f32(3 * height + half, depth)], [], (inputs,))
    edge_in = within_chip(edge)
    layer, tile, tall = (height, depth), (half, depth), (padded, depth)
    cell, old, *fine, even = call(
        own_kernel,
        [
            f32(layers, *layer), f32(layers, *tall), f32(layers - 1, *layer), f32(layers, *tall),
            f32(layers, *layer), f32(layers, *layer), f32(2, *layer), f32(2, *tall),
        ],
        [], (block_owner, inputs),
    )
    message, own2, known1, new, *margin = call(
        chip_kernel,
        [
            f32(chip_rows(height)[1], depth), f32(2, *tile), f32(*layer), f32(3, *layer),
            f32(2, *layer), f32(*tall), f32(*layer), f32(*layer), f32(2, *layer),
        ],
        [vmem(*tall), vmem(2, *tall), vmem(3, *tall), vmem(10, *layer)],
        (inputs, cell, old, *fine, even, edge_in),
    )
    within, fx2, *border = call(
        border_kernel,
        [
            f32(9, *tile), f32(*tile), f32(3, *layer), f32(*layer), f32(2, *layer),
            f32(padded, depth), f32(*layer), f32(*layer), f32(2, *layer),
        ],
        [
            vmem(1, padded, depth), vmem(2, padded, depth), vmem(4, padded, depth), vmem(8, *layer),
            vmem(2, padded, depth), vmem(2, *layer), vmem(2, *layer),
        ],
        (inputs, message, own2, known1, new, *fine, between_chips(message)),
    )
    within_in = within_chip(within)
    plain = f32(4, *tile)
    slots, *middle = call(
        middle_down_kernel,
        [f32(blocks // 2, 3, quarter, depth), plain, plain, plain, plain, f32(4, padded2, depth)] + [plain] * 3,
        [vmem(6, padded2, depth), vmem(3, *tile)],
        (within, fx2, within_in),
    )
    up = [2 * chip + chip % 2 for chip in range(blocks // 2)]
    down = [device ^ 1 for device in reversed(up)]
    kinds = [up, down]
    gathered = lax.all_to_all(slots, "gx", 0, 0, axis_index_groups=kinds, tiled=True)
    solved, owned = call(
        coarse_kernel,
        [f32(layers, *layer), f32(1, quarter, depth // 4)],
        [
            vmem(blocks // 4, quarter, depth), vmem(4, blocks // 4, quarter + 2 * PAD, depth), vmem(7, *tile),
            vmem(5, padded2, depth), vmem(layers + 2, padded, depth), vmem(5, *layer), vmem(layers, *layer),
            vmem(1, quarter, depth // 4), pltpu.SMEM((blocks,), jnp.int32),
            pltpu.SemaphoreType.DMA, pltpu.SemaphoreType.DMA((layers + 1,)),
        ],
        (block_owner, gathered, *middle, inputs, new, *margin, *fine, *border, within_in),
        pl.ANY,
    )
    return solved, owned


def solution(mesh):
    split = P(("groups", "gx"), None, None)
    return jax.shard_map(
        on_device,
        mesh=mesh,
        in_specs=(split, split, split, P("groups")),
        out_specs=(split, split),
        check_vma=False,
    )
```

```python
import jax
import jax.numpy as jnp
from jax import lax
from jax.experimental import pallas as pl
from jax.experimental.pallas import tpu as pltpu
from jax.sharding import PartitionSpec as P

STIFFNESS = 100.0
EPSILON = 0.01
COARSE_SWEEPS = 4
PAD = 8


def between_chips(block):
    return lax.ppermute(block, "gx", [(i, i + 1 if i % 2 else i - 1) for i in range(1, lax.axis_size("gx") - 1)])


def within_chip(block):
    return lax.ppermute(block, "gx", [(i, i ^ 1) for i in range(lax.axis_size("gx"))])


def chip_order(chips, kind):
    return [-(1, 3)[kind] * i % chips for i in range(chips)]


def by_side(across, within):
    on_left = lax.axis_index("gx") % 2 == 0
    return jnp.where(on_left, across, within), jnp.where(on_left, within, across)


def lanes_of(shape):
    return lax.broadcasted_iota(jnp.int32, shape, len(shape) - 1)


def rows_of(shape):
    return lax.broadcasted_iota(jnp.int32, shape, len(shape) - 2)


def ahead(values, step, axis):
    return pltpu.roll(values, values.shape[axis] - step, axis)


def behind(values, step, axis):
    return pltpu.roll(values, step, axis)


def with_partner(values, step, axis):
    index = lax.broadcasted_iota(jnp.int32, values.shape, axis)
    partner = jnp.where((index & step) == 0, ahead(values, step, axis), behind(values, step, axis))
    return values + partner


def even_row_sum(scratch, rows):
    return scratch[pl.ds(0, rows, 2), :] + scratch[pl.ds(1, rows, 2), :]


def core_of():
    return lax.axis_index("gx") % 2


def own_layer(u, layers):
    return u + core_of() * (layers - 1 - 2 * u)


def three_parts(ref):
    third = ref.shape[0] // 3
    return [ref.at[pl.ds(k * third, third)] for k in range(3)]


def odd_cells(ref, rows, first):
    return jnp.where(first, ref[pl.ds(0, rows, 2), :], ref[pl.ds(1, rows, 2), :])


def into_both_rows(ref, values):
    rows = values.shape[0]
    ref[pl.ds(0, rows, 2), :] = values
    ref[pl.ds(1, rows, 2), :] = values


def cell_coef(value):
    return STIFFNESS * (value * value + EPSILON)


class Plane:
    def __init__(self, height, depth):
        self.height, self.half, self.depth = height, height // 2, depth
        self.row, self.lane = rows_of((height, depth)), lanes_of((height, depth))
        self.parity = self.row + self.lane + core_of()
        self.half_lane = lanes_of((self.half, depth))
        self.body = pl.ds(PAD, height)
        self.up, self.down = pl.ds(PAD + 1, height), pl.ds(PAD - 1, height)

    def even(self, u):
        return ((self.parity + u) & 1) == 0

    def odd_first(self, u):
        return ((self.half_lane + core_of() + u) & 1) != 0

    def put(self, ref, values):
        edge = jnp.zeros((PAD, self.depth), jnp.float32)
        ref[:PAD] = edge
        ref[PAD + self.height:] = edge
        ref[self.body] = values

    def face_y(self, here):
        return jnp.where(self.row < self.height - 1, 0.5 * (here + ahead(here, 1, 0)), 0.0)

    def face_z(self, here):
        return jnp.where(self.lane < self.depth - 1, 0.5 * (here + ahead(here, 1, 1)), 0.0)

    def packed(self, outer, inner, core):
        return jnp.where((self.half_lane & 1) == core, outer, inner)

    def both_rows(self, ref):
        return even_row_sum(ref, self.half)

    def summed(self, values, ref):
        ref[...] = values
        return with_partner(self.both_rows(ref), 1, 1)

    def odd_rows(self, values, ref):
        ref[...] = values
        return with_partner(ref[pl.ds(1, self.half, 2), :], 1, 1)

    def odd_lanes(self, values, ref):
        ref[...] = values
        sums = self.both_rows(ref)
        return jnp.where((self.half_lane & 1) == 0, ahead(sums, 1, 1), sums)


def in_layer(plane, fy, fz, fzl, padded):
    here = padded[plane.body]
    total = fy[plane.body] * padded[plane.up] + fy[plane.down] * padded[plane.down]
    return total + (fz[...] * ahead(here, 1, 1) + fzl[...] * behind(here, 1, 1))


def edge_kernel(inputs, out):
    iterate, source, phase = three_parts(inputs)
    layers, height, depth = iterate.shape
    plane = Plane(height, depth)
    near, inner, far = [own_layer(u, layers) for u in (layers - 1, layers - 2, layers - 3)]
    coef_near, coef_inner, coef_far = [cell_coef(phase[k]) for k in (near, inner, far)]

    def around(here, e):
        fy, fz = plane.face_y(here), plane.face_z(here)
        fyl, fzl = behind(fy, 1, 0), behind(fz, 1, 1)
        total = fy * ahead(e, 1, 0) + fyl * behind(e, 1, 0)
        return total + fz * ahead(e, 1, 1) + fzl * behind(e, 1, 1), fy + fyl + fz + fzl

    face_near, face_far = 0.5 * (coef_inner + coef_near), 0.5 * (coef_inner + coef_far)
    total, weight = around(coef_inner, iterate[inner])
    total = total + face_near * iterate[near] + face_far * iterate[far]
    updated = (source[inner] + total) / (1.0 + (face_near + face_far + weight))
    total, _ = around(coef_near, iterate[near])
    known = jnp.where(plane.even(layers - 1), total + face_near * iterate[inner], face_near * updated)
    out[:height] = coef_near
    out[height:2 * height] = coef_inner
    out[2 * height:3 * height] = source[near] + known
    out[3 * height:] = odd_cells(iterate.at[near], plane.half, plane.odd_first(layers - 1))


def chip_rows(height):
    half, at, places = height // 2, 0, {}
    for name, size in (
        ("coef0", height), ("coef1", height), ("known0", height), ("old0", half), ("moved1", half), ("face2", half),
        ("source2", half), ("fx2", half), ("far2", half),
    ):
        places[name] = pl.ds(at, size)
        at += size
    return places, at


def own_kernel(owner_of, inputs, cell, old, fx, fy, fz, fzl, inv, even):
    iterate, source, phase = three_parts(inputs)
    layers, height, depth = iterate.shape
    plane = Plane(height, depth)
    body = plane.body
    for u in range(layers):
        cell[u] = cell_coef(phase[own_layer(u, layers)])
        plane.put(old.at[u], iterate[own_layer(u, layers)])
    for u in range(layers):
        here = cell[u]
        if u < layers - 1:
            fx[u] = 0.5 * (here + cell[u + 1])
        plane.put(fy.at[u], plane.face_y(here))
        face = plane.face_z(here)
        fz[u] = face
        fzl[u] = behind(face, 1, 1)
    for u in (1, 2):
        weight = (fx[u] + fx[u - 1]) + (fy[u, body] + fy[u, plane.down]) + (fz[u] + fzl[u])
        inverse = 1.0 / (1.0 + weight)
        inv[u - 1] = inverse
        around = in_layer(plane, fy.at[u], fz.at[u], fzl.at[u], old.at[u])
        total = source[own_layer(u, layers)] + around + (fx[u] * old[u + 1, body] + fx[u - 1] * old[u - 1, body])
        plane.put(even.at[u - 1], total * inverse)


def chip_kernel(
    inputs, cell, old_own, fx_own, fy_own, fz_own, fzl_own, inv_own, even_own, within_in,
    message, own2, known1, new, fx_more, fy_margin, fz_margin, fzl_margin, inv_more,
    old_margin, even_more, change, turn,
):
    iterate, source, phase = three_parts(inputs)
    layers, height, depth = iterate.shape
    plane = Plane(height, depth)
    body, half = plane.body, plane.half
    places, _ = chip_rows(height)
    margin = layers

    def part(k):
        return within_in[k * height:(k + 1) * height]

    def s(u):
        return source[own_layer(u, layers)]

    into_both_rows(turn.at[0], within_in[3 * height:])
    plane.put(old_margin, turn[0])
    fx_more[0] = 0.5 * (cell[layers - 1] + part(0))
    fx_more[1] = 0.5 * (part(0) + part(1))
    plane.put(fy_margin, plane.face_y(part(0)))
    face = plane.face_z(part(0))
    fz_margin[...] = face
    fzl_margin[...] = behind(face, 1, 1)
    fx = [fx_own.at[u] for u in range(3)] + [fx_more.at[0], fx_more.at[1]]
    fy = [fy_own.at[u] for u in range(layers)] + [fy_margin]
    fz = [fz_own.at[u] for u in range(layers)] + [fz_margin]
    fzl = [fzl_own.at[u] for u in range(layers)] + [fzl_margin]
    old = [old_own.at[u] for u in range(layers)] + [old_margin]
    inv = [None, inv_own.at[0], inv_own.at[1], inv_more.at[0], inv_more.at[1]]
    even = [None, even_own.at[0], even_own.at[1], even_more.at[0], even_more.at[1]]
    for u in (margin - 1, margin):
        weight = (fx[u][...] + fx[u - 1][...]) + (fy[u][body] + fy[u][plane.down]) + (fz[u][...] + fzl[u][...])
        inv[u][...] = 1.0 / (1.0 + weight)

    def around(ref, u):
        return in_layer(plane, fy[u], fz[u], fzl[u], ref[u])

    u = margin - 1
    total = s(u) + around(old, u) + (fx[u][...] * old[u + 1][body] + fx[u - 1][...] * old[u - 1][body])
    plane.put(even[u], total * inv[u][...])
    plane.put(even[margin], (part(2) + fx[u][...] * old[u][body]) * inv[margin][...])
    for u in range(2, margin + 1):
        if u < margin:
            total = s(u) + around(even, u) + (fx[u][...] * even[u + 1][body] + fx[u - 1][...] * even[u - 1][body])
        else:
            total = part(2) + around(even, u) + fx[u - 1][...] * even[u - 1][body]
        fresh = total * inv[u][...]
        new[u - 2] = fresh
        plane.put(change.at[u - 2], fresh - old[u][body])
    change = {u: change.at[u - 2] for u in range(2, margin + 1)}

    one = fx[1][...] * change[2][body]
    two = around(change, 2) + fx[2][...] * change[3][body]
    three = around(change, 3) + (fx[2][...] * change[2][body] + fx[3][...] * change[4][body])
    outer = jnp.where(plane.even(1), one, 0.0)
    inner = jnp.where(plane.even(2), two, 0.0) + jnp.where(plane.even(3), three, 0.0)
    core = core_of()

    def tile(name, outer, inner):
        message[places[name], :] = plane.packed(outer, inner, core)

    tile("source2", plane.summed(outer, turn.at[1]), plane.summed(inner, turn.at[2]))
    tile("fx2", plane.summed(fx[1][...], turn.at[3]), plane.summed(fx[3][...], turn.at[4]))
    fy2 = [plane.odd_rows(fy[u][body] + fy[u + 1][body], turn.at[5 + u // 2]) for u in (0, 2)]
    fz2 = [plane.odd_lanes(fz[u][...] + fz[u + 1][...], turn.at[7 + u // 2]) for u in (0, 2)]
    own2[0], own2[1] = plane.packed(*fy2, core), plane.packed(*fz2, core)
    tile("far2", fy2[1], fz2[1])
    for u in range(2):
        message[places["coef%d" % u], :] = cell[u]
    first = s(0) + around(old, 0) + fx[0][...] * old[1][body]
    second = s(0) + fx[0][...] * even[1][body]
    message[places["known0"], :] = jnp.where(plane.even(0), first, second)
    message[places["old0"], :] = odd_cells(iterate.at[own_layer(0, layers)], half, plane.odd_first(0))
    total = s(1) + around(even, 1) + fx[1][...] * even[2][body]
    known1[...] = total
    turn[9] = total * inv[1][...] - old[1][body]
    message[places["moved1"], :] = odd_cells(turn.at[9], half, plane.odd_first(1))
    message[places["face2"], :] = odd_cells(fx[1], half, plane.odd_first(1))


def border_kernel(
    inputs, message, own2, known1, new_in, fx_in, fy_in, fz_in, fzl_in, inv_in, across_in,
    within, fx2_in, new, known, fx, fy, fz, fzl, inv,
    old, even, change, turn, face_y, face_z, face_zl,
):
    iterate, source, _ = three_parts(inputs)
    layers, height, depth = iterate.shape
    plane = Plane(height, depth)
    body, half = plane.body, plane.half
    places, _ = chip_rows(height)
    core, last = core_of(), lax.axis_size("gx") - 1
    position = lax.axis_index("gx")

    def mine(name):
        return message[places[name], :]

    def theirs(name):
        return across_in[places[name], :]

    def opened(name, k):
        into_both_rows(turn.at[k], theirs(name))
        return turn[k]

    for k in range(2):
        here = theirs("coef%d" % k)
        plane.put(face_y.at[k], plane.face_y(here))
        face = plane.face_z(here)
        face_z[k] = face
        face_zl[k] = behind(face, 1, 1)
    fy[...], fz[...], fzl[...] = face_y[0], face_z[0], face_zl[0]
    there = position - 1 + 2 * core
    border = jnp.where((there >= 0) & (there <= last), 0.5 * (mine("coef0") + theirs("coef0")), 0.0)
    face1 = 0.5 * (theirs("coef0") + theirs("coef1"))
    face2 = opened("face2", 2)
    fx[0], fx[1] = border, face1

    def inverse(faces, fy, fz, fzl):
        weight = faces + (fy[body] + fy[plane.down]) + (fz[...] + fzl[...])
        return 1.0 / (1.0 + weight)

    inv_own = inverse(fx_in[0] + border, fy_in.at[0], fz_in.at[0], fzl_in.at[0])
    inv_near = inverse(border + face1, face_y.at[0], face_z.at[0], face_zl.at[0])
    inv_far = inverse(face1 + face2, face_y.at[1], face_z.at[1], face_zl.at[1])
    inv[0], inv[1] = inv_near, inv_own
    old_own, old_next = iterate[own_layer(0, layers)], iterate[own_layer(1, layers)]
    old_near, far = opened("old0", 0), opened("moved1", 1)
    even_own = (mine("known0") + border * old_near) * inv_own
    even_near = (theirs("known0") + border * old_own) * inv_near
    plane.put(even.at[0], even_near)
    plane.put(even.at[1], even_own)

    def near(ref, k):
        return in_layer(plane, face_y.at[k], face_z.at[k], face_zl.at[k], ref)

    def own(ref, u):
        return in_layer(plane, fy_in.at[u], fz_in.at[u], fzl_in.at[u], ref)

    odd_own = (mine("known0") + own(even.at[1], 0) + border * even_near) * inv_own
    odd_near = (theirs("known0") + near(even.at[0], 0) + border * even_own) * inv_near
    odd_next = (known1[...] + fx_in[0] * even_own) * inv_in[0]
    far = far + face1 * even_near * inv_far
    new[0], new[1], new[2] = odd_near, odd_own, odd_next
    near_by, here, following = odd_near - old_near, odd_own - old_own, odd_next - old_next
    for k, values in enumerate((far, near_by, here, following)):
        plane.put(change.at[k], values)
    plane.put(old.at[0], old_near)
    known[...] = theirs("known0") + face1 * far - near(old.at[0], 0)

    def residual(u, values):
        return jnp.where(plane.even(u), values, 0.0)

    own_outer = residual(1, own(change.at[3], 1) + fx_in[0] * here)
    own_outer = own_outer + residual(0, own(change.at[2], 0) + (fx_in[0] * following + border * near_by))
    own_inner = residual(2, fx_in[1] * following)
    its_outer = residual(-1, near(change.at[1], 0) + (face1 * far + border * here))
    its_outer = its_outer + residual(-2, near(change.at[0], 1) + face1 * near_by)
    its_inner = residual(-3, face2 * far)
    sums = [plane.summed(values, turn.at[3 + k]) for k, values in enumerate((own_outer, own_inner, its_outer, its_inner))]
    within[0] = mine("source2") + plane.packed(sums[0], sums[1], core)
    within[5] = theirs("source2") + plane.packed(sums[2], sums[3], 1 - core)
    within[6] = theirs("fx2")
    far2 = theirs("far2")
    far2_swap = jnp.where((plane.half_lane & 1) == 0, ahead(far2, 1, 1), behind(far2, 1, 1))
    near_fy2 = plane.odd_rows(face_y[0, body] + face_y[1, body], turn.at[1])
    near_fz2 = plane.odd_lanes(face_z[0] + face_z[1], turn.at[2])
    within[7] = plane.packed(near_fy2, far2_swap, 1 - core)
    within[8] = plane.packed(near_fz2, far2, 1 - core)
    fx2_in[...] = mine("fx2")
    middle = jnp.where((plane.half_lane & 1) == 0, ahead(mine("fx2"), 1, 1), behind(mine("fx2"), 1, 1))
    within[1] = plane.packed(plane.summed(border, turn.at[7]), middle, core)
    within[2], within[3] = own2[0], own2[1]
    turn[0] = source[own_layer(layers - 1, layers)] + fx_in[layers - 2] * new_in[layers - 4]
    within[4] = odd_cells(turn.at[0], half, jnp.logical_not(plane.odd_first(layers - 1)))


def neigh2(e2, fx2, fxl2, fy2, fz2, fzl2, first_of_two, tiles):
    half = fx2.shape[1]
    body, up, down = pl.ds(PAD, half), pl.ds(PAD + 1, half), pl.ds(PAD - 1, half)
    needed = range(tiles[0], tiles[-1] + 3)
    here = {j: e2[j, body] for j in needed}
    after = {j: ahead(here[j], 1, 1) for j in needed}
    before = {j: behind(here[j], 1, 1) for j in needed}
    found = []
    for j in tiles:
        k = j + 1
        upper = jnp.where(first_of_two, after[k], before[k + 1])
        lower = jnp.where(first_of_two, after[k - 1], before[k])
        sums = fx2[j] * upper + fxl2[j] * lower
        sums = sums + fy2[j, body] * e2[k, up] + fy2[j, down] * e2[k, down]
        sums = sums + fz2[j] * ahead(here[k], 2, 1) + fzl2[j] * behind(here[k], 2, 1)
        found.append(sums)
    return found


def parities2(half, lanes):
    row, lane = rows_of((half, lanes)), lanes_of((half, lanes))
    return (lane & 1) == 0, ((row + (lane & 1) + (lane >> 1)) & 1) == 0


def group(values):
    return with_partner(with_partner(values, 1, 1), 2, 1)


def packed_odd(values, pair):
    half, lanes = values.shape
    lane = lanes_of((half // 2, lanes))
    pair[...] = values
    return odd_cells(pair, half // 2, (((lane & 1) + (lane >> 1)) & 1) != 0)


def middle_down_kernel(
    own, fx2_in, within_in,
    slots, e2_out, s2, fx2, fxl2, fy2, fz2, fzl2, inv2,
    e2, pair,
):
    _, half, lanes = own.shape
    quarter = half // 2
    first_of_two, even2 = parities2(half, lanes)
    body, down = pl.ds(PAD, half), pl.ds(PAD - 1, half)
    edge = jnp.zeros((PAD, lanes), jnp.float32)
    for j in (0, 5):
        e2[j] = jnp.zeros((half + 2 * PAD, lanes), jnp.float32)

    def pair_of(k):
        return by_side(own[k], within_in[k])

    def four(k):
        (left, right), (far_left, far_right) = pair_of(k), pair_of(5 + k)
        return far_left, left, right, far_right

    for j, (source, fy, fz) in enumerate(zip(four(0), four(2), four(3))):
        s2[j] = source
        fy2[j, :PAD] = edge
        fy2[j, body] = fy
        fy2[j, PAD + half:] = edge
        fz2[j] = fz
        fzl2[j] = behind(fz, 2, 1)

    def between(left, right):
        return jnp.where(first_of_two, ahead(left, 1, 1), behind(right, 1, 1))

    fxl0, fxl1, fxr2, fxr3 = four(1)
    inner = fx2_in[...]
    fxr1, _ = by_side(inner, between(fxl1, inner))
    fxl2_, _ = by_side(between(inner, fxr2), inner)
    for j, (face, low) in enumerate(
        ((between(fxl0, fxl1), fxl0), (fxr1, fxl1), (fxr2, fxl2_), (fxr3, between(fxr2, fxr3)))
    ):
        fx2[j], fxl2[j] = face, low
        weight = face + low + fy2[j, body] + fy2[j, down] + fz2[j] + fzl2[j]
        inverse = 1.0 / (8.0 + weight)
        inv2[j] = inverse
        e2[j + 1, :PAD] = edge
        e2[j + 1, PAD + half:] = edge
        e2[j + 1, body] = s2[j] * inverse

    def neigh(tiles):
        return neigh2(e2, fx2, fxl2, fy2, fz2, fzl2, first_of_two, tiles)

    fresh = [(s2[j] + sums) * inv2[j] for j, sums in enumerate(neigh((0, 1, 2, 3)))]
    for j in range(4):
        e2[j + 1, body] = fresh[j]
        e2_out[j] = fresh[j]
    lane = lanes_of((quarter, lanes))
    odd_layer, odd_depth = (lane & 1) != 0, (lane & 2) != 0
    chips = slots.shape[0]
    for k, sums in enumerate(neigh((1, 2))):
        j = k + 1
        pair[k] = jnp.where(even2, sums, 0.0)
        item = (lane - (lax.axis_index("gx") // 2 * 2 + k) // (chips // 2)) & 3
        source = group(even_row_sum(pair.at[k], quarter))
        fx = group(jnp.where(odd_layer, even_row_sum(fx2.at[j], quarter), 0.0))
        fxl = group(jnp.where(odd_layer, 0.0, even_row_sum(fxl2.at[j], quarter)))
        fy = group(fy2[j, pl.ds(PAD + 1, quarter, 2), :])
        fz = group(jnp.where(odd_depth, even_row_sum(fz2.at[j], quarter), 0.0))
        weight = (fx + fxl) + (fy + behind(fy, 1, 0)) + (fz + behind(fz, 4, 1))
        start = source / (64.0 + weight)
        tile = jnp.where(item == 0, start, jnp.where(item == 1, fx, jnp.where(item == 2, fy, fz)))
        for c in range(chips):
            slots[c, k] = tile
    halo = packed_odd(jnp.where(first_of_two, fresh[2], fresh[1]), pair.at[2])
    for c in range(chips):
        slots[c, 2] = halo


def joined(one, two):
    return jnp.concatenate([part for part in (one, two) if part.shape[0]], 0)


class Level:
    def __init__(self, mass, source, faces, row_step, lane_step, slot_step):
        self.source, self.row_step, self.lane_step, self.slot_step = source, row_step, lane_step, slot_step
        self.fx, self.fy, self.fz = faces
        self.tiles = source.shape[0]
        shape = source.shape
        self.lane = lanes_of(shape)
        layer = lax.broadcasted_iota(jnp.int32, shape, 0) if self.tiles > 1 else self.lane // slot_step
        self.even = ((layer + rows_of(shape) // row_step + self.lane // lane_step) & 1) == 0
        self.fxl = self.lower(self.fx)
        self.fyl = self.row_shifts(self.fy)[1]
        self.fzl = behind(self.fz, lane_step, 2)
        weight = (self.fx + self.fxl) + (self.fy + self.fyl) + (self.fz + self.fzl)
        self.inv = 1.0 / (mass + weight)

    def upper(self, e):
        return joined(e[1:], ahead(e[:1], self.slot_step, 2))

    def lower(self, e):
        return joined(behind(e[-1:], self.slot_step, 2), e[:-1])

    def row_shifts(self, e):
        return ahead(e, self.row_step, 1), behind(e, self.row_step, 1)

    def neigh(self, e):
        above, below = self.row_shifts(e)
        total = (self.fx * self.upper(e) + self.fxl * self.lower(e)) + (self.fy * above + self.fyl * below)
        return total + (self.fz * ahead(e, self.lane_step, 2) + self.fzl * behind(e, self.lane_step, 2))

    def start(self):
        return self.source * self.inv

    def update(self, e):
        return self.start() + self.neigh(e) * self.inv

    def cycle(self, deeper):
        odd = self.update(self.start())
        residual = jnp.where(self.even, self.neigh(odd), 0.0)
        fix = deeper(self.restricted(residual), self.coarse_faces())
        even = self.update(odd + self.prolonged(fix))
        return jnp.where(self.even, even, self.update(even))

    def coarse_slot_step(self):
        return self.slot_step if self.tiles > 1 else 2 * self.slot_step

    def pairs(self, values):
        if self.tiles == 1:
            return with_partner(values, self.slot_step, 2)
        halves = values.reshape(self.tiles // 2, 2, *values.shape[1:])
        return halves[:, 0] + halves[:, 1]

    def odd_layers(self, values):
        if self.tiles == 1:
            return with_partner(jnp.where((self.lane & self.slot_step) != 0, values, 0.0), self.slot_step, 2)
        return values.reshape(self.tiles // 2, 2, *values.shape[1:])[:, 1]

    def row_pairs(self, values):
        return with_partner(values, self.row_step, 1)

    def odd_rows(self, values):
        odd = (rows_of(values.shape) & self.row_step) != 0
        return with_partner(jnp.where(odd, values, 0.0), self.row_step, 1)

    def restricted(self, values):
        return with_partner(self.row_pairs(self.pairs(values)), self.lane_step, 2)

    def coarse_faces(self):
        fx = with_partner(self.row_pairs(self.odd_layers(self.fx)), self.lane_step, 2)
        fy = with_partner(self.odd_rows(self.pairs(self.fy)), self.lane_step, 2)
        return fx, fy, self.restricted(jnp.where((self.lane & self.lane_step) != 0, self.fz, 0.0))

    def prolonged(self, fix):
        if self.tiles == 1:
            return fix
        both = jnp.concatenate([fix[:, None], fix[:, None]], 1)
        return both.reshape(self.tiles, *fix.shape[1:])


class Rows(Level):
    def __init__(self, mass, source, faces, scratch):
        self.scratch, self.used = scratch, 0
        self.rows = source.shape[1]
        super().__init__(mass, source, faces, 1, 4, 1)

    def start(self):
        return self.source

    def place(self):
        self.used += 1
        return self.scratch.at[self.used % self.scratch.shape[0]]

    def row_shifts(self, e):
        place = self.place()
        edge = jnp.zeros((e.shape[0], PAD, e.shape[2]), jnp.float32)
        place[:, :PAD] = edge
        place[:, PAD + self.rows:] = edge
        place[:, pl.ds(PAD, self.rows)] = e
        return place[:, pl.ds(PAD + 1, self.rows)], place[:, pl.ds(PAD - 1, self.rows)]

    def every_other(self, values, starts):
        place, tiles = self.place(), values.shape[0]
        place[:tiles, : self.rows] = values
        found = 0.0
        for start in starts:
            found = found + jnp.concatenate(
                [place[j, pl.ds(start, self.rows // 2, 2), :][None] for j in range(tiles)], 0
            )
        return found

    def row_pairs(self, values):
        return self.every_other(values, (0, 1))

    def odd_rows(self, values):
        return self.every_other(values, (1,))

    def prolonged(self, fix):
        place, tiles = self.place(), fix.shape[0]
        for j in range(tiles):
            into_both_rows(place.at[j, pl.ds(0, self.rows)], fix[j])
        return super().prolonged(place[:tiles, : self.rows])


def coarsest(mass, source, faces, *steps):
    row_step, lane_step, slot_step = steps
    level = Level(mass, source, faces, *steps)
    counts = source.shape[1] // row_step, source.shape[2] // lane_step, 4 // slot_step
    frames = [(m, k, q) for m in range(counts[0]) for k in range(counts[1]) for q in range(counts[2])]
    place = level.lane & 3

    def spread(values):
        copies = {}
        for m, k, q in frames:
            if k:
                copies[m, k, q] = behind(copies[m, 0, q], k * lane_step, 2)
            elif q:
                by = q * slot_step
                one, two = behind(copies[m, 0, 0], by, 2), ahead(copies[m, 0, 0], 4 - by, 2)
                copies[m, k, q] = jnp.where(place >= by, one, two)
            else:
                copies[m, k, q] = behind(values, m * row_step, 1) if m else values
        return copies

    start, inv, fx, fy, fz = [spread(values) for values in (source * level.inv, level.inv, level.fx, level.fy, level.fz)]

    def shifted(copies, frame, axis, by):
        moved = list(frame)
        moved[axis] = (frame[axis] - by) % counts[axis]
        return copies[tuple(moved)]

    def along_x(copies, frame, by):
        here, wrapped = copies[frame], shifted(copies, frame, 2, by)
        return joined(here[1:], wrapped[:1]) if by > 0 else joined(wrapped[-1:], here[:-1])

    weights = {}
    for frame in frames:
        pairs = [
            (fx[frame], along_x(fx, frame, -1)),
            (fy[frame], shifted(fy, frame, 0, -1)),
            (fz[frame], shifted(fz, frame, 1, -1)),
        ]
        weights[frame] = [(up * inv[frame], low * inv[frame]) for up, low in pairs]

    def update(e):
        fresh = {}
        for frame in frames:
            (x_up, x_low), (y_up, y_low), (z_up, z_low) = weights[frame]
            total = x_up * along_x(e, frame, 1) + x_low * along_x(e, frame, -1)
            total = total + (y_up * shifted(e, frame, 0, 1) + y_low * shifted(e, frame, 0, -1))
            total = total + (z_up * shifted(e, frame, 1, 1) + z_low * shifted(e, frame, 1, -1))
            fresh[frame] = start[frame] + total
        return fresh

    even = start
    odd = update(even)
    for turn in range(COARSE_SWEEPS - 1):
        even = update(odd)
        odd = update(even)
    return jnp.where(level.even, even[0, 0, 0], odd[0, 0, 0])


def small_cycle(mass, source, faces, row_step, lane_step, slot_step, between):
    if between == 0:
        return coarsest(mass, source, faces, row_step, lane_step, slot_step)
    level = Level(mass, source, faces, row_step, lane_step, slot_step)
    return level.cycle(
        lambda inner, inner_faces: small_cycle(
            8.0 * mass, inner, inner_faces, 2 * row_step, 2 * lane_step, level.coarse_slot_step(), between - 1
        )
    )


def coarse_kernel(
    owner_of, gathered, e2_in, s2_in, fx2_in, fxl2_in, fy2_in, fz2_in, fzl2_in, inv2_in,
    inputs, new_in, fx_more, fy_margin, fz_margin, fzl_margin, inv_more, fx_in, fy_in, fz_in, fzl_in, inv_in,
    new_out, known_out, fx_out, fy_out, fz_out, fzl_out, inv_out, within_in,
    solved_out, owned_out,
    e3, rows3, pair, e2, e1, cor, solved, owned, owner_here, fetch_sem, sems,
):
    fetch = pltpu.make_async_copy(owner_of, owner_here, fetch_sem)
    fetch.start()
    chips, _, quarter, lanes = gathered.shape
    blocks = 2 * chips
    half, height = 2 * quarter, 4 * quarter
    position, last = lax.axis_index("gx"), blocks - 1

    slot = lanes_of((quarter, lanes)) & 3
    spread = blocks // 4
    orders = [chip_order(chips, kind) for kind in range(2)]
    kind = (position // 2 + position) % 2

    def from_chip(chip, k):
        return jnp.where(kind == 0, gathered[orders[0].index(chip), k], gathered[orders[1].index(chip), k])

    tiles = [from_chip(chip, k) for chip in range(chips) for k in range(2)]
    items = []
    for k in range(4):
        packs = []
        for j in range(spread):
            value = tiles[j + (3 - k) % 4 * spread]
            for at in range(3):
                value = jnp.where(slot == at, tiles[j + (at - k) % 4 * spread], value)
            if k:
                value = jnp.where(slot < 4 - k, ahead(value, k, 1), behind(value, 4 - k, 1))
            packs.append(value[None])
        items.append(jnp.concatenate(packs, 0))
    third = Rows(64.0, items[0], items[1:], rows3)
    e3[...] = third.cycle(
        lambda inner, faces: small_cycle(512.0, inner, faces, 1, 8, third.coarse_slot_step(), 2)
    )

    fetch.wait()
    owner = owner_here[position]
    wide, narrow = lanes_of((lanes, lanes)), rows_of((lanes, lanes))
    take = jnp.where(narrow == 4 * wide + owner // spread, 1.0, 0.0)
    block = jnp.dot(
        e3[owner % spread], take, precision=lax.Precision.HIGHEST, preferred_element_type=jnp.float32
    )
    owned[0] = block[:, : lanes // 4]
    copies = [pltpu.make_async_copy(owned, owned_out, sems.at[0])]
    copies[0].start()

    first_of_two, even2 = parities2(half, lanes)
    body2 = pl.ds(PAD, half)
    edge = jnp.zeros((PAD, lanes), jnp.float32)
    core = core_of()
    s2, fx2, fxl2, fy2, fz2, fzl2, inv2 = [
        ref.at[pl.ds(core, 3)] for ref in (s2_in, fx2_in, fxl2_in, fy2_in, fz2_in, fzl2_in, inv2_in)
    ]
    next_chip = jnp.clip(position // 2 - 1 + 2 * core, 0, chips - 1)
    into_both_rows(pair.at[5], gathered[next_chip * jnp.where(kind == 0, chips - 1, pow(-3, -1, chips)) % chips, 2])
    halo = pair[5]
    before = (
        by_side(halo, e2_in[0])[0], by_side(jnp.where(first_of_two, halo, e2_in[0]), e2_in[1])[0],
        by_side(e2_in[1], e2_in[2])[0],
        by_side(e2_in[2], jnp.where(first_of_two, e2_in[3], halo))[0], by_side(e2_in[3], halo)[0],
    )
    for k in range(5):
        j = jnp.clip(position + k - 2, 0, last)
        into_both_rows(pair.at[k], group(jnp.where(slot == j // spread, e3[j % spread], 0.0)))
        e2[k, :PAD] = edge
        e2[k, PAD + half:] = edge
        e2[k, body2] = before[k] + pair[k]

    def update2():
        sums = neigh2(e2, fx2, fxl2, fy2, fz2, fzl2, first_of_two, (0, 1, 2))
        return [(s2[j] + sums[j]) * inv2[j] for j in range(3)]

    fresh = update2()
    for j in range(3):
        e2[j + 1, body2] = fresh[j]
    fixes2 = [jnp.where(even2, even, odd) for even, odd in zip(fresh, update2())]

    _, source, _ = three_parts(inputs)
    layers = source.shape[0]
    plane = Plane(height, lanes)
    body1 = plane.body
    near_lane = (lanes_of((half, lanes)) & 1) == core
    swaps = [jnp.where(first_of_two, ahead(v, 1, 1), behind(v, 1, 1)) for v in fixes2]
    outer, inner = by_side(fixes2[0], fixes2[2])
    outer_swap, inner_swap = by_side(swaps[0], swaps[2])
    coarse = (
        jnp.where(near_lane, outer_swap, outer), jnp.where(near_lane, fixes2[1], swaps[1]),
        jnp.where(near_lane, swaps[1], fixes2[1]), jnp.where(near_lane, inner, inner_swap),
    )
    fixes = []
    for k in range(4):
        into_both_rows(cor.at[k], coarse[k])
        fixes.append(cor[k])
    for u in range(-1, layers + 1):
        before = new_out[u + 1] if u < 2 else new_in[u - 2]
        plane.put(e1.at[u + 1], before + fixes[(u + 2) // 2])

    def fx1(u):
        if u < 0:
            return fx_out[-1 - u]
        return fx_in[u] if u < layers - 1 else fx_more[u - layers + 1]

    def inv1(u):
        if u <= 0:
            return inv_out[u + 1]
        return inv_in[u - 1] if u < layers - 1 else inv_more[u - layers + 1]

    def around1(u):
        if u < 0:
            return in_layer(plane, fy_out, fz_out, fzl_out, e1.at[0])
        if u == layers:
            return in_layer(plane, fy_margin, fz_margin, fzl_margin, e1.at[u + 1])
        return in_layer(plane, fy_in.at[u], fz_in.at[u], fzl_in.at[u], e1.at[u + 1])

    def updated1(u):
        sums = around1(u) + (fx1(u) * e1[u + 2, body1] + fx1(u - 1) * e1[u, body1])
        return (source[own_layer(u, layers)] + sums) * inv1(u)

    for u in range(layers):
        e1[u + 1, body1] = jnp.where(plane.even(u), updated1(u), e1[u + 1, body1])
    e1[0, body1] = (known_out[...] + fx1(-2) * fixes[0] + (around1(-1) + fx1(-1) * e1[1, body1])) * inv1(-1)
    into_both_rows(cor.at[4], within_in[4])
    sums = cor[4] + fx1(layers) * fixes[3] + (around1(layers) + fx1(layers - 1) * e1[layers, body1])
    e1[layers + 1, body1] = sums * inv1(layers)
    for u in range(layers):
        solved[u] = jnp.where(plane.even(u), e1[u + 1, body1], updated1(u))
        copies.append(
            pltpu.make_async_copy(solved.at[u], solved_out.at[own_layer(u, layers)], sems.at[u + 1])
        )
        copies[-1].start()
    for copy in copies:
        copy.wait()


def f32(*shape):
    return jax.ShapeDtypeStruct(shape, jnp.float32)


def vmem(*shape):
    return pltpu.VMEM(shape, jnp.float32)


def call(kernel, outs, scratch, operands, out_space=pltpu.VMEM):
    def size(shape):
        count = 4
        for extent in shape:
            count *= extent
        return count

    sized = [array for array in (*scratch, *outs, *operands) if hasattr(array, "shape")]
    asked = 8 * 2**20 + sum(size(array.shape) for array in sized)
    return pl.pallas_call(
        kernel,
        out_shape=tuple(outs),
        in_specs=[pl.BlockSpec(memory_space=pltpu.VMEM)] * len(operands),
        out_specs=tuple([pl.BlockSpec(memory_space=out_space)] * len(outs)),
        scratch_shapes=scratch,
        compiler_params=pltpu.CompilerParams(vmem_limit_bytes=asked),
    )(*operands)


def on_device(iterate, source, phase_field, block_owner):
    layers, height, depth = iterate.shape
    half, quarter = height // 2, height // 4
    blocks = lax.axis_size("gx")
    padded, padded2 = height + 2 * PAD, half + 2 * PAD
    inputs = sum(
        jnp.pad(block, ((k * layers, (2 - k) * layers), (0, 0), (0, 0)))
        for k, block in enumerate((iterate, source, phase_field))
    )
    edge, = call(edge_kernel, [f32(3 * height + half, depth)], [], (inputs,))
    edge_in = within_chip(edge)
    layer, tile, tall = (height, depth), (half, depth), (padded, depth)
    cell, old, *fine, even = call(
        own_kernel,
        [
            f32(layers, *layer), f32(layers, *tall), f32(layers - 1, *layer), f32(layers, *tall),
            f32(layers, *layer), f32(layers, *layer), f32(2, *layer), f32(2, *tall),
        ],
        [], (block_owner, inputs),
    )
    message, own2, known1, new, *margin = call(
        chip_kernel,
        [
            f32(chip_rows(height)[1], depth), f32(2, *tile), f32(*layer), f32(3, *layer),
            f32(2, *layer), f32(*tall), f32(*layer), f32(*layer), f32(2, *layer),
        ],
        [vmem(*tall), vmem(2, *tall), vmem(3, *tall), vmem(10, *layer)],
        (inputs, cell, old, *fine, even, edge_in),
    )
    within, fx2, *border = call(
        border_kernel,
        [
            f32(9, *tile), f32(*tile), f32(3, *layer), f32(*layer), f32(2, *layer),
            f32(padded, depth), f32(*layer), f32(*layer), f32(2, *layer),
        ],
        [
            vmem(1, padded, depth), vmem(2, padded, depth), vmem(4, padded, depth), vmem(8, *layer),
            vmem(2, padded, depth), vmem(2, *layer), vmem(2, *layer),
        ],
        (inputs, message, own2, known1, new, *fine, between_chips(message)),
    )
    within_in = within_chip(within)
    plain = f32(4, *tile)
    slots, *middle = call(
        middle_down_kernel,
        [f32(blocks // 2, 3, quarter, depth), plain, plain, plain, plain, f32(4, padded2, depth)] + [plain] * 3,
        [vmem(6, padded2, depth), vmem(3, *tile)],
        (within, fx2, within_in),
    )
    chips = blocks // 2
    kinds = [[2 * chip + (chip + core) % 2 for chip in chip_order(chips, core)] for core in range(2)]
    gathered = lax.all_to_all(slots, "gx", 0, 0, axis_index_groups=kinds, tiled=True)
    solved, owned = call(
        coarse_kernel,
        [f32(layers, *layer), f32(1, quarter, depth // 4)],
        [
            vmem(blocks // 4, quarter, depth), vmem(4, blocks // 4, quarter + 2 * PAD, depth), vmem(7, *tile),
            vmem(5, padded2, depth), vmem(layers + 2, padded, depth), vmem(5, *layer), vmem(layers, *layer),
            vmem(1, quarter, depth // 4), pltpu.SMEM((blocks,), jnp.int32),
            pltpu.SemaphoreType.DMA, pltpu.SemaphoreType.DMA((layers + 1,)),
        ],
        (block_owner, gathered, *middle, inputs, new, *margin, *fine, *border, within_in),
        pl.ANY,
    )
    return solved, owned


def solution(mesh):
    split = P(("groups", "gx"), None, None)
    return jax.shard_map(
        on_device,
        mesh=mesh,
        in_specs=(split, split, split, P("groups")),
        out_specs=(split, split),
        check_vma=False,
    )
```

```python
import jax
import jax.numpy as jnp
from jax import lax
from jax.experimental import pallas as pl
from jax.experimental.pallas import tpu as pltpu
from jax.sharding import PartitionSpec as P

STIFFNESS = 100.0
EPSILON = 0.01
COARSE_SWEEPS = 4
PAD = 8


def between_chips(block):
    return lax.ppermute(block, "gx", [(i, i + 1 if i % 2 else i - 1) for i in range(1, lax.axis_size("gx") - 1)])


def within_chip(block):
    return lax.ppermute(block, "gx", [(i, i ^ 1) for i in range(lax.axis_size("gx"))])


def chip_order(chips, kind):
    return list(reversed(range(chips))) if kind == 0 else list(range(chips))


def by_side(across, within):
    on_left = lax.axis_index("gx") % 2 == 0
    return jnp.where(on_left, across, within), jnp.where(on_left, within, across)


def lanes_of(shape):
    return lax.broadcasted_iota(jnp.int32, shape, len(shape) - 1)


def rows_of(shape):
    return lax.broadcasted_iota(jnp.int32, shape, len(shape) - 2)


def ahead(values, step, axis):
    return pltpu.roll(values, values.shape[axis] - step, axis)


def behind(values, step, axis):
    return pltpu.roll(values, step, axis)


def with_partner(values, step, axis):
    index = lax.broadcasted_iota(jnp.int32, values.shape, axis)
    partner = jnp.where((index & step) == 0, ahead(values, step, axis), behind(values, step, axis))
    return values + partner


def even_row_sum(scratch, rows):
    return scratch[pl.ds(0, rows, 2), :] + scratch[pl.ds(1, rows, 2), :]


def core_of():
    return lax.axis_index("gx") % 2


def own_layer(u, layers):
    return u + core_of() * (layers - 1 - 2 * u)


def three_parts(ref):
    third = ref.shape[0] // 3
    return [ref.at[pl.ds(k * third, third)] for k in range(3)]


def odd_cells(ref, rows, first):
    return jnp.where(first, ref[pl.ds(0, rows, 2), :], ref[pl.ds(1, rows, 2), :])


def into_both_rows(ref, values):
    rows = values.shape[0]
    ref[pl.ds(0, rows, 2), :] = values
    ref[pl.ds(1, rows, 2), :] = values


def cell_coef(value):
    return STIFFNESS * (value * value + EPSILON)


class Plane:
    def __init__(self, height, depth):
        self.height, self.half, self.depth = height, height // 2, depth
        self.row, self.lane = rows_of((height, depth)), lanes_of((height, depth))
        self.parity = self.row + self.lane + core_of()
        self.half_lane = lanes_of((self.half, depth))
        self.body = pl.ds(PAD, height)
        self.up, self.down = pl.ds(PAD + 1, height), pl.ds(PAD - 1, height)

    def even(self, u):
        return ((self.parity + u) & 1) == 0

    def odd_first(self, u):
        return ((self.half_lane + core_of() + u) & 1) != 0

    def put(self, ref, values):
        edge = jnp.zeros((PAD, self.depth), jnp.float32)
        ref[:PAD] = edge
        ref[PAD + self.height:] = edge
        ref[self.body] = values

    def face_y(self, here):
        return jnp.where(self.row < self.height - 1, 0.5 * (here + ahead(here, 1, 0)), 0.0)

    def face_z(self, here):
        return jnp.where(self.lane < self.depth - 1, 0.5 * (here + ahead(here, 1, 1)), 0.0)

    def packed(self, outer, inner, core):
        return jnp.where((self.half_lane & 1) == core, outer, inner)

    def both_rows(self, ref):
        return even_row_sum(ref, self.half)

    def summed(self, values, ref):
        ref[...] = values
        return with_partner(self.both_rows(ref), 1, 1)

    def odd_rows(self, values, ref):
        ref[...] = values
        return with_partner(ref[pl.ds(1, self.half, 2), :], 1, 1)

    def odd_lanes(self, values, ref):
        ref[...] = values
        sums = self.both_rows(ref)
        return jnp.where((self.half_lane & 1) == 0, ahead(sums, 1, 1), sums)


def in_layer(plane, fy, fz, fzl, padded):
    here = padded[plane.body]
    total = fy[plane.body] * padded[plane.up] + fy[plane.down] * padded[plane.down]
    return total + (fz[...] * ahead(here, 1, 1) + fzl[...] * behind(here, 1, 1))


def edge_kernel(inputs, out):
    iterate, source, phase = three_parts(inputs)
    layers, height, depth = iterate.shape
    plane = Plane(height, depth)
    near, inner, far = [own_layer(u, layers) for u in (layers - 1, layers - 2, layers - 3)]
    coef_near, coef_inner, coef_far = [cell_coef(phase[k]) for k in (near, inner, far)]

    def around(here, e):
        fy, fz = plane.face_y(here), plane.face_z(here)
        fyl, fzl = behind(fy, 1, 0), behind(fz, 1, 1)
        total = fy * ahead(e, 1, 0) + fyl * behind(e, 1, 0)
        return total + fz * ahead(e, 1, 1) + fzl * behind(e, 1, 1), fy + fyl + fz + fzl

    face_near, face_far = 0.5 * (coef_inner + coef_near), 0.5 * (coef_inner + coef_far)
    total, weight = around(coef_inner, iterate[inner])
    total = total + face_near * iterate[near] + face_far * iterate[far]
    updated = (source[inner] + total) / (1.0 + (face_near + face_far + weight))
    total, _ = around(coef_near, iterate[near])
    known = jnp.where(plane.even(layers - 1), total + face_near * iterate[inner], face_near * updated)
    out[:height] = coef_near
    out[height:2 * height] = coef_inner
    out[2 * height:3 * height] = source[near] + known
    out[3 * height:] = odd_cells(iterate.at[near], plane.half, plane.odd_first(layers - 1))


def chip_rows(height):
    half, at, places = height // 2, 0, {}
    for name, size in (
        ("coef0", height), ("coef1", height), ("known0", height), ("old0", half), ("moved1", half), ("face2", half),
        ("source2", half), ("fx2", half), ("far2", half),
    ):
        places[name] = pl.ds(at, size)
        at += size
    return places, at


def own_kernel(owner_of, inputs, cell, old, fx, fy, fz, fzl, inv, even):
    iterate, source, phase = three_parts(inputs)
    layers, height, depth = iterate.shape
    plane = Plane(height, depth)
    body = plane.body
    for u in range(layers):
        cell[u] = cell_coef(phase[own_layer(u, layers)])
        plane.put(old.at[u], iterate[own_layer(u, layers)])
    for u in range(layers):
        here = cell[u]
        if u < layers - 1:
            fx[u] = 0.5 * (here + cell[u + 1])
        plane.put(fy.at[u], plane.face_y(here))
        face = plane.face_z(here)
        fz[u] = face
        fzl[u] = behind(face, 1, 1)
    for u in (1, 2):
        weight = (fx[u] + fx[u - 1]) + (fy[u, body] + fy[u, plane.down]) + (fz[u] + fzl[u])
        inverse = 1.0 / (1.0 + weight)
        inv[u - 1] = inverse
        around = in_layer(plane, fy.at[u], fz.at[u], fzl.at[u], old.at[u])
        total = source[own_layer(u, layers)] + around + (fx[u] * old[u + 1, body] + fx[u - 1] * old[u - 1, body])
        plane.put(even.at[u - 1], total * inverse)


def chip_kernel(
    inputs, cell, old_own, fx_own, fy_own, fz_own, fzl_own, inv_own, even_own, within_in,
    message, own2, known1, new, fx_more, fy_margin, fz_margin, fzl_margin, inv_more,
    old_margin, even_more, change, turn,
):
    iterate, source, phase = three_parts(inputs)
    layers, height, depth = iterate.shape
    plane = Plane(height, depth)
    body, half = plane.body, plane.half
    places, _ = chip_rows(height)
    margin = layers

    def part(k):
        return within_in[k * height:(k + 1) * height]

    def s(u):
        return source[own_layer(u, layers)]

    into_both_rows(turn.at[0], within_in[3 * height:])
    plane.put(old_margin, turn[0])
    fx_more[0] = 0.5 * (cell[layers - 1] + part(0))
    fx_more[1] = 0.5 * (part(0) + part(1))
    plane.put(fy_margin, plane.face_y(part(0)))
    face = plane.face_z(part(0))
    fz_margin[...] = face
    fzl_margin[...] = behind(face, 1, 1)
    fx = [fx_own.at[u] for u in range(3)] + [fx_more.at[0], fx_more.at[1]]
    fy = [fy_own.at[u] for u in range(layers)] + [fy_margin]
    fz = [fz_own.at[u] for u in range(layers)] + [fz_margin]
    fzl = [fzl_own.at[u] for u in range(layers)] + [fzl_margin]
    old = [old_own.at[u] for u in range(layers)] + [old_margin]
    inv = [None, inv_own.at[0], inv_own.at[1], inv_more.at[0], inv_more.at[1]]
    even = [None, even_own.at[0], even_own.at[1], even_more.at[0], even_more.at[1]]
    for u in (margin - 1, margin):
        weight = (fx[u][...] + fx[u - 1][...]) + (fy[u][body] + fy[u][plane.down]) + (fz[u][...] + fzl[u][...])
        inv[u][...] = 1.0 / (1.0 + weight)

    def around(ref, u):
        return in_layer(plane, fy[u], fz[u], fzl[u], ref[u])

    u = margin - 1
    total = s(u) + around(old, u) + (fx[u][...] * old[u + 1][body] + fx[u - 1][...] * old[u - 1][body])
    plane.put(even[u], total * inv[u][...])
    plane.put(even[margin], (part(2) + fx[u][...] * old[u][body]) * inv[margin][...])
    for u in range(2, margin + 1):
        if u < margin:
            total = s(u) + around(even, u) + (fx[u][...] * even[u + 1][body] + fx[u - 1][...] * even[u - 1][body])
        else:
            total = part(2) + around(even, u) + fx[u - 1][...] * even[u - 1][body]
        fresh = total * inv[u][...]
        new[u - 2] = fresh
        plane.put(change.at[u - 2], fresh - old[u][body])
    change = {u: change.at[u - 2] for u in range(2, margin + 1)}

    one = fx[1][...] * change[2][body]
    two = around(change, 2) + fx[2][...] * change[3][body]
    three = around(change, 3) + (fx[2][...] * change[2][body] + fx[3][...] * change[4][body])
    outer = jnp.where(plane.even(1), one, 0.0)
    inner = jnp.where(plane.even(2), two, 0.0) + jnp.where(plane.even(3), three, 0.0)
    core = core_of()

    def tile(name, outer, inner):
        message[places[name], :] = plane.packed(outer, inner, core)

    tile("source2", plane.summed(outer, turn.at[1]), plane.summed(inner, turn.at[2]))
    tile("fx2", plane.summed(fx[1][...], turn.at[3]), plane.summed(fx[3][...], turn.at[4]))
    fy2 = [plane.odd_rows(fy[u][body] + fy[u + 1][body], turn.at[5 + u // 2]) for u in (0, 2)]
    fz2 = [plane.odd_lanes(fz[u][...] + fz[u + 1][...], turn.at[7 + u // 2]) for u in (0, 2)]
    own2[0], own2[1] = plane.packed(*fy2, core), plane.packed(*fz2, core)
    tile("far2", fy2[1], fz2[1])
    for u in range(2):
        message[places["coef%d" % u], :] = cell[u]
    first = s(0) + around(old, 0) + fx[0][...] * old[1][body]
    second = s(0) + fx[0][...] * even[1][body]
    message[places["known0"], :] = jnp.where(plane.even(0), first, second)
    message[places["old0"], :] = odd_cells(iterate.at[own_layer(0, layers)], half, plane.odd_first(0))
    total = s(1) + around(even, 1) + fx[1][...] * even[2][body]
    known1[...] = total
    turn[9] = total * inv[1][...] - old[1][body]
    message[places["moved1"], :] = odd_cells(turn.at[9], half, plane.odd_first(1))
    message[places["face2"], :] = odd_cells(fx[1], half, plane.odd_first(1))


def border_kernel(
    inputs, message, own2, known1, new_in, fx_in, fy_in, fz_in, fzl_in, inv_in, across_in,
    within, fx2_in, new, known, fx, fy, fz, fzl, inv,
    old, even, change, turn, face_y, face_z, face_zl,
):
    iterate, source, _ = three_parts(inputs)
    layers, height, depth = iterate.shape
    plane = Plane(height, depth)
    body, half = plane.body, plane.half
    places, _ = chip_rows(height)
    core, last = core_of(), lax.axis_size("gx") - 1
    position = lax.axis_index("gx")

    def mine(name):
        return message[places[name], :]

    def theirs(name):
        return across_in[places[name], :]

    def opened(name, k):
        into_both_rows(turn.at[k], theirs(name))
        return turn[k]

    for k in range(2):
        here = theirs("coef%d" % k)
        plane.put(face_y.at[k], plane.face_y(here))
        face = plane.face_z(here)
        face_z[k] = face
        face_zl[k] = behind(face, 1, 1)
    fy[...], fz[...], fzl[...] = face_y[0], face_z[0], face_zl[0]
    there = position - 1 + 2 * core
    border = jnp.where((there >= 0) & (there <= last), 0.5 * (mine("coef0") + theirs("coef0")), 0.0)
    face1 = 0.5 * (theirs("coef0") + theirs("coef1"))
    face2 = opened("face2", 2)
    fx[0], fx[1] = border, face1

    def inverse(faces, fy, fz, fzl):
        weight = faces + (fy[body] + fy[plane.down]) + (fz[...] + fzl[...])
        return 1.0 / (1.0 + weight)

    inv_own = inverse(fx_in[0] + border, fy_in.at[0], fz_in.at[0], fzl_in.at[0])
    inv_near = inverse(border + face1, face_y.at[0], face_z.at[0], face_zl.at[0])
    inv_far = inverse(face1 + face2, face_y.at[1], face_z.at[1], face_zl.at[1])
    inv[0], inv[1] = inv_near, inv_own
    old_own, old_next = iterate[own_layer(0, layers)], iterate[own_layer(1, layers)]
    old_near, far = opened("old0", 0), opened("moved1", 1)
    even_own = (mine("known0") + border * old_near) * inv_own
    even_near = (theirs("known0") + border * old_own) * inv_near
    plane.put(even.at[0], even_near)
    plane.put(even.at[1], even_own)

    def near(ref, k):
        return in_layer(plane, face_y.at[k], face_z.at[k], face_zl.at[k], ref)

    def own(ref, u):
        return in_layer(plane, fy_in.at[u], fz_in.at[u], fzl_in.at[u], ref)

    odd_own = (mine("known0") + own(even.at[1], 0) + border * even_near) * inv_own
    odd_near = (theirs("known0") + near(even.at[0], 0) + border * even_own) * inv_near
    odd_next = (known1[...] + fx_in[0] * even_own) * inv_in[0]
    far = far + face1 * even_near * inv_far
    new[0], new[1], new[2] = odd_near, odd_own, odd_next
    near_by, here, following = odd_near - old_near, odd_own - old_own, odd_next - old_next
    for k, values in enumerate((far, near_by, here, following)):
        plane.put(change.at[k], values)
    plane.put(old.at[0], old_near)
    known[...] = theirs("known0") + face1 * far - near(old.at[0], 0)

    def residual(u, values):
        return jnp.where(plane.even(u), values, 0.0)

    own_outer = residual(1, own(change.at[3], 1) + fx_in[0] * here)
    own_outer = own_outer + residual(0, own(change.at[2], 0) + (fx_in[0] * following + border * near_by))
    own_inner = residual(2, fx_in[1] * following)
    its_outer = residual(-1, near(change.at[1], 0) + (face1 * far + border * here))
    its_outer = its_outer + residual(-2, near(change.at[0], 1) + face1 * near_by)
    its_inner = residual(-3, face2 * far)
    sums = [plane.summed(values, turn.at[3 + k]) for k, values in enumerate((own_outer, own_inner, its_outer, its_inner))]
    within[0] = mine("source2") + plane.packed(sums[0], sums[1], core)
    within[5] = theirs("source2") + plane.packed(sums[2], sums[3], 1 - core)
    within[6] = theirs("fx2")
    far2 = theirs("far2")
    far2_swap = jnp.where((plane.half_lane & 1) == 0, ahead(far2, 1, 1), behind(far2, 1, 1))
    near_fy2 = plane.odd_rows(face_y[0, body] + face_y[1, body], turn.at[1])
    near_fz2 = plane.odd_lanes(face_z[0] + face_z[1], turn.at[2])
    within[7] = plane.packed(near_fy2, far2_swap, 1 - core)
    within[8] = plane.packed(near_fz2, far2, 1 - core)
    fx2_in[...] = mine("fx2")
    middle = jnp.where((plane.half_lane & 1) == 0, ahead(mine("fx2"), 1, 1), behind(mine("fx2"), 1, 1))
    within[1] = plane.packed(plane.summed(border, turn.at[7]), middle, core)
    within[2], within[3] = own2[0], own2[1]
    turn[0] = source[own_layer(layers - 1, layers)] + fx_in[layers - 2] * new_in[layers - 4]
    within[4] = odd_cells(turn.at[0], half, jnp.logical_not(plane.odd_first(layers - 1)))


def neigh2(e2, fx2, fxl2, fy2, fz2, fzl2, first_of_two, tiles):
    half = fx2.shape[1]
    body, up, down = pl.ds(PAD, half), pl.ds(PAD + 1, half), pl.ds(PAD - 1, half)
    needed = range(tiles[0], tiles[-1] + 3)
    here = {j: e2[j, body] for j in needed}
    after = {j: ahead(here[j], 1, 1) for j in needed}
    before = {j: behind(here[j], 1, 1) for j in needed}
    found = []
    for j in tiles:
        k = j + 1
        upper = jnp.where(first_of_two, after[k], before[k + 1])
        lower = jnp.where(first_of_two, after[k - 1], before[k])
        sums = fx2[j] * upper + fxl2[j] * lower
        sums = sums + fy2[j, body] * e2[k, up] + fy2[j, down] * e2[k, down]
        sums = sums + fz2[j] * ahead(here[k], 2, 1) + fzl2[j] * behind(here[k], 2, 1)
        found.append(sums)
    return found


def parities2(half, lanes):
    row, lane = rows_of((half, lanes)), lanes_of((half, lanes))
    return (lane & 1) == 0, ((row + (lane & 1) + (lane >> 1)) & 1) == 0


def group(values):
    return with_partner(with_partner(values, 1, 1), 2, 1)


def packed_odd(values, pair):
    half, lanes = values.shape
    lane = lanes_of((half // 2, lanes))
    pair[...] = values
    return odd_cells(pair, half // 2, (((lane & 1) + (lane >> 1)) & 1) != 0)


def middle_down_kernel(
    own, fx2_in, within_in,
    slots, e2_out, s2, fx2, fxl2, fy2, fz2, fzl2, inv2,
    e2, pair,
):
    _, half, lanes = own.shape
    quarter = half // 2
    first_of_two, even2 = parities2(half, lanes)
    body, down = pl.ds(PAD, half), pl.ds(PAD - 1, half)
    edge = jnp.zeros((PAD, lanes), jnp.float32)
    for j in (0, 5):
        e2[j] = jnp.zeros((half + 2 * PAD, lanes), jnp.float32)

    def pair_of(k):
        return by_side(own[k], within_in[k])

    def four(k):
        (left, right), (far_left, far_right) = pair_of(k), pair_of(5 + k)
        return far_left, left, right, far_right

    for j, (source, fy, fz) in enumerate(zip(four(0), four(2), four(3))):
        s2[j] = source
        fy2[j, :PAD] = edge
        fy2[j, body] = fy
        fy2[j, PAD + half:] = edge
        fz2[j] = fz
        fzl2[j] = behind(fz, 2, 1)

    def between(left, right):
        return jnp.where(first_of_two, ahead(left, 1, 1), behind(right, 1, 1))

    fxl0, fxl1, fxr2, fxr3 = four(1)
    inner = fx2_in[...]
    fxr1, _ = by_side(inner, between(fxl1, inner))
    fxl2_, _ = by_side(between(inner, fxr2), inner)
    for j, (face, low) in enumerate(
        ((between(fxl0, fxl1), fxl0), (fxr1, fxl1), (fxr2, fxl2_), (fxr3, between(fxr2, fxr3)))
    ):
        fx2[j], fxl2[j] = face, low
        weight = face + low + fy2[j, body] + fy2[j, down] + fz2[j] + fzl2[j]
        inverse = 1.0 / (8.0 + weight)
        inv2[j] = inverse
        e2[j + 1, :PAD] = edge
        e2[j + 1, PAD + half:] = edge
        e2[j + 1, body] = s2[j] * inverse

    def neigh(tiles):
        return neigh2(e2, fx2, fxl2, fy2, fz2, fzl2, first_of_two, tiles)

    fresh = [(s2[j] + sums) * inv2[j] for j, sums in enumerate(neigh((0, 1, 2, 3)))]
    for j in range(4):
        e2[j + 1, body] = fresh[j]
        e2_out[j] = fresh[j]
    lane = lanes_of((quarter, lanes))
    odd_layer, odd_depth = (lane & 1) != 0, (lane & 2) != 0
    chips = slots.shape[0]
    for k, sums in enumerate(neigh((1, 2))):
        j = k + 1
        pair[k] = jnp.where(even2, sums, 0.0)
        item = (lane - (lax.axis_index("gx") // 2 * 2 + k) // (chips // 2)) & 3
        source = group(even_row_sum(pair.at[k], quarter))
        fx = group(jnp.where(odd_layer, even_row_sum(fx2.at[j], quarter), 0.0))
        fxl = group(jnp.where(odd_layer, 0.0, even_row_sum(fxl2.at[j], quarter)))
        fy = group(fy2[j, pl.ds(PAD + 1, quarter, 2), :])
        fz = group(jnp.where(odd_depth, even_row_sum(fz2.at[j], quarter), 0.0))
        weight = (fx + fxl) + (fy + behind(fy, 1, 0)) + (fz + behind(fz, 4, 1))
        start = source / (64.0 + weight)
        tile = jnp.where(item == 0, start, jnp.where(item == 1, fx, jnp.where(item == 2, fy, fz)))
        for c in range(chips):
            slots[c, k] = tile
    halo = packed_odd(jnp.where(first_of_two, fresh[2], fresh[1]), pair.at[2])
    for c in range(chips):
        slots[c, 2] = halo


def joined(one, two):
    return jnp.concatenate([part for part in (one, two) if part.shape[0]], 0)


class Level:
    def __init__(self, mass, source, faces, row_step, lane_step, slot_step):
        self.source, self.row_step, self.lane_step, self.slot_step = source, row_step, lane_step, slot_step
        self.fx, self.fy, self.fz = faces
        self.tiles = source.shape[0]
        shape = source.shape
        self.lane = lanes_of(shape)
        layer = lax.broadcasted_iota(jnp.int32, shape, 0) if self.tiles > 1 else self.lane // slot_step
        self.even = ((layer + rows_of(shape) // row_step + self.lane // lane_step) & 1) == 0
        self.fxl = self.lower(self.fx)
        self.fyl = self.row_shifts(self.fy)[1]
        self.fzl = behind(self.fz, lane_step, 2)
        weight = (self.fx + self.fxl) + (self.fy + self.fyl) + (self.fz + self.fzl)
        self.inv = 1.0 / (mass + weight)

    def upper(self, e):
        return joined(e[1:], ahead(e[:1], self.slot_step, 2))

    def lower(self, e):
        return joined(behind(e[-1:], self.slot_step, 2), e[:-1])

    def row_shifts(self, e):
        return ahead(e, self.row_step, 1), behind(e, self.row_step, 1)

    def neigh(self, e):
        above, below = self.row_shifts(e)
        total = (self.fx * self.upper(e) + self.fxl * self.lower(e)) + (self.fy * above + self.fyl * below)
        return total + (self.fz * ahead(e, self.lane_step, 2) + self.fzl * behind(e, self.lane_step, 2))

    def start(self):
        return self.source * self.inv

    def update(self, e):
        return self.start() + self.neigh(e) * self.inv

    def cycle(self, deeper):
        odd = self.update(self.start())
        residual = jnp.where(self.even, self.neigh(odd), 0.0)
        fix = deeper(self.restricted(residual), self.coarse_faces())
        even = self.update(odd + self.prolonged(fix))
        return jnp.where(self.even, even, self.update(even))

    def coarse_slot_step(self):
        return self.slot_step if self.tiles > 1 else 2 * self.slot_step

    def pairs(self, values):
        if self.tiles == 1:
            return with_partner(values, self.slot_step, 2)
        halves = values.reshape(self.tiles // 2, 2, *values.shape[1:])
        return halves[:, 0] + halves[:, 1]

    def odd_layers(self, values):
        if self.tiles == 1:
            return with_partner(jnp.where((self.lane & self.slot_step) != 0, values, 0.0), self.slot_step, 2)
        return values.reshape(self.tiles // 2, 2, *values.shape[1:])[:, 1]

    def row_pairs(self, values):
        return with_partner(values, self.row_step, 1)

    def odd_rows(self, values):
        odd = (rows_of(values.shape) & self.row_step) != 0
        return with_partner(jnp.where(odd, values, 0.0), self.row_step, 1)

    def restricted(self, values):
        return with_partner(self.row_pairs(self.pairs(values)), self.lane_step, 2)

    def coarse_faces(self):
        fx = with_partner(self.row_pairs(self.odd_layers(self.fx)), self.lane_step, 2)
        fy = with_partner(self.odd_rows(self.pairs(self.fy)), self.lane_step, 2)
        return fx, fy, self.restricted(jnp.where((self.lane & self.lane_step) != 0, self.fz, 0.0))

    def prolonged(self, fix):
        if self.tiles == 1:
            return fix
        both = jnp.concatenate([fix[:, None], fix[:, None]], 1)
        return both.reshape(self.tiles, *fix.shape[1:])


class Rows(Level):
    def __init__(self, mass, source, faces, scratch):
        self.scratch, self.used = scratch, 0
        self.rows = source.shape[1]
        super().__init__(mass, source, faces, 1, 4, 1)

    def start(self):
        return self.source

    def place(self):
        self.used += 1
        return self.scratch.at[self.used % self.scratch.shape[0]]

    def row_shifts(self, e):
        place = self.place()
        edge = jnp.zeros((e.shape[0], PAD, e.shape[2]), jnp.float32)
        place[:, :PAD] = edge
        place[:, PAD + self.rows:] = edge
        place[:, pl.ds(PAD, self.rows)] = e
        return place[:, pl.ds(PAD + 1, self.rows)], place[:, pl.ds(PAD - 1, self.rows)]

    def every_other(self, values, starts):
        place, tiles = self.place(), values.shape[0]
        place[:tiles, : self.rows] = values
        found = 0.0
        for start in starts:
            found = found + jnp.concatenate(
                [place[j, pl.ds(start, self.rows // 2, 2), :][None] for j in range(tiles)], 0
            )
        return found

    def row_pairs(self, values):
        return self.every_other(values, (0, 1))

    def odd_rows(self, values):
        return self.every_other(values, (1,))

    def prolonged(self, fix):
        place, tiles = self.place(), fix.shape[0]
        for j in range(tiles):
            into_both_rows(place.at[j, pl.ds(0, self.rows)], fix[j])
        return super().prolonged(place[:tiles, : self.rows])


def coarsest(mass, source, faces, *steps):
    row_step, lane_step, slot_step = steps
    level = Level(mass, source, faces, *steps)
    counts = source.shape[1] // row_step, source.shape[2] // lane_step, 4 // slot_step
    frames = [(m, k, q) for m in range(counts[0]) for k in range(counts[1]) for q in range(counts[2])]
    place = level.lane & 3

    def spread(values):
        copies = {}
        for m, k, q in frames:
            if k:
                copies[m, k, q] = behind(copies[m, 0, q], k * lane_step, 2)
            elif q:
                by = q * slot_step
                one, two = behind(copies[m, 0, 0], by, 2), ahead(copies[m, 0, 0], 4 - by, 2)
                copies[m, k, q] = jnp.where(place >= by, one, two)
            else:
                copies[m, k, q] = behind(values, m * row_step, 1) if m else values
        return copies

    start, inv, fx, fy, fz = [spread(values) for values in (source * level.inv, level.inv, level.fx, level.fy, level.fz)]

    def shifted(copies, frame, axis, by):
        moved = list(frame)
        moved[axis] = (frame[axis] - by) % counts[axis]
        return copies[tuple(moved)]

    def along_x(copies, frame, by):
        here, wrapped = copies[frame], shifted(copies, frame, 2, by)
        return joined(here[1:], wrapped[:1]) if by > 0 else joined(wrapped[-1:], here[:-1])

    weights = {}
    for frame in frames:
        pairs = [
            (fx[frame], along_x(fx, frame, -1)),
            (fy[frame], shifted(fy, frame, 0, -1)),
            (fz[frame], shifted(fz, frame, 1, -1)),
        ]
        weights[frame] = [(up * inv[frame], low * inv[frame]) for up, low in pairs]

    def update(e):
        fresh = {}
        for frame in frames:
            (x_up, x_low), (y_up, y_low), (z_up, z_low) = weights[frame]
            total = x_up * along_x(e, frame, 1) + x_low * along_x(e, frame, -1)
            total = total + (y_up * shifted(e, frame, 0, 1) + y_low * shifted(e, frame, 0, -1))
            total = total + (z_up * shifted(e, frame, 1, 1) + z_low * shifted(e, frame, 1, -1))
            fresh[frame] = start[frame] + total
        return fresh

    even = start
    odd = update(even)
    for turn in range(COARSE_SWEEPS - 1):
        even = update(odd)
        odd = update(even)
    return jnp.where(level.even, even[0, 0, 0], odd[0, 0, 0])


def small_cycle(mass, source, faces, row_step, lane_step, slot_step, between):
    if between == 0:
        return coarsest(mass, source, faces, row_step, lane_step, slot_step)
    level = Level(mass, source, faces, row_step, lane_step, slot_step)
    return level.cycle(
        lambda inner, inner_faces: small_cycle(
            8.0 * mass, inner, inner_faces, 2 * row_step, 2 * lane_step, level.coarse_slot_step(), between - 1
        )
    )


def coarse_kernel(
    owner_of, gathered, e2_in, s2_in, fx2_in, fxl2_in, fy2_in, fz2_in, fzl2_in, inv2_in,
    inputs, new_in, fx_more, fy_margin, fz_margin, fzl_margin, inv_more, fx_in, fy_in, fz_in, fzl_in, inv_in,
    new_out, known_out, fx_out, fy_out, fz_out, fzl_out, inv_out, within_in,
    solved_out, owned_out,
    e3, rows3, pair, e2, e1, cor, solved, owned, owner_here, fetch_sem, sems,
):
    fetch = pltpu.make_async_copy(owner_of, owner_here, fetch_sem)
    fetch.start()
    chips, _, quarter, lanes = gathered.shape
    blocks = 2 * chips
    half, height = 2 * quarter, 4 * quarter
    position, last = lax.axis_index("gx"), blocks - 1

    slot = lanes_of((quarter, lanes)) & 3
    spread = blocks // 4
    orders = [chip_order(chips, kind) for kind in range(2)]
    kind = (position // 2 + position) % 2

    def from_chip(chip, k):
        return jnp.where(kind == 0, gathered[orders[0].index(chip), k], gathered[orders[1].index(chip), k])

    tiles = [from_chip(chip, k) for chip in range(chips) for k in range(2)]
    items = []
    for k in range(4):
        packs = []
        for j in range(spread):
            value = tiles[j + (3 - k) % 4 * spread]
            for at in range(3):
                value = jnp.where(slot == at, tiles[j + (at - k) % 4 * spread], value)
            if k:
                value = jnp.where(slot < 4 - k, ahead(value, k, 1), behind(value, 4 - k, 1))
            packs.append(value[None])
        items.append(jnp.concatenate(packs, 0))
    third = Rows(64.0, items[0], items[1:], rows3)
    e3[...] = third.cycle(
        lambda inner, faces: small_cycle(512.0, inner, faces, 1, 8, third.coarse_slot_step(), 2)
    )

    fetch.wait()
    owner = owner_here[position]
    wide, narrow = lanes_of((lanes, lanes)), rows_of((lanes, lanes))
    take = jnp.where(narrow == 4 * wide + owner // spread, 1.0, 0.0)
    block = jnp.dot(
        e3[owner % spread], take, precision=lax.Precision.HIGHEST, preferred_element_type=jnp.float32
    )
    owned[0] = block[:, : lanes // 4]
    copies = [pltpu.make_async_copy(owned, owned_out, sems.at[0])]
    copies[0].start()

    first_of_two, even2 = parities2(half, lanes)
    body2 = pl.ds(PAD, half)
    edge = jnp.zeros((PAD, lanes), jnp.float32)
    core = core_of()
    s2, fx2, fxl2, fy2, fz2, fzl2, inv2 = [
        ref.at[pl.ds(core, 3)] for ref in (s2_in, fx2_in, fxl2_in, fy2_in, fz2_in, fzl2_in, inv2_in)
    ]
    next_chip = jnp.clip(position // 2 - 1 + 2 * core, 0, chips - 1)
    into_both_rows(pair.at[5], gathered[jnp.where(kind == 0, chips - 1 - next_chip, next_chip), 2])
    halo = pair[5]
    before = (
        by_side(halo, e2_in[0])[0], by_side(jnp.where(first_of_two, halo, e2_in[0]), e2_in[1])[0],
        by_side(e2_in[1], e2_in[2])[0],
        by_side(e2_in[2], jnp.where(first_of_two, e2_in[3], halo))[0], by_side(e2_in[3], halo)[0],
    )
    for k in range(5):
        j = jnp.clip(position + k - 2, 0, last)
        into_both_rows(pair.at[k], group(jnp.where(slot == j // spread, e3[j % spread], 0.0)))
        e2[k, :PAD] = edge
        e2[k, PAD + half:] = edge
        e2[k, body2] = before[k] + pair[k]

    def update2():
        sums = neigh2(e2, fx2, fxl2, fy2, fz2, fzl2, first_of_two, (0, 1, 2))
        return [(s2[j] + sums[j]) * inv2[j] for j in range(3)]

    fresh = update2()
    for j in range(3):
        e2[j + 1, body2] = fresh[j]
    fixes2 = [jnp.where(even2, even, odd) for even, odd in zip(fresh, update2())]

    _, source, _ = three_parts(inputs)
    layers = source.shape[0]
    plane = Plane(height, lanes)
    body1 = plane.body
    near_lane = (lanes_of((half, lanes)) & 1) == core
    swaps = [jnp.where(first_of_two, ahead(v, 1, 1), behind(v, 1, 1)) for v in fixes2]
    outer, inner = by_side(fixes2[0], fixes2[2])
    outer_swap, inner_swap = by_side(swaps[0], swaps[2])
    coarse = (
        jnp.where(near_lane, outer_swap, outer), jnp.where(near_lane, fixes2[1], swaps[1]),
        jnp.where(near_lane, swaps[1], fixes2[1]), jnp.where(near_lane, inner, inner_swap),
    )
    fixes = []
    for k in range(4):
        into_both_rows(cor.at[k], coarse[k])
        fixes.append(cor[k])
    for u in range(-1, layers + 1):
        before = new_out[u + 1] if u < 2 else new_in[u - 2]
        plane.put(e1.at[u + 1], before + fixes[(u + 2) // 2])

    def fx1(u):
        if u < 0:
            return fx_out[-1 - u]
        return fx_in[u] if u < layers - 1 else fx_more[u - layers + 1]

    def inv1(u):
        if u <= 0:
            return inv_out[u + 1]
        return inv_in[u - 1] if u < layers - 1 else inv_more[u - layers + 1]

    def around1(u):
        if u < 0:
            return in_layer(plane, fy_out, fz_out, fzl_out, e1.at[0])
        if u == layers:
            return in_layer(plane, fy_margin, fz_margin, fzl_margin, e1.at[u + 1])
        return in_layer(plane, fy_in.at[u], fz_in.at[u], fzl_in.at[u], e1.at[u + 1])

    def updated1(u):
        sums = around1(u) + (fx1(u) * e1[u + 2, body1] + fx1(u - 1) * e1[u, body1])
        return (source[own_layer(u, layers)] + sums) * inv1(u)

    for u in range(layers):
        e1[u + 1, body1] = jnp.where(plane.even(u), updated1(u), e1[u + 1, body1])
    e1[0, body1] = (known_out[...] + fx1(-2) * fixes[0] + (around1(-1) + fx1(-1) * e1[1, body1])) * inv1(-1)
    into_both_rows(cor.at[4], within_in[4])
    sums = cor[4] + fx1(layers) * fixes[3] + (around1(layers) + fx1(layers - 1) * e1[layers, body1])
    e1[layers + 1, body1] = sums * inv1(layers)
    for u in range(layers):
        solved[u] = jnp.where(plane.even(u), e1[u + 1, body1], updated1(u))
        copies.append(
            pltpu.make_async_copy(solved.at[u], solved_out.at[own_layer(u, layers)], sems.at[u + 1])
        )
        copies[-1].start()
    for copy in copies:
        copy.wait()


def f32(*shape):
    return jax.ShapeDtypeStruct(shape, jnp.float32)


def vmem(*shape):
    return pltpu.VMEM(shape, jnp.float32)


def call(kernel, outs, scratch, operands, out_space=pltpu.VMEM):
    def size(shape):
        count = 4
        for extent in shape:
            count *= extent
        return count

    sized = [array for array in (*scratch, *outs, *operands) if hasattr(array, "shape")]
    asked = 8 * 2**20 + sum(size(array.shape) for array in sized)
    return pl.pallas_call(
        kernel,
        out_shape=tuple(outs),
        in_specs=[pl.BlockSpec(memory_space=pltpu.VMEM)] * len(operands),
        out_specs=tuple([pl.BlockSpec(memory_space=out_space)] * len(outs)),
        scratch_shapes=scratch,
        compiler_params=pltpu.CompilerParams(vmem_limit_bytes=asked),
    )(*operands)


def on_device(iterate, source, phase_field, block_owner):
    layers, height, depth = iterate.shape
    half, quarter = height // 2, height // 4
    blocks = lax.axis_size("gx")
    padded, padded2 = height + 2 * PAD, half + 2 * PAD
    inputs = sum(
        jnp.pad(block, ((k * layers, (2 - k) * layers), (0, 0), (0, 0)))
        for k, block in enumerate((iterate, source, phase_field))
    )
    edge, = call(edge_kernel, [f32(3 * height + half, depth)], [], (inputs,))
    edge_in = within_chip(edge)
    layer, tile, tall = (height, depth), (half, depth), (padded, depth)
    cell, old, *fine, even = call(
        own_kernel,
        [
            f32(layers, *layer), f32(layers, *tall), f32(layers - 1, *layer), f32(layers, *tall),
            f32(layers, *layer), f32(layers, *layer), f32(2, *layer), f32(2, *tall),
        ],
        [], (block_owner, inputs),
    )
    message, own2, known1, new, *margin = call(
        chip_kernel,
        [
            f32(chip_rows(height)[1], depth), f32(2, *tile), f32(*layer), f32(3, *layer),
            f32(2, *layer), f32(*tall), f32(*layer), f32(*layer), f32(2, *layer),
        ],
        [vmem(*tall), vmem(2, *tall), vmem(3, *tall), vmem(10, *layer)],
        (inputs, cell, old, *fine, even, edge_in),
    )
    within, fx2, *border = call(
        border_kernel,
        [
            f32(9, *tile), f32(*tile), f32(3, *layer), f32(*layer), f32(2, *layer),
            f32(padded, depth), f32(*layer), f32(*layer), f32(2, *layer),
        ],
        [
            vmem(1, padded, depth), vmem(2, padded, depth), vmem(4, padded, depth), vmem(8, *layer),
            vmem(2, padded, depth), vmem(2, *layer), vmem(2, *layer),
        ],
        (inputs, message, own2, known1, new, *fine, between_chips(message)),
    )
    within_in = within_chip(within)
    plain = f32(4, *tile)
    slots, *middle = call(
        middle_down_kernel,
        [f32(blocks // 2, 3, quarter, depth), plain, plain, plain, plain, f32(4, padded2, depth)] + [plain] * 3,
        [vmem(6, padded2, depth), vmem(3, *tile)],
        (within, fx2, within_in),
    )
    chips = blocks // 2
    kinds = [[2 * chip + (chip + core) % 2 for chip in chip_order(chips, core)] for core in range(2)]
    gathered = lax.all_to_all(slots, "gx", 0, 0, axis_index_groups=kinds, tiled=True)
    solved, owned = call(
        coarse_kernel,
        [f32(layers, *layer), f32(1, quarter, depth // 4)],
        [
            vmem(blocks // 4, quarter, depth), vmem(4, blocks // 4, quarter + 2 * PAD, depth), vmem(7, *tile),
            vmem(5, padded2, depth), vmem(layers + 2, padded, depth), vmem(5, *layer), vmem(layers, *layer),
            vmem(1, quarter, depth // 4), pltpu.SMEM((blocks,), jnp.int32),
            pltpu.SemaphoreType.DMA, pltpu.SemaphoreType.DMA((layers + 1,)),
        ],
        (block_owner, gathered, *middle, inputs, new, *margin, *fine, *border, within_in),
        pl.ANY,
    )
    return solved, owned


def solution(mesh):
    split = P(("groups", "gx"), None, None)
    return jax.shard_map(
        on_device,
        mesh=mesh,
        in_specs=(split, split, split, P("groups")),
        out_specs=(split, split),
        check_vma=False,
    )
```

```python
import jax
import jax.numpy as jnp
from jax import lax
from jax.experimental import pallas as pl
from jax.experimental.pallas import tpu as pltpu
from jax.sharding import PartitionSpec as P

STIFFNESS = 100.0
EPSILON = 0.01
COARSE_SWEEPS = 4
PAD = 8


def between_chips(block):
    return lax.ppermute(block, "gx", [(i, i + 1 if i % 2 else i - 1) for i in range(1, lax.axis_size("gx") - 1)])


def within_chip(block):
    return lax.ppermute(block, "gx", [(i, i ^ 1) for i in range(lax.axis_size("gx"))])


def by_side(across, within):
    on_left = lax.axis_index("gx") % 2 == 0
    return jnp.where(on_left, across, within), jnp.where(on_left, within, across)


def lanes_of(shape):
    return lax.broadcasted_iota(jnp.int32, shape, len(shape) - 1)


def rows_of(shape):
    return lax.broadcasted_iota(jnp.int32, shape, len(shape) - 2)


def ahead(values, step, axis):
    return pltpu.roll(values, values.shape[axis] - step, axis)


def behind(values, step, axis):
    return pltpu.roll(values, step, axis)


def with_partner(values, step, axis):
    index = lax.broadcasted_iota(jnp.int32, values.shape, axis)
    partner = jnp.where((index & step) == 0, ahead(values, step, axis), behind(values, step, axis))
    return values + partner


def even_row_sum(scratch, rows):
    return scratch[pl.ds(0, rows, 2), :] + scratch[pl.ds(1, rows, 2), :]


def core_of():
    return lax.axis_index("gx") % 2


def own_layer(u, layers):
    return u + core_of() * (layers - 1 - 2 * u)


def three_parts(ref):
    third = ref.shape[0] // 3
    return [ref.at[pl.ds(k * third, third)] for k in range(3)]


def odd_cells(ref, rows, first):
    return jnp.where(first, ref[pl.ds(0, rows, 2), :], ref[pl.ds(1, rows, 2), :])


def into_both_rows(ref, values):
    rows = values.shape[0]
    ref[pl.ds(0, rows, 2), :] = values
    ref[pl.ds(1, rows, 2), :] = values


def cell_coef(value):
    return STIFFNESS * (value * value + EPSILON)


class Plane:
    def __init__(self, height, depth):
        self.height, self.half, self.depth = height, height // 2, depth
        self.row, self.lane = rows_of((height, depth)), lanes_of((height, depth))
        self.parity = self.row + self.lane + core_of()
        self.half_lane = lanes_of((self.half, depth))
        self.body = pl.ds(PAD, height)
        self.up, self.down = pl.ds(PAD + 1, height), pl.ds(PAD - 1, height)

    def even(self, u):
        return ((self.parity + u) & 1) == 0

    def odd_first(self, u):
        return ((self.half_lane + core_of() + u) & 1) != 0

    def put(self, ref, values):
        edge = jnp.zeros((PAD, self.depth), jnp.float32)
        ref[:PAD] = edge
        ref[PAD + self.height:] = edge
        ref[self.body] = values

    def face_y(self, here):
        return jnp.where(self.row < self.height - 1, 0.5 * (here + ahead(here, 1, 0)), 0.0)

    def face_z(self, here):
        return jnp.where(self.lane < self.depth - 1, 0.5 * (here + ahead(here, 1, 1)), 0.0)

    def packed(self, outer, inner, core):
        return jnp.where((self.half_lane & 1) == core, outer, inner)

    def both_rows(self, ref):
        return even_row_sum(ref, self.half)

    def summed(self, values, ref):
        ref[...] = values
        return with_partner(self.both_rows(ref), 1, 1)

    def odd_rows(self, values, ref):
        ref[...] = values
        return with_partner(ref[pl.ds(1, self.half, 2), :], 1, 1)

    def odd_lanes(self, values, ref):
        ref[...] = values
        sums = self.both_rows(ref)
        return jnp.where((self.half_lane & 1) == 0, ahead(sums, 1, 1), sums)


def in_layer(plane, fy, fz, fzl, padded):
    here = padded[plane.body]
    total = fy[plane.body] * padded[plane.up] + fy[plane.down] * padded[plane.down]
    return total + (fz[...] * ahead(here, 1, 1) + fzl[...] * behind(here, 1, 1))


def edge_kernel(inputs, out):
    iterate, source, phase = three_parts(inputs)
    layers, height, depth = iterate.shape
    plane = Plane(height, depth)
    near, inner, far = [own_layer(u, layers) for u in (layers - 1, layers - 2, layers - 3)]
    coef_near, coef_inner, coef_far = [cell_coef(phase[k]) for k in (near, inner, far)]

    def around(here, e):
        fy, fz = plane.face_y(here), plane.face_z(here)
        fyl, fzl = behind(fy, 1, 0), behind(fz, 1, 1)
        total = fy * ahead(e, 1, 0) + fyl * behind(e, 1, 0)
        return total + fz * ahead(e, 1, 1) + fzl * behind(e, 1, 1), fy + fyl + fz + fzl

    face_near, face_far = 0.5 * (coef_inner + coef_near), 0.5 * (coef_inner + coef_far)
    total, weight = around(coef_inner, iterate[inner])
    total = total + face_near * iterate[near] + face_far * iterate[far]
    updated = (source[inner] + total) / (1.0 + (face_near + face_far + weight))
    total, _ = around(coef_near, iterate[near])
    known = jnp.where(plane.even(layers - 1), total + face_near * iterate[inner], face_near * updated)
    out[:height] = coef_near
    out[height:2 * height] = coef_inner
    out[2 * height:3 * height] = source[near] + known
    out[3 * height:] = odd_cells(iterate.at[near], plane.half, plane.odd_first(layers - 1))


def chip_rows(height):
    half, at, places = height // 2, 0, {}
    for name, size in (
        ("coef0", height), ("coef1", height), ("known0", height), ("old0", half), ("moved1", half), ("face2", half),
        ("source2", half), ("fx2", half), ("far2", half),
    ):
        places[name] = pl.ds(at, size)
        at += size
    return places, at


def own_kernel(owner_of, inputs, cell, old, fx, fy, fz, fzl, inv, even):
    iterate, source, phase = three_parts(inputs)
    layers, height, depth = iterate.shape
    plane = Plane(height, depth)
    body = plane.body
    for u in range(layers):
        cell[u] = cell_coef(phase[own_layer(u, layers)])
        plane.put(old.at[u], iterate[own_layer(u, layers)])
    for u in range(layers):
        here = cell[u]
        if u < layers - 1:
            fx[u] = 0.5 * (here + cell[u + 1])
        plane.put(fy.at[u], plane.face_y(here))
        face = plane.face_z(here)
        fz[u] = face
        fzl[u] = behind(face, 1, 1)
    for u in (1, 2):
        weight = (fx[u] + fx[u - 1]) + (fy[u, body] + fy[u, plane.down]) + (fz[u] + fzl[u])
        inverse = 1.0 / (1.0 + weight)
        inv[u - 1] = inverse
        around = in_layer(plane, fy.at[u], fz.at[u], fzl.at[u], old.at[u])
        total = source[own_layer(u, layers)] + around + (fx[u] * old[u + 1, body] + fx[u - 1] * old[u - 1, body])
        plane.put(even.at[u - 1], total * inverse)


def chip_kernel(
    inputs, cell, old_own, fx_own, fy_own, fz_own, fzl_own, inv_own, even_own, within_in,
    message, own2, known1, new, fx_more, fy_margin, fz_margin, fzl_margin, inv_more,
    old_margin, even_more, change, turn,
):
    iterate, source, phase = three_parts(inputs)
    layers, height, depth = iterate.shape
    plane = Plane(height, depth)
    body, half = plane.body, plane.half
    places, _ = chip_rows(height)
    margin = layers

    def part(k):
        return within_in[k * height:(k + 1) * height]

    def s(u):
        return source[own_layer(u, layers)]

    into_both_rows(turn.at[0], within_in[3 * height:])
    plane.put(old_margin, turn[0])
    fx_more[0] = 0.5 * (cell[layers - 1] + part(0))
    fx_more[1] = 0.5 * (part(0) + part(1))
    plane.put(fy_margin, plane.face_y(part(0)))
    face = plane.face_z(part(0))
    fz_margin[...] = face
    fzl_margin[...] = behind(face, 1, 1)
    fx = [fx_own.at[u] for u in range(3)] + [fx_more.at[0], fx_more.at[1]]
    fy = [fy_own.at[u] for u in range(layers)] + [fy_margin]
    fz = [fz_own.at[u] for u in range(layers)] + [fz_margin]
    fzl = [fzl_own.at[u] for u in range(layers)] + [fzl_margin]
    old = [old_own.at[u] for u in range(layers)] + [old_margin]
    inv = [None, inv_own.at[0], inv_own.at[1], inv_more.at[0], inv_more.at[1]]
    even = [None, even_own.at[0], even_own.at[1], even_more.at[0], even_more.at[1]]
    for u in (margin - 1, margin):
        weight = (fx[u][...] + fx[u - 1][...]) + (fy[u][body] + fy[u][plane.down]) + (fz[u][...] + fzl[u][...])
        inv[u][...] = 1.0 / (1.0 + weight)

    def around(ref, u):
        return in_layer(plane, fy[u], fz[u], fzl[u], ref[u])

    u = margin - 1
    total = s(u) + around(old, u) + (fx[u][...] * old[u + 1][body] + fx[u - 1][...] * old[u - 1][body])
    plane.put(even[u], total * inv[u][...])
    plane.put(even[margin], (part(2) + fx[u][...] * old[u][body]) * inv[margin][...])
    for u in range(2, margin + 1):
        if u < margin:
            total = s(u) + around(even, u) + (fx[u][...] * even[u + 1][body] + fx[u - 1][...] * even[u - 1][body])
        else:
            total = part(2) + around(even, u) + fx[u - 1][...] * even[u - 1][body]
        fresh = total * inv[u][...]
        new[u - 2] = fresh
        plane.put(change.at[u - 2], fresh - old[u][body])
    change = {u: change.at[u - 2] for u in range(2, margin + 1)}

    one = fx[1][...] * change[2][body]
    two = around(change, 2) + fx[2][...] * change[3][body]
    three = around(change, 3) + (fx[2][...] * change[2][body] + fx[3][...] * change[4][body])
    outer = jnp.where(plane.even(1), one, 0.0)
    inner = jnp.where(plane.even(2), two, 0.0) + jnp.where(plane.even(3), three, 0.0)
    core = core_of()

    def tile(name, outer, inner):
        message[places[name], :] = plane.packed(outer, inner, core)

    tile("source2", plane.summed(outer, turn.at[1]), plane.summed(inner, turn.at[2]))
    tile("fx2", plane.summed(fx[1][...], turn.at[3]), plane.summed(fx[3][...], turn.at[4]))
    fy2 = [plane.odd_rows(fy[u][body] + fy[u + 1][body], turn.at[5 + u // 2]) for u in (0, 2)]
    fz2 = [plane.odd_lanes(fz[u][...] + fz[u + 1][...], turn.at[7 + u // 2]) for u in (0, 2)]
    own2[0], own2[1] = plane.packed(*fy2, core), plane.packed(*fz2, core)
    tile("far2", fy2[1], fz2[1])
    for u in range(2):
        message[places["coef%d" % u], :] = cell[u]
    first = s(0) + around(old, 0) + fx[0][...] * old[1][body]
    second = s(0) + fx[0][...] * even[1][body]
    message[places["known0"], :] = jnp.where(plane.even(0), first, second)
    message[places["old0"], :] = odd_cells(iterate.at[own_layer(0, layers)], half, plane.odd_first(0))
    total = s(1) + around(even, 1) + fx[1][...] * even[2][body]
    known1[...] = total
    turn[9] = total * inv[1][...] - old[1][body]
    message[places["moved1"], :] = odd_cells(turn.at[9], half, plane.odd_first(1))
    message[places["face2"], :] = odd_cells(fx[1], half, plane.odd_first(1))


def border_kernel(
    inputs, message, own2, known1, new_in, fx_in, fy_in, fz_in, fzl_in, inv_in, across_in,
    within, fx2_in, new, known, fx, fy, fz, fzl, inv,
    old, even, change, turn, face_y, face_z, face_zl,
):
    iterate, source, _ = three_parts(inputs)
    layers, height, depth = iterate.shape
    plane = Plane(height, depth)
    body, half = plane.body, plane.half
    places, _ = chip_rows(height)
    core, last = core_of(), lax.axis_size("gx") - 1
    position = lax.axis_index("gx")

    def mine(name):
        return message[places[name], :]

    def theirs(name):
        return across_in[places[name], :]

    def opened(name, k):
        into_both_rows(turn.at[k], theirs(name))
        return turn[k]

    for k in range(2):
        here = theirs("coef%d" % k)
        plane.put(face_y.at[k], plane.face_y(here))
        face = plane.face_z(here)
        face_z[k] = face
        face_zl[k] = behind(face, 1, 1)
    fy[...], fz[...], fzl[...] = face_y[0], face_z[0], face_zl[0]
    there = position - 1 + 2 * core
    border = jnp.where((there >= 0) & (there <= last), 0.5 * (mine("coef0") + theirs("coef0")), 0.0)
    face1 = 0.5 * (theirs("coef0") + theirs("coef1"))
    face2 = opened("face2", 2)
    fx[0], fx[1] = border, face1

    def inverse(faces, fy, fz, fzl):
        weight = faces + (fy[body] + fy[plane.down]) + (fz[...] + fzl[...])
        return 1.0 / (1.0 + weight)

    inv_own = inverse(fx_in[0] + border, fy_in.at[0], fz_in.at[0], fzl_in.at[0])
    inv_near = inverse(border + face1, face_y.at[0], face_z.at[0], face_zl.at[0])
    inv_far = inverse(face1 + face2, face_y.at[1], face_z.at[1], face_zl.at[1])
    inv[0], inv[1] = inv_near, inv_own
    old_own, old_next = iterate[own_layer(0, layers)], iterate[own_layer(1, layers)]
    old_near, far = opened("old0", 0), opened("moved1", 1)
    even_own = (mine("known0") + border * old_near) * inv_own
    even_near = (theirs("known0") + border * old_own) * inv_near
    plane.put(even.at[0], even_near)
    plane.put(even.at[1], even_own)

    def near(ref, k):
        return in_layer(plane, face_y.at[k], face_z.at[k], face_zl.at[k], ref)

    def own(ref, u):
        return in_layer(plane, fy_in.at[u], fz_in.at[u], fzl_in.at[u], ref)

    odd_own = (mine("known0") + own(even.at[1], 0) + border * even_near) * inv_own
    odd_near = (theirs("known0") + near(even.at[0], 0) + border * even_own) * inv_near
    odd_next = (known1[...] + fx_in[0] * even_own) * inv_in[0]
    far = far + face1 * even_near * inv_far
    new[0], new[1], new[2] = odd_near, odd_own, odd_next
    near_by, here, following = odd_near - old_near, odd_own - old_own, odd_next - old_next
    for k, values in enumerate((far, near_by, here, following)):
        plane.put(change.at[k], values)
    plane.put(old.at[0], old_near)
    known[...] = theirs("known0") + face1 * far - near(old.at[0], 0)

    def residual(u, values):
        return jnp.where(plane.even(u), values, 0.0)

    own_outer = residual(1, own(change.at[3], 1) + fx_in[0] * here)
    own_outer = own_outer + residual(0, own(change.at[2], 0) + (fx_in[0] * following + border * near_by))
    own_inner = residual(2, fx_in[1] * following)
    its_outer = residual(-1, near(change.at[1], 0) + (face1 * far + border * here))
    its_outer = its_outer + residual(-2, near(change.at[0], 1) + face1 * near_by)
    its_inner = residual(-3, face2 * far)
    sums = [plane.summed(values, turn.at[3 + k]) for k, values in enumerate((own_outer, own_inner, its_outer, its_inner))]
    within[0] = mine("source2") + plane.packed(sums[0], sums[1], core)
    within[5] = theirs("source2") + plane.packed(sums[2], sums[3], 1 - core)
    within[6] = theirs("fx2")
    far2 = theirs("far2")
    far2_swap = jnp.where((plane.half_lane & 1) == 0, ahead(far2, 1, 1), behind(far2, 1, 1))
    near_fy2 = plane.odd_rows(face_y[0, body] + face_y[1, body], turn.at[1])
    near_fz2 = plane.odd_lanes(face_z[0] + face_z[1], turn.at[2])
    within[7] = plane.packed(near_fy2, far2_swap, 1 - core)
    within[8] = plane.packed(near_fz2, far2, 1 - core)
    fx2_in[...] = mine("fx2")
    middle = jnp.where((plane.half_lane & 1) == 0, ahead(mine("fx2"), 1, 1), behind(mine("fx2"), 1, 1))
    within[1] = plane.packed(plane.summed(border, turn.at[7]), middle, core)
    within[2], within[3] = own2[0], own2[1]
    turn[0] = source[own_layer(layers - 1, layers)] + fx_in[layers - 2] * new_in[layers - 4]
    within[4] = odd_cells(turn.at[0], half, jnp.logical_not(plane.odd_first(layers - 1)))


def neigh2(e2, fx2, fxl2, fy2, fz2, fzl2, first_of_two, tiles):
    half = fx2.shape[1]
    body, up, down = pl.ds(PAD, half), pl.ds(PAD + 1, half), pl.ds(PAD - 1, half)
    needed = range(tiles[0], tiles[-1] + 3)
    here = {j: e2[j, body] for j in needed}
    after = {j: ahead(here[j], 1, 1) for j in needed}
    before = {j: behind(here[j], 1, 1) for j in needed}
    found = []
    for j in tiles:
        k = j + 1
        upper = jnp.where(first_of_two, after[k], before[k + 1])
        lower = jnp.where(first_of_two, after[k - 1], before[k])
        sums = fx2[j] * upper + fxl2[j] * lower
        sums = sums + fy2[j, body] * e2[k, up] + fy2[j, down] * e2[k, down]
        sums = sums + fz2[j] * ahead(here[k], 2, 1) + fzl2[j] * behind(here[k], 2, 1)
        found.append(sums)
    return found


def parities2(half, lanes):
    row, lane = rows_of((half, lanes)), lanes_of((half, lanes))
    return (lane & 1) == 0, ((row + (lane & 1) + (lane >> 1)) & 1) == 0


def group(values):
    return with_partner(with_partner(values, 1, 1), 2, 1)


def packed_odd(values, pair):
    half, lanes = values.shape
    lane = lanes_of((half // 2, lanes))
    pair[...] = values
    return odd_cells(pair, half // 2, (((lane & 1) + (lane >> 1)) & 1) != 0)


def middle_down_kernel(
    own, fx2_in, within_in,
    slots, e2_out, s2, fx2, fxl2, fy2, fz2, fzl2, inv2,
    e2, pair,
):
    _, half, lanes = own.shape
    quarter = half // 2
    first_of_two, even2 = parities2(half, lanes)
    body, down = pl.ds(PAD, half), pl.ds(PAD - 1, half)
    edge = jnp.zeros((PAD, lanes), jnp.float32)
    for j in (0, 5):
        e2[j] = jnp.zeros((half + 2 * PAD, lanes), jnp.float32)

    def pair_of(k):
        return by_side(own[k], within_in[k])

    def four(k):
        (left, right), (far_left, far_right) = pair_of(k), pair_of(5 + k)
        return far_left, left, right, far_right

    for j, (source, fy, fz) in enumerate(zip(four(0), four(2), four(3))):
        s2[j] = source
        fy2[j, :PAD] = edge
        fy2[j, body] = fy
        fy2[j, PAD + half:] = edge
        fz2[j] = fz
        fzl2[j] = behind(fz, 2, 1)

    def between(left, right):
        return jnp.where(first_of_two, ahead(left, 1, 1), behind(right, 1, 1))

    fxl0, fxl1, fxr2, fxr3 = four(1)
    inner = fx2_in[...]
    fxr1, _ = by_side(inner, between(fxl1, inner))
    fxl2_, _ = by_side(between(inner, fxr2), inner)
    for j, (face, low) in enumerate(
        ((between(fxl0, fxl1), fxl0), (fxr1, fxl1), (fxr2, fxl2_), (fxr3, between(fxr2, fxr3)))
    ):
        fx2[j], fxl2[j] = face, low
        weight = face + low + fy2[j, body] + fy2[j, down] + fz2[j] + fzl2[j]
        inverse = 1.0 / (8.0 + weight)
        inv2[j] = inverse
        e2[j + 1, :PAD] = edge
        e2[j + 1, PAD + half:] = edge
        e2[j + 1, body] = s2[j] * inverse

    def neigh(tiles):
        return neigh2(e2, fx2, fxl2, fy2, fz2, fzl2, first_of_two, tiles)

    fresh = [(s2[j] + sums) * inv2[j] for j, sums in enumerate(neigh((0, 1, 2, 3)))]
    for j in range(4):
        e2[j + 1, body] = fresh[j]
        e2_out[j] = fresh[j]
    lane = lanes_of((quarter, lanes))
    odd_layer, odd_depth = (lane & 1) != 0, (lane & 2) != 0
    chips = slots.shape[0]
    for k, sums in enumerate(neigh((1, 2))):
        j = k + 1
        pair[k] = jnp.where(even2, sums, 0.0)
        item = (lane - (lax.axis_index("gx") // 2 * 2 + k) // (chips // 2)) & 3
        source = group(even_row_sum(pair.at[k], quarter))
        fx = group(jnp.where(odd_layer, even_row_sum(fx2.at[j], quarter), 0.0))
        fxl = group(jnp.where(odd_layer, 0.0, even_row_sum(fxl2.at[j], quarter)))
        fy = group(fy2[j, pl.ds(PAD + 1, quarter, 2), :])
        fz = group(jnp.where(odd_depth, even_row_sum(fz2.at[j], quarter), 0.0))
        weight = (fx + fxl) + (fy + behind(fy, 1, 0)) + (fz + behind(fz, 4, 1))
        start = source / (64.0 + weight)
        tile = jnp.where(item == 0, start, jnp.where(item == 1, fx, jnp.where(item == 2, fy, fz)))
        for c in range(chips):
            slots[c, k] = tile
    halo = packed_odd(jnp.where(first_of_two, fresh[2], fresh[1]), pair.at[2])
    for c in range(chips):
        slots[c, 2] = halo


def joined(one, two):
    return jnp.concatenate([part for part in (one, two) if part.shape[0]], 0)


class Level:
    def __init__(self, mass, source, faces, row_step, lane_step, slot_step):
        self.source, self.row_step, self.lane_step, self.slot_step = source, row_step, lane_step, slot_step
        self.fx, self.fy, self.fz = faces
        self.tiles = source.shape[0]
        shape = source.shape
        self.lane = lanes_of(shape)
        layer = lax.broadcasted_iota(jnp.int32, shape, 0) if self.tiles > 1 else self.lane // slot_step
        self.even = ((layer + rows_of(shape) // row_step + self.lane // lane_step) & 1) == 0
        self.fxl = self.lower(self.fx)
        self.fyl = self.row_shifts(self.fy)[1]
        self.fzl = behind(self.fz, lane_step, 2)
        weight = (self.fx + self.fxl) + (self.fy + self.fyl) + (self.fz + self.fzl)
        self.inv = 1.0 / (mass + weight)

    def upper(self, e):
        return joined(e[1:], ahead(e[:1], self.slot_step, 2))

    def lower(self, e):
        return joined(behind(e[-1:], self.slot_step, 2), e[:-1])

    def row_shifts(self, e):
        return ahead(e, self.row_step, 1), behind(e, self.row_step, 1)

    def neigh(self, e):
        above, below = self.row_shifts(e)
        total = (self.fx * self.upper(e) + self.fxl * self.lower(e)) + (self.fy * above + self.fyl * below)
        return total + (self.fz * ahead(e, self.lane_step, 2) + self.fzl * behind(e, self.lane_step, 2))

    def start(self):
        return self.source * self.inv

    def update(self, e):
        return self.start() + self.neigh(e) * self.inv

    def cycle(self, deeper):
        odd = self.update(self.start())
        residual = jnp.where(self.even, self.neigh(odd), 0.0)
        fix = deeper(self.restricted(residual), self.coarse_faces())
        even = self.update(odd + self.prolonged(fix))
        return jnp.where(self.even, even, self.update(even))

    def coarse_slot_step(self):
        return self.slot_step if self.tiles > 1 else 2 * self.slot_step

    def pairs(self, values):
        if self.tiles == 1:
            return with_partner(values, self.slot_step, 2)
        halves = values.reshape(self.tiles // 2, 2, *values.shape[1:])
        return halves[:, 0] + halves[:, 1]

    def odd_layers(self, values):
        if self.tiles == 1:
            return with_partner(jnp.where((self.lane & self.slot_step) != 0, values, 0.0), self.slot_step, 2)
        return values.reshape(self.tiles // 2, 2, *values.shape[1:])[:, 1]

    def row_pairs(self, values):
        return with_partner(values, self.row_step, 1)

    def odd_rows(self, values):
        odd = (rows_of(values.shape) & self.row_step) != 0
        return with_partner(jnp.where(odd, values, 0.0), self.row_step, 1)

    def restricted(self, values):
        return with_partner(self.row_pairs(self.pairs(values)), self.lane_step, 2)

    def coarse_faces(self):
        fx = with_partner(self.row_pairs(self.odd_layers(self.fx)), self.lane_step, 2)
        fy = with_partner(self.odd_rows(self.pairs(self.fy)), self.lane_step, 2)
        return fx, fy, self.restricted(jnp.where((self.lane & self.lane_step) != 0, self.fz, 0.0))

    def prolonged(self, fix):
        if self.tiles == 1:
            return fix
        both = jnp.concatenate([fix[:, None], fix[:, None]], 1)
        return both.reshape(self.tiles, *fix.shape[1:])


class Rows(Level):
    def __init__(self, mass, source, faces, scratch):
        self.scratch, self.used = scratch, 0
        self.rows = source.shape[1]
        super().__init__(mass, source, faces, 1, 4, 1)

    def start(self):
        return self.source

    def place(self):
        self.used += 1
        return self.scratch.at[self.used % self.scratch.shape[0]]

    def row_shifts(self, e):
        place = self.place()
        edge = jnp.zeros((e.shape[0], PAD, e.shape[2]), jnp.float32)
        place[:, :PAD] = edge
        place[:, PAD + self.rows:] = edge
        place[:, pl.ds(PAD, self.rows)] = e
        return place[:, pl.ds(PAD + 1, self.rows)], place[:, pl.ds(PAD - 1, self.rows)]

    def every_other(self, values, starts):
        place, tiles = self.place(), values.shape[0]
        place[:tiles, : self.rows] = values
        found = 0.0
        for start in starts:
            found = found + jnp.concatenate(
                [place[j, pl.ds(start, self.rows // 2, 2), :][None] for j in range(tiles)], 0
            )
        return found

    def row_pairs(self, values):
        return self.every_other(values, (0, 1))

    def odd_rows(self, values):
        return self.every_other(values, (1,))

    def prolonged(self, fix):
        place, tiles = self.place(), fix.shape[0]
        for j in range(tiles):
            into_both_rows(place.at[j, pl.ds(0, self.rows)], fix[j])
        return super().prolonged(place[:tiles, : self.rows])


def coarsest(mass, source, faces, *steps):
    row_step, lane_step, slot_step = steps
    level = Level(mass, source, faces, *steps)
    counts = source.shape[1] // row_step, source.shape[2] // lane_step, 4 // slot_step
    frames = [(m, k, q) for m in range(counts[0]) for k in range(counts[1]) for q in range(counts[2])]
    place = level.lane & 3

    def spread(values):
        copies = {}
        for m, k, q in frames:
            if k:
                copies[m, k, q] = behind(copies[m, 0, q], k * lane_step, 2)
            elif q:
                by = q * slot_step
                one, two = behind(copies[m, 0, 0], by, 2), ahead(copies[m, 0, 0], 4 - by, 2)
                copies[m, k, q] = jnp.where(place >= by, one, two)
            else:
                copies[m, k, q] = behind(values, m * row_step, 1) if m else values
        return copies

    start, inv, fx, fy, fz = [spread(values) for values in (source * level.inv, level.inv, level.fx, level.fy, level.fz)]

    def shifted(copies, frame, axis, by):
        moved = list(frame)
        moved[axis] = (frame[axis] - by) % counts[axis]
        return copies[tuple(moved)]

    def along_x(copies, frame, by):
        here, wrapped = copies[frame], shifted(copies, frame, 2, by)
        return joined(here[1:], wrapped[:1]) if by > 0 else joined(wrapped[-1:], here[:-1])

    same = level.tiles == 1 and counts[2] == 2, counts[0] == 2, counts[1] == 2
    weights = {}
    for frame in frames:
        pairs = [
            (fx[frame], along_x(fx, frame, -1)),
            (fy[frame], shifted(fy, frame, 0, -1)),
            (fz[frame], shifted(fz, frame, 1, -1)),
        ]
        weights[frame] = [
            ((up + low) * inv[frame], None) if merged else (up * inv[frame], low * inv[frame])
            for (up, low), merged in zip(pairs, same)
        ]

    def update(e):
        fresh = {}
        for frame in frames:
            moves = along_x, lambda c, f, by: shifted(c, f, 0, by), lambda c, f, by: shifted(c, f, 1, by)
            total = 0.0
            for (up, low), move in zip(weights[frame], moves):
                part = up * move(e, frame, 1)
                total = total + (part if low is None else part + low * move(e, frame, -1))
            fresh[frame] = start[frame] + total
        return fresh

    even = start
    odd = update(even)
    for turn in range(COARSE_SWEEPS - 1):
        even = update(odd)
        odd = update(even)
    return jnp.where(level.even, even[0, 0, 0], odd[0, 0, 0])


def small_cycle(mass, source, faces, row_step, lane_step, slot_step, between):
    if between == 0:
        return coarsest(mass, source, faces, row_step, lane_step, slot_step)
    level = Level(mass, source, faces, row_step, lane_step, slot_step)
    return level.cycle(
        lambda inner, inner_faces: small_cycle(
            8.0 * mass, inner, inner_faces, 2 * row_step, 2 * lane_step, level.coarse_slot_step(), between - 1
        )
    )


def coarse_kernel(
    owner_of, gathered, e2_in, s2_in, fx2_in, fxl2_in, fy2_in, fz2_in, fzl2_in, inv2_in,
    inputs, new_in, fx_more, fy_margin, fz_margin, fzl_margin, inv_more, fx_in, fy_in, fz_in, fzl_in, inv_in,
    new_out, known_out, fx_out, fy_out, fz_out, fzl_out, inv_out, within_in,
    solved_out, owned_out,
    e3, rows3, pair, e2, e1, cor, solved, owned, owner_here, fetch_sem, sems,
):
    fetch = pltpu.make_async_copy(owner_of, owner_here, fetch_sem)
    fetch.start()
    chips, _, quarter, lanes = gathered.shape
    blocks = 2 * chips
    half, height = 2 * quarter, 4 * quarter
    position, last = lax.axis_index("gx"), blocks - 1

    slot = lanes_of((quarter, lanes)) & 3
    spread = blocks // 4
    tiles = [gathered[chip, k] for chip in reversed(range(chips)) for k in range(2)]
    items = []
    for k in range(4):
        packs = []
        for j in range(spread):
            value = tiles[j + (3 - k) % 4 * spread]
            for at in range(3):
                value = jnp.where(slot == at, tiles[j + (at - k) % 4 * spread], value)
            if k:
                value = jnp.where(slot < 4 - k, ahead(value, k, 1), behind(value, 4 - k, 1))
            packs.append(value[None])
        items.append(jnp.concatenate(packs, 0))
    third = Rows(64.0, items[0], items[1:], rows3)
    e3[...] = third.cycle(
        lambda inner, faces: small_cycle(512.0, inner, faces, 1, 8, third.coarse_slot_step(), 2)
    )

    fetch.wait()
    owner = owner_here[position]
    wide, narrow = lanes_of((lanes, lanes)), rows_of((lanes, lanes))
    take = jnp.where(narrow == 4 * wide + owner // spread, 1.0, 0.0)
    block = jnp.dot(
        e3[owner % spread], take, precision=lax.Precision.HIGHEST, preferred_element_type=jnp.float32
    )
    owned[0] = block[:, : lanes // 4]
    copies = [pltpu.make_async_copy(owned, owned_out, sems.at[0])]
    copies[0].start()

    first_of_two, even2 = parities2(half, lanes)
    body2 = pl.ds(PAD, half)
    edge = jnp.zeros((PAD, lanes), jnp.float32)
    core = core_of()
    s2, fx2, fxl2, fy2, fz2, fzl2, inv2 = [
        ref.at[pl.ds(core, 3)] for ref in (s2_in, fx2_in, fxl2_in, fy2_in, fz2_in, fzl2_in, inv2_in)
    ]
    next_chip = jnp.clip(position // 2 - 1 + 2 * core, 0, chips - 1)
    into_both_rows(pair.at[5], gathered[chips - 1 - next_chip, 2])
    halo = pair[5]
    before = (
        by_side(halo, e2_in[0])[0], by_side(jnp.where(first_of_two, halo, e2_in[0]), e2_in[1])[0],
        by_side(e2_in[1], e2_in[2])[0],
        by_side(e2_in[2], jnp.where(first_of_two, e2_in[3], halo))[0], by_side(e2_in[3], halo)[0],
    )
    for k in range(5):
        j = jnp.clip(position + k - 2, 0, last)
        into_both_rows(pair.at[k], group(jnp.where(slot == j // spread, e3[j % spread], 0.0)))
        e2[k, :PAD] = edge
        e2[k, PAD + half:] = edge
        e2[k, body2] = before[k] + pair[k]

    def update2():
        sums = neigh2(e2, fx2, fxl2, fy2, fz2, fzl2, first_of_two, (0, 1, 2))
        return [(s2[j] + sums[j]) * inv2[j] for j in range(3)]

    fresh = update2()
    for j in range(3):
        e2[j + 1, body2] = fresh[j]
    fixes2 = [jnp.where(even2, even, odd) for even, odd in zip(fresh, update2())]

    _, source, _ = three_parts(inputs)
    layers = source.shape[0]
    plane = Plane(height, lanes)
    body1 = plane.body
    near_lane = (lanes_of((half, lanes)) & 1) == core
    swaps = [jnp.where(first_of_two, ahead(v, 1, 1), behind(v, 1, 1)) for v in fixes2]
    outer, inner = by_side(fixes2[0], fixes2[2])
    outer_swap, inner_swap = by_side(swaps[0], swaps[2])
    coarse = (
        jnp.where(near_lane, outer_swap, outer), jnp.where(near_lane, fixes2[1], swaps[1]),
        jnp.where(near_lane, swaps[1], fixes2[1]), jnp.where(near_lane, inner, inner_swap),
    )
    fixes = []
    for k in range(4):
        into_both_rows(cor.at[k], coarse[k])
        fixes.append(cor[k])
    for u in range(-1, layers + 1):
        before = new_out[u + 1] if u < 2 else new_in[u - 2]
        plane.put(e1.at[u + 1], before + fixes[(u + 2) // 2])

    def fx1(u):
        if u < 0:
            return fx_out[-1 - u]
        return fx_in[u] if u < layers - 1 else fx_more[u - layers + 1]

    def inv1(u):
        if u <= 0:
            return inv_out[u + 1]
        return inv_in[u - 1] if u < layers - 1 else inv_more[u - layers + 1]

    def around1(u):
        if u < 0:
            return in_layer(plane, fy_out, fz_out, fzl_out, e1.at[0])
        if u == layers:
            return in_layer(plane, fy_margin, fz_margin, fzl_margin, e1.at[u + 1])
        return in_layer(plane, fy_in.at[u], fz_in.at[u], fzl_in.at[u], e1.at[u + 1])

    def updated1(u):
        sums = around1(u) + (fx1(u) * e1[u + 2, body1] + fx1(u - 1) * e1[u, body1])
        return (source[own_layer(u, layers)] + sums) * inv1(u)

    for u in range(layers):
        e1[u + 1, body1] = jnp.where(plane.even(u), updated1(u), e1[u + 1, body1])
    e1[0, body1] = (known_out[...] + fx1(-2) * fixes[0] + (around1(-1) + fx1(-1) * e1[1, body1])) * inv1(-1)
    into_both_rows(cor.at[4], within_in[4])
    sums = cor[4] + fx1(layers) * fixes[3] + (around1(layers) + fx1(layers - 1) * e1[layers, body1])
    e1[layers + 1, body1] = sums * inv1(layers)
    for u in range(layers):
        solved[u] = jnp.where(plane.even(u), e1[u + 1, body1], updated1(u))
        copies.append(
            pltpu.make_async_copy(solved.at[u], solved_out.at[own_layer(u, layers)], sems.at[u + 1])
        )
        copies[-1].start()
    for copy in copies:
        copy.wait()


def f32(*shape):
    return jax.ShapeDtypeStruct(shape, jnp.float32)


def vmem(*shape):
    return pltpu.VMEM(shape, jnp.float32)


def call(kernel, outs, scratch, operands, out_space=pltpu.VMEM):
    def size(shape):
        count = 4
        for extent in shape:
            count *= extent
        return count

    sized = [array for array in (*scratch, *outs, *operands) if hasattr(array, "shape")]
    asked = 8 * 2**20 + sum(size(array.shape) for array in sized)
    return pl.pallas_call(
        kernel,
        out_shape=tuple(outs),
        in_specs=[pl.BlockSpec(memory_space=pltpu.VMEM)] * len(operands),
        out_specs=tuple([pl.BlockSpec(memory_space=out_space)] * len(outs)),
        scratch_shapes=scratch,
        compiler_params=pltpu.CompilerParams(vmem_limit_bytes=asked),
    )(*operands)


def on_device(iterate, source, phase_field, block_owner):
    layers, height, depth = iterate.shape
    half, quarter = height // 2, height // 4
    blocks = lax.axis_size("gx")
    padded, padded2 = height + 2 * PAD, half + 2 * PAD
    inputs = sum(
        jnp.pad(block, ((k * layers, (2 - k) * layers), (0, 0), (0, 0)))
        for k, block in enumerate((iterate, source, phase_field))
    )
    edge, = call(edge_kernel, [f32(3 * height + half, depth)], [], (inputs,))
    edge_in = within_chip(edge)
    layer, tile, tall = (height, depth), (half, depth), (padded, depth)
    cell, old, *fine, even = call(
        own_kernel,
        [
            f32(layers, *layer), f32(layers, *tall), f32(layers - 1, *layer), f32(layers, *tall),
            f32(layers, *layer), f32(layers, *layer), f32(2, *layer), f32(2, *tall),
        ],
        [], (block_owner, inputs),
    )
    message, own2, known1, new, *margin = call(
        chip_kernel,
        [
            f32(chip_rows(height)[1], depth), f32(2, *tile), f32(*layer), f32(3, *layer),
            f32(2, *layer), f32(*tall), f32(*layer), f32(*layer), f32(2, *layer),
        ],
        [vmem(*tall), vmem(2, *tall), vmem(3, *tall), vmem(10, *layer)],
        (inputs, cell, old, *fine, even, edge_in),
    )
    within, fx2, *border = call(
        border_kernel,
        [
            f32(9, *tile), f32(*tile), f32(3, *layer), f32(*layer), f32(2, *layer),
            f32(padded, depth), f32(*layer), f32(*layer), f32(2, *layer),
        ],
        [
            vmem(1, padded, depth), vmem(2, padded, depth), vmem(4, padded, depth), vmem(8, *layer),
            vmem(2, padded, depth), vmem(2, *layer), vmem(2, *layer),
        ],
        (inputs, message, own2, known1, new, *fine, between_chips(message)),
    )
    within_in = within_chip(within)
    plain = f32(4, *tile)
    slots, *middle = call(
        middle_down_kernel,
        [f32(blocks // 2, 3, quarter, depth), plain, plain, plain, plain, f32(4, padded2, depth)] + [plain] * 3,
        [vmem(6, padded2, depth), vmem(3, *tile)],
        (within, fx2, within_in),
    )
    kinds = [[2 * chip + (chip + core) % 2 for chip in reversed(range(blocks // 2))] for core in range(2)]
    gathered = lax.all_to_all(slots, "gx", 0, 0, axis_index_groups=kinds, tiled=True)
    solved, owned = call(
        coarse_kernel,
        [f32(layers, *layer), f32(1, quarter, depth // 4)],
        [
            vmem(blocks // 4, quarter, depth), vmem(4, blocks // 4, quarter + 2 * PAD, depth), vmem(7, *tile),
            vmem(5, padded2, depth), vmem(layers + 2, padded, depth), vmem(5, *layer), vmem(layers, *layer),
            vmem(1, quarter, depth // 4), pltpu.SMEM((blocks,), jnp.int32),
            pltpu.SemaphoreType.DMA, pltpu.SemaphoreType.DMA((layers + 1,)),
        ],
        (block_owner, gathered, *middle, inputs, new, *margin, *fine, *border, within_in),
        pl.ANY,
    )
    return solved, owned


def solution(mesh):
    split = P(("groups", "gx"), None, None)
    return jax.shard_map(
        on_device,
        mesh=mesh,
        in_specs=(split, split, split, P("groups")),
        out_specs=(split, split),
        check_vma=False,
    )
```

```python
import jax
import jax.numpy as jnp
from jax import lax
from jax.experimental import pallas as pl
from jax.experimental.pallas import tpu as pltpu
from jax.sharding import PartitionSpec as P

STIFFNESS = 100.0
EPSILON = 0.01
COARSE_SWEEPS = 4
PAD = 8


def between_chips(block):
    return lax.ppermute(block, "gx", [(i, i + 1 if i % 2 else i - 1) for i in range(1, lax.axis_size("gx") - 1)])


def within_chip(block):
    return lax.ppermute(block, "gx", [(i, i ^ 1) for i in range(lax.axis_size("gx"))])


def by_side(across, within):
    on_left = lax.axis_index("gx") % 2 == 0
    return jnp.where(on_left, across, within), jnp.where(on_left, within, across)


def lanes_of(shape):
    return lax.broadcasted_iota(jnp.int32, shape, len(shape) - 1)


def rows_of(shape):
    return lax.broadcasted_iota(jnp.int32, shape, len(shape) - 2)


def ahead(values, step, axis):
    return pltpu.roll(values, values.shape[axis] - step, axis)


def behind(values, step, axis):
    return pltpu.roll(values, step, axis)


def with_partner(values, step, axis):
    index = lax.broadcasted_iota(jnp.int32, values.shape, axis)
    partner = jnp.where((index & step) == 0, ahead(values, step, axis), behind(values, step, axis))
    return values + partner


def even_row_sum(scratch, rows):
    return scratch[pl.ds(0, rows, 2), :] + scratch[pl.ds(1, rows, 2), :]


def core_of():
    return lax.axis_index("gx") % 2


def own_layer(u, layers):
    return u + core_of() * (layers - 1 - 2 * u)


def three_parts(ref):
    third = ref.shape[0] // 3
    return [ref.at[pl.ds(k * third, third)] for k in range(3)]


def odd_cells(ref, rows, first):
    return jnp.where(first, ref[pl.ds(0, rows, 2), :], ref[pl.ds(1, rows, 2), :])


def into_both_rows(ref, values):
    rows = values.shape[0]
    ref[pl.ds(0, rows, 2), :] = values
    ref[pl.ds(1, rows, 2), :] = values


def cell_coef(value):
    return STIFFNESS * (value * value + EPSILON)


class Plane:
    def __init__(self, height, depth):
        self.height, self.half, self.depth = height, height // 2, depth
        self.row, self.lane = rows_of((height, depth)), lanes_of((height, depth))
        self.parity = self.row + self.lane + core_of()
        self.half_lane = lanes_of((self.half, depth))
        self.body = pl.ds(PAD, height)
        self.up, self.down = pl.ds(PAD + 1, height), pl.ds(PAD - 1, height)

    def even(self, u):
        return ((self.parity + u) & 1) == 0

    def odd_first(self, u):
        return ((self.half_lane + core_of() + u) & 1) != 0

    def put(self, ref, values):
        edge = jnp.zeros((PAD, self.depth), jnp.float32)
        ref[:PAD] = edge
        ref[PAD + self.height:] = edge
        ref[self.body] = values

    def face_y(self, here):
        return jnp.where(self.row < self.height - 1, 0.5 * (here + ahead(here, 1, 0)), 0.0)

    def face_z(self, here):
        return jnp.where(self.lane < self.depth - 1, 0.5 * (here + ahead(here, 1, 1)), 0.0)

    def packed(self, outer, inner, core):
        return jnp.where((self.half_lane & 1) == core, outer, inner)

    def both_rows(self, ref):
        return even_row_sum(ref, self.half)

    def summed(self, values, ref):
        ref[...] = values
        return with_partner(self.both_rows(ref), 1, 1)

    def odd_rows(self, values, ref):
        ref[...] = values
        return with_partner(ref[pl.ds(1, self.half, 2), :], 1, 1)

    def odd_lanes(self, values, ref):
        ref[...] = values
        sums = self.both_rows(ref)
        return jnp.where((self.half_lane & 1) == 0, ahead(sums, 1, 1), sums)


def in_layer(plane, fy, fz, fzl, padded):
    here = padded[plane.body]
    total = fy[plane.body] * padded[plane.up] + fy[plane.down] * padded[plane.down]
    return total + (fz[...] * ahead(here, 1, 1) + fzl[...] * behind(here, 1, 1))


def edge_kernel(inputs, out):
    iterate, source, phase = three_parts(inputs)
    layers, height, depth = iterate.shape
    plane = Plane(height, depth)
    near, inner, far = [own_layer(u, layers) for u in (layers - 1, layers - 2, layers - 3)]
    coef_near, coef_inner, coef_far = [cell_coef(phase[k]) for k in (near, inner, far)]

    def around(here, e):
        fy, fz = plane.face_y(here), plane.face_z(here)
        fyl, fzl = behind(fy, 1, 0), behind(fz, 1, 1)
        total = fy * ahead(e, 1, 0) + fyl * behind(e, 1, 0)
        return total + fz * ahead(e, 1, 1) + fzl * behind(e, 1, 1), fy + fyl + fz + fzl

    face_near, face_far = 0.5 * (coef_inner + coef_near), 0.5 * (coef_inner + coef_far)
    total, weight = around(coef_inner, iterate[inner])
    total = total + face_near * iterate[near] + face_far * iterate[far]
    updated = (source[inner] + total) / (1.0 + (face_near + face_far + weight))
    total, _ = around(coef_near, iterate[near])
    known = jnp.where(plane.even(layers - 1), total + face_near * iterate[inner], face_near * updated)
    out[:height] = coef_near
    out[height:2 * height] = coef_inner
    out[2 * height:3 * height] = source[near] + known
    out[3 * height:] = odd_cells(iterate.at[near], plane.half, plane.odd_first(layers - 1))


def chip_rows(height):
    half, at, places = height // 2, 0, {}
    for name, size in (
        ("coef0", height), ("coef1", height), ("known0", height), ("old0", half), ("moved1", half), ("face2", half),
        ("source2", half), ("fx2", half), ("far2", half),
    ):
        places[name] = pl.ds(at, size)
        at += size
    return places, at


def own_kernel(owner_of, inputs, cell, old, fx, fy, fz, fzl, inv, even):
    iterate, source, phase = three_parts(inputs)
    layers, height, depth = iterate.shape
    plane = Plane(height, depth)
    body = plane.body
    for u in range(layers):
        cell[u] = cell_coef(phase[own_layer(u, layers)])
        plane.put(old.at[u], iterate[own_layer(u, layers)])
    for u in range(layers):
        here = cell[u]
        if u < layers - 1:
            fx[u] = 0.5 * (here + cell[u + 1])
        plane.put(fy.at[u], plane.face_y(here))
        face = plane.face_z(here)
        fz[u] = face
        fzl[u] = behind(face, 1, 1)
    for u in (1, 2):
        weight = (fx[u] + fx[u - 1]) + (fy[u, body] + fy[u, plane.down]) + (fz[u] + fzl[u])
        inverse = 1.0 / (1.0 + weight)
        inv[u - 1] = inverse
        around = in_layer(plane, fy.at[u], fz.at[u], fzl.at[u], old.at[u])
        total = source[own_layer(u, layers)] + around + (fx[u] * old[u + 1, body] + fx[u - 1] * old[u - 1, body])
        plane.put(even.at[u - 1], total * inverse)


def chip_kernel(
    inputs, cell, old_own, fx_own, fy_own, fz_own, fzl_own, inv_own, even_own, within_in,
    message, own2, known1, new, fx_more, fy_margin, fz_margin, fzl_margin, inv_more,
    old_margin, even_more, change, turn,
):
    iterate, source, phase = three_parts(inputs)
    layers, height, depth = iterate.shape
    plane = Plane(height, depth)
    body, half = plane.body, plane.half
    places, _ = chip_rows(height)
    margin = layers

    def part(k):
        return within_in[k * height:(k + 1) * height]

    def s(u):
        return source[own_layer(u, layers)]

    into_both_rows(turn.at[0], within_in[3 * height:])
    plane.put(old_margin, turn[0])
    fx_more[0] = 0.5 * (cell[layers - 1] + part(0))
    fx_more[1] = 0.5 * (part(0) + part(1))
    plane.put(fy_margin, plane.face_y(part(0)))
    face = plane.face_z(part(0))
    fz_margin[...] = face
    fzl_margin[...] = behind(face, 1, 1)
    fx = [fx_own.at[u] for u in range(3)] + [fx_more.at[0], fx_more.at[1]]
    fy = [fy_own.at[u] for u in range(layers)] + [fy_margin]
    fz = [fz_own.at[u] for u in range(layers)] + [fz_margin]
    fzl = [fzl_own.at[u] for u in range(layers)] + [fzl_margin]
    old = [old_own.at[u] for u in range(layers)] + [old_margin]
    inv = [None, inv_own.at[0], inv_own.at[1], inv_more.at[0], inv_more.at[1]]
    even = [None, even_own.at[0], even_own.at[1], even_more.at[0], even_more.at[1]]
    for u in (margin - 1, margin):
        weight = (fx[u][...] + fx[u - 1][...]) + (fy[u][body] + fy[u][plane.down]) + (fz[u][...] + fzl[u][...])
        inv[u][...] = 1.0 / (1.0 + weight)

    def around(ref, u):
        return in_layer(plane, fy[u], fz[u], fzl[u], ref[u])

    u = margin - 1
    total = s(u) + around(old, u) + (fx[u][...] * old[u + 1][body] + fx[u - 1][...] * old[u - 1][body])
    plane.put(even[u], total * inv[u][...])
    plane.put(even[margin], (part(2) + fx[u][...] * old[u][body]) * inv[margin][...])
    for u in range(2, margin + 1):
        if u < margin:
            total = s(u) + around(even, u) + (fx[u][...] * even[u + 1][body] + fx[u - 1][...] * even[u - 1][body])
        else:
            total = part(2) + around(even, u) + fx[u - 1][...] * even[u - 1][body]
        fresh = total * inv[u][...]
        new[u - 2] = fresh
        plane.put(change.at[u - 2], fresh - old[u][body])
    change = {u: change.at[u - 2] for u in range(2, margin + 1)}

    one = fx[1][...] * change[2][body]
    two = around(change, 2) + fx[2][...] * change[3][body]
    three = around(change, 3) + (fx[2][...] * change[2][body] + fx[3][...] * change[4][body])
    outer = jnp.where(plane.even(1), one, 0.0)
    inner = jnp.where(plane.even(2), two, 0.0) + jnp.where(plane.even(3), three, 0.0)
    core = core_of()

    def tile(name, outer, inner):
        message[places[name], :] = plane.packed(outer, inner, core)

    tile("source2", plane.summed(outer, turn.at[1]), plane.summed(inner, turn.at[2]))
    tile("fx2", plane.summed(fx[1][...], turn.at[3]), plane.summed(fx[3][...], turn.at[4]))
    fy2 = [plane.odd_rows(fy[u][body] + fy[u + 1][body], turn.at[5 + u // 2]) for u in (0, 2)]
    fz2 = [plane.odd_lanes(fz[u][...] + fz[u + 1][...], turn.at[7 + u // 2]) for u in (0, 2)]
    own2[0], own2[1] = plane.packed(*fy2, core), plane.packed(*fz2, core)
    tile("far2", fy2[1], fz2[1])
    for u in range(2):
        message[places["coef%d" % u], :] = cell[u]
    first = s(0) + around(old, 0) + fx[0][...] * old[1][body]
    second = s(0) + fx[0][...] * even[1][body]
    message[places["known0"], :] = jnp.where(plane.even(0), first, second)
    message[places["old0"], :] = odd_cells(iterate.at[own_layer(0, layers)], half, plane.odd_first(0))
    total = s(1) + around(even, 1) + fx[1][...] * even[2][body]
    known1[...] = total
    turn[9] = total * inv[1][...] - old[1][body]
    message[places["moved1"], :] = odd_cells(turn.at[9], half, plane.odd_first(1))
    message[places["face2"], :] = odd_cells(fx[1], half, plane.odd_first(1))


def border_kernel(
    inputs, message, own2, known1, new_in, fx_in, fy_in, fz_in, fzl_in, inv_in, across_in,
    within, fx2_in, new, known, fx, fy, fz, fzl, inv,
    old, even, change, turn, face_y, face_z, face_zl,
):
    iterate, source, _ = three_parts(inputs)
    layers, height, depth = iterate.shape
    plane = Plane(height, depth)
    body, half = plane.body, plane.half
    places, _ = chip_rows(height)
    core, last = core_of(), lax.axis_size("gx") - 1
    position = lax.axis_index("gx")

    def mine(name):
        return message[places[name], :]

    def theirs(name):
        return across_in[places[name], :]

    def opened(name, k):
        into_both_rows(turn.at[k], theirs(name))
        return turn[k]

    for k in range(2):
        here = theirs("coef%d" % k)
        plane.put(face_y.at[k], plane.face_y(here))
        face = plane.face_z(here)
        face_z[k] = face
        face_zl[k] = behind(face, 1, 1)
    fy[...], fz[...], fzl[...] = face_y[0], face_z[0], face_zl[0]
    there = position - 1 + 2 * core
    border = jnp.where((there >= 0) & (there <= last), 0.5 * (mine("coef0") + theirs("coef0")), 0.0)
    face1 = 0.5 * (theirs("coef0") + theirs("coef1"))
    face2 = opened("face2", 2)
    fx[0], fx[1] = border, face1

    def inverse(faces, fy, fz, fzl):
        weight = faces + (fy[body] + fy[plane.down]) + (fz[...] + fzl[...])
        return 1.0 / (1.0 + weight)

    inv_own = inverse(fx_in[0] + border, fy_in.at[0], fz_in.at[0], fzl_in.at[0])
    inv_near = inverse(border + face1, face_y.at[0], face_z.at[0], face_zl.at[0])
    inv_far = inverse(face1 + face2, face_y.at[1], face_z.at[1], face_zl.at[1])
    inv[0], inv[1] = inv_near, inv_own
    old_own, old_next = iterate[own_layer(0, layers)], iterate[own_layer(1, layers)]
    old_near, far = opened("old0", 0), opened("moved1", 1)
    even_own = (mine("known0") + border * old_near) * inv_own
    even_near = (theirs("known0") + border * old_own) * inv_near
    plane.put(even.at[0], even_near)
    plane.put(even.at[1], even_own)

    def near(ref, k):
        return in_layer(plane, face_y.at[k], face_z.at[k], face_zl.at[k], ref)

    def own(ref, u):
        return in_layer(plane, fy_in.at[u], fz_in.at[u], fzl_in.at[u], ref)

    odd_own = (mine("known0") + own(even.at[1], 0) + border * even_near) * inv_own
    odd_near = (theirs("known0") + near(even.at[0], 0) + border * even_own) * inv_near
    odd_next = (known1[...] + fx_in[0] * even_own) * inv_in[0]
    far = far + face1 * even_near * inv_far
    new[0], new[1], new[2] = odd_near, odd_own, odd_next
    near_by, here, following = odd_near - old_near, odd_own - old_own, odd_next - old_next
    for k, values in enumerate((far, near_by, here, following)):
        plane.put(change.at[k], values)
    plane.put(old.at[0], old_near)
    known[...] = theirs("known0") + face1 * far - near(old.at[0], 0)

    def residual(u, values):
        return jnp.where(plane.even(u), values, 0.0)

    own_outer = residual(1, own(change.at[3], 1) + fx_in[0] * here)
    own_outer = own_outer + residual(0, own(change.at[2], 0) + (fx_in[0] * following + border * near_by))
    own_inner = residual(2, fx_in[1] * following)
    its_outer = residual(-1, near(change.at[1], 0) + (face1 * far + border * here))
    its_outer = its_outer + residual(-2, near(change.at[0], 1) + face1 * near_by)
    its_inner = residual(-3, face2 * far)
    sums = [plane.summed(values, turn.at[3 + k]) for k, values in enumerate((own_outer, own_inner, its_outer, its_inner))]
    within[0] = mine("source2") + plane.packed(sums[0], sums[1], core)
    within[5] = theirs("source2") + plane.packed(sums[2], sums[3], 1 - core)
    within[6] = theirs("fx2")
    far2 = theirs("far2")
    far2_swap = jnp.where((plane.half_lane & 1) == 0, ahead(far2, 1, 1), behind(far2, 1, 1))
    near_fy2 = plane.odd_rows(face_y[0, body] + face_y[1, body], turn.at[1])
    near_fz2 = plane.odd_lanes(face_z[0] + face_z[1], turn.at[2])
    within[7] = plane.packed(near_fy2, far2_swap, 1 - core)
    within[8] = plane.packed(near_fz2, far2, 1 - core)
    fx2_in[...] = mine("fx2")
    middle = jnp.where((plane.half_lane & 1) == 0, ahead(mine("fx2"), 1, 1), behind(mine("fx2"), 1, 1))
    within[1] = plane.packed(plane.summed(border, turn.at[7]), middle, core)
    within[2], within[3] = own2[0], own2[1]
    turn[0] = source[own_layer(layers - 1, layers)] + fx_in[layers - 2] * new_in[layers - 4]
    within[4] = odd_cells(turn.at[0], half, jnp.logical_not(plane.odd_first(layers - 1)))


def neigh2(e2, fx2, fxl2, fy2, fz2, fzl2, first_of_two, tiles):
    half = fx2.shape[1]
    body, up, down = pl.ds(PAD, half), pl.ds(PAD + 1, half), pl.ds(PAD - 1, half)
    needed = range(tiles[0], tiles[-1] + 3)
    here = {j: e2[j, body] for j in needed}
    after = {j: ahead(here[j], 1, 1) for j in needed}
    before = {j: behind(here[j], 1, 1) for j in needed}
    found = []
    for j in tiles:
        k = j + 1
        upper = jnp.where(first_of_two, after[k], before[k + 1])
        lower = jnp.where(first_of_two, after[k - 1], before[k])
        sums = fx2[j] * upper + fxl2[j] * lower
        sums = sums + fy2[j, body] * e2[k, up] + fy2[j, down] * e2[k, down]
        sums = sums + fz2[j] * ahead(here[k], 2, 1) + fzl2[j] * behind(here[k], 2, 1)
        found.append(sums)
    return found


def parities2(half, lanes):
    row, lane = rows_of((half, lanes)), lanes_of((half, lanes))
    return (lane & 1) == 0, ((row + (lane & 1) + (lane >> 1)) & 1) == 0


def group(values):
    return with_partner(with_partner(values, 1, 1), 2, 1)


def packed_odd(values, pair):
    half, lanes = values.shape
    lane = lanes_of((half // 2, lanes))
    pair[...] = values
    return odd_cells(pair, half // 2, (((lane & 1) + (lane >> 1)) & 1) != 0)


def middle_down_kernel(
    own, fx2_in, within_in,
    slots, e2_out, s2, fx2, fxl2, fy2, fz2, fzl2, inv2,
    e2, pair,
):
    _, half, lanes = own.shape
    quarter = half // 2
    first_of_two, even2 = parities2(half, lanes)
    body, down = pl.ds(PAD, half), pl.ds(PAD - 1, half)
    edge = jnp.zeros((PAD, lanes), jnp.float32)
    for j in (0, 5):
        e2[j] = jnp.zeros((half + 2 * PAD, lanes), jnp.float32)

    def pair_of(k):
        return by_side(own[k], within_in[k])

    def four(k):
        (left, right), (far_left, far_right) = pair_of(k), pair_of(5 + k)
        return far_left, left, right, far_right

    for j, (source, fy, fz) in enumerate(zip(four(0), four(2), four(3))):
        s2[j] = source
        fy2[j, :PAD] = edge
        fy2[j, body] = fy
        fy2[j, PAD + half:] = edge
        fz2[j] = fz
        fzl2[j] = behind(fz, 2, 1)

    def between(left, right):
        return jnp.where(first_of_two, ahead(left, 1, 1), behind(right, 1, 1))

    fxl0, fxl1, fxr2, fxr3 = four(1)
    inner = fx2_in[...]
    fxr1, _ = by_side(inner, between(fxl1, inner))
    fxl2_, _ = by_side(between(inner, fxr2), inner)
    for j, (face, low) in enumerate(
        ((between(fxl0, fxl1), fxl0), (fxr1, fxl1), (fxr2, fxl2_), (fxr3, between(fxr2, fxr3)))
    ):
        fx2[j], fxl2[j] = face, low
        weight = face + low + fy2[j, body] + fy2[j, down] + fz2[j] + fzl2[j]
        inverse = 1.0 / (8.0 + weight)
        inv2[j] = inverse
        e2[j + 1, :PAD] = edge
        e2[j + 1, PAD + half:] = edge
        e2[j + 1, body] = s2[j] * inverse

    def neigh(tiles):
        return neigh2(e2, fx2, fxl2, fy2, fz2, fzl2, first_of_two, tiles)

    fresh = [(s2[j] + sums) * inv2[j] for j, sums in enumerate(neigh((0, 1, 2, 3)))]
    for j in range(4):
        e2[j + 1, body] = fresh[j]
        e2_out[j] = fresh[j]
    lane = lanes_of((quarter, lanes))
    odd_layer, odd_depth = (lane & 1) != 0, (lane & 2) != 0
    chips = slots.shape[0]
    for k, sums in enumerate(neigh((1, 2))):
        j = k + 1
        pair[k] = jnp.where(even2, sums, 0.0)
        item = (lane - (lax.axis_index("gx") // 2 * 2 + k) // (chips // 2)) & 3
        source = group(even_row_sum(pair.at[k], quarter))
        fx = group(jnp.where(odd_layer, even_row_sum(fx2.at[j], quarter), 0.0))
        fxl = group(jnp.where(odd_layer, 0.0, even_row_sum(fxl2.at[j], quarter)))
        fy = group(fy2[j, pl.ds(PAD + 1, quarter, 2), :])
        fz = group(jnp.where(odd_depth, even_row_sum(fz2.at[j], quarter), 0.0))
        weight = (fx + fxl) + (fy + behind(fy, 1, 0)) + (fz + behind(fz, 4, 1))
        start = source / (64.0 + weight)
        tile = jnp.where(item == 0, start, jnp.where(item == 1, fx, jnp.where(item == 2, fy, fz)))
        for c in range(chips):
            slots[c, k] = tile
    halo = packed_odd(jnp.where(first_of_two, fresh[2], fresh[1]), pair.at[2])
    for c in range(chips):
        slots[c, 2] = halo


def joined(one, two):
    return jnp.concatenate([part for part in (one, two) if part.shape[0]], 0)


class Level:
    def __init__(self, mass, source, faces, row_step, lane_step, slot_step):
        self.source, self.row_step, self.lane_step, self.slot_step = source, row_step, lane_step, slot_step
        self.fx, self.fy, self.fz = faces
        self.tiles = source.shape[0]
        shape = source.shape
        self.lane = lanes_of(shape)
        layer = lax.broadcasted_iota(jnp.int32, shape, 0) if self.tiles > 1 else self.lane // slot_step
        self.even = ((layer + rows_of(shape) // row_step + self.lane // lane_step) & 1) == 0
        self.fxl = self.lower(self.fx)
        self.fyl = self.row_shifts(self.fy)[1]
        self.fzl = behind(self.fz, lane_step, 2)
        weight = (self.fx + self.fxl) + (self.fy + self.fyl) + (self.fz + self.fzl)
        self.inv = 1.0 / (mass + weight)

    def upper(self, e):
        return joined(e[1:], ahead(e[:1], self.slot_step, 2))

    def lower(self, e):
        return joined(behind(e[-1:], self.slot_step, 2), e[:-1])

    def row_shifts(self, e):
        return ahead(e, self.row_step, 1), behind(e, self.row_step, 1)

    def neigh(self, e):
        above, below = self.row_shifts(e)
        total = (self.fx * self.upper(e) + self.fxl * self.lower(e)) + (self.fy * above + self.fyl * below)
        return total + (self.fz * ahead(e, self.lane_step, 2) + self.fzl * behind(e, self.lane_step, 2))

    def start(self):
        return self.source * self.inv

    def update(self, e):
        return self.start() + self.neigh(e) * self.inv

    def cycle(self, deeper):
        odd = self.update(self.start())
        residual = jnp.where(self.even, self.neigh(odd), 0.0)
        fix = deeper(self.restricted(residual), self.coarse_faces())
        even = self.update(odd + self.prolonged(fix))
        return jnp.where(self.even, even, self.update(even))

    def coarse_slot_step(self):
        return self.slot_step if self.tiles > 1 else 2 * self.slot_step

    def pairs(self, values):
        if self.tiles == 1:
            return with_partner(values, self.slot_step, 2)
        halves = values.reshape(self.tiles // 2, 2, *values.shape[1:])
        return halves[:, 0] + halves[:, 1]

    def odd_layers(self, values):
        if self.tiles == 1:
            return with_partner(jnp.where((self.lane & self.slot_step) != 0, values, 0.0), self.slot_step, 2)
        return values.reshape(self.tiles // 2, 2, *values.shape[1:])[:, 1]

    def row_pairs(self, values):
        return with_partner(values, self.row_step, 1)

    def odd_rows(self, values):
        odd = (rows_of(values.shape) & self.row_step) != 0
        return with_partner(jnp.where(odd, values, 0.0), self.row_step, 1)

    def restricted(self, values):
        return with_partner(self.row_pairs(self.pairs(values)), self.lane_step, 2)

    def coarse_faces(self):
        fx = with_partner(self.row_pairs(self.odd_layers(self.fx)), self.lane_step, 2)
        fy = with_partner(self.odd_rows(self.pairs(self.fy)), self.lane_step, 2)
        return fx, fy, self.restricted(jnp.where((self.lane & self.lane_step) != 0, self.fz, 0.0))

    def prolonged(self, fix):
        if self.tiles == 1:
            return fix
        both = jnp.concatenate([fix[:, None], fix[:, None]], 1)
        return both.reshape(self.tiles, *fix.shape[1:])


class Rows(Level):
    def __init__(self, mass, source, faces, scratch):
        self.scratch, self.used = scratch, 0
        self.rows = source.shape[1]
        super().__init__(mass, source, faces, 1, 4, 1)

    def start(self):
        return self.source

    def place(self):
        self.used += 1
        return self.scratch.at[self.used % self.scratch.shape[0]]

    def row_shifts(self, e):
        place = self.place()
        edge = jnp.zeros((e.shape[0], PAD, e.shape[2]), jnp.float32)
        place[:, :PAD] = edge
        place[:, PAD + self.rows:] = edge
        place[:, pl.ds(PAD, self.rows)] = e
        return place[:, pl.ds(PAD + 1, self.rows)], place[:, pl.ds(PAD - 1, self.rows)]

    def every_other(self, values, starts):
        place, tiles = self.place(), values.shape[0]
        place[:tiles, : self.rows] = values
        found = 0.0
        for start in starts:
            found = found + jnp.concatenate(
                [place[j, pl.ds(start, self.rows // 2, 2), :][None] for j in range(tiles)], 0
            )
        return found

    def row_pairs(self, values):
        return self.every_other(values, (0, 1))

    def odd_rows(self, values):
        return self.every_other(values, (1,))

    def prolonged(self, fix):
        place, tiles = self.place(), fix.shape[0]
        for j in range(tiles):
            into_both_rows(place.at[j, pl.ds(0, self.rows)], fix[j])
        return super().prolonged(place[:tiles, : self.rows])


def coarsest(mass, source, faces, *steps):
    row_step, lane_step, slot_step = steps
    level = Level(mass, source, faces, *steps)
    counts = source.shape[1] // row_step, source.shape[2] // lane_step, 4 // slot_step
    frames = [(m, k, q) for m in range(counts[0]) for k in range(counts[1]) for q in range(counts[2])]
    place = level.lane & 3

    def spread(values):
        copies = {}
        for m, k, q in frames:
            if k:
                copies[m, k, q] = behind(copies[m, 0, q], k * lane_step, 2)
            elif q:
                by = q * slot_step
                one, two = behind(copies[m, 0, 0], by, 2), ahead(copies[m, 0, 0], 4 - by, 2)
                copies[m, k, q] = jnp.where(place >= by, one, two)
            else:
                copies[m, k, q] = behind(values, m * row_step, 1) if m else values
        return copies

    start, inv, fx, fy, fz = [spread(values) for values in (source * level.inv, level.inv, level.fx, level.fy, level.fz)]

    def shifted(copies, frame, axis, by):
        moved = list(frame)
        moved[axis] = (frame[axis] - by) % counts[axis]
        return copies[tuple(moved)]

    def along_x(copies, frame, by):
        here, wrapped = copies[frame], shifted(copies, frame, 2, by)
        return joined(here[1:], wrapped[:1]) if by > 0 else joined(wrapped[-1:], here[:-1])

    same = level.tiles == 1 and counts[2] == 2, counts[0] == 2, counts[1] == 2
    weights = {}
    for frame in frames:
        pairs = [
            (fx[frame], along_x(fx, frame, -1)),
            (fy[frame], shifted(fy, frame, 0, -1)),
            (fz[frame], shifted(fz, frame, 1, -1)),
        ]
        weights[frame] = [
            ((up + low) * inv[frame], None) if merged else (up * inv[frame], low * inv[frame])
            for (up, low), merged in zip(pairs, same)
        ]

    def update(e):
        fresh = {}
        for frame in frames:
            moves = along_x, lambda c, f, by: shifted(c, f, 0, by), lambda c, f, by: shifted(c, f, 1, by)
            total = 0.0
            for (up, low), move in zip(weights[frame], moves):
                part = up * move(e, frame, 1)
                total = total + (part if low is None else part + low * move(e, frame, -1))
            fresh[frame] = start[frame] + total
        return fresh

    even = start
    odd = update(even)
    for turn in range(COARSE_SWEEPS - 1):
        even = update(odd)
        odd = update(even)
    return jnp.where(level.even, even[0, 0, 0], odd[0, 0, 0])


def small_cycle(mass, source, faces, row_step, lane_step, slot_step, between):
    if between == 0:
        return coarsest(mass, source, faces, row_step, lane_step, slot_step)
    level = Level(mass, source, faces, row_step, lane_step, slot_step)
    return level.cycle(
        lambda inner, inner_faces: small_cycle(
            8.0 * mass, inner, inner_faces, 2 * row_step, 2 * lane_step, level.coarse_slot_step(), between - 1
        )
    )


def coarse_kernel(
    owner_of, gathered, e2_in, s2_in, fx2_in, fxl2_in, fy2_in, fz2_in, fzl2_in, inv2_in,
    inputs, new_in, fx_more, fy_margin, fz_margin, fzl_margin, inv_more, fx_in, fy_in, fz_in, fzl_in, inv_in,
    new_out, known_out, fx_out, fy_out, fz_out, fzl_out, inv_out, within_in,
    solved_out, owned_out,
    e3, rows3, pair, e2, e1, cor, solved, owned, owner_here, fetch_sem, sems,
):
    fetch = pltpu.make_async_copy(owner_of, owner_here, fetch_sem)
    fetch.start()
    chips, _, quarter, lanes = gathered.shape
    blocks = 2 * chips
    half, height = 2 * quarter, 4 * quarter
    position, last = lax.axis_index("gx"), blocks - 1

    slot = lanes_of((quarter, lanes)) & 3
    spread = blocks // 4
    tiles = [gathered[chip, k] for chip in reversed(range(chips)) for k in range(2)]
    items = []
    for k in range(4):
        packs = []
        for j in range(spread):
            value = tiles[j + (3 - k) % 4 * spread]
            for at in range(3):
                value = jnp.where(slot == at, tiles[j + (at - k) % 4 * spread], value)
            if k:
                value = jnp.where(slot < 4 - k, ahead(value, k, 1), behind(value, 4 - k, 1))
            packs.append(value[None])
        items.append(jnp.concatenate(packs, 0))
    third = Rows(64.0, items[0], items[1:], rows3)
    e3[...] = third.cycle(
        lambda inner, faces: small_cycle(512.0, inner, faces, 1, 8, third.coarse_slot_step(), 2)
    )

    fetch.wait()
    owner = owner_here[position]
    wide, narrow = lanes_of((lanes, lanes)), rows_of((lanes, lanes))
    take = jnp.where(narrow == 4 * wide + owner // spread, 1.0, 0.0)
    block = jnp.dot(
        e3[owner % spread], take, precision=lax.Precision.HIGHEST, preferred_element_type=jnp.float32
    )
    owned[0] = block[:, : lanes // 4]
    copies = [pltpu.make_async_copy(owned, owned_out, sems.at[0])]
    copies[0].start()

    first_of_two, even2 = parities2(half, lanes)
    body2 = pl.ds(PAD, half)
    edge = jnp.zeros((PAD, lanes), jnp.float32)
    core = core_of()
    s2, fx2, fxl2, fy2, fz2, fzl2, inv2 = [
        ref.at[pl.ds(core, 3)] for ref in (s2_in, fx2_in, fxl2_in, fy2_in, fz2_in, fzl2_in, inv2_in)
    ]
    next_chip = jnp.clip(position // 2 - 1 + 2 * core, 0, chips - 1)
    into_both_rows(pair.at[5], gathered[chips - 1 - next_chip, 2])
    halo = pair[5]
    before = (
        by_side(halo, e2_in[0])[0], by_side(jnp.where(first_of_two, halo, e2_in[0]), e2_in[1])[0],
        by_side(e2_in[1], e2_in[2])[0],
        by_side(e2_in[2], jnp.where(first_of_two, e2_in[3], halo))[0], by_side(e2_in[3], halo)[0],
    )
    for k in range(5):
        j = jnp.clip(position + k - 2, 0, last)
        into_both_rows(pair.at[k], group(jnp.where(slot == j // spread, e3[j % spread], 0.0)))
        e2[k, :PAD] = edge
        e2[k, PAD + half:] = edge
        e2[k, body2] = before[k] + pair[k]

    def update2():
        sums = neigh2(e2, fx2, fxl2, fy2, fz2, fzl2, first_of_two, (0, 1, 2))
        return [(s2[j] + sums[j]) * inv2[j] for j in range(3)]

    fresh = update2()
    for j in range(3):
        e2[j + 1, body2] = fresh[j]
    fixes2 = [jnp.where(even2, even, odd) for even, odd in zip(fresh, update2())]

    _, source, _ = three_parts(inputs)
    layers = source.shape[0]
    plane = Plane(height, lanes)
    body1 = plane.body
    near_lane = (lanes_of((half, lanes)) & 1) == core
    swaps = [jnp.where(first_of_two, ahead(v, 1, 1), behind(v, 1, 1)) for v in fixes2]
    outer, inner = by_side(fixes2[0], fixes2[2])
    outer_swap, inner_swap = by_side(swaps[0], swaps[2])
    coarse = (
        jnp.where(near_lane, outer_swap, outer), jnp.where(near_lane, fixes2[1], swaps[1]),
        jnp.where(near_lane, swaps[1], fixes2[1]), jnp.where(near_lane, inner, inner_swap),
    )
    fixes = []
    for k in range(4):
        into_both_rows(cor.at[k], coarse[k])
        fixes.append(cor[k])
    for u in range(-1, layers + 1):
        before = new_out[u + 1] if u < 2 else new_in[u - 2]
        plane.put(e1.at[u + 1], before + fixes[(u + 2) // 2])

    def fx1(u):
        if u < 0:
            return fx_out[-1 - u]
        return fx_in[u] if u < layers - 1 else fx_more[u - layers + 1]

    def inv1(u):
        if u <= 0:
            return inv_out[u + 1]
        return inv_in[u - 1] if u < layers - 1 else inv_more[u - layers + 1]

    def around1(u):
        if u < 0:
            return in_layer(plane, fy_out, fz_out, fzl_out, e1.at[0])
        if u == layers:
            return in_layer(plane, fy_margin, fz_margin, fzl_margin, e1.at[u + 1])
        return in_layer(plane, fy_in.at[u], fz_in.at[u], fzl_in.at[u], e1.at[u + 1])

    def updated1(u):
        sums = around1(u) + (fx1(u) * e1[u + 2, body1] + fx1(u - 1) * e1[u, body1])
        return (source[own_layer(u, layers)] + sums) * inv1(u)

    for u in range(layers):
        e1[u + 1, body1] = jnp.where(plane.even(u), updated1(u), e1[u + 1, body1])
    e1[0, body1] = (known_out[...] + fx1(-2) * fixes[0] + (around1(-1) + fx1(-1) * e1[1, body1])) * inv1(-1)
    into_both_rows(cor.at[4], within_in[4])
    sums = cor[4] + fx1(layers) * fixes[3] + (around1(layers) + fx1(layers - 1) * e1[layers, body1])
    e1[layers + 1, body1] = sums * inv1(layers)
    for u in range(layers):
        solved[u] = jnp.where(plane.even(u), e1[u + 1, body1], updated1(u))
        copies.append(
            pltpu.make_async_copy(solved.at[u], solved_out.at[own_layer(u, layers)], sems.at[u + 1])
        )
        copies[-1].start()
    for copy in copies:
        copy.wait()


def f32(*shape):
    return jax.ShapeDtypeStruct(shape, jnp.float32)


def vmem(*shape):
    return pltpu.VMEM(shape, jnp.float32)


def call(kernel, outs, scratch, operands, out_space=pltpu.VMEM):
    def size(shape):
        count = 4
        for extent in shape:
            count *= extent
        return count

    sized = [array for array in (*scratch, *outs, *operands) if hasattr(array, "shape")]
    asked = 8 * 2**20 + sum(size(array.shape) for array in sized)
    return pl.pallas_call(
        kernel,
        out_shape=tuple(outs),
        in_specs=[pl.BlockSpec(memory_space=pltpu.VMEM)] * len(operands),
        out_specs=tuple([pl.BlockSpec(memory_space=out_space)] * len(outs)),
        scratch_shapes=scratch,
        compiler_params=pltpu.CompilerParams(vmem_limit_bytes=asked),
    )(*operands)


def on_device(iterate, source, phase_field, block_owner):
    layers, height, depth = iterate.shape
    half, quarter = height // 2, height // 4
    blocks = lax.axis_size("gx")
    padded, padded2 = height + 2 * PAD, half + 2 * PAD
    inputs = sum(
        jnp.pad(block, ((k * layers, (2 - k) * layers), (0, 0), (0, 0)))
        for k, block in enumerate((iterate, source, phase_field))
    )
    edge, = call(edge_kernel, [f32(3 * height + half, depth)], [], (inputs,))
    edge_in = within_chip(edge)
    layer, tile, tall = (height, depth), (half, depth), (padded, depth)
    cell, old, *fine, even = call(
        own_kernel,
        [
            f32(layers, *layer), f32(layers, *tall), f32(layers - 1, *layer), f32(layers, *tall),
            f32(layers, *layer), f32(layers, *layer), f32(2, *layer), f32(2, *tall),
        ],
        [], (block_owner, inputs),
    )
    message, own2, known1, new, *margin = call(
        chip_kernel,
        [
            f32(chip_rows(height)[1], depth), f32(2, *tile), f32(*layer), f32(3, *layer),
            f32(2, *layer), f32(*tall), f32(*layer), f32(*layer), f32(2, *layer),
        ],
        [vmem(*tall), vmem(2, *tall), vmem(3, *tall), vmem(10, *layer)],
        (inputs, cell, old, *fine, even, edge_in),
    )
    within, fx2, *border = call(
        border_kernel,
        [
            f32(9, *tile), f32(*tile), f32(3, *layer), f32(*layer), f32(2, *layer),
            f32(padded, depth), f32(*layer), f32(*layer), f32(2, *layer),
        ],
        [
            vmem(1, padded, depth), vmem(2, padded, depth), vmem(4, padded, depth), vmem(8, *layer),
            vmem(2, padded, depth), vmem(2, *layer), vmem(2, *layer),
        ],
        (inputs, message, own2, known1, new, *fine, between_chips(message)),
    )
    within_in = within_chip(within)
    plain = f32(4, *tile)
    slots, *middle = call(
        middle_down_kernel,
        [f32(blocks // 2, 3, quarter, depth), plain, plain, plain, plain, f32(4, padded2, depth)] + [plain] * 3,
        [vmem(6, padded2, depth), vmem(3, *tile)],
        (within, fx2, within_in),
    )
    kinds = [[2 * chip + (chip // 2 + core) % 2 for chip in reversed(range(blocks // 2))] for core in range(2)]
    gathered = lax.all_to_all(slots, "gx", 0, 0, axis_index_groups=kinds, tiled=True)
    solved, owned = call(
        coarse_kernel,
        [f32(layers, *layer), f32(1, quarter, depth // 4)],
        [
            vmem(blocks // 4, quarter, depth), vmem(4, blocks // 4, quarter + 2 * PAD, depth), vmem(7, *tile),
            vmem(5, padded2, depth), vmem(layers + 2, padded, depth), vmem(5, *layer), vmem(layers, *layer),
            vmem(1, quarter, depth // 4), pltpu.SMEM((blocks,), jnp.int32),
            pltpu.SemaphoreType.DMA, pltpu.SemaphoreType.DMA((layers + 1,)),
        ],
        (block_owner, gathered, *middle, inputs, new, *margin, *fine, *border, within_in),
        pl.ANY,
    )
    return solved, owned


def solution(mesh):
    split = P(("groups", "gx"), None, None)
    return jax.shard_map(
        on_device,
        mesh=mesh,
        in_specs=(split, split, split, P("groups")),
        out_specs=(split, split),
        check_vma=False,
    )
```

```python
import jax
import jax.numpy as jnp
from jax import lax
from jax.experimental import pallas as pl
from jax.experimental.pallas import tpu as pltpu
from jax.sharding import PartitionSpec as P

STIFFNESS = 100.0
EPSILON = 0.01
COARSE_SWEEPS = 4
PAD = 8


def between_chips(block):
    return lax.ppermute(block, "gx", [(i, i + 1 if i % 2 else i - 1) for i in range(1, lax.axis_size("gx") - 1)])


def within_chip(block):
    return lax.ppermute(block, "gx", [(i, i ^ 1) for i in range(lax.axis_size("gx"))])


def by_side(across, within):
    on_left = lax.axis_index("gx") % 2 == 0
    return jnp.where(on_left, across, within), jnp.where(on_left, within, across)


def lanes_of(shape):
    return lax.broadcasted_iota(jnp.int32, shape, len(shape) - 1)


def rows_of(shape):
    return lax.broadcasted_iota(jnp.int32, shape, len(shape) - 2)


def ahead(values, step, axis):
    return pltpu.roll(values, values.shape[axis] - step, axis)


def behind(values, step, axis):
    return pltpu.roll(values, step, axis)


def with_partner(values, step, axis):
    index = lax.broadcasted_iota(jnp.int32, values.shape, axis)
    partner = jnp.where((index & step) == 0, ahead(values, step, axis), behind(values, step, axis))
    return values + partner


def even_row_sum(scratch, rows):
    return scratch[pl.ds(0, rows, 2), :] + scratch[pl.ds(1, rows, 2), :]


def core_of():
    return lax.axis_index("gx") % 2


def own_layer(u, layers):
    return u + core_of() * (layers - 1 - 2 * u)


def three_parts(ref):
    third = ref.shape[0] // 3
    return [ref.at[pl.ds(k * third, third)] for k in range(3)]


def odd_cells(ref, rows, first):
    return jnp.where(first, ref[pl.ds(0, rows, 2), :], ref[pl.ds(1, rows, 2), :])


def into_both_rows(ref, values):
    rows = values.shape[0]
    ref[pl.ds(0, rows, 2), :] = values
    ref[pl.ds(1, rows, 2), :] = values


def cell_coef(value):
    return STIFFNESS * (value * value + EPSILON)


class Plane:
    def __init__(self, height, depth):
        self.height, self.half, self.depth = height, height // 2, depth
        self.row, self.lane = rows_of((height, depth)), lanes_of((height, depth))
        self.parity = self.row + self.lane + core_of()
        self.half_lane = lanes_of((self.half, depth))
        self.body = pl.ds(PAD, height)
        self.up, self.down = pl.ds(PAD + 1, height), pl.ds(PAD - 1, height)

    def even(self, u):
        return ((self.parity + u) & 1) == 0

    def odd_first(self, u):
        return ((self.half_lane + core_of() + u) & 1) != 0

    def put(self, ref, values):
        edge = jnp.zeros((PAD, self.depth), jnp.float32)
        ref[:PAD] = edge
        ref[PAD + self.height:] = edge
        ref[self.body] = values

    def face_y(self, here):
        return jnp.where(self.row < self.height - 1, 0.5 * (here + ahead(here, 1, 0)), 0.0)

    def face_z(self, here):
        return jnp.where(self.lane < self.depth - 1, 0.5 * (here + ahead(here, 1, 1)), 0.0)

    def packed(self, outer, inner, core):
        return jnp.where((self.half_lane & 1) == core, outer, inner)

    def both_rows(self, ref):
        return even_row_sum(ref, self.half)

    def summed(self, values, ref):
        ref[...] = values
        return with_partner(self.both_rows(ref), 1, 1)

    def odd_rows(self, values, ref):
        ref[...] = values
        return with_partner(ref[pl.ds(1, self.half, 2), :], 1, 1)

    def odd_lanes(self, values, ref):
        ref[...] = values
        sums = self.both_rows(ref)
        return jnp.where((self.half_lane & 1) == 0, ahead(sums, 1, 1), sums)


def in_layer(plane, fy, fz, fzl, padded):
    here = padded[plane.body]
    total = fy[plane.body] * padded[plane.up] + fy[plane.down] * padded[plane.down]
    return total + (fz[...] * ahead(here, 1, 1) + fzl[...] * behind(here, 1, 1))


def edge_kernel(inputs, out):
    iterate, source, phase = three_parts(inputs)
    layers, height, depth = iterate.shape
    plane = Plane(height, depth)
    near, inner, far = [own_layer(u, layers) for u in (layers - 1, layers - 2, layers - 3)]
    coef_near, coef_inner, coef_far = [cell_coef(phase[k]) for k in (near, inner, far)]

    def around(here, e):
        fy, fz = plane.face_y(here), plane.face_z(here)
        fyl, fzl = behind(fy, 1, 0), behind(fz, 1, 1)
        total = fy * ahead(e, 1, 0) + fyl * behind(e, 1, 0)
        return total + fz * ahead(e, 1, 1) + fzl * behind(e, 1, 1), fy + fyl + fz + fzl

    face_near, face_far = 0.5 * (coef_inner + coef_near), 0.5 * (coef_inner + coef_far)
    total, weight = around(coef_inner, iterate[inner])
    total = total + face_near * iterate[near] + face_far * iterate[far]
    updated = (source[inner] + total) / (1.0 + (face_near + face_far + weight))
    total, _ = around(coef_near, iterate[near])
    known = jnp.where(plane.even(layers - 1), total + face_near * iterate[inner], face_near * updated)
    out[:height] = coef_near
    out[height:2 * height] = coef_inner
    out[2 * height:3 * height] = source[near] + known
    out[3 * height:] = odd_cells(iterate.at[near], plane.half, plane.odd_first(layers - 1))


def chip_rows(height):
    half, at, places = height // 2, 0, {}
    for name, size in (
        ("coef0", height), ("coef1", height), ("known0", height), ("old0", half), ("moved1", half), ("face2", half),
        ("source2", half), ("fx2", half), ("far2", half),
    ):
        places[name] = pl.ds(at, size)
        at += size
    return places, at


def own_kernel(owner_of, inputs, cell, old, fx, fy, fz, fzl, inv, even):
    iterate, source, phase = three_parts(inputs)
    layers, height, depth = iterate.shape
    plane = Plane(height, depth)
    body = plane.body
    for u in range(layers):
        cell[u] = cell_coef(phase[own_layer(u, layers)])
        plane.put(old.at[u], iterate[own_layer(u, layers)])
    for u in range(layers):
        here = cell[u]
        if u < layers - 1:
            fx[u] = 0.5 * (here + cell[u + 1])
        plane.put(fy.at[u], plane.face_y(here))
        face = plane.face_z(here)
        fz[u] = face
        fzl[u] = behind(face, 1, 1)
    for u in (1, 2):
        weight = (fx[u] + fx[u - 1]) + (fy[u, body] + fy[u, plane.down]) + (fz[u] + fzl[u])
        inverse = 1.0 / (1.0 + weight)
        inv[u - 1] = inverse
        around = in_layer(plane, fy.at[u], fz.at[u], fzl.at[u], old.at[u])
        total = source[own_layer(u, layers)] + around + (fx[u] * old[u + 1, body] + fx[u - 1] * old[u - 1, body])
        plane.put(even.at[u - 1], total * inverse)


def chip_kernel(
    inputs, cell, old_own, fx_own, fy_own, fz_own, fzl_own, inv_own, even_own, within_in,
    message, own2, known1, new, fx_more, fy_margin, fz_margin, fzl_margin, inv_more,
    old_margin, even_more, change, turn,
):
    iterate, source, phase = three_parts(inputs)
    layers, height, depth = iterate.shape
    plane = Plane(height, depth)
    body, half = plane.body, plane.half
    places, _ = chip_rows(height)
    margin = layers

    def part(k):
        return within_in[k * height:(k + 1) * height]

    def s(u):
        return source[own_layer(u, layers)]

    into_both_rows(turn.at[0], within_in[3 * height:])
    plane.put(old_margin, turn[0])
    fx_more[0] = 0.5 * (cell[layers - 1] + part(0))
    fx_more[1] = 0.5 * (part(0) + part(1))
    plane.put(fy_margin, plane.face_y(part(0)))
    face = plane.face_z(part(0))
    fz_margin[...] = face
    fzl_margin[...] = behind(face, 1, 1)
    fx = [fx_own.at[u] for u in range(3)] + [fx_more.at[0], fx_more.at[1]]
    fy = [fy_own.at[u] for u in range(layers)] + [fy_margin]
    fz = [fz_own.at[u] for u in range(layers)] + [fz_margin]
    fzl = [fzl_own.at[u] for u in range(layers)] + [fzl_margin]
    old = [old_own.at[u] for u in range(layers)] + [old_margin]
    inv = [None, inv_own.at[0], inv_own.at[1], inv_more.at[0], inv_more.at[1]]
    even = [None, even_own.at[0], even_own.at[1], even_more.at[0], even_more.at[1]]
    for u in (margin - 1, margin):
        weight = (fx[u][...] + fx[u - 1][...]) + (fy[u][body] + fy[u][plane.down]) + (fz[u][...] + fzl[u][...])
        inv[u][...] = 1.0 / (1.0 + weight)

    def around(ref, u):
        return in_layer(plane, fy[u], fz[u], fzl[u], ref[u])

    u = margin - 1
    total = s(u) + around(old, u) + (fx[u][...] * old[u + 1][body] + fx[u - 1][...] * old[u - 1][body])
    plane.put(even[u], total * inv[u][...])
    plane.put(even[margin], (part(2) + fx[u][...] * old[u][body]) * inv[margin][...])
    for u in range(2, margin + 1):
        if u < margin:
            total = s(u) + around(even, u) + (fx[u][...] * even[u + 1][body] + fx[u - 1][...] * even[u - 1][body])
        else:
            total = part(2) + around(even, u) + fx[u - 1][...] * even[u - 1][body]
        fresh = total * inv[u][...]
        new[u - 2] = fresh
        plane.put(change.at[u - 2], fresh - old[u][body])
    change = {u: change.at[u - 2] for u in range(2, margin + 1)}

    one = fx[1][...] * change[2][body]
    two = around(change, 2) + fx[2][...] * change[3][body]
    three = around(change, 3) + (fx[2][...] * change[2][body] + fx[3][...] * change[4][body])
    outer = jnp.where(plane.even(1), one, 0.0)
    inner = jnp.where(plane.even(2), two, 0.0) + jnp.where(plane.even(3), three, 0.0)
    core = core_of()

    def tile(name, outer, inner):
        message[places[name], :] = plane.packed(outer, inner, core)

    tile("source2", plane.summed(outer, turn.at[1]), plane.summed(inner, turn.at[2]))
    tile("fx2", plane.summed(fx[1][...], turn.at[3]), plane.summed(fx[3][...], turn.at[4]))
    fy2 = [plane.odd_rows(fy[u][body] + fy[u + 1][body], turn.at[5 + u // 2]) for u in (0, 2)]
    fz2 = [plane.odd_lanes(fz[u][...] + fz[u + 1][...], turn.at[7 + u // 2]) for u in (0, 2)]
    own2[0], own2[1] = plane.packed(*fy2, core), plane.packed(*fz2, core)
    tile("far2", fy2[1], fz2[1])
    for u in range(2):
        message[places["coef%d" % u], :] = cell[u]
    first = s(0) + around(old, 0) + fx[0][...] * old[1][body]
    second = s(0) + fx[0][...] * even[1][body]
    message[places["known0"], :] = jnp.where(plane.even(0), first, second)
    message[places["old0"], :] = odd_cells(iterate.at[own_layer(0, layers)], half, plane.odd_first(0))
    total = s(1) + around(even, 1) + fx[1][...] * even[2][body]
    known1[...] = total
    turn[9] = total * inv[1][...] - old[1][body]
    message[places["moved1"], :] = odd_cells(turn.at[9], half, plane.odd_first(1))
    message[places["face2"], :] = odd_cells(fx[1], half, plane.odd_first(1))


def border_kernel(
    inputs, message, own2, known1, new_in, fx_in, fy_in, fz_in, fzl_in, inv_in, across_in,
    within, fx2_in, new, known, fx, fy, fz, fzl, inv,
    old, even, change, turn, face_y, face_z, face_zl,
):
    iterate, source, _ = three_parts(inputs)
    layers, height, depth = iterate.shape
    plane = Plane(height, depth)
    body, half = plane.body, plane.half
    places, _ = chip_rows(height)
    core, last = core_of(), lax.axis_size("gx") - 1
    position = lax.axis_index("gx")

    def mine(name):
        return message[places[name], :]

    def theirs(name):
        return across_in[places[name], :]

    def opened(name, k):
        into_both_rows(turn.at[k], theirs(name))
        return turn[k]

    for k in range(2):
        here = theirs("coef%d" % k)
        plane.put(face_y.at[k], plane.face_y(here))
        face = plane.face_z(here)
        face_z[k] = face
        face_zl[k] = behind(face, 1, 1)
    fy[...], fz[...], fzl[...] = face_y[0], face_z[0], face_zl[0]
    there = position - 1 + 2 * core
    border = jnp.where((there >= 0) & (there <= last), 0.5 * (mine("coef0") + theirs("coef0")), 0.0)
    face1 = 0.5 * (theirs("coef0") + theirs("coef1"))
    face2 = opened("face2", 2)
    fx[0], fx[1] = border, face1

    def inverse(faces, fy, fz, fzl):
        weight = faces + (fy[body] + fy[plane.down]) + (fz[...] + fzl[...])
        return 1.0 / (1.0 + weight)

    inv_own = inverse(fx_in[0] + border, fy_in.at[0], fz_in.at[0], fzl_in.at[0])
    inv_near = inverse(border + face1, face_y.at[0], face_z.at[0], face_zl.at[0])
    inv_far = inverse(face1 + face2, face_y.at[1], face_z.at[1], face_zl.at[1])
    inv[0], inv[1] = inv_near, inv_own
    old_own, old_next = iterate[own_layer(0, layers)], iterate[own_layer(1, layers)]
    old_near, far = opened("old0", 0), opened("moved1", 1)
    even_own = (mine("known0") + border * old_near) * inv_own
    even_near = (theirs("known0") + border * old_own) * inv_near
    plane.put(even.at[0], even_near)
    plane.put(even.at[1], even_own)

    def near(ref, k):
        return in_layer(plane, face_y.at[k], face_z.at[k], face_zl.at[k], ref)

    def own(ref, u):
        return in_layer(plane, fy_in.at[u], fz_in.at[u], fzl_in.at[u], ref)

    odd_own = (mine("known0") + own(even.at[1], 0) + border * even_near) * inv_own
    odd_near = (theirs("known0") + near(even.at[0], 0) + border * even_own) * inv_near
    odd_next = (known1[...] + fx_in[0] * even_own) * inv_in[0]
    far = far + face1 * even_near * inv_far
    new[0], new[1], new[2] = odd_near, odd_own, odd_next
    near_by, here, following = odd_near - old_near, odd_own - old_own, odd_next - old_next
    for k, values in enumerate((far, near_by, here, following)):
        plane.put(change.at[k], values)
    plane.put(old.at[0], old_near)
    known[...] = theirs("known0") + face1 * far - near(old.at[0], 0)

    def residual(u, values):
        return jnp.where(plane.even(u), values, 0.0)

    own_outer = residual(1, own(change.at[3], 1) + fx_in[0] * here)
    own_outer = own_outer + residual(0, own(change.at[2], 0) + (fx_in[0] * following + border * near_by))
    own_inner = residual(2, fx_in[1] * following)
    its_outer = residual(-1, near(change.at[1], 0) + (face1 * far + border * here))
    its_outer = its_outer + residual(-2, near(change.at[0], 1) + face1 * near_by)
    its_inner = residual(-3, face2 * far)
    sums = [plane.summed(values, turn.at[3 + k]) for k, values in enumerate((own_outer, own_inner, its_outer, its_inner))]
    within[0] = mine("source2") + plane.packed(sums[0], sums[1], core)
    within[5] = theirs("source2") + plane.packed(sums[2], sums[3], 1 - core)
    within[6] = theirs("fx2")
    far2 = theirs("far2")
    far2_swap = jnp.where((plane.half_lane & 1) == 0, ahead(far2, 1, 1), behind(far2, 1, 1))
    near_fy2 = plane.odd_rows(face_y[0, body] + face_y[1, body], turn.at[1])
    near_fz2 = plane.odd_lanes(face_z[0] + face_z[1], turn.at[2])
    within[7] = plane.packed(near_fy2, far2_swap, 1 - core)
    within[8] = plane.packed(near_fz2, far2, 1 - core)
    fx2_in[...] = mine("fx2")
    middle = jnp.where((plane.half_lane & 1) == 0, ahead(mine("fx2"), 1, 1), behind(mine("fx2"), 1, 1))
    within[1] = plane.packed(plane.summed(border, turn.at[7]), middle, core)
    within[2], within[3] = own2[0], own2[1]
    turn[0] = source[own_layer(layers - 1, layers)] + fx_in[layers - 2] * new_in[layers - 4]
    within[4] = odd_cells(turn.at[0], half, jnp.logical_not(plane.odd_first(layers - 1)))


def neigh2(e2, fx2, fxl2, fy2, fz2, fzl2, first_of_two, tiles):
    half = fx2.shape[1]
    body, up, down = pl.ds(PAD, half), pl.ds(PAD + 1, half), pl.ds(PAD - 1, half)
    needed = range(tiles[0], tiles[-1] + 3)
    here = {j: e2[j, body] for j in needed}
    after = {j: ahead(here[j], 1, 1) for j in needed}
    before = {j: behind(here[j], 1, 1) for j in needed}
    found = []
    for j in tiles:
        k = j + 1
        upper = jnp.where(first_of_two, after[k], before[k + 1])
        lower = jnp.where(first_of_two, after[k - 1], before[k])
        sums = fx2[j] * upper + fxl2[j] * lower
        sums = sums + fy2[j, body] * e2[k, up] + fy2[j, down] * e2[k, down]
        sums = sums + fz2[j] * ahead(here[k], 2, 1) + fzl2[j] * behind(here[k], 2, 1)
        found.append(sums)
    return found


def parities2(half, lanes):
    row, lane = rows_of((half, lanes)), lanes_of((half, lanes))
    return (lane & 1) == 0, ((row + (lane & 1) + (lane >> 1)) & 1) == 0


def group(values):
    return with_partner(with_partner(values, 1, 1), 2, 1)


def packed_odd(values, pair):
    half, lanes = values.shape
    lane = lanes_of((half // 2, lanes))
    pair[...] = values
    return odd_cells(pair, half // 2, (((lane & 1) + (lane >> 1)) & 1) != 0)


def middle_down_kernel(
    own, fx2_in, within_in,
    slots, e2_out, s2, fx2, fxl2, fy2, fz2, fzl2, inv2,
    e2, pair,
):
    _, half, lanes = own.shape
    quarter = half // 2
    first_of_two, even2 = parities2(half, lanes)
    body, down = pl.ds(PAD, half), pl.ds(PAD - 1, half)
    edge = jnp.zeros((PAD, lanes), jnp.float32)
    for j in (0, 5):
        e2[j] = jnp.zeros((half + 2 * PAD, lanes), jnp.float32)

    def pair_of(k):
        return by_side(own[k], within_in[k])

    def four(k):
        (left, right), (far_left, far_right) = pair_of(k), pair_of(5 + k)
        return far_left, left, right, far_right

    for j, (source, fy, fz) in enumerate(zip(four(0), four(2), four(3))):
        s2[j] = source
        fy2[j, :PAD] = edge
        fy2[j, body] = fy
        fy2[j, PAD + half:] = edge
        fz2[j] = fz
        fzl2[j] = behind(fz, 2, 1)

    def between(left, right):
        return jnp.where(first_of_two, ahead(left, 1, 1), behind(right, 1, 1))

    fxl0, fxl1, fxr2, fxr3 = four(1)
    inner = fx2_in[...]
    fxr1, _ = by_side(inner, between(fxl1, inner))
    fxl2_, _ = by_side(between(inner, fxr2), inner)
    for j, (face, low) in enumerate(
        ((between(fxl0, fxl1), fxl0), (fxr1, fxl1), (fxr2, fxl2_), (fxr3, between(fxr2, fxr3)))
    ):
        fx2[j], fxl2[j] = face, low
        weight = face + low + fy2[j, body] + fy2[j, down] + fz2[j] + fzl2[j]
        inverse = 1.0 / (8.0 + weight)
        inv2[j] = inverse
        e2[j + 1, :PAD] = edge
        e2[j + 1, PAD + half:] = edge
        e2[j + 1, body] = s2[j] * inverse

    def neigh(tiles):
        return neigh2(e2, fx2, fxl2, fy2, fz2, fzl2, first_of_two, tiles)

    fresh = [(s2[j] + sums) * inv2[j] for j, sums in enumerate(neigh((0, 1, 2, 3)))]
    for j in range(4):
        e2[j + 1, body] = fresh[j]
        e2_out[j] = fresh[j]
    lane = lanes_of((quarter, lanes))
    odd_layer, odd_depth = (lane & 1) != 0, (lane & 2) != 0
    chips = slots.shape[0]
    for k, sums in enumerate(neigh((1, 2))):
        j = k + 1
        pair[k] = jnp.where(even2, sums, 0.0)
        item = (lane - (lax.axis_index("gx") // 2 * 2 + k) // (chips // 2)) & 3
        source = group(even_row_sum(pair.at[k], quarter))
        fx = group(jnp.where(odd_layer, even_row_sum(fx2.at[j], quarter), 0.0))
        fxl = group(jnp.where(odd_layer, 0.0, even_row_sum(fxl2.at[j], quarter)))
        fy = group(fy2[j, pl.ds(PAD + 1, quarter, 2), :])
        fz = group(jnp.where(odd_depth, even_row_sum(fz2.at[j], quarter), 0.0))
        weight = (fx + fxl) + (fy + behind(fy, 1, 0)) + (fz + behind(fz, 4, 1))
        start = source / (64.0 + weight)
        tile = jnp.where(item == 0, start, jnp.where(item == 1, fx, jnp.where(item == 2, fy, fz)))
        for c in range(chips):
            slots[c, k] = tile
    halo = packed_odd(jnp.where(first_of_two, fresh[2], fresh[1]), pair.at[2])
    for c in range(chips):
        slots[c, 2] = halo


def joined(one, two):
    return jnp.concatenate([part for part in (one, two) if part.shape[0]], 0)


class Level:
    def __init__(self, mass, source, faces, row_step, lane_step, slot_step):
        self.source, self.row_step, self.lane_step, self.slot_step = source, row_step, lane_step, slot_step
        self.fx, self.fy, self.fz = faces
        self.tiles = source.shape[0]
        shape = source.shape
        self.lane = lanes_of(shape)
        layer = lax.broadcasted_iota(jnp.int32, shape, 0) if self.tiles > 1 else self.lane // slot_step
        self.even = ((layer + rows_of(shape) // row_step + self.lane // lane_step) & 1) == 0
        self.fxl = self.lower(self.fx)
        self.fyl = self.row_shifts(self.fy)[1]
        self.fzl = behind(self.fz, lane_step, 2)
        weight = (self.fx + self.fxl) + (self.fy + self.fyl) + (self.fz + self.fzl)
        self.inv = 1.0 / (mass + weight)

    def upper(self, e):
        return joined(e[1:], ahead(e[:1], self.slot_step, 2))

    def lower(self, e):
        return joined(behind(e[-1:], self.slot_step, 2), e[:-1])

    def row_shifts(self, e):
        return ahead(e, self.row_step, 1), behind(e, self.row_step, 1)

    def neigh(self, e):
        above, below = self.row_shifts(e)
        total = (self.fx * self.upper(e) + self.fxl * self.lower(e)) + (self.fy * above + self.fyl * below)
        return total + (self.fz * ahead(e, self.lane_step, 2) + self.fzl * behind(e, self.lane_step, 2))

    def start(self):
        return self.source * self.inv

    def update(self, e):
        return self.start() + self.neigh(e) * self.inv

    def cycle(self, deeper):
        odd = self.update(self.start())
        residual = jnp.where(self.even, self.neigh(odd), 0.0)
        fix = deeper(self.restricted(residual), self.coarse_faces())
        even = self.update(odd + self.prolonged(fix))
        return jnp.where(self.even, even, self.update(even))

    def coarse_slot_step(self):
        return self.slot_step if self.tiles > 1 else 2 * self.slot_step

    def pairs(self, values):
        if self.tiles == 1:
            return with_partner(values, self.slot_step, 2)
        halves = values.reshape(self.tiles // 2, 2, *values.shape[1:])
        return halves[:, 0] + halves[:, 1]

    def odd_layers(self, values):
        if self.tiles == 1:
            return with_partner(jnp.where((self.lane & self.slot_step) != 0, values, 0.0), self.slot_step, 2)
        return values.reshape(self.tiles // 2, 2, *values.shape[1:])[:, 1]

    def row_pairs(self, values):
        return with_partner(values, self.row_step, 1)

    def odd_rows(self, values):
        odd = (rows_of(values.shape) & self.row_step) != 0
        return with_partner(jnp.where(odd, values, 0.0), self.row_step, 1)

    def restricted(self, values):
        return with_partner(self.row_pairs(self.pairs(values)), self.lane_step, 2)

    def coarse_faces(self):
        fx = with_partner(self.row_pairs(self.odd_layers(self.fx)), self.lane_step, 2)
        fy = with_partner(self.odd_rows(self.pairs(self.fy)), self.lane_step, 2)
        return fx, fy, self.restricted(jnp.where((self.lane & self.lane_step) != 0, self.fz, 0.0))

    def prolonged(self, fix):
        if self.tiles == 1:
            return fix
        both = jnp.concatenate([fix[:, None], fix[:, None]], 1)
        return both.reshape(self.tiles, *fix.shape[1:])


class Rows(Level):
    def __init__(self, mass, source, faces, scratch):
        self.scratch, self.used = scratch, 0
        self.rows = source.shape[1]
        super().__init__(mass, source, faces, 1, 4, 1)

    def start(self):
        return self.source

    def place(self):
        self.used += 1
        return self.scratch.at[self.used % self.scratch.shape[0]]

    def row_shifts(self, e):
        place = self.place()
        edge = jnp.zeros((e.shape[0], PAD, e.shape[2]), jnp.float32)
        place[:, :PAD] = edge
        place[:, PAD + self.rows:] = edge
        place[:, pl.ds(PAD, self.rows)] = e
        return place[:, pl.ds(PAD + 1, self.rows)], place[:, pl.ds(PAD - 1, self.rows)]

    def every_other(self, values, starts):
        place, tiles = self.place(), values.shape[0]
        place[:tiles, : self.rows] = values
        found = 0.0
        for start in starts:
            found = found + jnp.concatenate(
                [place[j, pl.ds(start, self.rows // 2, 2), :][None] for j in range(tiles)], 0
            )
        return found

    def row_pairs(self, values):
        return self.every_other(values, (0, 1))

    def odd_rows(self, values):
        return self.every_other(values, (1,))

    def prolonged(self, fix):
        place, tiles = self.place(), fix.shape[0]
        for j in range(tiles):
            into_both_rows(place.at[j, pl.ds(0, self.rows)], fix[j])
        return super().prolonged(place[:tiles, : self.rows])


def coarsest(mass, source, faces, *steps):
    row_step, lane_step, slot_step = steps
    level = Level(mass, source, faces, *steps)
    counts = source.shape[1] // row_step, source.shape[2] // lane_step, 4 // slot_step
    frames = [(m, k, q) for m in range(counts[0]) for k in range(counts[1]) for q in range(counts[2])]
    place = level.lane & 3

    def spread(values):
        copies = {}
        for m, k, q in frames:
            if k:
                copies[m, k, q] = behind(copies[m, 0, q], k * lane_step, 2)
            elif q:
                by = q * slot_step
                one, two = behind(copies[m, 0, 0], by, 2), ahead(copies[m, 0, 0], 4 - by, 2)
                copies[m, k, q] = jnp.where(place >= by, one, two)
            else:
                copies[m, k, q] = behind(values, m * row_step, 1) if m else values
        return copies

    start, inv, fx, fy, fz = [spread(values) for values in (source * level.inv, level.inv, level.fx, level.fy, level.fz)]

    def shifted(copies, frame, axis, by):
        moved = list(frame)
        moved[axis] = (frame[axis] - by) % counts[axis]
        return copies[tuple(moved)]

    def along_x(copies, frame, by):
        here, wrapped = copies[frame], shifted(copies, frame, 2, by)
        return joined(here[1:], wrapped[:1]) if by > 0 else joined(wrapped[-1:], here[:-1])

    same = level.tiles == 1 and counts[2] == 2, counts[0] == 2, counts[1] == 2
    weights = {}
    for frame in frames:
        pairs = [
            (fx[frame], along_x(fx, frame, -1)),
            (fy[frame], shifted(fy, frame, 0, -1)),
            (fz[frame], shifted(fz, frame, 1, -1)),
        ]
        weights[frame] = [
            ((up + low) * inv[frame], None) if merged else (up * inv[frame], low * inv[frame])
            for (up, low), merged in zip(pairs, same)
        ]

    def update(e):
        fresh = {}
        for frame in frames:
            moves = along_x, lambda c, f, by: shifted(c, f, 0, by), lambda c, f, by: shifted(c, f, 1, by)
            total = 0.0
            for (up, low), move in zip(weights[frame], moves):
                part = up * move(e, frame, 1)
                total = total + (part if low is None else part + low * move(e, frame, -1))
            fresh[frame] = start[frame] + total
        return fresh

    even = start
    odd = update(even)
    for turn in range(COARSE_SWEEPS - 1):
        even = update(odd)
        odd = update(even)
    return jnp.where(level.even, even[0, 0, 0], odd[0, 0, 0])


def small_cycle(mass, source, faces, row_step, lane_step, slot_step, between):
    if between == 0:
        return coarsest(mass, source, faces, row_step, lane_step, slot_step)
    level = Level(mass, source, faces, row_step, lane_step, slot_step)
    return level.cycle(
        lambda inner, inner_faces: small_cycle(
            8.0 * mass, inner, inner_faces, 2 * row_step, 2 * lane_step, level.coarse_slot_step(), between - 1
        )
    )


def coarse_kernel(
    owner_of, gathered, e2_in, s2_in, fx2_in, fxl2_in, fy2_in, fz2_in, fzl2_in, inv2_in,
    inputs, new_in, fx_more, fy_margin, fz_margin, fzl_margin, inv_more, fx_in, fy_in, fz_in, fzl_in, inv_in,
    new_out, known_out, fx_out, fy_out, fz_out, fzl_out, inv_out, within_in,
    solved_out, owned_out,
    e3, rows3, pair, e2, e1, cor, solved, owned, owner_here, fetch_sem, sems,
):
    fetch = pltpu.make_async_copy(owner_of, owner_here, fetch_sem)
    fetch.start()
    chips, _, quarter, lanes = gathered.shape
    blocks = 2 * chips
    half, height = 2 * quarter, 4 * quarter
    position, last = lax.axis_index("gx"), blocks - 1

    slot = lanes_of((quarter, lanes)) & 3
    spread = blocks // 4
    tiles = [gathered[-chip % chips, k] for chip in range(chips) for k in range(2)]
    items = []
    for k in range(4):
        packs = []
        for j in range(spread):
            value = tiles[j + (3 - k) % 4 * spread]
            for at in range(3):
                value = jnp.where(slot == at, tiles[j + (at - k) % 4 * spread], value)
            if k:
                value = jnp.where(slot < 4 - k, ahead(value, k, 1), behind(value, 4 - k, 1))
            packs.append(value[None])
        items.append(jnp.concatenate(packs, 0))
    third = Rows(64.0, items[0], items[1:], rows3)
    e3[...] = third.cycle(
        lambda inner, faces: small_cycle(512.0, inner, faces, 1, 8, third.coarse_slot_step(), 2)
    )

    fetch.wait()
    owner = owner_here[position]
    wide, narrow = lanes_of((lanes, lanes)), rows_of((lanes, lanes))
    take = jnp.where(narrow == 4 * wide + owner // spread, 1.0, 0.0)
    block = jnp.dot(
        e3[owner % spread], take, precision=lax.Precision.HIGHEST, preferred_element_type=jnp.float32
    )
    owned[0] = block[:, : lanes // 4]
    copies = [pltpu.make_async_copy(owned, owned_out, sems.at[0])]
    copies[0].start()

    first_of_two, even2 = parities2(half, lanes)
    body2 = pl.ds(PAD, half)
    edge = jnp.zeros((PAD, lanes), jnp.float32)
    core = core_of()
    s2, fx2, fxl2, fy2, fz2, fzl2, inv2 = [
        ref.at[pl.ds(core, 3)] for ref in (s2_in, fx2_in, fxl2_in, fy2_in, fz2_in, fzl2_in, inv2_in)
    ]
    next_chip = jnp.clip(position // 2 - 1 + 2 * core, 0, chips - 1)
    into_both_rows(pair.at[5], gathered[(chips - next_chip) % chips, 2])
    halo = pair[5]
    before = (
        by_side(halo, e2_in[0])[0], by_side(jnp.where(first_of_two, halo, e2_in[0]), e2_in[1])[0],
        by_side(e2_in[1], e2_in[2])[0],
        by_side(e2_in[2], jnp.where(first_of_two, e2_in[3], halo))[0], by_side(e2_in[3], halo)[0],
    )
    for k in range(5):
        j = jnp.clip(position + k - 2, 0, last)
        into_both_rows(pair.at[k], group(jnp.where(slot == j // spread, e3[j % spread], 0.0)))
        e2[k, :PAD] = edge
        e2[k, PAD + half:] = edge
        e2[k, body2] = before[k] + pair[k]

    def update2():
        sums = neigh2(e2, fx2, fxl2, fy2, fz2, fzl2, first_of_two, (0, 1, 2))
        return [(s2[j] + sums[j]) * inv2[j] for j in range(3)]

    fresh = update2()
    for j in range(3):
        e2[j + 1, body2] = fresh[j]
    fixes2 = [jnp.where(even2, even, odd) for even, odd in zip(fresh, update2())]

    _, source, _ = three_parts(inputs)
    layers = source.shape[0]
    plane = Plane(height, lanes)
    body1 = plane.body
    near_lane = (lanes_of((half, lanes)) & 1) == core
    swaps = [jnp.where(first_of_two, ahead(v, 1, 1), behind(v, 1, 1)) for v in fixes2]
    outer, inner = by_side(fixes2[0], fixes2[2])
    outer_swap, inner_swap = by_side(swaps[0], swaps[2])
    coarse = (
        jnp.where(near_lane, outer_swap, outer), jnp.where(near_lane, fixes2[1], swaps[1]),
        jnp.where(near_lane, swaps[1], fixes2[1]), jnp.where(near_lane, inner, inner_swap),
    )
    fixes = []
    for k in range(4):
        into_both_rows(cor.at[k], coarse[k])
        fixes.append(cor[k])
    for u in range(-1, layers + 1):
        before = new_out[u + 1] if u < 2 else new_in[u - 2]
        plane.put(e1.at[u + 1], before + fixes[(u + 2) // 2])

    def fx1(u):
        if u < 0:
            return fx_out[-1 - u]
        return fx_in[u] if u < layers - 1 else fx_more[u - layers + 1]

    def inv1(u):
        if u <= 0:
            return inv_out[u + 1]
        return inv_in[u - 1] if u < layers - 1 else inv_more[u - layers + 1]

    def around1(u):
        if u < 0:
            return in_layer(plane, fy_out, fz_out, fzl_out, e1.at[0])
        if u == layers:
            return in_layer(plane, fy_margin, fz_margin, fzl_margin, e1.at[u + 1])
        return in_layer(plane, fy_in.at[u], fz_in.at[u], fzl_in.at[u], e1.at[u + 1])

    def updated1(u):
        sums = around1(u) + (fx1(u) * e1[u + 2, body1] + fx1(u - 1) * e1[u, body1])
        return (source[own_layer(u, layers)] + sums) * inv1(u)

    for u in range(layers):
        e1[u + 1, body1] = jnp.where(plane.even(u), updated1(u), e1[u + 1, body1])
    e1[0, body1] = (known_out[...] + fx1(-2) * fixes[0] + (around1(-1) + fx1(-1) * e1[1, body1])) * inv1(-1)
    into_both_rows(cor.at[4], within_in[4])
    sums = cor[4] + fx1(layers) * fixes[3] + (around1(layers) + fx1(layers - 1) * e1[layers, body1])
    e1[layers + 1, body1] = sums * inv1(layers)
    for u in range(layers):
        solved[u] = jnp.where(plane.even(u), e1[u + 1, body1], updated1(u))
        copies.append(
            pltpu.make_async_copy(solved.at[u], solved_out.at[own_layer(u, layers)], sems.at[u + 1])
        )
        copies[-1].start()
    for copy in copies:
        copy.wait()


def f32(*shape):
    return jax.ShapeDtypeStruct(shape, jnp.float32)


def vmem(*shape):
    return pltpu.VMEM(shape, jnp.float32)


def call(kernel, outs, scratch, operands, out_space=pltpu.VMEM):
    def size(shape):
        count = 4
        for extent in shape:
            count *= extent
        return count

    sized = [array for array in (*scratch, *outs, *operands) if hasattr(array, "shape")]
    asked = 8 * 2**20 + sum(size(array.shape) for array in sized)
    return pl.pallas_call(
        kernel,
        out_shape=tuple(outs),
        in_specs=[pl.BlockSpec(memory_space=pltpu.VMEM)] * len(operands),
        out_specs=tuple([pl.BlockSpec(memory_space=out_space)] * len(outs)),
        scratch_shapes=scratch,
        compiler_params=pltpu.CompilerParams(vmem_limit_bytes=asked),
    )(*operands)


def on_device(iterate, source, phase_field, block_owner):
    layers, height, depth = iterate.shape
    half, quarter = height // 2, height // 4
    blocks = lax.axis_size("gx")
    padded, padded2 = height + 2 * PAD, half + 2 * PAD
    inputs = sum(
        jnp.pad(block, ((k * layers, (2 - k) * layers), (0, 0), (0, 0)))
        for k, block in enumerate((iterate, source, phase_field))
    )
    edge, = call(edge_kernel, [f32(3 * height + half, depth)], [], (inputs,))
    edge_in = within_chip(edge)
    layer, tile, tall = (height, depth), (half, depth), (padded, depth)
    cell, old, *fine, even = call(
        own_kernel,
        [
            f32(layers, *layer), f32(layers, *tall), f32(layers - 1, *layer), f32(layers, *tall),
            f32(layers, *layer), f32(layers, *layer), f32(2, *layer), f32(2, *tall),
        ],
        [], (block_owner, inputs),
    )
    message, own2, known1, new, *margin = call(
        chip_kernel,
        [
            f32(chip_rows(height)[1], depth), f32(2, *tile), f32(*layer), f32(3, *layer),
            f32(2, *layer), f32(*tall), f32(*layer), f32(*layer), f32(2, *layer),
        ],
        [vmem(*tall), vmem(2, *tall), vmem(3, *tall), vmem(10, *layer)],
        (inputs, cell, old, *fine, even, edge_in),
    )
    within, fx2, *border = call(
        border_kernel,
        [
            f32(9, *tile), f32(*tile), f32(3, *layer), f32(*layer), f32(2, *layer),
            f32(padded, depth), f32(*layer), f32(*layer), f32(2, *layer),
        ],
        [
            vmem(1, padded, depth), vmem(2, padded, depth), vmem(4, padded, depth), vmem(8, *layer),
            vmem(2, padded, depth), vmem(2, *layer), vmem(2, *layer),
        ],
        (inputs, message, own2, known1, new, *fine, between_chips(message)),
    )
    within_in = within_chip(within)
    plain = f32(4, *tile)
    slots, *middle = call(
        middle_down_kernel,
        [f32(blocks // 2, 3, quarter, depth), plain, plain, plain, plain, f32(4, padded2, depth)] + [plain] * 3,
        [vmem(6, padded2, depth), vmem(3, *tile)],
        (within, fx2, within_in),
    )
    downwards = [-place % (blocks // 2) for place in range(blocks // 2)]
    kinds = [[2 * chip + (chip // 2 + core) % 2 for chip in downwards] for core in range(2)]
    gathered = lax.all_to_all(slots, "gx", 0, 0, axis_index_groups=kinds, tiled=True)
    solved, owned = call(
        coarse_kernel,
        [f32(layers, *layer), f32(1, quarter, depth // 4)],
        [
            vmem(blocks // 4, quarter, depth), vmem(4, blocks // 4, quarter + 2 * PAD, depth), vmem(7, *tile),
            vmem(5, padded2, depth), vmem(layers + 2, padded, depth), vmem(5, *layer), vmem(layers, *layer),
            vmem(1, quarter, depth // 4), pltpu.SMEM((blocks,), jnp.int32),
            pltpu.SemaphoreType.DMA, pltpu.SemaphoreType.DMA((layers + 1,)),
        ],
        (block_owner, gathered, *middle, inputs, new, *margin, *fine, *border, within_in),
        pl.ANY,
    )
    return solved, owned


def solution(mesh):
    split = P(("groups", "gx"), None, None)
    return jax.shard_map(
        on_device,
        mesh=mesh,
        in_specs=(split, split, split, P("groups")),
        out_specs=(split, split),
        check_vma=False,
    )
```

```python
import jax
import jax.numpy as jnp
from jax import lax
from jax.experimental import pallas as pl
from jax.experimental.pallas import tpu as pltpu
from jax.sharding import PartitionSpec as P

STIFFNESS = 100.0
EPSILON = 0.01
COARSE_SWEEPS = 4
PAD = 8


def between_chips(block):
    return lax.ppermute(block, "gx", [(i, i + 1 if i % 2 else i - 1) for i in range(1, lax.axis_size("gx") - 1)])


def within_chip(block):
    return lax.ppermute(block, "gx", [(i, i ^ 1) for i in range(lax.axis_size("gx"))])


def by_side(across, within):
    on_left = lax.axis_index("gx") % 2 == 0
    return jnp.where(on_left, across, within), jnp.where(on_left, within, across)


def lanes_of(shape):
    return lax.broadcasted_iota(jnp.int32, shape, len(shape) - 1)


def rows_of(shape):
    return lax.broadcasted_iota(jnp.int32, shape, len(shape) - 2)


def ahead(values, step, axis):
    return pltpu.roll(values, values.shape[axis] - step, axis)


def behind(values, step, axis):
    return pltpu.roll(values, step, axis)


def with_partner(values, step, axis):
    index = lax.broadcasted_iota(jnp.int32, values.shape, axis)
    partner = jnp.where((index & step) == 0, ahead(values, step, axis), behind(values, step, axis))
    return values + partner


def even_row_sum(scratch, rows):
    return scratch[pl.ds(0, rows, 2), :] + scratch[pl.ds(1, rows, 2), :]


def core_of():
    return lax.axis_index("gx") % 2


def own_layer(u, layers):
    return u + core_of() * (layers - 1 - 2 * u)


def three_parts(ref):
    third = ref.shape[0] // 3
    return [ref.at[pl.ds(k * third, third)] for k in range(3)]


def odd_cells(ref, rows, first):
    return jnp.where(first, ref[pl.ds(0, rows, 2), :], ref[pl.ds(1, rows, 2), :])


def into_both_rows(ref, values):
    rows = values.shape[0]
    ref[pl.ds(0, rows, 2), :] = values
    ref[pl.ds(1, rows, 2), :] = values


def cell_coef(value):
    return STIFFNESS * (value * value + EPSILON)


class Plane:
    def __init__(self, height, depth):
        self.height, self.half, self.depth = height, height // 2, depth
        self.row, self.lane = rows_of((height, depth)), lanes_of((height, depth))
        self.parity = self.row + self.lane + core_of()
        self.half_lane = lanes_of((self.half, depth))
        self.body = pl.ds(PAD, height)
        self.up, self.down = pl.ds(PAD + 1, height), pl.ds(PAD - 1, height)

    def even(self, u):
        return ((self.parity + u) & 1) == 0

    def odd_first(self, u):
        return ((self.half_lane + core_of() + u) & 1) != 0

    def put(self, ref, values):
        edge = jnp.zeros((PAD, self.depth), jnp.float32)
        ref[:PAD] = edge
        ref[PAD + self.height:] = edge
        ref[self.body] = values

    def face_y(self, here):
        return jnp.where(self.row < self.height - 1, 0.5 * (here + ahead(here, 1, 0)), 0.0)

    def face_z(self, here):
        return jnp.where(self.lane < self.depth - 1, 0.5 * (here + ahead(here, 1, 1)), 0.0)

    def packed(self, outer, inner, core):
        return jnp.where((self.half_lane & 1) == core, outer, inner)

    def both_rows(self, ref):
        return even_row_sum(ref, self.half)

    def summed(self, values, ref):
        ref[...] = values
        return with_partner(self.both_rows(ref), 1, 1)

    def odd_rows(self, values, ref):
        ref[...] = values
        return with_partner(ref[pl.ds(1, self.half, 2), :], 1, 1)

    def odd_lanes(self, values, ref):
        ref[...] = values
        sums = self.both_rows(ref)
        return jnp.where((self.half_lane & 1) == 0, ahead(sums, 1, 1), sums)


def in_layer(plane, fy, fz, fzl, padded):
    here = padded[plane.body]
    total = fy[plane.body] * padded[plane.up] + fy[plane.down] * padded[plane.down]
    return total + (fz[...] * ahead(here, 1, 1) + fzl[...] * behind(here, 1, 1))


def edge_kernel(inputs, out):
    iterate, source, phase = three_parts(inputs)
    layers, height, depth = iterate.shape
    plane = Plane(height, depth)
    near, inner, far = [own_layer(u, layers) for u in (layers - 1, layers - 2, layers - 3)]
    coef_near, coef_inner, coef_far = [cell_coef(phase[k]) for k in (near, inner, far)]

    def around(here, e):
        fy, fz = plane.face_y(here), plane.face_z(here)
        fyl, fzl = behind(fy, 1, 0), behind(fz, 1, 1)
        total = fy * ahead(e, 1, 0) + fyl * behind(e, 1, 0)
        return total + fz * ahead(e, 1, 1) + fzl * behind(e, 1, 1), fy + fyl + fz + fzl

    face_near, face_far = 0.5 * (coef_inner + coef_near), 0.5 * (coef_inner + coef_far)
    total, weight = around(coef_inner, iterate[inner])
    total = total + face_near * iterate[near] + face_far * iterate[far]
    updated = (source[inner] + total) / (1.0 + (face_near + face_far + weight))
    total, _ = around(coef_near, iterate[near])
    known = jnp.where(plane.even(layers - 1), total + face_near * iterate[inner], face_near * updated)
    out[:height] = coef_near
    out[height:2 * height] = coef_inner
    out[2 * height:3 * height] = source[near] + known
    out[3 * height:] = odd_cells(iterate.at[near], plane.half, plane.odd_first(layers - 1))


def chip_rows(height):
    half, at, places = height // 2, 0, {}
    for name, size in (
        ("coef0", height), ("coef1", height), ("known0", height), ("old0", half), ("moved1", half), ("face2", half),
        ("source2", half), ("fx2", half), ("far2", half),
    ):
        places[name] = pl.ds(at, size)
        at += size
    return places, at


def own_kernel(owner_of, inputs, cell, old, fx, fy, fz, fzl, inv, even):
    iterate, source, phase = three_parts(inputs)
    layers, height, depth = iterate.shape
    plane = Plane(height, depth)
    body = plane.body
    for u in range(layers):
        cell[u] = cell_coef(phase[own_layer(u, layers)])
        plane.put(old.at[u], iterate[own_layer(u, layers)])
    for u in range(layers):
        here = cell[u]
        if u < layers - 1:
            fx[u] = 0.5 * (here + cell[u + 1])
        plane.put(fy.at[u], plane.face_y(here))
        face = plane.face_z(here)
        fz[u] = face
        fzl[u] = behind(face, 1, 1)
    for u in (1, 2):
        weight = (fx[u] + fx[u - 1]) + (fy[u, body] + fy[u, plane.down]) + (fz[u] + fzl[u])
        inverse = 1.0 / (1.0 + weight)
        inv[u - 1] = inverse
        around = in_layer(plane, fy.at[u], fz.at[u], fzl.at[u], old.at[u])
        total = source[own_layer(u, layers)] + around + (fx[u] * old[u + 1, body] + fx[u - 1] * old[u - 1, body])
        plane.put(even.at[u - 1], total * inverse)


def chip_kernel(
    inputs, cell, old_own, fx_own, fy_own, fz_own, fzl_own, inv_own, even_own, within_in,
    message, own2, known1, new, fx_more, fy_margin, fz_margin, fzl_margin, inv_more,
    old_margin, even_more, change, turn,
):
    iterate, source, phase = three_parts(inputs)
    layers, height, depth = iterate.shape
    plane = Plane(height, depth)
    body, half = plane.body, plane.half
    places, _ = chip_rows(height)
    margin = layers

    def part(k):
        return within_in[k * height:(k + 1) * height]

    def s(u):
        return source[own_layer(u, layers)]

    into_both_rows(turn.at[0], within_in[3 * height:])
    plane.put(old_margin, turn[0])
    fx_more[0] = 0.5 * (cell[layers - 1] + part(0))
    fx_more[1] = 0.5 * (part(0) + part(1))
    plane.put(fy_margin, plane.face_y(part(0)))
    face = plane.face_z(part(0))
    fz_margin[...] = face
    fzl_margin[...] = behind(face, 1, 1)
    fx = [fx_own.at[u] for u in range(3)] + [fx_more.at[0], fx_more.at[1]]
    fy = [fy_own.at[u] for u in range(layers)] + [fy_margin]
    fz = [fz_own.at[u] for u in range(layers)] + [fz_margin]
    fzl = [fzl_own.at[u] for u in range(layers)] + [fzl_margin]
    old = [old_own.at[u] for u in range(layers)] + [old_margin]
    inv = [None, inv_own.at[0], inv_own.at[1], inv_more.at[0], inv_more.at[1]]
    even = [None, even_own.at[0], even_own.at[1], even_more.at[0], even_more.at[1]]
    for u in (margin - 1, margin):
        weight = (fx[u][...] + fx[u - 1][...]) + (fy[u][body] + fy[u][plane.down]) + (fz[u][...] + fzl[u][...])
        inv[u][...] = 1.0 / (1.0 + weight)

    def around(ref, u):
        return in_layer(plane, fy[u], fz[u], fzl[u], ref[u])

    u = margin - 1
    total = s(u) + around(old, u) + (fx[u][...] * old[u + 1][body] + fx[u - 1][...] * old[u - 1][body])
    plane.put(even[u], total * inv[u][...])
    plane.put(even[margin], (part(2) + fx[u][...] * old[u][body]) * inv[margin][...])
    for u in range(2, margin + 1):
        if u < margin:
            total = s(u) + around(even, u) + (fx[u][...] * even[u + 1][body] + fx[u - 1][...] * even[u - 1][body])
        else:
            total = part(2) + around(even, u) + fx[u - 1][...] * even[u - 1][body]
        fresh = total * inv[u][...]
        new[u - 2] = fresh
        plane.put(change.at[u - 2], fresh - old[u][body])
    change = {u: change.at[u - 2] for u in range(2, margin + 1)}

    one = fx[1][...] * change[2][body]
    two = around(change, 2) + fx[2][...] * change[3][body]
    three = around(change, 3) + (fx[2][...] * change[2][body] + fx[3][...] * change[4][body])
    outer = jnp.where(plane.even(1), one, 0.0)
    inner = jnp.where(plane.even(2), two, 0.0) + jnp.where(plane.even(3), three, 0.0)
    core = core_of()

    def tile(name, outer, inner):
        message[places[name], :] = plane.packed(outer, inner, core)

    tile("source2", plane.summed(outer, turn.at[1]), plane.summed(inner, turn.at[2]))
    tile("fx2", plane.summed(fx[1][...], turn.at[3]), plane.summed(fx[3][...], turn.at[4]))
    fy2 = [plane.odd_rows(fy[u][body] + fy[u + 1][body], turn.at[5 + u // 2]) for u in (0, 2)]
    fz2 = [plane.odd_lanes(fz[u][...] + fz[u + 1][...], turn.at[7 + u // 2]) for u in (0, 2)]
    own2[0], own2[1] = plane.packed(*fy2, core), plane.packed(*fz2, core)
    tile("far2", fy2[1], fz2[1])
    for u in range(2):
        message[places["coef%d" % u], :] = cell[u]
    first = s(0) + around(old, 0) + fx[0][...] * old[1][body]
    second = s(0) + fx[0][...] * even[1][body]
    message[places["known0"], :] = jnp.where(plane.even(0), first, second)
    message[places["old0"], :] = odd_cells(iterate.at[own_layer(0, layers)], half, plane.odd_first(0))
    total = s(1) + around(even, 1) + fx[1][...] * even[2][body]
    known1[...] = total
    turn[9] = total * inv[1][...] - old[1][body]
    message[places["moved1"], :] = odd_cells(turn.at[9], half, plane.odd_first(1))
    message[places["face2"], :] = odd_cells(fx[1], half, plane.odd_first(1))


def border_kernel(
    inputs, message, own2, known1, new_in, fx_in, fy_in, fz_in, fzl_in, inv_in, across_in,
    within, fx2_in, new, known, fx, fy, fz, fzl, inv,
    old, even, change, turn, face_y, face_z, face_zl,
):
    iterate, source, _ = three_parts(inputs)
    layers, height, depth = iterate.shape
    plane = Plane(height, depth)
    body, half = plane.body, plane.half
    places, _ = chip_rows(height)
    core, last = core_of(), lax.axis_size("gx") - 1
    position = lax.axis_index("gx")

    def mine(name):
        return message[places[name], :]

    def theirs(name):
        return across_in[places[name], :]

    def opened(name, k):
        into_both_rows(turn.at[k], theirs(name))
        return turn[k]

    for k in range(2):
        here = theirs("coef%d" % k)
        plane.put(face_y.at[k], plane.face_y(here))
        face = plane.face_z(here)
        face_z[k] = face
        face_zl[k] = behind(face, 1, 1)
    fy[...], fz[...], fzl[...] = face_y[0], face_z[0], face_zl[0]
    there = position - 1 + 2 * core
    border = jnp.where((there >= 0) & (there <= last), 0.5 * (mine("coef0") + theirs("coef0")), 0.0)
    face1 = 0.5 * (theirs("coef0") + theirs("coef1"))
    face2 = opened("face2", 2)
    fx[0], fx[1] = border, face1

    def inverse(faces, fy, fz, fzl):
        weight = faces + (fy[body] + fy[plane.down]) + (fz[...] + fzl[...])
        return 1.0 / (1.0 + weight)

    inv_own = inverse(fx_in[0] + border, fy_in.at[0], fz_in.at[0], fzl_in.at[0])
    inv_near = inverse(border + face1, face_y.at[0], face_z.at[0], face_zl.at[0])
    inv_far = inverse(face1 + face2, face_y.at[1], face_z.at[1], face_zl.at[1])
    inv[0], inv[1] = inv_near, inv_own
    old_own, old_next = iterate[own_layer(0, layers)], iterate[own_layer(1, layers)]
    old_near, far = opened("old0", 0), opened("moved1", 1)
    even_own = (mine("known0") + border * old_near) * inv_own
    even_near = (theirs("known0") + border * old_own) * inv_near
    plane.put(even.at[0], even_near)
    plane.put(even.at[1], even_own)

    def near(ref, k):
        return in_layer(plane, face_y.at[k], face_z.at[k], face_zl.at[k], ref)

    def own(ref, u):
        return in_layer(plane, fy_in.at[u], fz_in.at[u], fzl_in.at[u], ref)

    odd_own = (mine("known0") + own(even.at[1], 0) + border * even_near) * inv_own
    odd_near = (theirs("known0") + near(even.at[0], 0) + border * even_own) * inv_near
    odd_next = (known1[...] + fx_in[0] * even_own) * inv_in[0]
    far = far + face1 * even_near * inv_far
    new[0], new[1], new[2] = odd_near, odd_own, odd_next
    near_by, here, following = odd_near - old_near, odd_own - old_own, odd_next - old_next
    for k, values in enumerate((far, near_by, here, following)):
        plane.put(change.at[k], values)
    plane.put(old.at[0], old_near)
    known[...] = theirs("known0") + face1 * far - near(old.at[0], 0)

    def residual(u, values):
        return jnp.where(plane.even(u), values, 0.0)

    own_outer = residual(1, own(change.at[3], 1) + fx_in[0] * here)
    own_outer = own_outer + residual(0, own(change.at[2], 0) + (fx_in[0] * following + border * near_by))
    own_inner = residual(2, fx_in[1] * following)
    its_outer = residual(-1, near(change.at[1], 0) + (face1 * far + border * here))
    its_outer = its_outer + residual(-2, near(change.at[0], 1) + face1 * near_by)
    its_inner = residual(-3, face2 * far)
    sums = [plane.summed(values, turn.at[3 + k]) for k, values in enumerate((own_outer, own_inner, its_outer, its_inner))]
    within[0] = mine("source2") + plane.packed(sums[0], sums[1], core)
    within[5] = theirs("source2") + plane.packed(sums[2], sums[3], 1 - core)
    within[6] = theirs("fx2")
    far2 = theirs("far2")
    far2_swap = jnp.where((plane.half_lane & 1) == 0, ahead(far2, 1, 1), behind(far2, 1, 1))
    near_fy2 = plane.odd_rows(face_y[0, body] + face_y[1, body], turn.at[1])
    near_fz2 = plane.odd_lanes(face_z[0] + face_z[1], turn.at[2])
    within[7] = plane.packed(near_fy2, far2_swap, 1 - core)
    within[8] = plane.packed(near_fz2, far2, 1 - core)
    fx2_in[...] = mine("fx2")
    middle = jnp.where((plane.half_lane & 1) == 0, ahead(mine("fx2"), 1, 1), behind(mine("fx2"), 1, 1))
    within[1] = plane.packed(plane.summed(border, turn.at[7]), middle, core)
    within[2], within[3] = own2[0], own2[1]
    turn[0] = source[own_layer(layers - 1, layers)] + fx_in[layers - 2] * new_in[layers - 4]
    within[4] = odd_cells(turn.at[0], half, jnp.logical_not(plane.odd_first(layers - 1)))


def neigh2(e2, fx2, fxl2, fy2, fz2, fzl2, first_of_two, tiles):
    half = fx2.shape[1]
    body, up, down = pl.ds(PAD, half), pl.ds(PAD + 1, half), pl.ds(PAD - 1, half)
    needed = range(tiles[0], tiles[-1] + 3)
    here = {j: e2[j, body] for j in needed}
    after = {j: ahead(here[j], 1, 1) for j in needed}
    before = {j: behind(here[j], 1, 1) for j in needed}
    found = []
    for j in tiles:
        k = j + 1
        upper = jnp.where(first_of_two, after[k], before[k + 1])
        lower = jnp.where(first_of_two, after[k - 1], before[k])
        sums = fx2[j] * upper + fxl2[j] * lower
        sums = sums + fy2[j, body] * e2[k, up] + fy2[j, down] * e2[k, down]
        sums = sums + fz2[j] * ahead(here[k], 2, 1) + fzl2[j] * behind(here[k], 2, 1)
        found.append(sums)
    return found


def parities2(half, lanes):
    row, lane = rows_of((half, lanes)), lanes_of((half, lanes))
    return (lane & 1) == 0, ((row + (lane & 1) + (lane >> 1)) & 1) == 0


def group(values):
    return with_partner(with_partner(values, 1, 1), 2, 1)


def packed_odd(values, pair):
    half, lanes = values.shape
    lane = lanes_of((half // 2, lanes))
    pair[...] = values
    return odd_cells(pair, half // 2, (((lane & 1) + (lane >> 1)) & 1) != 0)


def middle_down_kernel(
    own, fx2_in, within_in,
    slots, e2_out, s2, fx2, fxl2, fy2, fz2, fzl2, inv2,
    e2, pair,
):
    _, half, lanes = own.shape
    quarter = half // 2
    first_of_two, even2 = parities2(half, lanes)
    body, down = pl.ds(PAD, half), pl.ds(PAD - 1, half)
    edge = jnp.zeros((PAD, lanes), jnp.float32)
    for j in (0, 5):
        e2[j] = jnp.zeros((half + 2 * PAD, lanes), jnp.float32)

    def pair_of(k):
        return by_side(own[k], within_in[k])

    def four(k):
        (left, right), (far_left, far_right) = pair_of(k), pair_of(5 + k)
        return far_left, left, right, far_right

    for j, (source, fy, fz) in enumerate(zip(four(0), four(2), four(3))):
        s2[j] = source
        fy2[j, :PAD] = edge
        fy2[j, body] = fy
        fy2[j, PAD + half:] = edge
        fz2[j] = fz
        fzl2[j] = behind(fz, 2, 1)

    def between(left, right):
        return jnp.where(first_of_two, ahead(left, 1, 1), behind(right, 1, 1))

    fxl0, fxl1, fxr2, fxr3 = four(1)
    inner = fx2_in[...]
    fxr1, _ = by_side(inner, between(fxl1, inner))
    fxl2_, _ = by_side(between(inner, fxr2), inner)
    for j, (face, low) in enumerate(
        ((between(fxl0, fxl1), fxl0), (fxr1, fxl1), (fxr2, fxl2_), (fxr3, between(fxr2, fxr3)))
    ):
        fx2[j], fxl2[j] = face, low
        weight = face + low + fy2[j, body] + fy2[j, down] + fz2[j] + fzl2[j]
        inverse = 1.0 / (8.0 + weight)
        inv2[j] = inverse
        e2[j + 1, :PAD] = edge
        e2[j + 1, PAD + half:] = edge
        e2[j + 1, body] = s2[j] * inverse

    def neigh(tiles):
        return neigh2(e2, fx2, fxl2, fy2, fz2, fzl2, first_of_two, tiles)

    fresh = [(s2[j] + sums) * inv2[j] for j, sums in enumerate(neigh((0, 1, 2, 3)))]
    for j in range(4):
        e2[j + 1, body] = fresh[j]
        e2_out[j] = fresh[j]
    lane = lanes_of((quarter, lanes))
    odd_layer, odd_depth = (lane & 1) != 0, (lane & 2) != 0
    chips = slots.shape[0]
    for k, sums in enumerate(neigh((1, 2))):
        j = k + 1
        pair[k] = jnp.where(even2, sums, 0.0)
        item = (lane - (lax.axis_index("gx") // 2 * 2 + k) // (chips // 2)) & 3
        source = group(even_row_sum(pair.at[k], quarter))
        fx = group(jnp.where(odd_layer, even_row_sum(fx2.at[j], quarter), 0.0))
        fxl = group(jnp.where(odd_layer, 0.0, even_row_sum(fxl2.at[j], quarter)))
        fy = group(fy2[j, pl.ds(PAD + 1, quarter, 2), :])
        fz = group(jnp.where(odd_depth, even_row_sum(fz2.at[j], quarter), 0.0))
        weight = (fx + fxl) + (fy + behind(fy, 1, 0)) + (fz + behind(fz, 4, 1))
        start = source / (64.0 + weight)
        tile = jnp.where(item == 0, start, jnp.where(item == 1, fx, jnp.where(item == 2, fy, fz)))
        for c in range(chips):
            slots[c, k] = tile
    halo = packed_odd(jnp.where(first_of_two, fresh[2], fresh[1]), pair.at[2])
    for c in range(chips):
        slots[c, 2] = halo


def joined(one, two):
    return jnp.concatenate([part for part in (one, two) if part.shape[0]], 0)


class Level:
    def __init__(self, mass, source, faces, row_step, lane_step, slot_step):
        self.source, self.row_step, self.lane_step, self.slot_step = source, row_step, lane_step, slot_step
        self.fx, self.fy, self.fz = faces
        self.tiles = source.shape[0]
        shape = source.shape
        self.lane = lanes_of(shape)
        layer = lax.broadcasted_iota(jnp.int32, shape, 0) if self.tiles > 1 else self.lane // slot_step
        self.even = ((layer + rows_of(shape) // row_step + self.lane // lane_step) & 1) == 0
        self.fxl = self.lower(self.fx)
        self.fyl = self.row_shifts(self.fy)[1]
        self.fzl = behind(self.fz, lane_step, 2)
        weight = (self.fx + self.fxl) + (self.fy + self.fyl) + (self.fz + self.fzl)
        self.inv = 1.0 / (mass + weight)

    def upper(self, e):
        return joined(e[1:], ahead(e[:1], self.slot_step, 2))

    def lower(self, e):
        return joined(behind(e[-1:], self.slot_step, 2), e[:-1])

    def row_shifts(self, e):
        return ahead(e, self.row_step, 1), behind(e, self.row_step, 1)

    def neigh(self, e):
        above, below = self.row_shifts(e)
        total = (self.fx * self.upper(e) + self.fxl * self.lower(e)) + (self.fy * above + self.fyl * below)
        return total + (self.fz * ahead(e, self.lane_step, 2) + self.fzl * behind(e, self.lane_step, 2))

    def start(self):
        return self.source * self.inv

    def update(self, e):
        return self.start() + self.neigh(e) * self.inv

    def cycle(self, deeper):
        odd = self.update(self.start())
        residual = jnp.where(self.even, self.neigh(odd), 0.0)
        fix = deeper(self.restricted(residual), self.coarse_faces())
        even = self.update(odd + self.prolonged(fix))
        return jnp.where(self.even, even, self.update(even))

    def coarse_slot_step(self):
        return self.slot_step if self.tiles > 1 else 2 * self.slot_step

    def pairs(self, values):
        if self.tiles == 1:
            return with_partner(values, self.slot_step, 2)
        halves = values.reshape(self.tiles // 2, 2, *values.shape[1:])
        return halves[:, 0] + halves[:, 1]

    def odd_layers(self, values):
        if self.tiles == 1:
            return with_partner(jnp.where((self.lane & self.slot_step) != 0, values, 0.0), self.slot_step, 2)
        return values.reshape(self.tiles // 2, 2, *values.shape[1:])[:, 1]

    def row_pairs(self, values):
        return with_partner(values, self.row_step, 1)

    def odd_rows(self, values):
        odd = (rows_of(values.shape) & self.row_step) != 0
        return with_partner(jnp.where(odd, values, 0.0), self.row_step, 1)

    def restricted(self, values):
        return with_partner(self.row_pairs(self.pairs(values)), self.lane_step, 2)

    def coarse_faces(self):
        fx = with_partner(self.row_pairs(self.odd_layers(self.fx)), self.lane_step, 2)
        fy = with_partner(self.odd_rows(self.pairs(self.fy)), self.lane_step, 2)
        return fx, fy, self.restricted(jnp.where((self.lane & self.lane_step) != 0, self.fz, 0.0))

    def prolonged(self, fix):
        if self.tiles == 1:
            return fix
        both = jnp.concatenate([fix[:, None], fix[:, None]], 1)
        return both.reshape(self.tiles, *fix.shape[1:])


class Rows(Level):
    def __init__(self, mass, source, faces, scratch):
        self.scratch, self.used = scratch, 0
        self.rows = source.shape[1]
        super().__init__(mass, source, faces, 1, 4, 1)

    def start(self):
        return self.source

    def place(self):
        self.used += 1
        return self.scratch.at[self.used % self.scratch.shape[0]]

    def row_shifts(self, e):
        place = self.place()
        edge = jnp.zeros((e.shape[0], PAD, e.shape[2]), jnp.float32)
        place[:, :PAD] = edge
        place[:, PAD + self.rows:] = edge
        place[:, pl.ds(PAD, self.rows)] = e
        return place[:, pl.ds(PAD + 1, self.rows)], place[:, pl.ds(PAD - 1, self.rows)]

    def every_other(self, values, starts):
        place, tiles = self.place(), values.shape[0]
        place[:tiles, : self.rows] = values
        found = 0.0
        for start in starts:
            found = found + jnp.concatenate(
                [place[j, pl.ds(start, self.rows // 2, 2), :][None] for j in range(tiles)], 0
            )
        return found

    def row_pairs(self, values):
        return self.every_other(values, (0, 1))

    def odd_rows(self, values):
        return self.every_other(values, (1,))

    def prolonged(self, fix):
        place, tiles = self.place(), fix.shape[0]
        for j in range(tiles):
            into_both_rows(place.at[j, pl.ds(0, self.rows)], fix[j])
        return super().prolonged(place[:tiles, : self.rows])


def coarsest(mass, source, faces, *steps):
    row_step, lane_step, slot_step = steps
    level = Level(mass, source, faces, *steps)
    counts = source.shape[1] // row_step, source.shape[2] // lane_step, 4 // slot_step
    frames = [(m, k, q) for m in range(counts[0]) for k in range(counts[1]) for q in range(counts[2])]
    place = level.lane & 3

    def spread(values):
        copies = {}
        for m, k, q in frames:
            if k:
                copies[m, k, q] = behind(copies[m, 0, q], k * lane_step, 2)
            elif q:
                by = q * slot_step
                one, two = behind(copies[m, 0, 0], by, 2), ahead(copies[m, 0, 0], 4 - by, 2)
                copies[m, k, q] = jnp.where(place >= by, one, two)
            else:
                copies[m, k, q] = behind(values, m * row_step, 1) if m else values
        return copies

    start, inv, fx, fy, fz = [spread(values) for values in (source * level.inv, level.inv, level.fx, level.fy, level.fz)]

    def shifted(copies, frame, axis, by):
        moved = list(frame)
        moved[axis] = (frame[axis] - by) % counts[axis]
        return copies[tuple(moved)]

    def along_x(copies, frame, by):
        here, wrapped = copies[frame], shifted(copies, frame, 2, by)
        return joined(here[1:], wrapped[:1]) if by > 0 else joined(wrapped[-1:], here[:-1])

    same = level.tiles == 1 and counts[2] == 2, counts[0] == 2, counts[1] == 2
    weights = {}
    for frame in frames:
        pairs = [
            (fx[frame], along_x(fx, frame, -1)),
            (fy[frame], shifted(fy, frame, 0, -1)),
            (fz[frame], shifted(fz, frame, 1, -1)),
        ]
        weights[frame] = [
            ((up + low) * inv[frame], None) if merged else (up * inv[frame], low * inv[frame])
            for (up, low), merged in zip(pairs, same)
        ]

    def update(e):
        fresh = {}
        for frame in frames:
            moves = along_x, lambda c, f, by: shifted(c, f, 0, by), lambda c, f, by: shifted(c, f, 1, by)
            total = 0.0
            for (up, low), move in zip(weights[frame], moves):
                part = up * move(e, frame, 1)
                total = total + (part if low is None else part + low * move(e, frame, -1))
            fresh[frame] = start[frame] + total
        return fresh

    even = start
    odd = update(even)
    for turn in range(COARSE_SWEEPS - 1):
        even = update(odd)
        odd = update(even)
    return jnp.where(level.even, even[0, 0, 0], odd[0, 0, 0])


def small_cycle(mass, source, faces, row_step, lane_step, slot_step, between):
    if between == 0:
        return coarsest(mass, source, faces, row_step, lane_step, slot_step)
    level = Level(mass, source, faces, row_step, lane_step, slot_step)
    return level.cycle(
        lambda inner, inner_faces: small_cycle(
            8.0 * mass, inner, inner_faces, 2 * row_step, 2 * lane_step, level.coarse_slot_step(), between - 1
        )
    )


def coarse_kernel(
    owner_of, gathered, e2_in, s2_in, fx2_in, fxl2_in, fy2_in, fz2_in, fzl2_in, inv2_in,
    inputs, new_in, fx_more, fy_margin, fz_margin, fzl_margin, inv_more, fx_in, fy_in, fz_in, fzl_in, inv_in,
    new_out, known_out, fx_out, fy_out, fz_out, fzl_out, inv_out, within_in,
    solved_out, owned_out,
    e3, rows3, pair, e2, e1, cor, solved, owned, owner_here, fetch_sem, sems,
):
    fetch = pltpu.make_async_copy(owner_of, owner_here, fetch_sem)
    fetch.start()
    chips, _, quarter, lanes = gathered.shape
    blocks = 2 * chips
    half, height = 2 * quarter, 4 * quarter
    position, last = lax.axis_index("gx"), blocks - 1

    slot = lanes_of((quarter, lanes)) & 3
    spread = blocks // 4
    tiles = [gathered[chip, k] for chip in reversed(range(chips)) for k in range(2)]
    items = []
    for k in range(4):
        packs = []
        for j in range(spread):
            value = tiles[j + (3 - k) % 4 * spread]
            for at in range(3):
                value = jnp.where(slot == at, tiles[j + (at - k) % 4 * spread], value)
            if k:
                value = jnp.where(slot < 4 - k, ahead(value, k, 1), behind(value, 4 - k, 1))
            packs.append(value[None])
        items.append(jnp.concatenate(packs, 0))
    third = Rows(64.0, items[0], items[1:], rows3)
    e3[...] = third.cycle(
        lambda inner, faces: small_cycle(512.0, inner, faces, 1, 8, third.coarse_slot_step(), 2)
    )

    fetch.wait()
    owner = owner_here[position]
    shape = lanes // 4, lanes
    take = jnp.where(lanes_of(shape) == 4 * rows_of(shape) + owner // spread, 1.0, 0.0)
    owned[0] = lax.dot_general(
        e3[owner % spread], take, (((1,), (1,)), ((), ())),
        precision=lax.Precision.HIGHEST, preferred_element_type=jnp.float32,
    )
    copies = [pltpu.make_async_copy(owned, owned_out, sems.at[0])]
    copies[0].start()

    first_of_two, even2 = parities2(half, lanes)
    body2 = pl.ds(PAD, half)
    edge = jnp.zeros((PAD, lanes), jnp.float32)
    core = core_of()
    s2, fx2, fxl2, fy2, fz2, fzl2, inv2 = [
        ref.at[pl.ds(core, 3)] for ref in (s2_in, fx2_in, fxl2_in, fy2_in, fz2_in, fzl2_in, inv2_in)
    ]
    next_chip = jnp.clip(position // 2 - 1 + 2 * core, 0, chips - 1)
    into_both_rows(pair.at[5], gathered[chips - 1 - next_chip, 2])
    halo = pair[5]
    before = (
        by_side(halo, e2_in[0])[0], by_side(jnp.where(first_of_two, halo, e2_in[0]), e2_in[1])[0],
        by_side(e2_in[1], e2_in[2])[0],
        by_side(e2_in[2], jnp.where(first_of_two, e2_in[3], halo))[0], by_side(e2_in[3], halo)[0],
    )
    for k in range(5):
        j = jnp.clip(position + k - 2, 0, last)
        into_both_rows(pair.at[k], group(jnp.where(slot == j // spread, e3[j % spread], 0.0)))
        e2[k, :PAD] = edge
        e2[k, PAD + half:] = edge
        e2[k, body2] = before[k] + pair[k]

    def update2():
        sums = neigh2(e2, fx2, fxl2, fy2, fz2, fzl2, first_of_two, (0, 1, 2))
        return [(s2[j] + sums[j]) * inv2[j] for j in range(3)]

    fresh = update2()
    for j in range(3):
        e2[j + 1, body2] = fresh[j]
    fixes2 = [jnp.where(even2, even, odd) for even, odd in zip(fresh, update2())]

    _, source, _ = three_parts(inputs)
    layers = source.shape[0]
    plane = Plane(height, lanes)
    body1 = plane.body
    near_lane = (lanes_of((half, lanes)) & 1) == core
    swaps = [jnp.where(first_of_two, ahead(v, 1, 1), behind(v, 1, 1)) for v in fixes2]
    outer, inner = by_side(fixes2[0], fixes2[2])
    outer_swap, inner_swap = by_side(swaps[0], swaps[2])
    coarse = (
        jnp.where(near_lane, outer_swap, outer), jnp.where(near_lane, fixes2[1], swaps[1]),
        jnp.where(near_lane, swaps[1], fixes2[1]), jnp.where(near_lane, inner, inner_swap),
    )
    fixes = []
    for k in range(4):
        into_both_rows(cor.at[k], coarse[k])
        fixes.append(cor[k])
    for u in range(-1, layers + 1):
        before = new_out[u + 1] if u < 2 else new_in[u - 2]
        plane.put(e1.at[u + 1], before + fixes[(u + 2) // 2])

    def fx1(u):
        if u < 0:
            return fx_out[-1 - u]
        return fx_in[u] if u < layers - 1 else fx_more[u - layers + 1]

    def inv1(u):
        if u <= 0:
            return inv_out[u + 1]
        return inv_in[u - 1] if u < layers - 1 else inv_more[u - layers + 1]

    def around1(u):
        if u < 0:
            return in_layer(plane, fy_out, fz_out, fzl_out, e1.at[0])
        if u == layers:
            return in_layer(plane, fy_margin, fz_margin, fzl_margin, e1.at[u + 1])
        return in_layer(plane, fy_in.at[u], fz_in.at[u], fzl_in.at[u], e1.at[u + 1])

    def updated1(u):
        sums = around1(u) + (fx1(u) * e1[u + 2, body1] + fx1(u - 1) * e1[u, body1])
        return (source[own_layer(u, layers)] + sums) * inv1(u)

    for u in range(layers):
        e1[u + 1, body1] = jnp.where(plane.even(u), updated1(u), e1[u + 1, body1])
    e1[0, body1] = (known_out[...] + fx1(-2) * fixes[0] + (around1(-1) + fx1(-1) * e1[1, body1])) * inv1(-1)
    into_both_rows(cor.at[4], within_in[4])
    sums = cor[4] + fx1(layers) * fixes[3] + (around1(layers) + fx1(layers - 1) * e1[layers, body1])
    e1[layers + 1, body1] = sums * inv1(layers)
    for u in range(layers):
        solved[u] = jnp.where(plane.even(u), e1[u + 1, body1], updated1(u))
        copies.append(
            pltpu.make_async_copy(solved.at[u], solved_out.at[own_layer(u, layers)], sems.at[u + 1])
        )
        copies[-1].start()
    for copy in copies:
        copy.wait()


def f32(*shape):
    return jax.ShapeDtypeStruct(shape, jnp.float32)


def vmem(*shape):
    return pltpu.VMEM(shape, jnp.float32)


def call(kernel, outs, scratch, operands, out_space=pltpu.VMEM):
    def size(shape):
        count = 4
        for extent in shape:
            count *= extent
        return count

    sized = [array for array in (*scratch, *outs, *operands) if hasattr(array, "shape")]
    asked = 8 * 2**20 + sum(size(array.shape) for array in sized)
    return pl.pallas_call(
        kernel,
        out_shape=tuple(outs),
        in_specs=[pl.BlockSpec(memory_space=pltpu.VMEM)] * len(operands),
        out_specs=tuple([pl.BlockSpec(memory_space=out_space)] * len(outs)),
        scratch_shapes=scratch,
        compiler_params=pltpu.CompilerParams(vmem_limit_bytes=asked),
    )(*operands)


def on_device(iterate, source, phase_field, block_owner):
    layers, height, depth = iterate.shape
    half, quarter = height // 2, height // 4
    blocks = lax.axis_size("gx")
    padded, padded2 = height + 2 * PAD, half + 2 * PAD
    inputs = sum(
        jnp.pad(block, ((k * layers, (2 - k) * layers), (0, 0), (0, 0)))
        for k, block in enumerate((iterate, source, phase_field))
    )
    edge, = call(edge_kernel, [f32(3 * height + half, depth)], [], (inputs,))
    edge_in = within_chip(edge)
    layer, tile, tall = (height, depth), (half, depth), (padded, depth)
    cell, old, *fine, even = call(
        own_kernel,
        [
            f32(layers, *layer), f32(layers, *tall), f32(layers - 1, *layer), f32(layers, *tall),
            f32(layers, *layer), f32(layers, *layer), f32(2, *layer), f32(2, *tall),
        ],
        [], (block_owner, inputs),
    )
    message, own2, known1, new, *margin = call(
        chip_kernel,
        [
            f32(chip_rows(height)[1], depth), f32(2, *tile), f32(*layer), f32(3, *layer),
            f32(2, *layer), f32(*tall), f32(*layer), f32(*layer), f32(2, *layer),
        ],
        [vmem(*tall), vmem(2, *tall), vmem(3, *tall), vmem(10, *layer)],
        (inputs, cell, old, *fine, even, edge_in),
    )
    within, fx2, *border = call(
        border_kernel,
        [
            f32(9, *tile), f32(*tile), f32(3, *layer), f32(*layer), f32(2, *layer),
            f32(padded, depth), f32(*layer), f32(*layer), f32(2, *layer),
        ],
        [
            vmem(1, padded, depth), vmem(2, padded, depth), vmem(4, padded, depth), vmem(8, *layer),
            vmem(2, padded, depth), vmem(2, *layer), vmem(2, *layer),
        ],
        (inputs, message, own2, known1, new, *fine, between_chips(message)),
    )
    within_in = within_chip(within)
    plain = f32(4, *tile)
    slots, *middle = call(
        middle_down_kernel,
        [f32(blocks // 2, 3, quarter, depth), plain, plain, plain, plain, f32(4, padded2, depth)] + [plain] * 3,
        [vmem(6, padded2, depth), vmem(3, *tile)],
        (within, fx2, within_in),
    )
    kinds = [[2 * chip + (chip // 2 + core) % 2 for chip in reversed(range(blocks // 2))] for core in range(2)]
    gathered = lax.all_to_all(slots, "gx", 0, 0, axis_index_groups=kinds, tiled=True)
    solved, owned = call(
        coarse_kernel,
        [f32(layers, *layer), f32(1, quarter, depth // 4)],
        [
            vmem(blocks // 4, quarter, depth), vmem(4, blocks // 4, quarter + 2 * PAD, depth), vmem(7, *tile),
            vmem(5, padded2, depth), vmem(layers + 2, padded, depth), vmem(5, *layer), vmem(layers, *layer),
            vmem(1, quarter, depth // 4), pltpu.SMEM((blocks,), jnp.int32),
            pltpu.SemaphoreType.DMA, pltpu.SemaphoreType.DMA((layers + 1,)),
        ],
        (block_owner, gathered, *middle, inputs, new, *margin, *fine, *border, within_in),
        pl.ANY,
    )
    return solved, owned


def solution(mesh):
    split = P(("groups", "gx"), None, None)
    return jax.shard_map(
        on_device,
        mesh=mesh,
        in_specs=(split, split, split, P("groups")),
        out_specs=(split, split),
        check_vma=False,
    )
```

```python
import jax
import jax.numpy as jnp
from jax import lax
from jax.experimental import pallas as pl
from jax.experimental.pallas import tpu as pltpu
from jax.sharding import PartitionSpec as P

STIFFNESS = 100.0
EPSILON = 0.01
COARSE_SWEEPS = 4
PAD = 8


def between_chips(block):
    return lax.ppermute(block, "gx", [(i, i + 1 if i % 2 else i - 1) for i in range(1, lax.axis_size("gx") - 1)])


def within_chip(block):
    return lax.ppermute(block, "gx", [(i, i ^ 1) for i in range(lax.axis_size("gx"))])


def by_side(across, within):
    on_left = lax.axis_index("gx") % 2 == 0
    return jnp.where(on_left, across, within), jnp.where(on_left, within, across)


def lanes_of(shape):
    return lax.broadcasted_iota(jnp.int32, shape, len(shape) - 1)


def rows_of(shape):
    return lax.broadcasted_iota(jnp.int32, shape, len(shape) - 2)


def ahead(values, step, axis):
    return pltpu.roll(values, values.shape[axis] - step, axis)


def behind(values, step, axis):
    return pltpu.roll(values, step, axis)


def with_partner(values, step, axis):
    index = lax.broadcasted_iota(jnp.int32, values.shape, axis)
    partner = jnp.where((index & step) == 0, ahead(values, step, axis), behind(values, step, axis))
    return values + partner


def even_row_sum(scratch, rows):
    return scratch[pl.ds(0, rows, 2), :] + scratch[pl.ds(1, rows, 2), :]


def core_of():
    return lax.axis_index("gx") % 2


def own_layer(u, layers):
    return u + core_of() * (layers - 1 - 2 * u)


def three_parts(ref):
    third = ref.shape[0] // 3
    return [ref.at[pl.ds(k * third, third)] for k in range(3)]


def odd_cells(ref, rows, first):
    return jnp.where(first, ref[pl.ds(0, rows, 2), :], ref[pl.ds(1, rows, 2), :])


def into_both_rows(ref, values):
    rows = values.shape[0]
    ref[pl.ds(0, rows, 2), :] = values
    ref[pl.ds(1, rows, 2), :] = values


def cell_coef(value):
    return STIFFNESS * (value * value + EPSILON)


class Plane:
    def __init__(self, height, depth):
        self.height, self.half, self.depth = height, height // 2, depth
        self.row, self.lane = rows_of((height, depth)), lanes_of((height, depth))
        self.parity = self.row + self.lane + core_of()
        self.half_lane = lanes_of((self.half, depth))
        self.body = pl.ds(PAD, height)
        self.up, self.down = pl.ds(PAD + 1, height), pl.ds(PAD - 1, height)

    def even(self, u):
        return ((self.parity + u) & 1) == 0

    def odd_first(self, u):
        return ((self.half_lane + core_of() + u) & 1) != 0

    def put(self, ref, values):
        edge = jnp.zeros((PAD, self.depth), jnp.float32)
        ref[:PAD] = edge
        ref[PAD + self.height:] = edge
        ref[self.body] = values

    def face_y(self, here):
        return jnp.where(self.row < self.height - 1, 0.5 * (here + ahead(here, 1, 0)), 0.0)

    def face_z(self, here):
        return jnp.where(self.lane < self.depth - 1, 0.5 * (here + ahead(here, 1, 1)), 0.0)

    def packed(self, outer, inner, core):
        return jnp.where((self.half_lane & 1) == core, outer, inner)

    def both_rows(self, ref):
        return even_row_sum(ref, self.half)

    def summed(self, values, ref):
        ref[...] = values
        return with_partner(self.both_rows(ref), 1, 1)

    def odd_rows(self, values, ref):
        ref[...] = values
        return with_partner(ref[pl.ds(1, self.half, 2), :], 1, 1)

    def odd_lanes(self, values, ref):
        ref[...] = values
        sums = self.both_rows(ref)
        return jnp.where((self.half_lane & 1) == 0, ahead(sums, 1, 1), sums)


def in_layer(plane, fy, fz, fzl, padded):
    here = padded[plane.body]
    total = fy[plane.body] * padded[plane.up] + fy[plane.down] * padded[plane.down]
    return total + (fz[...] * ahead(here, 1, 1) + fzl[...] * behind(here, 1, 1))


def edge_kernel(inputs, out):
    iterate, source, phase = three_parts(inputs)
    layers, height, depth = iterate.shape
    plane = Plane(height, depth)
    near, inner, far = [own_layer(u, layers) for u in (layers - 1, layers - 2, layers - 3)]
    coef_near, coef_inner, coef_far = [cell_coef(phase[k]) for k in (near, inner, far)]

    def around(here, e):
        fy, fz = plane.face_y(here), plane.face_z(here)
        fyl, fzl = behind(fy, 1, 0), behind(fz, 1, 1)
        total = fy * ahead(e, 1, 0) + fyl * behind(e, 1, 0)
        return total + fz * ahead(e, 1, 1) + fzl * behind(e, 1, 1), fy + fyl + fz + fzl

    face_near, face_far = 0.5 * (coef_inner + coef_near), 0.5 * (coef_inner + coef_far)
    total, weight = around(coef_inner, iterate[inner])
    total = total + face_near * iterate[near] + face_far * iterate[far]
    updated = (source[inner] + total) / (1.0 + (face_near + face_far + weight))
    total, _ = around(coef_near, iterate[near])
    known = jnp.where(plane.even(layers - 1), total + face_near * iterate[inner], face_near * updated)
    out[:height] = coef_near
    out[height:2 * height] = coef_inner
    out[2 * height:3 * height] = source[near] + known
    out[3 * height:] = odd_cells(iterate.at[near], plane.half, plane.odd_first(layers - 1))


def chip_rows(height):
    half, at, places = height // 2, 0, {}
    for name, size in (
        ("coef0", height), ("coef1", height), ("known0", height), ("old0", half), ("moved1", half), ("face2", half),
        ("source2", half), ("fx2", half), ("far2", half),
    ):
        places[name] = pl.ds(at, size)
        at += size
    return places, at


def own_kernel(owner_of, inputs, cell, old, fx, fy, fz, fzl, inv, even):
    iterate, source, phase = three_parts(inputs)
    layers, height, depth = iterate.shape
    plane = Plane(height, depth)
    body = plane.body
    for u in range(layers):
        cell[u] = cell_coef(phase[own_layer(u, layers)])
        plane.put(old.at[u], iterate[own_layer(u, layers)])
    for u in range(layers):
        here = cell[u]
        if u < layers - 1:
            fx[u] = 0.5 * (here + cell[u + 1])
        plane.put(fy.at[u], plane.face_y(here))
        face = plane.face_z(here)
        fz[u] = face
        fzl[u] = behind(face, 1, 1)
    for u in (1, 2):
        weight = (fx[u] + fx[u - 1]) + (fy[u, body] + fy[u, plane.down]) + (fz[u] + fzl[u])
        inverse = 1.0 / (1.0 + weight)
        inv[u - 1] = inverse
        around = in_layer(plane, fy.at[u], fz.at[u], fzl.at[u], old.at[u])
        total = source[own_layer(u, layers)] + around + (fx[u] * old[u + 1, body] + fx[u - 1] * old[u - 1, body])
        plane.put(even.at[u - 1], total * inverse)


def chip_kernel(
    inputs, cell, old_own, fx_own, fy_own, fz_own, fzl_own, inv_own, even_own, within_in,
    message, own2, known1, new, fx_more, fy_margin, fz_margin, fzl_margin, inv_more,
    old_margin, even_more, change, turn,
):
    iterate, source, phase = three_parts(inputs)
    layers, height, depth = iterate.shape
    plane = Plane(height, depth)
    body, half = plane.body, plane.half
    places, _ = chip_rows(height)
    margin = layers

    def part(k):
        return within_in[k * height:(k + 1) * height]

    def s(u):
        return source[own_layer(u, layers)]

    into_both_rows(turn.at[0], within_in[3 * height:])
    plane.put(old_margin, turn[0])
    fx_more[0] = 0.5 * (cell[layers - 1] + part(0))
    fx_more[1] = 0.5 * (part(0) + part(1))
    plane.put(fy_margin, plane.face_y(part(0)))
    face = plane.face_z(part(0))
    fz_margin[...] = face
    fzl_margin[...] = behind(face, 1, 1)
    fx = [fx_own.at[u] for u in range(3)] + [fx_more.at[0], fx_more.at[1]]
    fy = [fy_own.at[u] for u in range(layers)] + [fy_margin]
    fz = [fz_own.at[u] for u in range(layers)] + [fz_margin]
    fzl = [fzl_own.at[u] for u in range(layers)] + [fzl_margin]
    old = [old_own.at[u] for u in range(layers)] + [old_margin]
    inv = [None, inv_own.at[0], inv_own.at[1], inv_more.at[0], inv_more.at[1]]
    even = [None, even_own.at[0], even_own.at[1], even_more.at[0], even_more.at[1]]
    for u in (margin - 1, margin):
        weight = (fx[u][...] + fx[u - 1][...]) + (fy[u][body] + fy[u][plane.down]) + (fz[u][...] + fzl[u][...])
        inv[u][...] = 1.0 / (1.0 + weight)

    def around(ref, u):
        return in_layer(plane, fy[u], fz[u], fzl[u], ref[u])

    u = margin - 1
    total = s(u) + around(old, u) + (fx[u][...] * old[u + 1][body] + fx[u - 1][...] * old[u - 1][body])
    plane.put(even[u], total * inv[u][...])
    plane.put(even[margin], (part(2) + fx[u][...] * old[u][body]) * inv[margin][...])
    for u in range(2, margin + 1):
        if u < margin:
            total = s(u) + around(even, u) + (fx[u][...] * even[u + 1][body] + fx[u - 1][...] * even[u - 1][body])
        else:
            total = part(2) + around(even, u) + fx[u - 1][...] * even[u - 1][body]
        fresh = total * inv[u][...]
        new[u - 2] = fresh
        plane.put(change.at[u - 2], fresh - old[u][body])
    change = {u: change.at[u - 2] for u in range(2, margin + 1)}

    one = fx[1][...] * change[2][body]
    two = around(change, 2) + fx[2][...] * change[3][body]
    three = around(change, 3) + (fx[2][...] * change[2][body] + fx[3][...] * change[4][body])
    outer = jnp.where(plane.even(1), one, 0.0)
    inner = jnp.where(plane.even(2), two, 0.0) + jnp.where(plane.even(3), three, 0.0)
    core = core_of()

    def tile(name, outer, inner):
        message[places[name], :] = plane.packed(outer, inner, core)

    tile("source2", plane.summed(outer, turn.at[1]), plane.summed(inner, turn.at[2]))
    tile("fx2", plane.summed(fx[1][...], turn.at[3]), plane.summed(fx[3][...], turn.at[4]))
    fy2 = [plane.odd_rows(fy[u][body] + fy[u + 1][body], turn.at[5 + u // 2]) for u in (0, 2)]
    fz2 = [plane.odd_lanes(fz[u][...] + fz[u + 1][...], turn.at[7 + u // 2]) for u in (0, 2)]
    own2[0], own2[1] = plane.packed(*fy2, core), plane.packed(*fz2, core)
    tile("far2", fy2[1], fz2[1])
    for u in range(2):
        message[places["coef%d" % u], :] = cell[u]
    first = s(0) + around(old, 0) + fx[0][...] * old[1][body]
    second = s(0) + fx[0][...] * even[1][body]
    message[places["known0"], :] = jnp.where(plane.even(0), first, second)
    message[places["old0"], :] = odd_cells(iterate.at[own_layer(0, layers)], half, plane.odd_first(0))
    total = s(1) + around(even, 1) + fx[1][...] * even[2][body]
    known1[...] = total
    turn[9] = total * inv[1][...] - old[1][body]
    message[places["moved1"], :] = odd_cells(turn.at[9], half, plane.odd_first(1))
    message[places["face2"], :] = odd_cells(fx[1], half, plane.odd_first(1))


def border_kernel(
    inputs, message, own2, known1, new_in, fx_in, fy_in, fz_in, fzl_in, inv_in, across_in,
    within, fx2_in, new, known, fx, fy, fz, fzl, inv,
    old, even, change, turn, face_y, face_z, face_zl,
):
    iterate, source, _ = three_parts(inputs)
    layers, height, depth = iterate.shape
    plane = Plane(height, depth)
    body, half = plane.body, plane.half
    places, _ = chip_rows(height)
    core, last = core_of(), lax.axis_size("gx") - 1
    position = lax.axis_index("gx")

    def mine(name):
        return message[places[name], :]

    def theirs(name):
        return across_in[places[name], :]

    def opened(name, k):
        into_both_rows(turn.at[k], theirs(name))
        return turn[k]

    for k in range(2):
        here = theirs("coef%d" % k)
        plane.put(face_y.at[k], plane.face_y(here))
        face = plane.face_z(here)
        face_z[k] = face
        face_zl[k] = behind(face, 1, 1)
    fy[...], fz[...], fzl[...] = face_y[0], face_z[0], face_zl[0]
    there = position - 1 + 2 * core
    border = jnp.where((there >= 0) & (there <= last), 0.5 * (mine("coef0") + theirs("coef0")), 0.0)
    face1 = 0.5 * (theirs("coef0") + theirs("coef1"))
    face2 = opened("face2", 2)
    fx[0], fx[1] = border, face1

    def inverse(faces, fy, fz, fzl):
        weight = faces + (fy[body] + fy[plane.down]) + (fz[...] + fzl[...])
        return 1.0 / (1.0 + weight)

    inv_own = inverse(fx_in[0] + border, fy_in.at[0], fz_in.at[0], fzl_in.at[0])
    inv_near = inverse(border + face1, face_y.at[0], face_z.at[0], face_zl.at[0])
    inv_far = inverse(face1 + face2, face_y.at[1], face_z.at[1], face_zl.at[1])
    inv[0], inv[1] = inv_near, inv_own
    old_own, old_next = iterate[own_layer(0, layers)], iterate[own_layer(1, layers)]
    old_near, far = opened("old0", 0), opened("moved1", 1)
    even_own = (mine("known0") + border * old_near) * inv_own
    even_near = (theirs("known0") + border * old_own) * inv_near
    plane.put(even.at[0], even_near)
    plane.put(even.at[1], even_own)

    def near(ref, k):
        return in_layer(plane, face_y.at[k], face_z.at[k], face_zl.at[k], ref)

    def own(ref, u):
        return in_layer(plane, fy_in.at[u], fz_in.at[u], fzl_in.at[u], ref)

    odd_own = (mine("known0") + own(even.at[1], 0) + border * even_near) * inv_own
    odd_near = (theirs("known0") + near(even.at[0], 0) + border * even_own) * inv_near
    odd_next = (known1[...] + fx_in[0] * even_own) * inv_in[0]
    far = far + face1 * even_near * inv_far
    new[0], new[1], new[2] = odd_near, odd_own, odd_next
    near_by, here, following = odd_near - old_near, odd_own - old_own, odd_next - old_next
    for k, values in enumerate((far, near_by, here, following)):
        plane.put(change.at[k], values)
    plane.put(old.at[0], old_near)
    known[...] = theirs("known0") + face1 * far - near(old.at[0], 0)

    def residual(u, values):
        return jnp.where(plane.even(u), values, 0.0)

    own_outer = residual(1, own(change.at[3], 1) + fx_in[0] * here)
    own_outer = own_outer + residual(0, own(change.at[2], 0) + (fx_in[0] * following + border * near_by))
    own_inner = residual(2, fx_in[1] * following)
    its_outer = residual(-1, near(change.at[1], 0) + (face1 * far + border * here))
    its_outer = its_outer + residual(-2, near(change.at[0], 1) + face1 * near_by)
    its_inner = residual(-3, face2 * far)
    sums = [plane.summed(values, turn.at[3 + k]) for k, values in enumerate((own_outer, own_inner, its_outer, its_inner))]
    within[0] = mine("source2") + plane.packed(sums[0], sums[1], core)
    within[5] = theirs("source2") + plane.packed(sums[2], sums[3], 1 - core)
    within[6] = theirs("fx2")
    far2 = theirs("far2")
    far2_swap = jnp.where((plane.half_lane & 1) == 0, ahead(far2, 1, 1), behind(far2, 1, 1))
    near_fy2 = plane.odd_rows(face_y[0, body] + face_y[1, body], turn.at[1])
    near_fz2 = plane.odd_lanes(face_z[0] + face_z[1], turn.at[2])
    within[7] = plane.packed(near_fy2, far2_swap, 1 - core)
    within[8] = plane.packed(near_fz2, far2, 1 - core)
    fx2_in[...] = mine("fx2")
    middle = jnp.where((plane.half_lane & 1) == 0, ahead(mine("fx2"), 1, 1), behind(mine("fx2"), 1, 1))
    within[1] = plane.packed(plane.summed(border, turn.at[7]), middle, core)
    within[2], within[3] = own2[0], own2[1]
    turn[0] = source[own_layer(layers - 1, layers)] + fx_in[layers - 2] * new_in[layers - 4]
    within[4] = odd_cells(turn.at[0], half, jnp.logical_not(plane.odd_first(layers - 1)))


def neigh2(e2, fx2, fxl2, fy2, fz2, fzl2, first_of_two, tiles):
    half = fx2.shape[1]
    body, up, down = pl.ds(PAD, half), pl.ds(PAD + 1, half), pl.ds(PAD - 1, half)
    needed = range(tiles[0], tiles[-1] + 3)
    here = {j: e2[j, body] for j in needed}
    after = {j: ahead(here[j], 1, 1) for j in needed}
    before = {j: behind(here[j], 1, 1) for j in needed}
    found = []
    for j in tiles:
        k = j + 1
        upper = jnp.where(first_of_two, after[k], before[k + 1])
        lower = jnp.where(first_of_two, after[k - 1], before[k])
        sums = fx2[j] * upper + fxl2[j] * lower
        sums = sums + fy2[j, body] * e2[k, up] + fy2[j, down] * e2[k, down]
        sums = sums + fz2[j] * ahead(here[k], 2, 1) + fzl2[j] * behind(here[k], 2, 1)
        found.append(sums)
    return found


def parities2(half, lanes):
    row, lane = rows_of((half, lanes)), lanes_of((half, lanes))
    return (lane & 1) == 0, ((row + (lane & 1) + (lane >> 1)) & 1) == 0


def group(values):
    return with_partner(with_partner(values, 1, 1), 2, 1)


def packed_odd(values, pair):
    half, lanes = values.shape
    lane = lanes_of((half // 2, lanes))
    pair[...] = values
    return odd_cells(pair, half // 2, (((lane & 1) + (lane >> 1)) & 1) != 0)


def middle_down_kernel(
    own, fx2_in, within_in,
    slots, e2_out, s2, fx2, fxl2, fy2, fz2, fzl2, inv2,
    e2, pair,
):
    _, half, lanes = own.shape
    quarter = half // 2
    first_of_two, even2 = parities2(half, lanes)
    body, down = pl.ds(PAD, half), pl.ds(PAD - 1, half)
    edge = jnp.zeros((PAD, lanes), jnp.float32)
    for j in (0, 5):
        e2[j] = jnp.zeros((half + 2 * PAD, lanes), jnp.float32)

    def pair_of(k):
        return by_side(own[k], within_in[k])

    def four(k):
        (left, right), (far_left, far_right) = pair_of(k), pair_of(5 + k)
        return far_left, left, right, far_right

    for j, (source, fy, fz) in enumerate(zip(four(0), four(2), four(3))):
        s2[j] = source
        fy2[j, :PAD] = edge
        fy2[j, body] = fy
        fy2[j, PAD + half:] = edge
        fz2[j] = fz
        fzl2[j] = behind(fz, 2, 1)

    def between(left, right):
        return jnp.where(first_of_two, ahead(left, 1, 1), behind(right, 1, 1))

    fxl0, fxl1, fxr2, fxr3 = four(1)
    inner = fx2_in[...]
    fxr1, _ = by_side(inner, between(fxl1, inner))
    fxl2_, _ = by_side(between(inner, fxr2), inner)
    for j, (face, low) in enumerate(
        ((between(fxl0, fxl1), fxl0), (fxr1, fxl1), (fxr2, fxl2_), (fxr3, between(fxr2, fxr3)))
    ):
        fx2[j], fxl2[j] = face, low
        weight = face + low + fy2[j, body] + fy2[j, down] + fz2[j] + fzl2[j]
        inverse = 1.0 / (8.0 + weight)
        inv2[j] = inverse
        e2[j + 1, :PAD] = edge
        e2[j + 1, PAD + half:] = edge
        e2[j + 1, body] = s2[j] * inverse

    def neigh(tiles):
        return neigh2(e2, fx2, fxl2, fy2, fz2, fzl2, first_of_two, tiles)

    fresh = [(s2[j] + sums) * inv2[j] for j, sums in enumerate(neigh((0, 1, 2, 3)))]
    for j in range(4):
        e2[j + 1, body] = fresh[j]
        e2_out[j] = fresh[j]
    lane = lanes_of((quarter, lanes))
    odd_layer, odd_depth = (lane & 1) != 0, (lane & 2) != 0
    chips = slots.shape[0]
    for k, sums in enumerate(neigh((1, 2))):
        j = k + 1
        pair[k] = jnp.where(even2, sums, 0.0)
        item = (lane - (lax.axis_index("gx") // 2 * 2 + k) // (chips // 2)) & 3
        source = group(even_row_sum(pair.at[k], quarter))
        fx = group(jnp.where(odd_layer, even_row_sum(fx2.at[j], quarter), 0.0))
        fxl = group(jnp.where(odd_layer, 0.0, even_row_sum(fxl2.at[j], quarter)))
        fy = group(fy2[j, pl.ds(PAD + 1, quarter, 2), :])
        fz = group(jnp.where(odd_depth, even_row_sum(fz2.at[j], quarter), 0.0))
        weight = (fx + fxl) + (fy + behind(fy, 1, 0)) + (fz + behind(fz, 4, 1))
        start = source / (64.0 + weight)
        tile = jnp.where(item == 0, start, jnp.where(item == 1, fx, jnp.where(item == 2, fy, fz)))
        for c in range(chips):
            slots[c, k] = tile
    halo = packed_odd(jnp.where(first_of_two, fresh[2], fresh[1]), pair.at[2])
    for c in range(chips):
        slots[c, 2] = halo


def joined(one, two):
    return jnp.concatenate([part for part in (one, two) if part.shape[0]], 0)


class Level:
    def __init__(self, mass, source, faces, row_step, lane_step, slot_step):
        self.source, self.row_step, self.lane_step, self.slot_step = source, row_step, lane_step, slot_step
        self.fx, self.fy, self.fz = faces
        self.tiles = source.shape[0]
        shape = source.shape
        self.lane = lanes_of(shape)
        layer = lax.broadcasted_iota(jnp.int32, shape, 0) if self.tiles > 1 else self.lane // slot_step
        self.even = ((layer + rows_of(shape) // row_step + self.lane // lane_step) & 1) == 0
        self.fxl = self.lower(self.fx)
        self.fyl = self.row_shifts(self.fy)[1]
        self.fzl = behind(self.fz, lane_step, 2)
        weight = (self.fx + self.fxl) + (self.fy + self.fyl) + (self.fz + self.fzl)
        self.inv = 1.0 / (mass + weight)

    def upper(self, e):
        return joined(e[1:], ahead(e[:1], self.slot_step, 2))

    def lower(self, e):
        return joined(behind(e[-1:], self.slot_step, 2), e[:-1])

    def row_shifts(self, e):
        return ahead(e, self.row_step, 1), behind(e, self.row_step, 1)

    def neigh(self, e):
        above, below = self.row_shifts(e)
        total = (self.fx * self.upper(e) + self.fxl * self.lower(e)) + (self.fy * above + self.fyl * below)
        return total + (self.fz * ahead(e, self.lane_step, 2) + self.fzl * behind(e, self.lane_step, 2))

    def start(self):
        return self.source * self.inv

    def update(self, e):
        return self.start() + self.neigh(e) * self.inv

    def cycle(self, deeper):
        odd = self.update(self.start())
        residual = jnp.where(self.even, self.neigh(odd), 0.0)
        fix = deeper(self.restricted(residual), self.coarse_faces())
        even = self.update(odd + self.prolonged(fix))
        return jnp.where(self.even, even, self.update(even))

    def coarse_slot_step(self):
        return self.slot_step if self.tiles > 1 else 2 * self.slot_step

    def pairs(self, values):
        if self.tiles == 1:
            return with_partner(values, self.slot_step, 2)
        halves = values.reshape(self.tiles // 2, 2, *values.shape[1:])
        return halves[:, 0] + halves[:, 1]

    def odd_layers(self, values):
        if self.tiles == 1:
            return with_partner(jnp.where((self.lane & self.slot_step) != 0, values, 0.0), self.slot_step, 2)
        return values.reshape(self.tiles // 2, 2, *values.shape[1:])[:, 1]

    def row_pairs(self, values):
        return with_partner(values, self.row_step, 1)

    def odd_rows(self, values):
        odd = (rows_of(values.shape) & self.row_step) != 0
        return with_partner(jnp.where(odd, values, 0.0), self.row_step, 1)

    def restricted(self, values):
        return with_partner(self.row_pairs(self.pairs(values)), self.lane_step, 2)

    def coarse_faces(self):
        fx = with_partner(self.row_pairs(self.odd_layers(self.fx)), self.lane_step, 2)
        fy = with_partner(self.odd_rows(self.pairs(self.fy)), self.lane_step, 2)
        return fx, fy, self.restricted(jnp.where((self.lane & self.lane_step) != 0, self.fz, 0.0))

    def prolonged(self, fix):
        if self.tiles == 1:
            return fix
        both = jnp.concatenate([fix[:, None], fix[:, None]], 1)
        return both.reshape(self.tiles, *fix.shape[1:])


class Rows(Level):
    def __init__(self, mass, source, faces, scratch):
        self.scratch, self.used = scratch, 0
        self.rows = source.shape[1]
        super().__init__(mass, source, faces, 1, 4, 1)

    def start(self):
        return self.source

    def place(self):
        self.used += 1
        return self.scratch.at[self.used % self.scratch.shape[0]]

    def row_shifts(self, e):
        place = self.place()
        edge = jnp.zeros((e.shape[0], PAD, e.shape[2]), jnp.float32)
        place[:, :PAD] = edge
        place[:, PAD + self.rows:] = edge
        place[:, pl.ds(PAD, self.rows)] = e
        return place[:, pl.ds(PAD + 1, self.rows)], place[:, pl.ds(PAD - 1, self.rows)]

    def every_other(self, values, starts):
        place, tiles = self.place(), values.shape[0]
        place[:tiles, : self.rows] = values
        found = 0.0
        for start in starts:
            found = found + jnp.concatenate(
                [place[j, pl.ds(start, self.rows // 2, 2), :][None] for j in range(tiles)], 0
            )
        return found

    def row_pairs(self, values):
        return self.every_other(values, (0, 1))

    def odd_rows(self, values):
        return self.every_other(values, (1,))

    def prolonged(self, fix):
        place, tiles = self.place(), fix.shape[0]
        for j in range(tiles):
            into_both_rows(place.at[j, pl.ds(0, self.rows)], fix[j])
        return super().prolonged(place[:tiles, : self.rows])


def coarsest(mass, source, faces, *steps):
    row_step, lane_step, slot_step = steps
    level = Level(mass, source, faces, *steps)
    counts = source.shape[1] // row_step, source.shape[2] // lane_step, 4 // slot_step
    frames = [(m, k, q) for m in range(counts[0]) for k in range(counts[1]) for q in range(counts[2])]
    place = level.lane & 3

    def spread(values):
        copies = {}
        for m, k, q in frames:
            if k:
                copies[m, k, q] = behind(copies[m, 0, q], k * lane_step, 2)
            elif q:
                by = q * slot_step
                one, two = behind(copies[m, 0, 0], by, 2), ahead(copies[m, 0, 0], 4 - by, 2)
                copies[m, k, q] = jnp.where(place >= by, one, two)
            else:
                copies[m, k, q] = behind(values, m * row_step, 1) if m else values
        return copies

    start, inv, fx, fy, fz = [spread(values) for values in (source * level.inv, level.inv, level.fx, level.fy, level.fz)]

    def shifted(copies, frame, axis, by):
        moved = list(frame)
        moved[axis] = (frame[axis] - by) % counts[axis]
        return copies[tuple(moved)]

    def along_x(copies, frame, by):
        here, wrapped = copies[frame], shifted(copies, frame, 2, by)
        return joined(here[1:], wrapped[:1]) if by > 0 else joined(wrapped[-1:], here[:-1])

    same = level.tiles == 1 and counts[2] == 2, counts[0] == 2, counts[1] == 2
    weights = {}
    for frame in frames:
        pairs = [
            (fx[frame], along_x(fx, frame, -1)),
            (fy[frame], shifted(fy, frame, 0, -1)),
            (fz[frame], shifted(fz, frame, 1, -1)),
        ]
        weights[frame] = [
            ((up + low) * inv[frame], None) if merged else (up * inv[frame], low * inv[frame])
            for (up, low), merged in zip(pairs, same)
        ]

    def update(e):
        fresh = {}
        for frame in frames:
            moves = along_x, lambda c, f, by: shifted(c, f, 0, by), lambda c, f, by: shifted(c, f, 1, by)
            total = 0.0
            for (up, low), move in zip(weights[frame], moves):
                part = up * move(e, frame, 1)
                total = total + (part if low is None else part + low * move(e, frame, -1))
            fresh[frame] = start[frame] + total
        return fresh

    even = start
    odd = update(even)
    for turn in range(COARSE_SWEEPS - 1):
        even = update(odd)
        odd = update(even)
    return jnp.where(level.even, even[0, 0, 0], odd[0, 0, 0])


def small_cycle(mass, source, faces, row_step, lane_step, slot_step, between):
    if between == 0:
        return coarsest(mass, source, faces, row_step, lane_step, slot_step)
    level = Level(mass, source, faces, row_step, lane_step, slot_step)
    return level.cycle(
        lambda inner, inner_faces: small_cycle(
            8.0 * mass, inner, inner_faces, 2 * row_step, 2 * lane_step, level.coarse_slot_step(), between - 1
        )
    )


def coarse_kernel(
    owner_of, gathered, e2_in, s2_in, fx2_in, fxl2_in, fy2_in, fz2_in, fzl2_in, inv2_in,
    inputs, new_in, fx_more, fy_margin, fz_margin, fzl_margin, inv_more, fx_in, fy_in, fz_in, fzl_in, inv_in,
    new_out, known_out, fx_out, fy_out, fz_out, fzl_out, inv_out, within_in,
    solved_out, owned_out,
    e3, rows3, pair, e2, e1, cor, solved, owned, owner_here, fetch_sem, sems,
):
    fetch = pltpu.make_async_copy(owner_of, owner_here, fetch_sem)
    fetch.start()
    chips, _, quarter, lanes = gathered.shape
    blocks = 2 * chips
    half, height = 2 * quarter, 4 * quarter
    position, last = lax.axis_index("gx"), blocks - 1

    slot = lanes_of((quarter, lanes)) & 3
    spread = blocks // 4
    tiles = [gathered[chip, k] for chip in reversed(range(chips)) for k in range(2)]
    items = []
    for k in range(4):
        packs = []
        for j in range(spread):
            value = tiles[j + (3 - k) % 4 * spread]
            for at in range(3):
                value = jnp.where(slot == at, tiles[j + (at - k) % 4 * spread], value)
            if k:
                value = jnp.where(slot < 4 - k, ahead(value, k, 1), behind(value, 4 - k, 1))
            packs.append(value[None])
        items.append(jnp.concatenate(packs, 0))
    third = Rows(64.0, items[0], items[1:], rows3)
    e3[...] = third.cycle(
        lambda inner, faces: small_cycle(512.0, inner, faces, 1, 8, third.coarse_slot_step(), 2)
    )

    first_of_two, even2 = parities2(half, lanes)
    body2 = pl.ds(PAD, half)
    edge = jnp.zeros((PAD, lanes), jnp.float32)
    core = core_of()
    s2, fx2, fxl2, fy2, fz2, fzl2, inv2 = [
        ref.at[pl.ds(core, 3)] for ref in (s2_in, fx2_in, fxl2_in, fy2_in, fz2_in, fzl2_in, inv2_in)
    ]
    next_chip = jnp.clip(position // 2 - 1 + 2 * core, 0, chips - 1)
    into_both_rows(pair.at[5], gathered[chips - 1 - next_chip, 2])
    halo = pair[5]
    before = (
        by_side(halo, e2_in[0])[0], by_side(jnp.where(first_of_two, halo, e2_in[0]), e2_in[1])[0],
        by_side(e2_in[1], e2_in[2])[0],
        by_side(e2_in[2], jnp.where(first_of_two, e2_in[3], halo))[0], by_side(e2_in[3], halo)[0],
    )
    for k in range(5):
        j = jnp.clip(position + k - 2, 0, last)
        into_both_rows(pair.at[k], group(jnp.where(slot == j // spread, e3[j % spread], 0.0)))
        e2[k, :PAD] = edge
        e2[k, PAD + half:] = edge
        e2[k, body2] = before[k] + pair[k]

    def update2():
        sums = neigh2(e2, fx2, fxl2, fy2, fz2, fzl2, first_of_two, (0, 1, 2))
        return [(s2[j] + sums[j]) * inv2[j] for j in range(3)]

    fresh = update2()
    for j in range(3):
        e2[j + 1, body2] = fresh[j]
    fixes2 = [jnp.where(even2, even, odd) for even, odd in zip(fresh, update2())]

    fetch.wait()
    owner = owner_here[position]
    shape = lanes // 4, lanes
    take = jnp.where(lanes_of(shape) == 4 * rows_of(shape) + owner // spread, 1.0, 0.0)
    owned[0] = lax.dot_general(
        e3[owner % spread], take, (((1,), (1,)), ((), ())),
        precision=lax.Precision.HIGHEST, preferred_element_type=jnp.float32,
    )
    copies = [pltpu.make_async_copy(owned, owned_out, sems.at[0])]
    copies[0].start()

    _, source, _ = three_parts(inputs)
    layers = source.shape[0]
    plane = Plane(height, lanes)
    body1 = plane.body
    near_lane = (lanes_of((half, lanes)) & 1) == core
    swaps = [jnp.where(first_of_two, ahead(v, 1, 1), behind(v, 1, 1)) for v in fixes2]
    outer, inner = by_side(fixes2[0], fixes2[2])
    outer_swap, inner_swap = by_side(swaps[0], swaps[2])
    coarse = (
        jnp.where(near_lane, outer_swap, outer), jnp.where(near_lane, fixes2[1], swaps[1]),
        jnp.where(near_lane, swaps[1], fixes2[1]), jnp.where(near_lane, inner, inner_swap),
    )
    fixes = []
    for k in range(4):
        into_both_rows(cor.at[k], coarse[k])
        fixes.append(cor[k])
    for u in range(-1, layers + 1):
        before = new_out[u + 1] if u < 2 else new_in[u - 2]
        plane.put(e1.at[u + 1], before + fixes[(u + 2) // 2])

    def fx1(u):
        if u < 0:
            return fx_out[-1 - u]
        return fx_in[u] if u < layers - 1 else fx_more[u - layers + 1]

    def inv1(u):
        if u <= 0:
            return inv_out[u + 1]
        return inv_in[u - 1] if u < layers - 1 else inv_more[u - layers + 1]

    def around1(u):
        if u < 0:
            return in_layer(plane, fy_out, fz_out, fzl_out, e1.at[0])
        if u == layers:
            return in_layer(plane, fy_margin, fz_margin, fzl_margin, e1.at[u + 1])
        return in_layer(plane, fy_in.at[u], fz_in.at[u], fzl_in.at[u], e1.at[u + 1])

    def updated1(u):
        sums = around1(u) + (fx1(u) * e1[u + 2, body1] + fx1(u - 1) * e1[u, body1])
        return (source[own_layer(u, layers)] + sums) * inv1(u)

    for u in range(layers):
        e1[u + 1, body1] = jnp.where(plane.even(u), updated1(u), e1[u + 1, body1])
    e1[0, body1] = (known_out[...] + fx1(-2) * fixes[0] + (around1(-1) + fx1(-1) * e1[1, body1])) * inv1(-1)
    into_both_rows(cor.at[4], within_in[4])
    sums = cor[4] + fx1(layers) * fixes[3] + (around1(layers) + fx1(layers - 1) * e1[layers, body1])
    e1[layers + 1, body1] = sums * inv1(layers)
    for u in range(layers):
        solved[u] = jnp.where(plane.even(u), e1[u + 1, body1], updated1(u))
        copies.append(
            pltpu.make_async_copy(solved.at[u], solved_out.at[own_layer(u, layers)], sems.at[u + 1])
        )
        copies[-1].start()
    for copy in copies:
        copy.wait()


def f32(*shape):
    return jax.ShapeDtypeStruct(shape, jnp.float32)


def vmem(*shape):
    return pltpu.VMEM(shape, jnp.float32)


def call(kernel, outs, scratch, operands, out_space=pltpu.VMEM):
    def size(shape):
        count = 4
        for extent in shape:
            count *= extent
        return count

    sized = [array for array in (*scratch, *outs, *operands) if hasattr(array, "shape")]
    asked = 8 * 2**20 + sum(size(array.shape) for array in sized)
    return pl.pallas_call(
        kernel,
        out_shape=tuple(outs),
        in_specs=[pl.BlockSpec(memory_space=pltpu.VMEM)] * len(operands),
        out_specs=tuple([pl.BlockSpec(memory_space=out_space)] * len(outs)),
        scratch_shapes=scratch,
        compiler_params=pltpu.CompilerParams(vmem_limit_bytes=asked),
    )(*operands)


def on_device(iterate, source, phase_field, block_owner):
    layers, height, depth = iterate.shape
    half, quarter = height // 2, height // 4
    blocks = lax.axis_size("gx")
    padded, padded2 = height + 2 * PAD, half + 2 * PAD
    inputs = sum(
        jnp.pad(block, ((k * layers, (2 - k) * layers), (0, 0), (0, 0)))
        for k, block in enumerate((iterate, source, phase_field))
    )
    edge, = call(edge_kernel, [f32(3 * height + half, depth)], [], (inputs,))
    edge_in = within_chip(edge)
    layer, tile, tall = (height, depth), (half, depth), (padded, depth)
    cell, old, *fine, even = call(
        own_kernel,
        [
            f32(layers, *layer), f32(layers, *tall), f32(layers - 1, *layer), f32(layers, *tall),
            f32(layers, *layer), f32(layers, *layer), f32(2, *layer), f32(2, *tall),
        ],
        [], (block_owner, inputs),
    )
    message, own2, known1, new, *margin = call(
        chip_kernel,
        [
            f32(chip_rows(height)[1], depth), f32(2, *tile), f32(*layer), f32(3, *layer),
            f32(2, *layer), f32(*tall), f32(*layer), f32(*layer), f32(2, *layer),
        ],
        [vmem(*tall), vmem(2, *tall), vmem(3, *tall), vmem(10, *layer)],
        (inputs, cell, old, *fine, even, edge_in),
    )
    within, fx2, *border = call(
        border_kernel,
        [
            f32(9, *tile), f32(*tile), f32(3, *layer), f32(*layer), f32(2, *layer),
            f32(padded, depth), f32(*layer), f32(*layer), f32(2, *layer),
        ],
        [
            vmem(1, padded, depth), vmem(2, padded, depth), vmem(4, padded, depth), vmem(8, *layer),
            vmem(2, padded, depth), vmem(2, *layer), vmem(2, *layer),
        ],
        (inputs, message, own2, known1, new, *fine, between_chips(message)),
    )
    within_in = within_chip(within)
    plain = f32(4, *tile)
    slots, *middle = call(
        middle_down_kernel,
        [f32(blocks // 2, 3, quarter, depth), plain, plain, plain, plain, f32(4, padded2, depth)] + [plain] * 3,
        [vmem(6, padded2, depth), vmem(3, *tile)],
        (within, fx2, within_in),
    )
    kinds = [[2 * chip + (chip // 2 + core) % 2 for chip in reversed(range(blocks // 2))] for core in range(2)]
    gathered = lax.all_to_all(slots, "gx", 0, 0, axis_index_groups=kinds, tiled=True)
    solved, owned = call(
        coarse_kernel,
        [f32(layers, *layer), f32(1, quarter, depth // 4)],
        [
            vmem(blocks // 4, quarter, depth), vmem(4, blocks // 4, quarter + 2 * PAD, depth), vmem(7, *tile),
            vmem(5, padded2, depth), vmem(layers + 2, padded, depth), vmem(5, *layer), vmem(layers, *layer),
            vmem(1, quarter, depth // 4), pltpu.SMEM((blocks,), jnp.int32),
            pltpu.SemaphoreType.DMA, pltpu.SemaphoreType.DMA((layers + 1,)),
        ],
        (block_owner, gathered, *middle, inputs, new, *margin, *fine, *border, within_in),
        pl.ANY,
    )
    return solved, owned


def solution(mesh):
    split = P(("groups", "gx"), None, None)
    return jax.shard_map(
        on_device,
        mesh=mesh,
        in_specs=(split, split, split, P("groups")),
        out_specs=(split, split),
        check_vma=False,
    )
```
